128 devices in a mesh: dp: 32 (over z, y, x_lo), mp: 4 (over x_hi, core).
Axes of the slice: x: 4 (x_hi: 2, x_lo: 2; x = x_hi * 2 + x_lo), y: 4, z: 4, core: 2. Of those that a mesh axis runs over, the one named last changes fastest.
Arguments:
- tokens: bfloat16 [32768, 768], P('dp'), may hold values from -6 to 6
- lengths: int32 [512], P('dp'), may hold values from 1 to 512, as said below
- pair_index: int32 [256], replicated, may hold values from 0 to 255, each once
- query_proj: bfloat16 [768, 768], P(None, 'mp'), may hold values from -0.21875 to 0.21875
- query_bias: bfloat16 [768], P('mp'), may hold values from -3 to 3
- key_proj: bfloat16 [768, 768], P(None, 'mp'), may hold values from -0.21875 to 0.21875
- value_proj: bfloat16 [768, 768], P(None, 'mp'), may hold values from -0.21875 to 0.21875
- value_bias: bfloat16 [768], P('mp'), may hold values from -3 to 3
- output_proj: bfloat16 [768, 768], P('mp'), may hold values from -1.75 to 1.75
- output_bias: bfloat16 [768], replicated, may hold values from -2 to 2
- attn_gain: bfloat16 [768], replicated, may hold values from 0.5 to 1.5
- attn_shift: bfloat16 [768], replicated, may hold values from -1 to 1
- inner_proj: bfloat16 [768, 3072], P(None, 'mp'), may hold values from -0.21875 to 0.21875
- inner_bias: bfloat16 [3072], P('mp'), may hold values from -3 to 3
- outer_proj: bfloat16 [3072, 768], P('mp'), may hold values from -0.109375 to 0.109375
- outer_bias: bfloat16 [768], replicated, may hold values from -1 to 1
- final_gain: bfloat16 [768], replicated, may hold values from 0.5 to 1.5
- final_shift: bfloat16 [768], replicated, may hold values from -0.29882812 to 0.29882812
Outputs:
- loss_value: float32 [], replicated
- token_grad: bfloat16 [32768, 768], P('dp')
- queryproj_grad: float32 [768, 768], P(None, 'mp')
- querybias_grad: float32 [768], P('mp')
- keyproj_grad: float32 [768, 768], P(None, 'mp')
- valueproj_grad: float32 [768, 768], P(None, 'mp')
- valuebias_grad: float32 [768], P('mp')
- outputproj_grad: float32 [768, 768], P('mp')
- outputbias_grad: float32 [768], replicated
- attngain_grad: float32 [768], replicated
- attnshift_grad: float32 [768], replicated
- innerproj_grad: float32 [768, 3072], P(None, 'mp')
- innerbias_grad: float32 [3072], P('mp')
- outerproj_grad: float32 [3072, 768], P('mp')
- outerbias_grad: float32 [768], replicated
- finalgain_grad: float32 [768], replicated
- finalshift_grad: float32 [768], replicated
The draws below stay inside these ranges and needn't reach their ends.
Inputs may be any that keep to these rules, and one draw needn't show every extreme that they name: Pack g's entries are 8 query lengths of at most 32 followed by 8 passage lengths; a pack's lengths sum to at most 1024; in every draw some pack holds a passage of exactly 512 tokens. `pair_index`: each query is named by exactly one passage.
All inputs are finite; a program needn't handle non-finite values.
Results may differ from the reference program's by a relative error of at most 0.025.
Values may be sent and summed in bfloat16 or wider, within the bound.
No kernel may reach another device: no remote copies, remote signals or barrier semaphores. Data moves between devices by JAX's collectives and lax.ppermute only.
A program may use at most 128 MiB of HBM per device.

```python
import math
import jax
import jax.numpy as jnp
from jax import lax

D = 768
HEADS = 12
HD = 64
FF = 3072
PAIR_DEV = 8
QUERY_MAX = 32
TOK_DEV = 1024
L_MAX = 512
PAIRS = 256
TOKENS = 32768
SEQ_ALL = 512


def draw_lengths(key, part):
    key = jax.random.fold_in(key, 11)
    group_count = SEQ_ALL // (2 * PAIR_DEV)
    subkeys = jax.random.split(key, 6)
    query_len = jax.random.randint(subkeys[0], (group_count, PAIR_DEV), 4, QUERY_MAX + 1)
    factor_one = jax.random.randint(subkeys[1], (group_count, PAIR_DEV), 4, 17)
    factor_two = jax.random.randint(subkeys[2], (group_count, PAIR_DEV), 4, 17)
    weight_group = jax.random.randint(subkeys[3], (group_count, 1), 1, 5)
    passage_len = jnp.maximum(1, L_MAX * factor_one * factor_two * weight_group // 1024)
    free_room = TOK_DEV - jnp.sum(query_len, axis=1, keepdims=True)
    passage_sum = jnp.sum(passage_len, axis=1, keepdims=True)
    shrunk = jnp.maximum(1, passage_len * (free_room - PAIR_DEV) // passage_sum)
    passage_len = jnp.where(passage_sum > free_room, shrunk, passage_len)
    chosen = jax.random.randint(subkeys[4], (), 0, group_count)
    small_tail = jax.random.randint(subkeys[5], (group_count, PAIR_DEV), 1, 17)
    column = jnp.arange(PAIR_DEV)[None, :]
    special_passage = jnp.where(column == 0, L_MAX, small_tail)
    is_chosen = (jnp.arange(group_count) == chosen)[:, None]
    passage_len = jnp.where(is_chosen, special_passage, passage_len)
    query_len = jnp.where(is_chosen, jnp.minimum(query_len, 16), query_len)
    return jnp.concatenate([query_len, passage_len], axis=1).reshape(-1).astype(jnp.int32)


def block_levels(rng, dims, cuts, least, largest):
    factor_of = 1.0
    for dim, parts in cuts:
        steps = jax.random.uniform(jax.random.fold_in(jax.random.fold_in(rng, 6), dim), (parts,), jnp.float32, least / len(cuts), largest / len(cuts))
        factor_of = factor_of * jnp.repeat(jnp.exp(steps), dims[dim] // parts).reshape((-1,) + (1,) * (len(dims) - 1 - dim))
    return factor_of


def scatter_about(rng, shape, width, bound, pieces=(), kind=jnp.bfloat16):
    level = block_levels(rng, shape, pieces, -0.22, 0.18) if pieces else 1.0
    array = jax.random.normal(rng, shape, jnp.float32) * width * level
    return jnp.minimum(jnp.maximum(array, -bound), bound).astype(kind)


def setup_inputs(seed: int = 0) -> dict:
    key_list = jax.random.split(jax.random.key(seed), 19)
    return {
        "tokens": scatter_about(key_list[0], (TOKENS, D), 1.0, 6.0, ((0, 32),)),
        "lengths": draw_lengths(jax.random.fold_in(key_list[18], 71), 0),
        "pair_index": jax.random.permutation(key_list[2], PAIRS).astype(jnp.int32),
        "query_proj": scatter_about(key_list[3], (D, D), D ** -0.5, 0.21875, ((1, 4),)),
        "query_bias": scatter_about(key_list[4], (D,), 0.5, 3.0, ((0, 4),)),
        "key_proj": scatter_about(key_list[5], (D, D), D ** -0.5, 0.21875, ((1, 4),)),
        "value_proj": scatter_about(key_list[6], (D, D), D ** -0.5, 0.21875, ((1, 4),)),
        "value_bias": scatter_about(key_list[7], (D,), 0.5, 3.0, ((0, 4),)),
        "output_proj": scatter_about(key_list[8], (D, D), (max(D // 64, 1)) ** -0.5, 1.75, ((0, 4),)),
        "output_bias": scatter_about(key_list[9], (D,), 0.3, 2.0),
        "attn_gain": jnp.clip(1.0 + 0.1 * jax.random.normal(key_list[10], (D,), jnp.float32), 0.5, 1.5).astype(jnp.bfloat16),
        "attn_shift": scatter_about(key_list[11], (D,), 0.2, 1.0),
        "inner_proj": scatter_about(key_list[12], (D, FF), D ** -0.5, 0.21875, ((1, 4),)),
        "inner_bias": scatter_about(key_list[13], (FF,), 0.5, 3.0, ((0, 4),)),
        "outer_proj": scatter_about(key_list[14], (FF, D), FF ** -0.5, 0.109375, ((0, 4),)),
        "outer_bias": scatter_about(key_list[15], (D,), 0.2, 1.0),
        "final_gain": jnp.clip(1.0 + 0.1 * jax.random.normal(key_list[16], (D,), jnp.float32), 0.5, 1.5).astype(jnp.bfloat16),
        "final_shift": scatter_about(key_list[17], (D,), 0.05, 0.29882812),
    }


EPS_NORM = 1e-06
SOFTMAX_WARMTH = 0.01
NEG_FILL = -1e+30

@jax.custom_vjp
def low(v):
    return lax.optimization_barrier(v.astype(jnp.bfloat16)).astype(jnp.float32)

@jax.custom_vjp
def low_back(v):
    return v

def low_keep(v):
    return (low(v), None)

def low_pass(kept, grad):
    return (grad,)

def back_keep(v):
    return (v, None)

def back_low(kept, grad):
    return (low(grad),)
low.defvjp(low_keep, low_pass)
low_back.defvjp(back_keep, back_low)

def precise_product(left_arg, right_arg):
    return jnp.dot(left_arg, right_arg, precision=lax.Precision.HIGHEST, preferred_element_type=jnp.float32)

def layer_norm(values, gain_vec, shift_vec):
    average = lax.optimization_barrier(jnp.mean(values, axis=-1, keepdims=True))
    centred = values - average
    rscale = lax.rsqrt(lax.optimization_barrier(jnp.mean(centred * centred, axis=-1, keepdims=True)) + EPS_NORM)
    return centred * rscale * gain_vec + shift_vec

def pack_forward(inputs, pack_lengths, params):
    query_proj, query_bias, key_proj, value_proj, value_bias, output_proj, output_bias, attn_gain, attn_shift, inner_proj, inner_bias, outer_proj, outer_bias, final_gain, final_shift = params
    row_count = inputs.shape[0]
    seq_count = pack_lengths.shape[0]
    seq_ends = jnp.cumsum(pack_lengths).astype(jnp.int32)
    position = jnp.arange(row_count, dtype=jnp.int32)
    segment = lax.optimization_barrier(jnp.sum((position[:, None] >= seq_ends[None, :]).astype(jnp.int32), axis=1))
    same_seq = segment[:, None] == segment[None, :]
    queries = low(low_back(precise_product(inputs, query_proj) + query_bias))
    keys_all = low(low_back(precise_product(inputs, key_proj)))
    values_all = low(low_back(precise_product(inputs, value_proj) + value_bias))
    query_heads = queries.reshape(row_count, HEADS, HD)
    key_heads = keys_all.reshape(row_count, HEADS, HD)
    value_heads = values_all.reshape(row_count, HEADS, HD)
    scaling = 1.0 / math.sqrt(HD)
    scores = low_back(jnp.einsum('qhd,khd->hqk', query_heads, key_heads, precision=lax.Precision.HIGHEST) * scaling)
    masked = jnp.where(same_seq[None], scores, NEG_FILL)
    row_max = lax.optimization_barrier(jnp.max(masked, axis=-1, keepdims=True))
    exp_scores = jnp.exp(masked - row_max)
    attn_probs = exp_scores / lax.optimization_barrier(jnp.sum(exp_scores, axis=-1, keepdims=True))
    mixed = jnp.einsum('hqk,khd->qhd', low(attn_probs), value_heads, precision=lax.Precision.HIGHEST)
    mixed = low(low_back(mixed.reshape(row_count, HEADS * HD)))
    attn_out = low_back(precise_product(mixed, output_proj) + output_bias)
    hidden_one = layer_norm(inputs + attn_out, attn_gain, attn_shift)
    up_lin = low_back(precise_product(low(hidden_one), inner_proj) + inner_bias)
    activation = low(jax.nn.gelu(up_lin, approximate=False))
    ffn_out = low_back(precise_product(activation, outer_proj) + outer_bias)
    final_out = layer_norm(hidden_one + ffn_out, final_gain, final_shift)
    member = (segment[None, :] == jnp.arange(seq_count, dtype=jnp.int32)[:, None]).astype(jnp.float32)
    return precise_product(member, final_out)

def unit_rows(pooled):
    return low(pooled * lax.rsqrt(lax.optimization_barrier(jnp.sum(pooled * pooled, axis=-1, keepdims=True)) + EPS_NORM))

def contrast_loss(inputs, lengths, pair_index, params):
    pack_rows = inputs.reshape(-1, TOK_DEV, D)
    pack_lengths = lengths.reshape(-1, 2 * PAIR_DEV)
    checkpointed = jax.checkpoint(pack_forward)
    pooled = lax.map(lambda pack_item: checkpointed(pack_item[0], pack_item[1], params), (pack_rows, pack_lengths))
    query_unit_vectors = unit_rows(pooled[:, :PAIR_DEV].reshape(PAIRS, D))
    passage_unit_vectors = unit_rows(pooled[:, PAIR_DEV:].reshape(PAIRS, D))
    similarity_matrix = precise_product(query_unit_vectors, passage_unit_vectors.T) / SOFTMAX_WARMTH
    row_max = lax.optimization_barrier(jnp.max(similarity_matrix, axis=1, keepdims=True))
    row_lse = row_max[:, 0] + jnp.log(lax.optimization_barrier(jnp.sum(jnp.exp(similarity_matrix - row_max), axis=1)))
    is_match = (pair_index[None, :] == jnp.arange(PAIRS, dtype=jnp.int32)[:, None]).astype(jnp.float32)
    positive = lax.optimization_barrier(jnp.sum(similarity_matrix * is_match, axis=1))
    return jnp.mean(row_lse - positive)

def reference(tokens, lengths, pair_index, query_proj, query_bias, key_proj, value_proj, value_bias, output_proj, output_bias, attn_gain, attn_shift, inner_proj, inner_bias, outer_proj, outer_bias, final_gain, final_shift):
    weights = tuple((matrix.astype(jnp.float32) for matrix in (query_proj, query_bias, key_proj, value_proj, value_bias, output_proj, output_bias, attn_gain, attn_shift, inner_proj, inner_bias, outer_proj, outer_bias, final_gain, final_shift)))
    inputs = tokens.astype(jnp.float32)

    def objective(inputs_arg, *params):
        return contrast_loss(inputs_arg, lengths, pair_index, params)
    loss_value, pullback = jax.vjp(objective, inputs, *weights)
    gradients = pullback(jnp.ones_like(loss_value))
    token_grad = gradients[0].astype(jnp.bfloat16)
    return (loss_value, token_grad, gradients[1], gradients[2], gradients[3], gradients[4], gradients[5], gradients[6], gradients[7], gradients[8], gradients[9], gradients[10], gradients[11], gradients[12], gradients[13], gradients[14], gradients[15])
```

```python
import math

import jax
import jax.numpy as jnp
from jax import lax
from jax.sharding import PartitionSpec as P

HD = 64
EPS_NORM = 1e-06
SOFTMAX_WARMTH = 0.01
NEG_FILL = -1e30
HIGHEST = lax.Precision.HIGHEST
F32 = jnp.float32
BF16 = jnp.bfloat16

CORE_SWAP = [(i, i ^ 1) for i in range(4)]
FAR_SWAP = [(i, i ^ 2) for i in range(4)]
NEAR_SWAP = [(i, i ^ 1) for i in range(32)]


def ring_shift(axis, step):
    pairs = []
    for i in range(32):
        z, y, x = i // 8, (i // 2) % 4, i % 2
        if axis == "z":
            z = (z + step) % 4
        else:
            y = (y + step) % 4
        pairs.append((i, (z * 4 + y) * 2 + x))
    return pairs


def ring_place(axis):
    index = lax.axis_index("dp")
    return index // 8 if axis == "z" else (index // 2) % 4


def ring_scatter(values, axis):
    place = ring_place(axis)
    rows = values.shape[0] // 4
    total = lax.dynamic_slice_in_dim(values, place * rows, rows, 0).astype(F32)
    arrived = []
    for step in (2, 1, 3):
        piece = lax.dynamic_slice_in_dim(values, ((place + step) % 4) * rows, rows, 0)
        arrived.append(lax.ppermute(piece, "dp", ring_shift(axis, step)))
    for piece in arrived:
        total = total + piece.astype(F32)
    return total


def ring_gather(values, axis, dtype):
    place = ring_place(axis)
    rows = values.shape[0]
    whole = jnp.zeros((4 * rows,) + values.shape[1:], dtype)
    whole = lax.dynamic_update_slice_in_dim(whole, values.astype(dtype), place * rows, 0)
    for step in (2, 1, 3):
        piece = lax.ppermute(values, "dp", ring_shift(axis, step))
        whole = lax.dynamic_update_slice_in_dim(
            whole, piece.astype(dtype), ((place - step) % 4) * rows, 0
        )
    return whole


def sum_over_dp(values, first, second):
    part = ring_scatter(values, first).astype(BF16)
    part = ring_scatter(part, second).astype(BF16)
    near = lax.ppermute(part, "dp", NEAR_SWAP)
    part = (part.astype(F32) + near.astype(F32)).astype(BF16)
    part = ring_gather(part, second, BF16)
    return ring_gather(part, first, F32)


def core_swap(values):
    return lax.ppermute(values, "mp", CORE_SWAP)


def sum_own_rows(own, other):
    pair = (own + core_swap(other).astype(F32)).astype(BF16)
    return pair.astype(F32) + lax.ppermute(pair, "mp", FAR_SWAP).astype(F32)


def both_halves(own):
    return jnp.concatenate([own, core_swap(own)], axis=0)


def norm_forward(values, gain_vec, shift_vec):
    average = jnp.mean(values, axis=-1, keepdims=True)
    centred = values - average
    rscale = lax.rsqrt(jnp.mean(centred * centred, axis=-1, keepdims=True) + EPS_NORM)
    normed = centred * rscale
    return (normed * gain_vec + shift_vec, normed, rscale)


def norm_backward(grad_out, normed, rscale, gain_vec):
    scaled = grad_out * gain_vec
    first_mean = jnp.mean(scaled, axis=-1, keepdims=True)
    cross_mean = jnp.mean(scaled * normed, axis=-1, keepdims=True)
    return rscale * (scaled - first_mean - normed * cross_mean)


def gelu_exact(values):
    return jax.nn.gelu(values, approximate=False)


def dot32(left, right):
    return jnp.dot(left, right, preferred_element_type=F32)


def dot_rows(left, right):
    return lax.dot_general(left, right, (((0,), (0,)), ((), ())), preferred_element_type=F32)


def dot_cols(left, right):
    return lax.dot_general(left, right, (((1,), (1,)), ((), ())), preferred_element_type=F32)


def local(
    tokens,
    lengths,
    pair_index,
    query_proj,
    query_bias,
    key_proj,
    value_proj,
    value_bias,
    output_proj,
    output_bias,
    attn_gain,
    attn_shift,
    inner_proj,
    inner_bias,
    outer_proj,
    outer_bias,
    final_gain,
    final_shift,
):
    row_count, width = tokens.shape
    half = row_count // 2
    seq_count = lengths.shape[0]
    pair_count = seq_count // 2
    overall_pair_count = pair_index.shape[0]
    local_width = query_proj.shape[1]
    head_count = local_width // HD
    scaling = 1.0 / math.sqrt(HD)
    core = lax.axis_index("mp") % 2
    my_index = lax.axis_index("dp")

    def own_first(values):
        return jnp.concatenate(
            [
                lax.dynamic_slice_in_dim(values, core * half, half, 0),
                lax.dynamic_slice_in_dim(values, (1 - core) * half, half, 0),
            ],
            axis=0,
        )

    rows = own_first(tokens)
    seq_ends = jnp.cumsum(lengths)
    position = (jnp.arange(row_count, dtype=jnp.int32) + core * half) % row_count
    segment = jnp.sum((position[:, None] >= seq_ends[None, :]).astype(jnp.int32), axis=1)
    same_seq = segment[:, None] == segment[None, :]
    member = (segment[None, :half] == jnp.arange(seq_count, dtype=jnp.int32)[:, None]).astype(F32)
    own_tokens = rows[:half].astype(F32)
    attn_gain_f = attn_gain.astype(F32)
    final_gain_f = final_gain.astype(F32)

    query_b = (dot32(rows, query_proj) + query_bias.astype(F32)).astype(BF16)
    key_b = dot32(rows, key_proj).astype(BF16)
    value_b = (dot32(rows, value_proj) + value_bias.astype(F32)).astype(BF16)
    query_heads = query_b.reshape(row_count, head_count, HD)
    key_heads = key_b.reshape(row_count, head_count, HD)
    value_heads = value_b.reshape(row_count, head_count, HD)

    def masked_scores():
        raw = (
            jnp.einsum("qhd,khd->hqk", query_heads, key_heads, preferred_element_type=F32) * scaling
        )
        return jnp.where(same_seq[None], raw, NEG_FILL)

    masked = masked_scores()
    row_max = jnp.max(masked, axis=-1, keepdims=True)
    exp_scores = jnp.exp(masked - row_max)
    row_total = jnp.sum(exp_scores, axis=-1, keepdims=True)
    row_lse = row_max + jnp.log(row_total)
    attn_probs = exp_scores / row_total
    mixed_b = (
        jnp.einsum(
            "hqk,khd->qhd", attn_probs.astype(BF16), value_heads, preferred_element_type=F32
        )
        .reshape(row_count, local_width)
        .astype(BF16)
    )
    attn_full = sum_own_rows(
        dot32(mixed_b[:half], output_proj), dot32(mixed_b[half:], output_proj).astype(BF16)
    ) + output_bias.astype(F32)
    hidden_one, normed_one, rscale_one = norm_forward(
        own_tokens + attn_full, attn_gain_f, attn_shift.astype(F32)
    )
    hidden_b = both_halves(hidden_one.astype(BF16))
    up_lin = dot32(hidden_b, inner_proj) + inner_bias.astype(F32)
    act_value, gelu_pull = jax.vjp(gelu_exact, up_lin)
    act_b = act_value.astype(BF16)
    ffn_full = sum_own_rows(
        dot32(act_b[:half], outer_proj), dot32(act_b[half:], outer_proj).astype(BF16)
    ) + outer_bias.astype(F32)
    final_out, normed_two, rscale_two = norm_forward(
        hidden_one + ffn_full, final_gain_f, final_shift.astype(F32)
    )
    pooled_part = jnp.dot(member, final_out, precision=HIGHEST)
    pooled = pooled_part + core_swap(pooled_part)
    pool_rscale = lax.rsqrt(jnp.sum(pooled * pooled, axis=-1, keepdims=True) + EPS_NORM)
    unit_b = (pooled * pool_rscale).astype(BF16)

    piece = lax.dynamic_slice_in_dim(unit_b, core * pair_count, pair_count, 0)
    near = lax.ppermute(piece, "dp", NEAR_SWAP)
    low = (my_index % 2) == 0
    piece = jnp.concatenate([jnp.where(low, piece, near), jnp.where(low, near, piece)], axis=0)
    piece = ring_gather(piece, "y", BF16)
    piece = ring_gather(piece, "z", BF16)
    swapped = core_swap(piece)
    query_units = jnp.where(core == 0, piece, swapped)
    passage_units = jnp.where(core == 0, swapped, piece)

    backward_scale = 1.0 / (overall_pair_count * SOFTMAX_WARMTH)
    similarity = dot_cols(query_units, passage_units) / SOFTMAX_WARMTH
    query_ids = jnp.arange(overall_pair_count, dtype=jnp.int32)
    is_match = (pair_index[None, :] == query_ids[:, None]).astype(F32)
    top = jnp.max(similarity, axis=1, keepdims=True)
    query_lse = top + jnp.log(jnp.sum(jnp.exp(similarity - top), axis=1, keepdims=True))
    loss_value = (
        jnp.sum(query_lse[:, 0] - jnp.sum(similarity * is_match, axis=1)) / overall_pair_count
    )
    coef = (jnp.exp(similarity - query_lse) - is_match) * backward_scale
    own_start = my_index * pair_count
    coef_query = lax.dynamic_slice_in_dim(coef, own_start, pair_count, 0)
    coef_passage = lax.dynamic_slice_in_dim(coef, own_start, pair_count, 1)
    grad_query = jnp.dot(coef_query, passage_units.astype(F32), precision=HIGHEST)
    grad_passage = lax.dot_general(
        coef_passage, query_units.astype(F32), (((0,), (0,)), ((), ())), precision=HIGHEST
    )
    grad_unit = jnp.concatenate([grad_query, grad_passage], axis=0)
    grad_pooled = (
        pool_rscale * grad_unit
        - pool_rscale**3 * jnp.sum(pooled * grad_unit, axis=-1, keepdims=True) * pooled
    )

    grad_final = jnp.einsum("st,sd->td", member, grad_pooled, precision=HIGHEST)
    finalgain_part = jnp.sum(grad_final * normed_two, axis=0)
    finalshift_part = jnp.sum(grad_final, axis=0)
    grad_second = norm_backward(grad_final, normed_two, rscale_two, final_gain_f)
    own_grad_ffn = grad_second.astype(BF16)
    outerbias_part = jnp.sum(own_grad_ffn.astype(F32), axis=0)
    grad_ffn_b = both_halves(own_grad_ffn)
    grad_act = dot_cols(grad_ffn_b, outer_proj)
    grad_up_b = gelu_pull(grad_act)[0].astype(BF16)
    grad_hidden = grad_second + sum_own_rows(
        dot_cols(grad_up_b[:half], inner_proj), dot_cols(grad_up_b[half:], inner_proj).astype(BF16)
    )
    outerproj_grad = sum_over_dp(dot_rows(act_b, grad_ffn_b).astype(BF16), "z", "y")
    innerproj_grad = sum_over_dp(dot_rows(hidden_b, grad_up_b).astype(BF16), "y", "z")
    innerbias_part = jnp.sum(grad_up_b.astype(F32), axis=0)

    attngain_part = jnp.sum(grad_hidden * normed_one, axis=0)
    attnshift_part = jnp.sum(grad_hidden, axis=0)
    grad_first = norm_backward(grad_hidden, normed_one, rscale_one, attn_gain_f)
    own_grad_attn = grad_first.astype(BF16)
    outputbias_part = jnp.sum(own_grad_attn.astype(F32), axis=0)
    grad_attn_b = both_halves(own_grad_attn)
    grad_mixed_b = dot_cols(grad_attn_b, output_proj).astype(BF16)
    grad_mixed_heads = grad_mixed_b.reshape(row_count, head_count, HD)
    probs_again = jnp.exp(masked_scores() - row_lse)
    grad_probs = jnp.einsum(
        "qhd,khd->hqk", grad_mixed_heads, value_heads, preferred_element_type=F32
    )
    row_inner = jnp.sum(probs_again * grad_probs, axis=-1, keepdims=True)
    grad_scores_b = (probs_again * (grad_probs - row_inner)).astype(BF16)
    grad_value_b = (
        jnp.einsum(
            "hqk,qhd->khd", probs_again.astype(BF16), grad_mixed_heads, preferred_element_type=F32
        )
        .astype(BF16)
        .reshape(row_count, local_width)
    )
    grad_query_b = (
        (jnp.einsum("hqk,khd->qhd", grad_scores_b, key_heads, preferred_element_type=F32) * scaling)
        .astype(BF16)
        .reshape(row_count, local_width)
    )
    grad_key_b = (
        (
            jnp.einsum("hqk,qhd->khd", grad_scores_b, query_heads, preferred_element_type=F32)
            * scaling
        )
        .astype(BF16)
        .reshape(row_count, local_width)
    )

    def input_part(span):
        return (
            dot_cols(grad_query_b[span], query_proj)
            + dot_cols(grad_key_b[span], key_proj)
            + dot_cols(grad_value_b[span], value_proj)
        )

    token_own = grad_first + sum_own_rows(
        input_part(slice(0, half)), input_part(slice(half, None)).astype(BF16)
    )
    token_grad = own_first(both_halves(token_own.astype(BF16)))

    paired = jnp.stack(
        [
            outputbias_part,
            attngain_part,
            attnshift_part,
            outerbias_part,
            finalgain_part,
            finalshift_part,
        ],
        axis=0,
    )
    paired = paired + core_swap(paired)
    querybias_part = jnp.sum(grad_query_b.astype(F32), axis=0)
    valuebias_part = jnp.sum(grad_value_b.astype(F32), axis=0)
    blank = jnp.zeros((width - 2 * local_width,), F32)
    vectors = jnp.concatenate(
        [
            paired,
            innerbias_part[None],
            jnp.concatenate([querybias_part, valuebias_part, blank])[None],
            jnp.zeros((120, width), F32),
        ],
        axis=0,
    )
    packed = jnp.concatenate(
        [
            dot_rows(grad_query_b, rows).astype(BF16),
            dot_rows(grad_key_b, rows).astype(BF16),
            dot_rows(grad_value_b, rows).astype(BF16),
            dot_rows(mixed_b, grad_attn_b).astype(BF16),
            vectors.astype(BF16),
        ],
        axis=0,
    )
    packed = sum_over_dp(packed, "z", "y")
    cuts = [packed[i * local_width : (i + 1) * local_width] for i in range(4)]
    vectors = packed[4 * local_width :]
    return (
        loss_value,
        token_grad,
        cuts[0].T,
        vectors[7, :local_width],
        cuts[1].T,
        cuts[2].T,
        vectors[7, local_width : 2 * local_width],
        cuts[3],
        vectors[0],
        vectors[1],
        vectors[2],
        innerproj_grad,
        vectors[6],
        outerproj_grad,
        vectors[3],
        vectors[4],
        vectors[5],
    )


def solution(mesh):
    column, row, split = P(None, "mp"), P("mp", None), P("mp")
    placed = (
        (P("dp", None), P("dp"), P())
        + (column, split, column, column, split, row)
        + (P(), P(), P())
        + (column, split, row)
        + (P(), P(), P())
    )
    given = (
        (P(), P("dp", None))
        + (column, split, column, column, split, row)
        + (P(), P(), P())
        + (column, split, row)
        + (P(), P(), P())
    )
    return jax.shard_map(local, mesh=mesh, in_specs=placed, out_specs=given, check_vma=False)
```

```python
import math

import jax
import jax.numpy as jnp
from jax import lax
from jax.sharding import PartitionSpec as P

HD = 64
EPS_NORM = 1e-06
SOFTMAX_WARMTH = 0.01
NEG_FILL = -1e30
HIGHEST = lax.Precision.HIGHEST
F32 = jnp.float32
BF16 = jnp.bfloat16

CORE_SWAP = [(i, i ^ 1) for i in range(4)]
FAR_SWAP = [(i, i ^ 2) for i in range(4)]


def trade(values):
    return lax.all_to_all(values, "dp", split_axis=0, concat_axis=0, tiled=True)


def share(values):
    spread = jnp.broadcast_to(values[None], (32,) + values.shape)
    return trade(spread.reshape((-1,) + values.shape[1:]))


def sum_over_dp(values):
    parts = trade(values).reshape((32, -1) + values.shape[1:])
    return share(jnp.sum(parts.astype(F32), axis=0).astype(BF16))


def core_swap(values):
    return lax.ppermute(values, "mp", CORE_SWAP)


def sum_own_rows(own, other):
    pair = (own + core_swap(other).astype(F32)).astype(BF16)
    return pair.astype(F32) + lax.ppermute(pair, "mp", FAR_SWAP).astype(F32)


def both_halves(own):
    return jnp.concatenate([own, core_swap(own)], axis=0)


def norm_forward(values, gain_vec, shift_vec):
    average = jnp.mean(values, axis=-1, keepdims=True)
    centred = values - average
    rscale = lax.rsqrt(jnp.mean(centred * centred, axis=-1, keepdims=True) + EPS_NORM)
    normed = centred * rscale
    return (normed * gain_vec + shift_vec, normed, rscale)


def norm_backward(grad_out, normed, rscale, gain_vec):
    scaled = grad_out * gain_vec
    first_mean = jnp.mean(scaled, axis=-1, keepdims=True)
    cross_mean = jnp.mean(scaled * normed, axis=-1, keepdims=True)
    return rscale * (scaled - first_mean - normed * cross_mean)


def gelu_exact(values):
    return jax.nn.gelu(values, approximate=False)


def dot32(left, right):
    return jnp.dot(left, right, preferred_element_type=F32)


def dot_rows(left, right):
    return lax.dot_general(left, right, (((0,), (0,)), ((), ())), preferred_element_type=F32)


def dot_cols(left, right):
    return lax.dot_general(left, right, (((1,), (1,)), ((), ())), preferred_element_type=F32)


def local(
    tokens,
    lengths,
    pair_index,
    query_proj,
    query_bias,
    key_proj,
    value_proj,
    value_bias,
    output_proj,
    output_bias,
    attn_gain,
    attn_shift,
    inner_proj,
    inner_bias,
    outer_proj,
    outer_bias,
    final_gain,
    final_shift,
):
    row_count, width = tokens.shape
    half = row_count // 2
    seq_count = lengths.shape[0]
    pair_count = seq_count // 2
    overall_pair_count = pair_index.shape[0]
    local_width = query_proj.shape[1]
    head_count = local_width // HD
    scaling = 1.0 / math.sqrt(HD)
    core = lax.axis_index("mp") % 2
    my_index = lax.axis_index("dp")

    def own_first(values):
        return jnp.concatenate(
            [
                lax.dynamic_slice_in_dim(values, core * half, half, 0),
                lax.dynamic_slice_in_dim(values, (1 - core) * half, half, 0),
            ],
            axis=0,
        )

    rows = own_first(tokens)
    seq_ends = jnp.cumsum(lengths)
    position = (jnp.arange(row_count, dtype=jnp.int32) + core * half) % row_count
    segment = jnp.sum((position[:, None] >= seq_ends[None, :]).astype(jnp.int32), axis=1)
    same_seq = segment[:, None] == segment[None, :]
    member = (segment[None, :half] == jnp.arange(seq_count, dtype=jnp.int32)[:, None]).astype(F32)
    own_tokens = rows[:half].astype(F32)
    attn_gain_f = attn_gain.astype(F32)
    final_gain_f = final_gain.astype(F32)

    query_b = (dot32(rows, query_proj) + query_bias.astype(F32)).astype(BF16)
    key_b = dot32(rows, key_proj).astype(BF16)
    value_b = (dot32(rows, value_proj) + value_bias.astype(F32)).astype(BF16)
    query_heads = query_b.reshape(row_count, head_count, HD)
    key_heads = key_b.reshape(row_count, head_count, HD)
    value_heads = value_b.reshape(row_count, head_count, HD)

    def masked_scores():
        raw = (
            jnp.einsum("qhd,khd->hqk", query_heads, key_heads, preferred_element_type=F32) * scaling
        )
        return jnp.where(same_seq[None], raw, NEG_FILL)

    masked = masked_scores()
    row_max = jnp.max(masked, axis=-1, keepdims=True)
    exp_scores = jnp.exp(masked - row_max)
    row_total = jnp.sum(exp_scores, axis=-1, keepdims=True)
    row_lse = row_max + jnp.log(row_total)
    attn_probs = exp_scores / row_total
    mixed_b = (
        jnp.einsum(
            "hqk,khd->qhd", attn_probs.astype(BF16), value_heads, preferred_element_type=F32
        )
        .reshape(row_count, local_width)
        .astype(BF16)
    )
    attn_full = sum_own_rows(
        dot32(mixed_b[:half], output_proj), dot32(mixed_b[half:], output_proj).astype(BF16)
    ) + output_bias.astype(F32)
    hidden_one, normed_one, rscale_one = norm_forward(
        own_tokens + attn_full, attn_gain_f, attn_shift.astype(F32)
    )
    hidden_b = both_halves(hidden_one.astype(BF16))
    up_lin = dot32(hidden_b, inner_proj) + inner_bias.astype(F32)
    act_value, gelu_pull = jax.vjp(gelu_exact, up_lin)
    act_b = act_value.astype(BF16)
    ffn_full = sum_own_rows(
        dot32(act_b[:half], outer_proj), dot32(act_b[half:], outer_proj).astype(BF16)
    ) + outer_bias.astype(F32)
    final_out, normed_two, rscale_two = norm_forward(
        hidden_one + ffn_full, final_gain_f, final_shift.astype(F32)
    )
    pooled_part = jnp.dot(member, final_out, precision=HIGHEST)
    pooled = pooled_part + core_swap(pooled_part)
    pool_rscale = lax.rsqrt(jnp.sum(pooled * pooled, axis=-1, keepdims=True) + EPS_NORM)
    unit_b = (pooled * pool_rscale).astype(BF16)

    piece = lax.dynamic_slice_in_dim(unit_b, core * pair_count, pair_count, 0)
    piece = share(piece)
    swapped = core_swap(piece)
    query_units = jnp.where(core == 0, piece, swapped)
    passage_units = jnp.where(core == 0, swapped, piece)

    backward_scale = 1.0 / (overall_pair_count * SOFTMAX_WARMTH)
    similarity = dot_cols(query_units, passage_units) / SOFTMAX_WARMTH
    query_ids = jnp.arange(overall_pair_count, dtype=jnp.int32)
    is_match = (pair_index[None, :] == query_ids[:, None]).astype(F32)
    top = jnp.max(similarity, axis=1, keepdims=True)
    query_lse = top + jnp.log(jnp.sum(jnp.exp(similarity - top), axis=1, keepdims=True))
    loss_value = (
        jnp.sum(query_lse[:, 0] - jnp.sum(similarity * is_match, axis=1)) / overall_pair_count
    )
    coef = (jnp.exp(similarity - query_lse) - is_match) * backward_scale
    own_start = my_index * pair_count
    coef_query = lax.dynamic_slice_in_dim(coef, own_start, pair_count, 0)
    coef_passage = lax.dynamic_slice_in_dim(coef, own_start, pair_count, 1)
    grad_query = jnp.dot(coef_query, passage_units.astype(F32), precision=HIGHEST)
    grad_passage = lax.dot_general(
        coef_passage, query_units.astype(F32), (((0,), (0,)), ((), ())), precision=HIGHEST
    )
    grad_unit = jnp.concatenate([grad_query, grad_passage], axis=0)
    grad_pooled = (
        pool_rscale * grad_unit
        - pool_rscale**3 * jnp.sum(pooled * grad_unit, axis=-1, keepdims=True) * pooled
    )

    grad_final = jnp.einsum("st,sd->td", member, grad_pooled, precision=HIGHEST)
    finalgain_part = jnp.sum(grad_final * normed_two, axis=0)
    finalshift_part = jnp.sum(grad_final, axis=0)
    grad_second = norm_backward(grad_final, normed_two, rscale_two, final_gain_f)
    own_grad_ffn = grad_second.astype(BF16)
    outerbias_part = jnp.sum(own_grad_ffn.astype(F32), axis=0)
    grad_ffn_b = both_halves(own_grad_ffn)
    grad_act = dot_cols(grad_ffn_b, outer_proj)
    grad_up_b = gelu_pull(grad_act)[0].astype(BF16)
    grad_hidden = grad_second + sum_own_rows(
        dot_cols(grad_up_b[:half], inner_proj), dot_cols(grad_up_b[half:], inner_proj).astype(BF16)
    )
    ffn_pack = jnp.concatenate(
        [dot_rows(act_b, grad_ffn_b).astype(BF16), dot_rows(hidden_b, grad_up_b).astype(BF16)],
        axis=0,
    )
    ffn_pack = sum_over_dp(ffn_pack).astype(F32)
    outerproj_grad = ffn_pack[:width]
    innerproj_grad = ffn_pack[width:]
    innerbias_part = jnp.sum(grad_up_b.astype(F32), axis=0)

    attngain_part = jnp.sum(grad_hidden * normed_one, axis=0)
    attnshift_part = jnp.sum(grad_hidden, axis=0)
    grad_first = norm_backward(grad_hidden, normed_one, rscale_one, attn_gain_f)
    own_grad_attn = grad_first.astype(BF16)
    outputbias_part = jnp.sum(own_grad_attn.astype(F32), axis=0)
    grad_attn_b = both_halves(own_grad_attn)
    grad_mixed_b = dot_cols(grad_attn_b, output_proj).astype(BF16)
    grad_mixed_heads = grad_mixed_b.reshape(row_count, head_count, HD)
    probs_again = jnp.exp(masked_scores() - row_lse)
    grad_probs = jnp.einsum(
        "qhd,khd->hqk", grad_mixed_heads, value_heads, preferred_element_type=F32
    )
    row_inner = jnp.sum(probs_again * grad_probs, axis=-1, keepdims=True)
    grad_scores_b = (probs_again * (grad_probs - row_inner)).astype(BF16)
    grad_value_b = (
        jnp.einsum(
            "hqk,qhd->khd", probs_again.astype(BF16), grad_mixed_heads, preferred_element_type=F32
        )
        .astype(BF16)
        .reshape(row_count, local_width)
    )
    grad_query_b = (
        (jnp.einsum("hqk,khd->qhd", grad_scores_b, key_heads, preferred_element_type=F32) * scaling)
        .astype(BF16)
        .reshape(row_count, local_width)
    )
    grad_key_b = (
        (
            jnp.einsum("hqk,qhd->khd", grad_scores_b, query_heads, preferred_element_type=F32)
            * scaling
        )
        .astype(BF16)
        .reshape(row_count, local_width)
    )

    def input_part(span):
        return (
            dot_cols(grad_query_b[span], query_proj)
            + dot_cols(grad_key_b[span], key_proj)
            + dot_cols(grad_value_b[span], value_proj)
        )

    token_own = grad_first + sum_own_rows(
        input_part(slice(0, half)), input_part(slice(half, None)).astype(BF16)
    )
    token_grad = own_first(both_halves(token_own.astype(BF16)))

    paired = jnp.stack(
        [
            outputbias_part,
            attngain_part,
            attnshift_part,
            outerbias_part,
            finalgain_part,
            finalshift_part,
        ],
        axis=0,
    )
    paired = paired + core_swap(paired)
    querybias_part = jnp.sum(grad_query_b.astype(F32), axis=0)
    valuebias_part = jnp.sum(grad_value_b.astype(F32), axis=0)
    blank = jnp.zeros((width - 2 * local_width,), F32)
    vectors = jnp.concatenate(
        [
            paired,
            innerbias_part[None],
            jnp.concatenate([querybias_part, valuebias_part, blank])[None],
        ],
        axis=0,
    )
    vectors = jnp.pad(vectors.T, ((0, 0), (0, 128 - vectors.shape[0])))
    packed = jnp.concatenate(
        [
            dot_rows(grad_query_b, rows).astype(BF16),
            dot_rows(grad_key_b, rows).astype(BF16),
            dot_rows(grad_value_b, rows).astype(BF16),
            dot_rows(mixed_b, grad_attn_b).astype(BF16),
        ],
        axis=0,
    )
    packed = jnp.concatenate([packed, vectors.astype(BF16)], axis=1)
    packed = sum_over_dp(packed).astype(F32)
    cuts = [packed[i * local_width : (i + 1) * local_width, :width] for i in range(4)]
    vectors = packed[:, width:].T
    return (
        loss_value,
        token_grad,
        cuts[0].T,
        vectors[7, :local_width],
        cuts[1].T,
        cuts[2].T,
        vectors[7, local_width : 2 * local_width],
        cuts[3],
        vectors[0],
        vectors[1],
        vectors[2],
        innerproj_grad,
        vectors[6],
        outerproj_grad,
        vectors[3],
        vectors[4],
        vectors[5],
    )


def solution(mesh):
    column, row, split = P(None, "mp"), P("mp", None), P("mp")
    placed = (
        (P("dp", None), P("dp"), P())
        + (column, split, column, column, split, row)
        + (P(), P(), P())
        + (column, split, row)
        + (P(), P(), P())
    )
    given = (
        (P(), P("dp", None))
        + (column, split, column, column, split, row)
        + (P(), P(), P())
        + (column, split, row)
        + (P(), P(), P())
    )
    return jax.shard_map(local, mesh=mesh, in_specs=placed, out_specs=given, check_vma=False)
```

```python
import functools
import math

import jax
import jax.numpy as jnp
from jax import lax
from jax.experimental import pallas as pl
from jax.experimental.pallas import tpu as pltpu
from jax.sharding import PartitionSpec as P

HD = 64
EPS_NORM = 1e-06
SOFTMAX_WARMTH = 0.01
NEG_FILL = -1e30
HIGHEST = lax.Precision.HIGHEST
F32 = jnp.float32
BF16 = jnp.bfloat16
QB = 256
KB = 128

CORE_SWAP = [(i, i ^ 1) for i in range(4)]
FAR_SWAP = [(i, i ^ 2) for i in range(4)]

SMEM = pl.BlockSpec(memory_space=pltpu.SMEM)
VMEM = pl.BlockSpec(memory_space=pltpu.VMEM)


def nn(left, right):
    return lax.dot_general(left, right, (((1,), (0,)), ((), ())), preferred_element_type=F32)


def nt(left, right):
    return lax.dot_general(left, right, (((1,), (1,)), ((), ())), preferred_element_type=F32)


def tn(left, right):
    return lax.dot_general(left, right, (((0,), (0,)), ((), ())), preferred_element_type=F32)


def place_of_block(block, core, rows):
    return ((block % 2) * 2 + block // 2) * QB + core * (rows // 2) & (rows - 1)


def spot_of_keys(j, core, rows):
    place = (j * KB + core * (rows // 2)) & (rows - 1)
    block = place // QB
    return pl.multiple_of(((block % 2) * 2 + block // 2) * QB + place % QB, KB)


def segment_bounds(lengths_ref):
    bounds, total = [], jnp.int32(0)
    for s in range(lengths_ref.shape[0]):
        start = total
        total = total + lengths_ref[s]
        bounds.append((start, total))
    return bounds


def block_span(bounds, first, rows):
    place = first + lax.broadcasted_iota(jnp.int32, (1, QB), 1)
    low, high = first, first + KB
    begin = jnp.full((1, QB), bounds[-1][1], jnp.int32)
    end = jnp.full((1, QB), rows, jnp.int32)
    for start, stop in bounds:
        inside = (place >= start) & (place < stop)
        begin = jnp.where(inside, start, begin)
        end = jnp.where(inside, stop, end)
        touches = (stop > first) & (start < first + QB) & (stop > start)
        low = jnp.where(touches, jnp.minimum(low, start), low)
        high = jnp.where(touches, jnp.maximum(high, stop), high)
    return low // KB, (high + KB - 1) // KB, begin, end


def head_copies(values, heads):
    lane = lax.broadcasted_iota(jnp.int32, values.shape, 1) // HD
    blank = jnp.zeros_like(values)
    return jnp.concatenate([jnp.where(lane == h, values, blank) for h in range(heads)], axis=0)


def span_mask(begin, end, block, heads):
    place = block * KB + lax.broadcasted_iota(jnp.int32, (KB, QB), 0)
    keep = (place >= begin) & (place < end)
    return jnp.concatenate([keep] * heads, axis=1)


def attend(heads, blocks, core, bounds, q_ref, k_ref, vt_ref, mixed_ref, lse_ref, acc_ref):
    rows = k_ref.shape[0]
    for i, block in enumerate(blocks):
        low, high, begin, end = block_span(bounds, place_of_block(block, core, rows), rows)
        stack = head_copies(q_ref[block * QB : (block + 1) * QB, :], heads)
        acc_ref[...] = jnp.zeros(acc_ref.shape, F32)

        def step(j, carry, stack=stack, begin=begin, end=end):
            top, total = carry
            spot = spot_of_keys(j, core, rows)
            scores = nt(k_ref[pl.ds(spot, KB), :], stack)
            scores = jnp.where(span_mask(begin, end, j, heads), scores, NEG_FILL)
            peak = jnp.maximum(top, jnp.max(scores, axis=0, keepdims=True))
            fade = jnp.exp(top - peak)
            probs = jnp.exp(scores - peak)
            total = total * fade + jnp.sum(probs, axis=0, keepdims=True)
            probs = probs.astype(BF16)
            for h in range(heads):
                part = slice(h * QB, (h + 1) * QB)
                span = slice(h * HD, (h + 1) * HD)
                acc_ref[span, :] = acc_ref[span, :] * fade[:, part] + nn(
                    vt_ref[span, pl.ds(spot, KB)], probs[:, part]
                )
            return peak, total

        top = jnp.full((1, heads * QB), NEG_FILL, F32)
        top, total = lax.fori_loop(
            low, high, step, (top, jnp.zeros((1, heads * QB), F32)), unroll=False
        )
        scale = 1.0 / total
        mixed = jnp.concatenate(
            [
                acc_ref[h * HD : (h + 1) * HD, :] * scale[:, h * QB : (h + 1) * QB]
                for h in range(heads)
            ],
            axis=0,
        )
        mixed_ref[i * QB : (i + 1) * QB, :] = mixed.T.astype(BF16)
        lse_ref[i, :, :] = jnp.broadcast_to(top + jnp.log(total), (8, heads * QB))


def attend_first(
    heads,
    blocks,
    lengths_ref,
    core_ref,
    tokens_ref,
    wqt_ref,
    bq_ref,
    wkt_ref,
    wvt_ref,
    bv_ref,
    bvt_ref,
    x_ref,
    q_ref,
    k_ref,
    v_ref,
    kt_ref,
    vt_ref,
    mixed_ref,
    lse_ref,
    acc_ref,
):
    rows = tokens_ref.shape[0]
    core = core_ref[0]
    for block in range(rows // QB):
        part = slice(block * QB, (block + 1) * QB)
        first = pl.multiple_of(place_of_block(block, core, rows), QB)
        x = tokens_ref[pl.ds(first, QB), :]
        x_ref[part, :] = x
        q = (nt(x, wqt_ref[...]) + bq_ref[...].astype(F32)).astype(BF16)
        q_ref[part, :] = q * BF16(0.125)
        k_ref[part, :] = nt(x, wkt_ref[...]).astype(BF16)
        kt_ref[:, part] = nt(wkt_ref[...], x).astype(BF16)
        v_ref[part, :] = (nt(x, wvt_ref[...]) + bv_ref[...].astype(F32)).astype(BF16)
        vt_ref[:, part] = (nt(wvt_ref[...], x) + bvt_ref[...].astype(F32)).astype(BF16)
    bounds = segment_bounds(lengths_ref)
    attend(heads, blocks, core, bounds, q_ref, k_ref, vt_ref, mixed_ref, lse_ref, acc_ref)


def attend_more(
    heads, blocks, lengths_ref, core_ref, q_ref, k_ref, vt_ref, mixed_ref, lse_ref, acc_ref
):
    bounds = segment_bounds(lengths_ref)
    attend(heads, blocks, core_ref[0], bounds, q_ref, k_ref, vt_ref, mixed_ref, lse_ref, acc_ref)


def attend_back(
    heads,
    blocks,
    lengths_ref,
    core_ref,
    grad_ref,
    wo_ref,
    mixed_ref,
    q_ref,
    k_ref,
    v_ref,
    kt_ref,
    lse_ref,
    dk_in_ref,
    dv_in_ref,
    dq_ref,
    dk_ref,
    dv_ref,
    dqt_ref,
):
    rows, width = q_ref.shape
    core = core_ref[0]
    bounds = segment_bounds(lengths_ref)
    dk_ref[...] = dk_in_ref[...]
    dv_ref[...] = dv_in_ref[...]
    lane = lax.broadcasted_iota(jnp.int32, (8, width), 1) // HD
    which = (lane == lax.broadcasted_iota(jnp.int32, (8, width), 0)).astype(F32)
    for i, block in enumerate(blocks):
        low, high, begin, end = block_span(bounds, place_of_block(block, core, rows), rows)
        part = slice(i * QB, (i + 1) * QB)
        grad_mixed = nt(grad_ref[part, :], wo_ref[...]).astype(BF16)
        product = grad_mixed.astype(F32) * mixed_ref[part, :].astype(F32)
        sums = lax.dot_general(
            which,
            product,
            (((1,), (1,)), ((), ())),
            precision=HIGHEST,
            preferred_element_type=F32,
        )
        delta = jnp.concatenate([sums[h : h + 1, :] for h in range(heads)], axis=1)
        lse = lse_ref[i, 0:1, :]
        q_stack = head_copies(q_ref[block * QB : (block + 1) * QB, :], heads)
        g_stack = head_copies(grad_mixed, heads)
        dqt_ref[...] = jnp.zeros(dqt_ref.shape, F32)

        def step(
            j, carry, delta=delta, lse=lse, q_stack=q_stack, g_stack=g_stack, begin=begin, end=end
        ):
            here = pl.ds(spot_of_keys(j, core, rows), KB)
            scores = nt(k_ref[here, :], q_stack)
            scores = jnp.where(span_mask(begin, end, j, heads), scores, NEG_FILL)
            probs = jnp.exp(scores - lse)
            grad = (probs * (nt(v_ref[here, :], g_stack) - delta)).astype(BF16)
            dv_ref[here, :] += nn(probs.astype(BF16), g_stack)
            dk_ref[here, :] += nn(grad, q_stack)
            for h in range(heads):
                span = slice(h * HD, (h + 1) * HD)
                dqt_ref[span, :] += nn(kt_ref[span, here], grad[:, h * QB : (h + 1) * QB])
            return carry

        lax.fori_loop(low, high, step, 0, unroll=False)
        dq_ref[part, :] = (dqt_ref[...].T * 0.125).astype(BF16)


def shaped(shape, dtype):
    return jax.ShapeDtypeStruct(shape, dtype)


PARAMS = pltpu.CompilerParams(vmem_limit_bytes=40 << 20)


def run_first(lengths, core, tokens, wqt, bq, wkt, wvt, bv, blocks):
    rows, width = tokens.shape[0], wqt.shape[0]
    heads, count = width // HD, len(blocks)
    return pl.pallas_call(
        functools.partial(attend_first, heads, blocks),
        out_shape=(shaped(tokens.shape, BF16),)
        + (shaped((rows, width), BF16),) * 3
        + (shaped((width, rows), BF16),) * 2
        + (shaped((count * QB, width), BF16), shaped((count, 8, heads * QB), F32)),
        in_specs=[SMEM] * 2 + [VMEM] * 7,
        out_specs=(VMEM,) * 8,
        scratch_shapes=[pltpu.VMEM((width, QB), F32)],
        compiler_params=PARAMS,
        name="attend_first",
        cost_estimate=pl.CostEstimate(
            flops=2_000_000_000, bytes_accessed=8_000_000, transcendentals=1_000_000
        ),
    )(lengths, core, tokens, wqt, bq.reshape(1, -1), wkt, wvt, bv.reshape(1, -1), bv.reshape(-1, 1))


def run_more(lengths, core, q, k, vt, blocks):
    rows, width = q.shape
    heads, count = width // HD, len(blocks)
    return pl.pallas_call(
        functools.partial(attend_more, heads, blocks),
        out_shape=(shaped((count * QB, width), BF16), shaped((count, 8, heads * QB), F32)),
        in_specs=[SMEM] * 2 + [VMEM] * 3,
        out_specs=(VMEM,) * 2,
        scratch_shapes=[pltpu.VMEM((width, QB), F32)],
        compiler_params=PARAMS,
        name="attend_more",
        cost_estimate=pl.CostEstimate(
            flops=1_000_000_000, bytes_accessed=8_000_000, transcendentals=1_000_000
        ),
    )(lengths, core, q, k, vt)


def run_back(lengths, core, grad, wo, mixed, q, k, v, kt, lse, dk, dv, blocks):
    rows, width = q.shape
    heads, count = width // HD, len(blocks)
    return pl.pallas_call(
        functools.partial(attend_back, heads, blocks),
        out_shape=(shaped((count * QB, width), BF16),) + (shaped((rows, width), F32),) * 2,
        in_specs=[SMEM] * 2 + [VMEM] * 10,
        out_specs=(VMEM,) * 3,
        scratch_shapes=[pltpu.VMEM((width, QB), F32)],
        compiler_params=PARAMS,
        name="attend_back",
        cost_estimate=pl.CostEstimate(
            flops=3_000_000_000, bytes_accessed=12_000_000, transcendentals=1_000_000
        ),
    )(lengths, core, grad, wo, mixed, q, k, v, kt, lse, dk, dv)


def trade(values):
    return lax.all_to_all(values, "dp", split_axis=0, concat_axis=0, tiled=True)


def share(values):
    spread = jnp.broadcast_to(values[None], (32,) + values.shape)
    return trade(spread.reshape((-1,) + values.shape[1:]))


def sum_parts(parts):
    parts = parts.reshape((32, -1) + parts.shape[1:])
    return jnp.sum(parts.astype(F32), axis=0).astype(BF16)


def core_swap(values):
    return lax.ppermute(values, "mp", CORE_SWAP)


def far_swap(values):
    return lax.ppermute(values, "mp", FAR_SWAP)


def pair_sum(own, other):
    return (own + core_swap(other.astype(BF16)).astype(F32)).astype(BF16)


def far_sum(pair):
    return pair.astype(F32) + far_swap(pair).astype(F32)


def both(own):
    return jnp.concatenate([own, core_swap(own)], axis=0)


def norm_forward(values, gain_vec, shift_vec):
    average = jnp.mean(values, axis=-1, keepdims=True)
    centred = values - average
    rscale = lax.rsqrt(jnp.mean(centred * centred, axis=-1, keepdims=True) + EPS_NORM)
    normed = centred * rscale
    return (normed * gain_vec + shift_vec, normed, rscale)


def norm_backward(grad_out, normed, rscale, gain_vec):
    scaled = grad_out * gain_vec
    first_mean = jnp.mean(scaled, axis=-1, keepdims=True)
    cross_mean = jnp.mean(scaled * normed, axis=-1, keepdims=True)
    return rscale * (scaled - first_mean - normed * cross_mean)


def gelu_and_slope(upper):
    below = 0.5 * (1.0 + lax.erf(upper * math.sqrt(0.5)))
    density = jnp.exp(-0.5 * upper * upper) * (1.0 / math.sqrt(2.0 * math.pi))
    return (upper * below).astype(BF16), (below + upper * density).astype(BF16)


def local(
    tokens,
    lengths,
    pair_index,
    query_proj,
    query_bias,
    key_proj,
    value_proj,
    value_bias,
    output_proj,
    output_bias,
    attn_gain,
    attn_shift,
    inner_proj,
    inner_bias,
    outer_proj,
    outer_bias,
    final_gain,
    final_shift,
):
    row_count, width = tokens.shape
    chunk = row_count // 2
    half = chunk // 2
    seq_count = lengths.shape[0]
    pair_count = seq_count // 2
    overall_pair_count = pair_index.shape[0]
    local_width = query_proj.shape[1]
    core = lax.axis_index("mp") % 2
    my_index = lax.axis_index("dp")
    core_arg = jnp.reshape(core, (1,)).astype(jnp.int32)
    attn_gain_f, attn_shift_f = attn_gain.astype(F32), attn_shift.astype(F32)
    final_gain_f, final_shift_f = final_gain.astype(F32), final_shift.astype(F32)
    query_t, key_t, value_t = query_proj.T, key_proj.T, value_proj.T
    chunk_blocks = ((0, 1), (2, 3))

    seq_ends = jnp.cumsum(lengths)
    seq_starts = seq_ends - lengths
    members = []
    for index in range(2):
        place = jnp.arange(half, dtype=jnp.int32) + index * half + core * chunk
        members.append(
            ((place[None] >= seq_starts[:, None]) & (place[None] < seq_ends[:, None])).astype(F32)
        )

    rows, query_b, key_b, value_b, key_tb, value_tb, mixed_one, lse_one = run_first(
        lengths, core_arg, tokens, query_t, query_bias, key_t, value_t, value_bias, chunk_blocks[0]
    )
    mixed_two, lse_two = run_more(lengths, core_arg, query_b, key_b, value_tb, chunk_blocks[1])
    mixed, lse = (mixed_one, mixed_two), (lse_one, lse_two)

    def part(values, index):
        return values[index * chunk : (index + 1) * chunk]

    hidden_f, hidden_b, normed_one, rscale_one, act_b, slope_b, ffn_pair = [], [], [], [], [], [], []
    attn_pair = [
        pair_sum(nn(mixed[i][:half], output_proj), nn(mixed[i][half:], output_proj))
        for i in range(2)
    ]
    for i in range(2):
        attn_full = far_sum(attn_pair[i]) + output_bias.astype(F32)
        own_tokens = part(rows, i)[:half].astype(F32)
        hidden, normed, rscale = norm_forward(own_tokens + attn_full, attn_gain_f, attn_shift_f)
        hidden_f.append(hidden)
        normed_one.append(normed)
        rscale_one.append(rscale)
        hidden_b.append(both(hidden.astype(BF16)))
        act, slope = gelu_and_slope(nn(hidden_b[i], inner_proj) + inner_bias.astype(F32))
        act_b.append(act)
        slope_b.append(slope)
        ffn_pair.append(pair_sum(nn(act[:half], outer_proj), nn(act[half:], outer_proj)))
    normed_two, rscale_two, pooled_part = [], [], 0.0
    for i in range(2):
        ffn_full = far_sum(ffn_pair[i]) + outer_bias.astype(F32)
        final_out, normed, rscale = norm_forward(
            hidden_f[i] + ffn_full, final_gain_f, final_shift_f
        )
        normed_two.append(normed)
        rscale_two.append(rscale)
        pooled_part = pooled_part + jnp.dot(members[i], final_out, precision=HIGHEST)
    pooled = pooled_part + core_swap(pooled_part)
    pool_rscale = lax.rsqrt(jnp.sum(pooled * pooled, axis=-1, keepdims=True) + EPS_NORM)
    unit_b = (pooled * pool_rscale).astype(BF16)

    piece = share(lax.dynamic_slice_in_dim(unit_b, core * pair_count, pair_count, 0))
    swapped = core_swap(piece)
    query_units = jnp.where(core == 0, piece, swapped)
    passage_units = jnp.where(core == 0, swapped, piece)

    backward_scale = 1.0 / (overall_pair_count * SOFTMAX_WARMTH)
    similarity = nt(query_units, passage_units) / SOFTMAX_WARMTH
    query_ids = jnp.arange(overall_pair_count, dtype=jnp.int32)
    is_match = (pair_index[None, :] == query_ids[:, None]).astype(F32)
    top = jnp.max(similarity, axis=1, keepdims=True)
    query_lse = top + jnp.log(jnp.sum(jnp.exp(similarity - top), axis=1, keepdims=True))
    loss_value = (
        jnp.sum(query_lse[:, 0] - jnp.sum(similarity * is_match, axis=1)) / overall_pair_count
    )
    coef = (jnp.exp(similarity - query_lse) - is_match) * backward_scale
    own_start = my_index * pair_count
    coef_query = lax.dynamic_slice_in_dim(coef, own_start, pair_count, 0)
    coef_passage = lax.dynamic_slice_in_dim(coef, own_start, pair_count, 1)
    grad_query = jnp.dot(coef_query, passage_units.astype(F32), precision=HIGHEST)
    grad_passage = lax.dot_general(
        coef_passage, query_units.astype(F32), (((0,), (0,)), ((), ())), precision=HIGHEST
    )
    grad_unit = jnp.concatenate([grad_query, grad_passage], axis=0)
    grad_pooled = (
        pool_rscale * grad_unit
        - pool_rscale**3 * jnp.sum(pooled * grad_unit, axis=-1, keepdims=True) * pooled
    )

    finalgain_part = finalshift_part = outerbias_part = innerbias_part = 0.0
    grad_second, grad_ffn_b, grad_up_b, hidden_pair = [], [], [], []
    for i in range(2):
        grad_final = jnp.einsum("st,sd->td", members[i], grad_pooled, precision=HIGHEST)
        finalgain_part += jnp.sum(grad_final * normed_two[i], axis=0)
        finalshift_part += jnp.sum(grad_final, axis=0)
        grad_second.append(norm_backward(grad_final, normed_two[i], rscale_two[i], final_gain_f))
        own_grad = grad_second[i].astype(BF16)
        outerbias_part += jnp.sum(own_grad.astype(F32), axis=0)
        grad_ffn_b.append(both(own_grad))
        grad_up = (nt(grad_ffn_b[i], outer_proj) * slope_b[i].astype(F32)).astype(BF16)
        innerbias_part += jnp.sum(grad_up.astype(F32), axis=0)
        grad_up_b.append(grad_up)
        hidden_pair.append(pair_sum(nt(grad_up[:half], inner_proj), nt(grad_up[half:], inner_proj)))
    ffn_pack = jnp.concatenate(
        [
            (tn(act_b[0], grad_ffn_b[0]) + tn(act_b[1], grad_ffn_b[1])).astype(BF16),
            (tn(hidden_b[0], grad_up_b[0]) + tn(hidden_b[1], grad_up_b[1])).astype(BF16),
        ],
        axis=0,
    )
    ffn_parts = trade(ffn_pack)

    attngain_part = attnshift_part = outputbias_part = 0.0
    grad_first, grad_attn_b = [], []
    for i in range(2):
        grad_hidden = grad_second[i] + far_sum(hidden_pair[i])
        attngain_part += jnp.sum(grad_hidden * normed_one[i], axis=0)
        attnshift_part += jnp.sum(grad_hidden, axis=0)
        grad_first.append(norm_backward(grad_hidden, normed_one[i], rscale_one[i], attn_gain_f))
        own_grad = grad_first[i].astype(BF16)
        outputbias_part += jnp.sum(own_grad.astype(F32), axis=0)
        grad_attn_b.append(both(own_grad))
    blank = jnp.zeros((row_count, local_width), F32)
    grad_query_one, key_acc, value_acc = run_back(
        lengths,
        core_arg,
        grad_attn_b[0],
        output_proj,
        mixed[0],
        query_b,
        key_b,
        value_b,
        key_tb,
        lse[0],
        blank,
        blank,
        chunk_blocks[0],
    )
    second_grad, ffn_parts = lax.optimization_barrier((grad_attn_b[1], ffn_parts))
    grad_query_two, key_acc, value_acc = run_back(
        lengths,
        core_arg,
        second_grad,
        output_proj,
        mixed[1],
        query_b,
        key_b,
        value_b,
        key_tb,
        lse[1],
        key_acc,
        value_acc,
        chunk_blocks[1],
    )
    ffn_sum = share(sum_parts(ffn_parts))
    grad_query_b = jnp.concatenate([grad_query_one, grad_query_two], axis=0)
    grad_key_b = key_acc.astype(BF16)
    grad_value_b = value_acc.astype(BF16)

    paired = jnp.stack(
        [
            outputbias_part,
            attngain_part,
            attnshift_part,
            outerbias_part,
            finalgain_part,
            finalshift_part,
        ],
        axis=0,
    )
    paired = paired + core_swap(paired)
    querybias_part = jnp.sum(grad_query_b.astype(F32), axis=0)
    valuebias_part = jnp.sum(grad_value_b.astype(F32), axis=0)
    vectors = jnp.concatenate(
        [
            paired,
            innerbias_part[None],
            jnp.concatenate(
                [querybias_part, valuebias_part, jnp.zeros((width - 2 * local_width,), F32)]
            )[None],
        ],
        axis=0,
    )
    vectors = jnp.pad(vectors.T, ((0, 0), (0, 128 - vectors.shape[0])))
    packed = jnp.concatenate(
        [
            tn(grad_query_b, rows).astype(BF16),
            tn(grad_key_b, rows).astype(BF16),
            tn(grad_value_b, rows).astype(BF16),
            (tn(mixed[0], grad_attn_b[0]) + tn(mixed[1], grad_attn_b[1])).astype(BF16),
        ],
        axis=0,
    )
    packed = jnp.concatenate([packed, vectors.astype(BF16)], axis=1)
    packed_parts = trade(packed)

    def input_part(first, count):
        span = slice(first, first + count)
        return (
            nt(grad_query_b[span], query_proj)
            + nt(grad_key_b[span], key_proj)
            + nt(grad_value_b[span], value_proj)
        )

    token_own = []
    for i in range(2):
        start = i * chunk
        pair = pair_sum(input_part(start, half), input_part(start + half, half))
        token_own.append((grad_first[i] + far_sum(pair)).astype(BF16))
    own_rows = jnp.concatenate(token_own, axis=0)
    other_rows = core_swap(own_rows)
    token_grad = jnp.where(
        core == 0,
        jnp.concatenate([own_rows, other_rows], axis=0),
        jnp.concatenate([other_rows, own_rows], axis=0),
    )

    packed_parts, ffn_sum = lax.optimization_barrier((packed_parts, ffn_sum))
    packed = share(sum_parts(packed_parts)).astype(F32)
    ffn_sum = ffn_sum.astype(F32)
    cuts = [packed[i * local_width : (i + 1) * local_width, :width] for i in range(4)]
    vectors = packed[:, width:].T
    return (
        loss_value,
        token_grad,
        cuts[0].T,
        vectors[7, :local_width],
        cuts[1].T,
        cuts[2].T,
        vectors[7, local_width : 2 * local_width],
        cuts[3],
        vectors[0],
        vectors[1],
        vectors[2],
        ffn_sum[width:],
        vectors[6],
        ffn_sum[:width],
        vectors[3],
        vectors[4],
        vectors[5],
    )


def solution(mesh):
    column, row, split = P(None, "mp"), P("mp", None), P("mp")
    placed = (
        (P("dp", None), P("dp"), P())
        + (column, split, column, column, split, row)
        + (P(), P(), P())
        + (column, split, row)
        + (P(), P(), P())
    )
    given = (
        (P(), P("dp", None))
        + (column, split, column, column, split, row)
        + (P(), P(), P())
        + (column, split, row)
        + (P(), P(), P())
    )
    return jax.shard_map(local, mesh=mesh, in_specs=placed, out_specs=given, check_vma=False)
```

```python
import functools
import math

import jax
import jax.numpy as jnp
from jax import lax
from jax.experimental import pallas as pl
from jax.experimental.pallas import tpu as pltpu
from jax.sharding import PartitionSpec as P

HD = 64
EPS_NORM = 1e-06
SOFTMAX_WARMTH = 0.01
NEG_FILL = -1e30
HIGHEST = lax.Precision.HIGHEST
F32 = jnp.float32
BF16 = jnp.bfloat16
QB = 256
KB = 128

CORE_SWAP = [(i, i ^ 1) for i in range(4)]
FAR_SWAP = [(i, i ^ 2) for i in range(4)]
NEAR_SWAP = [(i, i ^ 1) for i in range(32)]
PLANES = [[i * 2 + x for i in range(16)] for x in range(2)]

SMEM = pl.BlockSpec(memory_space=pltpu.SMEM)
VMEM = pl.BlockSpec(memory_space=pltpu.VMEM)


def nn(left, right):
    return lax.dot_general(left, right, (((1,), (0,)), ((), ())), preferred_element_type=F32)


def nt(left, right):
    return lax.dot_general(left, right, (((1,), (1,)), ((), ())), preferred_element_type=F32)


def tn(left, right):
    return lax.dot_general(left, right, (((0,), (0,)), ((), ())), preferred_element_type=F32)


def place_of_block(block, core, rows):
    return ((block % 2) * 2 + block // 2) * QB + core * (rows // 2) & (rows - 1)


def spot_of_keys(j, core, rows):
    place = (j * KB + core * (rows // 2)) & (rows - 1)
    block = place // QB
    return pl.multiple_of(((block % 2) * 2 + block // 2) * QB + place % QB, KB)


def segment_bounds(lengths_ref):
    bounds, total = [], jnp.int32(0)
    for s in range(lengths_ref.shape[0]):
        start = total
        total = total + lengths_ref[s]
        bounds.append((start, total))
    return bounds


def block_span(bounds, first, rows):
    place = first + lax.broadcasted_iota(jnp.int32, (1, QB), 1)
    low, high = first, first + KB
    begin = jnp.full((1, QB), bounds[-1][1], jnp.int32)
    end = jnp.full((1, QB), rows, jnp.int32)
    for start, stop in bounds:
        inside = (place >= start) & (place < stop)
        begin = jnp.where(inside, start, begin)
        end = jnp.where(inside, stop, end)
        touches = (stop > first) & (start < first + QB) & (stop > start)
        low = jnp.where(touches, jnp.minimum(low, start), low)
        high = jnp.where(touches, jnp.maximum(high, stop), high)
    return low // KB, (high + KB - 1) // KB, begin, end


def head_copies(values, heads):
    lane = lax.broadcasted_iota(jnp.int32, values.shape, 1) // HD
    blank = jnp.zeros_like(values)
    return jnp.concatenate([jnp.where(lane == h, values, blank) for h in range(heads)], axis=0)


def span_mask(begin, end, block, heads):
    place = block * KB + lax.broadcasted_iota(jnp.int32, (KB, QB), 0)
    keep = (place >= begin) & (place < end)
    return jnp.concatenate([keep] * heads, axis=1)


def attend(heads, blocks, core, bounds, q_ref, k_ref, vt_ref, mixed_ref, lse_ref, acc_ref):
    rows = k_ref.shape[0]
    for i, block in enumerate(blocks):
        low, high, begin, end = block_span(bounds, place_of_block(block, core, rows), rows)
        stack = head_copies(q_ref[block * QB : (block + 1) * QB, :], heads)
        acc_ref[...] = jnp.zeros(acc_ref.shape, F32)

        def step(j, carry, stack=stack, begin=begin, end=end):
            top, total = carry
            spot = spot_of_keys(j, core, rows)
            scores = nt(k_ref[pl.ds(spot, KB), :], stack)
            scores = jnp.where(span_mask(begin, end, j, heads), scores, NEG_FILL)
            peak = jnp.maximum(top, jnp.max(scores, axis=0, keepdims=True))
            fade = jnp.exp(top - peak)
            probs = jnp.exp(scores - peak)
            total = total * fade + jnp.sum(probs, axis=0, keepdims=True)
            probs = probs.astype(BF16)
            for h in range(heads):
                part = slice(h * QB, (h + 1) * QB)
                span = slice(h * HD, (h + 1) * HD)
                acc_ref[span, :] = acc_ref[span, :] * fade[:, part] + nn(
                    vt_ref[span, pl.ds(spot, KB)], probs[:, part]
                )
            return peak, total

        top = jnp.full((1, heads * QB), NEG_FILL, F32)
        top, total = lax.fori_loop(
            low, high, step, (top, jnp.zeros((1, heads * QB), F32)), unroll=False
        )
        scale = 1.0 / total
        mixed = jnp.concatenate(
            [
                acc_ref[h * HD : (h + 1) * HD, :] * scale[:, h * QB : (h + 1) * QB]
                for h in range(heads)
            ],
            axis=0,
        )
        mixed_ref[i * QB : (i + 1) * QB, :] = mixed.T.astype(BF16)
        lse_ref[i, :, :] = jnp.broadcast_to(top + jnp.log(total), (8, heads * QB))


def attend_first(
    heads,
    blocks,
    lengths_ref,
    core_ref,
    tokens_ref,
    wqt_ref,
    bq_ref,
    wkt_ref,
    wvt_ref,
    bv_ref,
    bvt_ref,
    x_ref,
    q_ref,
    k_ref,
    v_ref,
    kt_ref,
    vt_ref,
    mixed_ref,
    lse_ref,
    acc_ref,
):
    rows = tokens_ref.shape[0]
    core = core_ref[0]
    for block in range(rows // QB):
        part = slice(block * QB, (block + 1) * QB)
        first = pl.multiple_of(place_of_block(block, core, rows), QB)
        x = tokens_ref[pl.ds(first, QB), :]
        x_ref[part, :] = x
        q = (nt(x, wqt_ref[...]) + bq_ref[...].astype(F32)).astype(BF16)
        q_ref[part, :] = q * BF16(0.125)
        k_ref[part, :] = nt(x, wkt_ref[...]).astype(BF16)
        kt_ref[:, part] = nt(wkt_ref[...], x).astype(BF16)
        v_ref[part, :] = (nt(x, wvt_ref[...]) + bv_ref[...].astype(F32)).astype(BF16)
        vt_ref[:, part] = (nt(wvt_ref[...], x) + bvt_ref[...].astype(F32)).astype(BF16)
    bounds = segment_bounds(lengths_ref)
    attend(heads, blocks, core, bounds, q_ref, k_ref, vt_ref, mixed_ref, lse_ref, acc_ref)


def attend_more(
    heads, blocks, lengths_ref, core_ref, q_ref, k_ref, vt_ref, mixed_ref, lse_ref, acc_ref
):
    bounds = segment_bounds(lengths_ref)
    attend(heads, blocks, core_ref[0], bounds, q_ref, k_ref, vt_ref, mixed_ref, lse_ref, acc_ref)


def attend_back(
    heads,
    blocks,
    lengths_ref,
    core_ref,
    grad_ref,
    wo_ref,
    mixed_ref,
    q_ref,
    k_ref,
    v_ref,
    kt_ref,
    lse_ref,
    dk_in_ref,
    dv_in_ref,
    dq_ref,
    dk_ref,
    dv_ref,
    dqt_ref,
):
    rows, width = q_ref.shape
    core = core_ref[0]
    bounds = segment_bounds(lengths_ref)
    dk_ref[...] = dk_in_ref[...]
    dv_ref[...] = dv_in_ref[...]
    lane = lax.broadcasted_iota(jnp.int32, (8, width), 1) // HD
    which = (lane == lax.broadcasted_iota(jnp.int32, (8, width), 0)).astype(F32)
    for i, block in enumerate(blocks):
        low, high, begin, end = block_span(bounds, place_of_block(block, core, rows), rows)
        part = slice(i * QB, (i + 1) * QB)
        grad_mixed = nt(grad_ref[part, :], wo_ref[...]).astype(BF16)
        product = grad_mixed.astype(F32) * mixed_ref[part, :].astype(F32)
        sums = lax.dot_general(
            which,
            product,
            (((1,), (1,)), ((), ())),
            precision=HIGHEST,
            preferred_element_type=F32,
        )
        delta = jnp.concatenate([sums[h : h + 1, :] for h in range(heads)], axis=1)
        lse = lse_ref[i, 0:1, :]
        q_stack = head_copies(q_ref[block * QB : (block + 1) * QB, :], heads)
        g_stack = head_copies(grad_mixed, heads)
        dqt_ref[...] = jnp.zeros(dqt_ref.shape, F32)

        def step(
            j, carry, delta=delta, lse=lse, q_stack=q_stack, g_stack=g_stack, begin=begin, end=end
        ):
            here = pl.ds(spot_of_keys(j, core, rows), KB)
            scores = nt(k_ref[here, :], q_stack)
            scores = jnp.where(span_mask(begin, end, j, heads), scores, NEG_FILL)
            probs = jnp.exp(scores - lse)
            grad = (probs * (nt(v_ref[here, :], g_stack) - delta)).astype(BF16)
            dv_ref[here, :] += nn(probs.astype(BF16), g_stack)
            dk_ref[here, :] += nn(grad, q_stack)
            for h in range(heads):
                span = slice(h * HD, (h + 1) * HD)
                dqt_ref[span, :] += nn(kt_ref[span, here], grad[:, h * QB : (h + 1) * QB])
            return carry

        lax.fori_loop(low, high, step, 0, unroll=False)
        dq_ref[part, :] = (dqt_ref[...].T * 0.125).astype(BF16)


def shaped(shape, dtype):
    return jax.ShapeDtypeStruct(shape, dtype)


PARAMS = pltpu.CompilerParams(vmem_limit_bytes=16 << 20)


def run_first(lengths, core, tokens, wqt, bq, wkt, wvt, bv, blocks):
    rows, width = tokens.shape[0], wqt.shape[0]
    heads, count = width // HD, len(blocks)
    return pl.pallas_call(
        functools.partial(attend_first, heads, blocks),
        out_shape=(shaped(tokens.shape, BF16),)
        + (shaped((rows, width), BF16),) * 3
        + (shaped((width, rows), BF16),) * 2
        + (shaped((count * QB, width), BF16), shaped((count, 8, heads * QB), F32)),
        in_specs=[SMEM] * 2 + [VMEM] * 7,
        out_specs=(VMEM,) * 8,
        scratch_shapes=[pltpu.VMEM((width, QB), F32)],
        compiler_params=PARAMS,
        name="attend_first",
        cost_estimate=pl.CostEstimate(
            flops=2_000_000_000, bytes_accessed=8_000_000, transcendentals=1_000_000
        ),
    )(lengths, core, tokens, wqt, bq.reshape(1, -1), wkt, wvt, bv.reshape(1, -1), bv.reshape(-1, 1))


def run_more(lengths, core, q, k, vt, blocks):
    rows, width = q.shape
    heads, count = width // HD, len(blocks)
    return pl.pallas_call(
        functools.partial(attend_more, heads, blocks),
        out_shape=(shaped((count * QB, width), BF16), shaped((count, 8, heads * QB), F32)),
        in_specs=[SMEM] * 2 + [VMEM] * 3,
        out_specs=(VMEM,) * 2,
        scratch_shapes=[pltpu.VMEM((width, QB), F32)],
        compiler_params=PARAMS,
        name="attend_more",
        cost_estimate=pl.CostEstimate(
            flops=1_000_000_000, bytes_accessed=8_000_000, transcendentals=1_000_000
        ),
    )(lengths, core, q, k, vt)


def run_back(lengths, core, grad, wo, mixed, q, k, v, kt, lse, dk, dv, blocks):
    rows, width = q.shape
    heads, count = width // HD, len(blocks)
    return pl.pallas_call(
        functools.partial(attend_back, heads, blocks),
        out_shape=(shaped((count * QB, width), BF16),) + (shaped((rows, width), F32),) * 2,
        in_specs=[SMEM] * 2 + [VMEM] * 10,
        out_specs=(VMEM,) * 3,
        scratch_shapes=[pltpu.VMEM((width, QB), F32)],
        compiler_params=PARAMS,
        name="attend_back",
        cost_estimate=pl.CostEstimate(
            flops=3_000_000_000, bytes_accessed=12_000_000, transcendentals=1_000_000
        ),
    )(lengths, core, grad, wo, mixed, q, k, v, kt, lse, dk, dv)


def trade(values):
    return lax.all_to_all(
        values, "dp", split_axis=0, concat_axis=0, axis_index_groups=PLANES, tiled=True
    )


def share(values):
    spread = jnp.broadcast_to(values[None], (16,) + values.shape)
    return trade(spread.reshape((-1,) + values.shape[1:]))


def near_swap(values):
    return lax.ppermute(values, "dp", NEAR_SWAP)


def sum_parts(parts):
    parts = parts.reshape((16, -1) + parts.shape[1:])
    total = jnp.sum(parts.astype(F32), axis=0).astype(BF16)
    return (total.astype(F32) + near_swap(total).astype(F32)).astype(BF16)


def core_swap(values):
    return lax.ppermute(values, "mp", CORE_SWAP)


def far_swap(values):
    return lax.ppermute(values, "mp", FAR_SWAP)


def pair_sum(own, other):
    return (own + core_swap(other.astype(BF16)).astype(F32)).astype(BF16)


def after(values, *others):
    return lax.optimization_barrier((values, others))[0]


def both(own):
    return jnp.concatenate([own, core_swap(own)], axis=0)


def norm_forward(values, gain_vec, shift_vec):
    average = jnp.mean(values, axis=-1, keepdims=True)
    centred = values - average
    rscale = lax.rsqrt(jnp.mean(centred * centred, axis=-1, keepdims=True) + EPS_NORM)
    normed = centred * rscale
    return (normed * gain_vec + shift_vec, normed, rscale)


def norm_backward(grad_out, normed, rscale, gain_vec):
    scaled = grad_out * gain_vec
    first_mean = jnp.mean(scaled, axis=-1, keepdims=True)
    cross_mean = jnp.mean(scaled * normed, axis=-1, keepdims=True)
    return rscale * (scaled - first_mean - normed * cross_mean)


def gelu_and_slope(upper):
    below = 0.5 * (1.0 + lax.erf(upper * math.sqrt(0.5)))
    density = jnp.exp(-0.5 * upper * upper) * (1.0 / math.sqrt(2.0 * math.pi))
    return (upper * below).astype(BF16), (below + upper * density).astype(BF16)


def local(
    tokens,
    lengths,
    pair_index,
    query_proj,
    query_bias,
    key_proj,
    value_proj,
    value_bias,
    output_proj,
    output_bias,
    attn_gain,
    attn_shift,
    inner_proj,
    inner_bias,
    outer_proj,
    outer_bias,
    final_gain,
    final_shift,
):
    row_count, width = tokens.shape
    chunk = row_count // 2
    half = chunk // 2
    seq_count = lengths.shape[0]
    pair_count = seq_count // 2
    overall_pair_count = pair_index.shape[0]
    local_width = query_proj.shape[1]
    core = lax.axis_index("mp") % 2
    my_index = lax.axis_index("dp")
    core_arg = jnp.reshape(core, (1,)).astype(jnp.int32)
    attn_gain_f, attn_shift_f = attn_gain.astype(F32), attn_shift.astype(F32)
    final_gain_f, final_shift_f = final_gain.astype(F32), final_shift.astype(F32)
    query_t, key_t, value_t = query_proj.T, key_proj.T, value_proj.T
    chunk_blocks = ((0, 1), (2, 3))

    seq_ends = jnp.cumsum(lengths)
    seq_starts = seq_ends - lengths
    members = []
    for index in range(2):
        place = jnp.arange(half, dtype=jnp.int32) + index * half + core * chunk
        members.append(
            ((place[None] >= seq_starts[:, None]) & (place[None] < seq_ends[:, None])).astype(F32)
        )

    rows, query_b, key_b, value_b, key_tb, value_tb, mixed_one, lse_one = run_first(
        lengths, core_arg, tokens, query_t, query_bias, key_t, value_t, value_bias, chunk_blocks[0]
    )

    def project(mixed):
        return pair_sum(nn(mixed[:half], output_proj), nn(mixed[half:], output_proj))

    attn_pair = [project(mixed_one)]
    mixed_two, lse_two = run_more(
        lengths, core_arg, after(query_b, attn_pair[0]), key_b, value_tb, chunk_blocks[1]
    )
    mixed, lse = (mixed_one, mixed_two), (lse_one, lse_two)
    attn_pair.append(project(mixed_two))
    attn_far = [far_swap(pair) for pair in attn_pair]

    def part(values, index):
        return values[index * chunk : (index + 1) * chunk]

    hidden_f, hidden_b, normed_one, rscale_one, act_b, slope_b, ffn_pair = [], [], [], [], [], [], []
    for i in range(2):
        far = attn_far[i] if i == 0 else after(attn_far[i], ffn_pair[0])
        attn_full = attn_pair[i].astype(F32) + far.astype(F32) + output_bias.astype(F32)
        own_tokens = part(rows, i)[:half].astype(F32)
        hidden, normed, rscale = norm_forward(own_tokens + attn_full, attn_gain_f, attn_shift_f)
        hidden_f.append(hidden)
        normed_one.append(normed)
        rscale_one.append(rscale)
        hidden_b.append(both(hidden.astype(BF16)))
        act, slope = gelu_and_slope(nn(hidden_b[i], inner_proj) + inner_bias.astype(F32))
        act_b.append(act)
        slope_b.append(slope)
        ffn_pair.append(pair_sum(nn(act[:half], outer_proj), nn(act[half:], outer_proj)))
    normed_two, rscale_two, pooled_part = [], [], 0.0
    ffn_far = [far_swap(pair) for pair in ffn_pair]
    for i in range(2):
        far = ffn_far[i] if i == 0 else after(ffn_far[i], pooled_part)
        ffn_full = ffn_pair[i].astype(F32) + far.astype(F32) + outer_bias.astype(F32)
        final_out, normed, rscale = norm_forward(
            hidden_f[i] + ffn_full, final_gain_f, final_shift_f
        )
        normed_two.append(normed)
        rscale_two.append(rscale)
        pooled_part = pooled_part + jnp.dot(members[i], final_out, precision=HIGHEST)
    pooled = pooled_part + core_swap(pooled_part)
    pool_rscale = lax.rsqrt(jnp.sum(pooled * pooled, axis=-1, keepdims=True) + EPS_NORM)
    unit_b = (pooled * pool_rscale).astype(BF16)

    piece = lax.dynamic_slice_in_dim(unit_b, core * pair_count, pair_count, 0)
    near = near_swap(piece)
    low = (my_index % 2) == 0
    piece = jnp.concatenate([jnp.where(low, piece, near), jnp.where(low, near, piece)], axis=0)
    piece = share(piece)
    swapped = core_swap(piece)
    query_units = jnp.where(core == 0, piece, swapped)
    passage_units = jnp.where(core == 0, swapped, piece)

    backward_scale = 1.0 / (overall_pair_count * SOFTMAX_WARMTH)
    similarity = nt(query_units, passage_units) / SOFTMAX_WARMTH
    query_ids = jnp.arange(overall_pair_count, dtype=jnp.int32)
    is_match = (pair_index[None, :] == query_ids[:, None]).astype(F32)
    top = jnp.max(similarity, axis=1, keepdims=True)
    query_lse = top + jnp.log(jnp.sum(jnp.exp(similarity - top), axis=1, keepdims=True))
    loss_value = (
        jnp.sum(query_lse[:, 0] - jnp.sum(similarity * is_match, axis=1)) / overall_pair_count
    )
    coef = (jnp.exp(similarity - query_lse) - is_match) * backward_scale
    own_start = my_index * pair_count
    coef_query = lax.dynamic_slice_in_dim(coef, own_start, pair_count, 0)
    coef_passage = lax.dynamic_slice_in_dim(coef, own_start, pair_count, 1)
    grad_query = jnp.dot(coef_query, passage_units.astype(F32), precision=HIGHEST)
    grad_passage = lax.dot_general(
        coef_passage, query_units.astype(F32), (((0,), (0,)), ((), ())), precision=HIGHEST
    )
    grad_unit = jnp.concatenate([grad_query, grad_passage], axis=0)
    grad_pooled = (
        pool_rscale * grad_unit
        - pool_rscale**3 * jnp.sum(pooled * grad_unit, axis=-1, keepdims=True) * pooled
    )

    finalgain_part = finalshift_part = outerbias_part = innerbias_part = 0.0
    grad_second, grad_ffn_b, grad_up_b, hidden_pair = [], [], [], []
    for i in range(2):
        grad_final = jnp.einsum("st,sd->td", members[i], grad_pooled, precision=HIGHEST)
        finalgain_part += jnp.sum(grad_final * normed_two[i], axis=0)
        finalshift_part += jnp.sum(grad_final, axis=0)
        grad_second.append(norm_backward(grad_final, normed_two[i], rscale_two[i], final_gain_f))
        own_grad = grad_second[i].astype(BF16)
        outerbias_part += jnp.sum(own_grad.astype(F32), axis=0)
        whole_grad = both(own_grad)
        grad_ffn_b.append(whole_grad if i == 0 else after(whole_grad, hidden_pair[0]))
        grad_up = (nt(grad_ffn_b[i], outer_proj) * slope_b[i].astype(F32)).astype(BF16)
        innerbias_part += jnp.sum(grad_up.astype(F32), axis=0)
        grad_up_b.append(grad_up)
        hidden_pair.append(pair_sum(nt(grad_up[:half], inner_proj), nt(grad_up[half:], inner_proj)))
    hidden_far = [far_swap(pair) for pair in hidden_pair]
    late_act, late_hidden = after((act_b[0], hidden_b[0]), hidden_pair[1])
    ffn_pack = jnp.concatenate(
        [
            (tn(late_act, grad_ffn_b[0]) + tn(act_b[1], grad_ffn_b[1])).astype(BF16),
            (tn(late_hidden, grad_up_b[0]) + tn(hidden_b[1], grad_up_b[1])).astype(BF16),
        ],
        axis=0,
    )
    ffn_parts = trade(ffn_pack)

    attngain_part = attnshift_part = outputbias_part = 0.0
    key_acc = value_acc = jnp.zeros((row_count, local_width), F32)
    grad_first, grad_attn_b, grad_queries = [], [], []
    for i in range(2):
        far = hidden_far[i] if i == 0 else after(hidden_far[i], grad_queries[0])
        grad_hidden = grad_second[i] + (hidden_pair[i].astype(F32) + far.astype(F32))
        attngain_part += jnp.sum(grad_hidden * normed_one[i], axis=0)
        attnshift_part += jnp.sum(grad_hidden, axis=0)
        grad_first.append(norm_backward(grad_hidden, normed_one[i], rscale_one[i], attn_gain_f))
        own_grad = grad_first[i].astype(BF16)
        outputbias_part += jnp.sum(own_grad.astype(F32), axis=0)
        grad_attn_b.append(both(own_grad))
        grad_query, key_acc, value_acc = run_back(
            lengths,
            core_arg,
            grad_attn_b[i],
            output_proj,
            mixed[i],
            query_b,
            key_b,
            value_b,
            key_tb,
            lse[i],
            key_acc,
            value_acc,
            chunk_blocks[i],
        )
        grad_queries.append(grad_query)
    grad_query_b = jnp.concatenate(grad_queries, axis=0)
    grad_key_b = key_acc.astype(BF16)
    grad_value_b = value_acc.astype(BF16)

    paired = jnp.stack(
        [
            outputbias_part,
            attngain_part,
            attnshift_part,
            outerbias_part,
            finalgain_part,
            finalshift_part,
        ],
        axis=0,
    )
    paired = paired + core_swap(paired)
    querybias_part = jnp.sum(grad_query_b.astype(F32), axis=0)
    valuebias_part = jnp.sum(grad_value_b.astype(F32), axis=0)
    vectors = jnp.concatenate(
        [
            paired,
            innerbias_part[None],
            jnp.concatenate(
                [querybias_part, valuebias_part, jnp.zeros((width - 2 * local_width,), F32)]
            )[None],
        ],
        axis=0,
    )
    vectors = jnp.pad(vectors.T, ((0, 0), (0, 128 - vectors.shape[0])))
    packed = jnp.concatenate(
        [
            tn(grad_query_b, rows).astype(BF16),
            tn(grad_key_b, rows).astype(BF16),
            tn(grad_value_b, rows).astype(BF16),
            (tn(mixed[0], grad_attn_b[0]) + tn(mixed[1], grad_attn_b[1])).astype(BF16),
        ],
        axis=0,
    )
    packed = jnp.concatenate([packed, vectors.astype(BF16)], axis=1)
    packed_parts = trade(packed)
    ffn_sum = share(sum_parts(after(ffn_parts, packed)))
    late_query_b = after(grad_query_b, packed)

    def input_part(first, count):
        span = slice(first, first + count)
        return (
            nt(late_query_b[span], query_proj)
            + nt(grad_key_b[span], key_proj)
            + nt(grad_value_b[span], value_proj)
        )

    token_own = []
    for i in range(2):
        start = i * chunk
        pair = pair_sum(input_part(start, half), input_part(start + half, half))
        token_sum = pair.astype(F32) + far_swap(pair).astype(F32)
        token_own.append((grad_first[i] + token_sum).astype(BF16))
    own_rows = after(jnp.concatenate(token_own, axis=0), ffn_sum)
    other_rows = core_swap(own_rows)
    token_grad = jnp.where(
        core == 0,
        jnp.concatenate([own_rows, other_rows], axis=0),
        jnp.concatenate([other_rows, own_rows], axis=0),
    )

    packed = share(sum_parts(packed_parts)).astype(F32)
    ffn_sum = ffn_sum.astype(F32)
    cuts = [packed[i * local_width : (i + 1) * local_width, :width] for i in range(4)]
    vectors = packed[:, width:].T
    return (
        loss_value,
        token_grad,
        cuts[0].T,
        vectors[7, :local_width],
        cuts[1].T,
        cuts[2].T,
        vectors[7, local_width : 2 * local_width],
        cuts[3],
        vectors[0],
        vectors[1],
        vectors[2],
        ffn_sum[width:],
        vectors[6],
        ffn_sum[:width],
        vectors[3],
        vectors[4],
        vectors[5],
    )


def solution(mesh):
    column, row, split = P(None, "mp"), P("mp", None), P("mp")
    placed = (
        (P("dp", None), P("dp"), P())
        + (column, split, column, column, split, row)
        + (P(), P(), P())
        + (column, split, row)
        + (P(), P(), P())
    )
    given = (
        (P(), P("dp", None))
        + (column, split, column, column, split, row)
        + (P(), P(), P())
        + (column, split, row)
        + (P(), P(), P())
    )
    return jax.shard_map(local, mesh=mesh, in_specs=placed, out_specs=given, check_vma=False)
```

```python
import functools
import math

import jax
import jax.numpy as jnp
from jax import lax
from jax.experimental import pallas as pl
from jax.experimental.pallas import tpu as pltpu
from jax.sharding import PartitionSpec as P

HD = 64
EPS_NORM = 1e-06
SOFTMAX_WARMTH = 0.01
NEG_FILL = -1e30
HIGHEST = lax.Precision.HIGHEST
F32 = jnp.float32
BF16 = jnp.bfloat16
QB = 256
KB = 128

CORE_SWAP = [(i, i ^ 1) for i in range(4)]
FAR_SWAP = [(i, i ^ 2) for i in range(4)]
NEAR_SWAP = [(i, i ^ 1) for i in range(32)]
PLANES = [[i * 2 + x for i in range(16)] for x in range(2)]

SMEM = pl.BlockSpec(memory_space=pltpu.SMEM)
VMEM = pl.BlockSpec(memory_space=pltpu.VMEM)
ANY = pl.BlockSpec(memory_space=pl.ANY)


def nn(left, right):
    return lax.dot_general(left, right, (((1,), (0,)), ((), ())), preferred_element_type=F32)


def nt(left, right):
    return lax.dot_general(left, right, (((1,), (1,)), ((), ())), preferred_element_type=F32)


def tn(left, right):
    return lax.dot_general(left, right, (((0,), (0,)), ((), ())), preferred_element_type=F32)


def place_of_block(block, core, rows):
    return ((block % 2) * 2 + block // 2) * QB + core * (rows // 2) & (rows - 1)


def spot_of_keys(j, core, rows):
    place = (j * KB + core * (rows // 2)) & (rows - 1)
    block = place // QB
    return pl.multiple_of(((block % 2) * 2 + block // 2) * QB + place % QB, KB)


def segment_bounds(lengths_ref):
    bounds, total = [], jnp.int32(0)
    for s in range(lengths_ref.shape[0]):
        start = total
        total = total + lengths_ref[s]
        bounds.append((start, total))
    return bounds


def block_span(bounds, first, rows):
    place = first + lax.broadcasted_iota(jnp.int32, (1, QB), 1)
    low, high = first, first + KB
    begin = jnp.full((1, QB), bounds[-1][1], jnp.int32)
    end = jnp.full((1, QB), rows, jnp.int32)
    for start, stop in bounds:
        inside = (place >= start) & (place < stop)
        begin = jnp.where(inside, start, begin)
        end = jnp.where(inside, stop, end)
        touches = (stop > first) & (start < first + QB) & (stop > start)
        low = jnp.where(touches, jnp.minimum(low, start), low)
        high = jnp.where(touches, jnp.maximum(high, stop), high)
    return low // KB, (high + KB - 1) // KB, begin, end


def head_copies(values, heads):
    lane = lax.broadcasted_iota(jnp.int32, values.shape, 1) // HD
    blank = jnp.zeros_like(values)
    return jnp.concatenate([jnp.where(lane == h, values, blank) for h in range(heads)], axis=0)


def span_mask(begin, end, block, heads):
    place = block * KB + lax.broadcasted_iota(jnp.int32, (KB, QB), 0)
    keep = (place >= begin) & (place < end)
    return jnp.concatenate([keep] * heads, axis=1)


def attend(heads, blocks, core, bounds, q_ref, k_ref, vt_ref, mixed_ref, lse_ref, acc_ref):
    rows = k_ref.shape[0]
    for i, block in enumerate(blocks):
        low, high, begin, end = block_span(bounds, place_of_block(block, core, rows), rows)
        stack = head_copies(q_ref[block * QB : (block + 1) * QB, :], heads)
        acc_ref[...] = jnp.zeros(acc_ref.shape, F32)

        def step(j, carry, stack=stack, begin=begin, end=end):
            top, total = carry
            spot = spot_of_keys(j, core, rows)
            scores = nt(k_ref[pl.ds(spot, KB), :], stack)
            scores = jnp.where(span_mask(begin, end, j, heads), scores, NEG_FILL)
            peak = jnp.maximum(top, jnp.max(scores, axis=0, keepdims=True))
            fade = jnp.exp(top - peak)
            probs = jnp.exp(scores - peak)
            total = total * fade + jnp.sum(probs, axis=0, keepdims=True)
            probs = probs.astype(BF16)
            for h in range(heads):
                part = slice(h * QB, (h + 1) * QB)
                span = slice(h * HD, (h + 1) * HD)
                acc_ref[span, :] = acc_ref[span, :] * fade[:, part] + nn(
                    vt_ref[span, pl.ds(spot, KB)], probs[:, part]
                )
            return peak, total

        top = jnp.full((1, heads * QB), NEG_FILL, F32)
        top, total = lax.fori_loop(
            low, high, step, (top, jnp.zeros((1, heads * QB), F32)), unroll=False
        )
        scale = 1.0 / total
        mixed = jnp.concatenate(
            [
                acc_ref[h * HD : (h + 1) * HD, :] * scale[:, h * QB : (h + 1) * QB]
                for h in range(heads)
            ],
            axis=0,
        )
        mixed_ref[i * QB : (i + 1) * QB, :] = mixed.T.astype(BF16)
        lse_ref[i, :, :] = jnp.broadcast_to(top + jnp.log(total), (8, heads * QB))


def fetch(sources, targets, semaphores):
    copies = [
        pltpu.make_async_copy(source, target, semaphores.at[i])
        for i, (source, target) in enumerate(zip(sources, targets))
    ]
    for copy in copies:
        copy.start()
    return copies


def attend_first(
    heads,
    blocks,
    lengths_ref,
    core_ref,
    tokens_any,
    wqt_any,
    wkt_any,
    wvt_any,
    vectors_any,
    x_ref,
    q_ref,
    k_ref,
    v_ref,
    kt_ref,
    vt_ref,
    mixed_ref,
    lse_ref,
    acc_ref,
    wqt_ref,
    wkt_ref,
    wvt_ref,
    vectors_ref,
    semaphores,
):
    rows = x_ref.shape[0]
    width = heads * HD
    core = core_ref[0]
    sources = [vectors_any, wqt_any]
    targets = [vectors_ref, wqt_ref]
    for block in range(rows // QB):
        first = pl.multiple_of(place_of_block(block, core, rows), QB)
        sources.append(tokens_any.at[pl.ds(first, QB), :])
        targets.append(x_ref.at[pl.ds(block * QB, QB), :])
    copies = fetch(sources + [wkt_any, wvt_any], targets + [wkt_ref, wvt_ref], semaphores)
    for copy in copies:
        copy.wait()
    query_bias = vectors_ref[0:1, :width]
    value_bias = vectors_ref[1:2, :width]
    for block in range(rows // QB):
        part = slice(block * QB, (block + 1) * QB)
        x = x_ref[part, :]
        q = (nt(x, wqt_ref[...]) + query_bias).astype(BF16)
        q_ref[part, :] = q * BF16(0.125)
        k_ref[part, :] = nt(x, wkt_ref[...]).astype(BF16)
        kt_ref[:, part] = nt(wkt_ref[...], x).astype(BF16)
        v = nt(x, wvt_ref[...]) + value_bias
        v_ref[part, :] = v.astype(BF16)
        vt_ref[:, part] = v.T.astype(BF16)
    bounds = segment_bounds(lengths_ref)
    attend(heads, blocks, core, bounds, q_ref, k_ref, vt_ref, mixed_ref, lse_ref, acc_ref)


def attend_more(
    heads,
    blocks,
    lengths_ref,
    core_ref,
    q_any,
    k_any,
    vt_any,
    mixed_ref,
    lse_ref,
    acc_ref,
    q_ref,
    k_ref,
    vt_ref,
    semaphores,
):
    for copy in fetch((q_any, k_any, vt_any), (q_ref, k_ref, vt_ref), semaphores):
        copy.wait()
    bounds = segment_bounds(lengths_ref)
    attend(heads, blocks, core_ref[0], bounds, q_ref, k_ref, vt_ref, mixed_ref, lse_ref, acc_ref)


def attend_back(heads, inputs, lengths_ref, core_ref, *refs):
    sources, refs = refs[:inputs], refs[inputs:]
    gq_ref, gk_ref, gv_ref, pack_ref = refs[:4]
    dk_ref, dv_ref, dqt_ref, wo_acc_ref, semaphores = refs[4:9]
    targets = refs[9:]
    copies = fetch(sources, targets, semaphores)
    grads = targets[0:4]
    mixed = targets[4:6]
    lses = targets[6:8]
    wo_ref, q_ref, k_ref, v_ref, kt_ref, vectors_ref, x_ref = targets[8:]
    rows, width = q_ref.shape
    core = core_ref[0]
    bounds = segment_bounds(lengths_ref)
    dk_ref[...] = jnp.zeros(dk_ref.shape, F32)
    dv_ref[...] = jnp.zeros(dv_ref.shape, F32)
    lane = lax.broadcasted_iota(jnp.int32, (8, width), 1) // HD
    which = (lane == lax.broadcasted_iota(jnp.int32, (8, width), 0)).astype(F32)
    for copy in copies[:-1]:
        copy.wait()
    for block in range(rows // QB):
        low, high, begin, end = block_span(bounds, place_of_block(block, core, rows), rows)
        part = slice(block * QB, (block + 1) * QB)
        own = slice(block % 2 * QB, block % 2 * QB + QB)
        grad_attn = grads[block][...]
        mixed_here = mixed[block // 2][own, :]
        outer = tn(mixed_here, grad_attn)
        wo_acc_ref[...] = outer if block == 0 else wo_acc_ref[...] + outer
        grad_mixed = nt(grad_attn, wo_ref[...]).astype(BF16)
        product = grad_mixed.astype(F32) * mixed_here.astype(F32)
        sums = lax.dot_general(
            which,
            product,
            (((1,), (1,)), ((), ())),
            precision=HIGHEST,
            preferred_element_type=F32,
        )
        delta = jnp.concatenate([sums[h : h + 1, :] for h in range(heads)], axis=1)
        lse = lses[block // 2][block % 2, 0:1, :]
        q_stack = head_copies(q_ref[part, :], heads)
        g_stack = head_copies(grad_mixed, heads)
        dqt_ref[...] = jnp.zeros(dqt_ref.shape, F32)

        def step(
            j, carry, delta=delta, lse=lse, q_stack=q_stack, g_stack=g_stack, begin=begin, end=end
        ):
            here = pl.ds(spot_of_keys(j, core, rows), KB)
            scores = nt(k_ref[here, :], q_stack)
            scores = jnp.where(span_mask(begin, end, j, heads), scores, NEG_FILL)
            probs = jnp.exp(scores - lse)
            grad = (probs * (nt(v_ref[here, :], g_stack) - delta)).astype(BF16)
            dv_ref[here, :] += nn(probs.astype(BF16), g_stack)
            dk_ref[here, :] += nn(grad, q_stack)
            for h in range(heads):
                span = slice(h * HD, (h + 1) * HD)
                dqt_ref[span, :] += nn(kt_ref[span, here], grad[:, h * QB : (h + 1) * QB])
            return carry

        lax.fori_loop(low, high, step, 0, unroll=False)
        gq_ref[part, :] = (dqt_ref[...].T * 0.125).astype(BF16)
    gk_ref[...] = dk_ref[...].astype(BF16)
    gv_ref[...] = dv_ref[...].astype(BF16)
    copies[-1].wait()
    piece = pack_ref.shape[1] - 8
    per = width // piece
    for m, source in enumerate((gq_ref, gk_ref, gv_ref, None)):
        total = wo_acc_ref[...] if source is None else tn(source[...], x_ref[...])
        for t in range(per):
            cut = total[t * piece : (t + 1) * piece, :].astype(BF16)
            pack_ref[m * per + t, 0:piece, :] = cut
    sums = [
        jnp.sum(ref[...].astype(F32), axis=0, keepdims=True) for ref in (gq_ref, gv_ref)
    ]
    blank = jnp.zeros((1, 256 - width), F32)
    tail = jnp.concatenate([sums[0], blank, sums[1], blank, jnp.zeros((1, 256), F32)], axis=1)
    small = jnp.concatenate([vectors_ref[0:7, :], tail], axis=0).astype(BF16)
    for p in range(pack_ref.shape[0]):
        pack_ref[p, piece:, :] = small if p == 0 else jnp.zeros_like(small)


def shaped(shape, dtype):
    return jax.ShapeDtypeStruct(shape, dtype)


PARAMS = pltpu.CompilerParams(vmem_limit_bytes=24 << 20)
COST = pl.CostEstimate(flops=1024, bytes_accessed=1024, transcendentals=0)


def buffers(arrays):
    return [pltpu.VMEM(array.shape, array.dtype) for array in arrays]


def run_first(lengths, core, tokens, wqt, wkt, wvt, vectors, blocks):
    rows, width = tokens.shape[0], wqt.shape[0]
    heads, count = width // HD, len(blocks)
    return pl.pallas_call(
        functools.partial(attend_first, heads, blocks),
        out_shape=(shaped(tokens.shape, BF16),)
        + (shaped((rows, width), BF16),) * 3
        + (shaped((width, rows), BF16),) * 2
        + (shaped((count * QB, width), BF16), shaped((count, 8, heads * QB), F32)),
        in_specs=[SMEM] * 2 + [ANY] * 5,
        out_specs=(VMEM,) * 8,
        scratch_shapes=[pltpu.VMEM((width, QB), F32)]
        + buffers((wqt, wkt, wvt, vectors))
        + [pltpu.SemaphoreType.DMA((4 + rows // QB,))],
        compiler_params=PARAMS,
        name="attend_first",
        cost_estimate=COST,
    )(lengths, core, tokens, wqt, wkt, wvt, vectors)


def run_more(lengths, core, q, k, vt, blocks):
    rows, width = q.shape
    heads, count = width // HD, len(blocks)
    return pl.pallas_call(
        functools.partial(attend_more, heads, blocks),
        out_shape=(shaped((count * QB, width), BF16), shaped((count, 8, heads * QB), F32)),
        in_specs=[SMEM] * 2 + [ANY] * 3,
        out_specs=(VMEM,) * 2,
        scratch_shapes=[pltpu.VMEM((width, QB), F32)]
        + buffers((q, k, vt))
        + [pltpu.SemaphoreType.DMA((3,))],
        compiler_params=PARAMS,
        name="attend_more",
        cost_estimate=COST,
    )(lengths, core, q, k, vt)


def run_back(lengths, core, grads, mixed, lses, wo, q, k, v, kt, vectors, x):
    rows, width = q.shape
    heads = width // HD
    arrays = (*grads, *mixed, *lses, wo, q, k, v, kt, vectors, x)
    piece = 4 * width // 16
    return pl.pallas_call(
        functools.partial(attend_back, heads, len(arrays)),
        out_shape=(shaped((rows, width), BF16),) * 3
        + (shaped((16, piece + 8, x.shape[1]), BF16),),
        in_specs=[SMEM] * 2 + [ANY] * len(arrays),
        out_specs=(VMEM,) * 4,
        scratch_shapes=[pltpu.VMEM((rows, width), F32)] * 2
        + [pltpu.VMEM((width, QB), F32), pltpu.VMEM(wo.shape, F32)]
        + [pltpu.SemaphoreType.DMA((len(arrays),))]
        + buffers(arrays),
        compiler_params=PARAMS,
        name="attend_back",
        cost_estimate=COST,
    )(lengths, core, *arrays)


def trade(values):
    return lax.all_to_all(
        values, "dp", split_axis=0, concat_axis=0, axis_index_groups=PLANES, tiled=True
    )


def share(values):
    return trade(jnp.broadcast_to(values[None], (16,) + values.shape))


def near_swap(values):
    return lax.ppermute(values, "dp", NEAR_SWAP)


def sum_parts(parts):
    total = jnp.sum(parts.astype(F32), axis=0).astype(BF16)
    return (total.astype(F32) + near_swap(total).astype(F32)).astype(BF16)


def core_swap(values):
    return lax.ppermute(values, "mp", CORE_SWAP)


def far_swap(values):
    return lax.ppermute(values, "mp", FAR_SWAP)


def after(values, *others):
    return lax.optimization_barrier((values, others))[0]


def both(own):
    return jnp.concatenate([own, core_swap(own)], axis=0)


def norm_forward(values, gain_vec, shift_vec):
    average = jnp.mean(values, axis=-1, keepdims=True)
    centred = values - average
    rscale = lax.rsqrt(jnp.mean(centred * centred, axis=-1, keepdims=True) + EPS_NORM)
    normed = centred * rscale
    return (normed * gain_vec + shift_vec, normed, rscale)


def norm_backward(grad_out, normed, rscale, gain_vec):
    scaled = grad_out * gain_vec
    first_mean = jnp.mean(scaled, axis=-1, keepdims=True)
    cross_mean = jnp.mean(scaled * normed, axis=-1, keepdims=True)
    return rscale * (scaled - first_mean - normed * cross_mean)


def gelu_and_slope(upper):
    below = 0.5 * (1.0 + lax.erf(upper * math.sqrt(0.5)))
    density = jnp.exp(-0.5 * upper * upper) * (1.0 / math.sqrt(2.0 * math.pi))
    return (upper * below).astype(BF16), (below + upper * density).astype(BF16)


def local(
    tokens,
    lengths,
    pair_index,
    query_proj,
    query_bias,
    key_proj,
    value_proj,
    value_bias,
    output_proj,
    output_bias,
    attn_gain,
    attn_shift,
    inner_proj,
    inner_bias,
    outer_proj,
    outer_bias,
    final_gain,
    final_shift,
):
    row_count, width = tokens.shape
    chunk = row_count // 2
    half = chunk // 2
    seq_count = lengths.shape[0]
    pair_count = seq_count // 2
    overall_pair_count = pair_index.shape[0]
    local_width = query_proj.shape[1]
    core = lax.axis_index("mp") % 2
    my_index = lax.axis_index("dp")
    core_arg = jnp.reshape(core, (1,)).astype(jnp.int32)
    attn_gain_f, attn_shift_f = attn_gain.astype(F32), attn_shift.astype(F32)
    final_gain_f, final_shift_f = final_gain.astype(F32), final_shift.astype(F32)
    query_t, key_t, value_t = query_proj.T, key_proj.T, value_proj.T

    seq_ends = jnp.cumsum(lengths)
    seq_starts = seq_ends - lengths
    members = []
    for index in range(2):
        place = jnp.arange(half, dtype=jnp.int32) + index * half + core * chunk
        members.append(
            ((place[None] >= seq_starts[:, None]) & (place[None] < seq_ends[:, None])).astype(F32)
        )
    biases = jnp.stack(
        [jnp.pad(bias.astype(F32), (0, width - local_width)) for bias in (query_bias, value_bias)]
    )

    rows, query_b, key_b, value_b, key_tb, value_tb, mixed_a, lse_a = run_first(
        lengths, core_arg, tokens, query_t, key_t, value_t, biases, (0, 1)
    )

    def own_and_other(values, weights):
        return nn(values[:half], weights), nn(values[half:], weights).astype(BF16)

    def pair(own, arrived):
        return (own + arrived.astype(F32)).astype(BF16)

    def first_norm(index, pair_here, far):
        attn_full = pair_here.astype(F32) + far.astype(F32) + output_bias.astype(F32)
        own_tokens = rows[index * chunk : index * chunk + half].astype(F32)
        return norm_forward(own_tokens + attn_full, attn_gain_f, attn_shift_f)

    def feed_forward(own_hidden):
        whole = both(own_hidden)
        act, slope = gelu_and_slope(nn(whole, inner_proj) + inner_bias.astype(F32))
        return whole, act, slope

    def last_norm(hidden, pair_here, far):
        ffn_full = pair_here.astype(F32) + far.astype(F32) + outer_bias.astype(F32)
        return norm_forward(hidden + ffn_full, final_gain_f, final_shift_f)

    attn_own_a, attn_other_a = own_and_other(mixed_a, output_proj)
    attn_pair_a = pair(attn_own_a, core_swap(attn_other_a))
    attn_far_a = far_swap(attn_pair_a)
    mixed_b, lse_b = run_more(
        lengths, core_arg, after(query_b, attn_pair_a), key_b, value_tb, (2, 3)
    )
    attn_own_b, attn_other_b = own_and_other(mixed_b, output_proj)
    attn_swap_b = core_swap(attn_other_b)
    hidden_a, normed_one_a, rscale_one_a = first_norm(
        0, attn_pair_a, after(attn_far_a, attn_other_b)
    )
    own_hidden_a = hidden_a.astype(BF16)
    attn_pair_b = pair(attn_own_b, after(attn_swap_b, own_hidden_a))
    attn_far_b = far_swap(attn_pair_b)
    hidden_ab, act_a, slope_a = feed_forward(own_hidden_a)
    ffn_own_a, ffn_other_a = own_and_other(act_a, outer_proj)
    ffn_swap_a = core_swap(ffn_other_a)
    hidden_b, normed_one_b, rscale_one_b = first_norm(
        1, attn_pair_b, after(attn_far_b, ffn_other_a)
    )
    own_hidden_b = hidden_b.astype(BF16)
    ffn_pair_a = pair(ffn_own_a, after(ffn_swap_a, own_hidden_b))
    ffn_far_a = far_swap(ffn_pair_a)
    hidden_bb, act_b, slope_b = feed_forward(own_hidden_b)
    ffn_own_b, ffn_other_b = own_and_other(act_b, outer_proj)
    ffn_swap_b = core_swap(ffn_other_b)
    final_a, normed_two_a, rscale_two_a = last_norm(
        hidden_a, ffn_pair_a, after(ffn_far_a, ffn_other_b)
    )
    pooled_a = jnp.dot(members[0], final_a, precision=HIGHEST)
    ffn_pair_b = pair(ffn_own_b, after(ffn_swap_b, pooled_a))
    final_b, normed_two_b, rscale_two_b = last_norm(hidden_b, ffn_pair_b, far_swap(ffn_pair_b))
    pooled_part = pooled_a + jnp.dot(members[1], final_b, precision=HIGHEST)
    mixed, lse = (mixed_a, mixed_b), (lse_a, lse_b)
    hidden_whole, act, slope = (hidden_ab, hidden_bb), (act_a, act_b), (slope_a, slope_b)
    normed_one, rscale_one = (normed_one_a, normed_one_b), (rscale_one_a, rscale_one_b)
    normed_two, rscale_two = (normed_two_a, normed_two_b), (rscale_two_a, rscale_two_b)
    pooled = pooled_part + core_swap(pooled_part)
    pool_rscale = lax.rsqrt(jnp.sum(pooled * pooled, axis=-1, keepdims=True) + EPS_NORM)
    unit_b = (pooled * pool_rscale).astype(BF16)

    piece = lax.dynamic_slice_in_dim(unit_b, core * pair_count, pair_count, 0)
    near = near_swap(piece)
    low = (my_index % 2) == 0
    piece = jnp.concatenate([jnp.where(low, piece, near), jnp.where(low, near, piece)], axis=0)
    piece = share(piece).reshape(overall_pair_count, width)
    swapped = core_swap(piece)
    query_units = jnp.where(core == 0, piece, swapped)
    passage_units = jnp.where(core == 0, swapped, piece)

    backward_scale = 1.0 / (overall_pair_count * SOFTMAX_WARMTH)
    similarity = nt(query_units, passage_units) / SOFTMAX_WARMTH
    query_ids = jnp.arange(overall_pair_count, dtype=jnp.int32)
    is_match = (pair_index[None, :] == query_ids[:, None]).astype(F32)
    top = jnp.max(similarity, axis=1, keepdims=True)
    query_lse = top + jnp.log(jnp.sum(jnp.exp(similarity - top), axis=1, keepdims=True))
    loss_value = (
        jnp.sum(query_lse[:, 0] - jnp.sum(similarity * is_match, axis=1)) / overall_pair_count
    )
    coef = (jnp.exp(similarity - query_lse) - is_match) * backward_scale
    own_start = my_index * pair_count
    coef_query = lax.dynamic_slice_in_dim(coef, own_start, pair_count, 0)
    coef_passage = lax.dynamic_slice_in_dim(coef, own_start, pair_count, 1)
    grad_query = jnp.dot(coef_query, passage_units.astype(F32), precision=HIGHEST)
    grad_passage = lax.dot_general(
        coef_passage, query_units.astype(F32), (((0,), (0,)), ((), ())), precision=HIGHEST
    )
    grad_unit = jnp.concatenate([grad_query, grad_passage], axis=0)
    grad_pooled = (
        pool_rscale * grad_unit
        - pool_rscale**3 * jnp.sum(pooled * grad_unit, axis=-1, keepdims=True) * pooled
    )

    finalgain_part = finalshift_part = outerbias_part = innerbias_part = 0.0
    grad_second, grad_ffn, grad_up, hidden_other = [], [], [], []
    for i in range(2):
        grad_final = jnp.einsum("st,sd->td", members[i], grad_pooled, precision=HIGHEST)
        finalgain_part += jnp.sum(grad_final * normed_two[i], axis=0)
        finalshift_part += jnp.sum(grad_final, axis=0)
        grad_second.append(norm_backward(grad_final, normed_two[i], rscale_two[i], final_gain_f))
        own_grad = grad_second[i].astype(BF16)
        outerbias_part += jnp.sum(own_grad.astype(F32), axis=0)
        grad_ffn.append(both(own_grad))
        grad_up.append((nt(grad_ffn[i], outer_proj) * slope[i].astype(F32)).astype(BF16))
        innerbias_part += jnp.sum(grad_up[i].astype(F32), axis=0)
        hidden_other.append(core_swap(nt(grad_up[i][half:], inner_proj).astype(BF16)))
    hidden_pair = [pair(nt(grad_up[i][:half], inner_proj), hidden_other[i]) for i in range(2)]
    hidden_far = [far_swap(hidden_pair[i]) for i in range(2)]
    late_act, late_hidden = after((act, hidden_whole), hidden_pair)
    ffn_pack = jnp.concatenate(
        [
            (tn(late_act[0], grad_ffn[0]) + tn(late_act[1], grad_ffn[1])).astype(BF16),
            (tn(late_hidden[0], grad_up[0]) + tn(late_hidden[1], grad_up[1])).astype(BF16),
        ],
        axis=0,
    ).reshape(16, -1, width)
    ffn_parts = trade(ffn_pack)

    attngain_part = attnshift_part = outputbias_part = 0.0
    grad_first, grad_attn = [], []
    hidden_far = after(hidden_far, ffn_pack)
    for i in range(2):
        grad_hidden = grad_second[i] + (hidden_pair[i].astype(F32) + hidden_far[i].astype(F32))
        attngain_part += jnp.sum(grad_hidden * normed_one[i], axis=0)
        attnshift_part += jnp.sum(grad_hidden, axis=0)
        grad_first.append(norm_backward(grad_hidden, normed_one[i], rscale_one[i], attn_gain_f))
        own_grad = grad_first[i].astype(BF16)
        outputbias_part += jnp.sum(own_grad.astype(F32), axis=0)
        grad_attn += [own_grad, core_swap(own_grad)]
    paired = jnp.stack(
        [
            outputbias_part,
            attngain_part,
            attnshift_part,
            outerbias_part,
            finalgain_part,
            finalshift_part,
        ],
        axis=0,
    )
    paired = paired + core_swap(paired)
    vectors = jnp.concatenate(
        [paired, innerbias_part[None], jnp.zeros((1, width), F32)], axis=0
    )
    grad_query, grad_key, grad_value, packed = run_back(
        lengths,
        core_arg,
        grad_attn,
        mixed,
        lse,
        output_proj,
        query_b,
        key_b,
        value_b,
        key_tb,
        vectors,
        rows,
    )
    packed, ffn_parts = lax.optimization_barrier((packed, ffn_parts))
    packed_parts = trade(packed)
    ffn_reduced = sum_parts(ffn_parts)
    ffn_sum = lax.all_gather(ffn_reduced, "dp", axis_index_groups=PLANES, axis=0, tiled=True)
    late_query = after(grad_query, ffn_reduced)

    def input_part(first):
        span = slice(first, first + half)
        return (
            nt(late_query[span], query_proj)
            + nt(grad_key[span], key_proj)
            + nt(grad_value[span], value_proj)
        )

    token_other = [core_swap(input_part(i * chunk + half).astype(BF16)) for i in range(2)]
    token_pair = [pair(input_part(i * chunk), token_other[i]) for i in range(2)]
    token_far = [far_swap(token_pair[i]) for i in range(2)]
    packed_reduced = sum_parts(after(packed_parts, token_pair))
    token_far = after(token_far, packed_reduced, ffn_sum)
    token_own = [
        (grad_first[i] + (token_pair[i].astype(F32) + token_far[i].astype(F32))).astype(BF16)
        for i in range(2)
    ]
    own_rows = jnp.concatenate(token_own, axis=0)
    other_rows = core_swap(own_rows)
    token_grad = jnp.where(
        core == 0,
        jnp.concatenate([own_rows, other_rows], axis=0),
        jnp.concatenate([other_rows, own_rows], axis=0),
    )
    packed = share(packed_reduced).astype(F32)
    ffn_sum = ffn_sum.astype(F32)
    piece_rows = packed.shape[1] - 8
    cuts = packed[:, :piece_rows].reshape(4, local_width, width)
    vectors = packed[0, piece_rows:]
    return (
        loss_value,
        token_grad,
        cuts[0].T,
        vectors[7, :local_width],
        cuts[1].T,
        cuts[2].T,
        vectors[7, 256 : 256 + local_width],
        cuts[3],
        vectors[0],
        vectors[1],
        vectors[2],
        ffn_sum[width:],
        vectors[6],
        ffn_sum[:width],
        vectors[3],
        vectors[4],
        vectors[5],
    )


def solution(mesh):
    column, row, split = P(None, "mp"), P("mp", None), P("mp")
    placed = (
        (P("dp", None), P("dp"), P())
        + (column, split, column, column, split, row)
        + (P(), P(), P())
        + (column, split, row)
        + (P(), P(), P())
    )
    given = (
        (P(), P("dp", None))
        + (column, split, column, column, split, row)
        + (P(), P(), P())
        + (column, split, row)
        + (P(), P(), P())
    )
    return jax.shard_map(local, mesh=mesh, in_specs=placed, out_specs=given, check_vma=False)
```

```python
import functools
import math

import jax
import jax.numpy as jnp
from jax import lax
from jax.experimental import pallas as pl
from jax.experimental.pallas import tpu as pltpu
from jax.sharding import PartitionSpec as P

HD = 64
EPS_NORM = 1e-06
SOFTMAX_WARMTH = 0.01
NEG_FILL = -1e30
HIGHEST = lax.Precision.HIGHEST
F32 = jnp.float32
BF16 = jnp.bfloat16
QB = 256
KB = 128

CORE_SWAP = [(i, i ^ 1) for i in range(4)]
FAR_SWAP = [(i, i ^ 2) for i in range(4)]
NEAR_SWAP = [(i, i ^ 1) for i in range(32)]
PLANES = [[i * 2 + x for i in range(16)] for x in range(2)]

SMEM = pl.BlockSpec(memory_space=pltpu.SMEM)
VMEM = pl.BlockSpec(memory_space=pltpu.VMEM)
HBM = pl.BlockSpec(memory_space=pltpu.HBM)


def nn(left, right):
    return lax.dot_general(left, right, (((1,), (0,)), ((), ())), preferred_element_type=F32)


def nt(left, right):
    return lax.dot_general(left, right, (((1,), (1,)), ((), ())), preferred_element_type=F32)


def tn(left, right):
    return lax.dot_general(left, right, (((0,), (0,)), ((), ())), preferred_element_type=F32)


def place_of_block(block, core, rows):
    return ((block % 2) * 2 + block // 2) * QB + core * (rows // 2) & (rows - 1)


def spot_of_keys(j, core, rows):
    place = (j * KB + core * (rows // 2)) & (rows - 1)
    block = place // QB
    return pl.multiple_of(((block % 2) * 2 + block // 2) * QB + place % QB, KB)


def segment_bounds(lengths_ref):
    bounds, total = [], jnp.int32(0)
    for s in range(lengths_ref.shape[0]):
        start = total
        total = total + lengths_ref[s]
        bounds.append((start, total))
    return bounds


def block_span(bounds, first, rows):
    place = first + lax.broadcasted_iota(jnp.int32, (1, QB), 1)
    low, high = first, first + KB
    begin = jnp.full((1, QB), bounds[-1][1], jnp.int32)
    end = jnp.full((1, QB), rows, jnp.int32)
    for start, stop in bounds:
        inside = (place >= start) & (place < stop)
        begin = jnp.where(inside, start, begin)
        end = jnp.where(inside, stop, end)
        touches = (stop > first) & (start < first + QB) & (stop > start)
        low = jnp.where(touches, jnp.minimum(low, start), low)
        high = jnp.where(touches, jnp.maximum(high, stop), high)
    return low // KB, (high + KB - 1) // KB, begin, end


def head_copies(values, heads):
    lane = lax.broadcasted_iota(jnp.int32, values.shape, 1) // HD
    blank = jnp.zeros_like(values)
    return jnp.concatenate([jnp.where(lane == h, values, blank) for h in range(heads)], axis=0)


def span_mask(begin, end, block, heads):
    place = block * KB + lax.broadcasted_iota(jnp.int32, (KB, QB), 0)
    keep = (place >= begin) & (place < end)
    return jnp.concatenate([keep] * heads, axis=1)


def attend(heads, blocks, core, bounds, q_ref, k_ref, vt_ref, mixed_ref, lse_ref, acc_ref):
    rows = k_ref.shape[0]
    for i, block in enumerate(blocks):
        low, high, begin, end = block_span(bounds, place_of_block(block, core, rows), rows)
        stack = head_copies(q_ref[block * QB : (block + 1) * QB, :], heads)
        acc_ref[...] = jnp.zeros(acc_ref.shape, F32)

        def step(j, carry, stack=stack, begin=begin, end=end):
            top, total = carry
            spot = spot_of_keys(j, core, rows)
            scores = nt(k_ref[pl.ds(spot, KB), :], stack)
            scores = jnp.where(span_mask(begin, end, j, heads), scores, NEG_FILL)
            peak = jnp.maximum(top, jnp.max(scores, axis=0, keepdims=True))
            fade = jnp.exp(top - peak)
            probs = jnp.exp(scores - peak)
            total = total * fade + jnp.sum(probs, axis=0, keepdims=True)
            probs = probs.astype(BF16)
            for h in range(heads):
                part = slice(h * QB, (h + 1) * QB)
                span = slice(h * HD, (h + 1) * HD)
                acc_ref[span, :] = acc_ref[span, :] * fade[:, part] + nn(
                    vt_ref[span, pl.ds(spot, KB)], probs[:, part]
                )
            return peak, total

        top = jnp.full((1, heads * QB), NEG_FILL, F32)
        top, total = lax.fori_loop(
            low, high, step, (top, jnp.zeros((1, heads * QB), F32)), unroll=False
        )
        scale = 1.0 / total
        mixed = jnp.concatenate(
            [
                acc_ref[h * HD : (h + 1) * HD, :] * scale[:, h * QB : (h + 1) * QB]
                for h in range(heads)
            ],
            axis=0,
        )
        mixed_ref[i * QB : (i + 1) * QB, :] = mixed.T.astype(BF16)
        lse_ref[i, :, :] = jnp.broadcast_to(top + jnp.log(total), (8, heads * QB))


def fetch(sources, targets, semaphores):
    copies = [
        pltpu.make_async_copy(source, target, semaphores.at[i])
        for i, (source, target) in enumerate(zip(sources, targets))
    ]
    for copy in copies:
        copy.start()
    return copies


def attend_first(
    heads,
    blocks,
    lengths_ref,
    core_ref,
    tokens_hbm,
    wqt_hbm,
    wkt_hbm,
    wvt_hbm,
    vectors_hbm,
    *refs,
):
    outputs, refs = refs[:8], refs[8:]
    x_ref, q_ref, k_ref, v_ref, kt_ref, vt_ref, mixed_ref, lse_ref = refs[:8]
    acc_ref, wqt_ref, wkt_ref, wvt_ref, vectors_ref, semaphores, out_semaphores = refs[8:]
    rows = x_ref.shape[0]
    width = heads * HD
    core = core_ref[0]
    sources = [vectors_hbm, wqt_hbm]
    targets = [vectors_ref, wqt_ref]
    for block in range(rows // QB):
        first = pl.multiple_of(place_of_block(block, core, rows), QB)
        sources.append(tokens_hbm.at[pl.ds(first, QB), :])
        targets.append(x_ref.at[pl.ds(block * QB, QB), :])
    copies = fetch(sources + [wkt_hbm, wvt_hbm], targets + [wkt_ref, wvt_ref], semaphores)
    for copy in copies:
        copy.wait()
    query_bias = vectors_ref[0:1, :width]
    value_bias = vectors_ref[1:2, :width]
    for block in range(rows // QB):
        part = slice(block * QB, (block + 1) * QB)
        x = x_ref[part, :]
        q = (nt(x, wqt_ref[...]) + query_bias).astype(BF16)
        q_ref[part, :] = q * BF16(0.125)
        k_ref[part, :] = nt(x, wkt_ref[...]).astype(BF16)
        kt_ref[:, part] = nt(wkt_ref[...], x).astype(BF16)
        v = nt(x, wvt_ref[...]) + value_bias
        v_ref[part, :] = v.astype(BF16)
        vt_ref[:, part] = v.T.astype(BF16)
    copies = fetch(refs[:6], outputs[:6], out_semaphores)
    bounds = segment_bounds(lengths_ref)
    attend(heads, blocks, core, bounds, q_ref, k_ref, vt_ref, mixed_ref, lse_ref, acc_ref)
    copies += fetch(refs[6:8], outputs[6:], out_semaphores.at[6:8])
    for copy in copies:
        copy.wait()


def attend_more(heads, blocks, lengths_ref, core_ref, *refs):
    sources, outputs, refs = refs[:3], refs[3:5], refs[5:]
    q_ref, k_ref, vt_ref, mixed_ref, lse_ref, acc_ref, semaphores = refs
    for copy in fetch(sources, refs[:3], semaphores):
        copy.wait()
    bounds = segment_bounds(lengths_ref)
    attend(heads, blocks, core_ref[0], bounds, q_ref, k_ref, vt_ref, mixed_ref, lse_ref, acc_ref)
    for copy in fetch(refs[3:5], outputs, semaphores.at[3:5]):
        copy.wait()


def attend_back(heads, inputs, lengths_ref, core_ref, *refs):
    sources, refs = refs[:inputs], refs[inputs:]
    outputs, refs = refs[:4], refs[4:]
    gq_ref, gk_ref, gv_ref, pack_ref = refs[:4]
    dk_ref, dv_ref, dqt_ref, wo_acc_ref, semaphores, out_semaphores = refs[4:10]
    targets = refs[10:]
    copies = fetch(sources, targets, semaphores)
    grads = targets[0:4]
    mixed = targets[4:6]
    lses = targets[6:8]
    wo_ref, q_ref, k_ref, v_ref, kt_ref, vectors_ref, x_ref = targets[8:]
    rows, width = q_ref.shape
    core = core_ref[0]
    bounds = segment_bounds(lengths_ref)
    dk_ref[...] = jnp.zeros(dk_ref.shape, F32)
    dv_ref[...] = jnp.zeros(dv_ref.shape, F32)
    lane = lax.broadcasted_iota(jnp.int32, (8, width), 1) // HD
    which = (lane == lax.broadcasted_iota(jnp.int32, (8, width), 0)).astype(F32)
    for i in (0, 4, 6, 8, 9, 10, 11, 12):
        copies[i].wait()
    for block in range(rows // QB):
        if block > 0:
            copies[block].wait()
        if block == 2:
            copies[5].wait()
            copies[7].wait()
        low, high, begin, end = block_span(bounds, place_of_block(block, core, rows), rows)
        part = slice(block * QB, (block + 1) * QB)
        own = slice(block % 2 * QB, block % 2 * QB + QB)
        grad_attn = grads[block][...]
        mixed_here = mixed[block // 2][own, :]
        outer = tn(mixed_here, grad_attn)
        wo_acc_ref[...] = outer if block == 0 else wo_acc_ref[...] + outer
        grad_mixed = nt(grad_attn, wo_ref[...]).astype(BF16)
        product = grad_mixed.astype(F32) * mixed_here.astype(F32)
        sums = lax.dot_general(
            which,
            product,
            (((1,), (1,)), ((), ())),
            precision=HIGHEST,
            preferred_element_type=F32,
        )
        delta = jnp.concatenate([sums[h : h + 1, :] for h in range(heads)], axis=1)
        lse = lses[block // 2][block % 2, 0:1, :]
        q_stack = head_copies(q_ref[part, :], heads)
        g_stack = head_copies(grad_mixed, heads)
        dqt_ref[...] = jnp.zeros(dqt_ref.shape, F32)

        def step(
            j, carry, delta=delta, lse=lse, q_stack=q_stack, g_stack=g_stack, begin=begin, end=end
        ):
            here = pl.ds(spot_of_keys(j, core, rows), KB)
            scores = nt(k_ref[here, :], q_stack)
            scores = jnp.where(span_mask(begin, end, j, heads), scores, NEG_FILL)
            probs = jnp.exp(scores - lse)
            grad = (probs * (nt(v_ref[here, :], g_stack) - delta)).astype(BF16)
            dv_ref[here, :] += nn(probs.astype(BF16), g_stack)
            dk_ref[here, :] += nn(grad, q_stack)
            for h in range(heads):
                span = slice(h * HD, (h + 1) * HD)
                dqt_ref[span, :] += nn(kt_ref[span, here], grad[:, h * QB : (h + 1) * QB])
            return carry

        lax.fori_loop(low, high, step, 0, unroll=False)
        gq_ref[part, :] = (dqt_ref[...].T * 0.125).astype(BF16)
    gk_ref[...] = dk_ref[...].astype(BF16)
    gv_ref[...] = dv_ref[...].astype(BF16)
    copies[13].wait()
    copies[14].wait()
    outgoing = fetch(refs[:3], outputs[:3], out_semaphores)
    sums = [jnp.sum(ref[...].astype(F32), axis=0, keepdims=True) for ref in (gq_ref, gv_ref)]
    blank = jnp.zeros((1, 256 - width), F32)
    tail = jnp.concatenate([sums[0], blank, sums[1], blank, jnp.zeros((1, 256), F32)], axis=1)
    small = jnp.concatenate([vectors_ref[0:7, :], tail], axis=0).astype(BF16)
    piece = pack_ref.shape[1] - 8
    per = width // piece
    for m, source in enumerate((None, gq_ref, gk_ref, gv_ref)):
        total = wo_acc_ref[...] if source is None else tn(source[...], x_ref[...])
        for t in range(per):
            cut = total[t * piece : (t + 1) * piece, :].astype(BF16)
            pack_ref[m * per + t, 0:piece, :] = cut
            pack_ref[m * per + t, piece:, :] = small if m + t == 0 else jnp.zeros_like(small)
        here = pl.ds(m * per, per)
        copy = pltpu.make_async_copy(
            pack_ref.at[here], outputs[3].at[here], out_semaphores.at[3 + m]
        )
        copy.start()
        outgoing.append(copy)
    for copy in outgoing:
        copy.wait()


def shaped(shape, dtype):
    return jax.ShapeDtypeStruct(shape, dtype)


PARAMS = pltpu.CompilerParams(vmem_limit_bytes=24 << 20)
COST = pl.CostEstimate(flops=1024, bytes_accessed=1024, transcendentals=0)


def buffers(arrays):
    return [pltpu.VMEM(array.shape, array.dtype) for array in arrays]


def run_first(lengths, core, tokens, wqt, wkt, wvt, vectors, blocks):
    rows, width = tokens.shape[0], wqt.shape[0]
    heads, count = width // HD, len(blocks)
    outs = (
        (shaped(tokens.shape, BF16),)
        + (shaped((rows, width), BF16),) * 3
        + (shaped((width, rows), BF16),) * 2
        + (shaped((count * QB, width), BF16), shaped((count, 8, heads * QB), F32))
    )
    return pl.pallas_call(
        functools.partial(attend_first, heads, blocks),
        out_shape=outs,
        in_specs=[SMEM] * 2 + [HBM] * 5,
        out_specs=(HBM,) * 8,
        scratch_shapes=buffers(outs)
        + [pltpu.VMEM((width, QB), F32)]
        + buffers((wqt, wkt, wvt, vectors))
        + [pltpu.SemaphoreType.DMA((4 + rows // QB,)), pltpu.SemaphoreType.DMA((8,))],
        compiler_params=PARAMS,
        name="attend_first",
        cost_estimate=COST,
    )(lengths, core, tokens, wqt, wkt, wvt, vectors)


def run_more(lengths, core, q, k, vt, blocks):
    rows, width = q.shape
    heads, count = width // HD, len(blocks)
    outs = (shaped((count * QB, width), BF16), shaped((count, 8, heads * QB), F32))
    return pl.pallas_call(
        functools.partial(attend_more, heads, blocks),
        out_shape=outs,
        in_specs=[SMEM] * 2 + [HBM] * 3,
        out_specs=(HBM,) * 2,
        scratch_shapes=buffers((q, k, vt, *outs))
        + [pltpu.VMEM((width, QB), F32), pltpu.SemaphoreType.DMA((5,))],
        compiler_params=PARAMS,
        name="attend_more",
        cost_estimate=COST,
    )(lengths, core, q, k, vt)


def run_back(lengths, core, grads, mixed, lses, wo, q, k, v, kt, vectors, x):
    rows, width = q.shape
    heads = width // HD
    arrays = (*grads, *mixed, *lses, wo, q, k, v, kt, vectors, x)
    piece = 4 * width // 16
    outs = (shaped((rows, width), BF16),) * 3 + (shaped((16, piece + 8, x.shape[1]), BF16),)
    return pl.pallas_call(
        functools.partial(attend_back, heads, len(arrays)),
        out_shape=outs,
        in_specs=[SMEM] * 2 + [HBM] * len(arrays),
        out_specs=(HBM,) * 4,
        scratch_shapes=buffers(outs)
        + [pltpu.VMEM((rows, width), F32)] * 2
        + [pltpu.VMEM((width, QB), F32), pltpu.VMEM(wo.shape, F32)]
        + [pltpu.SemaphoreType.DMA((len(arrays),)), pltpu.SemaphoreType.DMA((7,))]
        + buffers(arrays),
        compiler_params=PARAMS,
        name="attend_back",
        cost_estimate=COST,
    )(lengths, core, *arrays)


def trade(values):
    return lax.all_to_all(
        values, "dp", split_axis=0, concat_axis=0, axis_index_groups=PLANES, tiled=True
    )


def share(values):
    return trade(jnp.broadcast_to(values[None], (16,) + values.shape))


def ring_shift(axis, step):
    pairs = []
    for i in range(32):
        z, y, x = i // 8, (i // 2) % 4, i % 2
        z, y = ((z + step) % 4, y) if axis == "z" else (z, (y + step) % 4)
        pairs.append((i, (z * 4 + y) * 2 + x))
    return pairs


def ring_pieces(values, axis):
    return [lax.ppermute(values, "dp", ring_shift(axis, step)) for step in (2, 1, 3)]


def ring_whole(values, pieces, axis, dtype):
    index = lax.axis_index("dp")
    place = index // 8 if axis == "z" else (index // 2) % 4
    whole = jnp.zeros((4,) + values.shape, dtype)
    whole = lax.dynamic_update_index_in_dim(whole, values.astype(dtype), place, 0)
    for step, piece in zip((2, 1, 3), pieces):
        whole = lax.dynamic_update_index_in_dim(
            whole, piece.astype(dtype), (place - step) % 4, 0
        )
    return whole


def near_swap(values):
    return lax.ppermute(values, "dp", NEAR_SWAP)


def sum_parts(parts):
    total = jnp.sum(parts.astype(F32), axis=0).astype(BF16)
    return (total.astype(F32) + near_swap(total).astype(F32)).astype(BF16)


def core_swap(values):
    return lax.ppermute(values, "mp", CORE_SWAP)


def far_swap(values):
    return lax.ppermute(values, "mp", FAR_SWAP)


def after(values, *others):
    return lax.optimization_barrier((values, others))[0]


def both(own):
    return jnp.concatenate([own, core_swap(own)], axis=0)


def norm_forward(values, gain_vec, shift_vec):
    average = jnp.mean(values, axis=-1, keepdims=True)
    centred = values - average
    rscale = lax.rsqrt(jnp.mean(centred * centred, axis=-1, keepdims=True) + EPS_NORM)
    normed = centred * rscale
    return (normed * gain_vec + shift_vec, normed, rscale)


def norm_backward(grad_out, normed, rscale, gain_vec):
    scaled = grad_out * gain_vec
    first_mean = jnp.mean(scaled, axis=-1, keepdims=True)
    cross_mean = jnp.mean(scaled * normed, axis=-1, keepdims=True)
    return rscale * (scaled - first_mean - normed * cross_mean)


def gelu_and_slope(upper):
    below = 0.5 * (1.0 + lax.erf(upper * math.sqrt(0.5)))
    density = jnp.exp(-0.5 * upper * upper) * (1.0 / math.sqrt(2.0 * math.pi))
    return (upper * below).astype(BF16), (below + upper * density).astype(BF16)


def local(
    tokens,
    lengths,
    pair_index,
    query_proj,
    query_bias,
    key_proj,
    value_proj,
    value_bias,
    output_proj,
    output_bias,
    attn_gain,
    attn_shift,
    inner_proj,
    inner_bias,
    outer_proj,
    outer_bias,
    final_gain,
    final_shift,
):
    row_count, width = tokens.shape
    chunk = row_count // 2
    half = chunk // 2
    seq_count = lengths.shape[0]
    pair_count = seq_count // 2
    overall_pair_count = pair_index.shape[0]
    local_width = query_proj.shape[1]
    core = lax.axis_index("mp") % 2
    my_index = lax.axis_index("dp")
    core_arg = jnp.reshape(core, (1,)).astype(jnp.int32)
    attn_gain_f, attn_shift_f = attn_gain.astype(F32), attn_shift.astype(F32)
    final_gain_f, final_shift_f = final_gain.astype(F32), final_shift.astype(F32)
    query_t, key_t, value_t = query_proj.T, key_proj.T, value_proj.T

    seq_ends = jnp.cumsum(lengths)
    seq_starts = seq_ends - lengths
    members = []
    for index in range(2):
        place = jnp.arange(half, dtype=jnp.int32) + index * half + core * chunk
        members.append(
            ((place[None] >= seq_starts[:, None]) & (place[None] < seq_ends[:, None])).astype(F32)
        )
    biases = jnp.stack(
        [jnp.pad(bias.astype(F32), (0, width - local_width)) for bias in (query_bias, value_bias)]
    )

    rows, query_b, key_b, value_b, key_tb, value_tb, mixed_a, lse_a = run_first(
        lengths, core_arg, tokens, query_t, key_t, value_t, biases, (0, 1)
    )

    def own_and_other(values, weights):
        return nn(values[:half], weights), nn(values[half:], weights).astype(BF16)

    def pair(own, arrived):
        return (own + arrived.astype(F32)).astype(BF16)

    def first_norm(index, pair_here, far):
        attn_full = pair_here.astype(F32) + far.astype(F32) + output_bias.astype(F32)
        own_tokens = rows[index * chunk : index * chunk + half].astype(F32)
        return norm_forward(own_tokens + attn_full, attn_gain_f, attn_shift_f)

    def feed_forward(own_hidden):
        whole = both(own_hidden)
        act, slope = gelu_and_slope(nn(whole, inner_proj) + inner_bias.astype(F32))
        return whole, act, slope

    def last_norm(hidden, pair_here, far):
        ffn_full = pair_here.astype(F32) + far.astype(F32) + outer_bias.astype(F32)
        return norm_forward(hidden + ffn_full, final_gain_f, final_shift_f)

    attn_own_a, attn_other_a = own_and_other(mixed_a, output_proj)
    attn_pair_a = pair(attn_own_a, core_swap(attn_other_a))
    attn_far_a = far_swap(attn_pair_a)
    mixed_b, lse_b = run_more(
        lengths, core_arg, after(query_b, attn_pair_a), key_b, value_tb, (2, 3)
    )
    attn_own_b, attn_other_b = own_and_other(mixed_b, output_proj)
    attn_swap_b = core_swap(attn_other_b)
    hidden_a, normed_one_a, rscale_one_a = first_norm(
        0, attn_pair_a, after(attn_far_a, attn_other_b)
    )
    own_hidden_a = hidden_a.astype(BF16)
    attn_pair_b = pair(attn_own_b, after(attn_swap_b, own_hidden_a))
    attn_far_b = far_swap(attn_pair_b)
    hidden_ab, act_a, slope_a = feed_forward(own_hidden_a)
    ffn_own_a, ffn_other_a = own_and_other(act_a, outer_proj)
    ffn_swap_a = core_swap(ffn_other_a)
    hidden_b, normed_one_b, rscale_one_b = first_norm(
        1, attn_pair_b, after(attn_far_b, ffn_other_a)
    )
    own_hidden_b = hidden_b.astype(BF16)
    ffn_pair_a = pair(ffn_own_a, after(ffn_swap_a, own_hidden_b))
    ffn_far_a = far_swap(ffn_pair_a)
    hidden_bb, act_b, slope_b = feed_forward(own_hidden_b)
    ffn_own_b, ffn_other_b = own_and_other(act_b, outer_proj)
    ffn_swap_b = core_swap(ffn_other_b)
    final_a, normed_two_a, rscale_two_a = last_norm(
        hidden_a, ffn_pair_a, after(ffn_far_a, ffn_other_b)
    )
    pooled_a = jnp.dot(members[0], final_a, precision=HIGHEST)
    ffn_pair_b = pair(ffn_own_b, after(ffn_swap_b, pooled_a))
    final_b, normed_two_b, rscale_two_b = last_norm(hidden_b, ffn_pair_b, far_swap(ffn_pair_b))
    pooled_part = pooled_a + jnp.dot(members[1], final_b, precision=HIGHEST)
    mixed, lse = (mixed_a, mixed_b), (lse_a, lse_b)
    hidden_whole, act, slope = (hidden_ab, hidden_bb), (act_a, act_b), (slope_a, slope_b)
    normed_one, rscale_one = (normed_one_a, normed_one_b), (rscale_one_a, rscale_one_b)
    normed_two, rscale_two = (normed_two_a, normed_two_b), (rscale_two_a, rscale_two_b)
    pooled = pooled_part + core_swap(pooled_part)
    pool_rscale = lax.rsqrt(jnp.sum(pooled * pooled, axis=-1, keepdims=True) + EPS_NORM)
    unit_b = (pooled * pool_rscale).astype(BF16)

    piece = lax.dynamic_slice_in_dim(unit_b, core * pair_count, pair_count, 0)
    near = near_swap(piece)
    low = (my_index % 2) == 0
    piece = jnp.concatenate([jnp.where(low, piece, near), jnp.where(low, near, piece)], axis=0)
    piece = share(piece).reshape(overall_pair_count, width)
    swapped = core_swap(piece)
    query_units = jnp.where(core == 0, piece, swapped)
    passage_units = jnp.where(core == 0, swapped, piece)

    backward_scale = 1.0 / (overall_pair_count * SOFTMAX_WARMTH)
    similarity = nt(query_units, passage_units) / SOFTMAX_WARMTH
    query_ids = jnp.arange(overall_pair_count, dtype=jnp.int32)
    is_match = (pair_index[None, :] == query_ids[:, None]).astype(F32)
    top = jnp.max(similarity, axis=1, keepdims=True)
    query_lse = top + jnp.log(jnp.sum(jnp.exp(similarity - top), axis=1, keepdims=True))
    loss_value = (
        jnp.sum(query_lse[:, 0] - jnp.sum(similarity * is_match, axis=1)) / overall_pair_count
    )
    coef = (jnp.exp(similarity - query_lse) - is_match) * backward_scale
    own_start = my_index * pair_count
    coef_query = lax.dynamic_slice_in_dim(coef, own_start, pair_count, 0)
    coef_passage = lax.dynamic_slice_in_dim(coef, own_start, pair_count, 1)
    grad_query = jnp.dot(coef_query, passage_units.astype(F32), precision=HIGHEST)
    grad_passage = lax.dot_general(
        coef_passage, query_units.astype(F32), (((0,), (0,)), ((), ())), precision=HIGHEST
    )
    grad_unit = jnp.concatenate([grad_query, grad_passage], axis=0)
    grad_pooled = (
        pool_rscale * grad_unit
        - pool_rscale**3 * jnp.sum(pooled * grad_unit, axis=-1, keepdims=True) * pooled
    )

    finalgain_part = finalshift_part = outerbias_part = innerbias_part = 0.0
    grad_second, grad_ffn, grad_up, hidden_other = [], [], [], []
    for i in range(2):
        grad_final = jnp.einsum("st,sd->td", members[i], grad_pooled, precision=HIGHEST)
        finalgain_part += jnp.sum(grad_final * normed_two[i], axis=0)
        finalshift_part += jnp.sum(grad_final, axis=0)
        grad_second.append(norm_backward(grad_final, normed_two[i], rscale_two[i], final_gain_f))
        own_grad = grad_second[i].astype(BF16)
        outerbias_part += jnp.sum(own_grad.astype(F32), axis=0)
        grad_ffn.append(both(own_grad))
        grad_up.append((nt(grad_ffn[i], outer_proj) * slope[i].astype(F32)).astype(BF16))
        innerbias_part += jnp.sum(grad_up[i].astype(F32), axis=0)
        hidden_other.append(core_swap(nt(grad_up[i][half:], inner_proj).astype(BF16)))
    hidden_pair = [pair(nt(grad_up[i][:half], inner_proj), hidden_other[i]) for i in range(2)]
    hidden_far = [far_swap(hidden_pair[i]) for i in range(2)]
    late_act, late_hidden = after((act, hidden_whole), hidden_pair)
    ffn_pack = jnp.concatenate(
        [
            (tn(late_act[0], grad_ffn[0]) + tn(late_act[1], grad_ffn[1])).astype(BF16),
            (tn(late_hidden[0], grad_up[0]) + tn(late_hidden[1], grad_up[1])).astype(BF16),
        ],
        axis=0,
    ).reshape(16, -1, width)
    ffn_parts = trade(ffn_pack)

    attngain_part = attnshift_part = outputbias_part = 0.0
    grad_first, grad_attn = [], []
    hidden_far = after(hidden_far, ffn_pack)
    for i in range(2):
        grad_hidden = grad_second[i] + (hidden_pair[i].astype(F32) + hidden_far[i].astype(F32))
        attngain_part += jnp.sum(grad_hidden * normed_one[i], axis=0)
        attnshift_part += jnp.sum(grad_hidden, axis=0)
        grad_first.append(norm_backward(grad_hidden, normed_one[i], rscale_one[i], attn_gain_f))
        own_grad = grad_first[i].astype(BF16)
        outputbias_part += jnp.sum(own_grad.astype(F32), axis=0)
        grad_attn += [own_grad, core_swap(own_grad)]
    paired = jnp.stack(
        [
            outputbias_part,
            attngain_part,
            attnshift_part,
            outerbias_part,
            finalgain_part,
            finalshift_part,
        ],
        axis=0,
    )
    paired = paired + core_swap(paired)
    vectors = jnp.concatenate(
        [paired, innerbias_part[None], jnp.zeros((1, width), F32)], axis=0
    )
    grad_query, grad_key, grad_value, packed = run_back(
        lengths,
        core_arg,
        grad_attn,
        mixed,
        lse,
        output_proj,
        query_b,
        key_b,
        value_b,
        key_tb,
        vectors,
        rows,
    )
    grad_query, packed, ffn_parts = lax.optimization_barrier((grad_query, packed, ffn_parts))
    packed_parts = trade(packed)
    ffn_reduced = sum_parts(ffn_parts)
    grad_query = after(grad_query, ffn_reduced)

    def input_part(first):
        span = slice(first, first + half)
        return (
            nt(grad_query[span], query_proj)
            + nt(grad_key[span], key_proj)
            + nt(grad_value[span], value_proj)
        )

    token_other = [input_part(i * chunk + half).astype(BF16) for i in range(2)]
    token_pair = [pair(input_part(i * chunk), core_swap(token_other[i])) for i in range(2)]
    token_far = [far_swap(token_pair[i]) for i in range(2)]
    ffn_ring = ring_whole(ffn_reduced, ring_pieces(ffn_reduced, "y"), "y", BF16)
    ffn_pieces = ring_pieces(ffn_ring, "z")
    packed_reduced = sum_parts(after(packed_parts, token_far[0], ffn_ring))
    packed_sum = share(packed_reduced)
    token_own = [
        (grad_first[i] + (token_pair[i].astype(F32) + token_far[i].astype(F32))).astype(BF16)
        for i in range(2)
    ]
    own_rows = jnp.concatenate(after(token_own, packed_sum), axis=0)
    ffn_sum = ring_whole(ffn_ring, ffn_pieces, "z", F32)
    other_rows = core_swap(own_rows)
    token_grad = jnp.where(
        core == 0,
        jnp.concatenate([own_rows, other_rows], axis=0),
        jnp.concatenate([other_rows, own_rows], axis=0),
    )
    packed = packed_sum.astype(F32)
    ffn_sum = ffn_sum.reshape(2 * width, width)
    piece_rows = packed.shape[1] - 8
    cuts = packed[:, :piece_rows].reshape(4, local_width, width)
    vectors = packed[0, piece_rows:]
    return (
        loss_value,
        token_grad,
        cuts[1].T,
        vectors[7, :local_width],
        cuts[2].T,
        cuts[3].T,
        vectors[7, 256 : 256 + local_width],
        cuts[0],
        vectors[0],
        vectors[1],
        vectors[2],
        ffn_sum[width:],
        vectors[6],
        ffn_sum[:width],
        vectors[3],
        vectors[4],
        vectors[5],
    )


def solution(mesh):
    column, row, split = P(None, "mp"), P("mp", None), P("mp")
    placed = (
        (P("dp", None), P("dp"), P())
        + (column, split, column, column, split, row)
        + (P(), P(), P())
        + (column, split, row)
        + (P(), P(), P())
    )
    given = (
        (P(), P("dp", None))
        + (column, split, column, column, split, row)
        + (P(), P(), P())
        + (column, split, row)
        + (P(), P(), P())
    )
    return jax.shard_map(local, mesh=mesh, in_specs=placed, out_specs=given, check_vma=False)
```

```python
import functools
import math

import jax
import jax.numpy as jnp
from jax import lax
from jax.experimental import pallas as pl
from jax.experimental.pallas import tpu as pltpu
from jax.sharding import PartitionSpec as P

HD = 64
EPS_NORM = 1e-06
SOFTMAX_WARMTH = 0.01
NEG_FILL = -1e30
HIGHEST = lax.Precision.HIGHEST
F32 = jnp.float32
BF16 = jnp.bfloat16
QB = 256
KB = 128

CORE_SWAP = [(i, i ^ 1) for i in range(4)]
FAR_SWAP = [(i, i ^ 2) for i in range(4)]
NEAR_SWAP = [(i, i ^ 1) for i in range(32)]
PLANES = [[i * 2 + x for i in range(16)] for x in range(2)]

SMEM = pl.BlockSpec(memory_space=pltpu.SMEM)
VMEM = pl.BlockSpec(memory_space=pltpu.VMEM)
HBM = pl.BlockSpec(memory_space=pltpu.HBM)


def nn(left, right):
    return lax.dot_general(left, right, (((1,), (0,)), ((), ())), preferred_element_type=F32)


def nt(left, right):
    return lax.dot_general(left, right, (((1,), (1,)), ((), ())), preferred_element_type=F32)


def tn(left, right):
    return lax.dot_general(left, right, (((0,), (0,)), ((), ())), preferred_element_type=F32)


def place_of_block(block, core, rows):
    return ((block % 2) * 2 + block // 2) * QB + core * (rows // 2) & (rows - 1)


def spot_of_keys(j, core, rows):
    place = (j * KB + core * (rows // 2)) & (rows - 1)
    block = place // QB
    return pl.multiple_of(((block % 2) * 2 + block // 2) * QB + place % QB, KB)


def segment_bounds(lengths_ref):
    bounds, total = [], jnp.int32(0)
    for s in range(lengths_ref.shape[0]):
        start = total
        total = total + lengths_ref[s]
        bounds.append((start, total))
    return bounds


def block_span(bounds, first, rows):
    place = first + lax.broadcasted_iota(jnp.int32, (1, QB), 1)
    low, high = first, first + KB
    begin = jnp.full((1, QB), bounds[-1][1], jnp.int32)
    end = jnp.full((1, QB), rows, jnp.int32)
    for start, stop in bounds:
        inside = (place >= start) & (place < stop)
        begin = jnp.where(inside, start, begin)
        end = jnp.where(inside, stop, end)
        touches = (stop > first) & (start < first + QB) & (stop > start)
        low = jnp.where(touches, jnp.minimum(low, start), low)
        high = jnp.where(touches, jnp.maximum(high, stop), high)
    return low // KB, (high + KB - 1) // KB, begin, end


def head_copies(values, heads):
    lane = lax.broadcasted_iota(jnp.int32, values.shape, 1) // HD
    blank = jnp.zeros_like(values)
    return jnp.concatenate([jnp.where(lane == h, values, blank) for h in range(heads)], axis=0)


def span_mask(begin, end, block, heads):
    place = block * KB + lax.broadcasted_iota(jnp.int32, (KB, QB), 0)
    keep = (place >= begin) & (place < end)
    return jnp.concatenate([keep] * heads, axis=1)


def attend(heads, blocks, core, bounds, q_ref, k_ref, vt_ref, mixed_ref, lse_ref, acc_ref):
    rows = k_ref.shape[0]
    for i, block in enumerate(blocks):
        low, high, begin, end = block_span(bounds, place_of_block(block, core, rows), rows)
        stack = head_copies(q_ref[block * QB : (block + 1) * QB, :], heads)
        acc_ref[...] = jnp.zeros(acc_ref.shape, F32)

        def step(j, carry, stack=stack, begin=begin, end=end):
            top, total = carry
            spot = spot_of_keys(j, core, rows)
            scores = nt(k_ref[pl.ds(spot, KB), :], stack)
            scores = jnp.where(span_mask(begin, end, j, heads), scores, NEG_FILL)
            peak = jnp.maximum(top, jnp.max(scores, axis=0, keepdims=True))
            fade = jnp.exp(top - peak)
            probs = jnp.exp(scores - peak)
            total = total * fade + jnp.sum(probs, axis=0, keepdims=True)
            probs = probs.astype(BF16)
            for h in range(heads):
                part = slice(h * QB, (h + 1) * QB)
                span = slice(h * HD, (h + 1) * HD)
                acc_ref[span, :] = acc_ref[span, :] * fade[:, part] + nn(
                    vt_ref[span, pl.ds(spot, KB)], probs[:, part]
                )
            return peak, total

        top = jnp.full((1, heads * QB), NEG_FILL, F32)
        top, total = lax.fori_loop(
            low, high, step, (top, jnp.zeros((1, heads * QB), F32)), unroll=False
        )
        scale = 1.0 / total
        mixed = jnp.concatenate(
            [
                acc_ref[h * HD : (h + 1) * HD, :] * scale[:, h * QB : (h + 1) * QB]
                for h in range(heads)
            ],
            axis=0,
        )
        mixed_ref[i * QB : (i + 1) * QB, :] = mixed.T.astype(BF16)
        lse_ref[i, :, :] = jnp.broadcast_to(top + jnp.log(total), (8, heads * QB))


def fetch(sources, targets, semaphores):
    copies = [
        pltpu.make_async_copy(source, target, semaphores.at[i])
        for i, (source, target) in enumerate(zip(sources, targets))
    ]
    for copy in copies:
        copy.start()
    return copies


def attend_first(
    heads,
    blocks,
    lengths_ref,
    core_ref,
    tokens_hbm,
    wqt_hbm,
    wkt_hbm,
    wvt_hbm,
    vectors_hbm,
    *refs,
):
    outputs, refs = refs[:8], refs[8:]
    x_ref, q_ref, k_ref, v_ref, kt_ref, vt_ref, mixed_ref, lse_ref = refs[:8]
    acc_ref, wqt_ref, wkt_ref, wvt_ref, vectors_ref, semaphores, out_semaphores = refs[8:]
    rows = x_ref.shape[0]
    width = heads * HD
    core = core_ref[0]
    sources = [vectors_hbm, wqt_hbm]
    targets = [vectors_ref, wqt_ref]
    for block in range(rows // QB):
        first = pl.multiple_of(place_of_block(block, core, rows), QB)
        sources.append(tokens_hbm.at[pl.ds(first, QB), :])
        targets.append(x_ref.at[pl.ds(block * QB, QB), :])
    copies = fetch(sources + [wkt_hbm, wvt_hbm], targets + [wkt_ref, wvt_ref], semaphores)
    for copy in copies:
        copy.wait()
    query_bias = vectors_ref[0:1, :width]
    value_bias = vectors_ref[1:2, :width]
    for block in range(rows // QB):
        part = slice(block * QB, (block + 1) * QB)
        x = x_ref[part, :]
        q = (nt(x, wqt_ref[...]) + query_bias).astype(BF16)
        q_ref[part, :] = q * BF16(0.125)
        k_ref[part, :] = nt(x, wkt_ref[...]).astype(BF16)
        kt_ref[:, part] = nt(wkt_ref[...], x).astype(BF16)
        v = nt(x, wvt_ref[...]) + value_bias
        v_ref[part, :] = v.astype(BF16)
        vt_ref[:, part] = v.T.astype(BF16)
    copies = fetch(refs[:6], outputs[:6], out_semaphores)
    bounds = segment_bounds(lengths_ref)
    attend(heads, blocks, core, bounds, q_ref, k_ref, vt_ref, mixed_ref, lse_ref, acc_ref)
    copies += fetch(refs[6:8], outputs[6:], out_semaphores.at[6:8])
    for copy in copies:
        copy.wait()


def attend_more(heads, blocks, lengths_ref, core_ref, *refs):
    sources, outputs, refs = refs[:3], refs[3:5], refs[5:]
    q_ref, k_ref, vt_ref, mixed_ref, lse_ref, acc_ref, semaphores = refs
    for copy in fetch(sources, refs[:3], semaphores):
        copy.wait()
    bounds = segment_bounds(lengths_ref)
    attend(heads, blocks, core_ref[0], bounds, q_ref, k_ref, vt_ref, mixed_ref, lse_ref, acc_ref)
    for copy in fetch(refs[3:5], outputs, semaphores.at[3:5]):
        copy.wait()


def attend_back(heads, inputs, lengths_ref, core_ref, *refs):
    sources, refs = refs[:inputs], refs[inputs:]
    outputs, refs = refs[:4], refs[4:]
    gq_ref, gk_ref, gv_ref, pack_ref = refs[:4]
    dk_ref, dv_ref, dqt_ref, wo_acc_ref, semaphores, out_semaphores = refs[4:10]
    targets = refs[10:]
    copies = fetch(sources, targets, semaphores)
    grads = targets[0:4]
    mixed = targets[4:6]
    lses = targets[6:8]
    wo_ref, q_ref, k_ref, v_ref, kt_ref, vectors_ref, x_ref, _ = targets[8:]
    rows, width = q_ref.shape
    core = core_ref[0]
    bounds = segment_bounds(lengths_ref)
    dk_ref[...] = jnp.zeros(dk_ref.shape, F32)
    dv_ref[...] = jnp.zeros(dv_ref.shape, F32)
    lane = lax.broadcasted_iota(jnp.int32, (8, width), 1) // HD
    which = (lane == lax.broadcasted_iota(jnp.int32, (8, width), 0)).astype(F32)
    for i in (0, 4, 6, 8, 9, 10, 11, 12):
        copies[i].wait()
    for block in range(rows // QB):
        if block > 0:
            copies[block].wait()
        if block == 2:
            copies[5].wait()
            copies[7].wait()
        low, high, begin, end = block_span(bounds, place_of_block(block, core, rows), rows)
        part = slice(block * QB, (block + 1) * QB)
        own = slice(block % 2 * QB, block % 2 * QB + QB)
        grad_attn = grads[block][...]
        mixed_here = mixed[block // 2][own, :]
        outer = tn(mixed_here, grad_attn)
        wo_acc_ref[...] = outer if block == 0 else wo_acc_ref[...] + outer
        grad_mixed = nt(grad_attn, wo_ref[...]).astype(BF16)
        product = grad_mixed.astype(F32) * mixed_here.astype(F32)
        sums = lax.dot_general(
            which,
            product,
            (((1,), (1,)), ((), ())),
            precision=HIGHEST,
            preferred_element_type=F32,
        )
        delta = jnp.concatenate([sums[h : h + 1, :] for h in range(heads)], axis=1)
        lse = lses[block // 2][block % 2, 0:1, :]
        q_stack = head_copies(q_ref[part, :], heads)
        g_stack = head_copies(grad_mixed, heads)
        dqt_ref[...] = jnp.zeros(dqt_ref.shape, F32)

        def step(
            j, carry, delta=delta, lse=lse, q_stack=q_stack, g_stack=g_stack, begin=begin, end=end
        ):
            here = pl.ds(spot_of_keys(j, core, rows), KB)
            scores = nt(k_ref[here, :], q_stack)
            scores = jnp.where(span_mask(begin, end, j, heads), scores, NEG_FILL)
            probs = jnp.exp(scores - lse)
            grad = (probs * (nt(v_ref[here, :], g_stack) - delta)).astype(BF16)
            dv_ref[here, :] += nn(probs.astype(BF16), g_stack)
            dk_ref[here, :] += nn(grad, q_stack)
            for h in range(heads):
                span = slice(h * HD, (h + 1) * HD)
                dqt_ref[span, :] += nn(kt_ref[span, here], grad[:, h * QB : (h + 1) * QB])
            return carry

        lax.fori_loop(low, high, step, 0, unroll=False)
        gq_ref[part, :] = (dqt_ref[...].T * 0.125).astype(BF16)
    gk_ref[...] = dk_ref[...].astype(BF16)
    gv_ref[...] = dv_ref[...].astype(BF16)
    copies[13].wait()
    copies[14].wait()
    copies[15].wait()
    outgoing = fetch(refs[:3], outputs[:3], out_semaphores)
    sums = [jnp.sum(ref[...].astype(F32), axis=0, keepdims=True) for ref in (gq_ref, gv_ref)]
    blank = jnp.zeros((1, 256 - width), F32)
    tail = jnp.concatenate([sums[0], blank, sums[1], blank, jnp.zeros((1, 256), F32)], axis=1)
    small = jnp.concatenate([vectors_ref[0:7, :], tail], axis=0).astype(BF16)
    piece = pack_ref.shape[1] - 8
    per = width // piece
    for m, source in enumerate((None, gq_ref, gk_ref, gv_ref)):
        total = wo_acc_ref[...] if source is None else tn(source[...], x_ref[...])
        for t in range(per):
            cut = total[t * piece : (t + 1) * piece, :].astype(BF16)
            pack_ref[m * per + t, 0:piece, :] = cut
            pack_ref[m * per + t, piece:, :] = small if m + t == 0 else jnp.zeros_like(small)
        here = pl.ds(m * per, per)
        copy = pltpu.make_async_copy(
            pack_ref.at[here], outputs[3].at[here], out_semaphores.at[3 + m]
        )
        copy.start()
        outgoing.append(copy)
    for copy in outgoing:
        copy.wait()


def shaped(shape, dtype):
    return jax.ShapeDtypeStruct(shape, dtype)


PARAMS = pltpu.CompilerParams(vmem_limit_bytes=60 << 20)
COST = pl.CostEstimate(flops=1024, bytes_accessed=1024, transcendentals=0)


def buffers(arrays):
    return [pltpu.VMEM(array.shape, array.dtype) for array in arrays]


def run_first(lengths, core, tokens, wqt, wkt, wvt, vectors, blocks):
    rows, width = tokens.shape[0], wqt.shape[0]
    heads, count = width // HD, len(blocks)
    outs = (
        (shaped(tokens.shape, BF16),)
        + (shaped((rows, width), BF16),) * 3
        + (shaped((width, rows), BF16),) * 2
        + (shaped((count * QB, width), BF16), shaped((count, 8, heads * QB), F32))
    )
    return pl.pallas_call(
        functools.partial(attend_first, heads, blocks),
        out_shape=outs,
        in_specs=[SMEM] * 2 + [HBM] * 5,
        out_specs=(HBM,) * 8,
        scratch_shapes=buffers(outs)
        + [pltpu.VMEM((width, QB), F32)]
        + buffers((wqt, wkt, wvt, vectors))
        + [pltpu.SemaphoreType.DMA((4 + rows // QB,)), pltpu.SemaphoreType.DMA((8,))],
        compiler_params=PARAMS,
        name="attend_first",
        cost_estimate=COST,
    )(lengths, core, tokens, wqt, wkt, wvt, vectors)


def run_more(lengths, core, q, k, vt, blocks):
    rows, width = q.shape
    heads, count = width // HD, len(blocks)
    outs = (shaped((count * QB, width), BF16), shaped((count, 8, heads * QB), F32))
    return pl.pallas_call(
        functools.partial(attend_more, heads, blocks),
        out_shape=outs,
        in_specs=[SMEM] * 2 + [HBM] * 3,
        out_specs=(HBM,) * 2,
        scratch_shapes=buffers((q, k, vt, *outs))
        + [pltpu.VMEM((width, QB), F32), pltpu.SemaphoreType.DMA((5,))],
        compiler_params=PARAMS,
        name="attend_more",
        cost_estimate=COST,
    )(lengths, core, q, k, vt)


def run_back(lengths, core, grads, mixed, lses, wo, q, k, v, kt, vectors, x, marker):
    rows, width = q.shape
    heads = width // HD
    arrays = (*grads, *mixed, *lses, wo, q, k, v, kt, vectors, x, marker)
    piece = 4 * width // 16
    outs = (shaped((rows, width), BF16),) * 3 + (shaped((16, piece + 8, x.shape[1]), BF16),)
    return pl.pallas_call(
        functools.partial(attend_back, heads, len(arrays)),
        out_shape=outs,
        in_specs=[SMEM] * 2 + [HBM] * len(arrays),
        out_specs=(HBM,) * 4,
        scratch_shapes=buffers(outs)
        + [pltpu.VMEM((rows, width), F32)] * 2
        + [pltpu.VMEM((width, QB), F32), pltpu.VMEM(wo.shape, F32)]
        + [pltpu.SemaphoreType.DMA((len(arrays),)), pltpu.SemaphoreType.DMA((7,))]
        + buffers(arrays),
        compiler_params=PARAMS,
        name="attend_back",
        cost_estimate=COST,
    )(lengths, core, *arrays)


def mark_kernel(source_ref, target_ref):
    del source_ref, target_ref


def mark(values):
    return pl.pallas_call(
        mark_kernel,
        out_shape=shaped(values.shape, values.dtype),
        in_specs=[HBM],
        out_specs=HBM,
        input_output_aliases={0: 0},
        compiler_params=PARAMS,
        name="mark",
        cost_estimate=pl.CostEstimate(flops=1 << 36, bytes_accessed=1 << 10, transcendentals=0),
    )(values)


def trade(values):
    return lax.all_to_all(
        values, "dp", split_axis=0, concat_axis=0, axis_index_groups=PLANES, tiled=True
    )


def share(values):
    return trade(jnp.broadcast_to(values[None], (16,) + values.shape))


def ring_shift(axis, step):
    pairs = []
    for i in range(32):
        z, y, x = i // 8, (i // 2) % 4, i % 2
        z, y = ((z + step) % 4, y) if axis == "z" else (z, (y + step) % 4)
        pairs.append((i, (z * 4 + y) * 2 + x))
    return pairs


def ring_pieces(values, axis):
    return [lax.ppermute(values, "dp", ring_shift(axis, step)) for step in (2, 1, 3)]


def ring_whole(values, pieces, axis, dtype):
    index = lax.axis_index("dp")
    place = index // 8 if axis == "z" else (index // 2) % 4
    whole = jnp.zeros((4,) + values.shape, dtype)
    whole = lax.dynamic_update_index_in_dim(whole, values.astype(dtype), place, 0)
    for step, piece in zip((2, 1, 3), pieces):
        whole = lax.dynamic_update_index_in_dim(
            whole, piece.astype(dtype), (place - step) % 4, 0
        )
    return whole


def near_swap(values):
    return lax.ppermute(values, "dp", NEAR_SWAP)


def plane_sum(parts):
    return jnp.sum(parts.astype(F32), axis=0).astype(BF16)


def near_sum(total):
    return (total.astype(F32) + near_swap(total).astype(F32)).astype(BF16)


def core_swap(values):
    return lax.ppermute(values, "mp", CORE_SWAP)


def marked_swap(values, marker):
    values, marker = tie(values, marker)
    return tie(core_swap(values), mark(marker))


def far_swap(values):
    return lax.ppermute(values, "mp", FAR_SWAP)


def tie(values, others):
    return lax.optimization_barrier((values, others))


def both(own):
    return jnp.concatenate([own, core_swap(own)], axis=0)


def norm_forward(values, gain_vec, shift_vec):
    average = jnp.mean(values, axis=-1, keepdims=True)
    centred = values - average
    rscale = lax.rsqrt(jnp.mean(centred * centred, axis=-1, keepdims=True) + EPS_NORM)
    normed = centred * rscale
    return (normed * gain_vec + shift_vec, normed, rscale)


def norm_backward(grad_out, normed, rscale, gain_vec):
    scaled = grad_out * gain_vec
    first_mean = jnp.mean(scaled, axis=-1, keepdims=True)
    cross_mean = jnp.mean(scaled * normed, axis=-1, keepdims=True)
    return rscale * (scaled - first_mean - normed * cross_mean)


def gelu_and_slope(upper):
    below = 0.5 * (1.0 + lax.erf(upper * math.sqrt(0.5)))
    density = jnp.exp(-0.5 * upper * upper) * (1.0 / math.sqrt(2.0 * math.pi))
    return (upper * below).astype(BF16), (below + upper * density).astype(BF16)


def local(
    tokens,
    lengths,
    pair_index,
    query_proj,
    query_bias,
    key_proj,
    value_proj,
    value_bias,
    output_proj,
    output_bias,
    attn_gain,
    attn_shift,
    inner_proj,
    inner_bias,
    outer_proj,
    outer_bias,
    final_gain,
    final_shift,
):
    row_count, width = tokens.shape
    chunk = row_count // 2
    half = chunk // 2
    seq_count = lengths.shape[0]
    pair_count = seq_count // 2
    overall_pair_count = pair_index.shape[0]
    local_width = query_proj.shape[1]
    core = lax.axis_index("mp") % 2
    my_index = lax.axis_index("dp")
    core_arg = jnp.reshape(core, (1,)).astype(jnp.int32)
    attn_gain_f, attn_shift_f = attn_gain.astype(F32), attn_shift.astype(F32)
    final_gain_f, final_shift_f = final_gain.astype(F32), final_shift.astype(F32)
    query_t, key_t, value_t = query_proj.T, key_proj.T, value_proj.T

    seq_ends = jnp.cumsum(lengths)
    seq_starts = seq_ends - lengths
    members = []
    for index in range(2):
        place = jnp.arange(half, dtype=jnp.int32) + index * half + core * chunk
        members.append(
            ((place[None] >= seq_starts[:, None]) & (place[None] < seq_ends[:, None])).astype(F32)
        )
    biases = jnp.stack(
        [jnp.pad(bias.astype(F32), (0, width - local_width)) for bias in (query_bias, value_bias)]
    )

    rows, query_b, key_b, value_b, key_tb, value_tb, mixed_a, lse_a = run_first(
        lengths, core_arg, tokens, query_t, key_t, value_t, biases, (0, 1)
    )

    def own_and_other(values, weights):
        return nn(values[:half], weights), nn(values[half:], weights).astype(BF16)

    def pair(own, arrived):
        return (own + arrived.astype(F32)).astype(BF16)

    def first_norm(index, pair_here, far):
        attn_full = pair_here.astype(F32) + far.astype(F32) + output_bias.astype(F32)
        own_tokens = rows[index * chunk : index * chunk + half].astype(F32)
        return norm_forward(own_tokens + attn_full, attn_gain_f, attn_shift_f)

    def feed_forward(own_hidden):
        whole = both(own_hidden)
        act, slope = gelu_and_slope(nn(whole, inner_proj) + inner_bias.astype(F32))
        return whole, act, slope

    def last_norm(hidden, pair_here, far):
        ffn_full = pair_here.astype(F32) + far.astype(F32) + outer_bias.astype(F32)
        return norm_forward(hidden + ffn_full, final_gain_f, final_shift_f)

    attn_own_a, attn_other_a = own_and_other(mixed_a, output_proj)
    attn_pair_a = pair(attn_own_a, core_swap(attn_other_a))
    attn_far_a = far_swap(attn_pair_a)
    late_query, late_pair = tie(query_b, attn_pair_a)
    mixed_b, lse_b = run_more(lengths, core_arg, late_query, key_b, value_tb, (2, 3))
    attn_own_b, attn_other_b = own_and_other(mixed_b, output_proj)
    attn_swap_b = core_swap(attn_other_b)
    attn_far_a, mixed_late = tie(attn_far_a, mixed_b)
    hidden_a, normed_one_a, rscale_one_a = first_norm(0, late_pair, attn_far_a)
    own_hidden_a = hidden_a.astype(BF16)
    attn_pair_b = pair(attn_own_b, attn_swap_b)
    attn_far_b = far_swap(attn_pair_b)
    hidden_ab, act_a, slope_a = feed_forward(own_hidden_a)
    ffn_own_a, ffn_other_a = own_and_other(act_a, outer_proj)
    arrived, marker = marked_swap(ffn_other_a, jnp.zeros((8, 128), F32))
    ffn_pair_a = pair(ffn_own_a, arrived)
    ffn_far_a = far_swap(ffn_pair_a)
    attn_far_b, late_pair_a = tie(attn_far_b, ffn_pair_a)
    hidden_b, normed_one_b, rscale_one_b = first_norm(1, attn_pair_b, attn_far_b)
    own_hidden_b = hidden_b.astype(BF16)
    hidden_bb, act_b, slope_b = feed_forward(own_hidden_b)
    ffn_own_b, ffn_other_b = own_and_other(act_b, outer_proj)
    arrived, marker = marked_swap(ffn_other_b, marker)
    ffn_pair_b = pair(ffn_own_b, arrived)
    ffn_far_a, late_pair_b = tie(ffn_far_a, ffn_pair_b)
    final_a, normed_two_a, rscale_two_a = last_norm(hidden_a, late_pair_a, ffn_far_a)
    pooled_a = jnp.dot(members[0], final_a, precision=HIGHEST)
    final_b, normed_two_b, rscale_two_b = last_norm(hidden_b, late_pair_b, far_swap(ffn_pair_b))
    pooled_part = pooled_a + jnp.dot(members[1], final_b, precision=HIGHEST)
    mixed, lse = (mixed_a, mixed_late), (lse_a, lse_b)
    hidden_whole, act, slope = (hidden_ab, hidden_bb), (act_a, act_b), (slope_a, slope_b)
    normed_one, rscale_one = (normed_one_a, normed_one_b), (rscale_one_a, rscale_one_b)
    normed_two, rscale_two = (normed_two_a, normed_two_b), (rscale_two_a, rscale_two_b)
    pooled = pooled_part + core_swap(pooled_part)
    pool_rscale = lax.rsqrt(jnp.sum(pooled * pooled, axis=-1, keepdims=True) + EPS_NORM)
    unit_b = (pooled * pool_rscale).astype(BF16)

    piece = lax.dynamic_slice_in_dim(unit_b, core * pair_count, pair_count, 0)
    near = near_swap(piece)
    low = (my_index % 2) == 0
    piece = jnp.concatenate([jnp.where(low, piece, near), jnp.where(low, near, piece)], axis=0)
    piece = share(piece).reshape(overall_pair_count, width)
    swapped = core_swap(piece)
    query_units = jnp.where(core == 0, piece, swapped)
    passage_units = jnp.where(core == 0, swapped, piece)

    backward_scale = 1.0 / (overall_pair_count * SOFTMAX_WARMTH)
    similarity = nt(query_units, passage_units) / SOFTMAX_WARMTH
    query_ids = jnp.arange(overall_pair_count, dtype=jnp.int32)
    is_match = (pair_index[None, :] == query_ids[:, None]).astype(F32)
    top = jnp.max(similarity, axis=1, keepdims=True)
    query_lse = top + jnp.log(jnp.sum(jnp.exp(similarity - top), axis=1, keepdims=True))
    loss_value = (
        jnp.sum(query_lse[:, 0] - jnp.sum(similarity * is_match, axis=1)) / overall_pair_count
    )
    coef = (jnp.exp(similarity - query_lse) - is_match) * backward_scale
    own_start = my_index * pair_count
    coef_query = lax.dynamic_slice_in_dim(coef, own_start, pair_count, 0)
    coef_passage = lax.dynamic_slice_in_dim(coef, own_start, pair_count, 1)
    grad_query = jnp.dot(coef_query, passage_units.astype(F32), precision=HIGHEST)
    grad_passage = lax.dot_general(
        coef_passage, query_units.astype(F32), (((0,), (0,)), ((), ())), precision=HIGHEST
    )
    grad_unit = jnp.concatenate([grad_query, grad_passage], axis=0)
    grad_pooled = (
        pool_rscale * grad_unit
        - pool_rscale**3 * jnp.sum(pooled * grad_unit, axis=-1, keepdims=True) * pooled
    )

    finalgain_part = finalshift_part = outerbias_part = innerbias_part = 0.0
    grad_second, grad_ffn, grad_up, hidden_other = [], [], [], []
    for i in range(2):
        grad_final = jnp.einsum("st,sd->td", members[i], grad_pooled, precision=HIGHEST)
        finalgain_part += jnp.sum(grad_final * normed_two[i], axis=0)
        finalshift_part += jnp.sum(grad_final, axis=0)
        grad_second.append(norm_backward(grad_final, normed_two[i], rscale_two[i], final_gain_f))
        own_grad = grad_second[i].astype(BF16)
        outerbias_part += jnp.sum(own_grad.astype(F32), axis=0)
        grad_ffn.append(both(own_grad))
        grad_up.append((nt(grad_ffn[i], outer_proj) * slope[i].astype(F32)).astype(BF16))
        innerbias_part += jnp.sum(grad_up[i].astype(F32), axis=0)
        other = nt(grad_up[i][half:], inner_proj).astype(BF16)
        arrived, marker = marked_swap(other, marker)
        hidden_other.append(arrived)
    hidden_pair = [pair(nt(grad_up[i][:half], inner_proj), hidden_other[i]) for i in range(2)]
    hidden_far = [far_swap(hidden_pair[i]) for i in range(2)]
    (late_act, late_hidden), hidden_pair = tie((act, hidden_whole), hidden_pair)
    ffn_pack = jnp.concatenate(
        [
            (tn(late_act[0], grad_ffn[0]) + tn(late_act[1], grad_ffn[1])).astype(BF16),
            (tn(late_hidden[0], grad_up[0]) + tn(late_hidden[1], grad_up[1])).astype(BF16),
        ],
        axis=0,
    ).reshape(16, -1, width)
    ffn_parts = trade(ffn_pack)

    attngain_part = attnshift_part = outputbias_part = 0.0
    grad_first, grad_attn = [], []
    for i in range(2):
        grad_hidden = grad_second[i] + (hidden_pair[i].astype(F32) + hidden_far[i].astype(F32))
        attngain_part += jnp.sum(grad_hidden * normed_one[i], axis=0)
        attnshift_part += jnp.sum(grad_hidden, axis=0)
        grad_first.append(norm_backward(grad_hidden, normed_one[i], rscale_one[i], attn_gain_f))
        own_grad = grad_first[i].astype(BF16)
        outputbias_part += jnp.sum(own_grad.astype(F32), axis=0)
        grad_attn += [own_grad, core_swap(own_grad)]
    paired = jnp.stack(
        [
            outputbias_part,
            attngain_part,
            attnshift_part,
            outerbias_part,
            finalgain_part,
            finalshift_part,
        ],
        axis=0,
    )
    paired = paired + core_swap(paired)
    vectors = jnp.concatenate(
        [paired, innerbias_part[None], jnp.zeros((1, width), F32)], axis=0
    )
    grad_query, grad_key, grad_value, packed = run_back(
        lengths,
        core_arg,
        grad_attn,
        mixed,
        lse,
        output_proj,
        query_b,
        key_b,
        value_b,
        key_tb,
        vectors,
        rows,
        marker,
    )
    grad_marker = jnp.zeros((8, 128), F32)
    (grad_query, packed), ffn_parts = tie((grad_query, packed), ffn_parts)
    packed_parts = trade(packed)
    ffn_reduced = near_sum(plane_sum(ffn_parts))
    grad_query, ffn_reduced = tie(grad_query, ffn_reduced)

    def input_part(first):
        span = slice(first, first + half)
        return (
            nt(grad_query[span], query_proj)
            + nt(grad_key[span], key_proj)
            + nt(grad_value[span], value_proj)
        )

    token_pair, marker = [], grad_marker
    for i in range(2):
        other = input_part(i * chunk + half).astype(BF16)
        arrived, marker = marked_swap(other, marker)
        token_pair.append(pair(input_part(i * chunk), arrived))
    loss_value = loss_value + marker[0, 0]
    token_far = [far_swap(token_pair[i]) for i in range(2)]
    ffn_pieces = ring_pieces(ffn_reduced, "y")
    packed_parts, token_far[0] = tie(packed_parts, token_far[0])
    packed_reduced = near_sum(plane_sum(packed_parts))
    ffn_pieces, packed_reduced = tie(ffn_pieces, packed_reduced)
    ffn_ring = ring_whole(ffn_reduced, ffn_pieces, "y", BF16)
    ffn_pieces = ring_pieces(ffn_ring, "z")
    packed_pieces = ring_pieces(packed_reduced, "z")
    packed_ring = ring_whole(packed_reduced, packed_pieces, "z", BF16)
    packed_pieces = ring_pieces(packed_ring, "y")
    token_far, late_ring = tie(token_far, packed_ring)
    ffn_pieces, late_ring = tie(ffn_pieces, late_ring)
    token_own = [
        (grad_first[i] + (token_pair[i].astype(F32) + token_far[i].astype(F32))).astype(BF16)
        for i in range(2)
    ]
    own_rows = jnp.concatenate(token_own, axis=0)
    other_rows = core_swap(own_rows)
    token_grad = jnp.where(
        core == 0,
        jnp.concatenate([own_rows, other_rows], axis=0),
        jnp.concatenate([other_rows, own_rows], axis=0),
    )
    ffn_sum = ring_whole(ffn_ring, ffn_pieces, "z", F32)
    ffn_sum = ffn_sum.reshape(2 * width, width)
    packed_pieces, (token_grad, ffn_sum) = tie(packed_pieces, (token_grad, ffn_sum))
    packed = ring_whole(late_ring, packed_pieces, "y", F32)
    packed = jnp.swapaxes(packed, 0, 1).reshape(16, -1, width)
    piece_rows = packed.shape[1] - 8
    cuts = packed[:, :piece_rows].reshape(4, local_width, width)
    vectors = packed[0, piece_rows:]
    return (
        loss_value,
        token_grad,
        cuts[1].T,
        vectors[7, :local_width],
        cuts[2].T,
        cuts[3].T,
        vectors[7, 256 : 256 + local_width],
        cuts[0],
        vectors[0],
        vectors[1],
        vectors[2],
        ffn_sum[width:],
        vectors[6],
        ffn_sum[:width],
        vectors[3],
        vectors[4],
        vectors[5],
    )


def solution(mesh):
    column, row, split = P(None, "mp"), P("mp", None), P("mp")
    placed = (
        (P("dp", None), P("dp"), P())
        + (column, split, column, column, split, row)
        + (P(), P(), P())
        + (column, split, row)
        + (P(), P(), P())
    )
    given = (
        (P(), P("dp", None))
        + (column, split, column, column, split, row)
        + (P(), P(), P())
        + (column, split, row)
        + (P(), P(), P())
    )
    return jax.shard_map(local, mesh=mesh, in_specs=placed, out_specs=given, check_vma=False)
```

```python
import functools
import math

import jax
import jax.numpy as jnp
from jax import lax
from jax.experimental import pallas as pl
from jax.experimental.pallas import tpu as pltpu
from jax.sharding import PartitionSpec as P

HD = 64
EPS_NORM = 1e-06
SOFTMAX_WARMTH = 0.01
NEG_FILL = -1e30
HIGHEST = lax.Precision.HIGHEST
F32 = jnp.float32
BF16 = jnp.bfloat16
QB = 256
KB = 128

CORE_SWAP = [(i, i ^ 1) for i in range(4)]
FAR_SWAP = [(i, i ^ 2) for i in range(4)]
NEAR_SWAP = [(i, i ^ 1) for i in range(32)]
PLANES = [[i * 2 + x for i in range(16)] for x in range(2)]

SMEM = pl.BlockSpec(memory_space=pltpu.SMEM)
VMEM = pl.BlockSpec(memory_space=pltpu.VMEM)
HBM = pl.BlockSpec(memory_space=pltpu.HBM)


def nn(left, right):
    return lax.dot_general(left, right, (((1,), (0,)), ((), ())), preferred_element_type=F32)


def nt(left, right):
    return lax.dot_general(left, right, (((1,), (1,)), ((), ())), preferred_element_type=F32)


def tn(left, right):
    return lax.dot_general(left, right, (((0,), (0,)), ((), ())), preferred_element_type=F32)


def place_of_block(block, core, rows):
    return ((block % 2) * 2 + block // 2) * QB + core * (rows // 2) & (rows - 1)


def spot_of_keys(j, core, rows):
    place = (j * KB + core * (rows // 2)) & (rows - 1)
    block = place // QB
    return pl.multiple_of(((block % 2) * 2 + block // 2) * QB + place % QB, KB)


def segment_bounds(lengths_ref):
    bounds, total = [], jnp.int32(0)
    for s in range(lengths_ref.shape[0]):
        start = total
        total = total + lengths_ref[s]
        bounds.append((start, total))
    return bounds


def block_span(bounds, first, rows):
    place = first + lax.broadcasted_iota(jnp.int32, (1, QB), 1)
    low, high = first, first + KB
    begin = jnp.full((1, QB), bounds[-1][1], jnp.int32)
    end = jnp.full((1, QB), rows, jnp.int32)
    for start, stop in bounds:
        inside = (place >= start) & (place < stop)
        begin = jnp.where(inside, start, begin)
        end = jnp.where(inside, stop, end)
        touches = (stop > first) & (start < first + QB) & (stop > start)
        low = jnp.where(touches, jnp.minimum(low, start), low)
        high = jnp.where(touches, jnp.maximum(high, stop), high)
    return low // KB, (high + KB - 1) // KB, begin, end


def head_copies(values, heads):
    lane = lax.broadcasted_iota(jnp.int32, values.shape, 1) // HD
    blank = jnp.zeros_like(values)
    return jnp.concatenate([jnp.where(lane == h, values, blank) for h in range(heads)], axis=0)


def span_mask(begin, end, block, heads):
    place = block * KB + lax.broadcasted_iota(jnp.int32, (KB, QB), 0)
    keep = (place >= begin) & (place < end)
    return jnp.concatenate([keep] * heads, axis=1)


def attend(heads, blocks, core, bounds, q_ref, k_ref, vt_ref, mixed_ref, lse_ref, acc_ref):
    rows = k_ref.shape[0]
    for i, block in enumerate(blocks):
        low, high, begin, end = block_span(bounds, place_of_block(block, core, rows), rows)
        stack = head_copies(q_ref[block * QB : (block + 1) * QB, :], heads)
        acc_ref[...] = jnp.zeros(acc_ref.shape, F32)

        def step(j, carry, stack=stack, begin=begin, end=end):
            top, total = carry
            spot = spot_of_keys(j, core, rows)
            scores = nt(k_ref[pl.ds(spot, KB), :], stack)
            scores = jnp.where(span_mask(begin, end, j, heads), scores, NEG_FILL)
            peak = jnp.maximum(top, jnp.max(scores, axis=0, keepdims=True))
            fade = jnp.exp(top - peak)
            probs = jnp.exp(scores - peak)
            total = total * fade + jnp.sum(probs, axis=0, keepdims=True)
            probs = probs.astype(BF16)
            for h in range(heads):
                part = slice(h * QB, (h + 1) * QB)
                span = slice(h * HD, (h + 1) * HD)
                acc_ref[span, :] = acc_ref[span, :] * fade[:, part] + nn(
                    vt_ref[span, pl.ds(spot, KB)], probs[:, part]
                )
            return peak, total

        top = jnp.full((1, heads * QB), NEG_FILL, F32)
        top, total = lax.fori_loop(
            low, high, step, (top, jnp.zeros((1, heads * QB), F32)), unroll=False
        )
        scale = 1.0 / total
        mixed = jnp.concatenate(
            [
                acc_ref[h * HD : (h + 1) * HD, :] * scale[:, h * QB : (h + 1) * QB]
                for h in range(heads)
            ],
            axis=0,
        )
        mixed_ref[i * QB : (i + 1) * QB, :] = mixed.T.astype(BF16)
        lse_ref[i, :, :] = jnp.broadcast_to(top + jnp.log(total), (8, heads * QB))


def fetch(sources, targets, semaphores):
    copies = [
        pltpu.make_async_copy(source, target, semaphores.at[i])
        for i, (source, target) in enumerate(zip(sources, targets))
    ]
    for copy in copies:
        copy.start()
    return copies


def attend_first(
    heads,
    blocks,
    lengths_ref,
    core_ref,
    tokens_hbm,
    wqt_hbm,
    wkt_hbm,
    wvt_hbm,
    vectors_hbm,
    *refs,
):
    outputs, refs = refs[:8], refs[8:]
    x_ref, q_ref, k_ref, v_ref, kt_ref, vt_ref, mixed_ref, lse_ref = refs[:8]
    acc_ref, wqt_ref, wkt_ref, wvt_ref, vectors_ref, semaphores, out_semaphores = refs[8:]
    rows = x_ref.shape[0]
    width = heads * HD
    core = core_ref[0]
    sources = [vectors_hbm, wqt_hbm]
    targets = [vectors_ref, wqt_ref]
    for block in range(rows // QB):
        first = pl.multiple_of(place_of_block(block, core, rows), QB)
        sources.append(tokens_hbm.at[pl.ds(first, QB), :])
        targets.append(x_ref.at[pl.ds(block * QB, QB), :])
    copies = fetch(sources + [wkt_hbm, wvt_hbm], targets + [wkt_ref, wvt_ref], semaphores)
    for copy in copies:
        copy.wait()
    query_bias = vectors_ref[0:1, :width]
    value_bias = vectors_ref[1:2, :width]
    for block in range(rows // QB):
        part = slice(block * QB, (block + 1) * QB)
        x = x_ref[part, :]
        q = (nt(x, wqt_ref[...]) + query_bias).astype(BF16)
        q_ref[part, :] = q * BF16(0.125)
        k_ref[part, :] = nt(x, wkt_ref[...]).astype(BF16)
        kt_ref[:, part] = nt(wkt_ref[...], x).astype(BF16)
        v = nt(x, wvt_ref[...]) + value_bias
        v_ref[part, :] = v.astype(BF16)
        vt_ref[:, part] = v.T.astype(BF16)
    copies = fetch(refs[:6], outputs[:6], out_semaphores)
    bounds = segment_bounds(lengths_ref)
    attend(heads, blocks, core, bounds, q_ref, k_ref, vt_ref, mixed_ref, lse_ref, acc_ref)
    copies += fetch(refs[6:8], outputs[6:], out_semaphores.at[6:8])
    for copy in copies:
        copy.wait()


def attend_more(heads, blocks, lengths_ref, core_ref, *refs):
    sources, outputs, refs = refs[:3], refs[3:5], refs[5:]
    q_ref, k_ref, vt_ref, mixed_ref, lse_ref, acc_ref, semaphores = refs
    for copy in fetch(sources, refs[:3], semaphores):
        copy.wait()
    bounds = segment_bounds(lengths_ref)
    attend(heads, blocks, core_ref[0], bounds, q_ref, k_ref, vt_ref, mixed_ref, lse_ref, acc_ref)
    for copy in fetch(refs[3:5], outputs, semaphores.at[3:5]):
        copy.wait()


def attend_back(heads, inputs, lengths_ref, core_ref, *refs):
    sources, refs = refs[:inputs], refs[inputs + 1 :]
    outputs, refs = refs[:4], refs[4:]
    gq_ref, gk_ref, gv_ref, pack_ref = refs[:4]
    dk_ref, dv_ref, dqt_ref, wo_acc_ref, semaphores, out_semaphores = refs[4:10]
    targets = refs[10:]
    copies = fetch(sources, targets, semaphores)
    grads = targets[0:4]
    mixed = targets[4:6]
    lses = targets[6:8]
    wo_ref, q_ref, k_ref, v_ref, kt_ref = targets[8:13]
    own_sums, other_sums, inner_a, inner_b, x_ref = targets[13:]
    rows, width = q_ref.shape
    core = core_ref[0]
    bounds = segment_bounds(lengths_ref)
    dk_ref[...] = jnp.zeros(dk_ref.shape, F32)
    dv_ref[...] = jnp.zeros(dv_ref.shape, F32)
    lane = lax.broadcasted_iota(jnp.int32, (8, width), 1) // HD
    which = (lane == lax.broadcasted_iota(jnp.int32, (8, width), 0)).astype(F32)
    for i in (0, 4, 6, 8, 9, 10, 11, 12):
        copies[i].wait()
    for block in range(rows // QB):
        if block > 0:
            copies[block].wait()
        if block == 2:
            copies[5].wait()
            copies[7].wait()
        low, high, begin, end = block_span(bounds, place_of_block(block, core, rows), rows)
        part = slice(block * QB, (block + 1) * QB)
        own = slice(block % 2 * QB, block % 2 * QB + QB)
        grad_attn = grads[block][...]
        mixed_here = mixed[block // 2][own, :]
        outer = tn(mixed_here, grad_attn)
        wo_acc_ref[...] = outer if block == 0 else wo_acc_ref[...] + outer
        grad_mixed = nt(grad_attn, wo_ref[...]).astype(BF16)
        product = grad_mixed.astype(F32) * mixed_here.astype(F32)
        sums = lax.dot_general(
            which,
            product,
            (((1,), (1,)), ((), ())),
            precision=HIGHEST,
            preferred_element_type=F32,
        )
        delta = jnp.concatenate([sums[h : h + 1, :] for h in range(heads)], axis=1)
        lse = lses[block // 2][block % 2, 0:1, :]
        q_stack = head_copies(q_ref[part, :], heads)
        g_stack = head_copies(grad_mixed, heads)
        dqt_ref[...] = jnp.zeros(dqt_ref.shape, F32)

        def step(
            j, carry, delta=delta, lse=lse, q_stack=q_stack, g_stack=g_stack, begin=begin, end=end
        ):
            here = pl.ds(spot_of_keys(j, core, rows), KB)
            scores = nt(k_ref[here, :], q_stack)
            scores = jnp.where(span_mask(begin, end, j, heads), scores, NEG_FILL)
            probs = jnp.exp(scores - lse)
            grad = (probs * (nt(v_ref[here, :], g_stack) - delta)).astype(BF16)
            dv_ref[here, :] += nn(probs.astype(BF16), g_stack)
            dk_ref[here, :] += nn(grad, q_stack)
            for h in range(heads):
                span = slice(h * HD, (h + 1) * HD)
                dqt_ref[span, :] += nn(kt_ref[span, here], grad[:, h * QB : (h + 1) * QB])
            return carry

        lax.fori_loop(low, high, step, 0, unroll=False)
        gq_ref[part, :] = (dqt_ref[...].T * 0.125).astype(BF16)
    gk_ref[...] = dk_ref[...].astype(BF16)
    gv_ref[...] = dv_ref[...].astype(BF16)
    for copy in copies[13:]:
        copy.wait()
    outgoing = fetch(refs[:3], outputs[:3], out_semaphores)
    sums = [jnp.sum(ref[...].astype(F32), axis=0, keepdims=True) for ref in (gq_ref, gv_ref)]
    blank = jnp.zeros((1, 256 - width), F32)
    tail = jnp.concatenate([sums[0], blank, sums[1], blank, jnp.zeros((1, 256), F32)], axis=1)
    inner = row_of(inner_a) + row_of(inner_b)
    paired = own_sums[0:6, :] + other_sums[0:6, :]
    small = jnp.concatenate([paired, inner, tail], axis=0).astype(BF16)
    piece = pack_ref.shape[1] - 8
    per = width // piece
    for m, source in enumerate((None, gq_ref, gk_ref, gv_ref)):
        total = wo_acc_ref[...] if source is None else tn(source[...], x_ref[...])
        for t in range(per):
            cut = total[t * piece : (t + 1) * piece, :].astype(BF16)
            pack_ref[m * per + t, 0:piece, :] = cut
            pack_ref[m * per + t, piece:, :] = small if m + t == 0 else jnp.zeros_like(small)
        here = pl.ds(m * per, per)
        copy = pltpu.make_async_copy(
            pack_ref.at[here], outputs[3].at[here], out_semaphores.at[3 + m]
        )
        copy.start()
        outgoing.append(copy)
    for copy in outgoing:
        copy.wait()


def shaped(shape, dtype):
    return jax.ShapeDtypeStruct(shape, dtype)


PARAMS = pltpu.CompilerParams(vmem_limit_bytes=60 << 20)
SMALL = pltpu.CompilerParams(vmem_limit_bytes=24 << 20)
COST = pl.CostEstimate(flops=1024, bytes_accessed=1024, transcendentals=0)


def buffers(arrays):
    return [pltpu.VMEM(array.shape, array.dtype) for array in arrays]


def run_first(lengths, core, tokens, wqt, wkt, wvt, vectors, blocks):
    rows, width = tokens.shape[0], wqt.shape[0]
    heads, count = width // HD, len(blocks)
    outs = (
        (shaped(tokens.shape, BF16),)
        + (shaped((rows, width), BF16),) * 3
        + (shaped((width, rows), BF16),) * 2
        + (shaped((count * QB, width), BF16), shaped((count, 8, heads * QB), F32))
    )
    return pl.pallas_call(
        functools.partial(attend_first, heads, blocks),
        out_shape=outs,
        in_specs=[SMEM] * 2 + [HBM] * 5,
        out_specs=(HBM,) * 8,
        scratch_shapes=buffers(outs)
        + [pltpu.VMEM((width, QB), F32)]
        + buffers((wqt, wkt, wvt, vectors))
        + [pltpu.SemaphoreType.DMA((4 + rows // QB,)), pltpu.SemaphoreType.DMA((8,))],
        compiler_params=PARAMS,
        name="attend_first",
        cost_estimate=COST,
    )(lengths, core, tokens, wqt, wkt, wvt, vectors)


def run_more(lengths, core, q, k, vt, blocks):
    rows, width = q.shape
    heads, count = width // HD, len(blocks)
    outs = (shaped((count * QB, width), BF16), shaped((count, 8, heads * QB), F32))
    return pl.pallas_call(
        functools.partial(attend_more, heads, blocks),
        out_shape=outs,
        in_specs=[SMEM] * 2 + [HBM] * 3,
        out_specs=(HBM,) * 2,
        scratch_shapes=buffers((q, k, vt, *outs))
        + [pltpu.VMEM((width, QB), F32), pltpu.SemaphoreType.DMA((5,))],
        compiler_params=PARAMS,
        name="attend_more",
        cost_estimate=COST,
    )(lengths, core, q, k, vt)


def run_back(lengths, core, arrays, marker):
    wo, q, x = arrays[8], arrays[9], arrays[-1]
    rows, width = q.shape
    heads = width // HD
    piece = 4 * width // 16
    outs = (shaped((rows, width), BF16),) * 3 + (shaped((16, piece + 8, x.shape[1]), BF16),)
    return pl.pallas_call(
        functools.partial(attend_back, heads, len(arrays)),
        out_shape=outs,
        in_specs=[SMEM] * 2 + [HBM] * (len(arrays) + 1),
        out_specs=(HBM,) * 4,
        scratch_shapes=buffers(outs)
        + [pltpu.VMEM((rows, width), F32)] * 2
        + [pltpu.VMEM((width, QB), F32), pltpu.VMEM(wo.shape, F32)]
        + [pltpu.SemaphoreType.DMA((len(arrays),)), pltpu.SemaphoreType.DMA((7,))]
        + buffers(arrays),
        compiler_params=PARAMS,
        name="attend_back",
        cost_estimate=COST,
    )(lengths, core, *arrays, marker)


def mark_kernel(source_ref, target_ref):
    del source_ref, target_ref


def mark(values):
    return pl.pallas_call(
        mark_kernel,
        out_shape=shaped(values.shape, values.dtype),
        in_specs=[HBM],
        out_specs=HBM,
        compiler_params=pltpu.CompilerParams(vmem_limit_bytes=1 << 20),
        name="mark",
        cost_estimate=pl.CostEstimate(flops=1 << 36, bytes_accessed=1 << 10, transcendentals=0),
    )(values)


def row_of(ref):
    return ref[...].astype(F32).reshape(1, -1)


def in_three(values):
    high = values.astype(BF16)
    rest = values - high.astype(F32)
    middle = rest.astype(BF16)
    return high, middle, (rest - middle.astype(F32)).astype(BF16)


def norm_step(grad, normed, rscale, gain):
    scaled = grad * gain
    first_mean = jnp.mean(scaled, axis=1, keepdims=True)
    cross_mean = jnp.mean(scaled * normed, axis=1, keepdims=True)
    return rscale * (scaled - first_mean - normed * cross_mean)


def column_sum(values):
    return jnp.sum(values, axis=0, keepdims=True)


def send_out(results, outputs, semaphores, which):
    copies = [
        pltpu.make_async_copy(results[k], outputs[k], semaphores.at[k]) for k in which
    ]
    for copy in copies:
        copy.start()
    return copies


def loss_back(lengths_ref, place_ref, *refs):
    sources, outputs, refs = refs[:9], refs[9:15], refs[15:]
    targets, results = refs[:9], refs[9:15]
    coef_ref, turned_ref, semaphores, out_semaphores = refs[15:]
    copies = fetch(sources, targets, semaphores)
    piece_ref, swapped_ref, pooled_ref, match_ref, gain_ref = targets[:5]
    core, index = place_ref[0], place_ref[1]
    bounds = segment_bounds(lengths_ref)
    for copy in copies[:5]:
        copy.wait()
    first = core == 0
    queries = jnp.where(first, piece_ref[...], swapped_ref[...])
    passages = jnp.where(first, swapped_ref[...], piece_ref[...])
    count = queries.shape[0]
    own = pooled_ref.shape[0] // 2
    similarity = nt(queries, passages) / SOFTMAX_WARMTH
    match = match_ref[...].reshape(1, -1)
    match = match == lax.broadcasted_iota(jnp.int32, (count, count), 0)
    top = jnp.max(similarity, axis=1, keepdims=True)
    lse = top + jnp.log(jnp.sum(jnp.exp(similarity - top), axis=1, keepdims=True))
    positive = jnp.sum(jnp.where(match, similarity, 0.0), axis=1, keepdims=True)
    loss = jnp.sum(lse - positive, axis=0, keepdims=True) / count
    results[5][...] = jnp.broadcast_to(loss, results[5].shape)
    coef = (jnp.exp(similarity - lse) - match.astype(F32)) * (1.0 / (count * SOFTMAX_WARMTH))
    coef_ref[...] = coef
    turned_ref[...] = coef.T
    here = pl.ds(pl.multiple_of(index * own, own), own)
    grad_query = sum(nn(part, passages) for part in in_three(coef_ref[here, :]))
    grad_passage = sum(nn(part, queries) for part in in_three(turned_ref[here, :]))
    grad_unit = jnp.concatenate([grad_query, grad_passage], axis=0)
    pooled = pooled_ref[...]
    rscale = lax.rsqrt(jnp.sum(pooled * pooled, axis=1, keepdims=True) + EPS_NORM)
    inner = jnp.sum(pooled * grad_unit, axis=1, keepdims=True)
    grad_pooled = rscale * grad_unit - rscale * rscale * rscale * inner * pooled
    seqs = 2 * own
    grad_pooled = jnp.concatenate(
        [grad_pooled, jnp.zeros((128 - seqs, grad_pooled.shape[1]), F32)], axis=0
    )
    parts = in_three(grad_pooled)
    lane = lax.broadcasted_iota(jnp.int32, (1, 128), 1)
    begin = end = jnp.zeros((1, 128), jnp.int32)
    for seq, (start, stop) in enumerate(bounds):
        begin = jnp.where(lane == seq, start, begin)
        end = jnp.where(lane == seq, stop, end)
    gain = row_of(gain_ref)
    sums = [0.0, 0.0, 0.0]
    outgoing = []
    for i in range(2):
        copies[5 + 2 * i].wait()
        copies[6 + 2 * i].wait()
        normed = targets[5 + 2 * i][...]
        place = core * (2 * QB) + i * QB + lax.broadcasted_iota(jnp.int32, (QB, 128), 0)
        member = jnp.where((place >= begin) & (place < end), 1.0, 0.0).astype(BF16)
        grad = sum(nn(member, part) for part in parts)
        second = norm_step(grad, normed, targets[6 + 2 * i][:, 0:1], gain)
        rounded = second.astype(BF16)
        results[i][...] = second
        results[2 + i][...] = rounded
        for k, values in enumerate((rounded.astype(F32), grad * normed, grad)):
            sums[k] = sums[k] + column_sum(values)
        outgoing += send_out(results, outputs, out_semaphores, (2 + i, i))
    results[4][...] = jnp.concatenate(sums + [jnp.zeros((5, sums[0].shape[1]), F32)], axis=0)
    outgoing += send_out(results, outputs, out_semaphores, (4, 5))
    for copy in outgoing:
        copy.wait()


def norm_back(*refs):
    sources, outputs, refs = refs[:12], refs[12:17], refs[17:]
    targets, results = refs[:12], refs[12:17]
    semaphores, out_semaphores = refs[17:]
    copies = fetch(sources, targets, semaphores)
    copies[0].wait()
    copies[1].wait()
    gain = row_of(targets[0])
    sums = [0.0, 0.0, 0.0]
    outgoing = []
    for i in range(2):
        for copy in copies[2 + 5 * i : 7 + 5 * i]:
            copy.wait()
        second, pair_here, far, normed, rscale = targets[2 + 5 * i : 7 + 5 * i]
        grad = second[...] + (pair_here[...].astype(F32) + far[...].astype(F32))
        normed = normed[...]
        first = norm_step(grad, normed, rscale[:, 0:1], gain)
        rounded = first.astype(BF16)
        results[i][...] = first
        results[2 + i][...] = rounded
        for k, values in enumerate((rounded.astype(F32), grad * normed, grad)):
            sums[k] = sums[k] + column_sum(values)
        outgoing += send_out(results, outputs, out_semaphores, (2 + i, i))
    blank = jnp.zeros((2, sums[0].shape[1]), F32)
    results[4][...] = jnp.concatenate(sums + [targets[1][0:3, :], blank], axis=0)
    outgoing += send_out(results, outputs, out_semaphores, (4,))
    for copy in outgoing:
        copy.wait()


def assemble(place_ref, *refs):
    sources, outputs, refs = refs[:8], refs[9:11], refs[11:]
    targets, results = refs[:8], refs[8:16]
    semaphores, out_semaphores = refs[16:]
    copies = fetch(sources, targets, semaphores)
    outgoing = []
    for k in range(8):
        copies[k].wait()
        results[k][...] = targets[k][...].astype(F32)
        step = (0, 2, 1, 3)[k % 4]
        spot = (place_ref[k // 4] + 4 - step) % 4
        goal = outputs[0].at[spot] if k < 4 else outputs[1].at[:, spot]
        copy = pltpu.make_async_copy(results[k], goal, out_semaphores.at[k])
        copy.start()
        outgoing.append(copy)
    for copy in outgoing:
        copy.wait()


def run_loss(lengths, place, arrays):
    rows, width = arrays[5].shape
    count = arrays[0].shape[0]
    outs = (
        (shaped((rows, width), F32),) * 2
        + (shaped((rows, width), BF16),) * 2
        + (shaped((8, width), F32), shaped((8, 128), F32))
    )
    return pl.pallas_call(
        loss_back,
        out_shape=outs,
        in_specs=[SMEM] * 2 + [HBM] * 9,
        out_specs=(HBM,) * 6,
        scratch_shapes=buffers(arrays)
        + buffers(outs)
        + [pltpu.VMEM((count, count), F32)] * 2
        + [pltpu.SemaphoreType.DMA((9,)), pltpu.SemaphoreType.DMA((6,))],
        compiler_params=SMALL,
        name="loss_back",
        cost_estimate=COST,
    )(lengths, place, *arrays)


def run_norm(arrays):
    rows, width = arrays[2].shape
    outs = (
        (shaped((rows, width), F32),) * 2
        + (shaped((rows, width), BF16),) * 2
        + (shaped((8, width), F32),)
    )
    return pl.pallas_call(
        norm_back,
        out_shape=outs,
        in_specs=[HBM] * 12,
        out_specs=(HBM,) * 5,
        scratch_shapes=buffers(arrays)
        + buffers(outs)
        + [pltpu.SemaphoreType.DMA((12,)), pltpu.SemaphoreType.DMA((5,))],
        compiler_params=SMALL,
        name="norm_back",
        cost_estimate=COST,
    )(*arrays)


def run_assemble(place, pieces, marker):
    piece = pieces[0].shape
    whole = shaped((4,) + piece, F32)
    return pl.pallas_call(
        assemble,
        out_shape=(whole, whole),
        in_specs=[SMEM] + [HBM] * 9,
        out_specs=(HBM,) * 2,
        scratch_shapes=buffers(pieces)
        + [pltpu.VMEM(piece, F32)] * 8
        + [pltpu.SemaphoreType.DMA((8,)), pltpu.SemaphoreType.DMA((8,))],
        compiler_params=SMALL,
        name="assemble",
        cost_estimate=COST,
    )(place, *pieces, marker)


def trade(values):
    return lax.all_to_all(
        values, "dp", split_axis=0, concat_axis=0, axis_index_groups=PLANES, tiled=True
    )


def share(values):
    return trade(jnp.broadcast_to(values[None], (16,) + values.shape))


def ring_shift(axis, step):
    pairs = []
    for i in range(32):
        z, y, x = i // 8, (i // 2) % 4, i % 2
        z, y = ((z + step) % 4, y) if axis == "z" else (z, (y + step) % 4)
        pairs.append((i, (z * 4 + y) * 2 + x))
    return pairs


def ring_pieces(values, axis):
    return [lax.ppermute(values, "dp", ring_shift(axis, step)) for step in (2, 1, 3)]


def ring_whole(values, pieces, axis, dtype):
    index = lax.axis_index("dp")
    place = index // 8 if axis == "z" else (index // 2) % 4
    whole = jnp.zeros((4,) + values.shape, dtype)
    whole = lax.dynamic_update_index_in_dim(whole, values.astype(dtype), place, 0)
    for step, piece in zip((2, 1, 3), pieces):
        whole = lax.dynamic_update_index_in_dim(
            whole, piece.astype(dtype), (place - step) % 4, 0
        )
    return whole


def near_swap(values):
    return lax.ppermute(values, "dp", NEAR_SWAP)


def plane_sum(parts):
    return jnp.sum(parts.astype(F32), axis=0).astype(BF16)


def near_sum(total):
    return (total.astype(F32) + near_swap(total).astype(F32)).astype(BF16)


def core_swap(values):
    return lax.ppermute(values, "mp", CORE_SWAP)


def fence(ready, later, marker):
    ready, marker = tie(ready, marker)
    later, marker = tie(later, mark(marker))
    return ready, later, marker


def marked_swap(values, marker):
    values, marker = tie(values, marker)
    return tie(core_swap(values), mark(marker))


def far_swap(values):
    return lax.ppermute(values, "mp", FAR_SWAP)


def tie(values, others):
    return lax.optimization_barrier((values, others))


def both(own):
    return jnp.concatenate([own, core_swap(own)], axis=0)


def norm_forward(values, gain_vec, shift_vec):
    average = jnp.mean(values, axis=-1, keepdims=True)
    centred = values - average
    rscale = lax.rsqrt(jnp.mean(centred * centred, axis=-1, keepdims=True) + EPS_NORM)
    normed = centred * rscale
    wide = jnp.broadcast_to(rscale, (values.shape[0], 128))
    return (normed * gain_vec + shift_vec, normed, wide)


def gelu_and_slope(upper):
    below = 0.5 * (1.0 + lax.erf(upper * math.sqrt(0.5)))
    density = jnp.exp(-0.5 * upper * upper) * (1.0 / math.sqrt(2.0 * math.pi))
    return (upper * below).astype(BF16), (below + upper * density).astype(BF16)


def local(
    tokens,
    lengths,
    pair_index,
    query_proj,
    query_bias,
    key_proj,
    value_proj,
    value_bias,
    output_proj,
    output_bias,
    attn_gain,
    attn_shift,
    inner_proj,
    inner_bias,
    outer_proj,
    outer_bias,
    final_gain,
    final_shift,
):
    row_count, width = tokens.shape
    chunk = row_count // 2
    half = chunk // 2
    seq_count = lengths.shape[0]
    pair_count = seq_count // 2
    overall_pair_count = pair_index.shape[0]
    local_width = query_proj.shape[1]
    core = lax.axis_index("mp") % 2
    my_index = lax.axis_index("dp")
    core_arg = jnp.reshape(core, (1,)).astype(jnp.int32)
    attn_gain_f, attn_shift_f = attn_gain.astype(F32), attn_shift.astype(F32)
    final_gain_f, final_shift_f = final_gain.astype(F32), final_shift.astype(F32)
    query_t, key_t, value_t = query_proj.T, key_proj.T, value_proj.T

    seq_ends = jnp.cumsum(lengths)
    seq_starts = seq_ends - lengths
    members = []
    for index in range(2):
        place = jnp.arange(half, dtype=jnp.int32) + index * half + core * chunk
        members.append(
            ((place[None] >= seq_starts[:, None]) & (place[None] < seq_ends[:, None])).astype(F32)
        )
    biases = jnp.stack(
        [jnp.pad(bias.astype(F32), (0, width - local_width)) for bias in (query_bias, value_bias)]
    )

    rows, query_b, key_b, value_b, key_tb, value_tb, mixed_a, lse_a = run_first(
        lengths, core_arg, tokens, query_t, key_t, value_t, biases, (0, 1)
    )

    def own_and_other(values, weights):
        return nn(values[:half], weights), nn(values[half:], weights).astype(BF16)

    def pair(own, arrived):
        return (own + arrived.astype(F32)).astype(BF16)

    def first_norm(index, pair_here, far):
        attn_full = pair_here.astype(F32) + far.astype(F32) + output_bias.astype(F32)
        own_tokens = rows[index * chunk : index * chunk + half].astype(F32)
        return norm_forward(own_tokens + attn_full, attn_gain_f, attn_shift_f)

    def feed_forward(own_hidden):
        whole = both(own_hidden)
        act, slope = gelu_and_slope(nn(whole, inner_proj) + inner_bias.astype(F32))
        return whole, act, slope

    def last_norm(hidden, pair_here, far):
        ffn_full = pair_here.astype(F32) + far.astype(F32) + outer_bias.astype(F32)
        return norm_forward(hidden + ffn_full, final_gain_f, final_shift_f)

    attn_own_a, attn_other_a = own_and_other(mixed_a, output_proj)
    attn_pair_a = pair(attn_own_a, core_swap(attn_other_a))
    attn_far_a = far_swap(attn_pair_a)
    late_query, late_pair = tie(query_b, attn_pair_a)
    mixed_b, lse_b = run_more(lengths, core_arg, late_query, key_b, value_tb, (2, 3))
    attn_own_b, attn_other_b = own_and_other(mixed_b, output_proj)
    attn_swap_b = core_swap(attn_other_b)
    attn_far_a, mixed_late = tie(attn_far_a, mixed_b)
    hidden_a, normed_one_a, rscale_one_a = first_norm(0, late_pair, attn_far_a)
    own_hidden_a = hidden_a.astype(BF16)
    attn_pair_b = pair(attn_own_b, attn_swap_b)
    attn_far_b = far_swap(attn_pair_b)
    hidden_ab, act_a, slope_a = feed_forward(own_hidden_a)
    ffn_own_a, ffn_other_a = own_and_other(act_a, outer_proj)
    arrived, marker = marked_swap(ffn_other_a, jnp.zeros((8, 128), F32))
    ffn_pair_a = pair(ffn_own_a, arrived)
    attn_far_b, ffn_pair_late = tie(attn_far_b, ffn_pair_a)
    ffn_far_a = far_swap(ffn_pair_a)
    hidden_b, normed_one_b, rscale_one_b = first_norm(1, attn_pair_b, attn_far_b)
    own_hidden_b = hidden_b.astype(BF16)
    hidden_bb, act_b, slope_b = feed_forward(own_hidden_b)
    ffn_own_b, ffn_other_b = own_and_other(act_b, outer_proj)
    arrived, marker = marked_swap(ffn_other_b, marker)
    ffn_pair_b = pair(ffn_own_b, arrived)
    ffn_pair_b, ffn_far_a, marker = fence(ffn_pair_b, ffn_far_a, marker)
    final_a, normed_two_a, rscale_two_a = last_norm(hidden_a, ffn_pair_late, ffn_far_a)
    pooled_a = jnp.dot(members[0], final_a, precision=HIGHEST)
    final_b, normed_two_b, rscale_two_b = last_norm(hidden_b, ffn_pair_b, far_swap(ffn_pair_b))
    pooled_part = pooled_a + jnp.dot(members[1], final_b, precision=HIGHEST)
    lse = (lse_a, lse_b)
    hidden_whole, act, slope = (hidden_ab, hidden_bb), (act_a, act_b), (slope_a, slope_b)
    normed_one, rscale_one = (normed_one_a, normed_one_b), (rscale_one_a, rscale_one_b)
    normed_two, rscale_two = (normed_two_a, normed_two_b), (rscale_two_a, rscale_two_b)
    pooled = pooled_part + core_swap(pooled_part)
    pool_rscale = lax.rsqrt(jnp.sum(pooled * pooled, axis=-1, keepdims=True) + EPS_NORM)
    unit_b = (pooled * pool_rscale).astype(BF16)

    piece = lax.dynamic_slice_in_dim(unit_b, core * pair_count, pair_count, 0)
    near = near_swap(piece)
    low = (my_index % 2) == 0
    piece = jnp.concatenate([jnp.where(low, piece, near), jnp.where(low, near, piece)], axis=0)
    piece = share(piece).reshape(overall_pair_count, width)
    place_arg = jnp.stack([core, my_index]).astype(jnp.int32)
    *grads, last_sums, loss = run_loss(
        lengths,
        place_arg,
        (
            piece,
            core_swap(piece),
            pooled,
            pair_index,
            final_gain,
            normed_two[0],
            rscale_two[0],
            normed_two[1],
            rscale_two[1],
        ),
    )
    grad_second, own_grad = grads[:2], grads[2:]

    inner_sums, grad_ffn, grad_up, hidden_other = [], [], [], []
    for i in range(2):
        grad_ffn.append(both(own_grad[i]))
        grad_up.append((nt(grad_ffn[i], outer_proj) * slope[i].astype(F32)).astype(BF16))
        inner_sums.append(jnp.sum(grad_up[i].astype(F32), axis=0))
        other = nt(grad_up[i][half:], inner_proj).astype(BF16)
        arrived, marker = marked_swap(other, marker)
        hidden_other.append(arrived)
    hidden_pair = [pair(nt(grad_up[i][:half], inner_proj), hidden_other[i]) for i in range(2)]
    hidden_far = [far_swap(hidden_pair[i]) for i in range(2)]
    (late_act, late_hidden), hidden_pair = tie((act, hidden_whole), hidden_pair)
    ffn_pack = jnp.concatenate(
        [
            (tn(late_act[0], grad_ffn[0]) + tn(late_act[1], grad_ffn[1]))
            .astype(BF16)
            .reshape(16, -1, width),
            (tn(late_hidden[0], grad_up[0]) + tn(late_hidden[1], grad_up[1]))
            .astype(BF16)
            .reshape(16, -1, width),
        ],
        axis=1,
    )
    ffn_pack, hidden_far, marker = fence(ffn_pack, hidden_far, marker)
    ffn_parts = trade(ffn_pack)

    *grads, sums = run_norm(
        (
            attn_gain,
            last_sums,
            grad_second[0],
            hidden_pair[0],
            hidden_far[0],
            normed_one[0],
            rscale_one[0],
            grad_second[1],
            hidden_pair[1],
            hidden_far[1],
            normed_one[1],
            rscale_one[1],
        )
    )
    grad_first, own_grad = grads[:2], grads[2:]
    grad_query, grad_key, grad_value, packed = run_back(
        lengths,
        core_arg,
        (
            own_grad[0],
            core_swap(own_grad[0]),
            own_grad[1],
            core_swap(own_grad[1]),
            mixed_a,
            mixed_late,
            *lse,
            output_proj,
            query_b,
            key_b,
            value_b,
            key_tb,
            sums,
            core_swap(sums),
            *inner_sums,
            rows,
        ),
        marker,
    )
    (grad_query, packed), ffn_parts = tie((grad_query, packed), ffn_parts)
    packed_parts = trade(packed)
    ffn_reduced = near_sum(plane_sum(ffn_parts))
    grad_query, ffn_reduced = tie(grad_query, ffn_reduced)

    def input_part(first):
        span = slice(first, first + half)
        return (
            nt(grad_query[span], query_proj)
            + nt(grad_key[span], key_proj)
            + nt(grad_value[span], value_proj)
        )

    token_pair, marker = [], jnp.zeros((8, 128), F32)
    for i in range(2):
        other = input_part(i * chunk + half).astype(BF16)
        arrived, marker = marked_swap(other, marker)
        token_pair.append(pair(input_part(i * chunk), arrived))
    cut = width // 16
    ffn_cuts = (ffn_reduced[:cut], ffn_reduced[cut:])
    axes = (("y", "z"), ("z", "y"))
    ffn_pieces = [ring_pieces(ffn_cuts[k], axes[k][0]) for k in range(2)]
    ffn_rings = [ring_whole(ffn_cuts[k], ffn_pieces[k], axes[k][0], BF16) for k in range(2)]
    (token_pair, ffn_rings), packed_parts, marker = fence(
        (token_pair, ffn_rings), packed_parts, marker
    )
    token_far = [far_swap(token_pair[i]) for i in range(2)]
    ffn_pieces = [ring_pieces(ffn_rings[k], axes[k][1]) for k in range(2)]
    packed_sum = share(near_sum(plane_sum(packed_parts)))
    packed_sum, (token_far, ffn_pieces) = tie(packed_sum, (token_far, ffn_pieces))
    token_own = [
        (grad_first[i] + (token_pair[i].astype(F32) + token_far[i].astype(F32))).astype(BF16)
        for i in range(2)
    ]
    own_rows = jnp.concatenate(token_own, axis=0)
    other_rows = core_swap(own_rows)
    token_grad = jnp.where(
        core == 0,
        jnp.concatenate([own_rows, other_rows], axis=0),
        jnp.concatenate([other_rows, own_rows], axis=0),
    )
    ffn_place = jnp.stack([my_index // 8, (my_index // 2) % 4]).astype(jnp.int32)
    outer_grad, inner_grad = run_assemble(
        ffn_place, (ffn_rings[0], *ffn_pieces[0], ffn_rings[1], *ffn_pieces[1]), marker
    )
    packed = packed_sum.astype(F32)
    piece_rows = packed.shape[1] - 8
    cuts = packed[:, :piece_rows].reshape(4, local_width, width)
    vectors = packed[0, piece_rows:]
    return (
        loss[0, 0],
        token_grad,
        cuts[1].T,
        vectors[7, :local_width],
        cuts[2].T,
        cuts[3].T,
        vectors[7, 256 : 256 + local_width],
        cuts[0],
        vectors[0],
        vectors[1],
        vectors[2],
        inner_grad.reshape(width, width),
        vectors[6],
        outer_grad.reshape(width, width),
        vectors[3],
        vectors[4],
        vectors[5],
    )


def solution(mesh):
    column, row, split = P(None, "mp"), P("mp", None), P("mp")
    placed = (
        (P("dp", None), P("dp"), P())
        + (column, split, column, column, split, row)
        + (P(), P(), P())
        + (column, split, row)
        + (P(), P(), P())
    )
    given = (
        (P(), P("dp", None))
        + (column, split, column, column, split, row)
        + (P(), P(), P())
        + (column, split, row)
        + (P(), P(), P())
    )
    return jax.shard_map(local, mesh=mesh, in_specs=placed, out_specs=given, check_vma=False)
```

```python
import functools
import math

import jax
import jax.numpy as jnp
from jax import lax
from jax.experimental import pallas as pl
from jax.experimental.pallas import tpu as pltpu
from jax.sharding import PartitionSpec as P

HD = 64
EPS_NORM = 1e-06
SOFTMAX_WARMTH = 0.01
NEG_FILL = -1e30
HIGHEST = lax.Precision.HIGHEST
F32 = jnp.float32
BF16 = jnp.bfloat16
QB = 256
KB = 128

CORE_SWAP = [(i, i ^ 1) for i in range(4)]
FAR_SWAP = [(i, i ^ 2) for i in range(4)]
NEAR_SWAP = [(i, i ^ 1) for i in range(32)]
PLANES = [[i * 2 + x for i in range(16)] for x in range(2)]

SMEM = pl.BlockSpec(memory_space=pltpu.SMEM)
VMEM = pl.BlockSpec(memory_space=pltpu.VMEM)
HBM = pl.BlockSpec(memory_space=pltpu.HBM)


def nn(left, right):
    return lax.dot_general(left, right, (((1,), (0,)), ((), ())), preferred_element_type=F32)


def nt(left, right):
    return lax.dot_general(left, right, (((1,), (1,)), ((), ())), preferred_element_type=F32)


def tn(left, right):
    return lax.dot_general(left, right, (((0,), (0,)), ((), ())), preferred_element_type=F32)


def place_of_block(block, core, rows):
    return ((block % 2) * 2 + block // 2) * QB + core * (rows // 2) & (rows - 1)


def spot_of_keys(j, core, rows):
    place = (j * KB + core * (rows // 2)) & (rows - 1)
    block = place // QB
    return pl.multiple_of(((block % 2) * 2 + block // 2) * QB + place % QB, KB)


def segment_bounds(lengths_ref):
    bounds, total = [], jnp.int32(0)
    for s in range(lengths_ref.shape[0]):
        start = total
        total = total + lengths_ref[s]
        bounds.append((start, total))
    return bounds


def block_span(bounds, first, rows):
    place = first + lax.broadcasted_iota(jnp.int32, (1, QB), 1)
    low, high = first, first + KB
    begin = jnp.full((1, QB), bounds[-1][1], jnp.int32)
    end = jnp.full((1, QB), rows, jnp.int32)
    for start, stop in bounds:
        inside = (place >= start) & (place < stop)
        begin = jnp.where(inside, start, begin)
        end = jnp.where(inside, stop, end)
        touches = (stop > first) & (start < first + QB) & (stop > start)
        low = jnp.where(touches, jnp.minimum(low, start), low)
        high = jnp.where(touches, jnp.maximum(high, stop), high)
    return low // KB, (high + KB - 1) // KB, begin, end


def head_copies(values, heads):
    lane = lax.broadcasted_iota(jnp.int32, values.shape, 1) // HD
    blank = jnp.zeros_like(values)
    return jnp.concatenate([jnp.where(lane == h, values, blank) for h in range(heads)], axis=0)


def span_mask(begin, end, block, heads):
    place = block * KB + lax.broadcasted_iota(jnp.int32, (KB, QB), 0)
    keep = (place >= begin) & (place < end)
    return jnp.concatenate([keep] * heads, axis=1)


def attend(heads, blocks, core, bounds, q_ref, k_ref, vt_ref, mixed_ref, lse_ref, acc_ref):
    rows = k_ref.shape[0]
    for i, block in enumerate(blocks):
        low, high, begin, end = block_span(bounds, place_of_block(block, core, rows), rows)
        stack = head_copies(q_ref[block * QB : (block + 1) * QB, :], heads)
        acc_ref[...] = jnp.zeros(acc_ref.shape, F32)

        def step(j, carry, stack=stack, begin=begin, end=end):
            top, total = carry
            spot = spot_of_keys(j, core, rows)
            scores = nt(k_ref[pl.ds(spot, KB), :], stack)
            scores = jnp.where(span_mask(begin, end, j, heads), scores, NEG_FILL)
            peak = jnp.maximum(top, jnp.max(scores, axis=0, keepdims=True))
            fade = jnp.exp(top - peak)
            probs = jnp.exp(scores - peak)
            total = total * fade + jnp.sum(probs, axis=0, keepdims=True)
            probs = probs.astype(BF16)
            for h in range(heads):
                part = slice(h * QB, (h + 1) * QB)
                span = slice(h * HD, (h + 1) * HD)
                acc_ref[span, :] = acc_ref[span, :] * fade[:, part] + nn(
                    vt_ref[span, pl.ds(spot, KB)], probs[:, part]
                )
            return peak, total

        top = jnp.full((1, heads * QB), NEG_FILL, F32)
        top, total = lax.fori_loop(
            low, high, step, (top, jnp.zeros((1, heads * QB), F32)), unroll=False
        )
        scale = 1.0 / total
        mixed = jnp.concatenate(
            [
                acc_ref[h * HD : (h + 1) * HD, :] * scale[:, h * QB : (h + 1) * QB]
                for h in range(heads)
            ],
            axis=0,
        )
        mixed_ref[i * QB : (i + 1) * QB, :] = mixed.T.astype(BF16)
        lse_ref[i, :, :] = jnp.broadcast_to(top + jnp.log(total), (8, heads * QB))


def fetch(sources, targets, semaphores):
    copies = [
        pltpu.make_async_copy(source, target, semaphores.at[i])
        for i, (source, target) in enumerate(zip(sources, targets))
    ]
    for copy in copies:
        copy.start()
    return copies


def project(mixed_ref, weights_ref, results, outputs, semaphores):
    results[1][...] = nn(mixed_ref[QB:, :], weights_ref[...]).astype(BF16)
    copies = send_out(results, outputs, semaphores, (1,))
    results[0][...] = nn(mixed_ref[:QB, :], weights_ref[...])
    return copies + send_out(results, outputs, semaphores, (0,))


def attend_first(heads, blocks, lengths_ref, core_ref, *refs):
    sources, outputs, refs = refs[:7], refs[7:17], refs[17:]
    results, targets, refs = refs[:10], refs[10:16], refs[16:]
    acc_ref, semaphores, out_semaphores = refs
    x_ref, q_ref, k_ref, v_ref, kt_ref, vt_ref, mixed_ref, lse_ref = results[:8]
    wqt_ref, wkt_ref, wvt_ref, bq_ref, bv_ref, wo_ref = targets
    rows = x_ref.shape[0]
    core = core_ref[0]
    copies = fetch(sources[1:], targets, semaphores)
    row_copies = []
    for block in range(rows // QB):
        first = pl.multiple_of(place_of_block(block, core, rows), QB)
        row_copies.append(
            pltpu.make_async_copy(
                sources[0].at[pl.ds(first, QB), :],
                x_ref.at[pl.ds(block * QB, QB), :],
                semaphores.at[6 + block],
            )
        )
        row_copies[-1].start()
    for copy in copies:
        copy.wait()
    query_bias, value_bias = row_of(bq_ref), row_of(bv_ref)
    for block in range(rows // QB):
        row_copies[block].wait()
        part = slice(block * QB, (block + 1) * QB)
        x = x_ref[part, :]
        q = (nt(x, wqt_ref[...]) + query_bias).astype(BF16)
        q_ref[part, :] = q * BF16(0.125)
        k_ref[part, :] = nt(x, wkt_ref[...]).astype(BF16)
        kt_ref[:, part] = nt(wkt_ref[...], x).astype(BF16)
        v = nt(x, wvt_ref[...]) + value_bias
        v_ref[part, :] = v.astype(BF16)
        vt_ref[:, part] = v.T.astype(BF16)
    outgoing = send_out(results, outputs, out_semaphores, range(6))
    bounds = segment_bounds(lengths_ref)
    attend(heads, blocks, core, bounds, q_ref, k_ref, vt_ref, mixed_ref, lse_ref, acc_ref)
    outgoing += project(mixed_ref, wo_ref, results[8:], outputs[8:], out_semaphores.at[8:])
    outgoing += send_out(results, outputs, out_semaphores, (6, 7))
    for copy in outgoing:
        copy.wait()


def attend_more(heads, blocks, lengths_ref, core_ref, *refs):
    sources, outputs, refs = refs[:4], refs[4:8], refs[8:]
    targets, results, refs = refs[:4], refs[4:8], refs[8:]
    acc_ref, semaphores, out_semaphores = refs
    q_ref, k_ref, vt_ref, wo_ref = targets
    mixed_ref, lse_ref = results[:2]
    for copy in fetch(sources, targets, semaphores):
        copy.wait()
    bounds = segment_bounds(lengths_ref)
    attend(heads, blocks, core_ref[0], bounds, q_ref, k_ref, vt_ref, mixed_ref, lse_ref, acc_ref)
    outgoing = project(mixed_ref, wo_ref, results[2:], outputs[2:], out_semaphores.at[2:])
    outgoing += send_out(results, outputs, out_semaphores, (0, 1))
    for copy in outgoing:
        copy.wait()


def attend_back(heads, inputs, lengths_ref, core_ref, *refs):
    sources, refs = refs[:inputs], refs[inputs + 1 :]
    outputs, refs = refs[:4], refs[4:]
    gq_ref, gk_ref, gv_ref, pack_ref = refs[:4]
    dk_ref, dv_ref, dqt_ref, wo_acc_ref, semaphores, out_semaphores = refs[4:10]
    targets = refs[10:]
    copies = fetch(sources, targets, semaphores)
    grads = targets[0:4]
    mixed = targets[4:6]
    lses = targets[6:8]
    wo_ref, q_ref, k_ref, v_ref, kt_ref = targets[8:13]
    own_sums, other_sums, inner_a, inner_b, x_ref = targets[13:]
    rows, width = q_ref.shape
    core = core_ref[0]
    bounds = segment_bounds(lengths_ref)
    dk_ref[...] = jnp.zeros(dk_ref.shape, F32)
    dv_ref[...] = jnp.zeros(dv_ref.shape, F32)
    lane = lax.broadcasted_iota(jnp.int32, (8, width), 1) // HD
    which = (lane == lax.broadcasted_iota(jnp.int32, (8, width), 0)).astype(F32)
    for i in (0, 4, 6, 8, 9, 10, 11, 12):
        copies[i].wait()
    for block in range(rows // QB):
        if block > 0:
            copies[block].wait()
        if block == 2:
            copies[5].wait()
            copies[7].wait()
        low, high, begin, end = block_span(bounds, place_of_block(block, core, rows), rows)
        part = slice(block * QB, (block + 1) * QB)
        own = slice(block % 2 * QB, block % 2 * QB + QB)
        grad_attn = grads[block][...]
        mixed_here = mixed[block // 2][own, :]
        outer = tn(mixed_here, grad_attn)
        wo_acc_ref[...] = outer if block == 0 else wo_acc_ref[...] + outer
        grad_mixed = nt(grad_attn, wo_ref[...]).astype(BF16)
        product = grad_mixed.astype(F32) * mixed_here.astype(F32)
        sums = lax.dot_general(
            which,
            product,
            (((1,), (1,)), ((), ())),
            precision=HIGHEST,
            preferred_element_type=F32,
        )
        delta = jnp.concatenate([sums[h : h + 1, :] for h in range(heads)], axis=1)
        lse = lses[block // 2][block % 2, 0:1, :]
        q_stack = head_copies(q_ref[part, :], heads)
        g_stack = head_copies(grad_mixed, heads)
        dqt_ref[...] = jnp.zeros(dqt_ref.shape, F32)

        def step(
            j, carry, delta=delta, lse=lse, q_stack=q_stack, g_stack=g_stack, begin=begin, end=end
        ):
            here = pl.ds(spot_of_keys(j, core, rows), KB)
            scores = nt(k_ref[here, :], q_stack)
            scores = jnp.where(span_mask(begin, end, j, heads), scores, NEG_FILL)
            probs = jnp.exp(scores - lse)
            grad = (probs * (nt(v_ref[here, :], g_stack) - delta)).astype(BF16)
            dv_ref[here, :] += nn(probs.astype(BF16), g_stack)
            dk_ref[here, :] += nn(grad, q_stack)
            for h in range(heads):
                span = slice(h * HD, (h + 1) * HD)
                dqt_ref[span, :] += nn(kt_ref[span, here], grad[:, h * QB : (h + 1) * QB])
            return carry

        lax.fori_loop(low, high, step, 0, unroll=False)
        gq_ref[part, :] = (dqt_ref[...].T * 0.125).astype(BF16)
    gk_ref[...] = dk_ref[...].astype(BF16)
    gv_ref[...] = dv_ref[...].astype(BF16)
    for copy in copies[13:]:
        copy.wait()
    outgoing = fetch(refs[:3], outputs[:3], out_semaphores)
    sums = [jnp.sum(ref[...].astype(F32), axis=0, keepdims=True) for ref in (gq_ref, gv_ref)]
    blank = jnp.zeros((1, 256 - width), F32)
    tail = jnp.concatenate([sums[0], blank, sums[1], blank, jnp.zeros((1, 256), F32)], axis=1)
    inner = row_of(inner_a) + row_of(inner_b)
    paired = own_sums[0:6, :] + other_sums[0:6, :]
    small = jnp.concatenate([paired, inner, tail], axis=0).astype(BF16)
    piece = pack_ref.shape[1] - 8
    per = width // piece
    for m, source in enumerate((None, gq_ref, gk_ref, gv_ref)):
        total = wo_acc_ref[...] if source is None else tn(source[...], x_ref[...])
        for t in range(per):
            cut = total[t * piece : (t + 1) * piece, :].astype(BF16)
            pack_ref[m * per + t, 0:piece, :] = cut
            pack_ref[m * per + t, piece:, :] = small if m + t == 0 else jnp.zeros_like(small)
        here = pl.ds(m * per, per)
        copy = pltpu.make_async_copy(
            pack_ref.at[here], outputs[3].at[here], out_semaphores.at[3 + m]
        )
        copy.start()
        outgoing.append(copy)
    for copy in outgoing:
        copy.wait()


def shaped(shape, dtype):
    return jax.ShapeDtypeStruct(shape, dtype)


PARAMS = pltpu.CompilerParams(vmem_limit_bytes=60 << 20)
SMALL = pltpu.CompilerParams(vmem_limit_bytes=60 << 20)
COST = pl.CostEstimate(flops=1024, bytes_accessed=1024, transcendentals=0)


def buffers(arrays):
    return [pltpu.VMEM(array.shape, array.dtype) for array in arrays]


def attend_shapes(count, heads, width):
    rows = count * QB
    return (
        shaped((rows, heads * HD), BF16),
        shaped((count, 8, heads * QB), F32),
        shaped((rows // 2, width), F32),
        shaped((rows // 2, width), BF16),
    )


def run_first(lengths, core, tokens, weights, blocks):
    rows, width = tokens.shape
    local_width = weights[0].shape[0]
    heads = local_width // HD
    outs = (
        (shaped(tokens.shape, BF16),)
        + (shaped((rows, local_width), BF16),) * 3
        + (shaped((local_width, rows), BF16),) * 2
        + attend_shapes(len(blocks), heads, width)
    )
    return pl.pallas_call(
        functools.partial(attend_first, heads, blocks),
        out_shape=outs,
        in_specs=[SMEM] * 2 + [HBM] * 7,
        out_specs=(HBM,) * 10,
        scratch_shapes=buffers(outs)
        + buffers(weights)
        + [pltpu.VMEM((local_width, QB), F32)]
        + [pltpu.SemaphoreType.DMA((6 + rows // QB,)), pltpu.SemaphoreType.DMA((10,))],
        compiler_params=PARAMS,
        name="attend_first",
        cost_estimate=COST,
    )(lengths, core, tokens, *weights)


def run_more(lengths, core, arrays, blocks):
    rows, local_width = arrays[0].shape
    heads = local_width // HD
    outs = attend_shapes(len(blocks), heads, arrays[3].shape[1])
    return pl.pallas_call(
        functools.partial(attend_more, heads, blocks),
        out_shape=outs,
        in_specs=[SMEM] * 2 + [HBM] * 4,
        out_specs=(HBM,) * 4,
        scratch_shapes=buffers(arrays)
        + buffers(outs)
        + [pltpu.VMEM((local_width, QB), F32)]
        + [pltpu.SemaphoreType.DMA((4,)), pltpu.SemaphoreType.DMA((4,))],
        compiler_params=PARAMS,
        name="attend_more",
        cost_estimate=COST,
    )(lengths, core, *arrays)


def run_back(lengths, core, arrays, marker):
    wo, q, x = arrays[8], arrays[9], arrays[-1]
    rows, width = q.shape
    heads = width // HD
    piece = 4 * width // 16
    outs = (shaped((rows, width), BF16),) * 3 + (shaped((16, piece + 8, x.shape[1]), BF16),)
    return pl.pallas_call(
        functools.partial(attend_back, heads, len(arrays)),
        out_shape=outs,
        in_specs=[SMEM] * 2 + [HBM] * (len(arrays) + 1),
        out_specs=(HBM,) * 4,
        scratch_shapes=buffers(outs)
        + [pltpu.VMEM((rows, width), F32)] * 2
        + [pltpu.VMEM((width, QB), F32), pltpu.VMEM(wo.shape, F32)]
        + [pltpu.SemaphoreType.DMA((len(arrays),)), pltpu.SemaphoreType.DMA((7,))]
        + buffers(arrays),
        compiler_params=PARAMS,
        name="attend_back",
        cost_estimate=COST,
    )(lengths, core, *arrays, marker)


def mark_kernel(source_ref, target_ref):
    del source_ref, target_ref


def mark(values):
    return pl.pallas_call(
        mark_kernel,
        out_shape=shaped(values.shape, values.dtype),
        in_specs=[HBM],
        out_specs=HBM,
        compiler_params=pltpu.CompilerParams(vmem_limit_bytes=1 << 20),
        name="mark",
        cost_estimate=pl.CostEstimate(flops=1 << 36, bytes_accessed=1 << 10, transcendentals=0),
    )(values)


def finish_kernel(source_ref, target_ref):
    del source_ref
    target_ref[...] = jnp.zeros(target_ref.shape, F32)


def finish(values):
    return pl.pallas_call(
        finish_kernel,
        out_shape=shaped(values.shape, values.dtype),
        in_specs=[HBM],
        out_specs=VMEM,
        compiler_params=pltpu.CompilerParams(vmem_limit_bytes=1 << 20),
        name="finish",
        cost_estimate=COST,
    )(values)


def row_of(ref):
    return ref[...].astype(F32).reshape(1, -1)


def in_three(values):
    high = values.astype(BF16)
    rest = values - high.astype(F32)
    middle = rest.astype(BF16)
    return high, middle, (rest - middle.astype(F32)).astype(BF16)


def norm_step(grad, normed, rscale, gain):
    scaled = grad * gain
    first_mean = jnp.mean(scaled, axis=1, keepdims=True)
    cross_mean = jnp.mean(scaled * normed, axis=1, keepdims=True)
    return rscale * (scaled - first_mean - normed * cross_mean)


def column_sum(values):
    return jnp.sum(values, axis=0, keepdims=True)


def send_out(results, outputs, semaphores, which):
    copies = [
        pltpu.make_async_copy(results[k], outputs[k], semaphores.at[k]) for k in which
    ]
    for copy in copies:
        copy.start()
    return copies


def loss_back(lengths_ref, place_ref, *refs):
    sources, outputs, refs = refs[:9], refs[9:15], refs[15:]
    targets, results = refs[:9], refs[9:15]
    coef_ref, turned_ref, semaphores, out_semaphores = refs[15:]
    copies = fetch(sources, targets, semaphores)
    piece_ref, swapped_ref, pooled_ref, match_ref, gain_ref = targets[:5]
    core, index = place_ref[0], place_ref[1]
    bounds = segment_bounds(lengths_ref)
    for copy in copies[:5]:
        copy.wait()
    first = core == 0
    queries = jnp.where(first, piece_ref[...], swapped_ref[...])
    passages = jnp.where(first, swapped_ref[...], piece_ref[...])
    count = queries.shape[0]
    own = pooled_ref.shape[0] // 2
    similarity = nt(queries, passages) / SOFTMAX_WARMTH
    match = match_ref[...].reshape(1, -1)
    match = match == lax.broadcasted_iota(jnp.int32, (count, count), 0)
    top = jnp.max(similarity, axis=1, keepdims=True)
    lse = top + jnp.log(jnp.sum(jnp.exp(similarity - top), axis=1, keepdims=True))
    positive = jnp.sum(jnp.where(match, similarity, 0.0), axis=1, keepdims=True)
    loss = jnp.sum(lse - positive, axis=0, keepdims=True) / count
    results[5][...] = jnp.broadcast_to(loss, results[5].shape)
    coef = (jnp.exp(similarity - lse) - match.astype(F32)) * (1.0 / (count * SOFTMAX_WARMTH))
    coef_ref[...] = coef
    turned_ref[...] = coef.T
    here = pl.ds(pl.multiple_of(index * own, own), own)
    grad_query = sum(nn(part, passages) for part in in_three(coef_ref[here, :]))
    grad_passage = sum(nn(part, queries) for part in in_three(turned_ref[here, :]))
    grad_unit = jnp.concatenate([grad_query, grad_passage], axis=0)
    pooled = pooled_ref[...]
    rscale = lax.rsqrt(jnp.sum(pooled * pooled, axis=1, keepdims=True) + EPS_NORM)
    inner = jnp.sum(pooled * grad_unit, axis=1, keepdims=True)
    grad_pooled = rscale * grad_unit - rscale * rscale * rscale * inner * pooled
    seqs = 2 * own
    grad_pooled = jnp.concatenate(
        [grad_pooled, jnp.zeros((128 - seqs, grad_pooled.shape[1]), F32)], axis=0
    )
    parts = in_three(grad_pooled)
    lane = lax.broadcasted_iota(jnp.int32, (1, 128), 1)
    begin = end = jnp.zeros((1, 128), jnp.int32)
    for seq, (start, stop) in enumerate(bounds):
        begin = jnp.where(lane == seq, start, begin)
        end = jnp.where(lane == seq, stop, end)
    gain = row_of(gain_ref)
    sums = [0.0, 0.0, 0.0]
    outgoing = []
    for i in range(2):
        copies[5 + 2 * i].wait()
        copies[6 + 2 * i].wait()
        normed = targets[5 + 2 * i][...]
        place = core * (2 * QB) + i * QB + lax.broadcasted_iota(jnp.int32, (QB, 128), 0)
        member = jnp.where((place >= begin) & (place < end), 1.0, 0.0).astype(BF16)
        grad = sum(nn(member, part) for part in parts)
        second = norm_step(grad, normed, targets[6 + 2 * i][:, 0:1], gain)
        rounded = second.astype(BF16)
        results[i][...] = second
        results[2 + i][...] = rounded
        for k, values in enumerate((rounded.astype(F32), grad * normed, grad)):
            sums[k] = sums[k] + column_sum(values)
        outgoing += send_out(results, outputs, out_semaphores, (2 + i, i))
    results[4][...] = jnp.concatenate(sums + [jnp.zeros((5, sums[0].shape[1]), F32)], axis=0)
    outgoing += send_out(results, outputs, out_semaphores, (4, 5))
    for copy in outgoing:
        copy.wait()


def norm_back(*refs):
    sources, outputs, refs = refs[:12], refs[12:17], refs[17:]
    targets, results = refs[:12], refs[12:17]
    semaphores, out_semaphores = refs[17:]
    copies = fetch(sources, targets, semaphores)
    copies[0].wait()
    copies[1].wait()
    gain = row_of(targets[0])
    sums = [0.0, 0.0, 0.0]
    outgoing = []
    for i in range(2):
        for copy in copies[2 + 5 * i : 7 + 5 * i]:
            copy.wait()
        second, pair_here, far, normed, rscale = targets[2 + 5 * i : 7 + 5 * i]
        grad = second[...] + (pair_here[...].astype(F32) + far[...].astype(F32))
        normed = normed[...]
        first = norm_step(grad, normed, rscale[:, 0:1], gain)
        rounded = first.astype(BF16)
        results[i][...] = first
        results[2 + i][...] = rounded
        for k, values in enumerate((rounded.astype(F32), grad * normed, grad)):
            sums[k] = sums[k] + column_sum(values)
        outgoing += send_out(results, outputs, out_semaphores, (2 + i, i))
    blank = jnp.zeros((2, sums[0].shape[1]), F32)
    results[4][...] = jnp.concatenate(sums + [targets[1][0:3, :], blank], axis=0)
    outgoing += send_out(results, outputs, out_semaphores, (4,))
    for copy in outgoing:
        copy.wait()


def spread(source, *refs):
    outputs, refs = refs[:7], refs[7:]
    targets, results, semaphores, out_semaphores = refs[:7], refs[7:14], refs[14], refs[15]
    piece = targets[0].shape[1]
    views = [source.at[:, pl.ds(0, piece), :], source.at[:, pl.ds(piece, piece), :]]
    for m in range(4):
        views.append(source.at[pl.ds(4 * m, 4), pl.ds(2 * piece, piece), :])
    views.append(source.at[0, pl.ds(3 * piece, 8), :])
    copies = fetch(views, targets, semaphores)
    outgoing = []
    for k, copy in enumerate(copies):
        copy.wait()
        results[k][...] = targets[k][...].astype(F32)
        outgoing += send_out(results, outputs, out_semaphores, (k,))
    for copy in outgoing:
        copy.wait()


def run_loss(lengths, place, arrays):
    rows, width = arrays[5].shape
    count = arrays[0].shape[0]
    outs = (
        (shaped((rows, width), F32),) * 2
        + (shaped((rows, width), BF16),) * 2
        + (shaped((8, width), F32), shaped((8, 128), F32))
    )
    return pl.pallas_call(
        loss_back,
        out_shape=outs,
        in_specs=[SMEM] * 2 + [HBM] * 9,
        out_specs=(HBM,) * 6,
        scratch_shapes=buffers(arrays)
        + buffers(outs)
        + [pltpu.VMEM((count, count), F32)] * 2
        + [pltpu.SemaphoreType.DMA((9,)), pltpu.SemaphoreType.DMA((6,))],
        compiler_params=SMALL,
        name="loss_back",
        cost_estimate=COST,
    )(lengths, place, *arrays)


def run_norm(arrays):
    rows, width = arrays[2].shape
    outs = (
        (shaped((rows, width), F32),) * 2
        + (shaped((rows, width), BF16),) * 2
        + (shaped((8, width), F32),)
    )
    return pl.pallas_call(
        norm_back,
        out_shape=outs,
        in_specs=[HBM] * 12,
        out_specs=(HBM,) * 5,
        scratch_shapes=buffers(arrays)
        + buffers(outs)
        + [pltpu.SemaphoreType.DMA((12,)), pltpu.SemaphoreType.DMA((5,))],
        compiler_params=SMALL,
        name="norm_back",
        cost_estimate=COST,
    )(*arrays)


def run_spread(gathered):
    pieces, rows, width = gathered.shape
    piece = (rows - 8) // 3
    shapes = [(pieces, piece, width)] * 2 + [(4, piece, width)] * 4 + [(8, width)]
    return pl.pallas_call(
        spread,
        out_shape=[shaped(shape, F32) for shape in shapes],
        in_specs=[HBM],
        out_specs=[HBM] * 7,
        scratch_shapes=[pltpu.VMEM(shape, BF16) for shape in shapes]
        + [pltpu.VMEM(shape, F32) for shape in shapes]
        + [pltpu.SemaphoreType.DMA((7,)), pltpu.SemaphoreType.DMA((7,))],
        compiler_params=SMALL,
        name="spread",
        cost_estimate=COST,
    )(gathered)


def trade(values):
    return lax.all_to_all(
        values, "dp", split_axis=0, concat_axis=0, axis_index_groups=PLANES, tiled=True
    )


def share(values):
    return trade(jnp.broadcast_to(values[None], (16,) + values.shape))


def tie(values, others):
    return lax.optimization_barrier((values, others))


class Marker:
    def __init__(self):
        self.state = jnp.zeros((8, 128), F32)

    def fence(self, ready, later):
        ready, state = tie(ready, self.state)
        later, self.state = tie(later, mark(state))
        return ready, later

    def moved(self, values, axis, pairs):
        values, state = tie(values, self.state)
        arrived, self.state = tie(lax.ppermute(values, axis, pairs), mark(state))
        return arrived

    def core_swap(self, values):
        return self.moved(values, "mp", CORE_SWAP)

    def near_swap(self, values):
        return self.moved(values, "dp", NEAR_SWAP)

    def both(self, own):
        return jnp.concatenate([own, self.core_swap(own)], axis=0)

    def near_sum(self, total):
        return (total.astype(F32) + self.near_swap(total).astype(F32)).astype(BF16)


def plane_sum(parts):
    return jnp.sum(parts.astype(F32), axis=0).astype(BF16)


def far_swap(values):
    return lax.ppermute(values, "mp", FAR_SWAP)


def norm_forward(values, gain_vec, shift_vec):
    average = jnp.mean(values, axis=-1, keepdims=True)
    centred = values - average
    rscale = lax.rsqrt(jnp.mean(centred * centred, axis=-1, keepdims=True) + EPS_NORM)
    normed = centred * rscale
    wide = jnp.broadcast_to(rscale, (values.shape[0], 128))
    return (normed * gain_vec + shift_vec, normed, wide)


def gelu_and_slope(upper):
    below = 0.5 * (1.0 + lax.erf(upper * math.sqrt(0.5)))
    density = jnp.exp(-0.5 * upper * upper) * (1.0 / math.sqrt(2.0 * math.pi))
    return (upper * below).astype(BF16), (below + upper * density).astype(BF16)


def local(
    tokens,
    lengths,
    pair_index,
    query_proj,
    query_bias,
    key_proj,
    value_proj,
    value_bias,
    output_proj,
    output_bias,
    attn_gain,
    attn_shift,
    inner_proj,
    inner_bias,
    outer_proj,
    outer_bias,
    final_gain,
    final_shift,
):
    row_count, width = tokens.shape
    chunk = row_count // 2
    half = chunk // 2
    seq_count = lengths.shape[0]
    pair_count = seq_count // 2
    overall_pair_count = pair_index.shape[0]
    local_width = query_proj.shape[1]
    core = lax.axis_index("mp") % 2
    my_index = lax.axis_index("dp")
    marker = Marker()
    core_arg = jnp.reshape(core, (1,)).astype(jnp.int32)
    attn_gain_f, attn_shift_f = attn_gain.astype(F32), attn_shift.astype(F32)
    final_gain_f, final_shift_f = final_gain.astype(F32), final_shift.astype(F32)
    query_t, key_t, value_t = query_proj.T, key_proj.T, value_proj.T

    seq_ends = jnp.cumsum(lengths)
    seq_starts = seq_ends - lengths
    members = []
    for index in range(2):
        place = jnp.arange(half, dtype=jnp.int32) + index * half + core * chunk
        members.append(
            ((place[None] >= seq_starts[:, None]) & (place[None] < seq_ends[:, None])).astype(F32)
        )
    weights = (query_t, key_t, value_t, query_bias, value_bias, output_proj)
    first = run_first(lengths, core_arg, tokens, weights, (0, 1))
    rows, query_b, key_b, value_b, key_tb, value_tb, mixed_a, lse_a = first[:8]
    attn_own_a, attn_other_a = first[8:]

    def own_and_other(values, weights):
        return nn(values[:half], weights), nn(values[half:], weights).astype(BF16)

    def pair(own, arrived):
        return (own + arrived.astype(F32)).astype(BF16)

    def first_norm(index, pair_here, far):
        attn_full = pair_here.astype(F32) + far.astype(F32) + output_bias.astype(F32)
        own_tokens = rows[index * chunk : index * chunk + half].astype(F32)
        return norm_forward(own_tokens + attn_full, attn_gain_f, attn_shift_f)

    def feed_forward(own_hidden):
        whole = marker.both(own_hidden)
        act, slope = gelu_and_slope(nn(whole, inner_proj) + inner_bias.astype(F32))
        return whole, act, slope

    def last_norm(hidden, pair_here, far):
        ffn_full = pair_here.astype(F32) + far.astype(F32) + outer_bias.astype(F32)
        return norm_forward(hidden + ffn_full, final_gain_f, final_shift_f)

    attn_pair_a = pair(attn_own_a, marker.core_swap(attn_other_a))
    attn_far_a = far_swap(attn_pair_a)
    late_query, late_pair = tie(query_b, attn_pair_a)
    mixed_b, lse_b, attn_own_b, attn_other_b = run_more(
        lengths, core_arg, (late_query, key_b, value_tb, output_proj), (2, 3)
    )
    attn_swap_b = marker.core_swap(attn_other_b)
    attn_far_a, mixed_late = tie(attn_far_a, mixed_b)
    hidden_a, normed_one_a, rscale_one_a = first_norm(0, late_pair, attn_far_a)
    own_hidden_a = hidden_a.astype(BF16)
    attn_pair_b = pair(attn_own_b, attn_swap_b)
    attn_far_b = far_swap(attn_pair_b)
    hidden_ab, act_a, slope_a = feed_forward(own_hidden_a)
    ffn_own_a, ffn_other_a = own_and_other(act_a, outer_proj)
    ffn_pair_a = pair(ffn_own_a, marker.core_swap(ffn_other_a))
    attn_far_b, ffn_pair_late = tie(attn_far_b, ffn_pair_a)
    ffn_far_a = far_swap(ffn_pair_a)
    hidden_b, normed_one_b, rscale_one_b = first_norm(1, attn_pair_b, attn_far_b)
    own_hidden_b = hidden_b.astype(BF16)
    hidden_bb, act_b, slope_b = feed_forward(own_hidden_b)
    ffn_own_b, ffn_other_b = own_and_other(act_b, outer_proj)
    ffn_pair_b = pair(ffn_own_b, marker.core_swap(ffn_other_b))
    ffn_pair_b, ffn_far_a = marker.fence(ffn_pair_b, ffn_far_a)
    final_a, normed_two_a, rscale_two_a = last_norm(hidden_a, ffn_pair_late, ffn_far_a)
    pooled_a = jnp.dot(members[0], final_a, precision=HIGHEST)
    final_b, normed_two_b, rscale_two_b = last_norm(hidden_b, ffn_pair_b, far_swap(ffn_pair_b))
    pooled_part = pooled_a + jnp.dot(members[1], final_b, precision=HIGHEST)
    lse = (lse_a, lse_b)
    hidden_whole, act, slope = (hidden_ab, hidden_bb), (act_a, act_b), (slope_a, slope_b)
    normed_one, rscale_one = (normed_one_a, normed_one_b), (rscale_one_a, rscale_one_b)
    normed_two, rscale_two = (normed_two_a, normed_two_b), (rscale_two_a, rscale_two_b)
    pooled = pooled_part + marker.core_swap(pooled_part)
    pool_rscale = lax.rsqrt(jnp.sum(pooled * pooled, axis=-1, keepdims=True) + EPS_NORM)
    unit_b = (pooled * pool_rscale).astype(BF16)

    piece = lax.dynamic_slice_in_dim(unit_b, core * pair_count, pair_count, 0)
    near = marker.near_swap(piece)
    low = (my_index % 2) == 0
    piece = jnp.concatenate([jnp.where(low, piece, near), jnp.where(low, near, piece)], axis=0)
    piece = share(piece).reshape(overall_pair_count, width)
    place_arg = jnp.stack([core, my_index]).astype(jnp.int32)
    *grads, last_sums, loss = run_loss(
        lengths,
        place_arg,
        (
            piece,
            marker.core_swap(piece),
            pooled,
            pair_index,
            final_gain,
            normed_two[0],
            rscale_two[0],
            normed_two[1],
            rscale_two[1],
        ),
    )
    grad_second, own_grad = grads[:2], grads[2:]

    inner_sums, grad_ffn, grad_up, hidden_other = [], [], [], []
    for i in range(2):
        grad_ffn.append(marker.both(own_grad[i]))
        grad_up.append((nt(grad_ffn[i], outer_proj) * slope[i].astype(F32)).astype(BF16))
        inner_sums.append(jnp.sum(grad_up[i].astype(F32), axis=0))
        other = nt(grad_up[i][half:], inner_proj).astype(BF16)
        hidden_other.append(marker.core_swap(other))
    hidden_pair = [pair(nt(grad_up[i][:half], inner_proj), hidden_other[i]) for i in range(2)]
    hidden_far = [far_swap(hidden_pair[i]) for i in range(2)]
    (late_act, late_hidden), hidden_pair = tie((act, hidden_whole), hidden_pair)
    ffn_pack = jnp.concatenate(
        [
            (tn(late_act[0], grad_ffn[0]) + tn(late_act[1], grad_ffn[1]))
            .astype(BF16)
            .reshape(16, -1, width),
            (tn(late_hidden[0], grad_up[0]) + tn(late_hidden[1], grad_up[1]))
            .astype(BF16)
            .reshape(16, -1, width),
        ],
        axis=1,
    )
    ffn_pack, hidden_far = marker.fence(ffn_pack, hidden_far)
    ffn_parts = trade(ffn_pack)

    *grads, sums = run_norm(
        (
            attn_gain,
            last_sums,
            grad_second[0],
            hidden_pair[0],
            hidden_far[0],
            normed_one[0],
            rscale_one[0],
            grad_second[1],
            hidden_pair[1],
            hidden_far[1],
            normed_one[1],
            rscale_one[1],
        )
    )
    grad_first, own_grad = grads[:2], grads[2:]
    (*own_grad, sums), state = tie((*own_grad, sums), marker.state)
    arrived = [lax.ppermute(values, "mp", CORE_SWAP) for values in (*own_grad, sums)]
    (*other_grad, other_sums), marker.state = tie(arrived, mark(state))
    grad_query, grad_key, grad_value, packed = run_back(
        lengths,
        core_arg,
        (
            own_grad[0],
            other_grad[0],
            own_grad[1],
            other_grad[1],
            mixed_a,
            mixed_late,
            *lse,
            output_proj,
            query_b,
            key_b,
            value_b,
            key_tb,
            sums,
            other_sums,
            *inner_sums,
            rows,
        ),
        marker.state,
    )
    (grad_query, packed), ffn_parts = tie((grad_query, packed), ffn_parts)
    packed_parts = trade(packed)
    marker = Marker()
    ffn_total = plane_sum(ffn_parts)
    ffn_near = lax.ppermute(ffn_total, "dp", NEAR_SWAP)
    ffn_reduced = (ffn_total.astype(F32) + ffn_near.astype(F32)).astype(BF16)
    grad_query, ffn_reduced = tie(grad_query, ffn_reduced)

    def input_part(first):
        span = slice(first, first + half)
        return (
            nt(grad_query[span], query_proj)
            + nt(grad_key[span], key_proj)
            + nt(grad_value[span], value_proj)
        )

    token_pair = []
    for i in range(2):
        other = input_part(i * chunk + half).astype(BF16)
        token_pair.append(pair(input_part(i * chunk), marker.core_swap(other)))
    token_pair, packed_parts = marker.fence(token_pair, packed_parts)
    token_far = [far_swap(token_pair[i]) for i in range(2)]
    packed_reduced = marker.near_sum(plane_sum(packed_parts))
    reduced, token_far = marker.fence(
        jnp.concatenate([ffn_reduced, packed_reduced], axis=0), token_far
    )
    gathered = share(reduced)
    token_own = [
        (grad_first[i] + (token_pair[i].astype(F32) + token_far[i].astype(F32))).astype(BF16)
        for i in range(2)
    ]
    own_rows = jnp.concatenate(token_own, axis=0)
    other_rows = lax.ppermute(own_rows, "mp", CORE_SWAP)
    token_grad = jnp.where(
        core == 0,
        jnp.concatenate([own_rows, other_rows], axis=0),
        jnp.concatenate([other_rows, own_rows], axis=0),
    )
    token_grad, gathered = tie(token_grad, gathered)
    closing = finish(marker.state)[0, 0]
    outer_grad, inner_grad, *cuts, vectors = run_spread(gathered)
    cuts = [values.reshape(local_width, width) for values in cuts]
    return (
        loss[0, 0] + closing,
        token_grad,
        cuts[1].T,
        vectors[7, :local_width],
        cuts[2].T,
        cuts[3].T,
        vectors[7, 256 : 256 + local_width],
        cuts[0],
        vectors[0],
        vectors[1],
        vectors[2],
        inner_grad.reshape(width, width),
        vectors[6],
        outer_grad.reshape(width, width),
        vectors[3],
        vectors[4],
        vectors[5],
    )


def solution(mesh):
    column, row, split = P(None, "mp"), P("mp", None), P("mp")
    placed = (
        (P("dp", None), P("dp"), P())
        + (column, split, column, column, split, row)
        + (P(), P(), P())
        + (column, split, row)
        + (P(), P(), P())
    )
    given = (
        (P(), P("dp", None))
        + (column, split, column, column, split, row)
        + (P(), P(), P())
        + (column, split, row)
        + (P(), P(), P())
    )
    return jax.shard_map(local, mesh=mesh, in_specs=placed, out_specs=given, check_vma=False)
```

```python
import functools
import math

import jax
import jax.numpy as jnp
from jax import lax
from jax.experimental import pallas as pl
from jax.experimental.pallas import tpu as pltpu
from jax.sharding import PartitionSpec as P

HD = 64
EPS_NORM = 1e-06
SOFTMAX_WARMTH = 0.01
NEG_FILL = -1e30
HIGHEST = lax.Precision.HIGHEST
F32 = jnp.float32
BF16 = jnp.bfloat16
QB = 256
KB = 128

CORE_SWAP = [(i, i ^ 1) for i in range(4)]
FAR_SWAP = [(i, i ^ 2) for i in range(4)]
NEAR_SWAP = [(i, i ^ 1) for i in range(32)]
PLANES = [[i * 2 + x for i in range(16)] for x in range(2)]
Z_RINGS = [[i + 8 * z for z in range(4)] for i in range(8)]
Y_RINGS = [[z * 8 + x + 2 * y for y in range(4)] for z in range(4) for x in range(2)]

SMEM = pl.BlockSpec(memory_space=pltpu.SMEM)
VMEM = pl.BlockSpec(memory_space=pltpu.VMEM)
HBM = pl.BlockSpec(memory_space=pltpu.HBM)


def nn(left, right):
    return lax.dot_general(left, right, (((1,), (0,)), ((), ())), preferred_element_type=F32)


def nt(left, right):
    return lax.dot_general(left, right, (((1,), (1,)), ((), ())), preferred_element_type=F32)


def tn(left, right):
    return lax.dot_general(left, right, (((0,), (0,)), ((), ())), preferred_element_type=F32)


def place_of_block(block, core, rows):
    return ((block % 2) * 2 + block // 2) * QB + core * (rows // 2) & (rows - 1)


def spot_of_keys(j, core, rows):
    place = (j * KB + core * (rows // 2)) & (rows - 1)
    block = place // QB
    return pl.multiple_of(((block % 2) * 2 + block // 2) * QB + place % QB, KB)


def segment_bounds(lengths_ref):
    bounds, total = [], jnp.int32(0)
    for s in range(lengths_ref.shape[0]):
        start = total
        total = total + lengths_ref[s]
        bounds.append((start, total))
    return bounds


def block_span(bounds, first, rows):
    place = first + lax.broadcasted_iota(jnp.int32, (1, QB), 1)
    low, high = first, first + KB
    begin = jnp.full((1, QB), bounds[-1][1], jnp.int32)
    end = jnp.full((1, QB), rows, jnp.int32)
    for start, stop in bounds:
        inside = (place >= start) & (place < stop)
        begin = jnp.where(inside, start, begin)
        end = jnp.where(inside, stop, end)
        touches = (stop > first) & (start < first + QB) & (stop > start)
        low = jnp.where(touches, jnp.minimum(low, start), low)
        high = jnp.where(touches, jnp.maximum(high, stop), high)
    return low // KB, (high + KB - 1) // KB, begin, end


def head_copies(values, heads):
    lane = lax.broadcasted_iota(jnp.int32, values.shape, 1) // HD
    blank = jnp.zeros_like(values)
    return jnp.concatenate([jnp.where(lane == h, values, blank) for h in range(heads)], axis=0)


def span_mask(begin, end, block, heads):
    place = block * KB + lax.broadcasted_iota(jnp.int32, (KB, QB), 0)
    keep = (place >= begin) & (place < end)
    return jnp.concatenate([keep] * heads, axis=1)


def attend(heads, blocks, core, bounds, q_ref, k_ref, vt_ref, mixed_ref, lse_ref, acc_ref):
    rows = k_ref.shape[0]
    for i, block in enumerate(blocks):
        low, high, begin, end = block_span(bounds, place_of_block(block, core, rows), rows)
        stack = head_copies(q_ref[block * QB : (block + 1) * QB, :], heads)
        acc_ref[...] = jnp.zeros(acc_ref.shape, F32)

        def step(j, carry, stack=stack, begin=begin, end=end):
            top, total = carry
            spot = spot_of_keys(j, core, rows)
            scores = nt(k_ref[pl.ds(spot, KB), :], stack)
            scores = jnp.where(span_mask(begin, end, j, heads), scores, NEG_FILL)
            peak = jnp.maximum(top, jnp.max(scores, axis=0, keepdims=True))
            fade = jnp.exp(top - peak)
            probs = jnp.exp(scores - peak)
            total = total * fade + jnp.sum(probs, axis=0, keepdims=True)
            probs = probs.astype(BF16)
            for h in range(heads):
                part = slice(h * QB, (h + 1) * QB)
                span = slice(h * HD, (h + 1) * HD)
                acc_ref[span, :] = acc_ref[span, :] * fade[:, part] + nn(
                    vt_ref[span, pl.ds(spot, KB)], probs[:, part]
                )
            return peak, total

        top = jnp.full((1, heads * QB), NEG_FILL, F32)
        top, total = lax.fori_loop(
            low, high, step, (top, jnp.zeros((1, heads * QB), F32)), unroll=False
        )
        scale = 1.0 / total
        mixed = jnp.concatenate(
            [
                acc_ref[h * HD : (h + 1) * HD, :] * scale[:, h * QB : (h + 1) * QB]
                for h in range(heads)
            ],
            axis=0,
        )
        mixed_ref[i * QB : (i + 1) * QB, :] = mixed.T.astype(BF16)
        lse_ref[i, :, :] = jnp.broadcast_to(top + jnp.log(total), (8, heads * QB))


def fetch(sources, targets, semaphores):
    copies = [
        pltpu.make_async_copy(source, target, semaphores.at[i])
        for i, (source, target) in enumerate(zip(sources, targets))
    ]
    for copy in copies:
        copy.start()
    return copies


def project(mixed_ref, weights_ref, results, outputs, semaphores):
    results[1][...] = nn(mixed_ref[QB:, :], weights_ref[...]).astype(BF16)
    copies = send_out(results, outputs, semaphores, (1,))
    results[0][...] = nn(mixed_ref[:QB, :], weights_ref[...])
    return copies + send_out(results, outputs, semaphores, (0,))


def attend_first(heads, blocks, lengths_ref, core_ref, *refs):
    sources, outputs, refs = refs[:7], refs[7:17], refs[17:]
    results, targets, refs = refs[:10], refs[10:16], refs[16:]
    acc_ref, semaphores, out_semaphores = refs
    x_ref, q_ref, k_ref, v_ref, kt_ref, vt_ref, mixed_ref, lse_ref = results[:8]
    wqt_ref, wkt_ref, wvt_ref, bq_ref, bv_ref, wo_ref = targets
    rows = x_ref.shape[0]
    core = core_ref[0]
    copies = fetch(sources[1:], targets, semaphores)
    row_copies = []
    for block in range(rows // QB):
        first = pl.multiple_of(place_of_block(block, core, rows), QB)
        row_copies.append(
            pltpu.make_async_copy(
                sources[0].at[pl.ds(first, QB), :],
                x_ref.at[pl.ds(block * QB, QB), :],
                semaphores.at[6 + block],
            )
        )
        row_copies[-1].start()
    for copy in copies:
        copy.wait()
    query_bias, value_bias = row_of(bq_ref), row_of(bv_ref)
    for block in range(rows // QB):
        row_copies[block].wait()
        part = slice(block * QB, (block + 1) * QB)
        x = x_ref[part, :]
        q = (nt(x, wqt_ref[...]) + query_bias).astype(BF16)
        q_ref[part, :] = q * BF16(0.125)
        k_ref[part, :] = nt(x, wkt_ref[...]).astype(BF16)
        kt_ref[:, part] = nt(wkt_ref[...], x).astype(BF16)
        v = nt(x, wvt_ref[...]) + value_bias
        v_ref[part, :] = v.astype(BF16)
        vt_ref[:, part] = v.T.astype(BF16)
    outgoing = send_out(results, outputs, out_semaphores, range(6))
    bounds = segment_bounds(lengths_ref)
    attend(heads, blocks, core, bounds, q_ref, k_ref, vt_ref, mixed_ref, lse_ref, acc_ref)
    outgoing += project(mixed_ref, wo_ref, results[8:], outputs[8:], out_semaphores.at[8:])
    outgoing += send_out(results, outputs, out_semaphores, (6, 7))
    for copy in outgoing:
        copy.wait()


def attend_more(heads, blocks, lengths_ref, core_ref, *refs):
    sources, outputs, refs = refs[:4], refs[4:8], refs[8:]
    targets, results, refs = refs[:4], refs[4:8], refs[8:]
    acc_ref, semaphores, out_semaphores = refs
    q_ref, k_ref, vt_ref, wo_ref = targets
    mixed_ref, lse_ref = results[:2]
    for copy in fetch(sources, targets, semaphores):
        copy.wait()
    bounds = segment_bounds(lengths_ref)
    attend(heads, blocks, core_ref[0], bounds, q_ref, k_ref, vt_ref, mixed_ref, lse_ref, acc_ref)
    outgoing = project(mixed_ref, wo_ref, results[2:], outputs[2:], out_semaphores.at[2:])
    outgoing += send_out(results, outputs, out_semaphores, (0, 1))
    for copy in outgoing:
        copy.wait()


def attend_back(heads, inputs, lengths_ref, core_ref, *refs):
    sources, refs = refs[:inputs], refs[inputs + 1 :]
    outputs, refs = refs[:4], refs[4:]
    gq_ref, gk_ref, gv_ref, pack_ref = refs[:4]
    dk_ref, dv_ref, dqt_ref, wo_acc_ref, semaphores, out_semaphores = refs[4:10]
    targets = refs[10:]
    copies = fetch(sources, targets, semaphores)
    grads = targets[0:4]
    mixed = targets[4:6]
    lses = targets[6:8]
    wo_ref, q_ref, k_ref, v_ref, kt_ref = targets[8:13]
    own_sums, other_sums, inner_a, inner_b, x_ref = targets[13:]
    rows, width = q_ref.shape
    core = core_ref[0]
    bounds = segment_bounds(lengths_ref)
    dk_ref[...] = jnp.zeros(dk_ref.shape, F32)
    dv_ref[...] = jnp.zeros(dv_ref.shape, F32)
    lane = lax.broadcasted_iota(jnp.int32, (8, width), 1) // HD
    which = (lane == lax.broadcasted_iota(jnp.int32, (8, width), 0)).astype(F32)
    for i in (0, 4, 6, 8, 9, 10, 11, 12):
        copies[i].wait()
    for block in range(rows // QB):
        if block > 0:
            copies[block].wait()
        if block == 2:
            copies[5].wait()
            copies[7].wait()
        low, high, begin, end = block_span(bounds, place_of_block(block, core, rows), rows)
        part = slice(block * QB, (block + 1) * QB)
        own = slice(block % 2 * QB, block % 2 * QB + QB)
        grad_attn = grads[block][...]
        mixed_here = mixed[block // 2][own, :]
        outer = tn(mixed_here, grad_attn)
        wo_acc_ref[...] = outer if block == 0 else wo_acc_ref[...] + outer
        grad_mixed = nt(grad_attn, wo_ref[...]).astype(BF16)
        product = grad_mixed.astype(F32) * mixed_here.astype(F32)
        sums = lax.dot_general(
            which,
            product,
            (((1,), (1,)), ((), ())),
            precision=HIGHEST,
            preferred_element_type=F32,
        )
        delta = jnp.concatenate([sums[h : h + 1, :] for h in range(heads)], axis=1)
        lse = lses[block // 2][block % 2, 0:1, :]
        q_stack = head_copies(q_ref[part, :], heads)
        g_stack = head_copies(grad_mixed, heads)
        dqt_ref[...] = jnp.zeros(dqt_ref.shape, F32)

        def step(
            j, carry, delta=delta, lse=lse, q_stack=q_stack, g_stack=g_stack, begin=begin, end=end
        ):
            here = pl.ds(spot_of_keys(j, core, rows), KB)
            scores = nt(k_ref[here, :], q_stack)
            scores = jnp.where(span_mask(begin, end, j, heads), scores, NEG_FILL)
            probs = jnp.exp(scores - lse)
            grad = (probs * (nt(v_ref[here, :], g_stack) - delta)).astype(BF16)
            dv_ref[here, :] += nn(probs.astype(BF16), g_stack)
            dk_ref[here, :] += nn(grad, q_stack)
            for h in range(heads):
                span = slice(h * HD, (h + 1) * HD)
                dqt_ref[span, :] += nn(kt_ref[span, here], grad[:, h * QB : (h + 1) * QB])
            return carry

        lax.fori_loop(low, high, step, 0, unroll=False)
        gq_ref[part, :] = (dqt_ref[...].T * 0.125).astype(BF16)
    gk_ref[...] = dk_ref[...].astype(BF16)
    gv_ref[...] = dv_ref[...].astype(BF16)
    for copy in copies[13:]:
        copy.wait()
    outgoing = fetch(refs[:3], outputs[:3], out_semaphores)
    sums = [jnp.sum(ref[...].astype(F32), axis=0, keepdims=True) for ref in (gq_ref, gv_ref)]
    blank = jnp.zeros((1, 256 - width), F32)
    tail = jnp.concatenate([sums[0], blank, sums[1], blank, jnp.zeros((1, 256), F32)], axis=1)
    inner = row_of(inner_a) + row_of(inner_b)
    paired = own_sums[0:6, :] + other_sums[0:6, :]
    small = jnp.concatenate([paired, inner, tail], axis=0).astype(BF16)
    piece = pack_ref.shape[1] - 8
    per = width // piece
    for m, source in enumerate((None, gq_ref, gk_ref, gv_ref)):
        total = wo_acc_ref[...] if source is None else tn(source[...], x_ref[...])
        for t in range(per):
            cut = total[t * piece : (t + 1) * piece, :].astype(BF16)
            pack_ref[m * per + t, 0:piece, :] = cut
            pack_ref[m * per + t, piece:, :] = small if m + t == 0 else jnp.zeros_like(small)
        here = pl.ds(m * per, per)
        copy = pltpu.make_async_copy(
            pack_ref.at[here], outputs[3].at[here], out_semaphores.at[3 + m]
        )
        copy.start()
        outgoing.append(copy)
    for copy in outgoing:
        copy.wait()


def shaped(shape, dtype):
    return jax.ShapeDtypeStruct(shape, dtype)


PARAMS = pltpu.CompilerParams(vmem_limit_bytes=60 << 20)
SMALL = pltpu.CompilerParams(vmem_limit_bytes=60 << 20)
COST = pl.CostEstimate(flops=1024, bytes_accessed=1024, transcendentals=0)


def buffers(arrays):
    return [pltpu.VMEM(array.shape, array.dtype) for array in arrays]


def attend_shapes(count, heads, width):
    rows = count * QB
    return (
        shaped((rows, heads * HD), BF16),
        shaped((count, 8, heads * QB), F32),
        shaped((rows // 2, width), F32),
        shaped((rows // 2, width), BF16),
    )


def run_first(lengths, core, tokens, weights, blocks):
    rows, width = tokens.shape
    local_width = weights[0].shape[0]
    heads = local_width // HD
    outs = (
        (shaped(tokens.shape, BF16),)
        + (shaped((rows, local_width), BF16),) * 3
        + (shaped((local_width, rows), BF16),) * 2
        + attend_shapes(len(blocks), heads, width)
    )
    return pl.pallas_call(
        functools.partial(attend_first, heads, blocks),
        out_shape=outs,
        in_specs=[SMEM] * 2 + [HBM] * 7,
        out_specs=(HBM,) * 10,
        scratch_shapes=buffers(outs)
        + buffers(weights)
        + [pltpu.VMEM((local_width, QB), F32)]
        + [pltpu.SemaphoreType.DMA((6 + rows // QB,)), pltpu.SemaphoreType.DMA((10,))],
        compiler_params=PARAMS,
        name="attend_first",
        cost_estimate=COST,
    )(lengths, core, tokens, *weights)


def run_more(lengths, core, arrays, blocks):
    rows, local_width = arrays[0].shape
    heads = local_width // HD
    outs = attend_shapes(len(blocks), heads, arrays[3].shape[1])
    return pl.pallas_call(
        functools.partial(attend_more, heads, blocks),
        out_shape=outs,
        in_specs=[SMEM] * 2 + [HBM] * 4,
        out_specs=(HBM,) * 4,
        scratch_shapes=buffers(arrays)
        + buffers(outs)
        + [pltpu.VMEM((local_width, QB), F32)]
        + [pltpu.SemaphoreType.DMA((4,)), pltpu.SemaphoreType.DMA((4,))],
        compiler_params=PARAMS,
        name="attend_more",
        cost_estimate=COST,
    )(lengths, core, *arrays)


def run_back(lengths, core, arrays, marker):
    wo, q, x = arrays[8], arrays[9], arrays[-1]
    rows, width = q.shape
    heads = width // HD
    piece = 4 * width // 16
    outs = (shaped((rows, width), BF16),) * 3 + (shaped((16, piece + 8, x.shape[1]), BF16),)
    return pl.pallas_call(
        functools.partial(attend_back, heads, len(arrays)),
        out_shape=outs,
        in_specs=[SMEM] * 2 + [HBM] * (len(arrays) + 1),
        out_specs=(HBM,) * 4,
        scratch_shapes=buffers(outs)
        + [pltpu.VMEM((rows, width), F32)] * 2
        + [pltpu.VMEM((width, QB), F32), pltpu.VMEM(wo.shape, F32)]
        + [pltpu.SemaphoreType.DMA((len(arrays),)), pltpu.SemaphoreType.DMA((7,))]
        + buffers(arrays),
        compiler_params=PARAMS,
        name="attend_back",
        cost_estimate=COST,
    )(lengths, core, *arrays, marker)


def mark_kernel(source_ref, target_ref):
    del source_ref, target_ref


def mark(values):
    return pl.pallas_call(
        mark_kernel,
        out_shape=shaped(values.shape, values.dtype),
        in_specs=[HBM],
        out_specs=HBM,
        compiler_params=pltpu.CompilerParams(vmem_limit_bytes=1 << 20),
        name="mark",
        cost_estimate=pl.CostEstimate(flops=1 << 36, bytes_accessed=1 << 10, transcendentals=0),
    )(values)


def finish_kernel(source_ref, target_ref):
    del source_ref
    target_ref[...] = jnp.zeros(target_ref.shape, F32)


def finish(values):
    return pl.pallas_call(
        finish_kernel,
        out_shape=shaped(values.shape, values.dtype),
        in_specs=[HBM],
        out_specs=VMEM,
        compiler_params=pltpu.CompilerParams(vmem_limit_bytes=1 << 20),
        name="finish",
        cost_estimate=COST,
    )(values)


def row_of(ref):
    return ref[...].astype(F32).reshape(1, -1)


def in_three(values):
    high = values.astype(BF16)
    rest = values - high.astype(F32)
    middle = rest.astype(BF16)
    return high, middle, (rest - middle.astype(F32)).astype(BF16)


def norm_step(grad, normed, rscale, gain):
    scaled = grad * gain
    first_mean = jnp.mean(scaled, axis=1, keepdims=True)
    cross_mean = jnp.mean(scaled * normed, axis=1, keepdims=True)
    return rscale * (scaled - first_mean - normed * cross_mean)


def column_of(ref):
    row = ref[...].reshape(1, -1)
    return jnp.broadcast_to(row, (128, row.shape[1])).T[:, 0:1]


def column_sum(values):
    return jnp.sum(values, axis=0, keepdims=True)


def send_out(results, outputs, semaphores, which):
    copies = [
        pltpu.make_async_copy(results[k], outputs[k], semaphores.at[k]) for k in which
    ]
    for copy in copies:
        copy.start()
    return copies


def loss_back(lengths_ref, place_ref, *refs):
    sources, outputs, refs = refs[:9], refs[9:15], refs[15:]
    targets, results = refs[:9], refs[9:15]
    coef_ref, turned_ref, semaphores, out_semaphores = refs[15:]
    copies = fetch(sources, targets, semaphores)
    piece_ref, swapped_ref, pooled_ref, match_ref, gain_ref = targets[:5]
    core, index = place_ref[0], place_ref[1]
    bounds = segment_bounds(lengths_ref)
    for copy in copies[:5]:
        copy.wait()
    first = core == 0
    queries = jnp.where(first, piece_ref[...], swapped_ref[...])
    passages = jnp.where(first, swapped_ref[...], piece_ref[...])
    count = queries.shape[0]
    own = pooled_ref.shape[0] // 2
    similarity = nt(queries, passages) / SOFTMAX_WARMTH
    match = match_ref[...].reshape(1, -1)
    match = match == lax.broadcasted_iota(jnp.int32, (count, count), 0)
    top = jnp.max(similarity, axis=1, keepdims=True)
    lse = top + jnp.log(jnp.sum(jnp.exp(similarity - top), axis=1, keepdims=True))
    positive = jnp.sum(jnp.where(match, similarity, 0.0), axis=1, keepdims=True)
    loss = jnp.sum(lse - positive, axis=0, keepdims=True) / count
    results[5][...] = jnp.broadcast_to(loss, results[5].shape)
    coef = (jnp.exp(similarity - lse) - match.astype(F32)) * (1.0 / (count * SOFTMAX_WARMTH))
    coef_ref[...] = coef
    turned_ref[...] = coef.T
    here = pl.ds(pl.multiple_of(index * own, own), own)
    grad_query = sum(nn(part, passages) for part in in_three(coef_ref[here, :]))
    grad_passage = sum(nn(part, queries) for part in in_three(turned_ref[here, :]))
    grad_unit = jnp.concatenate([grad_query, grad_passage], axis=0)
    pooled = pooled_ref[...]
    rscale = lax.rsqrt(jnp.sum(pooled * pooled, axis=1, keepdims=True) + EPS_NORM)
    inner = jnp.sum(pooled * grad_unit, axis=1, keepdims=True)
    grad_pooled = rscale * grad_unit - rscale * rscale * rscale * inner * pooled
    seqs = 2 * own
    grad_pooled = jnp.concatenate(
        [grad_pooled, jnp.zeros((128 - seqs, grad_pooled.shape[1]), F32)], axis=0
    )
    parts = in_three(grad_pooled)
    lane = lax.broadcasted_iota(jnp.int32, (1, 128), 1)
    begin = end = jnp.zeros((1, 128), jnp.int32)
    for seq, (start, stop) in enumerate(bounds):
        begin = jnp.where(lane == seq, start, begin)
        end = jnp.where(lane == seq, stop, end)
    gain = row_of(gain_ref)
    sums = [0.0, 0.0, 0.0]
    outgoing = []
    for i in range(2):
        copies[5 + 2 * i].wait()
        copies[6 + 2 * i].wait()
        normed = targets[5 + 2 * i][...]
        place = core * (2 * QB) + i * QB + lax.broadcasted_iota(jnp.int32, (QB, 128), 0)
        member = jnp.where((place >= begin) & (place < end), 1.0, 0.0).astype(BF16)
        grad = sum(nn(member, part) for part in parts)
        second = norm_step(grad, normed, column_of(targets[6 + 2 * i]), gain)
        rounded = second.astype(BF16)
        results[i][...] = second
        results[2 + i][...] = rounded
        for k, values in enumerate((rounded.astype(F32), grad * normed, grad)):
            sums[k] = sums[k] + column_sum(values)
        outgoing += send_out(results, outputs, out_semaphores, (2 + i, i))
    results[4][...] = jnp.concatenate(sums + [jnp.zeros((5, sums[0].shape[1]), F32)], axis=0)
    outgoing += send_out(results, outputs, out_semaphores, (4, 5))
    for copy in outgoing:
        copy.wait()


def norm_back(*refs):
    sources, outputs, refs = refs[:12], refs[12:17], refs[17:]
    targets, results = refs[:12], refs[12:17]
    semaphores, out_semaphores = refs[17:]
    copies = fetch(sources, targets, semaphores)
    copies[0].wait()
    copies[1].wait()
    gain = row_of(targets[0])
    sums = [0.0, 0.0, 0.0]
    outgoing = []
    for i in range(2):
        for copy in copies[2 + 5 * i : 7 + 5 * i]:
            copy.wait()
        second, pair_here, far, normed, rscale = targets[2 + 5 * i : 7 + 5 * i]
        grad = second[...] + (pair_here[...].astype(F32) + far[...].astype(F32))
        normed = normed[...]
        first = norm_step(grad, normed, column_of(rscale), gain)
        rounded = first.astype(BF16)
        results[i][...] = first
        results[2 + i][...] = rounded
        for k, values in enumerate((rounded.astype(F32), grad * normed, grad)):
            sums[k] = sums[k] + column_sum(values)
        outgoing += send_out(results, outputs, out_semaphores, (2 + i, i))
    blank = jnp.zeros((2, sums[0].shape[1]), F32)
    results[4][...] = jnp.concatenate(sums + [targets[1][0:3, :], blank], axis=0)
    outgoing += send_out(results, outputs, out_semaphores, (4,))
    for copy in outgoing:
        copy.wait()


STEPS = (0, 2, 1, 3)


def join(place_ref, *refs):
    sources, output, semaphores = refs[:4], refs[4], refs[5]
    copies = []
    for k in range(4):
        spot = (place_ref[0] + 4 - STEPS[k]) % 4
        copies.append(pltpu.make_async_copy(sources[k], output.at[spot], semaphores.at[k]))
        copies[-1].start()
    for copy in copies:
        copy.wait()


def spread(piece, place_ref, *refs):
    sources, outputs, refs = refs[:5], refs[5:12], refs[12:]
    by_z, by_y = refs[:2]
    results, semaphores, out_semaphores = refs[2:9], refs[9], refs[10]
    copies = [pltpu.make_async_copy(sources[0], by_z, semaphores.at[4])]
    for k in range(4):
        spot = (place_ref[1] + 4 - STEPS[k]) % 4
        copies.append(
            pltpu.make_async_copy(sources[1 + k], by_y.at[spot], semaphores.at[k])
        )
    for copy in copies:
        copy.start()
    part = piece // 2
    copies[0].wait()
    results[0][...] = by_z[:, :, :piece, :].astype(F32)
    outgoing = send_out(results, outputs, out_semaphores, (0,))
    for copy in copies[1:]:
        copy.wait()
    for y in range(4):
        results[1][:, y] = by_y[y, :, :piece, :].astype(F32)
    outgoing += send_out(results, outputs, out_semaphores, (1,))
    for m in range(4):
        results[2 + m][:, :part, :] = by_z[m, :, piece:, :].astype(F32)
        for y in range(4):
            results[2 + m][y, part:, :] = by_y[y, m, piece : piece + part, :].astype(F32)
        outgoing += send_out(results, outputs, out_semaphores, (2 + m,))
    results[6][...] = by_y[0, 0, piece + part :, :].astype(F32)
    outgoing += send_out(results, outputs, out_semaphores, (6,))
    for copy in outgoing:
        copy.wait()


def run_loss(lengths, place, arrays):
    rows, width = arrays[5].shape
    count = arrays[0].shape[0]
    outs = (
        (shaped((rows, width), F32),) * 2
        + (shaped((rows, width), BF16),) * 2
        + (shaped((8, width), F32), shaped((8, 128), F32))
    )
    return pl.pallas_call(
        loss_back,
        out_shape=outs,
        in_specs=[SMEM] * 2 + [HBM] * 9,
        out_specs=(HBM,) * 6,
        scratch_shapes=buffers(arrays)
        + buffers(outs)
        + [pltpu.VMEM((count, count), F32)] * 2
        + [pltpu.SemaphoreType.DMA((9,)), pltpu.SemaphoreType.DMA((6,))],
        compiler_params=SMALL,
        name="loss_back",
        cost_estimate=COST,
    )(lengths, place, *arrays)


def run_norm(arrays):
    rows, width = arrays[2].shape
    outs = (
        (shaped((rows, width), F32),) * 2
        + (shaped((rows, width), BF16),) * 2
        + (shaped((8, width), F32),)
    )
    return pl.pallas_call(
        norm_back,
        out_shape=outs,
        in_specs=[HBM] * 12,
        out_specs=(HBM,) * 5,
        scratch_shapes=buffers(arrays)
        + buffers(outs)
        + [pltpu.SemaphoreType.DMA((12,)), pltpu.SemaphoreType.DMA((5,))],
        compiler_params=SMALL,
        name="norm_back",
        cost_estimate=COST,
    )(*arrays)


def run_join(places, pieces):
    return pl.pallas_call(
        join,
        out_shape=shaped((4,) + pieces[0].shape, BF16),
        in_specs=[SMEM] + [HBM] * 4,
        out_specs=HBM,
        scratch_shapes=[pltpu.SemaphoreType.DMA((4,))],
        compiler_params=pltpu.CompilerParams(vmem_limit_bytes=1 << 20),
        name="join",
        cost_estimate=COST,
    )(places, *pieces)


def run_spread(places, gathered, pieces, piece):
    width = gathered.shape[3]
    shapes = [(4, 4, piece, width)] * 2 + [(4, piece, width)] * 4 + [(8, width)]
    return pl.pallas_call(
        functools.partial(spread, piece),
        out_shape=[shaped(shape, F32) for shape in shapes],
        in_specs=[SMEM] + [HBM] * 5,
        out_specs=[HBM] * 7,
        scratch_shapes=[pltpu.VMEM(gathered.shape, BF16)]
        + [pltpu.VMEM((4,) + pieces[0].shape, BF16)]
        + [pltpu.VMEM(shape, F32) for shape in shapes]
        + [pltpu.SemaphoreType.DMA((5,)), pltpu.SemaphoreType.DMA((7,))],
        compiler_params=SMALL,
        name="spread",
        cost_estimate=COST,
    )(places, gathered, *pieces)


def trade(values):
    return lax.all_to_all(
        values, "dp", split_axis=0, concat_axis=0, axis_index_groups=PLANES, tiled=True
    )


def share(values, groups):
    spread_out = jnp.broadcast_to(values[None], (len(groups[0]),) + values.shape)
    return lax.all_to_all(
        spread_out, "dp", split_axis=0, concat_axis=0, axis_index_groups=groups, tiled=True
    )


def ring_shift(axis, step):
    pairs = []
    for i in range(32):
        z, y, x = i // 8, (i // 2) % 4, i % 2
        z, y = ((z + step) % 4, y) if axis == "z" else (z, (y + step) % 4)
        pairs.append((i, (z * 4 + y) * 2 + x))
    return pairs


def ring_pieces(values, axis):
    return [lax.ppermute(values, "dp", ring_shift(axis, step)) for step in STEPS[1:]]


def tie(values, others):
    return lax.optimization_barrier((values, others))


class Marker:
    def __init__(self):
        self.state = jnp.zeros((8, 128), F32)

    def fence(self, ready, later):
        ready, state = tie(ready, self.state)
        later, self.state = tie(later, mark(state))
        return ready, later

    def moved(self, values, axis, pairs):
        values, state = tie(values, self.state)
        arrived, self.state = tie(lax.ppermute(values, axis, pairs), mark(state))
        return arrived

    def core_swap(self, values):
        return self.moved(values, "mp", CORE_SWAP)

    def near_swap(self, values):
        return self.moved(values, "dp", NEAR_SWAP)

    def both(self, own):
        return jnp.concatenate([own, self.core_swap(own)], axis=0)

    def near_sum(self, total):
        return (total.astype(F32) + self.near_swap(total).astype(F32)).astype(BF16)


def plane_sum(parts):
    return jnp.sum(parts.astype(F32), axis=0).astype(BF16)


def far_swap(values):
    return lax.ppermute(values, "mp", FAR_SWAP)


def norm_forward(values, gain_vec, shift_vec):
    average = jnp.mean(values, axis=-1, keepdims=True)
    centred = values - average
    rscale = lax.rsqrt(jnp.mean(centred * centred, axis=-1, keepdims=True) + EPS_NORM)
    normed = centred * rscale
    return (normed * gain_vec + shift_vec, normed, rscale[:, 0])


def gelu_and_slope(upper):
    below = 0.5 * (1.0 + lax.erf(upper * math.sqrt(0.5)))
    density = jnp.exp(-0.5 * upper * upper) * (1.0 / math.sqrt(2.0 * math.pi))
    return (upper * below).astype(BF16), (below + upper * density).astype(BF16)


def local(
    tokens,
    lengths,
    pair_index,
    query_proj,
    query_bias,
    key_proj,
    value_proj,
    value_bias,
    output_proj,
    output_bias,
    attn_gain,
    attn_shift,
    inner_proj,
    inner_bias,
    outer_proj,
    outer_bias,
    final_gain,
    final_shift,
):
    row_count, width = tokens.shape
    chunk = row_count // 2
    half = chunk // 2
    seq_count = lengths.shape[0]
    pair_count = seq_count // 2
    overall_pair_count = pair_index.shape[0]
    local_width = query_proj.shape[1]
    core = lax.axis_index("mp") % 2
    my_index = lax.axis_index("dp")
    marker = Marker()
    core_arg = jnp.reshape(core, (1,)).astype(jnp.int32)
    vectors = (output_bias, attn_gain, attn_shift, outer_bias, final_gain, final_shift)
    query_t, key_t, value_t = query_proj.T, key_proj.T, value_proj.T

    weights = (query_t, key_t, value_t, query_bias, value_bias, output_proj)
    first = run_first(lengths, core_arg, tokens, weights, (0, 1))
    rows, query_b, key_b, value_b, key_tb, value_tb, mixed_a, lse_a = first[:8]
    attn_own_a, attn_other_a = first[8:]

    def own_and_other(values, weights):
        return nn(values[:half], weights), nn(values[half:], weights).astype(BF16)

    def pair(own, arrived):
        return (own + arrived.astype(F32)).astype(BF16)

    def first_norm(index, pair_here, far):
        attn_full = pair_here.astype(F32) + far.astype(F32) + output_bias
        own_tokens = rows[index * chunk : index * chunk + half].astype(F32)
        return norm_forward(own_tokens + attn_full, attn_gain_f, attn_shift_f)

    def feed_forward(own_hidden):
        whole = marker.both(own_hidden)
        act, slope = gelu_and_slope(nn(whole, inner_proj) + inner_bias.astype(F32))
        return whole, act, slope

    def last_norm(hidden, pair_here, far):
        ffn_full = pair_here.astype(F32) + far.astype(F32) + outer_bias
        return norm_forward(hidden + ffn_full, final_gain_f, final_shift_f)

    attn_pair_a = pair(attn_own_a, marker.core_swap(attn_other_a))
    attn_far_a = far_swap(attn_pair_a)
    late, late_pair = tie((query_b, lengths, vectors), attn_pair_a)
    late_query, lengths, vectors = late
    vectors = [values.astype(F32) for values in vectors]
    output_bias, attn_gain_f, attn_shift_f, outer_bias, final_gain_f, final_shift_f = vectors
    seq_ends = jnp.cumsum(lengths)
    seq_starts = seq_ends - lengths
    members = []
    for index in range(2):
        place = jnp.arange(half, dtype=jnp.int32) + index * half + core * chunk
        members.append(
            ((place[None] >= seq_starts[:, None]) & (place[None] < seq_ends[:, None])).astype(F32)
        )
    mixed_b, lse_b, attn_own_b, attn_other_b = run_more(
        lengths, core_arg, (late_query, key_b, value_tb, output_proj), (2, 3)
    )
    attn_swap_b = marker.core_swap(attn_other_b)
    attn_far_a, mixed_late = tie(attn_far_a, mixed_b)
    hidden_a, normed_one_a, rscale_one_a = first_norm(0, late_pair, attn_far_a)
    own_hidden_a = hidden_a.astype(BF16)
    attn_pair_b = pair(attn_own_b, attn_swap_b)
    attn_far_b = far_swap(attn_pair_b)
    hidden_ab, act_a, slope_a = feed_forward(own_hidden_a)
    ffn_own_a, ffn_other_a = own_and_other(act_a, outer_proj)
    ffn_pair_a = pair(ffn_own_a, marker.core_swap(ffn_other_a))
    attn_far_b, ffn_pair_late = tie(attn_far_b, ffn_pair_a)
    ffn_far_a = far_swap(ffn_pair_a)
    hidden_b, normed_one_b, rscale_one_b = first_norm(1, attn_pair_b, attn_far_b)
    own_hidden_b = hidden_b.astype(BF16)
    hidden_bb, act_b, slope_b = feed_forward(own_hidden_b)
    ffn_own_b, ffn_other_b = own_and_other(act_b, outer_proj)
    ffn_pair_b = pair(ffn_own_b, marker.core_swap(ffn_other_b))
    ffn_pair_b, ffn_far_a = marker.fence(ffn_pair_b, ffn_far_a)
    final_a, normed_two_a, rscale_two_a = last_norm(hidden_a, ffn_pair_late, ffn_far_a)
    pooled_a = jnp.dot(members[0], final_a, precision=HIGHEST)
    final_b, normed_two_b, rscale_two_b = last_norm(hidden_b, ffn_pair_b, far_swap(ffn_pair_b))
    pooled_part = pooled_a + jnp.dot(members[1], final_b, precision=HIGHEST)
    lse = (lse_a, lse_b)
    hidden_whole, act, slope = (hidden_ab, hidden_bb), (act_a, act_b), (slope_a, slope_b)
    normed_one, rscale_one = (normed_one_a, normed_one_b), (rscale_one_a, rscale_one_b)
    normed_two, rscale_two = (normed_two_a, normed_two_b), (rscale_two_a, rscale_two_b)
    pooled = pooled_part + marker.core_swap(pooled_part)
    pool_rscale = lax.rsqrt(jnp.sum(pooled * pooled, axis=-1, keepdims=True) + EPS_NORM)
    unit_b = (pooled * pool_rscale).astype(BF16)

    piece = lax.dynamic_slice_in_dim(unit_b, core * pair_count, pair_count, 0)
    near = marker.near_swap(piece)
    low = (my_index % 2) == 0
    piece = jnp.concatenate([jnp.where(low, piece, near), jnp.where(low, near, piece)], axis=0)
    piece = share(piece, PLANES).reshape(overall_pair_count, width)
    place_arg = jnp.stack([core, my_index]).astype(jnp.int32)
    *grads, last_sums, loss = run_loss(
        lengths,
        place_arg,
        (
            piece,
            marker.core_swap(piece),
            pooled,
            pair_index,
            final_gain,
            normed_two[0],
            rscale_two[0],
            normed_two[1],
            rscale_two[1],
        ),
    )
    grad_second, own_grad = grads[:2], grads[2:]

    inner_sums, grad_ffn, grad_up, hidden_other = [], [], [], []
    for i in range(2):
        grad_ffn.append(marker.both(own_grad[i]))
        grad_up.append((nt(grad_ffn[i], outer_proj) * slope[i].astype(F32)).astype(BF16))
        inner_sums.append(jnp.sum(grad_up[i].astype(F32), axis=0))
        other = nt(grad_up[i][half:], inner_proj).astype(BF16)
        hidden_other.append(marker.core_swap(other))
    hidden_pair = [pair(nt(grad_up[i][:half], inner_proj), hidden_other[i]) for i in range(2)]
    hidden_far = [far_swap(hidden_pair[i]) for i in range(2)]
    (late_act, late_hidden), hidden_pair = tie((act, hidden_whole), hidden_pair)
    ffn_pack = jnp.concatenate(
        [
            (tn(late_act[0], grad_ffn[0]) + tn(late_act[1], grad_ffn[1]))
            .astype(BF16)
            .reshape(16, -1, width),
            (tn(late_hidden[0], grad_up[0]) + tn(late_hidden[1], grad_up[1]))
            .astype(BF16)
            .reshape(16, -1, width),
        ],
        axis=1,
    )
    ffn_pack, hidden_far = marker.fence(ffn_pack, hidden_far)
    ffn_parts = trade(ffn_pack)

    *grads, sums = run_norm(
        (
            attn_gain,
            last_sums,
            grad_second[0],
            hidden_pair[0],
            hidden_far[0],
            normed_one[0],
            rscale_one[0],
            grad_second[1],
            hidden_pair[1],
            hidden_far[1],
            normed_one[1],
            rscale_one[1],
        )
    )
    grad_first, own_grad = grads[:2], grads[2:]
    (*own_grad, sums), state = tie((*own_grad, sums), marker.state)
    arrived = [lax.ppermute(values, "mp", CORE_SWAP) for values in (*own_grad, sums)]
    (*other_grad, other_sums), marker.state = tie(arrived, mark(state))
    grad_query, grad_key, grad_value, packed = run_back(
        lengths,
        core_arg,
        (
            own_grad[0],
            other_grad[0],
            own_grad[1],
            other_grad[1],
            mixed_a,
            mixed_late,
            *lse,
            output_proj,
            query_b,
            key_b,
            value_b,
            key_tb,
            sums,
            other_sums,
            *inner_sums,
            rows,
        ),
        marker.state,
    )
    (grad_query, packed), ffn_parts = tie((grad_query, packed), ffn_parts)
    packed_parts = trade(packed)
    marker = Marker()
    ffn_total = plane_sum(ffn_parts)
    ffn_near = lax.ppermute(ffn_total, "dp", NEAR_SWAP)
    ffn_reduced = (ffn_total.astype(F32) + ffn_near.astype(F32)).astype(BF16)
    grad_query, ffn_reduced = tie(grad_query, ffn_reduced)

    def input_part(first):
        span = slice(first, first + half)
        return (
            nt(grad_query[span], query_proj)
            + nt(grad_key[span], key_proj)
            + nt(grad_value[span], value_proj)
        )

    token_pair = []
    for i in range(2):
        other = input_part(i * chunk + half).astype(BF16)
        token_pair.append(pair(input_part(i * chunk), marker.core_swap(other)))
    packed_parts, token_pair = tie(packed_parts, token_pair)
    packed_reduced = marker.near_sum(plane_sum(packed_parts))
    piece_rows = width // 16
    places = jnp.stack([my_index // 8, (my_index // 2) % 4]).astype(jnp.int32)
    halves = [
        jnp.concatenate([ffn_reduced[:piece_rows], packed_reduced[: piece_rows // 2]], axis=0),
        jnp.concatenate([ffn_reduced[piece_rows:], packed_reduced[piece_rows // 2 :]], axis=0),
    ]
    one_ring = share(halves[0], Y_RINGS)
    pieces = ring_pieces(halves[1], "z")
    halves, (one_ring, pieces, token_pair) = marker.fence(halves, (one_ring, pieces, token_pair))
    other_ring = run_join(places, (halves[1], *pieces))
    gathered = share(one_ring, Z_RINGS)
    pieces = ring_pieces(other_ring, "y")
    other_ring, token_pair = marker.fence(other_ring, token_pair)
    token_far = [far_swap(token_pair[i]) for i in range(2)]
    token_own = [
        (grad_first[i] + (token_pair[i].astype(F32) + token_far[i].astype(F32))).astype(BF16)
        for i in range(2)
    ]
    own_rows = jnp.concatenate(token_own, axis=0)
    other_rows = lax.ppermute(own_rows, "mp", CORE_SWAP)
    closing = finish(marker.state)[0, 0]
    outer_grad, inner_grad, *cuts, vectors = run_spread(
        places, gathered, (other_ring, *pieces), piece_rows
    )
    other_rows, outer_grad = tie(other_rows, outer_grad)
    token_grad = jnp.where(
        core == 0,
        jnp.concatenate([own_rows, other_rows], axis=0),
        jnp.concatenate([other_rows, own_rows], axis=0),
    )
    cuts = [values.reshape(local_width, width) for values in cuts]
    return (
        loss[0, 0] + closing,
        token_grad,
        cuts[1].T,
        vectors[7, :local_width],
        cuts[2].T,
        cuts[3].T,
        vectors[7, 256 : 256 + local_width],
        cuts[0],
        vectors[0],
        vectors[1],
        vectors[2],
        inner_grad.reshape(width, width),
        vectors[6],
        outer_grad.reshape(width, width),
        vectors[3],
        vectors[4],
        vectors[5],
    )


def solution(mesh):
    column, row, split = P(None, "mp"), P("mp", None), P("mp")
    placed = (
        (P("dp", None), P("dp"), P())
        + (column, split, column, column, split, row)
        + (P(), P(), P())
        + (column, split, row)
        + (P(), P(), P())
    )
    given = (
        (P(), P("dp", None))
        + (column, split, column, column, split, row)
        + (P(), P(), P())
        + (column, split, row)
        + (P(), P(), P())
    )
    return jax.shard_map(local, mesh=mesh, in_specs=placed, out_specs=given, check_vma=False)
```

```python
import functools
import math

import jax
import jax.numpy as jnp
from jax import lax
from jax.experimental import pallas as pl
from jax.experimental.pallas import tpu as pltpu
from jax.sharding import PartitionSpec as P

HD = 64
EPS_NORM = 1e-06
SOFTMAX_WARMTH = 0.01
NEG_FILL = -1e30
HIGHEST = lax.Precision.HIGHEST
F32 = jnp.float32
BF16 = jnp.bfloat16
QB = 256
KB = 256

CORE_SWAP = [(i, i ^ 1) for i in range(4)]
FAR_SWAP = [(i, i ^ 2) for i in range(4)]
NEAR_SWAP = [(i, i ^ 1) for i in range(32)]
PLANES = [[i * 2 + x for i in range(16)] for x in range(2)]
Z_RINGS = [[i + 8 * z for z in range(4)] for i in range(8)]
Y_RINGS = [[z * 8 + x + 2 * y for y in range(4)] for z in range(4) for x in range(2)]

SMEM = pl.BlockSpec(memory_space=pltpu.SMEM)
VMEM = pl.BlockSpec(memory_space=pltpu.VMEM)
HBM = pl.BlockSpec(memory_space=pltpu.HBM)


def nn(left, right):
    return lax.dot_general(left, right, (((1,), (0,)), ((), ())), preferred_element_type=F32)


def nt(left, right):
    return lax.dot_general(left, right, (((1,), (1,)), ((), ())), preferred_element_type=F32)


def tn(left, right):
    return lax.dot_general(left, right, (((0,), (0,)), ((), ())), preferred_element_type=F32)


def place_of_block(block, core, rows):
    return ((block % 2) * 2 + block // 2) * QB + core * (rows // 2) & (rows - 1)


def spot_of_keys(j, core, rows):
    place = (j * KB + core * (rows // 2)) & (rows - 1)
    block = place // QB
    return pl.multiple_of(((block % 2) * 2 + block // 2) * QB + place % QB, KB)


def segment_bounds(lengths_ref):
    bounds, total = [], jnp.int32(0)
    for s in range(lengths_ref.shape[0]):
        start = total
        total = total + lengths_ref[s]
        bounds.append((start, total))
    return bounds


def block_span(bounds, first, rows):
    place = first + lax.broadcasted_iota(jnp.int32, (1, QB), 1)
    low, high = first, first + KB
    begin = jnp.full((1, QB), bounds[-1][1], jnp.int32)
    end = jnp.full((1, QB), rows, jnp.int32)
    for start, stop in bounds:
        inside = (place >= start) & (place < stop)
        begin = jnp.where(inside, start, begin)
        end = jnp.where(inside, stop, end)
        touches = (stop > first) & (start < first + QB) & (stop > start)
        low = jnp.where(touches, jnp.minimum(low, start), low)
        high = jnp.where(touches, jnp.maximum(high, stop), high)
    return low // KB, (high + KB - 1) // KB, begin, end


def head_copies(values, heads):
    lane = lax.broadcasted_iota(jnp.int32, values.shape, 1) // HD
    blank = jnp.zeros_like(values)
    return jnp.concatenate([jnp.where(lane == h, values, blank) for h in range(heads)], axis=0)


def span_mask(begin, end, block, heads):
    place = block * KB + lax.broadcasted_iota(jnp.int32, (KB, QB), 0)
    keep = (place >= begin) & (place < end)
    return jnp.concatenate([keep] * heads, axis=1)


def attend(heads, blocks, core, bounds, q_ref, k_ref, vt_ref, mixed_ref, lse_ref, acc_ref):
    rows = k_ref.shape[0]
    for i, block in enumerate(blocks):
        low, high, begin, end = block_span(bounds, place_of_block(block, core, rows), rows)
        stack = head_copies(q_ref[block * QB : (block + 1) * QB, :], heads)
        acc_ref[...] = jnp.zeros(acc_ref.shape, F32)

        def step(j, carry, stack=stack, begin=begin, end=end):
            top, total = carry
            spot = spot_of_keys(j, core, rows)
            scores = nt(k_ref[pl.ds(spot, KB), :], stack)
            scores = jnp.where(span_mask(begin, end, j, heads), scores, NEG_FILL)
            peak = jnp.maximum(top, jnp.max(scores, axis=0, keepdims=True))
            fade = jnp.exp(top - peak)
            probs = jnp.exp(scores - peak)
            total = total * fade + jnp.sum(probs, axis=0, keepdims=True)
            probs = probs.astype(BF16)
            for h in range(heads):
                part = slice(h * QB, (h + 1) * QB)
                span = slice(h * HD, (h + 1) * HD)
                acc_ref[span, :] = acc_ref[span, :] * fade[:, part] + nn(
                    vt_ref[span, pl.ds(spot, KB)], probs[:, part]
                )
            return peak, total

        top = jnp.full((1, heads * QB), NEG_FILL, F32)
        top, total = lax.fori_loop(
            low, high, step, (top, jnp.zeros((1, heads * QB), F32)), unroll=False
        )
        scale = 1.0 / total
        mixed = jnp.concatenate(
            [
                acc_ref[h * HD : (h + 1) * HD, :] * scale[:, h * QB : (h + 1) * QB]
                for h in range(heads)
            ],
            axis=0,
        )
        mixed_ref[i * QB : (i + 1) * QB, :] = mixed.T.astype(BF16)
        lse_ref[i, :, :] = jnp.broadcast_to(top + jnp.log(total), (8, heads * QB))


def fetch(sources, targets, semaphores, order=()):
    copies = [
        pltpu.make_async_copy(source, target, semaphores.at[i])
        for i, (source, target) in enumerate(zip(sources, targets))
    ]
    for i in [*order, *(i for i in range(len(copies)) if i not in order)]:
        copies[i].start()
    return copies


def project(mixed_ref, weights_ref, results, outputs, semaphores):
    results[1][...] = nn(mixed_ref[QB:, :], weights_ref[...]).astype(BF16)
    copies = send_out(results, outputs, semaphores, (1,))
    results[0][...] = nn(mixed_ref[:QB, :], weights_ref[...])
    return copies + send_out(results, outputs, semaphores, (0,))


def attend_first(heads, blocks, lengths_ref, core_ref, *refs):
    sources, outputs, refs = refs[:13], refs[13:25], refs[25:]
    results, targets, refs = refs[:12], refs[12:24], refs[24:]
    acc_ref, semaphores, out_semaphores = refs
    x_ref, q_ref, k_ref, v_ref, kt_ref, vt_ref, mixed_ref, lse_ref = results[:8]
    wqt_ref, wkt_ref, wvt_ref, bq_ref, bv_ref, wo_ref = targets[:6]
    rows = x_ref.shape[0]
    core = core_ref[0]
    copies = fetch(sources[1:], targets, semaphores)
    row_copies = []
    for block in range(rows // QB):
        first = pl.multiple_of(place_of_block(block, core, rows), QB)
        row_copies.append(
            pltpu.make_async_copy(
                sources[0].at[pl.ds(first, QB), :],
                x_ref.at[pl.ds(block * QB, QB), :],
                semaphores.at[12 + block],
            )
        )
        row_copies[-1].start()
    for copy in copies:
        copy.wait()
    query_bias, value_bias = row_of(bq_ref), row_of(bv_ref)
    for block in range(rows // QB):
        row_copies[block].wait()
        part = slice(block * QB, (block + 1) * QB)
        x = x_ref[part, :]
        q = (nt(x, wqt_ref[...]) + query_bias).astype(BF16)
        q_ref[part, :] = q * BF16(0.125)
        k_ref[part, :] = nt(x, wkt_ref[...]).astype(BF16)
        kt_ref[:, part] = nt(wkt_ref[...], x).astype(BF16)
        v = nt(x, wvt_ref[...]) + value_bias
        v_ref[part, :] = v.astype(BF16)
        vt_ref[:, part] = v.T.astype(BF16)
    outgoing = send_out(results, outputs, out_semaphores, range(6))
    bounds = segment_bounds(lengths_ref)
    place = core * (2 * QB) + lax.broadcasted_iota(jnp.int32, (1, QB), 1)
    for i in range(2):
        member = [
            jnp.where((place + i * QB >= start) & (place + i * QB < stop), 1.0, 0.0)
            for start, stop in bounds
        ]
        results[10][i] = jnp.concatenate(member, axis=0)
    lines = [row_of(ref) for ref in targets[6:]]
    results[11][...] = jnp.concatenate(lines + [jnp.zeros((2, lines[0].shape[1]), F32)], axis=0)
    outgoing += send_out(results, outputs, out_semaphores, (10, 11))
    attend(heads, blocks, core, bounds, q_ref, k_ref, vt_ref, mixed_ref, lse_ref, acc_ref)
    outgoing += project(mixed_ref, wo_ref, results[8:], outputs[8:], out_semaphores.at[8:10])
    outgoing += send_out(results, outputs, out_semaphores, (6, 7))
    for copy in outgoing:
        copy.wait()


def attend_more(heads, blocks, lengths_ref, core_ref, *refs):
    sources, outputs, refs = refs[:4], refs[4:8], refs[8:]
    targets, results, refs = refs[:4], refs[4:8], refs[8:]
    acc_ref, semaphores, out_semaphores = refs
    q_ref, k_ref, vt_ref, wo_ref = targets
    mixed_ref, lse_ref = results[:2]
    for copy in fetch(sources, targets, semaphores):
        copy.wait()
    bounds = segment_bounds(lengths_ref)
    attend(heads, blocks, core_ref[0], bounds, q_ref, k_ref, vt_ref, mixed_ref, lse_ref, acc_ref)
    outgoing = project(mixed_ref, wo_ref, results[2:], outputs[2:], out_semaphores.at[2:])
    outgoing += send_out(results, outputs, out_semaphores, (0, 1))
    for copy in outgoing:
        copy.wait()


def attend_back(heads, inputs, lengths_ref, core_ref, *refs):
    sources, refs = refs[:inputs], refs[inputs + 1 :]
    outputs, refs = refs[:4], refs[4:]
    gq_ref, gk_ref, gv_ref, pack_ref = refs[:4]
    dk_ref, dv_ref, dqt_ref, wo_acc_ref, semaphores, out_semaphores = refs[4:10]
    targets = refs[10:]
    copies = fetch(sources, targets, semaphores, (10, 9, 11, 12, 0, 4, 8, 6, 1, 2, 3, 5, 7))
    grads = targets[0:4]
    mixed = targets[4:6]
    lses = targets[6:8]
    wo_ref, q_ref, k_ref, v_ref, kt_ref = targets[8:13]
    own_sums, other_sums, inner_a, inner_b, x_ref = targets[13:]
    rows, width = q_ref.shape
    core = core_ref[0]
    bounds = segment_bounds(lengths_ref)
    dk_ref[...] = jnp.zeros(dk_ref.shape, F32)
    dv_ref[...] = jnp.zeros(dv_ref.shape, F32)
    lane = lax.broadcasted_iota(jnp.int32, (8, width), 1) // HD
    which = (lane == lax.broadcasted_iota(jnp.int32, (8, width), 0)).astype(F32).astype(BF16)
    for i in (0, 4, 6, 8, 9, 10, 11, 12):
        copies[i].wait()
    for block in range(rows // QB):
        if block > 0:
            copies[block].wait()
        if block == 2:
            copies[5].wait()
            copies[7].wait()
        low, high, begin, end = block_span(bounds, place_of_block(block, core, rows), rows)
        part = slice(block * QB, (block + 1) * QB)
        own = slice(block % 2 * QB, block % 2 * QB + QB)
        grad_attn = grads[block][...]
        mixed_here = mixed[block // 2][own, :]
        outer = tn(mixed_here, grad_attn)
        wo_acc_ref[...] = outer if block == 0 else wo_acc_ref[...] + outer
        grad_mixed = nt(grad_attn, wo_ref[...]).astype(BF16)
        product = grad_mixed.astype(F32) * mixed_here.astype(F32)
        sums = sum(nt(which, part) for part in in_three(product)[:2])
        delta = jnp.concatenate([sums[h : h + 1, :] for h in range(heads)], axis=1)
        lse = lses[block // 2][block % 2, 0:1, :]
        q_stack = head_copies(q_ref[part, :], heads)
        g_stack = head_copies(grad_mixed, heads)
        dqt_ref[...] = jnp.zeros(dqt_ref.shape, F32)

        def step(
            j, carry, delta=delta, lse=lse, q_stack=q_stack, g_stack=g_stack, begin=begin, end=end
        ):
            here = pl.ds(spot_of_keys(j, core, rows), KB)
            scores = nt(k_ref[here, :], q_stack)
            scores = jnp.where(span_mask(begin, end, j, heads), scores, NEG_FILL)
            probs = jnp.exp(scores - lse)
            grad = (probs * (nt(v_ref[here, :], g_stack) - delta)).astype(BF16)
            dv_ref[here, :] += nn(probs.astype(BF16), g_stack)
            dk_ref[here, :] += nn(grad, q_stack)
            for h in range(heads):
                span = slice(h * HD, (h + 1) * HD)
                dqt_ref[span, :] += nn(kt_ref[span, here], grad[:, h * QB : (h + 1) * QB])
            return carry

        lax.fori_loop(low, high, step, 0, unroll=False)
        gq_ref[part, :] = (dqt_ref[...].T * 0.125).astype(BF16)
    gk_ref[...] = dk_ref[...].astype(BF16)
    gv_ref[...] = dv_ref[...].astype(BF16)
    for copy in copies[13:]:
        copy.wait()
    outgoing = fetch(refs[:3], outputs[:3], out_semaphores)
    sums = [jnp.sum(ref[...].astype(F32), axis=0, keepdims=True) for ref in (gq_ref, gv_ref)]
    blank = jnp.zeros((1, 256 - width), F32)
    tail = jnp.concatenate([sums[0], blank, sums[1], blank, jnp.zeros((1, 256), F32)], axis=1)
    inner = row_of(inner_a) + row_of(inner_b)
    paired = own_sums[0:6, :] + other_sums[0:6, :]
    small = jnp.concatenate([paired, inner, tail], axis=0).astype(BF16)
    piece = pack_ref.shape[1] - 8
    per = width // piece
    for m, source in enumerate((None, gq_ref, gk_ref, gv_ref)):
        total = wo_acc_ref[...] if source is None else tn(source[...], x_ref[...])
        for t in range(per):
            cut = total[t * piece : (t + 1) * piece, :].astype(BF16)
            pack_ref[m * per + t, 0:piece, :] = cut
            pack_ref[m * per + t, piece:, :] = small if m + t == 0 else jnp.zeros_like(small)
        here = pl.ds(m * per, per)
        copy = pltpu.make_async_copy(
            pack_ref.at[here], outputs[3].at[here], out_semaphores.at[3 + m]
        )
        copy.start()
        outgoing.append(copy)
    for copy in outgoing:
        copy.wait()


def shaped(shape, dtype):
    return jax.ShapeDtypeStruct(shape, dtype)


PARAMS = pltpu.CompilerParams(vmem_limit_bytes=60 << 20)
SMALL = pltpu.CompilerParams(vmem_limit_bytes=60 << 20)
COST = pl.CostEstimate(flops=1024, bytes_accessed=1024, transcendentals=0)


def buffers(arrays):
    return [pltpu.VMEM(array.shape, array.dtype) for array in arrays]


def attend_shapes(count, heads, width):
    rows = count * QB
    return (
        shaped((rows, heads * HD), BF16),
        shaped((count, 8, heads * QB), F32),
        shaped((rows // 2, width), F32),
        shaped((rows // 2, width), BF16),
    )


def run_first(lengths, core, tokens, weights, blocks):
    rows, width = tokens.shape
    local_width = weights[0].shape[0]
    heads = local_width // HD
    outs = (
        (shaped(tokens.shape, BF16),)
        + (shaped((rows, local_width), BF16),) * 3
        + (shaped((local_width, rows), BF16),) * 2
        + attend_shapes(len(blocks), heads, width)
        + (shaped((2, lengths.shape[0], QB), F32), shaped((8, width), F32))
    )
    return pl.pallas_call(
        functools.partial(attend_first, heads, blocks),
        out_shape=outs,
        in_specs=[SMEM] * 2 + [HBM] * 13,
        out_specs=(HBM,) * 12,
        scratch_shapes=buffers(outs)
        + buffers(weights)
        + [pltpu.VMEM((local_width, QB), F32)]
        + [pltpu.SemaphoreType.DMA((12 + rows // QB,)), pltpu.SemaphoreType.DMA((12,))],
        compiler_params=PARAMS,
        name="attend_first",
        cost_estimate=COST,
    )(lengths, core, tokens, *weights)


def run_more(lengths, core, arrays, blocks):
    rows, local_width = arrays[0].shape
    heads = local_width // HD
    outs = attend_shapes(len(blocks), heads, arrays[3].shape[1])
    return pl.pallas_call(
        functools.partial(attend_more, heads, blocks),
        out_shape=outs,
        in_specs=[SMEM] * 2 + [HBM] * 4,
        out_specs=(HBM,) * 4,
        scratch_shapes=buffers(arrays)
        + buffers(outs)
        + [pltpu.VMEM((local_width, QB), F32)]
        + [pltpu.SemaphoreType.DMA((4,)), pltpu.SemaphoreType.DMA((4,))],
        compiler_params=PARAMS,
        name="attend_more",
        cost_estimate=COST,
    )(lengths, core, *arrays)


def run_back(lengths, core, arrays, marker):
    wo, q, x = arrays[8], arrays[9], arrays[-1]
    rows, width = q.shape
    heads = width // HD
    piece = 4 * width // 16
    outs = (shaped((rows, width), BF16),) * 3 + (shaped((16, piece + 8, x.shape[1]), BF16),)
    return pl.pallas_call(
        functools.partial(attend_back, heads, len(arrays)),
        out_shape=outs,
        in_specs=[SMEM] * 2 + [HBM] * (len(arrays) + 1),
        out_specs=(HBM,) * 4,
        scratch_shapes=buffers(outs)
        + [pltpu.VMEM((rows, width), F32)] * 2
        + [pltpu.VMEM((width, QB), F32), pltpu.VMEM(wo.shape, F32)]
        + [pltpu.SemaphoreType.DMA((len(arrays),)), pltpu.SemaphoreType.DMA((7,))]
        + buffers(arrays),
        compiler_params=PARAMS,
        name="attend_back",
        cost_estimate=COST,
    )(lengths, core, *arrays, marker)


def mark_kernel(source_ref, target_ref):
    del source_ref, target_ref


def mark(values):
    return pl.pallas_call(
        mark_kernel,
        out_shape=shaped(values.shape, values.dtype),
        in_specs=[HBM],
        out_specs=HBM,
        compiler_params=pltpu.CompilerParams(vmem_limit_bytes=1 << 20),
        name="mark",
        cost_estimate=pl.CostEstimate(flops=1 << 36, bytes_accessed=1 << 10, transcendentals=0),
    )(values)


def finish_kernel(source_ref, target_ref):
    del source_ref
    target_ref[...] = jnp.zeros(target_ref.shape, F32)


def finish(values):
    return pl.pallas_call(
        finish_kernel,
        out_shape=shaped(values.shape, values.dtype),
        in_specs=[HBM],
        out_specs=VMEM,
        compiler_params=pltpu.CompilerParams(vmem_limit_bytes=1 << 20),
        name="finish",
        cost_estimate=COST,
    )(values)


def row_of(ref):
    return ref[...].astype(F32).reshape(1, -1)


def in_three(values):
    high = values.astype(BF16)
    rest = values - high.astype(F32)
    middle = rest.astype(BF16)
    return high, middle, (rest - middle.astype(F32)).astype(BF16)


def norm_step(grad, normed, rscale, gain):
    scaled = grad * gain
    first_mean = jnp.mean(scaled, axis=1, keepdims=True)
    cross_mean = jnp.mean(scaled * normed, axis=1, keepdims=True)
    return rscale * (scaled - first_mean - normed * cross_mean)


def column_of(ref):
    row = ref[...].reshape(1, -1)
    return jnp.broadcast_to(row, (128, row.shape[1])).T[:, 0:1]


def column_sum(values):
    return jnp.sum(values, axis=0, keepdims=True)


def send_out(results, outputs, semaphores, which):
    copies = [
        pltpu.make_async_copy(results[k], outputs[k], semaphores.at[k]) for k in which
    ]
    for copy in copies:
        copy.start()
    return copies


def loss_back(lengths_ref, place_ref, *refs):
    sources, outputs, refs = refs[:9], refs[9:15], refs[15:]
    targets, results = refs[:9], refs[9:15]
    coef_ref, turned_ref, semaphores, out_semaphores = refs[15:]
    copies = fetch(sources, targets, semaphores)
    piece_ref, swapped_ref, pooled_ref, match_ref, gain_ref = targets[:5]
    core, index = place_ref[0], place_ref[1]
    bounds = segment_bounds(lengths_ref)
    for copy in copies[:5]:
        copy.wait()
    first = core == 0
    queries = jnp.where(first, piece_ref[...], swapped_ref[...])
    passages = jnp.where(first, swapped_ref[...], piece_ref[...])
    count = queries.shape[0]
    own = pooled_ref.shape[0] // 2
    similarity = nt(queries, passages) / SOFTMAX_WARMTH
    match = match_ref[...].reshape(1, -1)
    match = match == lax.broadcasted_iota(jnp.int32, (count, count), 0)
    top = jnp.max(similarity, axis=1, keepdims=True)
    lse = top + jnp.log(jnp.sum(jnp.exp(similarity - top), axis=1, keepdims=True))
    positive = jnp.sum(jnp.where(match, similarity, 0.0), axis=1, keepdims=True)
    loss = jnp.sum(lse - positive, axis=0, keepdims=True) / count
    results[5][...] = jnp.broadcast_to(loss, results[5].shape)
    coef = (jnp.exp(similarity - lse) - match.astype(F32)) * (1.0 / (count * SOFTMAX_WARMTH))
    coef_ref[...] = coef
    turned_ref[...] = coef.T
    here = pl.ds(pl.multiple_of(index * own, own), own)
    grad_query = sum(nn(part, passages) for part in in_three(coef_ref[here, :]))
    grad_passage = sum(nn(part, queries) for part in in_three(turned_ref[here, :]))
    grad_unit = jnp.concatenate([grad_query, grad_passage], axis=0)
    pooled = pooled_ref[...]
    rscale = lax.rsqrt(jnp.sum(pooled * pooled, axis=1, keepdims=True) + EPS_NORM)
    inner = jnp.sum(pooled * grad_unit, axis=1, keepdims=True)
    grad_pooled = rscale * grad_unit - rscale * rscale * rscale * inner * pooled
    seqs = 2 * own
    grad_pooled = jnp.concatenate(
        [grad_pooled, jnp.zeros((128 - seqs, grad_pooled.shape[1]), F32)], axis=0
    )
    parts = in_three(grad_pooled)
    lane = lax.broadcasted_iota(jnp.int32, (1, 128), 1)
    begin = end = jnp.zeros((1, 128), jnp.int32)
    for seq, (start, stop) in enumerate(bounds):
        begin = jnp.where(lane == seq, start, begin)
        end = jnp.where(lane == seq, stop, end)
    gain = row_of(gain_ref)
    sums = [0.0, 0.0, 0.0]
    outgoing = []
    for i in range(2):
        copies[5 + 2 * i].wait()
        copies[6 + 2 * i].wait()
        normed = targets[5 + 2 * i][...]
        place = core * (2 * QB) + i * QB + lax.broadcasted_iota(jnp.int32, (QB, 128), 0)
        member = jnp.where((place >= begin) & (place < end), 1.0, 0.0).astype(BF16)
        grad = sum(nn(member, part) for part in parts)
        second = norm_step(grad, normed, column_of(targets[6 + 2 * i]), gain)
        rounded = second.astype(BF16)
        results[i][...] = second
        results[2 + i][...] = rounded
        for k, values in enumerate((rounded.astype(F32), grad * normed, grad)):
            sums[k] = sums[k] + column_sum(values)
        outgoing += send_out(results, outputs, out_semaphores, (2 + i, i))
    results[4][...] = jnp.concatenate(sums + [jnp.zeros((5, sums[0].shape[1]), F32)], axis=0)
    outgoing += send_out(results, outputs, out_semaphores, (4, 5))
    for copy in outgoing:
        copy.wait()


def norm_back(*refs):
    sources, outputs, refs = refs[:12], refs[12:17], refs[17:]
    targets, results = refs[:12], refs[12:17]
    semaphores, out_semaphores = refs[17:]
    copies = fetch(sources, targets, semaphores)
    copies[0].wait()
    copies[1].wait()
    gain = row_of(targets[0])
    sums = [0.0, 0.0, 0.0]
    outgoing = []
    for i in range(2):
        for copy in copies[2 + 5 * i : 7 + 5 * i]:
            copy.wait()
        second, pair_here, far, normed, rscale = targets[2 + 5 * i : 7 + 5 * i]
        grad = second[...] + (pair_here[...].astype(F32) + far[...].astype(F32))
        normed = normed[...]
        first = norm_step(grad, normed, column_of(rscale), gain)
        rounded = first.astype(BF16)
        results[i][...] = first
        results[2 + i][...] = rounded
        for k, values in enumerate((rounded.astype(F32), grad * normed, grad)):
            sums[k] = sums[k] + column_sum(values)
        outgoing += send_out(results, outputs, out_semaphores, (2 + i, i))
    blank = jnp.zeros((2, sums[0].shape[1]), F32)
    results[4][...] = jnp.concatenate(sums + [targets[1][0:3, :], blank], axis=0)
    outgoing += send_out(results, outputs, out_semaphores, (4,))
    for copy in outgoing:
        copy.wait()


STEPS = (0, 2, 1, 3)


def join(place_ref, *refs):
    sources, output, semaphores = refs[:4], refs[4], refs[5]
    copies = []
    for k in range(4):
        spot = (place_ref[0] + 4 - STEPS[k]) % 4
        copies.append(pltpu.make_async_copy(sources[k], output.at[spot], semaphores.at[k]))
        copies[-1].start()
    for copy in copies:
        copy.wait()


def spread(piece, place_ref, *refs):
    sources, outputs, refs = refs[:5], refs[5:20], refs[20:]
    by_z, by_y = refs[:2]
    results, semaphores, out_semaphores = refs[2:17], refs[17], refs[18]
    copies = [pltpu.make_async_copy(sources[0], by_z, semaphores.at[4])]
    for k in range(4):
        spot = (place_ref[1] + 4 - STEPS[k]) % 4
        copies.append(
            pltpu.make_async_copy(sources[1 + k], by_y.at[spot], semaphores.at[k])
        )
    for copy in copies:
        copy.start()
    part = piece // 2
    copies[0].wait()
    results[0][...] = by_z[:, :, :piece, :].astype(F32)
    outgoing = send_out(results, outputs, out_semaphores, (0,))
    for copy in copies[1:]:
        copy.wait()
    for y in range(4):
        results[1][:, y] = by_y[y, :, :piece, :].astype(F32)
    outgoing += send_out(results, outputs, out_semaphores, (1,))
    for m in range(4):
        results[2 + m][:, :part, :] = by_z[m, :, piece:, :].astype(F32)
        for y in range(4):
            results[2 + m][y, part:, :] = by_y[y, m, piece : piece + part, :].astype(F32)
        outgoing += send_out(results, outputs, out_semaphores, (2 + m,))
    small = by_y[0, 0, piece + part :, :].astype(F32)
    for k in range(7):
        results[6 + k][...] = small[k : k + 1, :].reshape(-1)
    count = results[13].shape[0]
    for k in range(2):
        results[13 + k][...] = small[7:8, 256 * k : 256 * k + count].reshape(-1)
    outgoing += send_out(results, outputs, out_semaphores, range(6, 15))
    for copy in outgoing:
        copy.wait()


def run_loss(lengths, place, arrays):
    rows, width = arrays[5].shape
    count = arrays[0].shape[0]
    outs = (
        (shaped((rows, width), F32),) * 2
        + (shaped((rows, width), BF16),) * 2
        + (shaped((8, width), F32), shaped((8, 128), F32))
    )
    return pl.pallas_call(
        loss_back,
        out_shape=outs,
        in_specs=[SMEM] * 2 + [HBM] * 9,
        out_specs=(HBM,) * 6,
        scratch_shapes=buffers(arrays)
        + buffers(outs)
        + [pltpu.VMEM((count, count), F32)] * 2
        + [pltpu.SemaphoreType.DMA((9,)), pltpu.SemaphoreType.DMA((6,))],
        compiler_params=SMALL,
        name="loss_back",
        cost_estimate=COST,
    )(lengths, place, *arrays)


def run_norm(arrays):
    rows, width = arrays[2].shape
    outs = (
        (shaped((rows, width), F32),) * 2
        + (shaped((rows, width), BF16),) * 2
        + (shaped((8, width), F32),)
    )
    return pl.pallas_call(
        norm_back,
        out_shape=outs,
        in_specs=[HBM] * 12,
        out_specs=(HBM,) * 5,
        scratch_shapes=buffers(arrays)
        + buffers(outs)
        + [pltpu.SemaphoreType.DMA((12,)), pltpu.SemaphoreType.DMA((5,))],
        compiler_params=SMALL,
        name="norm_back",
        cost_estimate=COST,
    )(*arrays)


def run_join(places, pieces):
    return pl.pallas_call(
        join,
        out_shape=shaped((4,) + pieces[0].shape, BF16),
        in_specs=[SMEM] + [HBM] * 4,
        out_specs=HBM,
        scratch_shapes=[pltpu.SemaphoreType.DMA((4,))],
        compiler_params=pltpu.CompilerParams(vmem_limit_bytes=1 << 20),
        name="join",
        cost_estimate=COST,
    )(places, *pieces)


def settle(core_ref, *refs):
    sources, output, semaphores = refs[:4], refs[4], refs[5]
    copies = []
    for k in range(4):
        first = (k // 2 + core_ref[0]) % 2 * (2 * QB) + k % 2 * QB
        spot = pl.ds(pl.multiple_of(first, QB), QB)
        copies.append(pltpu.make_async_copy(sources[k], output.at[spot, :], semaphores.at[k]))
        copies[-1].start()
    for copy in copies:
        copy.wait()


def run_settle(core, parts):
    rows, width = parts[0].shape
    return pl.pallas_call(
        settle,
        out_shape=shaped((4 * rows, width), BF16),
        in_specs=[SMEM] + [HBM] * 4,
        out_specs=HBM,
        scratch_shapes=[pltpu.SemaphoreType.DMA((4,))],
        compiler_params=pltpu.CompilerParams(vmem_limit_bytes=1 << 20),
        name="settle",
        cost_estimate=COST,
    )(core, *parts)


def run_spread(places, gathered, pieces, piece):
    width = gathered.shape[3]
    shapes = [(4, 4, piece, width)] * 2 + [(4, piece, width)] * 4
    shapes += [(width,)] * 7 + [(4 * piece,)] * 2
    return pl.pallas_call(
        functools.partial(spread, piece),
        out_shape=[shaped(shape, F32) for shape in shapes],
        in_specs=[SMEM] + [HBM] * 5,
        out_specs=[HBM] * 15,
        scratch_shapes=[pltpu.VMEM(gathered.shape, BF16)]
        + [pltpu.VMEM((4,) + pieces[0].shape, BF16)]
        + [pltpu.VMEM(shape, F32) for shape in shapes]
        + [pltpu.SemaphoreType.DMA((5,)), pltpu.SemaphoreType.DMA((15,))],
        compiler_params=SMALL,
        name="spread",
        cost_estimate=COST,
    )(places, gathered, *pieces)


def trade(values):
    return lax.all_to_all(
        values, "dp", split_axis=0, concat_axis=0, axis_index_groups=PLANES, tiled=True
    )


def share(values, groups):
    spread_out = jnp.broadcast_to(values[None], (len(groups[0]),) + values.shape)
    return lax.all_to_all(
        spread_out, "dp", split_axis=0, concat_axis=0, axis_index_groups=groups, tiled=True
    )


def ring_shift(axis, step):
    pairs = []
    for i in range(32):
        z, y, x = i // 8, (i // 2) % 4, i % 2
        z, y = ((z + step) % 4, y) if axis == "z" else (z, (y + step) % 4)
        pairs.append((i, (z * 4 + y) * 2 + x))
    return pairs


def ring_pieces(values, axis):
    return [lax.ppermute(values, "dp", ring_shift(axis, step)) for step in STEPS[1:]]


def tie(values, others):
    return lax.optimization_barrier((values, others))


class Marker:
    def __init__(self):
        self.state = jnp.zeros((8, 128), F32)

    def fence(self, ready, later):
        ready, state = tie(ready, self.state)
        later, self.state = tie(later, mark(state))
        return ready, later

    def moved(self, values, axis, pairs):
        values, state = tie(values, self.state)
        arrived, self.state = tie(lax.ppermute(values, axis, pairs), mark(state))
        return arrived

    def core_swap(self, values):
        return self.moved(values, "mp", CORE_SWAP)

    def near_swap(self, values):
        return self.moved(values, "dp", NEAR_SWAP)

    def both(self, own):
        return jnp.concatenate([own, self.core_swap(own)], axis=0)

    def near_sum(self, total):
        return (total.astype(F32) + self.near_swap(total).astype(F32)).astype(BF16)


def plane_sum(parts):
    return jnp.sum(parts.astype(F32), axis=0).astype(BF16)


def far_swap(values):
    return lax.ppermute(values, "mp", FAR_SWAP)


def norm_forward(values, gain_vec, shift_vec):
    average = jnp.mean(values, axis=-1, keepdims=True)
    centred = values - average
    rscale = lax.rsqrt(jnp.mean(centred * centred, axis=-1, keepdims=True) + EPS_NORM)
    normed = centred * rscale
    return (normed * gain_vec + shift_vec, normed, rscale[:, 0])


def gelu_and_slope(upper):
    below = 0.5 * (1.0 + lax.erf(upper * math.sqrt(0.5)))
    density = jnp.exp(-0.5 * upper * upper) * (1.0 / math.sqrt(2.0 * math.pi))
    return (upper * below).astype(BF16), (below + upper * density).astype(BF16)


def local(
    tokens,
    lengths,
    pair_index,
    query_proj,
    query_bias,
    key_proj,
    value_proj,
    value_bias,
    output_proj,
    output_bias,
    attn_gain,
    attn_shift,
    inner_proj,
    inner_bias,
    outer_proj,
    outer_bias,
    final_gain,
    final_shift,
):
    row_count, width = tokens.shape
    chunk = row_count // 2
    half = chunk // 2
    seq_count = lengths.shape[0]
    pair_count = seq_count // 2
    overall_pair_count = pair_index.shape[0]
    local_width = query_proj.shape[1]
    core = lax.axis_index("mp") % 2
    my_index = lax.axis_index("dp")
    marker = Marker()
    core_arg = jnp.reshape(core, (1,)).astype(jnp.int32)
    vectors = (output_bias, attn_gain, attn_shift, outer_bias, final_gain, final_shift)
    query_t, key_t, value_t = query_proj.T, key_proj.T, value_proj.T

    weights = (query_t, key_t, value_t, query_bias, value_bias, output_proj, *vectors)
    first = run_first(lengths, core_arg, tokens, weights, (0, 1))
    rows, query_b, key_b, value_b, key_tb, value_tb, mixed_a, lse_a = first[:8]
    attn_own_a, attn_other_a, members, vectors = first[8:]

    def own_and_other(values, weights):
        return nn(values[:half], weights), nn(values[half:], weights).astype(BF16)

    def pair(own, arrived):
        return (own + arrived.astype(F32)).astype(BF16)

    def first_norm(index, pair_here, far):
        attn_full = pair_here.astype(F32) + far.astype(F32) + output_bias
        own_tokens = rows[index * chunk : index * chunk + half].astype(F32)
        return norm_forward(own_tokens + attn_full, attn_gain_f, attn_shift_f)

    def feed_forward(own_hidden):
        whole = marker.both(own_hidden)
        act, slope = gelu_and_slope(nn(whole, inner_proj) + inner_bias.astype(F32))
        return whole, act, slope

    def last_norm(hidden, pair_here, far):
        ffn_full = pair_here.astype(F32) + far.astype(F32) + outer_bias
        return norm_forward(hidden + ffn_full, final_gain_f, final_shift_f)

    attn_pair_a = pair(attn_own_a, marker.core_swap(attn_other_a))
    attn_far_a = far_swap(attn_pair_a)
    output_bias, attn_gain_f, attn_shift_f = vectors[0], vectors[1], vectors[2]
    outer_bias, final_gain_f, final_shift_f = vectors[3], vectors[4], vectors[5]
    late_query, late_pair = tie(query_b, attn_pair_a)
    mixed_b, lse_b, attn_own_b, attn_other_b = run_more(
        lengths, core_arg, (late_query, key_b, value_tb, output_proj), (2, 3)
    )
    attn_swap_b = marker.core_swap(attn_other_b)
    attn_far_a, mixed_late = tie(attn_far_a, mixed_b)
    hidden_a, normed_one_a, rscale_one_a = first_norm(0, late_pair, attn_far_a)
    own_hidden_a = hidden_a.astype(BF16)
    attn_pair_b = pair(attn_own_b, attn_swap_b)
    attn_far_b = far_swap(attn_pair_b)
    hidden_ab, act_a, slope_a = feed_forward(own_hidden_a)
    ffn_own_a, ffn_other_a = own_and_other(act_a, outer_proj)
    ffn_pair_a = pair(ffn_own_a, marker.core_swap(ffn_other_a))
    attn_far_b, ffn_pair_late = tie(attn_far_b, ffn_pair_a)
    ffn_far_a = far_swap(ffn_pair_a)
    hidden_b, normed_one_b, rscale_one_b = first_norm(1, attn_pair_b, attn_far_b)
    own_hidden_b = hidden_b.astype(BF16)
    hidden_bb, act_b, slope_b = feed_forward(own_hidden_b)
    ffn_own_b, ffn_other_b = own_and_other(act_b, outer_proj)
    ffn_pair_b = pair(ffn_own_b, marker.core_swap(ffn_other_b))
    ffn_pair_b, ffn_far_a = marker.fence(ffn_pair_b, ffn_far_a)
    final_a, normed_two_a, rscale_two_a = last_norm(hidden_a, ffn_pair_late, ffn_far_a)
    pooled_a = jnp.dot(members[0], final_a, precision=HIGHEST)
    final_b, normed_two_b, rscale_two_b = last_norm(hidden_b, ffn_pair_b, far_swap(ffn_pair_b))
    pooled_part = pooled_a + jnp.dot(members[1], final_b, precision=HIGHEST)
    lse = (lse_a, lse_b)
    hidden_whole, act, slope = (hidden_ab, hidden_bb), (act_a, act_b), (slope_a, slope_b)
    normed_one, rscale_one = (normed_one_a, normed_one_b), (rscale_one_a, rscale_one_b)
    normed_two, rscale_two = (normed_two_a, normed_two_b), (rscale_two_a, rscale_two_b)
    pooled = pooled_part + marker.core_swap(pooled_part)
    pool_rscale = lax.rsqrt(jnp.sum(pooled * pooled, axis=-1, keepdims=True) + EPS_NORM)
    unit_b = (pooled * pool_rscale).astype(BF16)

    piece = lax.dynamic_slice_in_dim(unit_b, core * pair_count, pair_count, 0)
    near = marker.near_swap(piece)
    low = (my_index % 2) == 0
    piece = jnp.concatenate([jnp.where(low, piece, near), jnp.where(low, near, piece)], axis=0)
    piece = share(piece, PLANES).reshape(overall_pair_count, width)
    place_arg = jnp.stack([core, my_index]).astype(jnp.int32)
    *grads, last_sums, loss = run_loss(
        lengths,
        place_arg,
        (
            piece,
            marker.core_swap(piece),
            pooled,
            pair_index,
            final_gain,
            normed_two[0],
            rscale_two[0],
            normed_two[1],
            rscale_two[1],
        ),
    )
    grad_second, own_grad = grads[:2], grads[2:]

    inner_sums, grad_ffn, grad_up, hidden_other = [], [], [], []
    for i in range(2):
        grad_ffn.append(marker.both(own_grad[i]))
        grad_up.append((nt(grad_ffn[i], outer_proj) * slope[i].astype(F32)).astype(BF16))
        inner_sums.append(jnp.sum(grad_up[i].astype(F32), axis=0))
        other = nt(grad_up[i][half:], inner_proj).astype(BF16)
        hidden_other.append(marker.core_swap(other))
    hidden_pair = [pair(nt(grad_up[i][:half], inner_proj), hidden_other[i]) for i in range(2)]
    hidden_far = [far_swap(hidden_pair[i]) for i in range(2)]
    (late_act, late_hidden), hidden_pair = tie((act, hidden_whole), hidden_pair)
    ffn_pack = jnp.concatenate(
        [
            (tn(late_act[0], grad_ffn[0]) + tn(late_act[1], grad_ffn[1]))
            .astype(BF16)
            .reshape(16, -1, width),
            (tn(late_hidden[0], grad_up[0]) + tn(late_hidden[1], grad_up[1]))
            .astype(BF16)
            .reshape(16, -1, width),
        ],
        axis=1,
    )
    ffn_pack, hidden_far = marker.fence(ffn_pack, hidden_far)
    ffn_parts = trade(ffn_pack)

    *grads, sums = run_norm(
        (
            attn_gain,
            last_sums,
            grad_second[0],
            hidden_pair[0],
            hidden_far[0],
            normed_one[0],
            rscale_one[0],
            grad_second[1],
            hidden_pair[1],
            hidden_far[1],
            normed_one[1],
            rscale_one[1],
        )
    )
    grad_first, own_grad = grads[:2], grads[2:]
    (*own_grad, sums), state = tie((*own_grad, sums), marker.state)
    arrived = [lax.ppermute(values, "mp", CORE_SWAP) for values in (*own_grad, sums)]
    (*other_grad, other_sums), marker.state = tie(arrived, mark(state))
    grad_query, grad_key, grad_value, packed = run_back(
        lengths,
        core_arg,
        (
            own_grad[0],
            other_grad[0],
            own_grad[1],
            other_grad[1],
            mixed_a,
            mixed_late,
            *lse,
            output_proj,
            query_b,
            key_b,
            value_b,
            key_tb,
            sums,
            other_sums,
            *inner_sums,
            rows,
        ),
        marker.state,
    )
    (grad_query, packed), ffn_parts = tie((grad_query, packed), ffn_parts)
    packed_parts = trade(packed)
    marker = Marker()
    ffn_total = plane_sum(ffn_parts)
    ffn_near = lax.ppermute(ffn_total, "dp", NEAR_SWAP)
    ffn_reduced = (ffn_total.astype(F32) + ffn_near.astype(F32)).astype(BF16)
    grad_query, ffn_reduced = tie(grad_query, ffn_reduced)

    def input_part(first):
        span = slice(first, first + half)
        return (
            nt(grad_query[span], query_proj)
            + nt(grad_key[span], key_proj)
            + nt(grad_value[span], value_proj)
        )

    token_pair = []
    for i in range(2):
        other = input_part(i * chunk + half).astype(BF16)
        token_pair.append(pair(input_part(i * chunk), marker.core_swap(other)))
    packed_parts, token_pair = tie(packed_parts, token_pair)
    packed_reduced = marker.near_sum(plane_sum(packed_parts))
    piece_rows = width // 16
    places = jnp.stack([my_index // 8, (my_index // 2) % 4]).astype(jnp.int32)
    halves = [
        jnp.concatenate([ffn_reduced[:piece_rows], packed_reduced[: piece_rows // 2]], axis=0),
        jnp.concatenate([ffn_reduced[piece_rows:], packed_reduced[piece_rows // 2 :]], axis=0),
    ]
    one_ring = share(halves[0], Y_RINGS)
    pieces = ring_pieces(halves[1], "z")
    halves, (one_ring, pieces, token_pair) = marker.fence(halves, (one_ring, pieces, token_pair))
    other_ring = run_join(places, (halves[1], *pieces))
    gathered = share(one_ring, Z_RINGS)
    pieces = ring_pieces(other_ring, "y")
    other_ring, token_pair = marker.fence(other_ring, token_pair)
    token_far = [far_swap(token_pair[i]) for i in range(2)]
    token_own = [
        (grad_first[i] + (token_pair[i].astype(F32) + token_far[i].astype(F32))).astype(BF16)
        for i in range(2)
    ]
    token_other = [lax.ppermute(rows_here, "mp", CORE_SWAP) for rows_here in token_own]
    closing = finish(marker.state)[0, 0]
    outer_grad, inner_grad, *rest = run_spread(
        places, gathered, (other_ring, *pieces), piece_rows
    )
    cuts = [values.reshape(local_width, width) for values in rest[:4]]
    vectors = rest[4:]
    token_other, outer_grad = tie(token_other, outer_grad)
    token_grad = run_settle(core_arg, (*token_own, *token_other))
    return (
        loss[0, 0] + closing,
        token_grad,
        cuts[1].T,
        vectors[7],
        cuts[2].T,
        cuts[3].T,
        vectors[8],
        cuts[0],
        vectors[0],
        vectors[1],
        vectors[2],
        inner_grad.reshape(width, width),
        vectors[6],
        outer_grad.reshape(width, width),
        vectors[3],
        vectors[4],
        vectors[5],
    )


def solution(mesh):
    column, row, split = P(None, "mp"), P("mp", None), P("mp")
    placed = (
        (P("dp", None), P("dp"), P())
        + (column, split, column, column, split, row)
        + (P(), P(), P())
        + (column, split, row)
        + (P(), P(), P())
    )
    given = (
        (P(), P("dp", None))
        + (column, split, column, column, split, row)
        + (P(), P(), P())
        + (column, split, row)
        + (P(), P(), P())
    )
    return jax.shard_map(local, mesh=mesh, in_specs=placed, out_specs=given, check_vma=False)
```

```python
import functools
import math

import jax
import jax.numpy as jnp
from jax import lax
from jax.experimental import pallas as pl
from jax.experimental.pallas import tpu as pltpu
from jax.sharding import PartitionSpec as P

HD = 64
EPS_NORM = 1e-06
SOFTMAX_WARMTH = 0.01
NEG_FILL = -1e30
HIGHEST = lax.Precision.HIGHEST
F32 = jnp.float32
BF16 = jnp.bfloat16
QB = 256
KB = 256

CORE_SWAP = [(i, i ^ 1) for i in range(4)]
FAR_SWAP = [(i, i ^ 2) for i in range(4)]
NEAR_SWAP = [(i, i ^ 1) for i in range(32)]
PLANES = [[i * 2 + x for i in range(16)] for x in range(2)]
Z_RINGS = [[i + 8 * z for z in range(4)] for i in range(8)]
Y_RINGS = [[z * 8 + x + 2 * y for y in range(4)] for z in range(4) for x in range(2)]

SMEM = pl.BlockSpec(memory_space=pltpu.SMEM)
VMEM = pl.BlockSpec(memory_space=pltpu.VMEM)
HBM = pl.BlockSpec(memory_space=pltpu.HBM)


def nn(left, right):
    return lax.dot_general(left, right, (((1,), (0,)), ((), ())), preferred_element_type=F32)


def nt(left, right):
    return lax.dot_general(left, right, (((1,), (1,)), ((), ())), preferred_element_type=F32)


def tn(left, right):
    return lax.dot_general(left, right, (((0,), (0,)), ((), ())), preferred_element_type=F32)


def place_of_block(block, core, rows):
    return ((block % 2) * 2 + block // 2) * QB + core * (rows // 2) & (rows - 1)


def spot_of_keys(j, core, rows):
    place = (j * KB + core * (rows // 2)) & (rows - 1)
    block = place // QB
    return pl.multiple_of(((block % 2) * 2 + block // 2) * QB + place % QB, KB)


def segment_bounds(lengths_ref):
    bounds, total = [], jnp.int32(0)
    for s in range(lengths_ref.shape[0]):
        start = total
        total = total + lengths_ref[s]
        bounds.append((start, total))
    return bounds


def block_span(bounds, first, rows):
    place = first + lax.broadcasted_iota(jnp.int32, (1, QB), 1)
    low, high = first, first + KB
    begin = jnp.full((1, QB), bounds[-1][1], jnp.int32)
    end = jnp.full((1, QB), rows, jnp.int32)
    for start, stop in bounds:
        inside = (place >= start) & (place < stop)
        begin = jnp.where(inside, start, begin)
        end = jnp.where(inside, stop, end)
        touches = (stop > first) & (start < first + QB) & (stop > start)
        low = jnp.where(touches, jnp.minimum(low, start), low)
        high = jnp.where(touches, jnp.maximum(high, stop), high)
    return low // KB, (high + KB - 1) // KB, begin, end


def head_copies(values, heads):
    lane = lax.broadcasted_iota(jnp.int32, values.shape, 1) // HD
    blank = jnp.zeros_like(values)
    return jnp.concatenate([jnp.where(lane == h, values, blank) for h in range(heads)], axis=0)


def span_mask(begin, end, block, heads):
    place = block * KB + lax.broadcasted_iota(jnp.int32, (KB, QB), 0)
    keep = (place >= begin) & (place < end)
    return jnp.concatenate([keep] * heads, axis=1)


def attend(heads, blocks, core, bounds, q_ref, k_ref, vt_ref, mixed_ref, lse_ref, acc_ref):
    rows = k_ref.shape[0]
    for i, block in enumerate(blocks):
        low, high, begin, end = block_span(bounds, place_of_block(block, core, rows), rows)
        stack = head_copies(q_ref[block * QB : (block + 1) * QB, :], heads)
        acc_ref[...] = jnp.zeros(acc_ref.shape, F32)

        def step(j, carry, stack=stack, begin=begin, end=end):
            top, total = carry
            spot = spot_of_keys(j, core, rows)
            scores = nt(k_ref[pl.ds(spot, KB), :], stack)
            scores = jnp.where(span_mask(begin, end, j, heads), scores, NEG_FILL)
            peak = jnp.maximum(top, jnp.max(scores, axis=0, keepdims=True))
            fade = jnp.exp(top - peak)
            probs = jnp.exp(scores - peak)
            total = total * fade + jnp.sum(probs, axis=0, keepdims=True)
            probs = probs.astype(BF16)
            for h in range(heads):
                part = slice(h * QB, (h + 1) * QB)
                span = slice(h * HD, (h + 1) * HD)
                acc_ref[span, :] = acc_ref[span, :] * fade[:, part] + nn(
                    vt_ref[span, pl.ds(spot, KB)], probs[:, part]
                )
            return peak, total

        top = jnp.full((1, heads * QB), NEG_FILL, F32)
        top, total = lax.fori_loop(
            low, high, step, (top, jnp.zeros((1, heads * QB), F32)), unroll=False
        )
        scale = 1.0 / total
        mixed = jnp.concatenate(
            [
                acc_ref[h * HD : (h + 1) * HD, :] * scale[:, h * QB : (h + 1) * QB]
                for h in range(heads)
            ],
            axis=0,
        )
        mixed_ref[i * QB : (i + 1) * QB, :] = mixed.T.astype(BF16)
        lse_ref[i, :, :] = jnp.broadcast_to(top + jnp.log(total), (8, heads * QB))


def fetch(sources, targets, semaphores, order=()):
    copies = [
        pltpu.make_async_copy(source, target, semaphores.at[i])
        for i, (source, target) in enumerate(zip(sources, targets))
    ]
    for i in [*order, *(i for i in range(len(copies)) if i not in order)]:
        copies[i].start()
    return copies


def project(mixed_ref, weights_ref, results, outputs, semaphores):
    results[1][...] = nn(mixed_ref[QB:, :], weights_ref[...]).astype(BF16)
    copies = send_out(results, outputs, semaphores, (1,))
    results[0][...] = nn(mixed_ref[:QB, :], weights_ref[...])
    return copies + send_out(results, outputs, semaphores, (0,))


def attend_first(heads, blocks, lengths_ref, core_ref, *refs):
    sources, outputs, refs = refs[:13], refs[13:25], refs[25:]
    results, targets, refs = refs[:12], refs[12:24], refs[24:]
    acc_ref, semaphores, out_semaphores = refs
    x_ref, q_ref, k_ref, v_ref, kt_ref, vt_ref, mixed_ref, lse_ref = results[:8]
    wqt_ref, wkt_ref, wvt_ref, bq_ref, bv_ref, wo_ref = targets[:6]
    rows = x_ref.shape[0]
    core = core_ref[0]
    copies = fetch(sources[1:], targets, semaphores)
    row_copies = []
    for block in range(rows // QB):
        first = pl.multiple_of(place_of_block(block, core, rows), QB)
        row_copies.append(
            pltpu.make_async_copy(
                sources[0].at[pl.ds(first, QB), :],
                x_ref.at[pl.ds(block * QB, QB), :],
                semaphores.at[12 + block],
            )
        )
        row_copies[-1].start()
    for copy in copies:
        copy.wait()
    query_bias, value_bias = row_of(bq_ref), row_of(bv_ref)
    for block in range(rows // QB):
        row_copies[block].wait()
        part = slice(block * QB, (block + 1) * QB)
        x = x_ref[part, :]
        q = (nt(x, wqt_ref[...]) + query_bias).astype(BF16)
        q_ref[part, :] = q * BF16(0.125)
        k_ref[part, :] = nt(x, wkt_ref[...]).astype(BF16)
        kt_ref[:, part] = nt(wkt_ref[...], x).astype(BF16)
        v = nt(x, wvt_ref[...]) + value_bias
        v_ref[part, :] = v.astype(BF16)
        vt_ref[:, part] = v.T.astype(BF16)
    outgoing = send_out(results, outputs, out_semaphores, range(6))
    bounds = segment_bounds(lengths_ref)
    place = core * (2 * QB) + lax.broadcasted_iota(jnp.int32, (1, QB), 1)
    for i in range(2):
        member = [
            jnp.where((place + i * QB >= start) & (place + i * QB < stop), 1.0, 0.0)
            for start, stop in bounds
        ]
        results[10][i] = jnp.concatenate(member, axis=0)
    lines = [row_of(ref) for ref in targets[6:]]
    results[11][...] = jnp.concatenate(lines + [jnp.zeros((2, lines[0].shape[1]), F32)], axis=0)
    outgoing += send_out(results, outputs, out_semaphores, (10, 11))
    attend(heads, blocks, core, bounds, q_ref, k_ref, vt_ref, mixed_ref, lse_ref, acc_ref)
    outgoing += project(mixed_ref, wo_ref, results[8:], outputs[8:], out_semaphores.at[8:10])
    outgoing += send_out(results, outputs, out_semaphores, (6, 7))
    for copy in outgoing:
        copy.wait()


def attend_more(heads, blocks, lengths_ref, core_ref, *refs):
    sources, outputs, refs = refs[:4], refs[4:8], refs[8:]
    targets, results, refs = refs[:4], refs[4:8], refs[8:]
    acc_ref, semaphores, out_semaphores = refs
    q_ref, k_ref, vt_ref, wo_ref = targets
    mixed_ref, lse_ref = results[:2]
    for copy in fetch(sources, targets, semaphores):
        copy.wait()
    bounds = segment_bounds(lengths_ref)
    attend(heads, blocks, core_ref[0], bounds, q_ref, k_ref, vt_ref, mixed_ref, lse_ref, acc_ref)
    outgoing = project(mixed_ref, wo_ref, results[2:], outputs[2:], out_semaphores.at[2:])
    outgoing += send_out(results, outputs, out_semaphores, (0, 1))
    for copy in outgoing:
        copy.wait()


def attend_back(heads, inputs, lengths_ref, core_ref, *refs):
    sources, refs = refs[:inputs], refs[inputs + 1 :]
    outputs, refs = refs[:4], refs[4:]
    gq_ref, gk_ref, gv_ref, pack_ref = refs[:4]
    dk_ref, dv_ref, dqt_ref, wo_acc_ref, semaphores, out_semaphores = refs[4:10]
    targets = refs[10:]
    copies = fetch(sources, targets, semaphores, (10, 9, 11, 12, 0, 4, 8, 6, 1, 2, 3, 5, 7))
    grads = targets[0:4]
    mixed = targets[4:6]
    lses = targets[6:8]
    wo_ref, q_ref, k_ref, v_ref, kt_ref = targets[8:13]
    own_sums, other_sums, inner_a, inner_b, x_ref = targets[13:]
    rows, width = q_ref.shape
    core = core_ref[0]
    bounds = segment_bounds(lengths_ref)
    dk_ref[...] = jnp.zeros(dk_ref.shape, F32)
    dv_ref[...] = jnp.zeros(dv_ref.shape, F32)
    lane = lax.broadcasted_iota(jnp.int32, (8, width), 1) // HD
    which = (lane == lax.broadcasted_iota(jnp.int32, (8, width), 0)).astype(F32).astype(BF16)
    for i in (0, 4, 6, 8, 9, 10, 11, 12):
        copies[i].wait()
    for block in range(rows // QB):
        if block > 0:
            copies[block].wait()
        if block == 2:
            copies[5].wait()
            copies[7].wait()
        low, high, begin, end = block_span(bounds, place_of_block(block, core, rows), rows)
        part = slice(block * QB, (block + 1) * QB)
        own = slice(block % 2 * QB, block % 2 * QB + QB)
        grad_attn = grads[block][...]
        mixed_here = mixed[block // 2][own, :]
        outer = tn(mixed_here, grad_attn)
        wo_acc_ref[...] = outer if block == 0 else wo_acc_ref[...] + outer
        grad_mixed = nt(grad_attn, wo_ref[...]).astype(BF16)
        product = grad_mixed.astype(F32) * mixed_here.astype(F32)
        sums = sum(nt(which, part) for part in in_three(product)[:2])
        delta = jnp.concatenate([sums[h : h + 1, :] for h in range(heads)], axis=1)
        lse = lses[block // 2][block % 2, 0:1, :]
        q_stack = head_copies(q_ref[part, :], heads)
        g_stack = head_copies(grad_mixed, heads)
        dqt_ref[...] = jnp.zeros(dqt_ref.shape, F32)

        def step(
            j, carry, delta=delta, lse=lse, q_stack=q_stack, g_stack=g_stack, begin=begin, end=end
        ):
            here = pl.ds(spot_of_keys(j, core, rows), KB)
            scores = nt(k_ref[here, :], q_stack)
            scores = jnp.where(span_mask(begin, end, j, heads), scores, NEG_FILL)
            probs = jnp.exp(scores - lse)
            grad = (probs * (nt(v_ref[here, :], g_stack) - delta)).astype(BF16)
            dv_ref[here, :] += nn(probs.astype(BF16), g_stack)
            dk_ref[here, :] += nn(grad, q_stack)
            for h in range(heads):
                span = slice(h * HD, (h + 1) * HD)
                dqt_ref[span, :] += nn(kt_ref[span, here], grad[:, h * QB : (h + 1) * QB])
            return carry

        lax.fori_loop(low, high, step, 0, unroll=False)
        gq_ref[part, :] = (dqt_ref[...].T * 0.125).astype(BF16)
    gk_ref[...] = dk_ref[...].astype(BF16)
    gv_ref[...] = dv_ref[...].astype(BF16)
    for copy in copies[13:]:
        copy.wait()
    outgoing = fetch(refs[:3], outputs[:3], out_semaphores)
    sums = [jnp.sum(ref[...].astype(F32), axis=0, keepdims=True) for ref in (gq_ref, gv_ref)]
    blank = jnp.zeros((1, 256 - width), F32)
    tail = jnp.concatenate([sums[0], blank, sums[1], blank, jnp.zeros((1, 256), F32)], axis=1)
    inner = row_of(inner_a) + row_of(inner_b)
    paired = own_sums[0:6, :] + other_sums[0:6, :]
    small = jnp.concatenate([paired, inner, tail], axis=0).astype(BF16)
    piece = pack_ref.shape[1] - 8
    per = width // piece
    for m, source in enumerate((None, gq_ref, gk_ref, gv_ref)):
        total = wo_acc_ref[...] if source is None else tn(source[...], x_ref[...])
        for t in range(per):
            cut = total[t * piece : (t + 1) * piece, :].astype(BF16)
            pack_ref[m * per + t, 0:piece, :] = cut
            pack_ref[m * per + t, piece:, :] = small if m + t == 0 else jnp.zeros_like(small)
        here = pl.ds(m * per, per)
        copy = pltpu.make_async_copy(
            pack_ref.at[here], outputs[3].at[here], out_semaphores.at[3 + m]
        )
        copy.start()
        outgoing.append(copy)
    for copy in outgoing:
        copy.wait()


def shaped(shape, dtype):
    return jax.ShapeDtypeStruct(shape, dtype)


PARAMS = pltpu.CompilerParams(vmem_limit_bytes=60 << 20)
SMALL = pltpu.CompilerParams(vmem_limit_bytes=60 << 20)
COST = pl.CostEstimate(flops=1024, bytes_accessed=1024, transcendentals=0)


def buffers(arrays):
    return [pltpu.VMEM(array.shape, array.dtype) for array in arrays]


def attend_shapes(count, heads, width):
    rows = count * QB
    return (
        shaped((rows, heads * HD), BF16),
        shaped((count, 8, heads * QB), F32),
        shaped((rows // 2, width), F32),
        shaped((rows // 2, width), BF16),
    )


def run_first(lengths, core, tokens, weights, blocks):
    rows, width = tokens.shape
    local_width = weights[0].shape[0]
    heads = local_width // HD
    outs = (
        (shaped(tokens.shape, BF16),)
        + (shaped((rows, local_width), BF16),) * 3
        + (shaped((local_width, rows), BF16),) * 2
        + attend_shapes(len(blocks), heads, width)
        + (shaped((2, lengths.shape[0], QB), F32), shaped((8, width), F32))
    )
    return pl.pallas_call(
        functools.partial(attend_first, heads, blocks),
        out_shape=outs,
        in_specs=[SMEM] * 2 + [HBM] * 13,
        out_specs=(HBM,) * 12,
        scratch_shapes=buffers(outs)
        + buffers(weights)
        + [pltpu.VMEM((local_width, QB), F32)]
        + [pltpu.SemaphoreType.DMA((12 + rows // QB,)), pltpu.SemaphoreType.DMA((12,))],
        compiler_params=PARAMS,
        name="attend_first",
        cost_estimate=COST,
    )(lengths, core, tokens, *weights)


def run_more(lengths, core, arrays, blocks):
    rows, local_width = arrays[0].shape
    heads = local_width // HD
    outs = attend_shapes(len(blocks), heads, arrays[3].shape[1])
    return pl.pallas_call(
        functools.partial(attend_more, heads, blocks),
        out_shape=outs,
        in_specs=[SMEM] * 2 + [HBM] * 4,
        out_specs=(HBM,) * 4,
        scratch_shapes=buffers(arrays)
        + buffers(outs)
        + [pltpu.VMEM((local_width, QB), F32)]
        + [pltpu.SemaphoreType.DMA((4,)), pltpu.SemaphoreType.DMA((4,))],
        compiler_params=PARAMS,
        name="attend_more",
        cost_estimate=COST,
    )(lengths, core, *arrays)


def run_back(lengths, core, arrays, marker):
    wo, q, x = arrays[8], arrays[9], arrays[-1]
    rows, width = q.shape
    heads = width // HD
    piece = 4 * width // 16
    outs = (shaped((rows, width), BF16),) * 3 + (shaped((16, piece + 8, x.shape[1]), BF16),)
    return pl.pallas_call(
        functools.partial(attend_back, heads, len(arrays)),
        out_shape=outs,
        in_specs=[SMEM] * 2 + [HBM] * (len(arrays) + 1),
        out_specs=(HBM,) * 4,
        scratch_shapes=buffers(outs)
        + [pltpu.VMEM((rows, width), F32)] * 2
        + [pltpu.VMEM((width, QB), F32), pltpu.VMEM(wo.shape, F32)]
        + [pltpu.SemaphoreType.DMA((len(arrays),)), pltpu.SemaphoreType.DMA((7,))]
        + buffers(arrays),
        compiler_params=PARAMS,
        name="attend_back",
        cost_estimate=COST,
    )(lengths, core, *arrays, marker)


def mark_kernel(source_ref, target_ref):
    del source_ref, target_ref


def mark(values):
    return pl.pallas_call(
        mark_kernel,
        out_shape=shaped(values.shape, values.dtype),
        in_specs=[HBM],
        out_specs=HBM,
        compiler_params=pltpu.CompilerParams(vmem_limit_bytes=1 << 20),
        name="mark",
        cost_estimate=pl.CostEstimate(flops=1 << 36, bytes_accessed=1 << 10, transcendentals=0),
    )(values)


def finish_kernel(source_ref, target_ref):
    del source_ref
    target_ref[...] = jnp.zeros(target_ref.shape, F32)


def finish(values):
    return pl.pallas_call(
        finish_kernel,
        out_shape=shaped(values.shape, values.dtype),
        in_specs=[HBM],
        out_specs=VMEM,
        compiler_params=pltpu.CompilerParams(vmem_limit_bytes=1 << 20),
        name="finish",
        cost_estimate=COST,
    )(values)


def row_of(ref):
    return ref[...].astype(F32).reshape(1, -1)


def in_three(values):
    high = values.astype(BF16)
    rest = values - high.astype(F32)
    middle = rest.astype(BF16)
    return high, middle, (rest - middle.astype(F32)).astype(BF16)


def norm_step(grad, normed, rscale, gain):
    scaled = grad * gain
    first_mean = jnp.mean(scaled, axis=1, keepdims=True)
    cross_mean = jnp.mean(scaled * normed, axis=1, keepdims=True)
    return rscale * (scaled - first_mean - normed * cross_mean)


def column_of(ref):
    row = ref[...].reshape(1, -1)
    return jnp.broadcast_to(row, (128, row.shape[1])).T[:, 0:1]


def column_sum(values):
    return jnp.sum(values, axis=0, keepdims=True)


def send_out(results, outputs, semaphores, which):
    copies = [
        pltpu.make_async_copy(results[k], outputs[k], semaphores.at[k]) for k in which
    ]
    for copy in copies:
        copy.start()
    return copies


def loss_back(lengths_ref, place_ref, *refs):
    sources, outputs, refs = refs[:9], refs[9:15], refs[15:]
    targets, results = refs[:9], refs[9:15]
    coef_ref, turned_ref, semaphores, out_semaphores = refs[15:]
    copies = fetch(sources, targets, semaphores)
    piece_ref, swapped_ref, pooled_ref, match_ref, gain_ref = targets[:5]
    core, index = place_ref[0], place_ref[1]
    bounds = segment_bounds(lengths_ref)
    for copy in copies[:5]:
        copy.wait()
    first = core == 0
    queries = jnp.where(first, piece_ref[...], swapped_ref[...])
    passages = jnp.where(first, swapped_ref[...], piece_ref[...])
    count = queries.shape[0]
    own = pooled_ref.shape[0] // 2
    similarity = nt(queries, passages) / SOFTMAX_WARMTH
    match = match_ref[...].reshape(1, -1)
    match = match == lax.broadcasted_iota(jnp.int32, (count, count), 0)
    top = jnp.max(similarity, axis=1, keepdims=True)
    lse = top + jnp.log(jnp.sum(jnp.exp(similarity - top), axis=1, keepdims=True))
    positive = jnp.sum(jnp.where(match, similarity, 0.0), axis=1, keepdims=True)
    loss = jnp.sum(lse - positive, axis=0, keepdims=True) / count
    results[5][...] = jnp.broadcast_to(loss, results[5].shape)
    coef = (jnp.exp(similarity - lse) - match.astype(F32)) * (1.0 / (count * SOFTMAX_WARMTH))
    coef_ref[...] = coef
    turned_ref[...] = coef.T
    here = pl.ds(pl.multiple_of(index * own, own), own)
    grad_query = sum(nn(part, passages) for part in in_three(coef_ref[here, :]))
    grad_passage = sum(nn(part, queries) for part in in_three(turned_ref[here, :]))
    grad_unit = jnp.concatenate([grad_query, grad_passage], axis=0)
    pooled = pooled_ref[...]
    rscale = lax.rsqrt(jnp.sum(pooled * pooled, axis=1, keepdims=True) + EPS_NORM)
    inner = jnp.sum(pooled * grad_unit, axis=1, keepdims=True)
    grad_pooled = rscale * grad_unit - rscale * rscale * rscale * inner * pooled
    seqs = 2 * own
    grad_pooled = jnp.concatenate(
        [grad_pooled, jnp.zeros((128 - seqs, grad_pooled.shape[1]), F32)], axis=0
    )
    parts = in_three(grad_pooled)
    lane = lax.broadcasted_iota(jnp.int32, (1, 128), 1)
    begin = end = jnp.zeros((1, 128), jnp.int32)
    for seq, (start, stop) in enumerate(bounds):
        begin = jnp.where(lane == seq, start, begin)
        end = jnp.where(lane == seq, stop, end)
    gain = row_of(gain_ref)
    sums = [0.0, 0.0, 0.0]
    outgoing = []
    for i in range(2):
        copies[5 + 2 * i].wait()
        copies[6 + 2 * i].wait()
        normed = targets[5 + 2 * i][...]
        place = core * (2 * QB) + i * QB + lax.broadcasted_iota(jnp.int32, (QB, 128), 0)
        member = jnp.where((place >= begin) & (place < end), 1.0, 0.0).astype(BF16)
        grad = sum(nn(member, part) for part in parts)
        second = norm_step(grad, normed, column_of(targets[6 + 2 * i]), gain)
        rounded = second.astype(BF16)
        results[i][...] = second
        results[2 + i][...] = rounded
        for k, values in enumerate((rounded.astype(F32), grad * normed, grad)):
            sums[k] = sums[k] + column_sum(values)
        outgoing += send_out(results, outputs, out_semaphores, (2 + i, i))
    blanks = [jnp.zeros((n, sums[0].shape[1]), F32) for n in (3, 2)]
    results[4][...] = jnp.concatenate([blanks[0], *sums, blanks[1]], axis=0)
    outgoing += send_out(results, outputs, out_semaphores, (4, 5))
    for copy in outgoing:
        copy.wait()


def norm_back(*refs):
    sources, outputs, refs = refs[:7], refs[7:10], refs[10:]
    targets, results = refs[:7], refs[7:10]
    semaphores, out_semaphores = refs[10:]
    for copy in fetch(sources, targets, semaphores):
        copy.wait()
    gain = row_of(targets[0])
    second, pair_here, far, normed, rscale = targets[2:]
    grad = second[...] + (pair_here[...].astype(F32) + far[...].astype(F32))
    normed = normed[...]
    first = norm_step(grad, normed, column_of(rscale), gain)
    rounded = first.astype(BF16)
    results[1][...] = rounded
    outgoing = send_out(results, outputs, out_semaphores, (1,))
    results[0][...] = first
    outgoing += send_out(results, outputs, out_semaphores, (0,))
    results[2][...] = targets[1][...]
    for k, values in enumerate((rounded.astype(F32), grad * normed, grad)):
        results[2][k : k + 1, :] += column_sum(values)
    outgoing += send_out(results, outputs, out_semaphores, (2,))
    for copy in outgoing:
        copy.wait()


STEPS = (0, 2, 1, 3)


def join(place_ref, *refs):
    sources, output, semaphores = refs[:4], refs[4], refs[5]
    copies = []
    for k in range(4):
        spot = (place_ref[0] + 4 - STEPS[k]) % 4
        copies.append(pltpu.make_async_copy(sources[k], output.at[spot], semaphores.at[k]))
        copies[-1].start()
    for copy in copies:
        copy.wait()


def spread(piece, place_ref, *refs):
    sources, outputs, refs = refs[:5], refs[5:20], refs[20:]
    by_z, by_y = refs[:2]
    results, semaphores, out_semaphores = refs[2:17], refs[17], refs[18]
    copies = [pltpu.make_async_copy(sources[0], by_z, semaphores.at[4])]
    for k in range(4):
        spot = (place_ref[1] + 4 - STEPS[k]) % 4
        copies.append(
            pltpu.make_async_copy(sources[1 + k], by_y.at[spot], semaphores.at[k])
        )
    for copy in copies:
        copy.start()
    part = piece // 2
    copies[0].wait()
    results[0][...] = by_z[:, :, :piece, :].astype(F32)
    outgoing = send_out(results, outputs, out_semaphores, (0,))
    for copy in copies[1:]:
        copy.wait()
    for y in range(4):
        results[1][:, y] = by_y[y, :, :piece, :].astype(F32)
    outgoing += send_out(results, outputs, out_semaphores, (1,))
    for m in range(4):
        results[2 + m][:, :part, :] = by_z[m, :, piece:, :].astype(F32)
        for y in range(4):
            results[2 + m][y, part:, :] = by_y[y, m, piece : piece + part, :].astype(F32)
        outgoing += send_out(results, outputs, out_semaphores, (2 + m,))
    small = by_y[0, 0, piece + part :, :].astype(F32)
    for k in range(7):
        results[6 + k][...] = small[k : k + 1, :].reshape(-1)
    count = results[13].shape[0]
    for k in range(2):
        results[13 + k][...] = small[7:8, 256 * k : 256 * k + count].reshape(-1)
    outgoing += send_out(results, outputs, out_semaphores, range(6, 15))
    for copy in outgoing:
        copy.wait()


def run_loss(lengths, place, arrays):
    rows, width = arrays[5].shape
    count = arrays[0].shape[0]
    outs = (
        (shaped((rows, width), F32),) * 2
        + (shaped((rows, width), BF16),) * 2
        + (shaped((8, width), F32), shaped((8, 128), F32))
    )
    return pl.pallas_call(
        loss_back,
        out_shape=outs,
        in_specs=[SMEM] * 2 + [HBM] * 9,
        out_specs=(HBM,) * 6,
        scratch_shapes=buffers(arrays)
        + buffers(outs)
        + [pltpu.VMEM((count, count), F32)] * 2
        + [pltpu.SemaphoreType.DMA((9,)), pltpu.SemaphoreType.DMA((6,))],
        compiler_params=SMALL,
        name="loss_back",
        cost_estimate=COST,
    )(lengths, place, *arrays)


def run_norm(arrays):
    rows, width = arrays[2].shape
    outs = (shaped((rows, width), F32), shaped((rows, width), BF16), shaped((8, width), F32))
    return pl.pallas_call(
        norm_back,
        out_shape=outs,
        in_specs=[HBM] * 7,
        out_specs=(HBM,) * 3,
        scratch_shapes=buffers(arrays)
        + buffers(outs)
        + [pltpu.SemaphoreType.DMA((7,)), pltpu.SemaphoreType.DMA((3,))],
        compiler_params=SMALL,
        name="norm_back",
        cost_estimate=COST,
    )(*arrays)


def run_join(places, pieces):
    return pl.pallas_call(
        join,
        out_shape=shaped((4,) + pieces[0].shape, BF16),
        in_specs=[SMEM] + [HBM] * 4,
        out_specs=HBM,
        scratch_shapes=[pltpu.SemaphoreType.DMA((4,))],
        compiler_params=pltpu.CompilerParams(vmem_limit_bytes=1 << 20),
        name="join",
        cost_estimate=COST,
    )(places, *pieces)


def settle(core_ref, *refs):
    sources, output, semaphores = refs[:4], refs[4], refs[5]
    copies = []
    for k in range(4):
        first = (k // 2 + core_ref[0]) % 2 * (2 * QB) + k % 2 * QB
        spot = pl.ds(pl.multiple_of(first, QB), QB)
        copies.append(pltpu.make_async_copy(sources[k], output.at[spot, :], semaphores.at[k]))
        copies[-1].start()
    for copy in copies:
        copy.wait()


def run_settle(core, parts):
    rows, width = parts[0].shape
    return pl.pallas_call(
        settle,
        out_shape=shaped((4 * rows, width), BF16),
        in_specs=[SMEM] + [HBM] * 4,
        out_specs=HBM,
        scratch_shapes=[pltpu.SemaphoreType.DMA((4,))],
        compiler_params=pltpu.CompilerParams(vmem_limit_bytes=1 << 20),
        name="settle",
        cost_estimate=COST,
    )(core, *parts)


def run_spread(places, gathered, pieces, piece):
    width = gathered.shape[3]
    shapes = [(4, 4, piece, width)] * 2 + [(4, piece, width)] * 4
    shapes += [(width,)] * 7 + [(4 * piece,)] * 2
    return pl.pallas_call(
        functools.partial(spread, piece),
        out_shape=[shaped(shape, F32) for shape in shapes],
        in_specs=[SMEM] + [HBM] * 5,
        out_specs=[HBM] * 15,
        scratch_shapes=[pltpu.VMEM(gathered.shape, BF16)]
        + [pltpu.VMEM((4,) + pieces[0].shape, BF16)]
        + [pltpu.VMEM(shape, F32) for shape in shapes]
        + [pltpu.SemaphoreType.DMA((5,)), pltpu.SemaphoreType.DMA((15,))],
        compiler_params=SMALL,
        name="spread",
        cost_estimate=COST,
    )(places, gathered, *pieces)


def trade(values):
    return lax.all_to_all(
        values, "dp", split_axis=0, concat_axis=0, axis_index_groups=PLANES, tiled=True
    )


def share(values, groups):
    spread_out = jnp.broadcast_to(values[None], (len(groups[0]),) + values.shape)
    return lax.all_to_all(
        spread_out, "dp", split_axis=0, concat_axis=0, axis_index_groups=groups, tiled=True
    )


def ring_shift(axis, step):
    pairs = []
    for i in range(32):
        z, y, x = i // 8, (i // 2) % 4, i % 2
        z, y = ((z + step) % 4, y) if axis == "z" else (z, (y + step) % 4)
        pairs.append((i, (z * 4 + y) * 2 + x))
    return pairs


def ring_pieces(values, axis):
    return [lax.ppermute(values, "dp", ring_shift(axis, step)) for step in STEPS[1:]]


def tie(values, others):
    return lax.optimization_barrier((values, others))


class Marker:
    def __init__(self):
        self.state = jnp.zeros((8, 128), F32)

    def fence(self, ready, later):
        ready, state = tie(ready, self.state)
        later, self.state = tie(later, mark(state))
        return ready, later

    def moved(self, values, axis, pairs):
        values, state = tie(values, self.state)
        arrived, self.state = tie(lax.ppermute(values, axis, pairs), mark(state))
        return arrived

    def core_swap(self, values):
        return self.moved(values, "mp", CORE_SWAP)

    def near_swap(self, values):
        return self.moved(values, "dp", NEAR_SWAP)

    def both(self, own):
        return jnp.concatenate([own, self.core_swap(own)], axis=0)

    def near_sum(self, total):
        return (total.astype(F32) + self.near_swap(total).astype(F32)).astype(BF16)


def plane_sum(parts):
    return jnp.sum(parts.astype(F32), axis=0).astype(BF16)


def far_swap(values):
    return lax.ppermute(values, "mp", FAR_SWAP)


def norm_forward(values, gain_vec, shift_vec):
    average = jnp.mean(values, axis=-1, keepdims=True)
    centred = values - average
    rscale = lax.rsqrt(jnp.mean(centred * centred, axis=-1, keepdims=True) + EPS_NORM)
    normed = centred * rscale
    return (normed * gain_vec + shift_vec, normed, rscale[:, 0])


def gelu_and_slope(upper):
    below = 0.5 * (1.0 + lax.erf(upper * math.sqrt(0.5)))
    density = jnp.exp(-0.5 * upper * upper) * (1.0 / math.sqrt(2.0 * math.pi))
    return (upper * below).astype(BF16), (below + upper * density).astype(BF16)


def local(
    tokens,
    lengths,
    pair_index,
    query_proj,
    query_bias,
    key_proj,
    value_proj,
    value_bias,
    output_proj,
    output_bias,
    attn_gain,
    attn_shift,
    inner_proj,
    inner_bias,
    outer_proj,
    outer_bias,
    final_gain,
    final_shift,
):
    row_count, width = tokens.shape
    chunk = row_count // 2
    half = chunk // 2
    seq_count = lengths.shape[0]
    pair_count = seq_count // 2
    overall_pair_count = pair_index.shape[0]
    local_width = query_proj.shape[1]
    core = lax.axis_index("mp") % 2
    my_index = lax.axis_index("dp")
    marker = Marker()
    core_arg = jnp.reshape(core, (1,)).astype(jnp.int32)
    vectors = (output_bias, attn_gain, attn_shift, outer_bias, final_gain, final_shift)
    query_t, key_t, value_t = query_proj.T, key_proj.T, value_proj.T

    weights = (query_t, key_t, value_t, query_bias, value_bias, output_proj, *vectors)
    first = run_first(lengths, core_arg, tokens, weights, (0, 1))
    rows, query_b, key_b, value_b, key_tb, value_tb, mixed_a, lse_a = first[:8]
    attn_own_a, attn_other_a, members, vectors = first[8:]

    def own_and_other(values, weights):
        return nn(values[:half], weights), nn(values[half:], weights).astype(BF16)

    def pair(own, arrived):
        return (own + arrived.astype(F32)).astype(BF16)

    def first_norm(index, pair_here, far):
        attn_full = pair_here.astype(F32) + far.astype(F32) + output_bias
        own_tokens = rows[index * chunk : index * chunk + half].astype(F32)
        return norm_forward(own_tokens + attn_full, attn_gain_f, attn_shift_f)

    def feed_forward(own_hidden):
        whole = marker.both(own_hidden)
        act, slope = gelu_and_slope(nn(whole, inner_proj) + inner_bias.astype(F32))
        return whole, act, slope

    def last_norm(hidden, pair_here, far):
        ffn_full = pair_here.astype(F32) + far.astype(F32) + outer_bias
        return norm_forward(hidden + ffn_full, final_gain_f, final_shift_f)

    attn_pair_a = pair(attn_own_a, marker.core_swap(attn_other_a))
    attn_far_a = far_swap(attn_pair_a)
    output_bias, attn_gain_f, attn_shift_f = vectors[0], vectors[1], vectors[2]
    outer_bias, final_gain_f, final_shift_f = vectors[3], vectors[4], vectors[5]
    late_query, late_pair = tie(query_b, attn_pair_a)
    mixed_b, lse_b, attn_own_b, attn_other_b = run_more(
        lengths, core_arg, (late_query, key_b, value_tb, output_proj), (2, 3)
    )
    attn_pair_b = pair(attn_own_b, marker.core_swap(attn_other_b))
    attn_far_b = far_swap(attn_pair_b)
    attn_far_a, attn_pair_b = tie(attn_far_a, attn_pair_b)
    hidden_a, normed_one_a, rscale_one_a = first_norm(0, late_pair, attn_far_a)
    own_hidden_a = hidden_a.astype(BF16)
    hidden_ab, act_a, slope_a = feed_forward(own_hidden_a)
    ffn_own_a, ffn_other_a = own_and_other(act_a, outer_proj)
    ffn_pair_a = pair(ffn_own_a, marker.core_swap(ffn_other_a))
    attn_far_b, ffn_pair_late = tie(attn_far_b, ffn_pair_a)
    ffn_far_a = far_swap(ffn_pair_a)
    hidden_b, normed_one_b, rscale_one_b = first_norm(1, attn_pair_b, attn_far_b)
    own_hidden_b = hidden_b.astype(BF16)
    hidden_bb, act_b, slope_b = feed_forward(own_hidden_b)
    ffn_own_b, ffn_other_b = own_and_other(act_b, outer_proj)
    ffn_pair_b = pair(ffn_own_b, marker.core_swap(ffn_other_b))
    ffn_pair_b, ffn_far_a = marker.fence(ffn_pair_b, ffn_far_a)
    final_a, normed_two_a, rscale_two_a = last_norm(hidden_a, ffn_pair_late, ffn_far_a)
    pooled_a = jnp.dot(members[0], final_a, precision=HIGHEST)
    final_b, normed_two_b, rscale_two_b = last_norm(hidden_b, ffn_pair_b, far_swap(ffn_pair_b))
    pooled_part = pooled_a + jnp.dot(members[1], final_b, precision=HIGHEST)
    lse = (lse_a, lse_b)
    hidden_whole, act, slope = (hidden_ab, hidden_bb), (act_a, act_b), (slope_a, slope_b)
    normed_one, rscale_one = (normed_one_a, normed_one_b), (rscale_one_a, rscale_one_b)
    normed_two, rscale_two = (normed_two_a, normed_two_b), (rscale_two_a, rscale_two_b)
    pooled = pooled_part + marker.core_swap(pooled_part)
    pool_rscale = lax.rsqrt(jnp.sum(pooled * pooled, axis=-1, keepdims=True) + EPS_NORM)
    unit_b = (pooled * pool_rscale).astype(BF16)

    piece = lax.dynamic_slice_in_dim(unit_b, core * pair_count, pair_count, 0)
    near = marker.near_swap(piece)
    low = (my_index % 2) == 0
    piece = jnp.concatenate([jnp.where(low, piece, near), jnp.where(low, near, piece)], axis=0)
    piece = share(piece, PLANES).reshape(overall_pair_count, width)
    place_arg = jnp.stack([core, my_index]).astype(jnp.int32)
    *grads, last_sums, loss = run_loss(
        lengths,
        place_arg,
        (
            piece,
            marker.core_swap(piece),
            pooled,
            pair_index,
            final_gain,
            normed_two[0],
            rscale_two[0],
            normed_two[1],
            rscale_two[1],
        ),
    )
    grad_second, own_grad = grads[:2], grads[2:]

    inner_sums, grad_ffn, grad_up, hidden_other = [], [], [], []
    for i in range(2):
        grad_ffn.append(marker.both(own_grad[i]))
        grad_up.append((nt(grad_ffn[i], outer_proj) * slope[i].astype(F32)).astype(BF16))
        inner_sums.append(jnp.sum(grad_up[i].astype(F32), axis=0))
        other = nt(grad_up[i][half:], inner_proj).astype(BF16)
        hidden_other.append(marker.core_swap(other))
    hidden_pair = [pair(nt(grad_up[i][:half], inner_proj), hidden_other[i]) for i in range(2)]
    hidden_far = [far_swap(hidden_pair[i]) for i in range(2)]
    (late_act, late_hidden), hidden_pair = tie((act, hidden_whole), hidden_pair)
    ffn_pack = jnp.concatenate(
        [
            (tn(late_act[0], grad_ffn[0]) + tn(late_act[1], grad_ffn[1]))
            .astype(BF16)
            .reshape(16, -1, width),
            (tn(late_hidden[0], grad_up[0]) + tn(late_hidden[1], grad_up[1]))
            .astype(BF16)
            .reshape(16, -1, width),
        ],
        axis=1,
    )
    ffn_pack, hidden_far = marker.fence(ffn_pack, hidden_far)
    ffn_parts = trade(ffn_pack)

    grad_first, own_grad, other_grad, sums = [], [], [], last_sums
    for i in range(2):
        first, rounded, sums = run_norm(
            (
                attn_gain,
                sums,
                grad_second[i],
                hidden_pair[i],
                hidden_far[i],
                normed_one[i],
                rscale_one[i],
            )
        )
        grad_first.append(first)
        own_grad.append(rounded)
        if i == 0:
            other_grad.append(marker.core_swap(rounded))
            hidden_far[1], marker.state = tie(hidden_far[1], marker.state)
    (rounded, sums), state = tie((rounded, sums), marker.state)
    arrived = [lax.ppermute(values, "mp", CORE_SWAP) for values in (rounded, sums)]
    (arrived, other_sums), marker.state = tie(arrived, mark(state))
    other_grad.append(arrived)
    own_grad[1] = rounded
    grad_query, grad_key, grad_value, packed = run_back(
        lengths,
        core_arg,
        (
            own_grad[0],
            other_grad[0],
            own_grad[1],
            other_grad[1],
            mixed_a,
            mixed_b,
            *lse,
            output_proj,
            query_b,
            key_b,
            value_b,
            key_tb,
            sums,
            other_sums,
            *inner_sums,
            rows,
        ),
        marker.state,
    )
    marker = Marker()

    def input_part(first):
        span = slice(first, first + half)
        return (
            nt(grad_query[span], query_proj)
            + nt(grad_key[span], key_proj)
            + nt(grad_value[span], value_proj)
        )

    token_pair = []
    for i in range(2):
        other = input_part(i * chunk + half).astype(BF16)
        token_pair.append(pair(input_part(i * chunk), marker.core_swap(other)))
    token_pair, (packed, ffn_parts) = marker.fence(token_pair, (packed, ffn_parts))
    token_far = [far_swap(token_pair[i]) for i in range(2)]
    packed_parts = trade(packed)
    ffn_total = plane_sum(ffn_parts)
    ffn_near = lax.ppermute(ffn_total, "dp", NEAR_SWAP)
    ffn_reduced = (ffn_total.astype(F32) + ffn_near.astype(F32)).astype(BF16)
    token_far, ffn_reduced = tie(token_far, ffn_reduced)
    token_own = [
        (grad_first[i] + (token_pair[i].astype(F32) + token_far[i].astype(F32))).astype(BF16)
        for i in range(2)
    ]
    token_other = [lax.ppermute(rows_here, "mp", CORE_SWAP) for rows_here in token_own]
    packed_parts, token_other = tie(packed_parts, token_other)
    packed_reduced = marker.near_sum(plane_sum(packed_parts))
    piece_rows = width // 16
    places = jnp.stack([my_index // 8, (my_index // 2) % 4]).astype(jnp.int32)
    halves = [
        jnp.concatenate([ffn_reduced[:piece_rows], packed_reduced[: piece_rows // 2]], axis=0),
        jnp.concatenate([ffn_reduced[piece_rows:], packed_reduced[piece_rows // 2 :]], axis=0),
    ]
    one_ring = share(halves[0], Y_RINGS)
    pieces = ring_pieces(halves[1], "z")
    halves, (one_ring, pieces) = marker.fence(halves, (one_ring, pieces))
    other_ring = run_join(places, (halves[1], *pieces))
    gathered = share(one_ring, Z_RINGS)
    pieces = ring_pieces(other_ring, "y")
    token_grad = run_settle(core_arg, (*token_own, *token_other))
    gathered, token_grad = tie(gathered, token_grad)
    closing = finish(marker.state)[0, 0]
    outer_grad, inner_grad, *rest = run_spread(
        places, gathered, (other_ring, *pieces), piece_rows
    )
    cuts = [values.reshape(local_width, width) for values in rest[:4]]
    vectors = rest[4:]
    return (
        loss[0, 0] + closing,
        token_grad,
        cuts[1].T,
        vectors[7],
        cuts[2].T,
        cuts[3].T,
        vectors[8],
        cuts[0],
        vectors[0],
        vectors[1],
        vectors[2],
        inner_grad.reshape(width, width),
        vectors[6],
        outer_grad.reshape(width, width),
        vectors[3],
        vectors[4],
        vectors[5],
    )


def solution(mesh):
    column, row, split = P(None, "mp"), P("mp", None), P("mp")
    placed = (
        (P("dp", None), P("dp"), P())
        + (column, split, column, column, split, row)
        + (P(), P(), P())
        + (column, split, row)
        + (P(), P(), P())
    )
    given = (
        (P(), P("dp", None))
        + (column, split, column, column, split, row)
        + (P(), P(), P())
        + (column, split, row)
        + (P(), P(), P())
    )
    return jax.shard_map(local, mesh=mesh, in_specs=placed, out_specs=given, check_vma=False)
```

```python
import functools
import math

import jax
import jax.numpy as jnp
from jax import lax
from jax.experimental import pallas as pl
from jax.experimental.pallas import tpu as pltpu
from jax.sharding import PartitionSpec as P

HD = 64
EPS_NORM = 1e-06
SOFTMAX_WARMTH = 0.01
NEG_FILL = -1e30
HIGHEST = lax.Precision.HIGHEST
F32 = jnp.float32
BF16 = jnp.bfloat16
QB = 256
KB = 256

CORE_SWAP = [(i, i ^ 1) for i in range(4)]
FAR_SWAP = [(i, i ^ 2) for i in range(4)]
NEAR_SWAP = [(i, i ^ 1) for i in range(32)]
PLANES = [[i * 2 + x for i in range(16)] for x in range(2)]

SMEM = pl.BlockSpec(memory_space=pltpu.SMEM)
VMEM = pl.BlockSpec(memory_space=pltpu.VMEM)
HBM = pl.BlockSpec(memory_space=pltpu.HBM)


def nn(left, right):
    return lax.dot_general(left, right, (((1,), (0,)), ((), ())), preferred_element_type=F32)


def nt(left, right):
    return lax.dot_general(left, right, (((1,), (1,)), ((), ())), preferred_element_type=F32)


def tn(left, right):
    return lax.dot_general(left, right, (((0,), (0,)), ((), ())), preferred_element_type=F32)


def place_of_block(block, core, rows):
    return ((block % 2) * 2 + block // 2) * QB + core * (rows // 2) & (rows - 1)


def spot_of_keys(j, core, rows):
    place = (j * KB + core * (rows // 2)) & (rows - 1)
    block = place // QB
    return pl.multiple_of(((block % 2) * 2 + block // 2) * QB + place % QB, KB)


def segment_bounds(lengths_ref):
    bounds, total = [], jnp.int32(0)
    for s in range(lengths_ref.shape[0]):
        start = total
        total = total + lengths_ref[s]
        bounds.append((start, total))
    return bounds


def block_span(bounds, first, rows):
    place = first + lax.broadcasted_iota(jnp.int32, (1, QB), 1)
    low, high = first, first + KB
    begin = jnp.full((1, QB), bounds[-1][1], jnp.int32)
    end = jnp.full((1, QB), rows, jnp.int32)
    for start, stop in bounds:
        inside = (place >= start) & (place < stop)
        begin = jnp.where(inside, start, begin)
        end = jnp.where(inside, stop, end)
        touches = (stop > first) & (start < first + QB) & (stop > start)
        low = jnp.where(touches, jnp.minimum(low, start), low)
        high = jnp.where(touches, jnp.maximum(high, stop), high)
    return low // KB, (high + KB - 1) // KB, begin, end


def head_copies(values, heads):
    lane = lax.broadcasted_iota(jnp.int32, values.shape, 1) // HD
    blank = jnp.zeros_like(values)
    return jnp.concatenate([jnp.where(lane == h, values, blank) for h in range(heads)], axis=0)


def span_mask(begin, end, block, heads):
    place = block * KB + lax.broadcasted_iota(jnp.int32, (KB, QB), 0)
    keep = (place >= begin) & (place < end)
    return jnp.concatenate([keep] * heads, axis=1)


def attend(heads, blocks, core, bounds, q_ref, k_ref, vt_ref, mixed_ref, lse_ref, acc_ref):
    rows = k_ref.shape[0]
    for i, block in enumerate(blocks):
        low, high, begin, end = block_span(bounds, place_of_block(block, core, rows), rows)
        stack = head_copies(q_ref[block * QB : (block + 1) * QB, :], heads)
        acc_ref[...] = jnp.zeros(acc_ref.shape, F32)

        def step(j, carry, stack=stack, begin=begin, end=end):
            top, total = carry
            spot = spot_of_keys(j, core, rows)
            scores = nt(k_ref[pl.ds(spot, KB), :], stack)
            scores = jnp.where(span_mask(begin, end, j, heads), scores, NEG_FILL)
            peak = jnp.maximum(top, jnp.max(scores, axis=0, keepdims=True))
            fade = jnp.exp(top - peak)
            probs = jnp.exp(scores - peak)
            total = total * fade + jnp.sum(probs, axis=0, keepdims=True)
            probs = probs.astype(BF16)
            for h in range(heads):
                part = slice(h * QB, (h + 1) * QB)
                span = slice(h * HD, (h + 1) * HD)
                acc_ref[span, :] = acc_ref[span, :] * fade[:, part] + nn(
                    vt_ref[span, pl.ds(spot, KB)], probs[:, part]
                )
            return peak, total

        top = jnp.full((1, heads * QB), NEG_FILL, F32)
        top, total = lax.fori_loop(
            low, high, step, (top, jnp.zeros((1, heads * QB), F32)), unroll=False
        )
        scale = 1.0 / total
        mixed = jnp.concatenate(
            [
                acc_ref[h * HD : (h + 1) * HD, :] * scale[:, h * QB : (h + 1) * QB]
                for h in range(heads)
            ],
            axis=0,
        )
        mixed_ref[i * QB : (i + 1) * QB, :] = mixed.T.astype(BF16)
        lse_ref[i, :, :] = jnp.broadcast_to(top + jnp.log(total), (8, heads * QB))


def fetch(sources, targets, semaphores, order=()):
    copies = [
        pltpu.make_async_copy(source, target, semaphores.at[i])
        for i, (source, target) in enumerate(zip(sources, targets))
    ]
    for i in [*order, *(i for i in range(len(copies)) if i not in order)]:
        copies[i].start()
    return copies


def project(mixed_ref, weights_ref, results, outputs, semaphores):
    results[1][...] = nn(mixed_ref[QB:, :], weights_ref[...]).astype(BF16)
    copies = send_out(results, outputs, semaphores, (1,))
    results[0][...] = nn(mixed_ref[:QB, :], weights_ref[...])
    return copies + send_out(results, outputs, semaphores, (0,))


def attend_first(heads, blocks, lengths_ref, core_ref, *refs):
    sources, outputs, refs = refs[:13], refs[13:25], refs[25:]
    results, targets, refs = refs[:12], refs[12:24], refs[24:]
    acc_ref, semaphores, out_semaphores = refs
    x_ref, q_ref, k_ref, v_ref, kt_ref, vt_ref, mixed_ref, lse_ref = results[:8]
    wqt_ref, wkt_ref, wvt_ref, bq_ref, bv_ref, wo_ref = targets[:6]
    rows = x_ref.shape[0]
    core = core_ref[0]
    copies = fetch(sources[1:], targets, semaphores)
    row_copies = []
    for block in range(rows // QB):
        first = pl.multiple_of(place_of_block(block, core, rows), QB)
        row_copies.append(
            pltpu.make_async_copy(
                sources[0].at[pl.ds(first, QB), :],
                x_ref.at[pl.ds(block * QB, QB), :],
                semaphores.at[12 + block],
            )
        )
        row_copies[-1].start()
    for copy in copies:
        copy.wait()
    query_bias, value_bias = row_of(bq_ref), row_of(bv_ref)
    for block in range(rows // QB):
        row_copies[block].wait()
        part = slice(block * QB, (block + 1) * QB)
        x = x_ref[part, :]
        q = (nt(x, wqt_ref[...]) + query_bias).astype(BF16)
        q_ref[part, :] = q * BF16(0.125)
        k_ref[part, :] = nt(x, wkt_ref[...]).astype(BF16)
        kt_ref[:, part] = nt(wkt_ref[...], x).astype(BF16)
        v = nt(x, wvt_ref[...]) + value_bias
        v_ref[part, :] = v.astype(BF16)
        vt_ref[:, part] = v.T.astype(BF16)
    outgoing = send_out(results, outputs, out_semaphores, range(6))
    bounds = segment_bounds(lengths_ref)
    place = core * (2 * QB) + lax.broadcasted_iota(jnp.int32, (1, QB), 1)
    for i in range(2):
        member = [
            jnp.where((place + i * QB >= start) & (place + i * QB < stop), 1.0, 0.0)
            for start, stop in bounds
        ]
        results[10][i] = jnp.concatenate(member, axis=0)
    lines = [row_of(ref) for ref in targets[6:]]
    results[11][...] = jnp.concatenate(lines + [jnp.zeros((2, lines[0].shape[1]), F32)], axis=0)
    outgoing += send_out(results, outputs, out_semaphores, (10, 11))
    attend(heads, blocks, core, bounds, q_ref, k_ref, vt_ref, mixed_ref, lse_ref, acc_ref)
    outgoing += project(mixed_ref, wo_ref, results[8:], outputs[8:], out_semaphores.at[8:10])
    outgoing += send_out(results, outputs, out_semaphores, (6, 7))
    for copy in outgoing:
        copy.wait()


def attend_more(heads, blocks, lengths_ref, core_ref, *refs):
    sources, outputs, refs = refs[:4], refs[4:8], refs[8:]
    targets, results, refs = refs[:4], refs[4:8], refs[8:]
    acc_ref, semaphores, out_semaphores = refs
    q_ref, k_ref, vt_ref, wo_ref = targets
    mixed_ref, lse_ref = results[:2]
    for copy in fetch(sources, targets, semaphores):
        copy.wait()
    bounds = segment_bounds(lengths_ref)
    attend(heads, blocks, core_ref[0], bounds, q_ref, k_ref, vt_ref, mixed_ref, lse_ref, acc_ref)
    outgoing = project(mixed_ref, wo_ref, results[2:], outputs[2:], out_semaphores.at[2:])
    outgoing += send_out(results, outputs, out_semaphores, (0, 1))
    for copy in outgoing:
        copy.wait()


def attend_back(heads, inputs, lengths_ref, core_ref, *refs):
    sources, refs = refs[:inputs], refs[inputs + 1 :]
    outputs, refs = refs[:4], refs[4:]
    gq_ref, gk_ref, gv_ref, pack_ref = refs[:4]
    dk_ref, dv_ref, dqt_ref, wo_acc_ref, semaphores, out_semaphores = refs[4:10]
    targets = refs[10:]
    copies = fetch(sources, targets, semaphores, (10, 9, 11, 12, 0, 4, 8, 6, 1, 2, 3, 5, 7))
    grads = targets[0:4]
    mixed = targets[4:6]
    lses = targets[6:8]
    wo_ref, q_ref, k_ref, v_ref, kt_ref = targets[8:13]
    own_sums, other_sums, inner_a, inner_b, x_ref = targets[13:]
    rows, width = q_ref.shape
    core = core_ref[0]
    bounds = segment_bounds(lengths_ref)
    dk_ref[...] = jnp.zeros(dk_ref.shape, F32)
    dv_ref[...] = jnp.zeros(dv_ref.shape, F32)
    lane = lax.broadcasted_iota(jnp.int32, (8, width), 1) // HD
    which = (lane == lax.broadcasted_iota(jnp.int32, (8, width), 0)).astype(F32).astype(BF16)
    for i in (0, 4, 6, 8, 9, 10, 11, 12):
        copies[i].wait()
    for block in range(rows // QB):
        if block > 0:
            copies[block].wait()
        if block == 2:
            copies[5].wait()
            copies[7].wait()
        low, high, begin, end = block_span(bounds, place_of_block(block, core, rows), rows)
        part = slice(block * QB, (block + 1) * QB)
        own = slice(block % 2 * QB, block % 2 * QB + QB)
        grad_attn = grads[block][...]
        mixed_here = mixed[block // 2][own, :]
        outer = tn(mixed_here, grad_attn)
        wo_acc_ref[...] = outer if block == 0 else wo_acc_ref[...] + outer
        grad_mixed = nt(grad_attn, wo_ref[...]).astype(BF16)
        product = grad_mixed.astype(F32) * mixed_here.astype(F32)
        sums = sum(nt(which, part) for part in in_three(product)[:2])
        delta = jnp.concatenate([sums[h : h + 1, :] for h in range(heads)], axis=1)
        lse = lses[block // 2][block % 2, 0:1, :]
        q_stack = head_copies(q_ref[part, :], heads)
        g_stack = head_copies(grad_mixed, heads)
        dqt_ref[...] = jnp.zeros(dqt_ref.shape, F32)

        def step(
            j, carry, delta=delta, lse=lse, q_stack=q_stack, g_stack=g_stack, begin=begin, end=end
        ):
            here = pl.ds(spot_of_keys(j, core, rows), KB)
            scores = nt(k_ref[here, :], q_stack)
            scores = jnp.where(span_mask(begin, end, j, heads), scores, NEG_FILL)
            probs = jnp.exp(scores - lse)
            grad = (probs * (nt(v_ref[here, :], g_stack) - delta)).astype(BF16)
            dv_ref[here, :] += nn(probs.astype(BF16), g_stack)
            dk_ref[here, :] += nn(grad, q_stack)
            for h in range(heads):
                span = slice(h * HD, (h + 1) * HD)
                dqt_ref[span, :] += nn(kt_ref[span, here], grad[:, h * QB : (h + 1) * QB])
            return carry

        lax.fori_loop(low, high, step, 0, unroll=False)
        gq_ref[part, :] = (dqt_ref[...].T * 0.125).astype(BF16)
    gk_ref[...] = dk_ref[...].astype(BF16)
    gv_ref[...] = dv_ref[...].astype(BF16)
    for copy in copies[13:]:
        copy.wait()
    outgoing = fetch(refs[:3], outputs[:3], out_semaphores)
    sums = [jnp.sum(ref[...].astype(F32), axis=0, keepdims=True) for ref in (gq_ref, gv_ref)]
    blank = jnp.zeros((1, 256 - width), F32)
    tail = jnp.concatenate([sums[0], blank, sums[1], blank, jnp.zeros((1, 256), F32)], axis=1)
    inner = row_of(inner_a) + row_of(inner_b)
    paired = own_sums[0:6, :] + other_sums[0:6, :]
    small = jnp.concatenate([paired, inner, tail], axis=0).astype(BF16)
    piece = pack_ref.shape[1] - 8
    per = width // piece
    for m, source in enumerate((None, gq_ref, gk_ref, gv_ref)):
        total = wo_acc_ref[...] if source is None else tn(source[...], x_ref[...])
        for t in range(per):
            cut = total[t * piece : (t + 1) * piece, :].astype(BF16)
            pack_ref[m * per + t, 0:piece, :] = cut
            pack_ref[m * per + t, piece:, :] = small if m + t == 0 else jnp.zeros_like(small)
        here = pl.ds(m * per, per)
        copy = pltpu.make_async_copy(
            pack_ref.at[here], outputs[3].at[here], out_semaphores.at[3 + m]
        )
        copy.start()
        outgoing.append(copy)
    for copy in outgoing:
        copy.wait()


def shaped(shape, dtype):
    return jax.ShapeDtypeStruct(shape, dtype)


PARAMS = pltpu.CompilerParams(vmem_limit_bytes=60 << 20)
SMALL = pltpu.CompilerParams(vmem_limit_bytes=60 << 20)
COST = pl.CostEstimate(flops=1024, bytes_accessed=1024, transcendentals=0)


def buffers(arrays):
    return [pltpu.VMEM(array.shape, array.dtype) for array in arrays]


def attend_shapes(count, heads, width):
    rows = count * QB
    return (
        shaped((rows, heads * HD), BF16),
        shaped((count, 8, heads * QB), F32),
        shaped((rows // 2, width), F32),
        shaped((rows // 2, width), BF16),
    )


def run_first(lengths, core, tokens, weights, blocks):
    rows, width = tokens.shape
    local_width = weights[0].shape[0]
    heads = local_width // HD
    outs = (
        (shaped(tokens.shape, BF16),)
        + (shaped((rows, local_width), BF16),) * 3
        + (shaped((local_width, rows), BF16),) * 2
        + attend_shapes(len(blocks), heads, width)
        + (shaped((2, lengths.shape[0], QB), F32), shaped((8, width), F32))
    )
    return pl.pallas_call(
        functools.partial(attend_first, heads, blocks),
        out_shape=outs,
        in_specs=[SMEM] * 2 + [HBM] * 13,
        out_specs=(HBM,) * 12,
        scratch_shapes=buffers(outs)
        + buffers(weights)
        + [pltpu.VMEM((local_width, QB), F32)]
        + [pltpu.SemaphoreType.DMA((12 + rows // QB,)), pltpu.SemaphoreType.DMA((12,))],
        compiler_params=PARAMS,
        name="attend_first",
        cost_estimate=COST,
    )(lengths, core, tokens, *weights)


def run_more(lengths, core, arrays, blocks):
    rows, local_width = arrays[0].shape
    heads = local_width // HD
    outs = attend_shapes(len(blocks), heads, arrays[3].shape[1])
    return pl.pallas_call(
        functools.partial(attend_more, heads, blocks),
        out_shape=outs,
        in_specs=[SMEM] * 2 + [HBM] * 4,
        out_specs=(HBM,) * 4,
        scratch_shapes=buffers(arrays)
        + buffers(outs)
        + [pltpu.VMEM((local_width, QB), F32)]
        + [pltpu.SemaphoreType.DMA((4,)), pltpu.SemaphoreType.DMA((4,))],
        compiler_params=PARAMS,
        name="attend_more",
        cost_estimate=COST,
    )(lengths, core, *arrays)


def run_back(lengths, core, arrays, marker):
    wo, q, x = arrays[8], arrays[9], arrays[-1]
    rows, width = q.shape
    heads = width // HD
    piece = 4 * width // 16
    outs = (shaped((rows, width), BF16),) * 3 + (shaped((16, piece + 8, x.shape[1]), BF16),)
    return pl.pallas_call(
        functools.partial(attend_back, heads, len(arrays)),
        out_shape=outs,
        in_specs=[SMEM] * 2 + [HBM] * (len(arrays) + 1),
        out_specs=(HBM,) * 4,
        scratch_shapes=buffers(outs)
        + [pltpu.VMEM((rows, width), F32)] * 2
        + [pltpu.VMEM((width, QB), F32), pltpu.VMEM(wo.shape, F32)]
        + [pltpu.SemaphoreType.DMA((len(arrays),)), pltpu.SemaphoreType.DMA((7,))]
        + buffers(arrays),
        compiler_params=PARAMS,
        name="attend_back",
        cost_estimate=COST,
    )(lengths, core, *arrays, marker)


def mark_kernel(source_ref, target_ref):
    del source_ref, target_ref


def mark(values):
    return pl.pallas_call(
        mark_kernel,
        out_shape=shaped(values.shape, values.dtype),
        in_specs=[HBM],
        out_specs=HBM,
        compiler_params=pltpu.CompilerParams(vmem_limit_bytes=1 << 20),
        name="mark",
        cost_estimate=pl.CostEstimate(flops=1 << 36, bytes_accessed=1 << 10, transcendentals=0),
    )(values)


def finish_kernel(source_ref, target_ref):
    del source_ref
    target_ref[...] = jnp.zeros(target_ref.shape, F32)


def finish(values):
    return pl.pallas_call(
        finish_kernel,
        out_shape=shaped(values.shape, values.dtype),
        in_specs=[HBM],
        out_specs=VMEM,
        compiler_params=pltpu.CompilerParams(vmem_limit_bytes=1 << 20),
        name="finish",
        cost_estimate=COST,
    )(values)


def row_of(ref):
    return ref[...].astype(F32).reshape(1, -1)


def in_three(values):
    high = values.astype(BF16)
    rest = values - high.astype(F32)
    middle = rest.astype(BF16)
    return high, middle, (rest - middle.astype(F32)).astype(BF16)


def norm_step(grad, normed, rscale, gain):
    scaled = grad * gain
    first_mean = jnp.mean(scaled, axis=1, keepdims=True)
    cross_mean = jnp.mean(scaled * normed, axis=1, keepdims=True)
    return rscale * (scaled - first_mean - normed * cross_mean)


def column_of(ref):
    row = ref[...].reshape(1, -1)
    return jnp.broadcast_to(row, (128, row.shape[1])).T[:, 0:1]


def column_sum(values):
    return jnp.sum(values, axis=0, keepdims=True)


def send_out(results, outputs, semaphores, which):
    copies = [
        pltpu.make_async_copy(results[k], outputs[k], semaphores.at[k]) for k in which
    ]
    for copy in copies:
        copy.start()
    return copies


def loss_back(lengths_ref, place_ref, *refs):
    sources, outputs, refs = refs[:9], refs[9:15], refs[15:]
    targets, results = refs[:9], refs[9:15]
    coef_ref, turned_ref, semaphores, out_semaphores = refs[15:]
    copies = fetch(sources, targets, semaphores)
    piece_ref, swapped_ref, pooled_ref, match_ref, gain_ref = targets[:5]
    core, index = place_ref[0], place_ref[1]
    bounds = segment_bounds(lengths_ref)
    for copy in copies[:5]:
        copy.wait()
    first = core == 0
    queries = jnp.where(first, piece_ref[...], swapped_ref[...])
    passages = jnp.where(first, swapped_ref[...], piece_ref[...])
    count = queries.shape[0]
    own = pooled_ref.shape[0] // 2
    similarity = nt(queries, passages) / SOFTMAX_WARMTH
    match = match_ref[...].reshape(1, -1)
    match = match == lax.broadcasted_iota(jnp.int32, (count, count), 0)
    top = jnp.max(similarity, axis=1, keepdims=True)
    lse = top + jnp.log(jnp.sum(jnp.exp(similarity - top), axis=1, keepdims=True))
    positive = jnp.sum(jnp.where(match, similarity, 0.0), axis=1, keepdims=True)
    loss = jnp.sum(lse - positive, axis=0, keepdims=True) / count
    results[5][...] = jnp.broadcast_to(loss, results[5].shape)
    coef = (jnp.exp(similarity - lse) - match.astype(F32)) * (1.0 / (count * SOFTMAX_WARMTH))
    coef_ref[...] = coef
    turned_ref[...] = coef.T
    here = pl.ds(pl.multiple_of(index * own, own), own)
    grad_query = sum(nn(part, passages) for part in in_three(coef_ref[here, :]))
    grad_passage = sum(nn(part, queries) for part in in_three(turned_ref[here, :]))
    grad_unit = jnp.concatenate([grad_query, grad_passage], axis=0)
    pooled = pooled_ref[...]
    rscale = lax.rsqrt(jnp.sum(pooled * pooled, axis=1, keepdims=True) + EPS_NORM)
    inner = jnp.sum(pooled * grad_unit, axis=1, keepdims=True)
    grad_pooled = rscale * grad_unit - rscale * rscale * rscale * inner * pooled
    seqs = 2 * own
    grad_pooled = jnp.concatenate(
        [grad_pooled, jnp.zeros((128 - seqs, grad_pooled.shape[1]), F32)], axis=0
    )
    parts = in_three(grad_pooled)
    lane = lax.broadcasted_iota(jnp.int32, (1, 128), 1)
    begin = end = jnp.zeros((1, 128), jnp.int32)
    for seq, (start, stop) in enumerate(bounds):
        begin = jnp.where(lane == seq, start, begin)
        end = jnp.where(lane == seq, stop, end)
    gain = row_of(gain_ref)
    sums = [0.0, 0.0, 0.0]
    outgoing = []
    for i in range(2):
        copies[5 + 2 * i].wait()
        copies[6 + 2 * i].wait()
        normed = targets[5 + 2 * i][...]
        place = core * (2 * QB) + i * QB + lax.broadcasted_iota(jnp.int32, (QB, 128), 0)
        member = jnp.where((place >= begin) & (place < end), 1.0, 0.0).astype(BF16)
        grad = sum(nn(member, part) for part in parts)
        second = norm_step(grad, normed, column_of(targets[6 + 2 * i]), gain)
        rounded = second.astype(BF16)
        results[i][...] = second
        results[2 + i][...] = rounded
        for k, values in enumerate((rounded.astype(F32), grad * normed, grad)):
            sums[k] = sums[k] + column_sum(values)
        outgoing += send_out(results, outputs, out_semaphores, (2 + i, i))
    results[4][...] = jnp.concatenate(sums + [jnp.zeros((5, sums[0].shape[1]), F32)], axis=0)
    outgoing += send_out(results, outputs, out_semaphores, (4, 5))
    for copy in outgoing:
        copy.wait()


def norm_back(*refs):
    sources, outputs, refs = refs[:12], refs[12:17], refs[17:]
    targets, results = refs[:12], refs[12:17]
    semaphores, out_semaphores = refs[17:]
    copies = fetch(sources, targets, semaphores)
    copies[0].wait()
    copies[1].wait()
    gain = row_of(targets[0])
    sums = [0.0, 0.0, 0.0]
    outgoing = []
    for i in range(2):
        for copy in copies[2 + 5 * i : 7 + 5 * i]:
            copy.wait()
        second, pair_here, far, normed, rscale = targets[2 + 5 * i : 7 + 5 * i]
        grad = second[...] + (pair_here[...].astype(F32) + far[...].astype(F32))
        normed = normed[...]
        first = norm_step(grad, normed, column_of(rscale), gain)
        rounded = first.astype(BF16)
        results[i][...] = first
        results[2 + i][...] = rounded
        for k, values in enumerate((rounded.astype(F32), grad * normed, grad)):
            sums[k] = sums[k] + column_sum(values)
        outgoing += send_out(results, outputs, out_semaphores, (2 + i, i))
    blank = jnp.zeros((2, sums[0].shape[1]), F32)
    results[4][...] = jnp.concatenate(sums + [targets[1][0:3, :], blank], axis=0)
    outgoing += send_out(results, outputs, out_semaphores, (4,))
    for copy in outgoing:
        copy.wait()


STEPS = (0, 2, 1, 3)


def join(place_ref, *refs):
    sources, output, semaphores = refs[:4], refs[4], refs[5]
    copies = []
    for k in range(4):
        spot = (place_ref[0] + 4 - STEPS[k]) % 4
        copies.append(pltpu.make_async_copy(sources[k], output.at[spot], semaphores.at[k]))
        copies[-1].start()
    for copy in copies:
        copy.wait()


def spread_outer(place_ref, *refs):
    sources, output, refs = refs[:4], refs[4], refs[5:]
    targets, results, semaphores, out_semaphores = refs[:4], refs[4:8], refs[8], refs[9]
    outgoing = []
    for k, copy in enumerate(fetch(sources, targets, semaphores)):
        copy.wait()
        results[k][...] = targets[k][...].astype(F32)
        spot = (place_ref[0] + 4 - STEPS[k]) % 4
        outgoing.append(
            pltpu.make_async_copy(results[k], output.at[spot], out_semaphores.at[k])
        )
        outgoing[-1].start()
    for copy in outgoing:
        copy.wait()


def spread(piece, place_ref, *refs):
    sources, outputs, refs = refs[:4], refs[4:18], refs[18:]
    by_y, results, semaphores, out_semaphores = refs[0], refs[1:15], refs[15], refs[16]
    copies = []
    for k in range(4):
        spot = (place_ref[0] + 4 - STEPS[k]) % 4
        copies.append(pltpu.make_async_copy(sources[k], by_y.at[spot], semaphores.at[k]))
        copies[-1].start()
    for copy in copies:
        copy.wait()
    for y in range(4):
        results[0][:, y] = by_y[y, :, :piece, :].astype(F32)
    outgoing = send_out(results, outputs, out_semaphores, (0,))
    for m in range(4):
        results[1 + m][...] = by_y[:, m, piece : 2 * piece, :].astype(F32)
        outgoing += send_out(results, outputs, out_semaphores, (1 + m,))
    small = by_y[0, 0, 2 * piece :, :].astype(F32)
    for k in range(7):
        results[5 + k][...] = small[k : k + 1, :].reshape(-1)
    count = results[12].shape[0]
    for k in range(2):
        results[12 + k][...] = small[7:8, 256 * k : 256 * k + count].reshape(-1)
    outgoing += send_out(results, outputs, out_semaphores, range(5, 14))
    for copy in outgoing:
        copy.wait()


def run_loss(lengths, place, arrays):
    rows, width = arrays[5].shape
    count = arrays[0].shape[0]
    outs = (
        (shaped((rows, width), F32),) * 2
        + (shaped((rows, width), BF16),) * 2
        + (shaped((8, width), F32), shaped((8, 128), F32))
    )
    return pl.pallas_call(
        loss_back,
        out_shape=outs,
        in_specs=[SMEM] * 2 + [HBM] * 9,
        out_specs=(HBM,) * 6,
        scratch_shapes=buffers(arrays)
        + buffers(outs)
        + [pltpu.VMEM((count, count), F32)] * 2
        + [pltpu.SemaphoreType.DMA((9,)), pltpu.SemaphoreType.DMA((6,))],
        compiler_params=SMALL,
        name="loss_back",
        cost_estimate=COST,
    )(lengths, place, *arrays)


def run_norm(arrays):
    rows, width = arrays[2].shape
    outs = (
        (shaped((rows, width), F32),) * 2
        + (shaped((rows, width), BF16),) * 2
        + (shaped((8, width), F32),)
    )
    return pl.pallas_call(
        norm_back,
        out_shape=outs,
        in_specs=[HBM] * 12,
        out_specs=(HBM,) * 5,
        scratch_shapes=buffers(arrays)
        + buffers(outs)
        + [pltpu.SemaphoreType.DMA((12,)), pltpu.SemaphoreType.DMA((5,))],
        compiler_params=SMALL,
        name="norm_back",
        cost_estimate=COST,
    )(*arrays)


def run_join(places, pieces):
    return pl.pallas_call(
        join,
        out_shape=shaped((4,) + pieces[0].shape, BF16),
        in_specs=[SMEM] + [HBM] * 4,
        out_specs=HBM,
        scratch_shapes=[pltpu.SemaphoreType.DMA((4,))],
        compiler_params=pltpu.CompilerParams(vmem_limit_bytes=1 << 20),
        name="join",
        cost_estimate=COST,
    )(places, *pieces)


def settle(core_ref, *refs):
    sources, output, semaphores = refs[:4], refs[4], refs[5]
    copies = []
    for k in range(4):
        first = (k // 2 + core_ref[0]) % 2 * (2 * QB) + k % 2 * QB
        spot = pl.ds(pl.multiple_of(first, QB), QB)
        copies.append(pltpu.make_async_copy(sources[k], output.at[spot, :], semaphores.at[k]))
        copies[-1].start()
    for copy in copies:
        copy.wait()


def run_settle(core, parts):
    rows, width = parts[0].shape
    return pl.pallas_call(
        settle,
        out_shape=shaped((4 * rows, width), BF16),
        in_specs=[SMEM] + [HBM] * 4,
        out_specs=HBM,
        scratch_shapes=[pltpu.SemaphoreType.DMA((4,))],
        compiler_params=pltpu.CompilerParams(vmem_limit_bytes=1 << 20),
        name="settle",
        cost_estimate=COST,
    )(core, *parts)


def run_spread_outer(place, pieces):
    shape = pieces[0].shape
    return pl.pallas_call(
        spread_outer,
        out_shape=shaped((4,) + shape, F32),
        in_specs=[SMEM] + [HBM] * 4,
        out_specs=HBM,
        scratch_shapes=buffers(pieces)
        + [pltpu.VMEM(shape, F32)] * 4
        + [pltpu.SemaphoreType.DMA((4,)), pltpu.SemaphoreType.DMA((4,))],
        compiler_params=SMALL,
        name="spread_outer",
        cost_estimate=COST,
    )(place, *pieces)


def run_spread(place, pieces, piece):
    width = pieces[0].shape[2]
    shapes = [(4, 4, piece, width)] + [(4, piece, width)] * 4
    shapes += [(width,)] * 7 + [(4 * piece,)] * 2
    return pl.pallas_call(
        functools.partial(spread, piece),
        out_shape=[shaped(shape, F32) for shape in shapes],
        in_specs=[SMEM] + [HBM] * 4,
        out_specs=[HBM] * 14,
        scratch_shapes=[pltpu.VMEM((4,) + pieces[0].shape, BF16)]
        + [pltpu.VMEM(shape, F32) for shape in shapes]
        + [pltpu.SemaphoreType.DMA((4,)), pltpu.SemaphoreType.DMA((14,))],
        compiler_params=SMALL,
        name="spread",
        cost_estimate=COST,
    )(place, *pieces)


def trade(values):
    return lax.all_to_all(
        values, "dp", split_axis=0, concat_axis=0, axis_index_groups=PLANES, tiled=True
    )


def share(values, groups):
    spread_out = jnp.broadcast_to(values[None], (len(groups[0]),) + values.shape)
    return lax.all_to_all(
        spread_out, "dp", split_axis=0, concat_axis=0, axis_index_groups=groups, tiled=True
    )


def ring_shift(axis, step):
    pairs = []
    for i in range(32):
        z, y, x = i // 8, (i // 2) % 4, i % 2
        z, y = ((z + step) % 4, y) if axis == "z" else (z, (y + step) % 4)
        pairs.append((i, (z * 4 + y) * 2 + x))
    return pairs


def ring_pieces(values, axis):
    return [lax.ppermute(values, "dp", ring_shift(axis, step)) for step in STEPS[1:]]


def tie(values, others):
    return lax.optimization_barrier((values, others))


class Marker:
    def __init__(self):
        self.state = jnp.zeros((8, 128), F32)

    def fence(self, ready, later):
        ready, state = tie(ready, self.state)
        later, self.state = tie(later, mark(state))
        return ready, later

    def moved(self, values, axis, pairs):
        values, state = tie(values, self.state)
        arrived, self.state = tie(lax.ppermute(values, axis, pairs), mark(state))
        return arrived

    def core_swap(self, values):
        return self.moved(values, "mp", CORE_SWAP)

    def near_swap(self, values):
        return self.moved(values, "dp", NEAR_SWAP)

    def both(self, own):
        return jnp.concatenate([own, self.core_swap(own)], axis=0)

    def near_sum(self, total):
        return (total.astype(F32) + self.near_swap(total).astype(F32)).astype(BF16)


def plane_sum(parts):
    return jnp.sum(parts.astype(F32), axis=0).astype(BF16)


def far_swap(values):
    return lax.ppermute(values, "mp", FAR_SWAP)


def norm_forward(values, gain_vec, shift_vec):
    average = jnp.mean(values, axis=-1, keepdims=True)
    centred = values - average
    rscale = lax.rsqrt(jnp.mean(centred * centred, axis=-1, keepdims=True) + EPS_NORM)
    normed = centred * rscale
    return (normed * gain_vec + shift_vec, normed, rscale[:, 0])


def gelu_and_slope(upper):
    below = 0.5 * (1.0 + lax.erf(upper * math.sqrt(0.5)))
    density = jnp.exp(-0.5 * upper * upper) * (1.0 / math.sqrt(2.0 * math.pi))
    return (upper * below).astype(BF16), (below + upper * density).astype(BF16)


def local(
    tokens,
    lengths,
    pair_index,
    query_proj,
    query_bias,
    key_proj,
    value_proj,
    value_bias,
    output_proj,
    output_bias,
    attn_gain,
    attn_shift,
    inner_proj,
    inner_bias,
    outer_proj,
    outer_bias,
    final_gain,
    final_shift,
):
    row_count, width = tokens.shape
    chunk = row_count // 2
    half = chunk // 2
    seq_count = lengths.shape[0]
    pair_count = seq_count // 2
    overall_pair_count = pair_index.shape[0]
    local_width = query_proj.shape[1]
    core = lax.axis_index("mp") % 2
    my_index = lax.axis_index("dp")
    marker = Marker()
    core_arg = jnp.reshape(core, (1,)).astype(jnp.int32)
    vectors = (output_bias, attn_gain, attn_shift, outer_bias, final_gain, final_shift)
    query_t, key_t, value_t = query_proj.T, key_proj.T, value_proj.T

    weights = (query_t, key_t, value_t, query_bias, value_bias, output_proj, *vectors)
    first = run_first(lengths, core_arg, tokens, weights, (0, 1))
    rows, query_b, key_b, value_b, key_tb, value_tb, mixed_a, lse_a = first[:8]
    attn_own_a, attn_other_a, members, vectors = first[8:]

    def own_and_other(values, weights):
        return nn(values[:half], weights), nn(values[half:], weights).astype(BF16)

    def pair(own, arrived):
        return (own + arrived.astype(F32)).astype(BF16)

    def first_norm(index, pair_here, far):
        attn_full = pair_here.astype(F32) + far.astype(F32) + output_bias
        own_tokens = rows[index * chunk : index * chunk + half].astype(F32)
        return norm_forward(own_tokens + attn_full, attn_gain_f, attn_shift_f)

    def feed_forward(own_hidden):
        whole = marker.both(own_hidden)
        act, slope = gelu_and_slope(nn(whole, inner_proj) + inner_bias.astype(F32))
        return whole, act, slope

    def last_norm(hidden, pair_here, far):
        ffn_full = pair_here.astype(F32) + far.astype(F32) + outer_bias
        return norm_forward(hidden + ffn_full, final_gain_f, final_shift_f)

    attn_pair_a = pair(attn_own_a, marker.core_swap(attn_other_a))
    attn_far_a = far_swap(attn_pair_a)
    output_bias, attn_gain_f, attn_shift_f = vectors[0], vectors[1], vectors[2]
    outer_bias, final_gain_f, final_shift_f = vectors[3], vectors[4], vectors[5]
    late_query, late_pair = tie(query_b, attn_pair_a)
    mixed_b, lse_b, attn_own_b, attn_other_b = run_more(
        lengths, core_arg, (late_query, key_b, value_tb, output_proj), (2, 3)
    )
    attn_pair_b = pair(attn_own_b, marker.core_swap(attn_other_b))
    attn_far_b = far_swap(attn_pair_b)
    attn_far_a, attn_pair_b = tie(attn_far_a, attn_pair_b)
    hidden_a, normed_one_a, rscale_one_a = first_norm(0, late_pair, attn_far_a)
    own_hidden_a = hidden_a.astype(BF16)
    hidden_ab, act_a, slope_a = feed_forward(own_hidden_a)
    ffn_own_a, ffn_other_a = own_and_other(act_a, outer_proj)
    ffn_pair_a = pair(ffn_own_a, marker.core_swap(ffn_other_a))
    attn_far_b, ffn_pair_late = tie(attn_far_b, ffn_pair_a)
    ffn_far_a = far_swap(ffn_pair_a)
    hidden_b, normed_one_b, rscale_one_b = first_norm(1, attn_pair_b, attn_far_b)
    own_hidden_b = hidden_b.astype(BF16)
    hidden_bb, act_b, slope_b = feed_forward(own_hidden_b)
    ffn_own_b, ffn_other_b = own_and_other(act_b, outer_proj)
    ffn_pair_b = pair(ffn_own_b, marker.core_swap(ffn_other_b))
    ffn_pair_b, ffn_far_a = marker.fence(ffn_pair_b, ffn_far_a)
    final_a, normed_two_a, rscale_two_a = last_norm(hidden_a, ffn_pair_late, ffn_far_a)
    pooled_a = jnp.dot(members[0], final_a, precision=HIGHEST)
    final_b, normed_two_b, rscale_two_b = last_norm(hidden_b, ffn_pair_b, far_swap(ffn_pair_b))
    pooled_part = pooled_a + jnp.dot(members[1], final_b, precision=HIGHEST)
    lse = (lse_a, lse_b)
    hidden_whole, act, slope = (hidden_ab, hidden_bb), (act_a, act_b), (slope_a, slope_b)
    normed_one, rscale_one = (normed_one_a, normed_one_b), (rscale_one_a, rscale_one_b)
    normed_two, rscale_two = (normed_two_a, normed_two_b), (rscale_two_a, rscale_two_b)
    pooled = pooled_part + marker.core_swap(pooled_part)
    pool_rscale = lax.rsqrt(jnp.sum(pooled * pooled, axis=-1, keepdims=True) + EPS_NORM)
    unit_b = (pooled * pool_rscale).astype(BF16)

    piece = lax.dynamic_slice_in_dim(unit_b, core * pair_count, pair_count, 0)
    near = marker.near_swap(piece)
    low = (my_index % 2) == 0
    piece = jnp.concatenate([jnp.where(low, piece, near), jnp.where(low, near, piece)], axis=0)
    piece = share(piece, PLANES).reshape(overall_pair_count, width)
    place_arg = jnp.stack([core, my_index]).astype(jnp.int32)
    *grads, last_sums, loss = run_loss(
        lengths,
        place_arg,
        (
            piece,
            marker.core_swap(piece),
            pooled,
            pair_index,
            final_gain,
            normed_two[0],
            rscale_two[0],
            normed_two[1],
            rscale_two[1],
        ),
    )
    grad_second, own_grad = grads[:2], grads[2:]

    inner_sums, grad_ffn, grad_up, hidden_other = [], [], [], []
    for i in range(2):
        grad_ffn.append(marker.both(own_grad[i]))
        grad_up.append((nt(grad_ffn[i], outer_proj) * slope[i].astype(F32)).astype(BF16))
        inner_sums.append(jnp.sum(grad_up[i].astype(F32), axis=0))
        other = nt(grad_up[i][half:], inner_proj).astype(BF16)
        hidden_other.append(marker.core_swap(other))
    hidden_pair = [pair(nt(grad_up[i][:half], inner_proj), hidden_other[i]) for i in range(2)]
    hidden_far = [far_swap(hidden_pair[i]) for i in range(2)]
    (late_act, late_hidden), hidden_pair = tie((act, hidden_whole), hidden_pair)
    ffn_pack = jnp.concatenate(
        [
            (tn(late_act[0], grad_ffn[0]) + tn(late_act[1], grad_ffn[1]))
            .astype(BF16)
            .reshape(16, -1, width),
            (tn(late_hidden[0], grad_up[0]) + tn(late_hidden[1], grad_up[1]))
            .astype(BF16)
            .reshape(16, -1, width),
        ],
        axis=1,
    )
    ffn_pack, hidden_far = marker.fence(ffn_pack, hidden_far)
    ffn_parts = trade(ffn_pack)

    *grads, sums = run_norm(
        (
            attn_gain,
            last_sums,
            grad_second[0],
            hidden_pair[0],
            hidden_far[0],
            normed_one[0],
            rscale_one[0],
            grad_second[1],
            hidden_pair[1],
            hidden_far[1],
            normed_one[1],
            rscale_one[1],
        )
    )
    grad_first, own_grad = grads[:2], grads[2:]
    (*own_grad, sums), state = tie((*own_grad, sums), marker.state)
    arrived = [lax.ppermute(values, "mp", CORE_SWAP) for values in (*own_grad, sums)]
    (*other_grad, other_sums), marker.state = tie(arrived, mark(state))
    grad_query, grad_key, grad_value, packed = run_back(
        lengths,
        core_arg,
        (
            own_grad[0],
            other_grad[0],
            own_grad[1],
            other_grad[1],
            mixed_a,
            mixed_b,
            *lse,
            output_proj,
            query_b,
            key_b,
            value_b,
            key_tb,
            sums,
            other_sums,
            *inner_sums,
            rows,
        ),
        marker.state,
    )
    marker = Marker()

    def input_part(first):
        span = slice(first, first + half)
        return (
            nt(grad_query[span], query_proj)
            + nt(grad_key[span], key_proj)
            + nt(grad_value[span], value_proj)
        )

    token_pair = []
    for i in range(2):
        other = input_part(i * chunk + half).astype(BF16)
        token_pair.append(pair(input_part(i * chunk), marker.core_swap(other)))
    token_pair, (packed, ffn_parts) = marker.fence(token_pair, (packed, ffn_parts))
    packed, ffn_parts = marker.fence(packed, ffn_parts)
    packed_parts = trade(packed)
    ffn_reduced = marker.near_sum(plane_sum(ffn_parts))

    piece_rows = width // 16
    places = jnp.stack([my_index // 8, (my_index // 2) % 4]).astype(jnp.int32)
    outer_part, inner_part = ffn_reduced[:piece_rows], ffn_reduced[piece_rows:]
    pieces = ring_pieces(outer_part, "y")
    outer_part, pieces = marker.fence(outer_part, pieces)
    outer_ring = run_join(places[1:], (outer_part, *pieces))
    outer_pieces = ring_pieces(outer_ring, "z")
    outer_ring, packed_parts = marker.fence(outer_ring, packed_parts)
    packed_reduced = marker.near_sum(plane_sum(packed_parts))
    outer_pieces, packed_reduced = tie(outer_pieces, packed_reduced)
    rest_part = jnp.concatenate([inner_part, packed_reduced], axis=0)
    pieces = ring_pieces(rest_part, "z")
    rest_part, pieces = marker.fence(rest_part, pieces)
    rest_ring = run_join(places[:1], (rest_part, *pieces))
    rest_pieces = ring_pieces(rest_ring, "y")
    rest_ring, (outer_pieces, token_pair) = marker.fence(rest_ring, (outer_pieces, token_pair))
    token_far = [far_swap(token_pair[i]) for i in range(2)]
    outer_grad = run_spread_outer(places[:1], (outer_ring, *outer_pieces))
    token_own = [
        (grad_first[i] + (token_pair[i].astype(F32) + token_far[i].astype(F32))).astype(BF16)
        for i in range(2)
    ]
    token_other = [marker.core_swap(rows_here) for rows_here in token_own]
    token_grad = run_settle(core_arg, (*token_own, *token_other))
    rest_pieces, token_grad = tie(rest_pieces, token_grad)
    closing = finish(marker.state)[0, 0]
    inner_grad, *rest = run_spread(places[1:], (rest_ring, *rest_pieces), piece_rows)
    cuts = [values.reshape(local_width, width) for values in rest[:4]]
    vectors = rest[4:]
    return (
        loss[0, 0] + closing,
        token_grad,
        cuts[1].T,
        vectors[7],
        cuts[2].T,
        cuts[3].T,
        vectors[8],
        cuts[0],
        vectors[0],
        vectors[1],
        vectors[2],
        inner_grad.reshape(width, width),
        vectors[6],
        outer_grad.reshape(width, width),
        vectors[3],
        vectors[4],
        vectors[5],
    )


def solution(mesh):
    column, row, split = P(None, "mp"), P("mp", None), P("mp")
    placed = (
        (P("dp", None), P("dp"), P())
        + (column, split, column, column, split, row)
        + (P(), P(), P())
        + (column, split, row)
        + (P(), P(), P())
    )
    given = (
        (P(), P("dp", None))
        + (column, split, column, column, split, row)
        + (P(), P(), P())
        + (column, split, row)
        + (P(), P(), P())
    )
    return jax.shard_map(local, mesh=mesh, in_specs=placed, out_specs=given, check_vma=False)
```

```python
import functools
import math

import jax
import jax.numpy as jnp
from jax import lax
from jax.experimental import pallas as pl
from jax.experimental.pallas import tpu as pltpu
from jax.sharding import PartitionSpec as P

HD = 64
EPS_NORM = 1e-06
SOFTMAX_WARMTH = 0.01
NEG_FILL = -1e30
HIGHEST = lax.Precision.HIGHEST
F32 = jnp.float32
BF16 = jnp.bfloat16
QB = 256
KB = 256

CORE_SWAP = [(i, i ^ 1) for i in range(4)]
FAR_SWAP = [(i, i ^ 2) for i in range(4)]
NEAR_SWAP = [(i, i ^ 1) for i in range(32)]
PLANES = [[i * 2 + x for i in range(16)] for x in range(2)]
Z_RINGS = [[i + 8 * z for z in range(4)] for i in range(8)]
Y_RINGS = [[z * 8 + x + 2 * y for y in range(4)] for z in range(4) for x in range(2)]

SMEM = pl.BlockSpec(memory_space=pltpu.SMEM)
VMEM = pl.BlockSpec(memory_space=pltpu.VMEM)
HBM = pl.BlockSpec(memory_space=pltpu.HBM)


def nn(left, right):
    return lax.dot_general(left, right, (((1,), (0,)), ((), ())), preferred_element_type=F32)


def nt(left, right):
    return lax.dot_general(left, right, (((1,), (1,)), ((), ())), preferred_element_type=F32)


def tn(left, right):
    return lax.dot_general(left, right, (((0,), (0,)), ((), ())), preferred_element_type=F32)


def place_of_block(block, core, rows):
    return ((block % 2) * 2 + block // 2) * QB + core * (rows // 2) & (rows - 1)


def spot_of_keys(j, core, rows):
    place = (j * KB + core * (rows // 2)) & (rows - 1)
    block = place // QB
    return pl.multiple_of(((block % 2) * 2 + block // 2) * QB + place % QB, KB)


def segment_bounds(lengths_ref):
    bounds, total = [], jnp.int32(0)
    for s in range(lengths_ref.shape[0]):
        start = total
        total = total + lengths_ref[s]
        bounds.append((start, total))
    return bounds


def block_span(bounds, first, rows):
    place = first + lax.broadcasted_iota(jnp.int32, (1, QB), 1)
    low, high = first, first + KB
    begin = jnp.full((1, QB), bounds[-1][1], jnp.int32)
    end = jnp.full((1, QB), rows, jnp.int32)
    for start, stop in bounds:
        inside = (place >= start) & (place < stop)
        begin = jnp.where(inside, start, begin)
        end = jnp.where(inside, stop, end)
        touches = (stop > first) & (start < first + QB) & (stop > start)
        low = jnp.where(touches, jnp.minimum(low, start), low)
        high = jnp.where(touches, jnp.maximum(high, stop), high)
    return low // KB, (high + KB - 1) // KB, begin, end


def head_copies(values, heads):
    lane = lax.broadcasted_iota(jnp.int32, values.shape, 1) // HD
    blank = jnp.zeros_like(values)
    return jnp.concatenate([jnp.where(lane == h, values, blank) for h in range(heads)], axis=0)


def span_mask(begin, end, block, heads):
    place = block * KB + lax.broadcasted_iota(jnp.int32, (KB, QB), 0)
    keep = (place >= begin) & (place < end)
    return jnp.concatenate([keep] * heads, axis=1)


def attend(heads, blocks, core, bounds, q_ref, k_ref, vt_ref, mixed_ref, lse_ref, acc_ref):
    rows = k_ref.shape[0]
    for i, block in enumerate(blocks):
        low, high, begin, end = block_span(bounds, place_of_block(block, core, rows), rows)
        stack = head_copies(q_ref[block * QB : (block + 1) * QB, :], heads)
        acc_ref[...] = jnp.zeros(acc_ref.shape, F32)

        def step(j, carry, stack=stack, begin=begin, end=end):
            top, total = carry
            spot = spot_of_keys(j, core, rows)
            scores = nt(k_ref[pl.ds(spot, KB), :], stack)
            scores = jnp.where(span_mask(begin, end, j, heads), scores, NEG_FILL)
            peak = jnp.maximum(top, jnp.max(scores, axis=0, keepdims=True))
            fade = jnp.exp(top - peak)
            probs = jnp.exp(scores - peak)
            total = total * fade + jnp.sum(probs, axis=0, keepdims=True)
            probs = probs.astype(BF16)
            for h in range(heads):
                part = slice(h * QB, (h + 1) * QB)
                span = slice(h * HD, (h + 1) * HD)
                acc_ref[span, :] = acc_ref[span, :] * fade[:, part] + nn(
                    vt_ref[span, pl.ds(spot, KB)], probs[:, part]
                )
            return peak, total

        top = jnp.full((1, heads * QB), NEG_FILL, F32)
        top, total = lax.fori_loop(
            low, high, step, (top, jnp.zeros((1, heads * QB), F32)), unroll=False
        )
        scale = 1.0 / total
        mixed = jnp.concatenate(
            [
                acc_ref[h * HD : (h + 1) * HD, :] * scale[:, h * QB : (h + 1) * QB]
                for h in range(heads)
            ],
            axis=0,
        )
        mixed_ref[i * QB : (i + 1) * QB, :] = mixed.T.astype(BF16)
        lse_ref[i, :, :] = jnp.broadcast_to(top + jnp.log(total), (8, heads * QB))


def fetch(sources, targets, semaphores, order=()):
    copies = [
        pltpu.make_async_copy(source, target, semaphores.at[i])
        for i, (source, target) in enumerate(zip(sources, targets))
    ]
    for i in [*order, *(i for i in range(len(copies)) if i not in order)]:
        copies[i].start()
    return copies


def project(mixed_ref, weights_ref, results, outputs, semaphores):
    results[1][...] = nn(mixed_ref[QB:, :], weights_ref[...]).astype(BF16)
    copies = send_out(results, outputs, semaphores, (1,))
    results[0][...] = nn(mixed_ref[:QB, :], weights_ref[...])
    return copies + send_out(results, outputs, semaphores, (0,))


def attend_first(heads, blocks, lengths_ref, core_ref, *refs):
    sources, outputs, refs = refs[:13], refs[13:25], refs[25:]
    results, targets, refs = refs[:12], refs[12:24], refs[24:]
    acc_ref, semaphores, out_semaphores = refs
    x_ref, q_ref, k_ref, v_ref, kt_ref, vt_ref, mixed_ref, lse_ref = results[:8]
    wqt_ref, wkt_ref, wvt_ref, bq_ref, bv_ref, wo_ref = targets[:6]
    rows = x_ref.shape[0]
    core = core_ref[0]
    copies = fetch(sources[1:], targets, semaphores)
    row_copies = []
    for block in range(rows // QB):
        first = pl.multiple_of(place_of_block(block, core, rows), QB)
        row_copies.append(
            pltpu.make_async_copy(
                sources[0].at[pl.ds(first, QB), :],
                x_ref.at[pl.ds(block * QB, QB), :],
                semaphores.at[12 + block],
            )
        )
        row_copies[-1].start()
    for copy in copies:
        copy.wait()
    query_bias, value_bias = row_of(bq_ref), row_of(bv_ref)
    for block in range(rows // QB):
        row_copies[block].wait()
        part = slice(block * QB, (block + 1) * QB)
        x = x_ref[part, :]
        q = (nt(x, wqt_ref[...]) + query_bias).astype(BF16)
        q_ref[part, :] = q * BF16(0.125)
        k_ref[part, :] = nt(x, wkt_ref[...]).astype(BF16)
        kt_ref[:, part] = nt(wkt_ref[...], x).astype(BF16)
        v = nt(x, wvt_ref[...]) + value_bias
        v_ref[part, :] = v.astype(BF16)
        vt_ref[:, part] = v.T.astype(BF16)
    outgoing = send_out(results, outputs, out_semaphores, range(6))
    bounds = segment_bounds(lengths_ref)
    place = core * (2 * QB) + lax.broadcasted_iota(jnp.int32, (1, QB), 1)
    for i in range(2):
        member = [
            jnp.where((place + i * QB >= start) & (place + i * QB < stop), 1.0, 0.0)
            for start, stop in bounds
        ]
        results[10][i] = jnp.concatenate(member, axis=0)
    lines = [row_of(ref) for ref in targets[6:]]
    results[11][...] = jnp.concatenate(lines + [jnp.zeros((2, lines[0].shape[1]), F32)], axis=0)
    outgoing += send_out(results, outputs, out_semaphores, (10, 11))
    attend(heads, blocks, core, bounds, q_ref, k_ref, vt_ref, mixed_ref, lse_ref, acc_ref)
    outgoing += project(mixed_ref, wo_ref, results[8:], outputs[8:], out_semaphores.at[8:10])
    outgoing += send_out(results, outputs, out_semaphores, (6, 7))
    for copy in outgoing:
        copy.wait()


def attend_more(heads, blocks, lengths_ref, core_ref, *refs):
    sources, outputs, refs = refs[:4], refs[4:8], refs[8:]
    targets, results, refs = refs[:4], refs[4:8], refs[8:]
    acc_ref, semaphores, out_semaphores = refs
    q_ref, k_ref, vt_ref, wo_ref = targets
    mixed_ref, lse_ref = results[:2]
    for copy in fetch(sources, targets, semaphores):
        copy.wait()
    bounds = segment_bounds(lengths_ref)
    attend(heads, blocks, core_ref[0], bounds, q_ref, k_ref, vt_ref, mixed_ref, lse_ref, acc_ref)
    outgoing = project(mixed_ref, wo_ref, results[2:], outputs[2:], out_semaphores.at[2:])
    outgoing += send_out(results, outputs, out_semaphores, (0, 1))
    for copy in outgoing:
        copy.wait()


def attend_back(heads, inputs, lengths_ref, core_ref, *refs):
    sources, refs = refs[:inputs], refs[inputs + 1 :]
    outputs, refs = refs[:4], refs[4:]
    gq_ref, gk_ref, gv_ref, pack_ref = refs[:4]
    dk_ref, dv_ref, dqt_ref, wo_acc_ref, semaphores, out_semaphores = refs[4:10]
    targets = refs[10:]
    copies = fetch(sources, targets, semaphores, (10, 9, 11, 12, 0, 4, 8, 6, 1, 2, 3, 5, 7))
    grads = targets[0:4]
    mixed = targets[4:6]
    lses = targets[6:8]
    wo_ref, q_ref, k_ref, v_ref, kt_ref = targets[8:13]
    own_sums, other_sums, inner_a, inner_b, x_ref = targets[13:]
    rows, width = q_ref.shape
    core = core_ref[0]
    bounds = segment_bounds(lengths_ref)
    dk_ref[...] = jnp.zeros(dk_ref.shape, F32)
    dv_ref[...] = jnp.zeros(dv_ref.shape, F32)
    lane = lax.broadcasted_iota(jnp.int32, (8, width), 1) // HD
    which = (lane == lax.broadcasted_iota(jnp.int32, (8, width), 0)).astype(F32).astype(BF16)
    for i in (0, 4, 6, 8, 9, 10, 11, 12):
        copies[i].wait()
    for block in range(rows // QB):
        if block > 0:
            copies[block].wait()
        if block == 2:
            copies[5].wait()
            copies[7].wait()
        low, high, begin, end = block_span(bounds, place_of_block(block, core, rows), rows)
        part = slice(block * QB, (block + 1) * QB)
        own = slice(block % 2 * QB, block % 2 * QB + QB)
        grad_attn = grads[block][...]
        mixed_here = mixed[block // 2][own, :]
        outer = tn(mixed_here, grad_attn)
        wo_acc_ref[...] = outer if block == 0 else wo_acc_ref[...] + outer
        grad_mixed = nt(grad_attn, wo_ref[...]).astype(BF16)
        product = grad_mixed.astype(F32) * mixed_here.astype(F32)
        sums = sum(nt(which, part) for part in in_three(product)[:2])
        delta = jnp.concatenate([sums[h : h + 1, :] for h in range(heads)], axis=1)
        lse = lses[block // 2][block % 2, 0:1, :]
        q_stack = head_copies(q_ref[part, :], heads)
        g_stack = head_copies(grad_mixed, heads)
        dqt_ref[...] = jnp.zeros(dqt_ref.shape, F32)

        def step(
            j, carry, delta=delta, lse=lse, q_stack=q_stack, g_stack=g_stack, begin=begin, end=end
        ):
            here = pl.ds(spot_of_keys(j, core, rows), KB)
            scores = nt(k_ref[here, :], q_stack)
            scores = jnp.where(span_mask(begin, end, j, heads), scores, NEG_FILL)
            probs = jnp.exp(scores - lse)
            grad = (probs * (nt(v_ref[here, :], g_stack) - delta)).astype(BF16)
            dv_ref[here, :] += nn(probs.astype(BF16), g_stack)
            dk_ref[here, :] += nn(grad, q_stack)
            for h in range(heads):
                span = slice(h * HD, (h + 1) * HD)
                dqt_ref[span, :] += nn(kt_ref[span, here], grad[:, h * QB : (h + 1) * QB])
            return carry

        lax.fori_loop(low, high, step, 0, unroll=False)
        gq_ref[part, :] = (dqt_ref[...].T * 0.125).astype(BF16)
    gk_ref[...] = dk_ref[...].astype(BF16)
    gv_ref[...] = dv_ref[...].astype(BF16)
    for copy in copies[13:]:
        copy.wait()
    outgoing = fetch(refs[:3], outputs[:3], out_semaphores)
    sums = [jnp.sum(ref[...].astype(F32), axis=0, keepdims=True) for ref in (gq_ref, gv_ref)]
    blank = jnp.zeros((1, 256 - width), F32)
    tail = jnp.concatenate([sums[0], blank, sums[1], blank, jnp.zeros((1, 256), F32)], axis=1)
    inner = row_of(inner_a) + row_of(inner_b)
    paired = own_sums[0:6, :] + other_sums[0:6, :]
    small = [paired, inner, tail, jnp.zeros((8, tail.shape[1]), F32)]
    small = jnp.concatenate(small, axis=0).astype(BF16)
    piece = pack_ref.shape[1] - 16
    per = width // piece
    for m, source in enumerate((None, gq_ref, gk_ref, gv_ref)):
        total = wo_acc_ref[...] if source is None else tn(source[...], x_ref[...])
        for t in range(per):
            cut = total[t * piece : (t + 1) * piece, :].astype(BF16)
            pack_ref[m * per + t, 0:piece, :] = cut
            pack_ref[m * per + t, piece:, :] = small if m + t == 0 else jnp.zeros_like(small)
        here = pl.ds(m * per, per)
        copy = pltpu.make_async_copy(
            pack_ref.at[here], outputs[3].at[here], out_semaphores.at[3 + m]
        )
        copy.start()
        outgoing.append(copy)
    for copy in outgoing:
        copy.wait()


def shaped(shape, dtype):
    return jax.ShapeDtypeStruct(shape, dtype)


PARAMS = pltpu.CompilerParams(vmem_limit_bytes=60 << 20)
SMALL = pltpu.CompilerParams(vmem_limit_bytes=60 << 20)
COST = pl.CostEstimate(flops=1024, bytes_accessed=1024, transcendentals=0)


def buffers(arrays):
    return [pltpu.VMEM(array.shape, array.dtype) for array in arrays]


def attend_shapes(count, heads, width):
    rows = count * QB
    return (
        shaped((rows, heads * HD), BF16),
        shaped((count, 8, heads * QB), F32),
        shaped((rows // 2, width), F32),
        shaped((rows // 2, width), BF16),
    )


def run_first(lengths, core, tokens, weights, blocks):
    rows, width = tokens.shape
    local_width = weights[0].shape[0]
    heads = local_width // HD
    outs = (
        (shaped(tokens.shape, BF16),)
        + (shaped((rows, local_width), BF16),) * 3
        + (shaped((local_width, rows), BF16),) * 2
        + attend_shapes(len(blocks), heads, width)
        + (shaped((2, lengths.shape[0], QB), F32), shaped((8, width), F32))
    )
    return pl.pallas_call(
        functools.partial(attend_first, heads, blocks),
        out_shape=outs,
        in_specs=[SMEM] * 2 + [HBM] * 13,
        out_specs=(HBM,) * 12,
        scratch_shapes=buffers(outs)
        + buffers(weights)
        + [pltpu.VMEM((local_width, QB), F32)]
        + [pltpu.SemaphoreType.DMA((12 + rows // QB,)), pltpu.SemaphoreType.DMA((12,))],
        compiler_params=PARAMS,
        name="attend_first",
        cost_estimate=COST,
    )(lengths, core, tokens, *weights)


def run_more(lengths, core, arrays, blocks):
    rows, local_width = arrays[0].shape
    heads = local_width // HD
    outs = attend_shapes(len(blocks), heads, arrays[3].shape[1])
    return pl.pallas_call(
        functools.partial(attend_more, heads, blocks),
        out_shape=outs,
        in_specs=[SMEM] * 2 + [HBM] * 4,
        out_specs=(HBM,) * 4,
        scratch_shapes=buffers(arrays)
        + buffers(outs)
        + [pltpu.VMEM((local_width, QB), F32)]
        + [pltpu.SemaphoreType.DMA((4,)), pltpu.SemaphoreType.DMA((4,))],
        compiler_params=PARAMS,
        name="attend_more",
        cost_estimate=COST,
    )(lengths, core, *arrays)


def run_back(lengths, core, arrays, marker):
    wo, q, x = arrays[8], arrays[9], arrays[-1]
    rows, width = q.shape
    heads = width // HD
    piece = 4 * width // 16
    outs = (shaped((rows, width), BF16),) * 3 + (shaped((16, piece + 16, x.shape[1]), BF16),)
    return pl.pallas_call(
        functools.partial(attend_back, heads, len(arrays)),
        out_shape=outs,
        in_specs=[SMEM] * 2 + [HBM] * (len(arrays) + 1),
        out_specs=(HBM,) * 4,
        scratch_shapes=buffers(outs)
        + [pltpu.VMEM((rows, width), F32)] * 2
        + [pltpu.VMEM((width, QB), F32), pltpu.VMEM(wo.shape, F32)]
        + [pltpu.SemaphoreType.DMA((len(arrays),)), pltpu.SemaphoreType.DMA((7,))]
        + buffers(arrays),
        compiler_params=PARAMS,
        name="attend_back",
        cost_estimate=COST,
    )(lengths, core, *arrays, marker)


def mark_kernel(source_ref, target_ref):
    del source_ref, target_ref


def mark(values):
    return pl.pallas_call(
        mark_kernel,
        out_shape=shaped(values.shape, values.dtype),
        in_specs=[HBM],
        out_specs=HBM,
        compiler_params=pltpu.CompilerParams(vmem_limit_bytes=1 << 20),
        name="mark",
        cost_estimate=pl.CostEstimate(flops=1 << 36, bytes_accessed=1 << 10, transcendentals=0),
    )(values)


def finish_kernel(source_ref, target_ref):
    del source_ref
    target_ref[...] = jnp.zeros(target_ref.shape, F32)


def finish(values):
    return pl.pallas_call(
        finish_kernel,
        out_shape=shaped(values.shape, values.dtype),
        in_specs=[HBM],
        out_specs=VMEM,
        compiler_params=pltpu.CompilerParams(vmem_limit_bytes=1 << 20),
        name="finish",
        cost_estimate=COST,
    )(values)


def row_of(ref):
    return ref[...].astype(F32).reshape(1, -1)


def in_three(values):
    high = values.astype(BF16)
    rest = values - high.astype(F32)
    middle = rest.astype(BF16)
    return high, middle, (rest - middle.astype(F32)).astype(BF16)


def norm_step(grad, normed, rscale, gain):
    scaled = grad * gain
    first_mean = jnp.mean(scaled, axis=1, keepdims=True)
    cross_mean = jnp.mean(scaled * normed, axis=1, keepdims=True)
    return rscale * (scaled - first_mean - normed * cross_mean)


def column_of(ref):
    row = ref[...].reshape(1, -1)
    return jnp.broadcast_to(row, (128, row.shape[1])).T[:, 0:1]


def column_sum(values):
    return jnp.sum(values, axis=0, keepdims=True)


def send_out(results, outputs, semaphores, which):
    copies = [
        pltpu.make_async_copy(results[k], outputs[k], semaphores.at[k]) for k in which
    ]
    for copy in copies:
        copy.start()
    return copies


def loss_back(lengths_ref, place_ref, *refs):
    sources, outputs, refs = refs[:9], refs[9:15], refs[15:]
    targets, results = refs[:9], refs[9:15]
    coef_ref, turned_ref, semaphores, out_semaphores = refs[15:]
    copies = fetch(sources, targets, semaphores)
    piece_ref, swapped_ref, pooled_ref, match_ref, gain_ref = targets[:5]
    core, index = place_ref[0], place_ref[1]
    bounds = segment_bounds(lengths_ref)
    for copy in copies[:5]:
        copy.wait()
    first = core == 0
    queries = jnp.where(first, piece_ref[...], swapped_ref[...])
    passages = jnp.where(first, swapped_ref[...], piece_ref[...])
    count = queries.shape[0]
    own = pooled_ref.shape[0] // 2
    similarity = nt(queries, passages) / SOFTMAX_WARMTH
    match = match_ref[...].reshape(1, -1)
    match = match == lax.broadcasted_iota(jnp.int32, (count, count), 0)
    top = jnp.max(similarity, axis=1, keepdims=True)
    lse = top + jnp.log(jnp.sum(jnp.exp(similarity - top), axis=1, keepdims=True))
    positive = jnp.sum(jnp.where(match, similarity, 0.0), axis=1, keepdims=True)
    loss = jnp.sum(lse - positive, axis=0, keepdims=True) / count
    results[5][...] = jnp.broadcast_to(loss, results[5].shape)
    coef = (jnp.exp(similarity - lse) - match.astype(F32)) * (1.0 / (count * SOFTMAX_WARMTH))
    coef_ref[...] = coef
    turned_ref[...] = coef.T
    here = pl.ds(pl.multiple_of(index * own, own), own)
    grad_query = sum(nn(part, passages) for part in in_three(coef_ref[here, :]))
    grad_passage = sum(nn(part, queries) for part in in_three(turned_ref[here, :]))
    grad_unit = jnp.concatenate([grad_query, grad_passage], axis=0)
    pooled = pooled_ref[...]
    rscale = lax.rsqrt(jnp.sum(pooled * pooled, axis=1, keepdims=True) + EPS_NORM)
    inner = jnp.sum(pooled * grad_unit, axis=1, keepdims=True)
    grad_pooled = rscale * grad_unit - rscale * rscale * rscale * inner * pooled
    seqs = 2 * own
    grad_pooled = jnp.concatenate(
        [grad_pooled, jnp.zeros((128 - seqs, grad_pooled.shape[1]), F32)], axis=0
    )
    parts = in_three(grad_pooled)
    lane = lax.broadcasted_iota(jnp.int32, (1, 128), 1)
    begin = end = jnp.zeros((1, 128), jnp.int32)
    for seq, (start, stop) in enumerate(bounds):
        begin = jnp.where(lane == seq, start, begin)
        end = jnp.where(lane == seq, stop, end)
    gain = row_of(gain_ref)
    sums = [0.0, 0.0, 0.0]
    outgoing = []
    for i in range(2):
        copies[5 + 2 * i].wait()
        copies[6 + 2 * i].wait()
        normed = targets[5 + 2 * i][...]
        place = core * (2 * QB) + i * QB + lax.broadcasted_iota(jnp.int32, (QB, 128), 0)
        member = jnp.where((place >= begin) & (place < end), 1.0, 0.0).astype(BF16)
        grad = sum(nn(member, part) for part in parts)
        second = norm_step(grad, normed, column_of(targets[6 + 2 * i]), gain)
        rounded = second.astype(BF16)
        results[i][...] = second
        results[2 + i][...] = rounded
        for k, values in enumerate((rounded.astype(F32), grad * normed, grad)):
            sums[k] = sums[k] + column_sum(values)
        outgoing += send_out(results, outputs, out_semaphores, (2 + i, i))
    results[4][...] = jnp.concatenate(sums + [jnp.zeros((5, sums[0].shape[1]), F32)], axis=0)
    outgoing += send_out(results, outputs, out_semaphores, (4, 5))
    for copy in outgoing:
        copy.wait()


def norm_back(*refs):
    sources, outputs, refs = refs[:12], refs[12:17], refs[17:]
    targets, results = refs[:12], refs[12:17]
    semaphores, out_semaphores = refs[17:]
    copies = fetch(sources, targets, semaphores)
    copies[0].wait()
    copies[1].wait()
    gain = row_of(targets[0])
    sums = [0.0, 0.0, 0.0]
    outgoing = []
    for i in range(2):
        for copy in copies[2 + 5 * i : 7 + 5 * i]:
            copy.wait()
        second, pair_here, far, normed, rscale = targets[2 + 5 * i : 7 + 5 * i]
        grad = second[...] + (pair_here[...].astype(F32) + far[...].astype(F32))
        normed = normed[...]
        first = norm_step(grad, normed, column_of(rscale), gain)
        rounded = first.astype(BF16)
        results[i][...] = first
        results[2 + i][...] = rounded
        for k, values in enumerate((rounded.astype(F32), grad * normed, grad)):
            sums[k] = sums[k] + column_sum(values)
        outgoing += send_out(results, outputs, out_semaphores, (2 + i, i))
    blank = jnp.zeros((2, sums[0].shape[1]), F32)
    results[4][...] = jnp.concatenate(sums + [targets[1][0:3, :], blank], axis=0)
    outgoing += send_out(results, outputs, out_semaphores, (4,))
    for copy in outgoing:
        copy.wait()


STEPS = (0, 2, 1, 3)


def join(place_ref, *refs):
    sources, output, semaphores = refs[:4], refs[4], refs[5]
    copies = []
    for k in range(4):
        spot = (place_ref[0] + 4 - STEPS[k]) % 4
        copies.append(pltpu.make_async_copy(sources[k], output.at[spot], semaphores.at[k]))
        copies[-1].start()
    for copy in copies:
        copy.wait()


def spread(piece, place_ref, *refs):
    sources, outputs, refs = refs[:5], refs[5:20], refs[20:]
    by_z, by_y = refs[:2]
    results, semaphores, out_semaphores = refs[2:17], refs[17], refs[18]
    copies = [pltpu.make_async_copy(sources[0], by_z, semaphores.at[4])]
    for k in range(4):
        spot = (place_ref[1] + 4 - STEPS[k]) % 4
        copies.append(
            pltpu.make_async_copy(sources[1 + k], by_y.at[spot], semaphores.at[k])
        )
    for copy in copies:
        copy.start()
    part = piece // 3
    copies[0].wait()
    results[0][...] = by_z[:, :, :piece, :].astype(F32)
    outgoing = send_out(results, outputs, out_semaphores, (0,))
    for copy in copies[1:]:
        copy.wait()
    for y in range(4):
        results[1][:, y] = by_y[y, :, :piece, :].astype(F32)
    outgoing += send_out(results, outputs, out_semaphores, (1,))
    for m in range(4):
        results[2 + m][:, :part, :] = by_z[m, :, piece:, :].astype(F32)
        for y in range(4):
            results[2 + m][y, part:, :] = by_y[y, m, piece : 2 * piece - part, :].astype(F32)
        outgoing += send_out(results, outputs, out_semaphores, (2 + m,))
    small = by_y[0, 0, 2 * piece - part :, :].astype(F32)
    for k in range(7):
        results[6 + k][...] = small[k : k + 1, :].reshape(-1)
    count = results[13].shape[0]
    for k in range(2):
        results[13 + k][...] = small[7:8, 256 * k : 256 * k + count].reshape(-1)
    outgoing += send_out(results, outputs, out_semaphores, range(6, 15))
    for copy in outgoing:
        copy.wait()


def run_loss(lengths, place, arrays):
    rows, width = arrays[5].shape
    count = arrays[0].shape[0]
    outs = (
        (shaped((rows, width), F32),) * 2
        + (shaped((rows, width), BF16),) * 2
        + (shaped((8, width), F32), shaped((8, 128), F32))
    )
    return pl.pallas_call(
        loss_back,
        out_shape=outs,
        in_specs=[SMEM] * 2 + [HBM] * 9,
        out_specs=(HBM,) * 6,
        scratch_shapes=buffers(arrays)
        + buffers(outs)
        + [pltpu.VMEM((count, count), F32)] * 2
        + [pltpu.SemaphoreType.DMA((9,)), pltpu.SemaphoreType.DMA((6,))],
        compiler_params=SMALL,
        name="loss_back",
        cost_estimate=COST,
    )(lengths, place, *arrays)


def run_norm(arrays):
    rows, width = arrays[2].shape
    outs = (
        (shaped((rows, width), F32),) * 2
        + (shaped((rows, width), BF16),) * 2
        + (shaped((8, width), F32),)
    )
    return pl.pallas_call(
        norm_back,
        out_shape=outs,
        in_specs=[HBM] * 12,
        out_specs=(HBM,) * 5,
        scratch_shapes=buffers(arrays)
        + buffers(outs)
        + [pltpu.SemaphoreType.DMA((12,)), pltpu.SemaphoreType.DMA((5,))],
        compiler_params=SMALL,
        name="norm_back",
        cost_estimate=COST,
    )(*arrays)


def run_join(places, pieces):
    return pl.pallas_call(
        join,
        out_shape=shaped((4,) + pieces[0].shape, BF16),
        in_specs=[SMEM] + [HBM] * 4,
        out_specs=HBM,
        scratch_shapes=[pltpu.SemaphoreType.DMA((4,))],
        compiler_params=pltpu.CompilerParams(vmem_limit_bytes=1 << 20),
        name="join",
        cost_estimate=COST,
    )(places, *pieces)


def settle(core_ref, *refs):
    sources, output, semaphores = refs[:4], refs[4], refs[5]
    copies = []
    for k in range(4):
        first = (k // 2 + core_ref[0]) % 2 * (2 * QB) + k % 2 * QB
        spot = pl.ds(pl.multiple_of(first, QB), QB)
        copies.append(pltpu.make_async_copy(sources[k], output.at[spot, :], semaphores.at[k]))
        copies[-1].start()
    for copy in copies:
        copy.wait()


def run_settle(core, parts):
    rows, width = parts[0].shape
    return pl.pallas_call(
        settle,
        out_shape=shaped((4 * rows, width), BF16),
        in_specs=[SMEM] + [HBM] * 4,
        out_specs=HBM,
        scratch_shapes=[pltpu.SemaphoreType.DMA((4,))],
        compiler_params=pltpu.CompilerParams(vmem_limit_bytes=1 << 20),
        name="settle",
        cost_estimate=COST,
    )(core, *parts)


def run_spread(places, gathered, pieces, piece):
    width = gathered.shape[3]
    shapes = [(4, 4, piece, width)] * 2 + [(4, piece, width)] * 4
    shapes += [(width,)] * 7 + [(4 * piece,)] * 2
    return pl.pallas_call(
        functools.partial(spread, piece),
        out_shape=[shaped(shape, F32) for shape in shapes],
        in_specs=[SMEM] + [HBM] * 5,
        out_specs=[HBM] * 15,
        scratch_shapes=[pltpu.VMEM(gathered.shape, BF16)]
        + [pltpu.VMEM((4,) + pieces[0].shape, BF16)]
        + [pltpu.VMEM(shape, F32) for shape in shapes]
        + [pltpu.SemaphoreType.DMA((5,)), pltpu.SemaphoreType.DMA((15,))],
        compiler_params=SMALL,
        name="spread",
        cost_estimate=COST,
    )(places, gathered, *pieces)


def trade(values):
    return lax.all_to_all(
        values, "dp", split_axis=0, concat_axis=0, axis_index_groups=PLANES, tiled=True
    )


def share(values, groups):
    spread_out = jnp.broadcast_to(values[None], (len(groups[0]),) + values.shape)
    return lax.all_to_all(
        spread_out, "dp", split_axis=0, concat_axis=0, axis_index_groups=groups, tiled=True
    )


def ring_shift(axis, step):
    pairs = []
    for i in range(32):
        z, y, x = i // 8, (i // 2) % 4, i % 2
        z, y = ((z + step) % 4, y) if axis == "z" else (z, (y + step) % 4)
        pairs.append((i, (z * 4 + y) * 2 + x))
    return pairs


def ring_pieces(values, axis):
    return [lax.ppermute(values, "dp", ring_shift(axis, step)) for step in STEPS[1:]]


def tie(values, others):
    return lax.optimization_barrier((values, others))


class Marker:
    def __init__(self):
        self.state = jnp.zeros((8, 128), F32)

    def fence(self, ready, later):
        ready, state = tie(ready, self.state)
        later, self.state = tie(later, mark(state))
        return ready, later

    def moved(self, values, axis, pairs):
        values, state = tie(values, self.state)
        arrived, self.state = tie(lax.ppermute(values, axis, pairs), mark(state))
        return arrived

    def core_swap(self, values):
        return self.moved(values, "mp", CORE_SWAP)

    def near_swap(self, values):
        return self.moved(values, "dp", NEAR_SWAP)

    def both(self, own):
        return jnp.concatenate([own, self.core_swap(own)], axis=0)

    def near_sum(self, total):
        return (total.astype(F32) + self.near_swap(total).astype(F32)).astype(BF16)


def plane_sum(parts):
    return jnp.sum(parts.astype(F32), axis=0).astype(BF16)


def far_swap(values):
    return lax.ppermute(values, "mp", FAR_SWAP)


def norm_forward(values, gain_vec, shift_vec):
    average = jnp.mean(values, axis=-1, keepdims=True)
    centred = values - average
    rscale = lax.rsqrt(jnp.mean(centred * centred, axis=-1, keepdims=True) + EPS_NORM)
    normed = centred * rscale
    return (normed * gain_vec + shift_vec, normed, rscale[:, 0])


def gelu_and_slope(upper):
    below = 0.5 * (1.0 + lax.erf(upper * math.sqrt(0.5)))
    density = jnp.exp(-0.5 * upper * upper) * (1.0 / math.sqrt(2.0 * math.pi))
    return (upper * below).astype(BF16), (below + upper * density).astype(BF16)


def local(
    tokens,
    lengths,
    pair_index,
    query_proj,
    query_bias,
    key_proj,
    value_proj,
    value_bias,
    output_proj,
    output_bias,
    attn_gain,
    attn_shift,
    inner_proj,
    inner_bias,
    outer_proj,
    outer_bias,
    final_gain,
    final_shift,
):
    row_count, width = tokens.shape
    chunk = row_count // 2
    half = chunk // 2
    seq_count = lengths.shape[0]
    pair_count = seq_count // 2
    overall_pair_count = pair_index.shape[0]
    local_width = query_proj.shape[1]
    core = lax.axis_index("mp") % 2
    my_index = lax.axis_index("dp")
    marker = Marker()
    core_arg = jnp.reshape(core, (1,)).astype(jnp.int32)
    vectors = (output_bias, attn_gain, attn_shift, outer_bias, final_gain, final_shift)
    query_t, key_t, value_t = query_proj.T, key_proj.T, value_proj.T

    weights = (query_t, key_t, value_t, query_bias, value_bias, output_proj, *vectors)
    first = run_first(lengths, core_arg, tokens, weights, (0, 1))
    rows, query_b, key_b, value_b, key_tb, value_tb, mixed_a, lse_a = first[:8]
    attn_own_a, attn_other_a, members, vectors = first[8:]

    def own_and_other(values, weights):
        return nn(values[:half], weights), nn(values[half:], weights).astype(BF16)

    def pair(own, arrived):
        return (own + arrived.astype(F32)).astype(BF16)

    def first_norm(index, pair_here, far):
        attn_full = pair_here.astype(F32) + far.astype(F32) + output_bias
        own_tokens = rows[index * chunk : index * chunk + half].astype(F32)
        return norm_forward(own_tokens + attn_full, attn_gain_f, attn_shift_f)

    def feed_forward(own_hidden):
        whole = marker.both(own_hidden)
        act, slope = gelu_and_slope(nn(whole, inner_proj) + inner_bias.astype(F32))
        return whole, act, slope

    def last_norm(hidden, pair_here, far):
        ffn_full = pair_here.astype(F32) + far.astype(F32) + outer_bias
        return norm_forward(hidden + ffn_full, final_gain_f, final_shift_f)

    attn_pair_a = pair(attn_own_a, marker.core_swap(attn_other_a))
    attn_far_a = far_swap(attn_pair_a)
    output_bias, attn_gain_f, attn_shift_f = vectors[0], vectors[1], vectors[2]
    outer_bias, final_gain_f, final_shift_f = vectors[3], vectors[4], vectors[5]
    late_query, late_pair = tie(query_b, attn_pair_a)
    mixed_b, lse_b, attn_own_b, attn_other_b = run_more(
        lengths, core_arg, (late_query, key_b, value_tb, output_proj), (2, 3)
    )
    attn_pair_b = pair(attn_own_b, marker.core_swap(attn_other_b))
    attn_far_b = far_swap(attn_pair_b)
    attn_far_a, attn_pair_b = tie(attn_far_a, attn_pair_b)
    hidden_a, normed_one_a, rscale_one_a = first_norm(0, late_pair, attn_far_a)
    own_hidden_a = hidden_a.astype(BF16)
    hidden_ab, act_a, slope_a = feed_forward(own_hidden_a)
    ffn_own_a, ffn_other_a = own_and_other(act_a, outer_proj)
    ffn_pair_a = pair(ffn_own_a, marker.core_swap(ffn_other_a))
    attn_far_b, ffn_pair_late = tie(attn_far_b, ffn_pair_a)
    ffn_far_a = far_swap(ffn_pair_a)
    hidden_b, normed_one_b, rscale_one_b = first_norm(1, attn_pair_b, attn_far_b)
    own_hidden_b = hidden_b.astype(BF16)
    hidden_bb, act_b, slope_b = feed_forward(own_hidden_b)
    ffn_own_b, ffn_other_b = own_and_other(act_b, outer_proj)
    ffn_pair_b = pair(ffn_own_b, marker.core_swap(ffn_other_b))
    ffn_pair_b, ffn_far_a = marker.fence(ffn_pair_b, ffn_far_a)
    final_a, normed_two_a, rscale_two_a = last_norm(hidden_a, ffn_pair_late, ffn_far_a)
    pooled_a = jnp.dot(members[0], final_a, precision=HIGHEST)
    final_b, normed_two_b, rscale_two_b = last_norm(hidden_b, ffn_pair_b, far_swap(ffn_pair_b))
    pooled_part = pooled_a + jnp.dot(members[1], final_b, precision=HIGHEST)
    lse = (lse_a, lse_b)
    hidden_whole, act, slope = (hidden_ab, hidden_bb), (act_a, act_b), (slope_a, slope_b)
    normed_one, rscale_one = (normed_one_a, normed_one_b), (rscale_one_a, rscale_one_b)
    normed_two, rscale_two = (normed_two_a, normed_two_b), (rscale_two_a, rscale_two_b)
    pooled = pooled_part + marker.core_swap(pooled_part)
    pool_rscale = lax.rsqrt(jnp.sum(pooled * pooled, axis=-1, keepdims=True) + EPS_NORM)
    unit_b = (pooled * pool_rscale).astype(BF16)

    piece = lax.dynamic_slice_in_dim(unit_b, core * pair_count, pair_count, 0)
    near = marker.near_swap(piece)
    low = (my_index % 2) == 0
    piece = jnp.concatenate([jnp.where(low, piece, near), jnp.where(low, near, piece)], axis=0)
    piece = share(piece, PLANES).reshape(overall_pair_count, width)
    place_arg = jnp.stack([core, my_index]).astype(jnp.int32)
    *grads, last_sums, loss = run_loss(
        lengths,
        place_arg,
        (
            piece,
            marker.core_swap(piece),
            pooled,
            pair_index,
            final_gain,
            normed_two[0],
            rscale_two[0],
            normed_two[1],
            rscale_two[1],
        ),
    )
    grad_second, own_grad = grads[:2], grads[2:]

    inner_sums, grad_ffn, grad_up, hidden_other = [], [], [], []
    for i in range(2):
        grad_ffn.append(marker.both(own_grad[i]))
        grad_up.append((nt(grad_ffn[i], outer_proj) * slope[i].astype(F32)).astype(BF16))
        inner_sums.append(jnp.sum(grad_up[i].astype(F32), axis=0))
        other = nt(grad_up[i][half:], inner_proj).astype(BF16)
        hidden_other.append(marker.core_swap(other))
    hidden_pair = [pair(nt(grad_up[i][:half], inner_proj), hidden_other[i]) for i in range(2)]
    hidden_far = [far_swap(hidden_pair[i]) for i in range(2)]
    (late_act, late_hidden), hidden_pair = tie((act, hidden_whole), hidden_pair)
    ffn_pack = jnp.concatenate(
        [
            (tn(late_act[0], grad_ffn[0]) + tn(late_act[1], grad_ffn[1]))
            .astype(BF16)
            .reshape(16, -1, width),
            (tn(late_hidden[0], grad_up[0]) + tn(late_hidden[1], grad_up[1]))
            .astype(BF16)
            .reshape(16, -1, width),
        ],
        axis=1,
    )
    ffn_pack, hidden_far = marker.fence(ffn_pack, hidden_far)
    ffn_parts = trade(ffn_pack)

    *grads, sums = run_norm(
        (
            attn_gain,
            last_sums,
            grad_second[0],
            hidden_pair[0],
            hidden_far[0],
            normed_one[0],
            rscale_one[0],
            grad_second[1],
            hidden_pair[1],
            hidden_far[1],
            normed_one[1],
            rscale_one[1],
        )
    )
    grad_first, own_grad = grads[:2], grads[2:]
    (*own_grad, sums), state = tie((*own_grad, sums), marker.state)
    arrived = [lax.ppermute(values, "mp", CORE_SWAP) for values in (*own_grad, sums)]
    (*other_grad, other_sums), marker.state = tie(arrived, mark(state))
    grad_query, grad_key, grad_value, packed = run_back(
        lengths,
        core_arg,
        (
            own_grad[0],
            other_grad[0],
            own_grad[1],
            other_grad[1],
            mixed_a,
            mixed_b,
            *lse,
            output_proj,
            query_b,
            key_b,
            value_b,
            key_tb,
            sums,
            other_sums,
            *inner_sums,
            rows,
        ),
        marker.state,
    )
    marker = Marker()

    def input_part(first):
        span = slice(first, first + half)
        return (
            nt(grad_query[span], query_proj)
            + nt(grad_key[span], key_proj)
            + nt(grad_value[span], value_proj)
        )

    token_pair = []
    for i in range(2):
        other = input_part(i * chunk + half).astype(BF16)
        token_pair.append(pair(input_part(i * chunk), marker.core_swap(other)))
    token_pair, (packed, ffn_parts) = marker.fence(token_pair, (packed, ffn_parts))
    packed_parts = trade(packed)
    ffn_total = plane_sum(ffn_parts)
    ffn_near = lax.ppermute(ffn_total, "dp", NEAR_SWAP)
    ffn_reduced = (ffn_total.astype(F32) + ffn_near.astype(F32)).astype(BF16)
    ffn_reduced, token_pair = tie(ffn_reduced, token_pair)
    token_pair, packed_parts = marker.fence(token_pair, packed_parts)
    token_far = [far_swap(token_pair[i]) for i in range(2)]
    packed_reduced = marker.near_sum(plane_sum(packed_parts))
    piece_rows = width // 16
    places = jnp.stack([my_index // 8, (my_index // 2) % 4]).astype(jnp.int32)
    halves = [
        jnp.concatenate([ffn_reduced[:piece_rows], packed_reduced[: piece_rows // 3]], axis=0),
        jnp.concatenate([ffn_reduced[piece_rows:], packed_reduced[piece_rows // 3 :]], axis=0),
    ]
    one_ring = share(halves[0], Y_RINGS)
    pieces = ring_pieces(halves[1], "z")
    halves, (one_ring, pieces) = marker.fence(halves, (one_ring, pieces))
    other_ring = run_join(places, (halves[1], *pieces))
    pieces = ring_pieces(other_ring, "y")
    other_ring, one_ring = marker.fence(other_ring, one_ring)
    one_ring, token_far = marker.fence(one_ring, token_far)
    gathered = share(one_ring, Z_RINGS)
    token_own = [
        (grad_first[i] + (token_pair[i].astype(F32) + token_far[i].astype(F32))).astype(BF16)
        for i in range(2)
    ]
    token_other = [lax.ppermute(rows_here, "mp", CORE_SWAP) for rows_here in token_own]
    token_grad = run_settle(core_arg, (*token_own, *token_other))
    gathered, token_grad = tie(gathered, token_grad)
    closing = finish(marker.state)[0, 0]
    outer_grad, inner_grad, *rest = run_spread(
        places, gathered, (other_ring, *pieces), piece_rows
    )
    cuts = [values.reshape(local_width, width) for values in rest[:4]]
    vectors = rest[4:]
    return (
        loss[0, 0] + closing,
        token_grad,
        cuts[1].T,
        vectors[7],
        cuts[2].T,
        cuts[3].T,
        vectors[8],
        cuts[0],
        vectors[0],
        vectors[1],
        vectors[2],
        inner_grad.reshape(width, width),
        vectors[6],
        outer_grad.reshape(width, width),
        vectors[3],
        vectors[4],
        vectors[5],
    )


def solution(mesh):
    column, row, split = P(None, "mp"), P("mp", None), P("mp")
    placed = (
        (P("dp", None), P("dp"), P())
        + (column, split, column, column, split, row)
        + (P(), P(), P())
        + (column, split, row)
        + (P(), P(), P())
    )
    given = (
        (P(), P("dp", None))
        + (column, split, column, column, split, row)
        + (P(), P(), P())
        + (column, split, row)
        + (P(), P(), P())
    )
    return jax.shard_map(local, mesh=mesh, in_specs=placed, out_specs=given, check_vma=False)
```

```python
import functools
import math

import jax
import jax.numpy as jnp
from jax import lax
from jax.experimental import pallas as pl
from jax.experimental.pallas import tpu as pltpu
from jax.sharding import PartitionSpec as P

HD = 64
EPS_NORM = 1e-06
SOFTMAX_WARMTH = 0.01
NEG_FILL = -1e30
HIGHEST = lax.Precision.HIGHEST
F32 = jnp.float32
BF16 = jnp.bfloat16
QB = 256
KB = 256

CORE_SWAP = [(i, i ^ 1) for i in range(4)]
FAR_SWAP = [(i, i ^ 2) for i in range(4)]
NEAR_SWAP = [(i, i ^ 1) for i in range(32)]
PLANES = [[i * 2 + x for i in range(16)] for x in range(2)]
Z_RINGS = [[i + 8 * z for z in range(4)] for i in range(8)]
Y_RINGS = [[z * 8 + x + 2 * y for y in range(4)] for z in range(4) for x in range(2)]

SMEM = pl.BlockSpec(memory_space=pltpu.SMEM)
VMEM = pl.BlockSpec(memory_space=pltpu.VMEM)
HBM = pl.BlockSpec(memory_space=pltpu.HBM)


def nn(left, right):
    return lax.dot_general(left, right, (((1,), (0,)), ((), ())), preferred_element_type=F32)


def nt(left, right):
    return lax.dot_general(left, right, (((1,), (1,)), ((), ())), preferred_element_type=F32)


def tn(left, right):
    return lax.dot_general(left, right, (((0,), (0,)), ((), ())), preferred_element_type=F32)


def place_of_block(block, core, rows):
    return ((block % 2) * 2 + block // 2) * QB + core * (rows // 2) & (rows - 1)


def spot_of_keys(j, core, rows):
    place = (j * KB + core * (rows // 2)) & (rows - 1)
    block = place // QB
    return pl.multiple_of(((block % 2) * 2 + block // 2) * QB + place % QB, KB)


def segment_bounds(lengths_ref):
    bounds, total = [], jnp.int32(0)
    for s in range(lengths_ref.shape[0]):
        start = total
        total = total + lengths_ref[s]
        bounds.append((start, total))
    return bounds


def block_span(bounds, first, rows):
    place = first + lax.broadcasted_iota(jnp.int32, (1, QB), 1)
    low, high = first, first + KB
    begin = jnp.full((1, QB), bounds[-1][1], jnp.int32)
    end = jnp.full((1, QB), rows, jnp.int32)
    for start, stop in bounds:
        inside = (place >= start) & (place < stop)
        begin = jnp.where(inside, start, begin)
        end = jnp.where(inside, stop, end)
        touches = (stop > first) & (start < first + QB) & (stop > start)
        low = jnp.where(touches, jnp.minimum(low, start), low)
        high = jnp.where(touches, jnp.maximum(high, stop), high)
    return low // KB, (high + KB - 1) // KB, begin, end


def head_copies(values, heads):
    lane = lax.broadcasted_iota(jnp.int32, values.shape, 1) // HD
    blank = jnp.zeros_like(values)
    return jnp.concatenate([jnp.where(lane == h, values, blank) for h in range(heads)], axis=0)


def span_mask(begin, end, block, heads):
    place = block * KB + lax.broadcasted_iota(jnp.int32, (KB, QB), 0)
    keep = (place >= begin) & (place < end)
    return jnp.concatenate([keep] * heads, axis=1)


def attend(heads, blocks, core, bounds, q_ref, k_ref, vt_ref, mixed_ref, lse_ref, acc_ref):
    rows = k_ref.shape[0]
    for i, block in enumerate(blocks):
        low, high, begin, end = block_span(bounds, place_of_block(block, core, rows), rows)
        stack = head_copies(q_ref[block * QB : (block + 1) * QB, :], heads)
        acc_ref[...] = jnp.zeros(acc_ref.shape, F32)

        def step(j, carry, stack=stack, begin=begin, end=end):
            top, total = carry
            spot = spot_of_keys(j, core, rows)
            scores = nt(k_ref[pl.ds(spot, KB), :], stack)
            scores = jnp.where(span_mask(begin, end, j, heads), scores, NEG_FILL)
            peak = jnp.maximum(top, jnp.max(scores, axis=0, keepdims=True))
            fade = jnp.exp(top - peak)
            probs = jnp.exp(scores - peak)
            total = total * fade + jnp.sum(probs, axis=0, keepdims=True)
            probs = probs.astype(BF16)
            for h in range(heads):
                part = slice(h * QB, (h + 1) * QB)
                span = slice(h * HD, (h + 1) * HD)
                acc_ref[span, :] = acc_ref[span, :] * fade[:, part] + nn(
                    vt_ref[span, pl.ds(spot, KB)], probs[:, part]
                )
            return peak, total

        top = jnp.full((1, heads * QB), NEG_FILL, F32)
        top, total = lax.fori_loop(
            low, high, step, (top, jnp.zeros((1, heads * QB), F32)), unroll=False
        )
        scale = 1.0 / total
        mixed = jnp.concatenate(
            [
                acc_ref[h * HD : (h + 1) * HD, :] * scale[:, h * QB : (h + 1) * QB]
                for h in range(heads)
            ],
            axis=0,
        )
        mixed_ref[i * QB : (i + 1) * QB, :] = mixed.T.astype(BF16)
        lse_ref[i, :, :] = jnp.broadcast_to(top + jnp.log(total), (8, heads * QB))


def fetch(sources, targets, semaphores, order=()):
    copies = [
        pltpu.make_async_copy(source, target, semaphores.at[i])
        for i, (source, target) in enumerate(zip(sources, targets))
    ]
    for i in [*order, *(i for i in range(len(copies)) if i not in order)]:
        copies[i].start()
    return copies


def project(mixed_ref, weights_ref, results, outputs, semaphores):
    results[1][...] = nn(mixed_ref[QB:, :], weights_ref[...]).astype(BF16)
    copies = send_out(results, outputs, semaphores, (1,))
    results[0][...] = nn(mixed_ref[:QB, :], weights_ref[...])
    return copies + send_out(results, outputs, semaphores, (0,))


def attend_first(heads, blocks, lengths_ref, core_ref, *refs):
    sources, outputs, refs = refs[:13], refs[13:25], refs[25:]
    results, targets, refs = refs[:12], refs[12:24], refs[24:]
    acc_ref, semaphores, out_semaphores = refs
    x_ref, q_ref, k_ref, v_ref, kt_ref, vt_ref, mixed_ref, lse_ref = results[:8]
    wqt_ref, wkt_ref, wvt_ref, bq_ref, bv_ref, wo_ref = targets[:6]
    rows = x_ref.shape[0]
    core = core_ref[0]
    copies = fetch(sources[1:], targets, semaphores)
    row_copies = []
    for block in range(rows // QB):
        first = pl.multiple_of(place_of_block(block, core, rows), QB)
        row_copies.append(
            pltpu.make_async_copy(
                sources[0].at[pl.ds(first, QB), :],
                x_ref.at[pl.ds(block * QB, QB), :],
                semaphores.at[12 + block],
            )
        )
        row_copies[-1].start()
    for copy in copies:
        copy.wait()
    query_bias, value_bias = row_of(bq_ref), row_of(bv_ref)
    for block in range(rows // QB):
        row_copies[block].wait()
        part = slice(block * QB, (block + 1) * QB)
        x = x_ref[part, :]
        q = (nt(x, wqt_ref[...]) + query_bias).astype(BF16)
        q_ref[part, :] = q * BF16(0.125)
        k_ref[part, :] = nt(x, wkt_ref[...]).astype(BF16)
        kt_ref[:, part] = nt(wkt_ref[...], x).astype(BF16)
        v = nt(x, wvt_ref[...]) + value_bias
        v_ref[part, :] = v.astype(BF16)
        vt_ref[:, part] = v.T.astype(BF16)
    outgoing = send_out(results, outputs, out_semaphores, range(6))
    bounds = segment_bounds(lengths_ref)
    place = core * (2 * QB) + lax.broadcasted_iota(jnp.int32, (1, QB), 1)
    for i in range(2):
        member = [
            jnp.where((place + i * QB >= start) & (place + i * QB < stop), 1.0, 0.0)
            for start, stop in bounds
        ]
        results[10][i] = jnp.concatenate(member, axis=0)
    lines = [row_of(ref) for ref in targets[6:]]
    results[11][...] = jnp.concatenate(lines + [jnp.zeros((2, lines[0].shape[1]), F32)], axis=0)
    outgoing += send_out(results, outputs, out_semaphores, (10, 11))
    attend(heads, blocks, core, bounds, q_ref, k_ref, vt_ref, mixed_ref, lse_ref, acc_ref)
    outgoing += project(mixed_ref, wo_ref, results[8:], outputs[8:], out_semaphores.at[8:10])
    outgoing += send_out(results, outputs, out_semaphores, (6, 7))
    for copy in outgoing:
        copy.wait()


def attend_more(heads, blocks, lengths_ref, core_ref, *refs):
    sources, outputs, refs = refs[:4], refs[4:8], refs[8:]
    targets, results, refs = refs[:4], refs[4:8], refs[8:]
    acc_ref, semaphores, out_semaphores = refs
    q_ref, k_ref, vt_ref, wo_ref = targets
    mixed_ref, lse_ref = results[:2]
    for copy in fetch(sources, targets, semaphores):
        copy.wait()
    bounds = segment_bounds(lengths_ref)
    attend(heads, blocks, core_ref[0], bounds, q_ref, k_ref, vt_ref, mixed_ref, lse_ref, acc_ref)
    outgoing = project(mixed_ref, wo_ref, results[2:], outputs[2:], out_semaphores.at[2:])
    outgoing += send_out(results, outputs, out_semaphores, (0, 1))
    for copy in outgoing:
        copy.wait()


def attend_back(heads, inputs, lengths_ref, core_ref, *refs):
    sources, refs = refs[:inputs], refs[inputs + 1 :]
    outputs, refs = refs[:4], refs[4:]
    gq_ref, gk_ref, gv_ref, pack_ref = refs[:4]
    dk_ref, dv_ref, dqt_ref, wo_acc_ref, semaphores, out_semaphores = refs[4:10]
    targets = refs[10:]
    copies = fetch(sources, targets, semaphores, (10, 9, 11, 12, 0, 4, 8, 6, 1, 2, 3, 5, 7))
    grads = targets[0:4]
    mixed = targets[4:6]
    lses = targets[6:8]
    wo_ref, q_ref, k_ref, v_ref, kt_ref = targets[8:13]
    own_sums, other_sums, inner_a, inner_b, x_ref = targets[13:]
    rows, width = q_ref.shape
    core = core_ref[0]
    bounds = segment_bounds(lengths_ref)
    dk_ref[...] = jnp.zeros(dk_ref.shape, F32)
    dv_ref[...] = jnp.zeros(dv_ref.shape, F32)
    lane = lax.broadcasted_iota(jnp.int32, (8, width), 1) // HD
    which = (lane == lax.broadcasted_iota(jnp.int32, (8, width), 0)).astype(F32).astype(BF16)
    for i in (0, 4, 6, 8, 9, 10, 11, 12):
        copies[i].wait()
    for block in range(rows // QB):
        if block > 0:
            copies[block].wait()
        if block == 2:
            copies[5].wait()
            copies[7].wait()
        low, high, begin, end = block_span(bounds, place_of_block(block, core, rows), rows)
        part = slice(block * QB, (block + 1) * QB)
        own = slice(block % 2 * QB, block % 2 * QB + QB)
        grad_attn = grads[block][...]
        mixed_here = mixed[block // 2][own, :]
        outer = tn(mixed_here, grad_attn)
        wo_acc_ref[...] = outer if block == 0 else wo_acc_ref[...] + outer
        grad_mixed = nt(grad_attn, wo_ref[...]).astype(BF16)
        product = grad_mixed.astype(F32) * mixed_here.astype(F32)
        sums = sum(nt(which, part) for part in in_three(product)[:2])
        delta = jnp.concatenate([sums[h : h + 1, :] for h in range(heads)], axis=1)
        lse = lses[block // 2][block % 2, 0:1, :]
        q_stack = head_copies(q_ref[part, :], heads)
        g_stack = head_copies(grad_mixed, heads)
        dqt_ref[...] = jnp.zeros(dqt_ref.shape, F32)

        def step(
            j, carry, delta=delta, lse=lse, q_stack=q_stack, g_stack=g_stack, begin=begin, end=end
        ):
            here = pl.ds(spot_of_keys(j, core, rows), KB)
            scores = nt(k_ref[here, :], q_stack)
            scores = jnp.where(span_mask(begin, end, j, heads), scores, NEG_FILL)
            probs = jnp.exp(scores - lse)
            grad = (probs * (nt(v_ref[here, :], g_stack) - delta)).astype(BF16)
            dv_ref[here, :] += nn(probs.astype(BF16), g_stack)
            dk_ref[here, :] += nn(grad, q_stack)
            for h in range(heads):
                span = slice(h * HD, (h + 1) * HD)
                dqt_ref[span, :] += nn(kt_ref[span, here], grad[:, h * QB : (h + 1) * QB])
            return carry

        lax.fori_loop(low, high, step, 0, unroll=False)
        gq_ref[part, :] = (dqt_ref[...].T * 0.125).astype(BF16)
    gk_ref[...] = dk_ref[...].astype(BF16)
    gv_ref[...] = dv_ref[...].astype(BF16)
    for copy in copies[13:]:
        copy.wait()
    outgoing = fetch(refs[:3], outputs[:3], out_semaphores)
    sums = [jnp.sum(ref[...].astype(F32), axis=0, keepdims=True) for ref in (gq_ref, gv_ref)]
    blank = jnp.zeros((1, 256 - width), F32)
    tail = jnp.concatenate([sums[0], blank, sums[1], blank, jnp.zeros((1, 256), F32)], axis=1)
    inner = row_of(inner_a) + row_of(inner_b)
    paired = own_sums[0:6, :] + other_sums[0:6, :]
    small = [paired, inner, tail, jnp.zeros((8, tail.shape[1]), F32)]
    small = jnp.concatenate(small, axis=0).astype(BF16)
    piece = pack_ref.shape[1] - 16
    per = width // piece
    for m, source in enumerate((None, gq_ref, gk_ref, gv_ref)):
        total = wo_acc_ref[...] if source is None else tn(source[...], x_ref[...])
        for t in range(per):
            cut = total[t * piece : (t + 1) * piece, :].astype(BF16)
            pack_ref[m * per + t, 0:piece, :] = cut
            pack_ref[m * per + t, piece:, :] = small if m + t == 0 else jnp.zeros_like(small)
        here = pl.ds(m * per, per)
        copy = pltpu.make_async_copy(
            pack_ref.at[here], outputs[3].at[here], out_semaphores.at[3 + m]
        )
        copy.start()
        outgoing.append(copy)
    for copy in outgoing:
        copy.wait()


def shaped(shape, dtype):
    return jax.ShapeDtypeStruct(shape, dtype)


PARAMS = pltpu.CompilerParams(vmem_limit_bytes=60 << 20)
SMALL = pltpu.CompilerParams(vmem_limit_bytes=60 << 20)
COST = pl.CostEstimate(flops=1024, bytes_accessed=1024, transcendentals=0)


def buffers(arrays):
    return [pltpu.VMEM(array.shape, array.dtype) for array in arrays]


def attend_shapes(count, heads, width):
    rows = count * QB
    return (
        shaped((rows, heads * HD), BF16),
        shaped((count, 8, heads * QB), F32),
        shaped((rows // 2, width), F32),
        shaped((rows // 2, width), BF16),
    )


def run_first(lengths, core, tokens, weights, blocks):
    rows, width = tokens.shape
    local_width = weights[0].shape[0]
    heads = local_width // HD
    outs = (
        (shaped(tokens.shape, BF16),)
        + (shaped((rows, local_width), BF16),) * 3
        + (shaped((local_width, rows), BF16),) * 2
        + attend_shapes(len(blocks), heads, width)
        + (shaped((2, lengths.shape[0], QB), F32), shaped((8, width), F32))
    )
    return pl.pallas_call(
        functools.partial(attend_first, heads, blocks),
        out_shape=outs,
        in_specs=[SMEM] * 2 + [HBM] * 13,
        out_specs=(HBM,) * 12,
        scratch_shapes=buffers(outs)
        + buffers(weights)
        + [pltpu.VMEM((local_width, QB), F32)]
        + [pltpu.SemaphoreType.DMA((12 + rows // QB,)), pltpu.SemaphoreType.DMA((12,))],
        compiler_params=PARAMS,
        name="attend_first",
        cost_estimate=COST,
    )(lengths, core, tokens, *weights)


def run_more(lengths, core, arrays, blocks):
    rows, local_width = arrays[0].shape
    heads = local_width // HD
    outs = attend_shapes(len(blocks), heads, arrays[3].shape[1])
    return pl.pallas_call(
        functools.partial(attend_more, heads, blocks),
        out_shape=outs,
        in_specs=[SMEM] * 2 + [HBM] * 4,
        out_specs=(HBM,) * 4,
        scratch_shapes=buffers(arrays)
        + buffers(outs)
        + [pltpu.VMEM((local_width, QB), F32)]
        + [pltpu.SemaphoreType.DMA((4,)), pltpu.SemaphoreType.DMA((4,))],
        compiler_params=PARAMS,
        name="attend_more",
        cost_estimate=COST,
    )(lengths, core, *arrays)


def run_back(lengths, core, arrays, marker):
    wo, q, x = arrays[8], arrays[9], arrays[-1]
    rows, width = q.shape
    heads = width // HD
    piece = 4 * width // 16
    outs = (shaped((rows, width), BF16),) * 3 + (shaped((16, piece + 16, x.shape[1]), BF16),)
    return pl.pallas_call(
        functools.partial(attend_back, heads, len(arrays)),
        out_shape=outs,
        in_specs=[SMEM] * 2 + [HBM] * (len(arrays) + 1),
        out_specs=(HBM,) * 4,
        scratch_shapes=buffers(outs)
        + [pltpu.VMEM((rows, width), F32)] * 2
        + [pltpu.VMEM((width, QB), F32), pltpu.VMEM(wo.shape, F32)]
        + [pltpu.SemaphoreType.DMA((len(arrays),)), pltpu.SemaphoreType.DMA((7,))]
        + buffers(arrays),
        compiler_params=PARAMS,
        name="attend_back",
        cost_estimate=COST,
    )(lengths, core, *arrays, marker)


def mark_kernel(source_ref, target_ref):
    del source_ref, target_ref


def mark(values):
    return pl.pallas_call(
        mark_kernel,
        out_shape=shaped(values.shape, values.dtype),
        in_specs=[HBM],
        out_specs=HBM,
        compiler_params=pltpu.CompilerParams(vmem_limit_bytes=1 << 20),
        name="mark",
        cost_estimate=pl.CostEstimate(flops=1 << 36, bytes_accessed=1 << 10, transcendentals=0),
    )(values)


def finish_kernel(source_ref, target_ref):
    del source_ref
    target_ref[...] = jnp.zeros(target_ref.shape, F32)


def finish(values):
    return pl.pallas_call(
        finish_kernel,
        out_shape=shaped(values.shape, values.dtype),
        in_specs=[HBM],
        out_specs=VMEM,
        compiler_params=pltpu.CompilerParams(vmem_limit_bytes=1 << 20),
        name="finish",
        cost_estimate=COST,
    )(values)


def row_of(ref):
    return ref[...].astype(F32).reshape(1, -1)


def in_three(values):
    high = values.astype(BF16)
    rest = values - high.astype(F32)
    middle = rest.astype(BF16)
    return high, middle, (rest - middle.astype(F32)).astype(BF16)


def norm_step(grad, normed, rscale, gain):
    scaled = grad * gain
    first_mean = jnp.mean(scaled, axis=1, keepdims=True)
    cross_mean = jnp.mean(scaled * normed, axis=1, keepdims=True)
    return rscale * (scaled - first_mean - normed * cross_mean)


def column_of(ref):
    row = ref[...].reshape(1, -1)
    return jnp.broadcast_to(row, (128, row.shape[1])).T[:, 0:1]


def column_sum(values):
    return jnp.sum(values, axis=0, keepdims=True)


def send_out(results, outputs, semaphores, which):
    copies = [
        pltpu.make_async_copy(results[k], outputs[k], semaphores.at[k]) for k in which
    ]
    for copy in copies:
        copy.start()
    return copies


def loss_back(lengths_ref, place_ref, *refs):
    sources, outputs, refs = refs[:9], refs[9:15], refs[15:]
    targets, results = refs[:9], refs[9:15]
    coef_ref, turned_ref, semaphores, out_semaphores = refs[15:]
    copies = fetch(sources, targets, semaphores)
    piece_ref, swapped_ref, pooled_ref, match_ref, gain_ref = targets[:5]
    core, index = place_ref[0], place_ref[1]
    bounds = segment_bounds(lengths_ref)
    for copy in copies[:5]:
        copy.wait()
    first = core == 0
    queries = jnp.where(first, piece_ref[...], swapped_ref[...])
    passages = jnp.where(first, swapped_ref[...], piece_ref[...])
    count = queries.shape[0]
    own = pooled_ref.shape[0] // 2
    similarity = nt(queries, passages) / SOFTMAX_WARMTH
    match = match_ref[...].reshape(1, -1)
    match = match == lax.broadcasted_iota(jnp.int32, (count, count), 0)
    top = jnp.max(similarity, axis=1, keepdims=True)
    lse = top + jnp.log(jnp.sum(jnp.exp(similarity - top), axis=1, keepdims=True))
    positive = jnp.sum(jnp.where(match, similarity, 0.0), axis=1, keepdims=True)
    loss = jnp.sum(lse - positive, axis=0, keepdims=True) / count
    results[5][...] = jnp.broadcast_to(loss, results[5].shape)
    coef = (jnp.exp(similarity - lse) - match.astype(F32)) * (1.0 / (count * SOFTMAX_WARMTH))
    coef_ref[...] = coef
    turned_ref[...] = coef.T
    here = pl.ds(pl.multiple_of(index * own, own), own)
    grad_query = sum(nn(part, passages) for part in in_three(coef_ref[here, :]))
    grad_passage = sum(nn(part, queries) for part in in_three(turned_ref[here, :]))
    grad_unit = jnp.concatenate([grad_query, grad_passage], axis=0)
    pooled = pooled_ref[...]
    rscale = lax.rsqrt(jnp.sum(pooled * pooled, axis=1, keepdims=True) + EPS_NORM)
    inner = jnp.sum(pooled * grad_unit, axis=1, keepdims=True)
    grad_pooled = rscale * grad_unit - rscale * rscale * rscale * inner * pooled
    seqs = 2 * own
    grad_pooled = jnp.concatenate(
        [grad_pooled, jnp.zeros((128 - seqs, grad_pooled.shape[1]), F32)], axis=0
    )
    parts = in_three(grad_pooled)
    lane = lax.broadcasted_iota(jnp.int32, (1, 128), 1)
    begin = end = jnp.zeros((1, 128), jnp.int32)
    for seq, (start, stop) in enumerate(bounds):
        begin = jnp.where(lane == seq, start, begin)
        end = jnp.where(lane == seq, stop, end)
    gain = row_of(gain_ref)
    sums = [0.0, 0.0, 0.0]
    outgoing = []
    for i in range(2):
        copies[5 + 2 * i].wait()
        copies[6 + 2 * i].wait()
        normed = targets[5 + 2 * i][...]
        place = core * (2 * QB) + i * QB + lax.broadcasted_iota(jnp.int32, (QB, 128), 0)
        member = jnp.where((place >= begin) & (place < end), 1.0, 0.0).astype(BF16)
        grad = sum(nn(member, part) for part in parts)
        second = norm_step(grad, normed, column_of(targets[6 + 2 * i]), gain)
        rounded = second.astype(BF16)
        results[i][...] = second
        results[2 + i][...] = rounded
        for k, values in enumerate((rounded.astype(F32), grad * normed, grad)):
            sums[k] = sums[k] + column_sum(values)
        outgoing += send_out(results, outputs, out_semaphores, (2 + i, i))
    results[4][...] = jnp.concatenate(sums + [jnp.zeros((5, sums[0].shape[1]), F32)], axis=0)
    outgoing += send_out(results, outputs, out_semaphores, (4, 5))
    for copy in outgoing:
        copy.wait()


def norm_back(*refs):
    sources, outputs, refs = refs[:12], refs[12:17], refs[17:]
    targets, results = refs[:12], refs[12:17]
    semaphores, out_semaphores = refs[17:]
    copies = fetch(sources, targets, semaphores)
    copies[0].wait()
    copies[1].wait()
    gain = row_of(targets[0])
    sums = [0.0, 0.0, 0.0]
    outgoing = []
    for i in range(2):
        for copy in copies[2 + 5 * i : 7 + 5 * i]:
            copy.wait()
        second, pair_here, far, normed, rscale = targets[2 + 5 * i : 7 + 5 * i]
        grad = second[...] + (pair_here[...].astype(F32) + far[...].astype(F32))
        normed = normed[...]
        first = norm_step(grad, normed, column_of(rscale), gain)
        rounded = first.astype(BF16)
        results[i][...] = first
        results[2 + i][...] = rounded
        for k, values in enumerate((rounded.astype(F32), grad * normed, grad)):
            sums[k] = sums[k] + column_sum(values)
        outgoing += send_out(results, outputs, out_semaphores, (2 + i, i))
    blank = jnp.zeros((2, sums[0].shape[1]), F32)
    results[4][...] = jnp.concatenate(sums + [targets[1][0:3, :], blank], axis=0)
    outgoing += send_out(results, outputs, out_semaphores, (4,))
    for copy in outgoing:
        copy.wait()


STEPS = (0, 2, 1, 3)


def join(place_ref, *refs):
    sources, output, semaphores = refs[:4], refs[4], refs[5]
    copies = []
    for k in range(4):
        spot = (place_ref[0] + 4 - STEPS[k]) % 4
        copies.append(pltpu.make_async_copy(sources[k], output.at[spot], semaphores.at[k]))
        copies[-1].start()
    for copy in copies:
        copy.wait()


def spread(piece, place_ref, *refs):
    sources, outputs, refs = refs[:5], refs[5:20], refs[20:]
    by_z, by_y = refs[:2]
    results, semaphores, out_semaphores = refs[2:17], refs[17], refs[18]
    copies = [pltpu.make_async_copy(sources[0], by_z, semaphores.at[4])]
    for k in range(4):
        spot = (place_ref[1] + 4 - STEPS[k]) % 4
        copies.append(
            pltpu.make_async_copy(sources[1 + k], by_y.at[spot], semaphores.at[k])
        )
    for copy in copies:
        copy.start()
    part = piece // 3
    copies[0].wait()
    results[0][...] = by_z[:, :, :piece, :].astype(F32)
    outgoing = send_out(results, outputs, out_semaphores, (0,))
    for copy in copies[1:]:
        copy.wait()
    for y in range(4):
        results[1][:, y] = by_y[y, :, :piece, :].astype(F32)
    outgoing += send_out(results, outputs, out_semaphores, (1,))
    for m in range(4):
        results[2 + m][:, :part, :] = by_z[m, :, piece:, :].astype(F32)
        for y in range(4):
            results[2 + m][y, part:, :] = by_y[y, m, piece : 2 * piece - part, :].astype(F32)
        outgoing += send_out(results, outputs, out_semaphores, (2 + m,))
    small = by_y[0, 0, 2 * piece - part :, :].astype(F32)
    for k in range(7):
        results[6 + k][...] = small[k : k + 1, :].reshape(-1)
    count = results[13].shape[0]
    for k in range(2):
        results[13 + k][...] = small[7:8, 256 * k : 256 * k + count].reshape(-1)
    outgoing += send_out(results, outputs, out_semaphores, range(6, 15))
    for copy in outgoing:
        copy.wait()


def run_loss(lengths, place, arrays):
    rows, width = arrays[5].shape
    count = arrays[0].shape[0]
    outs = (
        (shaped((rows, width), F32),) * 2
        + (shaped((rows, width), BF16),) * 2
        + (shaped((8, width), F32), shaped((8, 128), F32))
    )
    return pl.pallas_call(
        loss_back,
        out_shape=outs,
        in_specs=[SMEM] * 2 + [HBM] * 9,
        out_specs=(HBM,) * 6,
        scratch_shapes=buffers(arrays)
        + buffers(outs)
        + [pltpu.VMEM((count, count), F32)] * 2
        + [pltpu.SemaphoreType.DMA((9,)), pltpu.SemaphoreType.DMA((6,))],
        compiler_params=SMALL,
        name="loss_back",
        cost_estimate=COST,
    )(lengths, place, *arrays)


def run_norm(arrays):
    rows, width = arrays[2].shape
    outs = (
        (shaped((rows, width), F32),) * 2
        + (shaped((rows, width), BF16),) * 2
        + (shaped((8, width), F32),)
    )
    return pl.pallas_call(
        norm_back,
        out_shape=outs,
        in_specs=[HBM] * 12,
        out_specs=(HBM,) * 5,
        scratch_shapes=buffers(arrays)
        + buffers(outs)
        + [pltpu.SemaphoreType.DMA((12,)), pltpu.SemaphoreType.DMA((5,))],
        compiler_params=SMALL,
        name="norm_back",
        cost_estimate=COST,
    )(*arrays)


def run_join(places, pieces):
    return pl.pallas_call(
        join,
        out_shape=shaped((4,) + pieces[0].shape, BF16),
        in_specs=[SMEM] + [HBM] * 4,
        out_specs=HBM,
        scratch_shapes=[pltpu.SemaphoreType.DMA((4,))],
        compiler_params=pltpu.CompilerParams(vmem_limit_bytes=1 << 20),
        name="join",
        cost_estimate=COST,
    )(places, *pieces)


def settle(core_ref, *refs):
    sources, output, semaphores = refs[:4], refs[4], refs[5]
    copies = []
    for k in range(4):
        first = (k // 2 + core_ref[0]) % 2 * (2 * QB) + k % 2 * QB
        spot = pl.ds(pl.multiple_of(first, QB), QB)
        copies.append(pltpu.make_async_copy(sources[k], output.at[spot, :], semaphores.at[k]))
        copies[-1].start()
    for copy in copies:
        copy.wait()


def run_settle(core, parts):
    rows, width = parts[0].shape
    return pl.pallas_call(
        settle,
        out_shape=shaped((4 * rows, width), BF16),
        in_specs=[SMEM] + [HBM] * 4,
        out_specs=HBM,
        scratch_shapes=[pltpu.SemaphoreType.DMA((4,))],
        compiler_params=pltpu.CompilerParams(vmem_limit_bytes=1 << 20),
        name="settle",
        cost_estimate=COST,
    )(core, *parts)


def run_spread(places, gathered, pieces, piece):
    width = gathered.shape[3]
    shapes = [(4, 4, piece, width)] * 2 + [(4, piece, width)] * 4
    shapes += [(width,)] * 7 + [(4 * piece,)] * 2
    return pl.pallas_call(
        functools.partial(spread, piece),
        out_shape=[shaped(shape, F32) for shape in shapes],
        in_specs=[SMEM] + [HBM] * 5,
        out_specs=[HBM] * 15,
        scratch_shapes=[pltpu.VMEM(gathered.shape, BF16)]
        + [pltpu.VMEM((4,) + pieces[0].shape, BF16)]
        + [pltpu.VMEM(shape, F32) for shape in shapes]
        + [pltpu.SemaphoreType.DMA((5,)), pltpu.SemaphoreType.DMA((15,))],
        compiler_params=SMALL,
        name="spread",
        cost_estimate=COST,
    )(places, gathered, *pieces)


def trade(values):
    return lax.all_to_all(
        values, "dp", split_axis=0, concat_axis=0, axis_index_groups=PLANES, tiled=True
    )


def share(values, groups):
    count = 32 if groups is None else len(groups[0])
    spread_out = jnp.broadcast_to(values[None], (count,) + values.shape)
    return lax.all_to_all(
        spread_out, "dp", split_axis=0, concat_axis=0, axis_index_groups=groups, tiled=True
    )


def ring_shift(axis, step):
    pairs = []
    for i in range(32):
        z, y, x = i // 8, (i // 2) % 4, i % 2
        z, y = ((z + step) % 4, y) if axis == "z" else (z, (y + step) % 4)
        pairs.append((i, (z * 4 + y) * 2 + x))
    return pairs


def ring_pieces(values, axis):
    return [lax.ppermute(values, "dp", ring_shift(axis, step)) for step in STEPS[1:]]


def tie(values, others):
    return lax.optimization_barrier((values, others))


class Marker:
    def __init__(self):
        self.state = jnp.zeros((8, 128), F32)

    def fence(self, ready, later):
        ready, state = tie(ready, self.state)
        later, self.state = tie(later, mark(state))
        return ready, later

    def moved(self, values, axis, pairs):
        values, state = tie(values, self.state)
        arrived, self.state = tie(lax.ppermute(values, axis, pairs), mark(state))
        return arrived

    def core_swap(self, values):
        return self.moved(values, "mp", CORE_SWAP)

    def near_swap(self, values):
        return self.moved(values, "dp", NEAR_SWAP)

    def both(self, own):
        return jnp.concatenate([own, self.core_swap(own)], axis=0)

    def near_sum(self, total):
        return (total.astype(F32) + self.near_swap(total).astype(F32)).astype(BF16)


def plane_sum(parts):
    return jnp.sum(parts.astype(F32), axis=0).astype(BF16)


def far_swap(values):
    return lax.ppermute(values, "mp", FAR_SWAP)


def norm_forward(values, gain_vec, shift_vec):
    average = jnp.mean(values, axis=-1, keepdims=True)
    centred = values - average
    rscale = lax.rsqrt(jnp.mean(centred * centred, axis=-1, keepdims=True) + EPS_NORM)
    normed = centred * rscale
    return (normed * gain_vec + shift_vec, normed, rscale[:, 0])


def gelu_and_slope(upper):
    below = 0.5 * (1.0 + lax.erf(upper * math.sqrt(0.5)))
    density = jnp.exp(-0.5 * upper * upper) * (1.0 / math.sqrt(2.0 * math.pi))
    return (upper * below).astype(BF16), (below + upper * density).astype(BF16)


def local(
    tokens,
    lengths,
    pair_index,
    query_proj,
    query_bias,
    key_proj,
    value_proj,
    value_bias,
    output_proj,
    output_bias,
    attn_gain,
    attn_shift,
    inner_proj,
    inner_bias,
    outer_proj,
    outer_bias,
    final_gain,
    final_shift,
):
    row_count, width = tokens.shape
    chunk = row_count // 2
    half = chunk // 2
    seq_count = lengths.shape[0]
    pair_count = seq_count // 2
    overall_pair_count = pair_index.shape[0]
    local_width = query_proj.shape[1]
    core = lax.axis_index("mp") % 2
    my_index = lax.axis_index("dp")
    marker = Marker()
    core_arg = jnp.reshape(core, (1,)).astype(jnp.int32)
    vectors = (output_bias, attn_gain, attn_shift, outer_bias, final_gain, final_shift)
    query_t, key_t, value_t = query_proj.T, key_proj.T, value_proj.T

    weights = (query_t, key_t, value_t, query_bias, value_bias, output_proj, *vectors)
    first = run_first(lengths, core_arg, tokens, weights, (0, 1))
    rows, query_b, key_b, value_b, key_tb, value_tb, mixed_a, lse_a = first[:8]
    attn_own_a, attn_other_a, members, vectors = first[8:]

    def own_and_other(values, weights):
        return nn(values[:half], weights), nn(values[half:], weights).astype(BF16)

    def pair(own, arrived):
        return (own + arrived.astype(F32)).astype(BF16)

    def first_norm(index, pair_here, far):
        attn_full = pair_here.astype(F32) + far.astype(F32) + output_bias
        own_tokens = rows[index * chunk : index * chunk + half].astype(F32)
        return norm_forward(own_tokens + attn_full, attn_gain_f, attn_shift_f)

    def feed_forward(own_hidden):
        whole = marker.both(own_hidden)
        act, slope = gelu_and_slope(nn(whole, inner_proj) + inner_bias.astype(F32))
        return whole, act, slope

    def last_norm(hidden, pair_here, far):
        ffn_full = pair_here.astype(F32) + far.astype(F32) + outer_bias
        return norm_forward(hidden + ffn_full, final_gain_f, final_shift_f)

    attn_pair_a = pair(attn_own_a, marker.core_swap(attn_other_a))
    attn_far_a = far_swap(attn_pair_a)
    output_bias, attn_gain_f, attn_shift_f = vectors[0], vectors[1], vectors[2]
    outer_bias, final_gain_f, final_shift_f = vectors[3], vectors[4], vectors[5]
    late_query, late_pair = tie(query_b, attn_pair_a)
    mixed_b, lse_b, attn_own_b, attn_other_b = run_more(
        lengths, core_arg, (late_query, key_b, value_tb, output_proj), (2, 3)
    )
    attn_pair_b = pair(attn_own_b, marker.core_swap(attn_other_b))
    attn_far_b = far_swap(attn_pair_b)
    attn_far_a, attn_pair_b = tie(attn_far_a, attn_pair_b)
    hidden_a, normed_one_a, rscale_one_a = first_norm(0, late_pair, attn_far_a)
    own_hidden_a = hidden_a.astype(BF16)
    hidden_ab, act_a, slope_a = feed_forward(own_hidden_a)
    ffn_own_a, ffn_other_a = own_and_other(act_a, outer_proj)
    ffn_pair_a = pair(ffn_own_a, marker.core_swap(ffn_other_a))
    attn_far_b, ffn_pair_late = tie(attn_far_b, ffn_pair_a)
    ffn_far_a = far_swap(ffn_pair_a)
    hidden_b, normed_one_b, rscale_one_b = first_norm(1, attn_pair_b, attn_far_b)
    own_hidden_b = hidden_b.astype(BF16)
    hidden_bb, act_b, slope_b = feed_forward(own_hidden_b)
    ffn_own_b, ffn_other_b = own_and_other(act_b, outer_proj)
    ffn_pair_b = pair(ffn_own_b, marker.core_swap(ffn_other_b))
    ffn_pair_b, ffn_far_a = marker.fence(ffn_pair_b, ffn_far_a)
    final_a, normed_two_a, rscale_two_a = last_norm(hidden_a, ffn_pair_late, ffn_far_a)
    pooled_a = jnp.dot(members[0], final_a, precision=HIGHEST)
    final_b, normed_two_b, rscale_two_b = last_norm(hidden_b, ffn_pair_b, far_swap(ffn_pair_b))
    pooled_part = pooled_a + jnp.dot(members[1], final_b, precision=HIGHEST)
    lse = (lse_a, lse_b)
    hidden_whole, act, slope = (hidden_ab, hidden_bb), (act_a, act_b), (slope_a, slope_b)
    normed_one, rscale_one = (normed_one_a, normed_one_b), (rscale_one_a, rscale_one_b)
    normed_two, rscale_two = (normed_two_a, normed_two_b), (rscale_two_a, rscale_two_b)
    pooled = pooled_part + marker.core_swap(pooled_part)
    pool_rscale = lax.rsqrt(jnp.sum(pooled * pooled, axis=-1, keepdims=True) + EPS_NORM)
    unit_b = (pooled * pool_rscale).astype(BF16)

    piece = lax.dynamic_slice_in_dim(unit_b, core * pair_count, pair_count, 0)
    piece = share(piece, None).reshape(overall_pair_count, width)
    place_arg = jnp.stack([core, my_index]).astype(jnp.int32)
    *grads, last_sums, loss = run_loss(
        lengths,
        place_arg,
        (
            piece,
            marker.core_swap(piece),
            pooled,
            pair_index,
            final_gain,
            normed_two[0],
            rscale_two[0],
            normed_two[1],
            rscale_two[1],
        ),
    )
    grad_second, own_grad = grads[:2], grads[2:]

    inner_sums, grad_up = [], []
    grad_ffn = [marker.both(values) for values in own_grad]

    def feed_back(index, grad):
        grad_up.append((nt(grad, outer_proj) * slope[index].astype(F32)).astype(BF16))
        inner_sums.append(jnp.sum(grad_up[index].astype(F32), axis=0))
        other = nt(grad_up[index][half:], inner_proj).astype(BF16)
        arrived = marker.core_swap(other)
        return pair(nt(grad_up[index][:half], inner_proj), arrived)

    def weight_grad(left, right):
        total = tn(left[0], right[0]) + tn(left[1], right[1])
        return total.astype(BF16).reshape(16, -1, width)

    hidden_pair_a = feed_back(0, grad_ffn[0])
    hidden_far_a = far_swap(hidden_pair_a)
    late_act, hidden_pair_a = tie(act, hidden_pair_a)
    outer_pack, late_grad = marker.fence(weight_grad(late_act, grad_ffn), grad_ffn[1])
    outer_parts = trade(outer_pack)
    hidden_pair_b = feed_back(1, late_grad)
    hidden_far_b = far_swap(hidden_pair_b)
    late_hidden, hidden_pair_b = tie(hidden_whole, hidden_pair_b)
    inner_pack = weight_grad(late_hidden, grad_up)
    inner_pack, (hidden_far_a, hidden_far_b) = marker.fence(
        inner_pack, (hidden_far_a, hidden_far_b)
    )
    hidden_pair, hidden_far = (hidden_pair_a, hidden_pair_b), (hidden_far_a, hidden_far_b)
    inner_parts = trade(inner_pack)

    *grads, sums = run_norm(
        (
            attn_gain,
            last_sums,
            grad_second[0],
            hidden_pair[0],
            hidden_far[0],
            normed_one[0],
            rscale_one[0],
            grad_second[1],
            hidden_pair[1],
            hidden_far[1],
            normed_one[1],
            rscale_one[1],
        )
    )
    grad_first, own_grad = grads[:2], grads[2:]
    arrived = [lax.ppermute(values, "mp", CORE_SWAP) for values in (*own_grad, sums)]
    (*other_grad, other_sums), outer_parts = tie(arrived, outer_parts)
    grad_query, grad_key, grad_value, packed = run_back(
        lengths,
        core_arg,
        (
            own_grad[0],
            other_grad[0],
            own_grad[1],
            other_grad[1],
            mixed_a,
            mixed_b,
            *lse,
            output_proj,
            query_b,
            key_b,
            value_b,
            key_tb,
            sums,
            other_sums,
            *inner_sums,
            rows,
        ),
        marker.state,
    )
    marker = Marker()

    def input_part(first):
        span = slice(first, first + half)
        return (
            nt(grad_query[span], query_proj)
            + nt(grad_key[span], key_proj)
            + nt(grad_value[span], value_proj)
        )

    token_pair = []
    for i in range(2):
        other = input_part(i * chunk + half).astype(BF16)
        token_pair.append(pair(input_part(i * chunk), marker.core_swap(other)))
    token_pair, (packed, inner_parts) = marker.fence(token_pair, (packed, inner_parts))
    packed_parts = trade(packed)
    ffn_total = jnp.concatenate([plane_sum(outer_parts), plane_sum(inner_parts)], axis=0)
    ffn_near = lax.ppermute(ffn_total, "dp", NEAR_SWAP)
    ffn_reduced = (ffn_total.astype(F32) + ffn_near.astype(F32)).astype(BF16)
    ffn_reduced, token_pair = tie(ffn_reduced, token_pair)
    token_pair, packed_parts = marker.fence(token_pair, packed_parts)
    token_far = [far_swap(token_pair[i]) for i in range(2)]
    packed_reduced = marker.near_sum(plane_sum(packed_parts))
    piece_rows = width // 16
    places = jnp.stack([my_index // 8, (my_index // 2) % 4]).astype(jnp.int32)
    halves = [
        jnp.concatenate([ffn_reduced[:piece_rows], packed_reduced[: piece_rows // 3]], axis=0),
        jnp.concatenate([ffn_reduced[piece_rows:], packed_reduced[piece_rows // 3 :]], axis=0),
    ]
    one_ring = share(halves[0], Y_RINGS)
    pieces = ring_pieces(halves[1], "z")
    halves, (one_ring, pieces) = marker.fence(halves, (one_ring, pieces))
    other_ring = run_join(places, (halves[1], *pieces))
    pieces = ring_pieces(other_ring, "y")
    other_ring, one_ring = marker.fence(other_ring, one_ring)
    one_ring, token_far = marker.fence(one_ring, token_far)
    gathered = share(one_ring, Z_RINGS)
    token_own = [
        (grad_first[i] + (token_pair[i].astype(F32) + token_far[i].astype(F32))).astype(BF16)
        for i in range(2)
    ]
    token_other = [lax.ppermute(rows_here, "mp", CORE_SWAP) for rows_here in token_own]
    token_grad = run_settle(core_arg, (*token_own, *token_other))
    gathered, token_grad = tie(gathered, token_grad)
    closing = finish(marker.state)[0, 0]
    outer_grad, inner_grad, *rest = run_spread(
        places, gathered, (other_ring, *pieces), piece_rows
    )
    cuts = [values.reshape(local_width, width) for values in rest[:4]]
    vectors = rest[4:]
    return (
        loss[0, 0] + closing,
        token_grad,
        cuts[1].T,
        vectors[7],
        cuts[2].T,
        cuts[3].T,
        vectors[8],
        cuts[0],
        vectors[0],
        vectors[1],
        vectors[2],
        inner_grad.reshape(width, width),
        vectors[6],
        outer_grad.reshape(width, width),
        vectors[3],
        vectors[4],
        vectors[5],
    )


def solution(mesh):
    column, row, split = P(None, "mp"), P("mp", None), P("mp")
    placed = (
        (P("dp", None), P("dp"), P())
        + (column, split, column, column, split, row)
        + (P(), P(), P())
        + (column, split, row)
        + (P(), P(), P())
    )
    given = (
        (P(), P("dp", None))
        + (column, split, column, column, split, row)
        + (P(), P(), P())
        + (column, split, row)
        + (P(), P(), P())
    )
    return jax.shard_map(local, mesh=mesh, in_specs=placed, out_specs=given, check_vma=False)
```

```python
import functools
import math

import jax
import jax.numpy as jnp
from jax import lax
from jax.experimental import pallas as pl
from jax.experimental.pallas import tpu as pltpu
from jax.sharding import PartitionSpec as P

HD = 64
EPS_NORM = 1e-06
SOFTMAX_WARMTH = 0.01
NEG_FILL = -1e30
HIGHEST = lax.Precision.HIGHEST
F32 = jnp.float32
BF16 = jnp.bfloat16
QB = 256
KB = 256

CORE_SWAP = [(i, i ^ 1) for i in range(4)]
FAR_SWAP = [(i, i ^ 2) for i in range(4)]
NEAR_SWAP = [(i, i ^ 1) for i in range(32)]
PLANES = [[i * 2 + x for i in range(16)] for x in range(2)]
Z_RINGS = [[i + 8 * z for z in range(4)] for i in range(8)]

SMEM = pl.BlockSpec(memory_space=pltpu.SMEM)
VMEM = pl.BlockSpec(memory_space=pltpu.VMEM)
HBM = pl.BlockSpec(memory_space=pltpu.HBM)


def nn(left, right):
    return lax.dot_general(left, right, (((1,), (0,)), ((), ())), preferred_element_type=F32)


def nt(left, right):
    return lax.dot_general(left, right, (((1,), (1,)), ((), ())), preferred_element_type=F32)


def tn(left, right):
    return lax.dot_general(left, right, (((0,), (0,)), ((), ())), preferred_element_type=F32)


def place_of_block(block, core, rows):
    return ((block % 2) * 2 + block // 2) * QB + core * (rows // 2) & (rows - 1)


def spot_of_keys(j, core, rows):
    place = (j * KB + core * (rows // 2)) & (rows - 1)
    block = place // QB
    return pl.multiple_of(((block % 2) * 2 + block // 2) * QB + place % QB, KB)


def segment_bounds(lengths_ref):
    bounds, total = [], jnp.int32(0)
    for s in range(lengths_ref.shape[0]):
        start = total
        total = total + lengths_ref[s]
        bounds.append((start, total))
    return bounds


def block_span(bounds, first, rows):
    place = first + lax.broadcasted_iota(jnp.int32, (1, QB), 1)
    low, high = first, first + KB
    begin = jnp.full((1, QB), bounds[-1][1], jnp.int32)
    end = jnp.full((1, QB), rows, jnp.int32)
    for start, stop in bounds:
        inside = (place >= start) & (place < stop)
        begin = jnp.where(inside, start, begin)
        end = jnp.where(inside, stop, end)
        touches = (stop > first) & (start < first + QB) & (stop > start)
        low = jnp.where(touches, jnp.minimum(low, start), low)
        high = jnp.where(touches, jnp.maximum(high, stop), high)
    return low // KB, (high + KB - 1) // KB, begin, end


def head_copies(values, heads):
    lane = lax.broadcasted_iota(jnp.int32, values.shape, 1) // HD
    blank = jnp.zeros_like(values)
    return jnp.concatenate([jnp.where(lane == h, values, blank) for h in range(heads)], axis=0)


def span_mask(begin, end, block, heads):
    place = block * KB + lax.broadcasted_iota(jnp.int32, (KB, QB), 0)
    keep = (place >= begin) & (place < end)
    return jnp.concatenate([keep] * heads, axis=1)


def attend(heads, blocks, core, bounds, q_ref, k_ref, vt_ref, mixed_ref, lse_ref, acc_ref):
    rows = k_ref.shape[0]
    for i, block in enumerate(blocks):
        low, high, begin, end = block_span(bounds, place_of_block(block, core, rows), rows)
        stack = head_copies(q_ref[block * QB : (block + 1) * QB, :], heads)
        acc_ref[...] = jnp.zeros(acc_ref.shape, F32)

        def step(j, carry, stack=stack, begin=begin, end=end):
            top, total = carry
            spot = spot_of_keys(j, core, rows)
            scores = nt(k_ref[pl.ds(spot, KB), :], stack)
            scores = jnp.where(span_mask(begin, end, j, heads), scores, NEG_FILL)
            peak = jnp.maximum(top, jnp.max(scores, axis=0, keepdims=True))
            fade = jnp.exp(top - peak)
            probs = jnp.exp(scores - peak)
            total = total * fade + jnp.sum(probs, axis=0, keepdims=True)
            probs = probs.astype(BF16)
            for h in range(heads):
                part = slice(h * QB, (h + 1) * QB)
                span = slice(h * HD, (h + 1) * HD)
                acc_ref[span, :] = acc_ref[span, :] * fade[:, part] + nn(
                    vt_ref[span, pl.ds(spot, KB)], probs[:, part]
                )
            return peak, total

        top = jnp.full((1, heads * QB), NEG_FILL, F32)
        top, total = lax.fori_loop(
            low, high, step, (top, jnp.zeros((1, heads * QB), F32)), unroll=False
        )
        scale = 1.0 / total
        mixed = jnp.concatenate(
            [
                acc_ref[h * HD : (h + 1) * HD, :] * scale[:, h * QB : (h + 1) * QB]
                for h in range(heads)
            ],
            axis=0,
        )
        mixed_ref[i * QB : (i + 1) * QB, :] = mixed.T.astype(BF16)
        lse_ref[i, :, :] = jnp.broadcast_to(top + jnp.log(total), (8, heads * QB))


def fetch(sources, targets, semaphores, order=()):
    copies = [
        pltpu.make_async_copy(source, target, semaphores.at[i])
        for i, (source, target) in enumerate(zip(sources, targets))
    ]
    for i in [*order, *(i for i in range(len(copies)) if i not in order)]:
        copies[i].start()
    return copies


def project(mixed_ref, weights_ref, results, outputs, semaphores):
    results[1][...] = nn(mixed_ref[QB:, :], weights_ref[...]).astype(BF16)
    copies = send_out(results, outputs, semaphores, (1,))
    results[0][...] = nn(mixed_ref[:QB, :], weights_ref[...])
    return copies + send_out(results, outputs, semaphores, (0,))


def attend_first(heads, blocks, lengths_ref, core_ref, *refs):
    sources, outputs, refs = refs[:13], refs[13:25], refs[25:]
    results, targets, refs = refs[:12], refs[12:24], refs[24:]
    acc_ref, semaphores, out_semaphores = refs
    x_ref, q_ref, k_ref, v_ref, kt_ref, vt_ref, mixed_ref, lse_ref = results[:8]
    wqt_ref, wkt_ref, wvt_ref, bq_ref, bv_ref, wo_ref = targets[:6]
    rows = x_ref.shape[0]
    core = core_ref[0]
    copies = fetch(sources[1:], targets, semaphores)
    row_copies = []
    for block in range(rows // QB):
        first = pl.multiple_of(place_of_block(block, core, rows), QB)
        row_copies.append(
            pltpu.make_async_copy(
                sources[0].at[pl.ds(first, QB), :],
                x_ref.at[pl.ds(block * QB, QB), :],
                semaphores.at[12 + block],
            )
        )
        row_copies[-1].start()
    for copy in copies:
        copy.wait()
    query_bias, value_bias = row_of(bq_ref), row_of(bv_ref)
    for block in range(rows // QB):
        row_copies[block].wait()
        part = slice(block * QB, (block + 1) * QB)
        x = x_ref[part, :]
        q = (nt(x, wqt_ref[...]) + query_bias).astype(BF16)
        q_ref[part, :] = q * BF16(0.125)
        k_ref[part, :] = nt(x, wkt_ref[...]).astype(BF16)
        kt_ref[:, part] = nt(wkt_ref[...], x).astype(BF16)
        v = nt(x, wvt_ref[...]) + value_bias
        v_ref[part, :] = v.astype(BF16)
        vt_ref[:, part] = v.T.astype(BF16)
    outgoing = send_out(results, outputs, out_semaphores, range(6))
    bounds = segment_bounds(lengths_ref)
    place = core * (2 * QB) + lax.broadcasted_iota(jnp.int32, (1, QB), 1)
    for i in range(2):
        member = [
            jnp.where((place + i * QB >= start) & (place + i * QB < stop), 1.0, 0.0)
            for start, stop in bounds
        ]
        results[10][i] = jnp.concatenate(member, axis=0)
    lines = [row_of(ref) for ref in targets[6:]]
    results[11][...] = jnp.concatenate(lines + [jnp.zeros((2, lines[0].shape[1]), F32)], axis=0)
    outgoing += send_out(results, outputs, out_semaphores, (10, 11))
    attend(heads, blocks, core, bounds, q_ref, k_ref, vt_ref, mixed_ref, lse_ref, acc_ref)
    outgoing += project(mixed_ref, wo_ref, results[8:], outputs[8:], out_semaphores.at[8:10])
    outgoing += send_out(results, outputs, out_semaphores, (6, 7))
    for copy in outgoing:
        copy.wait()


def attend_more(heads, blocks, lengths_ref, core_ref, *refs):
    sources, outputs, refs = refs[:4], refs[4:8], refs[8:]
    targets, results, refs = refs[:4], refs[4:8], refs[8:]
    acc_ref, semaphores, out_semaphores = refs
    q_ref, k_ref, vt_ref, wo_ref = targets
    mixed_ref, lse_ref = results[:2]
    for copy in fetch(sources, targets, semaphores):
        copy.wait()
    bounds = segment_bounds(lengths_ref)
    attend(heads, blocks, core_ref[0], bounds, q_ref, k_ref, vt_ref, mixed_ref, lse_ref, acc_ref)
    outgoing = project(mixed_ref, wo_ref, results[2:], outputs[2:], out_semaphores.at[2:])
    outgoing += send_out(results, outputs, out_semaphores, (0, 1))
    for copy in outgoing:
        copy.wait()


def attend_back(heads, inputs, lengths_ref, core_ref, *refs):
    sources, refs = refs[:inputs], refs[inputs + 1 :]
    outputs, refs = refs[:4], refs[4:]
    gq_ref, gk_ref, gv_ref, pack_ref = refs[:4]
    dk_ref, dv_ref, dqt_ref, wo_acc_ref, semaphores, out_semaphores = refs[4:10]
    targets = refs[10:]
    copies = fetch(sources, targets, semaphores, (10, 9, 11, 12, 0, 4, 8, 6, 1, 2, 3, 5, 7))
    grads = targets[0:4]
    mixed = targets[4:6]
    lses = targets[6:8]
    wo_ref, q_ref, k_ref, v_ref, kt_ref = targets[8:13]
    own_sums, other_sums, inner_a, inner_b, x_ref = targets[13:]
    rows, width = q_ref.shape
    core = core_ref[0]
    bounds = segment_bounds(lengths_ref)
    dk_ref[...] = jnp.zeros(dk_ref.shape, F32)
    dv_ref[...] = jnp.zeros(dv_ref.shape, F32)
    lane = lax.broadcasted_iota(jnp.int32, (8, width), 1) // HD
    which = (lane == lax.broadcasted_iota(jnp.int32, (8, width), 0)).astype(F32).astype(BF16)
    for i in (0, 4, 6, 8, 9, 10, 11, 12):
        copies[i].wait()
    for block in range(rows // QB):
        if block > 0:
            copies[block].wait()
        if block == 2:
            copies[5].wait()
            copies[7].wait()
        low, high, begin, end = block_span(bounds, place_of_block(block, core, rows), rows)
        part = slice(block * QB, (block + 1) * QB)
        own = slice(block % 2 * QB, block % 2 * QB + QB)
        grad_attn = grads[block][...]
        mixed_here = mixed[block // 2][own, :]
        outer = tn(mixed_here, grad_attn)
        wo_acc_ref[...] = outer if block == 0 else wo_acc_ref[...] + outer
        grad_mixed = nt(grad_attn, wo_ref[...]).astype(BF16)
        product = grad_mixed.astype(F32) * mixed_here.astype(F32)
        sums = sum(nt(which, part) for part in in_three(product)[:2])
        delta = jnp.concatenate([sums[h : h + 1, :] for h in range(heads)], axis=1)
        lse = lses[block // 2][block % 2, 0:1, :]
        q_stack = head_copies(q_ref[part, :], heads)
        g_stack = head_copies(grad_mixed, heads)
        dqt_ref[...] = jnp.zeros(dqt_ref.shape, F32)

        def step(
            j, carry, delta=delta, lse=lse, q_stack=q_stack, g_stack=g_stack, begin=begin, end=end
        ):
            here = pl.ds(spot_of_keys(j, core, rows), KB)
            scores = nt(k_ref[here, :], q_stack)
            scores = jnp.where(span_mask(begin, end, j, heads), scores, NEG_FILL)
            probs = jnp.exp(scores - lse)
            grad = (probs * (nt(v_ref[here, :], g_stack) - delta)).astype(BF16)
            dv_ref[here, :] += nn(probs.astype(BF16), g_stack)
            dk_ref[here, :] += nn(grad, q_stack)
            for h in range(heads):
                span = slice(h * HD, (h + 1) * HD)
                dqt_ref[span, :] += nn(kt_ref[span, here], grad[:, h * QB : (h + 1) * QB])
            return carry

        lax.fori_loop(low, high, step, 0, unroll=False)
        gq_ref[part, :] = (dqt_ref[...].T * 0.125).astype(BF16)
    gk_ref[...] = dk_ref[...].astype(BF16)
    gv_ref[...] = dv_ref[...].astype(BF16)
    for copy in copies[13:]:
        copy.wait()
    outgoing = fetch(refs[:3], outputs[:3], out_semaphores)
    sums = [jnp.sum(ref[...].astype(F32), axis=0, keepdims=True) for ref in (gq_ref, gv_ref)]
    blank = jnp.zeros((1, 256 - width), F32)
    tail = jnp.concatenate([sums[0], blank, sums[1], blank, jnp.zeros((1, 256), F32)], axis=1)
    inner = row_of(inner_a) + row_of(inner_b)
    paired = own_sums[0:6, :] + other_sums[0:6, :]
    small = [paired, inner, tail, jnp.zeros((8, tail.shape[1]), F32)]
    small = jnp.concatenate(small, axis=0).astype(BF16)
    piece = pack_ref.shape[1] - 16
    per = width // piece
    for m, source in enumerate((None, gq_ref, gk_ref, gv_ref)):
        total = wo_acc_ref[...] if source is None else tn(source[...], x_ref[...])
        for t in range(per):
            cut = total[t * piece : (t + 1) * piece, :].astype(BF16)
            pack_ref[m * per + t, 0:piece, :] = cut
            pack_ref[m * per + t, piece:, :] = small if m + t == 0 else jnp.zeros_like(small)
        here = pl.ds(m * per, per)
        copy = pltpu.make_async_copy(
            pack_ref.at[here], outputs[3].at[here], out_semaphores.at[3 + m]
        )
        copy.start()
        outgoing.append(copy)
    for copy in outgoing:
        copy.wait()


def shaped(shape, dtype):
    return jax.ShapeDtypeStruct(shape, dtype)


PARAMS = pltpu.CompilerParams(vmem_limit_bytes=60 << 20)
SMALL = pltpu.CompilerParams(vmem_limit_bytes=60 << 20)
COST = pl.CostEstimate(flops=1024, bytes_accessed=1024, transcendentals=0)


def buffers(arrays):
    return [pltpu.VMEM(array.shape, array.dtype) for array in arrays]


def attend_shapes(count, heads, width):
    rows = count * QB
    return (
        shaped((rows, heads * HD), BF16),
        shaped((count, 8, heads * QB), F32),
        shaped((rows // 2, width), F32),
        shaped((rows // 2, width), BF16),
    )


def run_first(lengths, core, tokens, weights, blocks):
    rows, width = tokens.shape
    local_width = weights[0].shape[0]
    heads = local_width // HD
    outs = (
        (shaped(tokens.shape, BF16),)
        + (shaped((rows, local_width), BF16),) * 3
        + (shaped((local_width, rows), BF16),) * 2
        + attend_shapes(len(blocks), heads, width)
        + (shaped((2, lengths.shape[0], QB), F32), shaped((8, width), F32))
    )
    return pl.pallas_call(
        functools.partial(attend_first, heads, blocks),
        out_shape=outs,
        in_specs=[SMEM] * 2 + [HBM] * 13,
        out_specs=(HBM,) * 12,
        scratch_shapes=buffers(outs)
        + buffers(weights)
        + [pltpu.VMEM((local_width, QB), F32)]
        + [pltpu.SemaphoreType.DMA((12 + rows // QB,)), pltpu.SemaphoreType.DMA((12,))],
        compiler_params=PARAMS,
        name="attend_first",
        cost_estimate=COST,
    )(lengths, core, tokens, *weights)


def run_more(lengths, core, arrays, blocks):
    rows, local_width = arrays[0].shape
    heads = local_width // HD
    outs = attend_shapes(len(blocks), heads, arrays[3].shape[1])
    return pl.pallas_call(
        functools.partial(attend_more, heads, blocks),
        out_shape=outs,
        in_specs=[SMEM] * 2 + [HBM] * 4,
        out_specs=(HBM,) * 4,
        scratch_shapes=buffers(arrays)
        + buffers(outs)
        + [pltpu.VMEM((local_width, QB), F32)]
        + [pltpu.SemaphoreType.DMA((4,)), pltpu.SemaphoreType.DMA((4,))],
        compiler_params=PARAMS,
        name="attend_more",
        cost_estimate=COST,
    )(lengths, core, *arrays)


def run_back(lengths, core, arrays, marker):
    wo, q, x = arrays[8], arrays[9], arrays[-1]
    rows, width = q.shape
    heads = width // HD
    piece = 4 * width // 16
    outs = (shaped((rows, width), BF16),) * 3 + (shaped((16, piece + 16, x.shape[1]), BF16),)
    return pl.pallas_call(
        functools.partial(attend_back, heads, len(arrays)),
        out_shape=outs,
        in_specs=[SMEM] * 2 + [HBM] * (len(arrays) + 1),
        out_specs=(HBM,) * 4,
        scratch_shapes=buffers(outs)
        + [pltpu.VMEM((rows, width), F32)] * 2
        + [pltpu.VMEM((width, QB), F32), pltpu.VMEM(wo.shape, F32)]
        + [pltpu.SemaphoreType.DMA((len(arrays),)), pltpu.SemaphoreType.DMA((7,))]
        + buffers(arrays),
        compiler_params=PARAMS,
        name="attend_back",
        cost_estimate=COST,
    )(lengths, core, *arrays, marker)


def mark_kernel(source_ref, target_ref):
    del source_ref, target_ref


def mark(values):
    return pl.pallas_call(
        mark_kernel,
        out_shape=shaped(values.shape, values.dtype),
        in_specs=[HBM],
        out_specs=HBM,
        compiler_params=pltpu.CompilerParams(vmem_limit_bytes=1 << 20),
        name="mark",
        cost_estimate=pl.CostEstimate(flops=1 << 36, bytes_accessed=1 << 10, transcendentals=0),
    )(values)


def finish_kernel(source_ref, target_ref):
    del source_ref
    target_ref[...] = jnp.zeros(target_ref.shape, F32)


def finish(values):
    return pl.pallas_call(
        finish_kernel,
        out_shape=shaped(values.shape, values.dtype),
        in_specs=[HBM],
        out_specs=VMEM,
        compiler_params=pltpu.CompilerParams(vmem_limit_bytes=1 << 20),
        name="finish",
        cost_estimate=COST,
    )(values)


def row_of(ref):
    return ref[...].astype(F32).reshape(1, -1)


def in_three(values):
    high = values.astype(BF16)
    rest = values - high.astype(F32)
    middle = rest.astype(BF16)
    return high, middle, (rest - middle.astype(F32)).astype(BF16)


def norm_step(grad, normed, rscale, gain):
    scaled = grad * gain
    first_mean = jnp.mean(scaled, axis=1, keepdims=True)
    cross_mean = jnp.mean(scaled * normed, axis=1, keepdims=True)
    return rscale * (scaled - first_mean - normed * cross_mean)


def column_of(ref):
    row = ref[...].reshape(1, -1)
    return jnp.broadcast_to(row, (128, row.shape[1])).T[:, 0:1]


def column_sum(values):
    return jnp.sum(values, axis=0, keepdims=True)


def send_out(results, outputs, semaphores, which):
    copies = [
        pltpu.make_async_copy(results[k], outputs[k], semaphores.at[k]) for k in which
    ]
    for copy in copies:
        copy.start()
    return copies


def loss_back(lengths_ref, place_ref, *refs):
    sources, outputs, refs = refs[:9], refs[9:15], refs[15:]
    targets, results = refs[:9], refs[9:15]
    coef_ref, turned_ref, semaphores, out_semaphores = refs[15:]
    copies = fetch(sources, targets, semaphores)
    piece_ref, swapped_ref, pooled_ref, match_ref, gain_ref = targets[:5]
    core, index = place_ref[0], place_ref[1]
    bounds = segment_bounds(lengths_ref)
    for copy in copies[:5]:
        copy.wait()
    first = core == 0
    queries = jnp.where(first, piece_ref[...], swapped_ref[...])
    passages = jnp.where(first, swapped_ref[...], piece_ref[...])
    count = queries.shape[0]
    own = pooled_ref.shape[0] // 2
    similarity = nt(queries, passages) / SOFTMAX_WARMTH
    match = match_ref[...].reshape(1, -1)
    match = match == lax.broadcasted_iota(jnp.int32, (count, count), 0)
    top = jnp.max(similarity, axis=1, keepdims=True)
    lse = top + jnp.log(jnp.sum(jnp.exp(similarity - top), axis=1, keepdims=True))
    positive = jnp.sum(jnp.where(match, similarity, 0.0), axis=1, keepdims=True)
    loss = jnp.sum(lse - positive, axis=0, keepdims=True) / count
    results[5][...] = jnp.broadcast_to(loss, results[5].shape)
    coef = (jnp.exp(similarity - lse) - match.astype(F32)) * (1.0 / (count * SOFTMAX_WARMTH))
    coef_ref[...] = coef
    turned_ref[...] = coef.T
    here = pl.ds(pl.multiple_of(index * own, own), own)
    grad_query = sum(nn(part, passages) for part in in_three(coef_ref[here, :]))
    grad_passage = sum(nn(part, queries) for part in in_three(turned_ref[here, :]))
    grad_unit = jnp.concatenate([grad_query, grad_passage], axis=0)
    pooled = pooled_ref[...]
    rscale = lax.rsqrt(jnp.sum(pooled * pooled, axis=1, keepdims=True) + EPS_NORM)
    inner = jnp.sum(pooled * grad_unit, axis=1, keepdims=True)
    grad_pooled = rscale * grad_unit - rscale * rscale * rscale * inner * pooled
    seqs = 2 * own
    grad_pooled = jnp.concatenate(
        [grad_pooled, jnp.zeros((128 - seqs, grad_pooled.shape[1]), F32)], axis=0
    )
    parts = in_three(grad_pooled)
    lane = lax.broadcasted_iota(jnp.int32, (1, 128), 1)
    begin = end = jnp.zeros((1, 128), jnp.int32)
    for seq, (start, stop) in enumerate(bounds):
        begin = jnp.where(lane == seq, start, begin)
        end = jnp.where(lane == seq, stop, end)
    gain = row_of(gain_ref)
    sums = [0.0, 0.0, 0.0]
    outgoing = []
    for i in range(2):
        copies[5 + 2 * i].wait()
        copies[6 + 2 * i].wait()
        normed = targets[5 + 2 * i][...]
        place = core * (2 * QB) + i * QB + lax.broadcasted_iota(jnp.int32, (QB, 128), 0)
        member = jnp.where((place >= begin) & (place < end), 1.0, 0.0).astype(BF16)
        grad = sum(nn(member, part) for part in parts)
        second = norm_step(grad, normed, column_of(targets[6 + 2 * i]), gain)
        rounded = second.astype(BF16)
        results[i][...] = second
        results[2 + i][...] = rounded
        for k, values in enumerate((rounded.astype(F32), grad * normed, grad)):
            sums[k] = sums[k] + column_sum(values)
        outgoing += send_out(results, outputs, out_semaphores, (2 + i, i))
    results[4][...] = jnp.concatenate(sums + [jnp.zeros((5, sums[0].shape[1]), F32)], axis=0)
    outgoing += send_out(results, outputs, out_semaphores, (4, 5))
    for copy in outgoing:
        copy.wait()


def norm_back(*refs):
    sources, outputs, refs = refs[:12], refs[12:17], refs[17:]
    targets, results = refs[:12], refs[12:17]
    semaphores, out_semaphores = refs[17:]
    copies = fetch(sources, targets, semaphores)
    copies[0].wait()
    copies[1].wait()
    gain = row_of(targets[0])
    sums = [0.0, 0.0, 0.0]
    outgoing = []
    for i in range(2):
        for copy in copies[2 + 5 * i : 7 + 5 * i]:
            copy.wait()
        second, pair_here, far, normed, rscale = targets[2 + 5 * i : 7 + 5 * i]
        grad = second[...] + (pair_here[...].astype(F32) + far[...].astype(F32))
        normed = normed[...]
        first = norm_step(grad, normed, column_of(rscale), gain)
        rounded = first.astype(BF16)
        results[i][...] = first
        results[2 + i][...] = rounded
        for k, values in enumerate((rounded.astype(F32), grad * normed, grad)):
            sums[k] = sums[k] + column_sum(values)
        outgoing += send_out(results, outputs, out_semaphores, (2 + i, i))
    blank = jnp.zeros((2, sums[0].shape[1]), F32)
    results[4][...] = jnp.concatenate(sums + [targets[1][0:3, :], blank], axis=0)
    outgoing += send_out(results, outputs, out_semaphores, (4,))
    for copy in outgoing:
        copy.wait()


STEPS = (0, 2, 1, 3)


def join(copies_of_each, place_ref, *refs):
    sources, output, semaphores = refs[:4], refs[4], refs[5]
    copies = []
    for k in range(4):
        spot = (place_ref[0] + 4 - STEPS[k]) % 4
        for r in range(copies_of_each):
            goal = output.at[spot] if copies_of_each == 1 else output.at[r, spot]
            semaphore = semaphores.at[k * copies_of_each + r]
            copies.append(pltpu.make_async_copy(sources[k], goal, semaphore))
            copies[-1].start()
    for copy in copies:
        copy.wait()


def place_block(piece, part, block_ref, spot, outputs, buffers_, semaphores, first):
    inner, cuts = buffers_
    inner[...] = block_ref[:, :piece, :].astype(F32)
    cuts[...] = block_ref[:, piece : 2 * piece - part, :].astype(F32)
    copies = [pltpu.make_async_copy(inner, outputs[0].at[:, spot], semaphores.at[first])]
    for m in range(4):
        goal = outputs[1 + m].at[spot, pl.ds(part, piece - part), :]
        copies.append(pltpu.make_async_copy(cuts.at[m], goal, semaphores.at[first + 1 + m]))
    for copy in copies:
        copy.start()
    return copies


def place_vectors(piece, part, block_ref, spot, outputs, vectors, semaphores, first):
    @pl.when(spot == 0)
    def _():
        small = block_ref[0, 2 * piece - part :, :].astype(F32)
        for k in range(7):
            vectors[k][...] = small[k : k + 1, :].reshape(-1)
        count = vectors[7].shape[0]
        for k in range(2):
            vectors[7 + k][...] = small[7:8, 256 * k : 256 * k + count].reshape(-1)
        copies = [
            pltpu.make_async_copy(vectors[k], outputs[5 + k], semaphores.at[first + k])
            for k in range(9)
        ]
        for copy in copies:
            copy.start()
        for copy in copies:
            copy.wait()


def spread_some(piece, part, count, place_ref, *refs):
    sources, outputs, refs = refs[:count], refs[count : count + 14], refs[count + 14 :]
    blocks, refs = refs[:count], refs[count:]
    buffers_, vectors, refs = refs[: 2 * count], refs[2 * count : 2 * count + 9], refs[-2:]
    arrivals = fetch(sources, blocks, refs[0])
    outgoing, spots = [], []
    for k in range(count):
        arrivals[k].wait()
        spots.append((place_ref[1] + 4 - STEPS[k]) % 4)
        outgoing += place_block(
            piece, part, blocks[k], spots[k], outputs, buffers_[2 * k : 2 * k + 2], refs[1], 5 * k
        )
    for k in range(count):
        place_vectors(piece, part, blocks[k], spots[k], outputs, vectors, refs[1], 5 * count)
    for copy in outgoing:
        copy.wait()


def spread_rest(piece, part, place_ref, *refs):
    sources, outputs, refs = refs[:2], refs[16:31], refs[31:]
    block, by_z, refs = refs[0], refs[1], refs[2:]
    buffers_, outer, heads, vectors, refs = refs[:2], refs[2], refs[3], refs[4:13], refs[13:]
    semaphores, out_semaphores = refs
    arrivals = fetch(sources, (block, by_z), semaphores)
    spot = (place_ref[1] + 4 - STEPS[3]) % 4
    arrivals[0].wait()
    outgoing = place_block(piece, part, block, spot, outputs, buffers_, out_semaphores, 0)
    arrivals[1].wait()
    outer[...] = by_z[:, :, :piece, :].astype(F32)
    copies = [pltpu.make_async_copy(outer, outputs[14], out_semaphores.at[5])]
    copies[0].start()
    heads[...] = by_z[:, :, piece:, :].astype(F32)
    for m in range(4):
        goal = outputs[1 + m].at[:, pl.ds(0, part), :]
        copies.append(pltpu.make_async_copy(heads.at[m], goal, out_semaphores.at[6 + m]))
        copies[-1].start()
    place_vectors(piece, part, block, spot, outputs, vectors, out_semaphores, 10)
    for copy in outgoing + copies:
        copy.wait()


def run_loss(lengths, place, arrays):
    rows, width = arrays[5].shape
    count = arrays[0].shape[0]
    outs = (
        (shaped((rows, width), F32),) * 2
        + (shaped((rows, width), BF16),) * 2
        + (shaped((8, width), F32), shaped((8, 128), F32))
    )
    return pl.pallas_call(
        loss_back,
        out_shape=outs,
        in_specs=[SMEM] * 2 + [HBM] * 9,
        out_specs=(HBM,) * 6,
        scratch_shapes=buffers(arrays)
        + buffers(outs)
        + [pltpu.VMEM((count, count), F32)] * 2
        + [pltpu.SemaphoreType.DMA((9,)), pltpu.SemaphoreType.DMA((6,))],
        compiler_params=SMALL,
        name="loss_back",
        cost_estimate=COST,
    )(lengths, place, *arrays)


def run_norm(arrays):
    rows, width = arrays[2].shape
    outs = (
        (shaped((rows, width), F32),) * 2
        + (shaped((rows, width), BF16),) * 2
        + (shaped((8, width), F32),)
    )
    return pl.pallas_call(
        norm_back,
        out_shape=outs,
        in_specs=[HBM] * 12,
        out_specs=(HBM,) * 5,
        scratch_shapes=buffers(arrays)
        + buffers(outs)
        + [pltpu.SemaphoreType.DMA((12,)), pltpu.SemaphoreType.DMA((5,))],
        compiler_params=SMALL,
        name="norm_back",
        cost_estimate=COST,
    )(*arrays)


def run_join(place, pieces, copies_of_each):
    lead = (4,) if copies_of_each == 1 else (copies_of_each, 4)
    return pl.pallas_call(
        functools.partial(join, copies_of_each),
        out_shape=shaped(lead + pieces[0].shape, BF16),
        in_specs=[SMEM] + [HBM] * 4,
        out_specs=HBM,
        scratch_shapes=[pltpu.SemaphoreType.DMA((4 * copies_of_each,))],
        compiler_params=pltpu.CompilerParams(vmem_limit_bytes=1 << 20),
        name="join",
        cost_estimate=COST,
    )(place, *pieces)


def settle(core_ref, *refs):
    sources, output, semaphores = refs[:4], refs[4], refs[5]
    copies = []
    for k in range(4):
        first = (k // 2 + core_ref[0]) % 2 * (2 * QB) + k % 2 * QB
        spot = pl.ds(pl.multiple_of(first, QB), QB)
        copies.append(pltpu.make_async_copy(sources[k], output.at[spot, :], semaphores.at[k]))
        copies[-1].start()
    for copy in copies:
        copy.wait()


def run_settle(core, parts):
    rows, width = parts[0].shape
    return pl.pallas_call(
        settle,
        out_shape=shaped((4 * rows, width), BF16),
        in_specs=[SMEM] + [HBM] * 4,
        out_specs=HBM,
        scratch_shapes=[pltpu.SemaphoreType.DMA((4,))],
        compiler_params=pltpu.CompilerParams(vmem_limit_bytes=1 << 20),
        name="settle",
        cost_estimate=COST,
    )(core, *parts)


def spread_shapes(piece, width):
    shapes = [(4, 4, piece, width)] + [(4, piece, width)] * 4
    return shapes + [(width,)] * 7 + [(4 * piece,)] * 2


def run_spread_some(places, blocks, piece, part):
    width = blocks[0].shape[2]
    shapes = spread_shapes(piece, width)
    count = len(blocks)
    pair_of = [pltpu.VMEM((4, piece, width), F32), pltpu.VMEM((4, piece - part, width), F32)]
    return pl.pallas_call(
        functools.partial(spread_some, piece, part, count),
        out_shape=[shaped(shape, F32) for shape in shapes],
        in_specs=[SMEM] + [HBM] * count,
        out_specs=[HBM] * 14,
        scratch_shapes=buffers(blocks)
        + pair_of * count
        + [pltpu.VMEM(shape, F32) for shape in shapes[5:]]
        + [pltpu.SemaphoreType.DMA((count,)), pltpu.SemaphoreType.DMA((5 * count + 9,))],
        compiler_params=SMALL,
        name="spread_some",
        cost_estimate=COST,
    )(places, *blocks)


def run_spread_rest(places, block, gathered, so_far, piece, part):
    width = block.shape[2]
    shapes = spread_shapes(piece, width)
    outer = (4, 4, piece, width)
    return pl.pallas_call(
        functools.partial(spread_rest, piece, part),
        out_shape=[shaped(shape, F32) for shape in shapes + [outer]],
        in_specs=[SMEM] + [HBM] * 16,
        out_specs=[HBM] * 15,
        input_output_aliases={3 + k: k for k in range(14)},
        scratch_shapes=[pltpu.VMEM(block.shape, BF16), pltpu.VMEM(gathered.shape, BF16)]
        + [pltpu.VMEM((4, piece, width), F32), pltpu.VMEM((4, piece - part, width), F32)]
        + [pltpu.VMEM(outer, F32), pltpu.VMEM((4, 4, part, width), F32)]
        + [pltpu.VMEM(shape, F32) for shape in shapes[5:]]
        + [pltpu.SemaphoreType.DMA((2,)), pltpu.SemaphoreType.DMA((19,))],
        compiler_params=SMALL,
        name="spread_rest",
        cost_estimate=COST,
    )(places, block, gathered, *so_far)


def trade(values):
    return lax.all_to_all(
        values, "dp", split_axis=0, concat_axis=0, axis_index_groups=PLANES, tiled=True
    )


def share(values):
    spread_out = jnp.broadcast_to(values[None], (32,) + values.shape)
    return lax.all_to_all(spread_out, "dp", split_axis=0, concat_axis=0, tiled=True)


def trade_z(values):
    return lax.all_to_all(
        values, "dp", split_axis=0, concat_axis=0, axis_index_groups=Z_RINGS, tiled=True
    )


def ring_shift(axis, step):
    pairs = []
    for i in range(32):
        z, y, x = i // 8, (i // 2) % 4, i % 2
        z, y = ((z + step) % 4, y) if axis == "z" else (z, (y + step) % 4)
        pairs.append((i, (z * 4 + y) * 2 + x))
    return pairs


def ring_pieces(values, axis):
    return [lax.ppermute(values, "dp", ring_shift(axis, step)) for step in STEPS[1:]]


def tie(values, others):
    return lax.optimization_barrier((values, others))


class Marker:
    def __init__(self):
        self.state = jnp.zeros((8, 128), F32)

    def fence(self, ready, later):
        ready, state = tie(ready, self.state)
        later, self.state = tie(later, mark(state))
        return ready, later

    def moved(self, values, axis, pairs):
        values, state = tie(values, self.state)
        arrived, self.state = tie(lax.ppermute(values, axis, pairs), mark(state))
        return arrived

    def core_swap(self, values):
        return self.moved(values, "mp", CORE_SWAP)

    def near_swap(self, values):
        return self.moved(values, "dp", NEAR_SWAP)

    def both(self, own):
        return jnp.concatenate([own, self.core_swap(own)], axis=0)

    def near_sum(self, total):
        return (total.astype(F32) + self.near_swap(total).astype(F32)).astype(BF16)


def plane_sum(parts):
    return jnp.sum(parts.astype(F32), axis=0).astype(BF16)


def far_swap(values):
    return lax.ppermute(values, "mp", FAR_SWAP)


def norm_forward(values, gain_vec, shift_vec):
    average = jnp.mean(values, axis=-1, keepdims=True)
    centred = values - average
    rscale = lax.rsqrt(jnp.mean(centred * centred, axis=-1, keepdims=True) + EPS_NORM)
    normed = centred * rscale
    return (normed * gain_vec + shift_vec, normed, rscale[:, 0])


def gelu_and_slope(upper):
    below = 0.5 * (1.0 + lax.erf(upper * math.sqrt(0.5)))
    density = jnp.exp(-0.5 * upper * upper) * (1.0 / math.sqrt(2.0 * math.pi))
    return (upper * below).astype(BF16), (below + upper * density).astype(BF16)


def local(
    tokens,
    lengths,
    pair_index,
    query_proj,
    query_bias,
    key_proj,
    value_proj,
    value_bias,
    output_proj,
    output_bias,
    attn_gain,
    attn_shift,
    inner_proj,
    inner_bias,
    outer_proj,
    outer_bias,
    final_gain,
    final_shift,
):
    row_count, width = tokens.shape
    chunk = row_count // 2
    half = chunk // 2
    seq_count = lengths.shape[0]
    pair_count = seq_count // 2
    overall_pair_count = pair_index.shape[0]
    local_width = query_proj.shape[1]
    core = lax.axis_index("mp") % 2
    my_index = lax.axis_index("dp")
    marker = Marker()
    core_arg = jnp.reshape(core, (1,)).astype(jnp.int32)
    vectors = (output_bias, attn_gain, attn_shift, outer_bias, final_gain, final_shift)
    query_t, key_t, value_t = query_proj.T, key_proj.T, value_proj.T

    weights = (query_t, key_t, value_t, query_bias, value_bias, output_proj, *vectors)
    first = run_first(lengths, core_arg, tokens, weights, (0, 1))
    rows, query_b, key_b, value_b, key_tb, value_tb, mixed_a, lse_a = first[:8]
    attn_own_a, attn_other_a, members, vectors = first[8:]

    def own_and_other(values, weights):
        return nn(values[:half], weights), nn(values[half:], weights).astype(BF16)

    def pair(own, arrived):
        return (own + arrived.astype(F32)).astype(BF16)

    def first_norm(index, pair_here, far):
        attn_full = pair_here.astype(F32) + far.astype(F32) + output_bias
        own_tokens = rows[index * chunk : index * chunk + half].astype(F32)
        return norm_forward(own_tokens + attn_full, attn_gain_f, attn_shift_f)

    def feed_forward(own_hidden):
        whole = marker.both(own_hidden)
        act, slope = gelu_and_slope(nn(whole, inner_proj) + inner_bias.astype(F32))
        return whole, act, slope

    def last_norm(hidden, pair_here, far):
        ffn_full = pair_here.astype(F32) + far.astype(F32) + outer_bias
        return norm_forward(hidden + ffn_full, final_gain_f, final_shift_f)

    attn_pair_a = pair(attn_own_a, marker.core_swap(attn_other_a))
    attn_far_a = far_swap(attn_pair_a)
    output_bias, attn_gain_f, attn_shift_f = vectors[0], vectors[1], vectors[2]
    outer_bias, final_gain_f, final_shift_f = vectors[3], vectors[4], vectors[5]
    late_query, late_pair = tie(query_b, attn_pair_a)
    mixed_b, lse_b, attn_own_b, attn_other_b = run_more(
        lengths, core_arg, (late_query, key_b, value_tb, output_proj), (2, 3)
    )
    attn_pair_b = pair(attn_own_b, marker.core_swap(attn_other_b))
    attn_far_b = far_swap(attn_pair_b)
    attn_far_a, attn_pair_b = tie(attn_far_a, attn_pair_b)
    hidden_a, normed_one_a, rscale_one_a = first_norm(0, late_pair, attn_far_a)
    own_hidden_a = hidden_a.astype(BF16)
    hidden_ab, act_a, slope_a = feed_forward(own_hidden_a)
    ffn_own_a, ffn_other_a = own_and_other(act_a, outer_proj)
    ffn_pair_a = pair(ffn_own_a, marker.core_swap(ffn_other_a))
    attn_far_b, ffn_pair_late = tie(attn_far_b, ffn_pair_a)
    ffn_far_a = far_swap(ffn_pair_a)
    hidden_b, normed_one_b, rscale_one_b = first_norm(1, attn_pair_b, attn_far_b)
    own_hidden_b = hidden_b.astype(BF16)
    hidden_bb, act_b, slope_b = feed_forward(own_hidden_b)
    ffn_own_b, ffn_other_b = own_and_other(act_b, outer_proj)
    ffn_pair_b = pair(ffn_own_b, marker.core_swap(ffn_other_b))
    ffn_pair_b, ffn_far_a = marker.fence(ffn_pair_b, ffn_far_a)
    final_a, normed_two_a, rscale_two_a = last_norm(hidden_a, ffn_pair_late, ffn_far_a)
    pooled_a = jnp.dot(members[0], final_a, precision=HIGHEST)
    final_b, normed_two_b, rscale_two_b = last_norm(hidden_b, ffn_pair_b, far_swap(ffn_pair_b))
    pooled_part = pooled_a + jnp.dot(members[1], final_b, precision=HIGHEST)
    lse = (lse_a, lse_b)
    hidden_whole, act, slope = (hidden_ab, hidden_bb), (act_a, act_b), (slope_a, slope_b)
    normed_one, rscale_one = (normed_one_a, normed_one_b), (rscale_one_a, rscale_one_b)
    normed_two, rscale_two = (normed_two_a, normed_two_b), (rscale_two_a, rscale_two_b)
    pooled = pooled_part + marker.core_swap(pooled_part)
    pool_rscale = lax.rsqrt(jnp.sum(pooled * pooled, axis=-1, keepdims=True) + EPS_NORM)
    unit_b = (pooled * pool_rscale).astype(BF16)

    piece = lax.dynamic_slice_in_dim(unit_b, core * pair_count, pair_count, 0)
    piece = share(piece).reshape(overall_pair_count, width)
    place_arg = jnp.stack([core, my_index]).astype(jnp.int32)
    *grads, last_sums, loss = run_loss(
        lengths,
        place_arg,
        (
            piece,
            marker.core_swap(piece),
            pooled,
            pair_index,
            final_gain,
            normed_two[0],
            rscale_two[0],
            normed_two[1],
            rscale_two[1],
        ),
    )
    grad_second, own_grad = grads[:2], grads[2:]

    inner_sums, grad_ffn, grad_up, hidden_other = [], [], [], []
    for i in range(2):
        grad_ffn.append(marker.both(own_grad[i]))
        grad_up.append((nt(grad_ffn[i], outer_proj) * slope[i].astype(F32)).astype(BF16))
        inner_sums.append(jnp.sum(grad_up[i].astype(F32), axis=0))
        other = nt(grad_up[i][half:], inner_proj).astype(BF16)
        hidden_other.append(marker.core_swap(other))
    hidden_pair = [pair(nt(grad_up[i][:half], inner_proj), hidden_other[i]) for i in range(2)]
    hidden_far = [far_swap(hidden_pair[i]) for i in range(2)]
    (late_act, late_hidden), hidden_pair = tie((act, hidden_whole), hidden_pair)
    ffn_pack = jnp.concatenate(
        [
            (tn(late_act[0], grad_ffn[0]) + tn(late_act[1], grad_ffn[1]))
            .astype(BF16)
            .reshape(16, -1, width),
            (tn(late_hidden[0], grad_up[0]) + tn(late_hidden[1], grad_up[1]))
            .astype(BF16)
            .reshape(16, -1, width),
        ],
        axis=1,
    )
    ffn_pack, hidden_far = marker.fence(ffn_pack, hidden_far)
    ffn_parts = trade(ffn_pack)

    *grads, sums = run_norm(
        (
            attn_gain,
            last_sums,
            grad_second[0],
            hidden_pair[0],
            hidden_far[0],
            normed_one[0],
            rscale_one[0],
            grad_second[1],
            hidden_pair[1],
            hidden_far[1],
            normed_one[1],
            rscale_one[1],
        )
    )
    grad_first, own_grad = grads[:2], grads[2:]
    (*own_grad, sums), state = tie((*own_grad, sums), marker.state)
    arrived = [lax.ppermute(values, "mp", CORE_SWAP) for values in (*own_grad, sums)]
    (*other_grad, other_sums), marker.state = tie(arrived, mark(state))
    grad_query, grad_key, grad_value, packed = run_back(
        lengths,
        core_arg,
        (
            own_grad[0],
            other_grad[0],
            own_grad[1],
            other_grad[1],
            mixed_a,
            mixed_b,
            *lse,
            output_proj,
            query_b,
            key_b,
            value_b,
            key_tb,
            sums,
            other_sums,
            *inner_sums,
            rows,
        ),
        marker.state,
    )
    marker = Marker()

    def input_part(first):
        span = slice(first, first + half)
        return (
            nt(grad_query[span], query_proj)
            + nt(grad_key[span], key_proj)
            + nt(grad_value[span], value_proj)
        )

    token_pair = []
    for i in range(2):
        other = input_part(i * chunk + half).astype(BF16)
        token_pair.append(pair(input_part(i * chunk), marker.core_swap(other)))
    token_pair, (packed, ffn_parts) = marker.fence(token_pair, (packed, ffn_parts))
    packed_parts = trade(packed)
    ffn_total = plane_sum(ffn_parts)
    ffn_near = lax.ppermute(ffn_total, "dp", NEAR_SWAP)
    ffn_reduced = (ffn_total.astype(F32) + ffn_near.astype(F32)).astype(BF16)
    ffn_reduced, token_pair = tie(ffn_reduced, token_pair)
    token_pair, packed_parts = marker.fence(token_pair, packed_parts)
    token_far = [far_swap(token_pair[i]) for i in range(2)]
    packed_reduced = marker.near_sum(plane_sum(packed_parts))
    token_far, packed_reduced = tie(token_far, packed_reduced)
    piece_rows = width // 16
    places = jnp.stack([my_index // 8, (my_index // 2) % 4]).astype(jnp.int32)
    halves = [
        jnp.concatenate([ffn_reduced[:piece_rows], packed_reduced[: piece_rows // 3]], axis=0),
        jnp.concatenate([ffn_reduced[piece_rows:], packed_reduced[piece_rows // 3 :]], axis=0),
    ]
    pieces = [ring_pieces(halves[1], "z"), ring_pieces(halves[0], "y")]
    halves, pieces = marker.fence(halves, pieces)
    other_ring = run_join(places[:1], (halves[1], *pieces[0]), 1)
    one_ring = run_join(places[1:], (halves[0], *pieces[1]), 4)
    pieces = ring_pieces(other_ring, "y")
    other_ring, one_ring = marker.fence(other_ring, one_ring)
    gathered = trade_z(one_ring)
    one_ring, token_far = marker.fence(one_ring, token_far)
    token_own = [
        (grad_first[i] + (token_pair[i].astype(F32) + token_far[i].astype(F32))).astype(BF16)
        for i in range(2)
    ]
    token_other = [lax.ppermute(rows_here, "mp", CORE_SWAP) for rows_here in token_own]
    token_grad = run_settle(core_arg, (*token_own, *token_other))
    closing = finish(marker.state)[0, 0]
    part = piece_rows // 3
    so_far = run_spread_some(places, (other_ring, pieces[0], pieces[1]), piece_rows, part)
    so_far, token_grad = tie(so_far, token_grad)
    *rest, outer_grad = run_spread_rest(places, pieces[2], gathered, so_far, piece_rows, part)
    inner_grad, *rest = rest
    cuts = [values.reshape(local_width, width) for values in rest[:4]]
    vectors = rest[4:]
    return (
        loss[0, 0] + closing,
        token_grad,
        cuts[1].T,
        vectors[7],
        cuts[2].T,
        cuts[3].T,
        vectors[8],
        cuts[0],
        vectors[0],
        vectors[1],
        vectors[2],
        inner_grad.reshape(width, width),
        vectors[6],
        outer_grad.reshape(width, width),
        vectors[3],
        vectors[4],
        vectors[5],
    )


def solution(mesh):
    column, row, split = P(None, "mp"), P("mp", None), P("mp")
    placed = (
        (P("dp", None), P("dp"), P())
        + (column, split, column, column, split, row)
        + (P(), P(), P())
        + (column, split, row)
        + (P(), P(), P())
    )
    given = (
        (P(), P("dp", None))
        + (column, split, column, column, split, row)
        + (P(), P(), P())
        + (column, split, row)
        + (P(), P(), P())
    )
    return jax.shard_map(local, mesh=mesh, in_specs=placed, out_specs=given, check_vma=False)
```

```python
import functools
import math

import jax
import jax.numpy as jnp
from jax import lax
from jax.experimental import pallas as pl
from jax.experimental.pallas import tpu as pltpu
from jax.sharding import PartitionSpec as P

HD = 64
EPS_NORM = 1e-06
SOFTMAX_WARMTH = 0.01
NEG_FILL = -1e30
HIGHEST = lax.Precision.HIGHEST
F32 = jnp.float32
BF16 = jnp.bfloat16
QB = 256
KB = 256

CORE_SWAP = [(i, i ^ 1) for i in range(4)]
FAR_SWAP = [(i, i ^ 2) for i in range(4)]
NEAR_SWAP = [(i, i ^ 1) for i in range(32)]
PLANES = [[i * 2 + x for i in range(16)] for x in range(2)]
Z_RINGS = [[i + 8 * z for z in range(4)] for i in range(8)]

SMEM = pl.BlockSpec(memory_space=pltpu.SMEM)
VMEM = pl.BlockSpec(memory_space=pltpu.VMEM)
HBM = pl.BlockSpec(memory_space=pltpu.HBM)


def nn(left, right):
    return lax.dot_general(left, right, (((1,), (0,)), ((), ())), preferred_element_type=F32)


def nt(left, right):
    return lax.dot_general(left, right, (((1,), (1,)), ((), ())), preferred_element_type=F32)


def tn(left, right):
    return lax.dot_general(left, right, (((0,), (0,)), ((), ())), preferred_element_type=F32)


def place_of_block(block, core, rows):
    return ((block % 2) * 2 + block // 2) * QB + core * (rows // 2) & (rows - 1)


def spot_of_keys(j, core, rows):
    place = (j * KB + core * (rows // 2)) & (rows - 1)
    block = place // QB
    return pl.multiple_of(((block % 2) * 2 + block // 2) * QB + place % QB, KB)


def segment_bounds(lengths_ref):
    bounds, total = [], jnp.int32(0)
    for s in range(lengths_ref.shape[0]):
        start = total
        total = total + lengths_ref[s]
        bounds.append((start, total))
    return bounds


def block_span(bounds, first, rows):
    place = first + lax.broadcasted_iota(jnp.int32, (1, QB), 1)
    low, high = first, first + KB
    begin = jnp.full((1, QB), bounds[-1][1], jnp.int32)
    end = jnp.full((1, QB), rows, jnp.int32)
    for start, stop in bounds:
        inside = (place >= start) & (place < stop)
        begin = jnp.where(inside, start, begin)
        end = jnp.where(inside, stop, end)
        touches = (stop > first) & (start < first + QB) & (stop > start)
        low = jnp.where(touches, jnp.minimum(low, start), low)
        high = jnp.where(touches, jnp.maximum(high, stop), high)
    return low // KB, (high + KB - 1) // KB, begin, end


def head_copies(values, heads):
    lane = lax.broadcasted_iota(jnp.int32, values.shape, 1) // HD
    blank = jnp.zeros_like(values)
    return jnp.concatenate([jnp.where(lane == h, values, blank) for h in range(heads)], axis=0)


def span_mask(begin, end, block, heads):
    place = block * KB + lax.broadcasted_iota(jnp.int32, (KB, QB), 0)
    keep = (place >= begin) & (place < end)
    return jnp.concatenate([keep] * heads, axis=1)


def attend(heads, blocks, core, bounds, q_ref, k_ref, vt_ref, mixed_ref, lse_ref, acc_ref):
    rows = k_ref.shape[0]
    for i, block in enumerate(blocks):
        low, high, begin, end = block_span(bounds, place_of_block(block, core, rows), rows)
        stack = head_copies(q_ref[block * QB : (block + 1) * QB, :], heads)
        acc_ref[...] = jnp.zeros(acc_ref.shape, F32)

        def step(j, carry, stack=stack, begin=begin, end=end):
            top, total = carry
            spot = spot_of_keys(j, core, rows)
            scores = nt(k_ref[pl.ds(spot, KB), :], stack)
            scores = jnp.where(span_mask(begin, end, j, heads), scores, NEG_FILL)
            peak = jnp.maximum(top, jnp.max(scores, axis=0, keepdims=True))
            fade = jnp.exp(top - peak)
            probs = jnp.exp(scores - peak)
            total = total * fade + jnp.sum(probs, axis=0, keepdims=True)
            probs = probs.astype(BF16)
            for h in range(heads):
                part = slice(h * QB, (h + 1) * QB)
                span = slice(h * HD, (h + 1) * HD)
                acc_ref[span, :] = acc_ref[span, :] * fade[:, part] + nn(
                    vt_ref[span, pl.ds(spot, KB)], probs[:, part]
                )
            return peak, total

        top = jnp.full((1, heads * QB), NEG_FILL, F32)
        top, total = lax.fori_loop(
            low, high, step, (top, jnp.zeros((1, heads * QB), F32)), unroll=False
        )
        scale = 1.0 / total
        mixed = jnp.concatenate(
            [
                acc_ref[h * HD : (h + 1) * HD, :] * scale[:, h * QB : (h + 1) * QB]
                for h in range(heads)
            ],
            axis=0,
        )
        mixed_ref[i * QB : (i + 1) * QB, :] = mixed.T.astype(BF16)
        lse_ref[i, :, :] = jnp.broadcast_to(top + jnp.log(total), (8, heads * QB))


def fetch(sources, targets, semaphores, order=()):
    copies = [
        pltpu.make_async_copy(source, target, semaphores.at[i])
        for i, (source, target) in enumerate(zip(sources, targets))
    ]
    for i in [*order, *(i for i in range(len(copies)) if i not in order)]:
        copies[i].start()
    return copies


def project(mixed_ref, weights_ref, results, outputs, semaphores):
    results[1][...] = nn(mixed_ref[QB:, :], weights_ref[...]).astype(BF16)
    copies = send_out(results, outputs, semaphores, (1,))
    results[0][...] = nn(mixed_ref[:QB, :], weights_ref[...])
    return copies + send_out(results, outputs, semaphores, (0,))


def attend_first(heads, blocks, lengths_ref, core_ref, *refs):
    sources, outputs, refs = refs[:13], refs[13:25], refs[25:]
    results, targets, refs = refs[:12], refs[12:24], refs[24:]
    acc_ref, semaphores, out_semaphores = refs
    x_ref, q_ref, k_ref, v_ref, kt_ref, vt_ref, mixed_ref, lse_ref = results[:8]
    wqt_ref, wkt_ref, wvt_ref, bq_ref, bv_ref, wo_ref = targets[:6]
    rows = x_ref.shape[0]
    core = core_ref[0]
    copies = fetch(sources[1:], targets, semaphores)
    row_copies = []
    for block in range(rows // QB):
        first = pl.multiple_of(place_of_block(block, core, rows), QB)
        row_copies.append(
            pltpu.make_async_copy(
                sources[0].at[pl.ds(first, QB), :],
                x_ref.at[pl.ds(block * QB, QB), :],
                semaphores.at[12 + block],
            )
        )
        row_copies[-1].start()
    for copy in copies:
        copy.wait()
    query_bias, value_bias = row_of(bq_ref), row_of(bv_ref)
    for block in range(rows // QB):
        row_copies[block].wait()
        part = slice(block * QB, (block + 1) * QB)
        x = x_ref[part, :]
        q = (nt(x, wqt_ref[...]) + query_bias).astype(BF16)
        q_ref[part, :] = q * BF16(0.125)
        k_ref[part, :] = nt(x, wkt_ref[...]).astype(BF16)
        kt_ref[:, part] = nt(wkt_ref[...], x).astype(BF16)
        v = nt(x, wvt_ref[...]) + value_bias
        v_ref[part, :] = v.astype(BF16)
        vt_ref[:, part] = v.T.astype(BF16)
    outgoing = send_out(results, outputs, out_semaphores, range(6))
    bounds = segment_bounds(lengths_ref)
    place = core * (2 * QB) + lax.broadcasted_iota(jnp.int32, (1, QB), 1)
    for i in range(2):
        member = [
            jnp.where((place + i * QB >= start) & (place + i * QB < stop), 1.0, 0.0)
            for start, stop in bounds
        ]
        results[10][i] = jnp.concatenate(member, axis=0)
    lines = [row_of(ref) for ref in targets[6:]]
    results[11][...] = jnp.concatenate(lines + [jnp.zeros((2, lines[0].shape[1]), F32)], axis=0)
    outgoing += send_out(results, outputs, out_semaphores, (10, 11))
    attend(heads, blocks, core, bounds, q_ref, k_ref, vt_ref, mixed_ref, lse_ref, acc_ref)
    outgoing += project(mixed_ref, wo_ref, results[8:], outputs[8:], out_semaphores.at[8:10])
    outgoing += send_out(results, outputs, out_semaphores, (6, 7))
    for copy in outgoing:
        copy.wait()


def attend_more(heads, blocks, lengths_ref, core_ref, *refs):
    sources, outputs, refs = refs[:4], refs[4:8], refs[8:]
    targets, results, refs = refs[:4], refs[4:8], refs[8:]
    acc_ref, semaphores, out_semaphores = refs
    q_ref, k_ref, vt_ref, wo_ref = targets
    mixed_ref, lse_ref = results[:2]
    for copy in fetch(sources, targets, semaphores):
        copy.wait()
    bounds = segment_bounds(lengths_ref)
    attend(heads, blocks, core_ref[0], bounds, q_ref, k_ref, vt_ref, mixed_ref, lse_ref, acc_ref)
    outgoing = project(mixed_ref, wo_ref, results[2:], outputs[2:], out_semaphores.at[2:])
    outgoing += send_out(results, outputs, out_semaphores, (0, 1))
    for copy in outgoing:
        copy.wait()


def attend_back(heads, inputs, lengths_ref, core_ref, *refs):
    sources, refs = refs[:inputs], refs[inputs + 1 :]
    outputs, refs = refs[:4], refs[4:]
    gq_ref, gk_ref, gv_ref, pack_ref = refs[:4]
    dk_ref, dv_ref, dqt_ref, wo_acc_ref, semaphores, out_semaphores = refs[4:10]
    targets = refs[10:]
    copies = fetch(sources, targets, semaphores, (10, 9, 11, 12, 0, 4, 8, 6, 1, 2, 3, 5, 7))
    grads = targets[0:4]
    mixed = targets[4:6]
    lses = targets[6:8]
    wo_ref, q_ref, k_ref, v_ref, kt_ref = targets[8:13]
    own_sums, other_sums, inner_a, inner_b, x_ref = targets[13:]
    rows, width = q_ref.shape
    core = core_ref[0]
    bounds = segment_bounds(lengths_ref)
    dk_ref[...] = jnp.zeros(dk_ref.shape, F32)
    dv_ref[...] = jnp.zeros(dv_ref.shape, F32)
    lane = lax.broadcasted_iota(jnp.int32, (8, width), 1) // HD
    which = (lane == lax.broadcasted_iota(jnp.int32, (8, width), 0)).astype(F32).astype(BF16)
    for i in (0, 4, 6, 8, 9, 10, 11, 12):
        copies[i].wait()
    for block in range(rows // QB):
        if block > 0:
            copies[block].wait()
        if block == 2:
            copies[5].wait()
            copies[7].wait()
        low, high, begin, end = block_span(bounds, place_of_block(block, core, rows), rows)
        part = slice(block * QB, (block + 1) * QB)
        own = slice(block % 2 * QB, block % 2 * QB + QB)
        grad_attn = grads[block][...]
        mixed_here = mixed[block // 2][own, :]
        outer = tn(mixed_here, grad_attn)
        wo_acc_ref[...] = outer if block == 0 else wo_acc_ref[...] + outer
        grad_mixed = nt(grad_attn, wo_ref[...]).astype(BF16)
        product = grad_mixed.astype(F32) * mixed_here.astype(F32)
        sums = sum(nt(which, part) for part in in_three(product)[:2])
        delta = jnp.concatenate([sums[h : h + 1, :] for h in range(heads)], axis=1)
        lse = lses[block // 2][block % 2, 0:1, :]
        q_stack = head_copies(q_ref[part, :], heads)
        g_stack = head_copies(grad_mixed, heads)
        dqt_ref[...] = jnp.zeros(dqt_ref.shape, F32)

        def step(
            j, carry, delta=delta, lse=lse, q_stack=q_stack, g_stack=g_stack, begin=begin, end=end
        ):
            here = pl.ds(spot_of_keys(j, core, rows), KB)
            scores = nt(k_ref[here, :], q_stack)
            scores = jnp.where(span_mask(begin, end, j, heads), scores, NEG_FILL)
            probs = jnp.exp(scores - lse)
            grad = (probs * (nt(v_ref[here, :], g_stack) - delta)).astype(BF16)
            dv_ref[here, :] += nn(probs.astype(BF16), g_stack)
            dk_ref[here, :] += nn(grad, q_stack)
            for h in range(heads):
                span = slice(h * HD, (h + 1) * HD)
                dqt_ref[span, :] += nn(kt_ref[span, here], grad[:, h * QB : (h + 1) * QB])
            return carry

        lax.fori_loop(low, high, step, 0, unroll=False)
        gq_ref[part, :] = (dqt_ref[...].T * 0.125).astype(BF16)
    gk_ref[...] = dk_ref[...].astype(BF16)
    gv_ref[...] = dv_ref[...].astype(BF16)
    for copy in copies[13:]:
        copy.wait()
    outgoing = fetch(refs[:3], outputs[:3], out_semaphores)
    sums = [jnp.sum(ref[...].astype(F32), axis=0, keepdims=True) for ref in (gq_ref, gv_ref)]
    blank = jnp.zeros((1, 256 - width), F32)
    tail = jnp.concatenate([sums[0], blank, sums[1], blank, jnp.zeros((1, 256), F32)], axis=1)
    inner = row_of(inner_a) + row_of(inner_b)
    paired = own_sums[0:6, :] + other_sums[0:6, :]
    small = [paired, inner, tail, jnp.zeros((8, tail.shape[1]), F32)]
    small = jnp.concatenate(small, axis=0).astype(BF16)
    piece = pack_ref.shape[1] - 16
    per = width // piece
    for m, source in enumerate((None, gq_ref, gk_ref, gv_ref)):
        total = wo_acc_ref[...] if source is None else tn(source[...], x_ref[...])
        for t in range(per):
            cut = total[t * piece : (t + 1) * piece, :].astype(BF16)
            pack_ref[m * per + t, 0:piece, :] = cut
            pack_ref[m * per + t, piece:, :] = small if m + t == 0 else jnp.zeros_like(small)
        here = pl.ds(m * per, per)
        copy = pltpu.make_async_copy(
            pack_ref.at[here], outputs[3].at[here], out_semaphores.at[3 + m]
        )
        copy.start()
        outgoing.append(copy)
    for copy in outgoing:
        copy.wait()


def shaped(shape, dtype):
    return jax.ShapeDtypeStruct(shape, dtype)


PARAMS = pltpu.CompilerParams(vmem_limit_bytes=60 << 20)
SMALL = pltpu.CompilerParams(vmem_limit_bytes=60 << 20)
SHARED = pltpu.CompilerParams(vmem_limit_bytes=24 << 20)
COST = pl.CostEstimate(flops=1024, bytes_accessed=1024, transcendentals=0)


def buffers(arrays):
    return [pltpu.VMEM(array.shape, array.dtype) for array in arrays]


def attend_shapes(count, heads, width):
    rows = count * QB
    return (
        shaped((rows, heads * HD), BF16),
        shaped((count, 8, heads * QB), F32),
        shaped((rows // 2, width), F32),
        shaped((rows // 2, width), BF16),
    )


def run_first(lengths, core, tokens, weights, blocks):
    rows, width = tokens.shape
    local_width = weights[0].shape[0]
    heads = local_width // HD
    outs = (
        (shaped(tokens.shape, BF16),)
        + (shaped((rows, local_width), BF16),) * 3
        + (shaped((local_width, rows), BF16),) * 2
        + attend_shapes(len(blocks), heads, width)
        + (shaped((2, lengths.shape[0], QB), F32), shaped((8, width), F32))
    )
    return pl.pallas_call(
        functools.partial(attend_first, heads, blocks),
        out_shape=outs,
        in_specs=[SMEM] * 2 + [HBM] * 13,
        out_specs=(HBM,) * 12,
        scratch_shapes=buffers(outs)
        + buffers(weights)
        + [pltpu.VMEM((local_width, QB), F32)]
        + [pltpu.SemaphoreType.DMA((12 + rows // QB,)), pltpu.SemaphoreType.DMA((12,))],
        compiler_params=PARAMS,
        name="attend_first",
        cost_estimate=COST,
    )(lengths, core, tokens, *weights)


def run_more(lengths, core, arrays, blocks):
    rows, local_width = arrays[0].shape
    heads = local_width // HD
    outs = attend_shapes(len(blocks), heads, arrays[3].shape[1])
    return pl.pallas_call(
        functools.partial(attend_more, heads, blocks),
        out_shape=outs,
        in_specs=[SMEM] * 2 + [HBM] * 4,
        out_specs=(HBM,) * 4,
        scratch_shapes=buffers(arrays)
        + buffers(outs)
        + [pltpu.VMEM((local_width, QB), F32)]
        + [pltpu.SemaphoreType.DMA((4,)), pltpu.SemaphoreType.DMA((4,))],
        compiler_params=PARAMS,
        name="attend_more",
        cost_estimate=COST,
    )(lengths, core, *arrays)


def run_back(lengths, core, arrays, marker):
    wo, q, x = arrays[8], arrays[9], arrays[-1]
    rows, width = q.shape
    heads = width // HD
    piece = 4 * width // 16
    outs = (shaped((rows, width), BF16),) * 3 + (shaped((16, piece + 16, x.shape[1]), BF16),)
    return pl.pallas_call(
        functools.partial(attend_back, heads, len(arrays)),
        out_shape=outs,
        in_specs=[SMEM] * 2 + [HBM] * (len(arrays) + 1),
        out_specs=(HBM,) * 4,
        scratch_shapes=buffers(outs)
        + [pltpu.VMEM((rows, width), F32)] * 2
        + [pltpu.VMEM((width, QB), F32), pltpu.VMEM(wo.shape, F32)]
        + [pltpu.SemaphoreType.DMA((len(arrays),)), pltpu.SemaphoreType.DMA((7,))]
        + buffers(arrays),
        compiler_params=PARAMS,
        name="attend_back",
        cost_estimate=COST,
    )(lengths, core, *arrays, marker)


def mark_kernel(source_ref, target_ref):
    del source_ref, target_ref


def mark(values):
    return pl.pallas_call(
        mark_kernel,
        out_shape=shaped(values.shape, values.dtype),
        in_specs=[HBM],
        out_specs=HBM,
        compiler_params=pltpu.CompilerParams(vmem_limit_bytes=1 << 20),
        name="mark",
        cost_estimate=pl.CostEstimate(flops=1 << 36, bytes_accessed=1 << 10, transcendentals=0),
    )(values)


def finish_kernel(source_ref, target_ref):
    del source_ref
    target_ref[...] = jnp.zeros(target_ref.shape, F32)


def finish(values):
    return pl.pallas_call(
        finish_kernel,
        out_shape=shaped(values.shape, values.dtype),
        in_specs=[HBM],
        out_specs=VMEM,
        compiler_params=pltpu.CompilerParams(vmem_limit_bytes=1 << 20),
        name="finish",
        cost_estimate=COST,
    )(values)


def row_of(ref):
    return ref[...].astype(F32).reshape(1, -1)


def in_three(values):
    high = values.astype(BF16)
    rest = values - high.astype(F32)
    middle = rest.astype(BF16)
    return high, middle, (rest - middle.astype(F32)).astype(BF16)


def norm_step(grad, normed, rscale, gain):
    scaled = grad * gain
    first_mean = jnp.mean(scaled, axis=1, keepdims=True)
    cross_mean = jnp.mean(scaled * normed, axis=1, keepdims=True)
    return rscale * (scaled - first_mean - normed * cross_mean)


def column_of(ref):
    row = ref[...].reshape(1, -1)
    return jnp.broadcast_to(row, (128, row.shape[1])).T[:, 0:1]


def column_sum(values):
    return jnp.sum(values, axis=0, keepdims=True)


def send_out(results, outputs, semaphores, which):
    copies = [
        pltpu.make_async_copy(results[k], outputs[k], semaphores.at[k]) for k in which
    ]
    for copy in copies:
        copy.start()
    return copies


def loss_back(lengths_ref, place_ref, *refs):
    sources, outputs, refs = refs[:9], refs[9:15], refs[15:]
    targets, results = refs[:9], refs[9:15]
    coef_ref, turned_ref, semaphores, out_semaphores = refs[15:]
    copies = fetch(sources, targets, semaphores)
    piece_ref, swapped_ref, pooled_ref, match_ref, gain_ref = targets[:5]
    core, index = place_ref[0], place_ref[1]
    bounds = segment_bounds(lengths_ref)
    for copy in copies[:5]:
        copy.wait()
    first = core == 0
    queries = jnp.where(first, piece_ref[...], swapped_ref[...])
    passages = jnp.where(first, swapped_ref[...], piece_ref[...])
    count = queries.shape[0]
    own = pooled_ref.shape[0] // 2
    similarity = nt(queries, passages) / SOFTMAX_WARMTH
    match = match_ref[...].reshape(1, -1)
    match = match == lax.broadcasted_iota(jnp.int32, (count, count), 0)
    top = jnp.max(similarity, axis=1, keepdims=True)
    lse = top + jnp.log(jnp.sum(jnp.exp(similarity - top), axis=1, keepdims=True))
    positive = jnp.sum(jnp.where(match, similarity, 0.0), axis=1, keepdims=True)
    loss = jnp.sum(lse - positive, axis=0, keepdims=True) / count
    results[5][...] = jnp.broadcast_to(loss, results[5].shape)
    coef = (jnp.exp(similarity - lse) - match.astype(F32)) * (1.0 / (count * SOFTMAX_WARMTH))
    coef_ref[...] = coef
    turned_ref[...] = coef.T
    here = pl.ds(pl.multiple_of(index * own, own), own)
    grad_query = sum(nn(part, passages) for part in in_three(coef_ref[here, :]))
    grad_passage = sum(nn(part, queries) for part in in_three(turned_ref[here, :]))
    grad_unit = jnp.concatenate([grad_query, grad_passage], axis=0)
    pooled = pooled_ref[...]
    rscale = lax.rsqrt(jnp.sum(pooled * pooled, axis=1, keepdims=True) + EPS_NORM)
    inner = jnp.sum(pooled * grad_unit, axis=1, keepdims=True)
    grad_pooled = rscale * grad_unit - rscale * rscale * rscale * inner * pooled
    seqs = 2 * own
    grad_pooled = jnp.concatenate(
        [grad_pooled, jnp.zeros((128 - seqs, grad_pooled.shape[1]), F32)], axis=0
    )
    parts = in_three(grad_pooled)
    lane = lax.broadcasted_iota(jnp.int32, (1, 128), 1)
    begin = end = jnp.zeros((1, 128), jnp.int32)
    for seq, (start, stop) in enumerate(bounds):
        begin = jnp.where(lane == seq, start, begin)
        end = jnp.where(lane == seq, stop, end)
    gain = row_of(gain_ref)
    sums = [0.0, 0.0, 0.0]
    outgoing = []
    for i in range(2):
        copies[5 + 2 * i].wait()
        copies[6 + 2 * i].wait()
        normed = targets[5 + 2 * i][...]
        place = core * (2 * QB) + i * QB + lax.broadcasted_iota(jnp.int32, (QB, 128), 0)
        member = jnp.where((place >= begin) & (place < end), 1.0, 0.0).astype(BF16)
        grad = sum(nn(member, part) for part in parts)
        second = norm_step(grad, normed, column_of(targets[6 + 2 * i]), gain)
        rounded = second.astype(BF16)
        results[i][...] = second
        results[2 + i][...] = rounded
        for k, values in enumerate((rounded.astype(F32), grad * normed, grad)):
            sums[k] = sums[k] + column_sum(values)
        outgoing += send_out(results, outputs, out_semaphores, (2 + i, i))
    results[4][...] = jnp.concatenate(sums + [jnp.zeros((5, sums[0].shape[1]), F32)], axis=0)
    outgoing += send_out(results, outputs, out_semaphores, (4, 5))
    for copy in outgoing:
        copy.wait()


def norm_back(*refs):
    sources, outputs, refs = refs[:12], refs[12:17], refs[17:]
    targets, results = refs[:12], refs[12:17]
    semaphores, out_semaphores = refs[17:]
    copies = fetch(sources, targets, semaphores)
    copies[0].wait()
    copies[1].wait()
    gain = row_of(targets[0])
    sums = [0.0, 0.0, 0.0]
    outgoing = []
    for i in range(2):
        for copy in copies[2 + 5 * i : 7 + 5 * i]:
            copy.wait()
        second, pair_here, far, normed, rscale = targets[2 + 5 * i : 7 + 5 * i]
        grad = second[...] + (pair_here[...].astype(F32) + far[...].astype(F32))
        normed = normed[...]
        first = norm_step(grad, normed, column_of(rscale), gain)
        rounded = first.astype(BF16)
        results[i][...] = first
        results[2 + i][...] = rounded
        for k, values in enumerate((rounded.astype(F32), grad * normed, grad)):
            sums[k] = sums[k] + column_sum(values)
        outgoing += send_out(results, outputs, out_semaphores, (2 + i, i))
    blank = jnp.zeros((2, sums[0].shape[1]), F32)
    results[4][...] = jnp.concatenate(sums + [targets[1][0:3, :], blank], axis=0)
    outgoing += send_out(results, outputs, out_semaphores, (4,))
    for copy in outgoing:
        copy.wait()


STEPS = (0, 2, 1, 3)


def join(copies_of_each, place_ref, *refs):
    sources, output, semaphores = refs[:4], refs[4], refs[5]
    copies = []
    for k in range(4):
        spot = (place_ref[0] + 4 - STEPS[k]) % 4
        for r in range(copies_of_each):
            goal = output.at[spot] if copies_of_each == 1 else output.at[r, spot]
            semaphore = semaphores.at[k * copies_of_each + r]
            copies.append(pltpu.make_async_copy(sources[k], goal, semaphore))
            copies[-1].start()
    for copy in copies:
        copy.wait()


def place_block(piece, part, block_ref, spot, outputs, buffers_, semaphores, first):
    inner, cuts = buffers_
    inner[...] = block_ref[:, :piece, :].astype(F32)
    cuts[...] = block_ref[:, piece : 2 * piece - part, :].astype(F32)
    copies = [pltpu.make_async_copy(inner, outputs[0].at[:, spot], semaphores.at[first])]
    for m in range(4):
        goal = outputs[1 + m].at[spot, pl.ds(part, piece - part), :]
        copies.append(pltpu.make_async_copy(cuts.at[m], goal, semaphores.at[first + 1 + m]))
    for copy in copies:
        copy.start()
    return copies


def place_vectors(piece, part, block_ref, spot, outputs, vectors, semaphores, first):
    @pl.when(spot == 0)
    def _():
        small = block_ref[0, 2 * piece - part :, :].astype(F32)
        for k in range(7):
            vectors[k][...] = small[k : k + 1, :].reshape(-1)
        count = vectors[7].shape[0]
        for k in range(2):
            vectors[7 + k][...] = small[7:8, 256 * k : 256 * k + count].reshape(-1)
        copies = [
            pltpu.make_async_copy(vectors[k], outputs[5 + k], semaphores.at[first + k])
            for k in range(9)
        ]
        for copy in copies:
            copy.start()
        for copy in copies:
            copy.wait()


def spread_some(piece, part, count, place_ref, *refs):
    sources, outputs, refs = refs[:count], refs[count : count + 14], refs[count + 14 :]
    blocks, refs = refs[:count], refs[count:]
    buffers_, vectors, refs = refs[: 2 * count], refs[2 * count : 2 * count + 9], refs[-2:]
    arrivals = fetch(sources, blocks, refs[0])
    outgoing, spots = [], []
    for k in range(count):
        arrivals[k].wait()
        spots.append((place_ref[1] + 4 - STEPS[k]) % 4)
        outgoing += place_block(
            piece, part, blocks[k], spots[k], outputs, buffers_[2 * k : 2 * k + 2], refs[1], 5 * k
        )
    for k in range(count):
        place_vectors(piece, part, blocks[k], spots[k], outputs, vectors, refs[1], 5 * count)
    for copy in outgoing:
        copy.wait()


def spread_rest(piece, part, place_ref, *refs):
    sources, outputs, refs = refs[:3], refs[17:32], refs[32:]
    blocks, by_z, refs = refs[:2], refs[2], refs[3:]
    buffers_, outer, heads, vectors, refs = refs[:4], refs[4], refs[5], refs[6:15], refs[15:]
    semaphores, out_semaphores = refs
    arrivals = fetch(sources, (*blocks, by_z), semaphores)
    outgoing, spots = [], []
    for k in range(2):
        spots.append((place_ref[1] + 4 - STEPS[2 + k]) % 4)
        arrivals[k].wait()
        outgoing += place_block(
            piece,
            part,
            blocks[k],
            spots[k],
            outputs,
            buffers_[2 * k : 2 * k + 2],
            out_semaphores,
            5 * k,
        )
    arrivals[2].wait()
    outer[...] = by_z[:, :, :piece, :].astype(F32)
    copies = [pltpu.make_async_copy(outer, outputs[14], out_semaphores.at[10])]
    copies[0].start()
    heads[...] = by_z[:, :, piece:, :].astype(F32)
    for m in range(4):
        goal = outputs[1 + m].at[:, pl.ds(0, part), :]
        copies.append(pltpu.make_async_copy(heads.at[m], goal, out_semaphores.at[11 + m]))
        copies[-1].start()
    for k in range(2):
        place_vectors(piece, part, blocks[k], spots[k], outputs, vectors, out_semaphores, 15)
    for copy in outgoing + copies:
        copy.wait()


def run_loss(lengths, place, arrays):
    rows, width = arrays[5].shape
    count = arrays[0].shape[0]
    outs = (
        (shaped((rows, width), F32),) * 2
        + (shaped((rows, width), BF16),) * 2
        + (shaped((8, width), F32), shaped((8, 128), F32))
    )
    return pl.pallas_call(
        loss_back,
        out_shape=outs,
        in_specs=[SMEM] * 2 + [HBM] * 9,
        out_specs=(HBM,) * 6,
        scratch_shapes=buffers(arrays)
        + buffers(outs)
        + [pltpu.VMEM((count, count), F32)] * 2
        + [pltpu.SemaphoreType.DMA((9,)), pltpu.SemaphoreType.DMA((6,))],
        compiler_params=SHARED,
        name="loss_back",
        cost_estimate=COST,
    )(lengths, place, *arrays)


def run_norm(arrays):
    rows, width = arrays[2].shape
    outs = (
        (shaped((rows, width), F32),) * 2
        + (shaped((rows, width), BF16),) * 2
        + (shaped((8, width), F32),)
    )
    return pl.pallas_call(
        norm_back,
        out_shape=outs,
        in_specs=[HBM] * 12,
        out_specs=(HBM,) * 5,
        scratch_shapes=buffers(arrays)
        + buffers(outs)
        + [pltpu.SemaphoreType.DMA((12,)), pltpu.SemaphoreType.DMA((5,))],
        compiler_params=SMALL,
        name="norm_back",
        cost_estimate=COST,
    )(*arrays)


def run_join(place, pieces, copies_of_each):
    lead = (4,) if copies_of_each == 1 else (copies_of_each, 4)
    return pl.pallas_call(
        functools.partial(join, copies_of_each),
        out_shape=shaped(lead + pieces[0].shape, BF16),
        in_specs=[SMEM] + [HBM] * 4,
        out_specs=HBM,
        scratch_shapes=[pltpu.SemaphoreType.DMA((4 * copies_of_each,))],
        compiler_params=pltpu.CompilerParams(vmem_limit_bytes=1 << 20),
        name="join",
        cost_estimate=COST,
    )(place, *pieces)


def settle(core_ref, *refs):
    sources, output, semaphores = refs[:4], refs[4], refs[5]
    copies = []
    for k in range(4):
        first = (k // 2 + core_ref[0]) % 2 * (2 * QB) + k % 2 * QB
        spot = pl.ds(pl.multiple_of(first, QB), QB)
        copies.append(pltpu.make_async_copy(sources[k], output.at[spot, :], semaphores.at[k]))
        copies[-1].start()
    for copy in copies:
        copy.wait()


def run_settle(core, parts):
    rows, width = parts[0].shape
    return pl.pallas_call(
        settle,
        out_shape=shaped((4 * rows, width), BF16),
        in_specs=[SMEM] + [HBM] * 4,
        out_specs=HBM,
        scratch_shapes=[pltpu.SemaphoreType.DMA((4,))],
        compiler_params=pltpu.CompilerParams(vmem_limit_bytes=1 << 20),
        name="settle",
        cost_estimate=COST,
    )(core, *parts)


def spread_shapes(piece, width):
    shapes = [(4, 4, piece, width)] + [(4, piece, width)] * 4
    return shapes + [(width,)] * 7 + [(4 * piece,)] * 2


def run_spread_some(places, blocks, piece, part):
    width = blocks[0].shape[2]
    shapes = spread_shapes(piece, width)
    count = len(blocks)
    pair_of = [pltpu.VMEM((4, piece, width), F32), pltpu.VMEM((4, piece - part, width), F32)]
    return pl.pallas_call(
        functools.partial(spread_some, piece, part, count),
        out_shape=[shaped(shape, F32) for shape in shapes],
        in_specs=[SMEM] + [HBM] * count,
        out_specs=[HBM] * 14,
        scratch_shapes=buffers(blocks)
        + pair_of * count
        + [pltpu.VMEM(shape, F32) for shape in shapes[5:]]
        + [pltpu.SemaphoreType.DMA((count,)), pltpu.SemaphoreType.DMA((5 * count + 9,))],
        compiler_params=SHARED,
        name="spread_some",
        cost_estimate=COST,
    )(places, *blocks)


def run_spread_rest(places, blocks, gathered, so_far, piece, part):
    width = gathered.shape[3]
    shapes = spread_shapes(piece, width)
    outer = (4, 4, piece, width)
    pair_of = [pltpu.VMEM((4, piece, width), F32), pltpu.VMEM((4, piece - part, width), F32)]
    return pl.pallas_call(
        functools.partial(spread_rest, piece, part),
        out_shape=[shaped(shape, F32) for shape in shapes + [outer]],
        in_specs=[SMEM] + [HBM] * 17,
        out_specs=[HBM] * 15,
        input_output_aliases={4 + k: k for k in range(14)},
        scratch_shapes=buffers((*blocks, gathered))
        + pair_of * 2
        + [pltpu.VMEM(outer, F32), pltpu.VMEM((4, 4, part, width), F32)]
        + [pltpu.VMEM(shape, F32) for shape in shapes[5:]]
        + [pltpu.SemaphoreType.DMA((3,)), pltpu.SemaphoreType.DMA((24,))],
        compiler_params=SHARED,
        name="spread_rest",
        cost_estimate=COST,
    )(places, *blocks, gathered, *so_far)


def trade(values):
    return lax.all_to_all(
        values, "dp", split_axis=0, concat_axis=0, axis_index_groups=PLANES, tiled=True
    )


def share(values):
    spread_out = jnp.broadcast_to(values[None], (32,) + values.shape)
    return lax.all_to_all(spread_out, "dp", split_axis=0, concat_axis=0, tiled=True)


def trade_z(values):
    return lax.all_to_all(
        values, "dp", split_axis=0, concat_axis=0, axis_index_groups=Z_RINGS, tiled=True
    )


def ring_shift(axis, step):
    pairs = []
    for i in range(32):
        z, y, x = i // 8, (i // 2) % 4, i % 2
        z, y = ((z + step) % 4, y) if axis == "z" else (z, (y + step) % 4)
        pairs.append((i, (z * 4 + y) * 2 + x))
    return pairs


def ring_pieces(values, axis):
    return [lax.ppermute(values, "dp", ring_shift(axis, step)) for step in STEPS[1:]]


def tie(values, others):
    return lax.optimization_barrier((values, others))


class Marker:
    def __init__(self):
        self.state = jnp.zeros((8, 128), F32)

    def fence(self, ready, later):
        ready, state = tie(ready, self.state)
        later, self.state = tie(later, mark(state))
        return ready, later

    def moved(self, values, axis, pairs):
        values, state = tie(values, self.state)
        arrived, self.state = tie(lax.ppermute(values, axis, pairs), mark(state))
        return arrived

    def core_swap(self, values):
        return self.moved(values, "mp", CORE_SWAP)

    def near_swap(self, values):
        return self.moved(values, "dp", NEAR_SWAP)

    def both(self, own):
        return jnp.concatenate([own, self.core_swap(own)], axis=0)

    def near_sum(self, total):
        return (total.astype(F32) + self.near_swap(total).astype(F32)).astype(BF16)


def plane_sum(parts):
    return jnp.sum(parts.astype(F32), axis=0).astype(BF16)


def far_swap(values):
    return lax.ppermute(values, "mp", FAR_SWAP)


def norm_forward(values, gain_vec, shift_vec):
    average = jnp.mean(values, axis=-1, keepdims=True)
    centred = values - average
    rscale = lax.rsqrt(jnp.mean(centred * centred, axis=-1, keepdims=True) + EPS_NORM)
    normed = centred * rscale
    return (normed * gain_vec + shift_vec, normed, rscale[:, 0])


def gelu_and_slope(upper):
    below = 0.5 * (1.0 + lax.erf(upper * math.sqrt(0.5)))
    density = jnp.exp(-0.5 * upper * upper) * (1.0 / math.sqrt(2.0 * math.pi))
    return (upper * below).astype(BF16), (below + upper * density).astype(BF16)


def local(
    tokens,
    lengths,
    pair_index,
    query_proj,
    query_bias,
    key_proj,
    value_proj,
    value_bias,
    output_proj,
    output_bias,
    attn_gain,
    attn_shift,
    inner_proj,
    inner_bias,
    outer_proj,
    outer_bias,
    final_gain,
    final_shift,
):
    row_count, width = tokens.shape
    chunk = row_count // 2
    half = chunk // 2
    seq_count = lengths.shape[0]
    pair_count = seq_count // 2
    overall_pair_count = pair_index.shape[0]
    local_width = query_proj.shape[1]
    core = lax.axis_index("mp") % 2
    my_index = lax.axis_index("dp")
    marker = Marker()
    core_arg = jnp.reshape(core, (1,)).astype(jnp.int32)
    vectors = (output_bias, attn_gain, attn_shift, outer_bias, final_gain, final_shift)
    query_t, key_t, value_t = query_proj.T, key_proj.T, value_proj.T

    weights = (query_t, key_t, value_t, query_bias, value_bias, output_proj, *vectors)
    first = run_first(lengths, core_arg, tokens, weights, (0, 1))
    rows, query_b, key_b, value_b, key_tb, value_tb, mixed_a, lse_a = first[:8]
    attn_own_a, attn_other_a, members, vectors = first[8:]

    def own_and_other(values, weights):
        return nn(values[:half], weights), nn(values[half:], weights).astype(BF16)

    def pair(own, arrived):
        return (own + arrived.astype(F32)).astype(BF16)

    def first_norm(index, pair_here, far):
        attn_full = pair_here.astype(F32) + far.astype(F32) + output_bias
        own_tokens = rows[index * chunk : index * chunk + half].astype(F32)
        return norm_forward(own_tokens + attn_full, attn_gain_f, attn_shift_f)

    def feed_forward(own_hidden):
        whole = marker.both(own_hidden)
        act, slope = gelu_and_slope(nn(whole, inner_proj) + inner_bias.astype(F32))
        return whole, act, slope

    def last_norm(hidden, pair_here, far):
        ffn_full = pair_here.astype(F32) + far.astype(F32) + outer_bias
        return norm_forward(hidden + ffn_full, final_gain_f, final_shift_f)

    attn_pair_a = pair(attn_own_a, marker.core_swap(attn_other_a))
    attn_far_a = far_swap(attn_pair_a)
    output_bias, attn_gain_f, attn_shift_f = vectors[0], vectors[1], vectors[2]
    outer_bias, final_gain_f, final_shift_f = vectors[3], vectors[4], vectors[5]
    late_query, late_pair = tie(query_b, attn_pair_a)
    mixed_b, lse_b, attn_own_b, attn_other_b = run_more(
        lengths, core_arg, (late_query, key_b, value_tb, output_proj), (2, 3)
    )
    attn_pair_b = pair(attn_own_b, marker.core_swap(attn_other_b))
    attn_far_b = far_swap(attn_pair_b)
    attn_far_a, attn_pair_b = tie(attn_far_a, attn_pair_b)
    hidden_a, normed_one_a, rscale_one_a = first_norm(0, late_pair, attn_far_a)
    own_hidden_a = hidden_a.astype(BF16)
    hidden_ab, act_a, slope_a = feed_forward(own_hidden_a)
    ffn_own_a, ffn_other_a = own_and_other(act_a, outer_proj)
    ffn_pair_a = pair(ffn_own_a, marker.core_swap(ffn_other_a))
    attn_far_b, ffn_pair_late = tie(attn_far_b, ffn_pair_a)
    ffn_far_a = far_swap(ffn_pair_a)
    hidden_b, normed_one_b, rscale_one_b = first_norm(1, attn_pair_b, attn_far_b)
    own_hidden_b = hidden_b.astype(BF16)
    hidden_bb, act_b, slope_b = feed_forward(own_hidden_b)
    ffn_own_b, ffn_other_b = own_and_other(act_b, outer_proj)
    ffn_pair_b = pair(ffn_own_b, marker.core_swap(ffn_other_b))
    ffn_pair_b, ffn_far_a = marker.fence(ffn_pair_b, ffn_far_a)
    final_a, normed_two_a, rscale_two_a = last_norm(hidden_a, ffn_pair_late, ffn_far_a)
    pooled_a = jnp.dot(members[0], final_a, precision=HIGHEST)
    final_b, normed_two_b, rscale_two_b = last_norm(hidden_b, ffn_pair_b, far_swap(ffn_pair_b))
    pooled_part = pooled_a + jnp.dot(members[1], final_b, precision=HIGHEST)
    lse = (lse_a, lse_b)
    hidden_whole, act, slope = (hidden_ab, hidden_bb), (act_a, act_b), (slope_a, slope_b)
    normed_one, rscale_one = (normed_one_a, normed_one_b), (rscale_one_a, rscale_one_b)
    normed_two, rscale_two = (normed_two_a, normed_two_b), (rscale_two_a, rscale_two_b)
    pooled = pooled_part + marker.core_swap(pooled_part)
    pool_rscale = lax.rsqrt(jnp.sum(pooled * pooled, axis=-1, keepdims=True) + EPS_NORM)
    unit_b = (pooled * pool_rscale).astype(BF16)

    piece = lax.dynamic_slice_in_dim(unit_b, core * pair_count, pair_count, 0)
    piece = share(piece).reshape(overall_pair_count, width)
    place_arg = jnp.stack([core, my_index]).astype(jnp.int32)
    *grads, last_sums, loss = run_loss(
        lengths,
        place_arg,
        (
            piece,
            marker.core_swap(piece),
            pooled,
            pair_index,
            final_gain,
            normed_two[0],
            rscale_two[0],
            normed_two[1],
            rscale_two[1],
        ),
    )
    grad_second, own_grad = grads[:2], grads[2:]

    inner_sums, grad_ffn, grad_up, hidden_other, outer_sums = [], [], [], [], []
    for i in range(2):
        grad_ffn.append(marker.both(own_grad[i]))
        grad_up.append((nt(grad_ffn[i], outer_proj) * slope[i].astype(F32)).astype(BF16))
        inner_sums.append(jnp.sum(grad_up[i].astype(F32), axis=0))
        other = nt(grad_up[i][half:], inner_proj).astype(BF16)
        late_act, other = tie(act[i], other)
        outer_sums.append(tn(late_act, grad_ffn[i]))
        swap = marker.core_swap if i else lambda rows_here: lax.ppermute(rows_here, "mp", CORE_SWAP)
        arrived, outer_sums[i] = tie(swap(other), outer_sums[i])
        hidden_other.append(arrived)
    hidden_pair = [pair(nt(grad_up[i][:half], inner_proj), hidden_other[i]) for i in range(2)]
    hidden_far = [far_swap(hidden_pair[i]) for i in range(2)]
    late_hidden, hidden_pair = tie(hidden_whole, hidden_pair)
    ffn_pack = jnp.concatenate(
        [
            (outer_sums[0] + outer_sums[1])
            .astype(BF16)
            .reshape(16, -1, width),
            (tn(late_hidden[0], grad_up[0]) + tn(late_hidden[1], grad_up[1]))
            .astype(BF16)
            .reshape(16, -1, width),
        ],
        axis=1,
    )
    ffn_pack, hidden_far = marker.fence(ffn_pack, hidden_far)
    ffn_parts = trade(ffn_pack)

    *grads, sums = run_norm(
        (
            attn_gain,
            last_sums,
            grad_second[0],
            hidden_pair[0],
            hidden_far[0],
            normed_one[0],
            rscale_one[0],
            grad_second[1],
            hidden_pair[1],
            hidden_far[1],
            normed_one[1],
            rscale_one[1],
        )
    )
    grad_first, own_grad = grads[:2], grads[2:]
    (*own_grad, sums), state = tie((*own_grad, sums), marker.state)
    arrived = [lax.ppermute(values, "mp", CORE_SWAP) for values in (*own_grad, sums)]
    (*other_grad, other_sums), marker.state = tie(arrived, mark(state))
    grad_query, grad_key, grad_value, packed = run_back(
        lengths,
        core_arg,
        (
            own_grad[0],
            other_grad[0],
            own_grad[1],
            other_grad[1],
            mixed_a,
            mixed_b,
            *lse,
            output_proj,
            query_b,
            key_b,
            value_b,
            key_tb,
            sums,
            other_sums,
            *inner_sums,
            rows,
        ),
        marker.state,
    )
    marker = Marker()

    def input_part(first):
        span = slice(first, first + half)
        return (
            nt(grad_query[span], query_proj)
            + nt(grad_key[span], key_proj)
            + nt(grad_value[span], value_proj)
        )

    token_pair = []
    for i in range(2):
        other = input_part(i * chunk + half).astype(BF16)
        token_pair.append(pair(input_part(i * chunk), marker.core_swap(other)))
    token_pair, (packed, ffn_parts) = marker.fence(token_pair, (packed, ffn_parts))
    (packed, token_pair), ffn_parts = marker.fence((packed, token_pair), ffn_parts)
    packed_parts = trade(packed)
    token_far = [far_swap(token_pair[i]) for i in range(2)]
    ffn_total = plane_sum(ffn_parts)
    ffn_near = lax.ppermute(ffn_total, "dp", NEAR_SWAP)
    ffn_reduced = (ffn_total.astype(F32) + ffn_near.astype(F32)).astype(BF16)
    ffn_reduced, packed_parts = tie(ffn_reduced, packed_parts)
    packed_reduced = marker.near_sum(plane_sum(packed_parts))
    token_far, packed_reduced = tie(token_far, packed_reduced)
    piece_rows = width // 16
    places = jnp.stack([my_index // 8, (my_index // 2) % 4]).astype(jnp.int32)
    halves = [
        jnp.concatenate([ffn_reduced[:piece_rows], packed_reduced[: piece_rows // 3]], axis=0),
        jnp.concatenate([ffn_reduced[piece_rows:], packed_reduced[piece_rows // 3 :]], axis=0),
    ]
    pieces = [ring_pieces(halves[1], "z"), ring_pieces(halves[0], "y")]
    halves, pieces = marker.fence(halves, pieces)
    other_ring = run_join(places[:1], (halves[1], *pieces[0]), 1)
    one_ring = run_join(places[1:], (halves[0], *pieces[1]), 4)
    pieces = ring_pieces(other_ring, "y")
    other_ring, one_ring = marker.fence(other_ring, one_ring)
    gathered = trade_z(one_ring)
    one_ring, token_far = marker.fence(one_ring, token_far)
    token_own = [
        (grad_first[i] + (token_pair[i].astype(F32) + token_far[i].astype(F32))).astype(BF16)
        for i in range(2)
    ]
    token_other = [lax.ppermute(rows_here, "mp", CORE_SWAP) for rows_here in token_own]
    token_grad = run_settle(core_arg, (*token_own, *token_other))
    closing = finish(marker.state)[0, 0]
    part = piece_rows // 3
    so_far = run_spread_some(places, (other_ring, pieces[0]), piece_rows, part)
    so_far, token_grad = tie(so_far, token_grad)
    *rest, outer_grad = run_spread_rest(
        places, pieces[1:], gathered, so_far, piece_rows, part
    )
    inner_grad, *rest = rest
    cuts = [values.reshape(local_width, width) for values in rest[:4]]
    vectors = rest[4:]
    return (
        loss[0, 0] + closing,
        token_grad,
        cuts[1].T,
        vectors[7],
        cuts[2].T,
        cuts[3].T,
        vectors[8],
        cuts[0],
        vectors[0],
        vectors[1],
        vectors[2],
        inner_grad.reshape(width, width),
        vectors[6],
        outer_grad.reshape(width, width),
        vectors[3],
        vectors[4],
        vectors[5],
    )


def solution(mesh):
    column, row, split = P(None, "mp"), P("mp", None), P("mp")
    placed = (
        (P("dp", None), P("dp"), P())
        + (column, split, column, column, split, row)
        + (P(), P(), P())
        + (column, split, row)
        + (P(), P(), P())
    )
    given = (
        (P(), P("dp", None))
        + (column, split, column, column, split, row)
        + (P(), P(), P())
        + (column, split, row)
        + (P(), P(), P())
    )
    return jax.shard_map(local, mesh=mesh, in_specs=placed, out_specs=given, check_vma=False)
```

```python
import functools
import math

import jax
import jax.numpy as jnp
from jax import lax
from jax.experimental import pallas as pl
from jax.experimental.pallas import tpu as pltpu
from jax.sharding import PartitionSpec as P

HD = 64
EPS_NORM = 1e-06
SOFTMAX_WARMTH = 0.01
NEG_FILL = -1e30
HIGHEST = lax.Precision.HIGHEST
F32 = jnp.float32
BF16 = jnp.bfloat16
QB = 256
KB = 256

CORE_SWAP = [(i, i ^ 1) for i in range(4)]
FAR_SWAP = [(i, i ^ 2) for i in range(4)]
NEAR_SWAP = [(i, i ^ 1) for i in range(32)]
PLANES = [[i * 2 + x for i in range(16)] for x in range(2)]
Z_RINGS = [[i + 8 * z for z in range(4)] for i in range(8)]

SMEM = pl.BlockSpec(memory_space=pltpu.SMEM)
VMEM = pl.BlockSpec(memory_space=pltpu.VMEM)
HBM = pl.BlockSpec(memory_space=pltpu.HBM)


def nn(left, right):
    return lax.dot_general(left, right, (((1,), (0,)), ((), ())), preferred_element_type=F32)


def nt(left, right):
    return lax.dot_general(left, right, (((1,), (1,)), ((), ())), preferred_element_type=F32)


def tn(left, right):
    return lax.dot_general(left, right, (((0,), (0,)), ((), ())), preferred_element_type=F32)


def place_of_block(block, core, rows):
    return ((block % 2) * 2 + block // 2) * QB + core * (rows // 2) & (rows - 1)


def spot_of_keys(j, core, rows):
    place = (j * KB + core * (rows // 2)) & (rows - 1)
    block = place // QB
    return pl.multiple_of(((block % 2) * 2 + block // 2) * QB + place % QB, KB)


def segment_bounds(lengths_ref):
    bounds, total = [], jnp.int32(0)
    for s in range(lengths_ref.shape[0]):
        start = total
        total = total + lengths_ref[s]
        bounds.append((start, total))
    return bounds


def block_span(bounds, first, rows):
    place = first + lax.broadcasted_iota(jnp.int32, (1, QB), 1)
    low, high = first, first + KB
    begin = jnp.full((1, QB), bounds[-1][1], jnp.int32)
    end = jnp.full((1, QB), rows, jnp.int32)
    for start, stop in bounds:
        inside = (place >= start) & (place < stop)
        begin = jnp.where(inside, start, begin)
        end = jnp.where(inside, stop, end)
        touches = (stop > first) & (start < first + QB) & (stop > start)
        low = jnp.where(touches, jnp.minimum(low, start), low)
        high = jnp.where(touches, jnp.maximum(high, stop), high)
    return low // KB, (high + KB - 1) // KB, begin, end


def head_copies(values, heads):
    lane = lax.broadcasted_iota(jnp.int32, values.shape, 1) // HD
    blank = jnp.zeros_like(values)
    return jnp.concatenate([jnp.where(lane == h, values, blank) for h in range(heads)], axis=0)


def span_mask(begin, end, block, heads):
    place = block * KB + lax.broadcasted_iota(jnp.int32, (KB, QB), 0)
    keep = (place >= begin) & (place < end)
    return jnp.concatenate([keep] * heads, axis=1)


def attend(heads, blocks, core, bounds, q_ref, k_ref, vt_ref, mixed_ref, lse_ref, acc_ref):
    rows = k_ref.shape[0]
    for i, block in enumerate(blocks):
        low, high, begin, end = block_span(bounds, place_of_block(block, core, rows), rows)
        stack = head_copies(q_ref[block * QB : (block + 1) * QB, :], heads)
        acc_ref[...] = jnp.zeros(acc_ref.shape, F32)

        def step(j, carry, stack=stack, begin=begin, end=end):
            top, total = carry
            spot = spot_of_keys(j, core, rows)
            scores = nt(k_ref[pl.ds(spot, KB), :], stack)
            scores = jnp.where(span_mask(begin, end, j, heads), scores, NEG_FILL)
            peak = jnp.maximum(top, jnp.max(scores, axis=0, keepdims=True))
            fade = jnp.exp(top - peak)
            probs = jnp.exp(scores - peak)
            total = total * fade + jnp.sum(probs, axis=0, keepdims=True)
            probs = probs.astype(BF16)
            for h in range(heads):
                part = slice(h * QB, (h + 1) * QB)
                span = slice(h * HD, (h + 1) * HD)
                acc_ref[span, :] = acc_ref[span, :] * fade[:, part] + nn(
                    vt_ref[span, pl.ds(spot, KB)], probs[:, part]
                )
            return peak, total

        top = jnp.full((1, heads * QB), NEG_FILL, F32)
        top, total = lax.fori_loop(
            low, high, step, (top, jnp.zeros((1, heads * QB), F32)), unroll=False
        )
        scale = 1.0 / total
        mixed = jnp.concatenate(
            [
                acc_ref[h * HD : (h + 1) * HD, :] * scale[:, h * QB : (h + 1) * QB]
                for h in range(heads)
            ],
            axis=0,
        )
        mixed_ref[i * QB : (i + 1) * QB, :] = mixed.T.astype(BF16)
        lse_ref[i, :, :] = jnp.broadcast_to(top + jnp.log(total), (8, heads * QB))


def fetch(sources, targets, semaphores, order=()):
    copies = [
        pltpu.make_async_copy(source, target, semaphores.at[i])
        for i, (source, target) in enumerate(zip(sources, targets))
    ]
    for i in [*order, *(i for i in range(len(copies)) if i not in order)]:
        copies[i].start()
    return copies


def project(mixed_ref, weights_ref, results, outputs, semaphores):
    results[1][...] = nn(mixed_ref[QB:, :], weights_ref[...]).astype(BF16)
    copies = send_out(results, outputs, semaphores, (1,))
    results[0][...] = nn(mixed_ref[:QB, :], weights_ref[...])
    return copies + send_out(results, outputs, semaphores, (0,))


def attend_first(heads, blocks, lengths_ref, core_ref, *refs):
    sources, outputs, refs = refs[:13], refs[13:25], refs[25:]
    results, targets, refs = refs[:12], refs[12:24], refs[24:]
    acc_ref, semaphores, out_semaphores = refs
    x_ref, q_ref, k_ref, v_ref, kt_ref, vt_ref, mixed_ref, lse_ref = results[:8]
    wqt_ref, wkt_ref, wvt_ref, bq_ref, bv_ref, wo_ref = targets[:6]
    rows = x_ref.shape[0]
    core = core_ref[0]
    copies = fetch(sources[1:], targets, semaphores)
    row_copies = []
    for block in range(rows // QB):
        first = pl.multiple_of(place_of_block(block, core, rows), QB)
        row_copies.append(
            pltpu.make_async_copy(
                sources[0].at[pl.ds(first, QB), :],
                x_ref.at[pl.ds(block * QB, QB), :],
                semaphores.at[12 + block],
            )
        )
        row_copies[-1].start()
    for copy in copies:
        copy.wait()
    query_bias, value_bias = row_of(bq_ref), row_of(bv_ref)
    for block in range(rows // QB):
        row_copies[block].wait()
        part = slice(block * QB, (block + 1) * QB)
        x = x_ref[part, :]
        q = (nt(x, wqt_ref[...]) + query_bias).astype(BF16)
        q_ref[part, :] = q * BF16(0.125)
        k_ref[part, :] = nt(x, wkt_ref[...]).astype(BF16)
        kt_ref[:, part] = nt(wkt_ref[...], x).astype(BF16)
        v = nt(x, wvt_ref[...]) + value_bias
        v_ref[part, :] = v.astype(BF16)
        vt_ref[:, part] = v.T.astype(BF16)
    outgoing = send_out(results, outputs, out_semaphores, range(6))
    bounds = segment_bounds(lengths_ref)
    place = core * (2 * QB) + lax.broadcasted_iota(jnp.int32, (1, QB), 1)
    for i in range(2):
        member = [
            jnp.where((place + i * QB >= start) & (place + i * QB < stop), 1.0, 0.0)
            for start, stop in bounds
        ]
        results[10][i] = jnp.concatenate(member, axis=0)
    lines = [row_of(ref) for ref in targets[6:]]
    results[11][...] = jnp.concatenate(lines + [jnp.zeros((2, lines[0].shape[1]), F32)], axis=0)
    outgoing += send_out(results, outputs, out_semaphores, (10, 11))
    attend(heads, blocks, core, bounds, q_ref, k_ref, vt_ref, mixed_ref, lse_ref, acc_ref)
    outgoing += project(mixed_ref, wo_ref, results[8:], outputs[8:], out_semaphores.at[8:10])
    outgoing += send_out(results, outputs, out_semaphores, (6, 7))
    for copy in outgoing:
        copy.wait()


def attend_more(heads, blocks, lengths_ref, core_ref, *refs):
    sources, outputs, refs = refs[:4], refs[4:8], refs[8:]
    targets, results, refs = refs[:4], refs[4:8], refs[8:]
    acc_ref, semaphores, out_semaphores = refs
    q_ref, k_ref, vt_ref, wo_ref = targets
    mixed_ref, lse_ref = results[:2]
    for copy in fetch(sources, targets, semaphores):
        copy.wait()
    bounds = segment_bounds(lengths_ref)
    attend(heads, blocks, core_ref[0], bounds, q_ref, k_ref, vt_ref, mixed_ref, lse_ref, acc_ref)
    outgoing = project(mixed_ref, wo_ref, results[2:], outputs[2:], out_semaphores.at[2:])
    outgoing += send_out(results, outputs, out_semaphores, (0, 1))
    for copy in outgoing:
        copy.wait()


def attend_back(heads, inputs, lengths_ref, core_ref, *refs):
    sources, refs = refs[:inputs], refs[inputs:]
    outputs, refs = refs[:4], refs[4:]
    gq_ref, gk_ref, gv_ref, pack_ref = refs[:4]
    dk_ref, dv_ref, dqt_ref, wo_acc_ref, semaphores, out_semaphores = refs[4:10]
    targets = refs[10:]
    copies = fetch(sources, targets, semaphores, (10, 9, 11, 12, 0, 4, 8, 6, 1, 2, 3, 5, 7))
    grads = targets[0:4]
    mixed = targets[4:6]
    lses = targets[6:8]
    wo_ref, q_ref, k_ref, v_ref, kt_ref = targets[8:13]
    own_sums, other_sums, inner_a, inner_b, x_ref = targets[13:]
    rows, width = q_ref.shape
    core = core_ref[0]
    bounds = segment_bounds(lengths_ref)
    dk_ref[...] = jnp.zeros(dk_ref.shape, F32)
    dv_ref[...] = jnp.zeros(dv_ref.shape, F32)
    lane = lax.broadcasted_iota(jnp.int32, (8, width), 1) // HD
    which = (lane == lax.broadcasted_iota(jnp.int32, (8, width), 0)).astype(F32).astype(BF16)
    for i in (0, 4, 6, 8, 9, 10, 11, 12):
        copies[i].wait()
    for block in range(rows // QB):
        if block > 0:
            copies[block].wait()
        if block == 2:
            copies[5].wait()
            copies[7].wait()
        low, high, begin, end = block_span(bounds, place_of_block(block, core, rows), rows)
        part = slice(block * QB, (block + 1) * QB)
        own = slice(block % 2 * QB, block % 2 * QB + QB)
        grad_attn = grads[block][...]
        mixed_here = mixed[block // 2][own, :]
        outer = tn(mixed_here, grad_attn)
        wo_acc_ref[...] = outer if block == 0 else wo_acc_ref[...] + outer
        grad_mixed = nt(grad_attn, wo_ref[...]).astype(BF16)
        product = grad_mixed.astype(F32) * mixed_here.astype(F32)
        sums = sum(nt(which, part) for part in in_three(product)[:2])
        delta = jnp.concatenate([sums[h : h + 1, :] for h in range(heads)], axis=1)
        lse = lses[block // 2][block % 2, 0:1, :]
        q_stack = head_copies(q_ref[part, :], heads)
        g_stack = head_copies(grad_mixed, heads)
        dqt_ref[...] = jnp.zeros(dqt_ref.shape, F32)

        def step(
            j, carry, delta=delta, lse=lse, q_stack=q_stack, g_stack=g_stack, begin=begin, end=end
        ):
            here = pl.ds(spot_of_keys(j, core, rows), KB)
            scores = nt(k_ref[here, :], q_stack)
            scores = jnp.where(span_mask(begin, end, j, heads), scores, NEG_FILL)
            probs = jnp.exp(scores - lse)
            grad = (probs * (nt(v_ref[here, :], g_stack) - delta)).astype(BF16)
            dv_ref[here, :] += nn(probs.astype(BF16), g_stack)
            dk_ref[here, :] += nn(grad, q_stack)
            for h in range(heads):
                span = slice(h * HD, (h + 1) * HD)
                dqt_ref[span, :] += nn(kt_ref[span, here], grad[:, h * QB : (h + 1) * QB])
            return carry

        lax.fori_loop(low, high, step, 0, unroll=False)
        gq_ref[part, :] = (dqt_ref[...].T * 0.125).astype(BF16)
    gk_ref[...] = dk_ref[...].astype(BF16)
    gv_ref[...] = dv_ref[...].astype(BF16)
    for copy in copies[13:]:
        copy.wait()
    outgoing = fetch(refs[:3], outputs[:3], out_semaphores)
    sums = [jnp.sum(ref[...].astype(F32), axis=0, keepdims=True) for ref in (gq_ref, gv_ref)]
    blank = jnp.zeros((1, 256 - width), F32)
    tail = jnp.concatenate([sums[0], blank, sums[1], blank, jnp.zeros((1, 256), F32)], axis=1)
    inner = row_of(inner_a) + row_of(inner_b)
    paired = own_sums[0:6, :] + other_sums[0:6, :]
    small = [paired, inner, tail, jnp.zeros((8, tail.shape[1]), F32)]
    small = jnp.concatenate(small, axis=0).astype(BF16)
    piece = pack_ref.shape[1] - 16
    per = width // piece
    for m, source in enumerate((None, gq_ref, gk_ref, gv_ref)):
        total = wo_acc_ref[...] if source is None else tn(source[...], x_ref[...])
        for t in range(per):
            cut = total[t * piece : (t + 1) * piece, :].astype(BF16)
            pack_ref[m * per + t, 0:piece, :] = cut
            pack_ref[m * per + t, piece:, :] = small if m + t == 0 else jnp.zeros_like(small)
        here = pl.ds(m * per, per)
        copy = pltpu.make_async_copy(
            pack_ref.at[here], outputs[3].at[here], out_semaphores.at[3 + m]
        )
        copy.start()
        outgoing.append(copy)
    for copy in outgoing:
        copy.wait()


def shaped(shape, dtype):
    return jax.ShapeDtypeStruct(shape, dtype)


PARAMS = pltpu.CompilerParams(vmem_limit_bytes=60 << 20)
SMALL = pltpu.CompilerParams(vmem_limit_bytes=60 << 20)
SHARED = pltpu.CompilerParams(vmem_limit_bytes=24 << 20)
COST = pl.CostEstimate(flops=1024, bytes_accessed=1024, transcendentals=0)


def buffers(arrays):
    return [pltpu.VMEM(array.shape, array.dtype) for array in arrays]


def attend_shapes(count, heads, width):
    rows = count * QB
    return (
        shaped((rows, heads * HD), BF16),
        shaped((count, 8, heads * QB), F32),
        shaped((rows // 2, width), F32),
        shaped((rows // 2, width), BF16),
    )


def run_first(lengths, core, tokens, weights, blocks):
    rows, width = tokens.shape
    local_width = weights[0].shape[0]
    heads = local_width // HD
    outs = (
        (shaped(tokens.shape, BF16),)
        + (shaped((rows, local_width), BF16),) * 3
        + (shaped((local_width, rows), BF16),) * 2
        + attend_shapes(len(blocks), heads, width)
        + (shaped((2, lengths.shape[0], QB), F32), shaped((8, width), F32))
    )
    return pl.pallas_call(
        functools.partial(attend_first, heads, blocks),
        out_shape=outs,
        in_specs=[SMEM] * 2 + [HBM] * 13,
        out_specs=(HBM,) * 12,
        scratch_shapes=buffers(outs)
        + buffers(weights)
        + [pltpu.VMEM((local_width, QB), F32)]
        + [pltpu.SemaphoreType.DMA((12 + rows // QB,)), pltpu.SemaphoreType.DMA((12,))],
        compiler_params=PARAMS,
        name="attend_first",
        cost_estimate=COST,
    )(lengths, core, tokens, *weights)


def run_more(lengths, core, arrays, blocks):
    rows, local_width = arrays[0].shape
    heads = local_width // HD
    outs = attend_shapes(len(blocks), heads, arrays[3].shape[1])
    return pl.pallas_call(
        functools.partial(attend_more, heads, blocks),
        out_shape=outs,
        in_specs=[SMEM] * 2 + [HBM] * 4,
        out_specs=(HBM,) * 4,
        scratch_shapes=buffers(arrays)
        + buffers(outs)
        + [pltpu.VMEM((local_width, QB), F32)]
        + [pltpu.SemaphoreType.DMA((4,)), pltpu.SemaphoreType.DMA((4,))],
        compiler_params=PARAMS,
        name="attend_more",
        cost_estimate=COST,
    )(lengths, core, *arrays)


def run_back(lengths, core, arrays):
    wo, q, x = arrays[8], arrays[9], arrays[-1]
    rows, width = q.shape
    heads = width // HD
    piece = 4 * width // 16
    outs = (shaped((rows, width), BF16),) * 3 + (shaped((16, piece + 16, x.shape[1]), BF16),)
    return pl.pallas_call(
        functools.partial(attend_back, heads, len(arrays)),
        out_shape=outs,
        in_specs=[SMEM] * 2 + [HBM] * len(arrays),
        out_specs=(HBM,) * 4,
        scratch_shapes=buffers(outs)
        + [pltpu.VMEM((rows, width), F32)] * 2
        + [pltpu.VMEM((width, QB), F32), pltpu.VMEM(wo.shape, F32)]
        + [pltpu.SemaphoreType.DMA((len(arrays),)), pltpu.SemaphoreType.DMA((7,))]
        + buffers(arrays),
        compiler_params=PARAMS,
        name="attend_back",
        cost_estimate=COST,
    )(lengths, core, *arrays)


def mark_kernel(source_ref, target_ref):
    del source_ref, target_ref


def mark(values):
    return pl.pallas_call(
        mark_kernel,
        out_shape=shaped(values.shape, values.dtype),
        in_specs=[HBM],
        out_specs=HBM,
        compiler_params=pltpu.CompilerParams(vmem_limit_bytes=1 << 20),
        name="mark",
        cost_estimate=pl.CostEstimate(flops=1 << 36, bytes_accessed=1 << 10, transcendentals=0),
    )(values)


def finish_kernel(source_ref, target_ref):
    del source_ref
    target_ref[...] = jnp.zeros(target_ref.shape, F32)


def finish(values):
    return pl.pallas_call(
        finish_kernel,
        out_shape=shaped(values.shape, values.dtype),
        in_specs=[HBM],
        out_specs=VMEM,
        compiler_params=pltpu.CompilerParams(vmem_limit_bytes=1 << 20),
        name="finish",
        cost_estimate=COST,
    )(values)


def no_kernel(target_ref):
    del target_ref


def room(shape):
    return pl.pallas_call(
        no_kernel,
        out_shape=shaped(shape, BF16),
        out_specs=HBM,
        compiler_params=pltpu.CompilerParams(vmem_limit_bytes=1 << 20),
        name="room",
        cost_estimate=COST,
    )()


def row_of(ref):
    return ref[...].astype(F32).reshape(1, -1)


def in_three(values):
    high = values.astype(BF16)
    rest = values - high.astype(F32)
    middle = rest.astype(BF16)
    return high, middle, (rest - middle.astype(F32)).astype(BF16)


def norm_step(grad, normed, rscale, gain):
    scaled = grad * gain
    first_mean = jnp.mean(scaled, axis=1, keepdims=True)
    cross_mean = jnp.mean(scaled * normed, axis=1, keepdims=True)
    return rscale * (scaled - first_mean - normed * cross_mean)


def column_of(ref):
    row = ref[...].reshape(1, -1)
    return jnp.broadcast_to(row, (128, row.shape[1])).T[:, 0:1]


def column_sum(values):
    return jnp.sum(values, axis=0, keepdims=True)


def send_out(results, outputs, semaphores, which):
    copies = [
        pltpu.make_async_copy(results[k], outputs[k], semaphores.at[k]) for k in which
    ]
    for copy in copies:
        copy.start()
    return copies


def loss_back(lengths_ref, place_ref, *refs):
    sources, outputs, refs = refs[:9], refs[9:15], refs[15:]
    targets, results = refs[:9], refs[9:15]
    coef_ref, turned_ref, semaphores, out_semaphores = refs[15:]
    copies = fetch(sources, targets, semaphores)
    piece_ref, swapped_ref, pooled_ref, match_ref, gain_ref = targets[:5]
    core, index = place_ref[0], place_ref[1]
    bounds = segment_bounds(lengths_ref)
    for copy in copies[:5]:
        copy.wait()
    first = core == 0
    queries = jnp.where(first, piece_ref[...], swapped_ref[...])
    passages = jnp.where(first, swapped_ref[...], piece_ref[...])
    count = queries.shape[0]
    own = pooled_ref.shape[0] // 2
    similarity = nt(queries, passages) / SOFTMAX_WARMTH
    match = match_ref[...].reshape(1, -1)
    match = match == lax.broadcasted_iota(jnp.int32, (count, count), 0)
    top = jnp.max(similarity, axis=1, keepdims=True)
    lse = top + jnp.log(jnp.sum(jnp.exp(similarity - top), axis=1, keepdims=True))
    positive = jnp.sum(jnp.where(match, similarity, 0.0), axis=1, keepdims=True)
    loss = jnp.sum(lse - positive, axis=0, keepdims=True) / count
    results[5][...] = jnp.broadcast_to(loss, results[5].shape)
    coef = (jnp.exp(similarity - lse) - match.astype(F32)) * (1.0 / (count * SOFTMAX_WARMTH))
    coef_ref[...] = coef
    turned_ref[...] = coef.T
    here = pl.ds(pl.multiple_of(index * own, own), own)
    grad_query = sum(nn(part, passages) for part in in_three(coef_ref[here, :]))
    grad_passage = sum(nn(part, queries) for part in in_three(turned_ref[here, :]))
    grad_unit = jnp.concatenate([grad_query, grad_passage], axis=0)
    pooled = pooled_ref[...]
    rscale = lax.rsqrt(jnp.sum(pooled * pooled, axis=1, keepdims=True) + EPS_NORM)
    inner = jnp.sum(pooled * grad_unit, axis=1, keepdims=True)
    grad_pooled = rscale * grad_unit - rscale * rscale * rscale * inner * pooled
    seqs = 2 * own
    grad_pooled = jnp.concatenate(
        [grad_pooled, jnp.zeros((128 - seqs, grad_pooled.shape[1]), F32)], axis=0
    )
    parts = in_three(grad_pooled)
    lane = lax.broadcasted_iota(jnp.int32, (1, 128), 1)
    begin = end = jnp.zeros((1, 128), jnp.int32)
    for seq, (start, stop) in enumerate(bounds):
        begin = jnp.where(lane == seq, start, begin)
        end = jnp.where(lane == seq, stop, end)
    gain = row_of(gain_ref)
    sums = [0.0, 0.0, 0.0]
    outgoing = []
    for i in range(2):
        copies[5 + 2 * i].wait()
        copies[6 + 2 * i].wait()
        normed = targets[5 + 2 * i][...]
        place = core * (2 * QB) + i * QB + lax.broadcasted_iota(jnp.int32, (QB, 128), 0)
        member = jnp.where((place >= begin) & (place < end), 1.0, 0.0).astype(BF16)
        grad = sum(nn(member, part) for part in parts)
        second = norm_step(grad, normed, column_of(targets[6 + 2 * i]), gain)
        rounded = second.astype(BF16)
        results[i][...] = second
        results[2 + i][...] = rounded
        for k, values in enumerate((rounded.astype(F32), grad * normed, grad)):
            sums[k] = sums[k] + column_sum(values)
        outgoing += send_out(results, outputs, out_semaphores, (2 + i, i))
    results[4][...] = jnp.concatenate(sums + [jnp.zeros((5, sums[0].shape[1]), F32)], axis=0)
    outgoing += send_out(results, outputs, out_semaphores, (4, 5))
    for copy in outgoing:
        copy.wait()


def norm_back(*refs):
    sources, outputs, refs = refs[:12], refs[12:17], refs[17:]
    targets, results = refs[:12], refs[12:17]
    semaphores, out_semaphores = refs[17:]
    copies = fetch(sources, targets, semaphores)
    copies[0].wait()
    copies[1].wait()
    gain = row_of(targets[0])
    sums = [0.0, 0.0, 0.0]
    outgoing = []
    for i in range(2):
        for copy in copies[2 + 5 * i : 7 + 5 * i]:
            copy.wait()
        second, pair_here, far, normed, rscale = targets[2 + 5 * i : 7 + 5 * i]
        grad = second[...] + (pair_here[...].astype(F32) + far[...].astype(F32))
        normed = normed[...]
        first = norm_step(grad, normed, column_of(rscale), gain)
        rounded = first.astype(BF16)
        results[i][...] = first
        results[2 + i][...] = rounded
        for k, values in enumerate((rounded.astype(F32), grad * normed, grad)):
            sums[k] = sums[k] + column_sum(values)
        outgoing += send_out(results, outputs, out_semaphores, (2 + i, i))
    blank = jnp.zeros((2, sums[0].shape[1]), F32)
    results[4][...] = jnp.concatenate(sums + [targets[1][0:3, :], blank], axis=0)
    outgoing += send_out(results, outputs, out_semaphores, (4,))
    for copy in outgoing:
        copy.wait()


STEPS = (0, 2, 1, 3)


def join(copies_of_each, place_ref, *refs):
    sources, output, semaphores = refs[:4], refs[4], refs[5]
    copies = []
    for k in range(4):
        spot = (place_ref[0] + 4 - STEPS[k]) % 4
        for r in range(copies_of_each):
            goal = output.at[spot] if copies_of_each == 1 else output.at[r, spot]
            semaphore = semaphores.at[k * copies_of_each + r]
            copies.append(pltpu.make_async_copy(sources[k], goal, semaphore))
            copies[-1].start()
    for copy in copies:
        copy.wait()


def place_block(piece, part, block_ref, spot, outputs, buffers_, semaphores, first):
    inner, cuts = buffers_
    inner[...] = block_ref[:, :piece, :].astype(F32)
    cuts[...] = block_ref[:, piece : 2 * piece - part, :].astype(F32)
    copies = [pltpu.make_async_copy(inner, outputs[0].at[:, spot], semaphores.at[first])]
    for m in range(4):
        goal = outputs[1 + m].at[spot, pl.ds(part, piece - part), :]
        copies.append(pltpu.make_async_copy(cuts.at[m], goal, semaphores.at[first + 1 + m]))
    for copy in copies:
        copy.start()
    return copies


def place_vectors(piece, part, block_ref, spot, outputs, vectors, semaphores, first):
    @pl.when(spot == 0)
    def _():
        small = block_ref[0, 2 * piece - part :, :].astype(F32)
        for k in range(7):
            vectors[k][...] = small[k : k + 1, :].reshape(-1)
        count = vectors[7].shape[0]
        for k in range(2):
            vectors[7 + k][...] = small[7:8, 256 * k : 256 * k + count].reshape(-1)
        copies = [
            pltpu.make_async_copy(vectors[k], outputs[5 + k], semaphores.at[first + k])
            for k in range(9)
        ]
        for copy in copies:
            copy.start()
        for copy in copies:
            copy.wait()


def spread_some(piece, part, count, place_ref, *refs):
    sources, outputs, refs = refs[:count], refs[count : count + 14], refs[count + 14 :]
    blocks, refs = refs[:count], refs[count:]
    buffers_, vectors, refs = refs[: 2 * count], refs[2 * count : 2 * count + 9], refs[-2:]
    arrivals = fetch(sources, blocks, refs[0])
    outgoing, spots = [], []
    for k in range(count):
        arrivals[k].wait()
        spots.append((place_ref[1] + 4 - STEPS[k]) % 4)
        outgoing += place_block(
            piece, part, blocks[k], spots[k], outputs, buffers_[2 * k : 2 * k + 2], refs[1], 5 * k
        )
    for k in range(count):
        place_vectors(piece, part, blocks[k], spots[k], outputs, vectors, refs[1], 5 * count)
    for copy in outgoing:
        copy.wait()


def spread_rest(piece, part, place_ref, *refs):
    sources, outputs, refs = refs[:3], refs[17:32], refs[32:]
    blocks, by_z, refs = refs[:2], refs[2], refs[3:]
    buffers_, outer, heads, vectors, refs = refs[:4], refs[4], refs[5], refs[6:15], refs[15:]
    semaphores, out_semaphores = refs
    arrivals = fetch(sources, (*blocks, by_z), semaphores)
    outgoing, spots = [], []
    for k in range(2):
        spots.append((place_ref[1] + 4 - STEPS[2 + k]) % 4)
        arrivals[k].wait()
        outgoing += place_block(
            piece,
            part,
            blocks[k],
            spots[k],
            outputs,
            buffers_[2 * k : 2 * k + 2],
            out_semaphores,
            5 * k,
        )
    arrivals[2].wait()
    outer[...] = by_z[:, :, :piece, :].astype(F32)
    copies = [pltpu.make_async_copy(outer, outputs[14], out_semaphores.at[10])]
    copies[0].start()
    heads[...] = by_z[:, :, piece:, :].astype(F32)
    for m in range(4):
        goal = outputs[1 + m].at[:, pl.ds(0, part), :]
        copies.append(pltpu.make_async_copy(heads.at[m], goal, out_semaphores.at[11 + m]))
        copies[-1].start()
    for k in range(2):
        place_vectors(piece, part, blocks[k], spots[k], outputs, vectors, out_semaphores, 15)
    for copy in outgoing + copies:
        copy.wait()


def run_loss(lengths, place, arrays):
    rows, width = arrays[5].shape
    count = arrays[0].shape[0]
    outs = (
        (shaped((rows, width), F32),) * 2
        + (shaped((rows, width), BF16),) * 2
        + (shaped((8, width), F32), shaped((8, 128), F32))
    )
    return pl.pallas_call(
        loss_back,
        out_shape=outs,
        in_specs=[SMEM] * 2 + [HBM] * 9,
        out_specs=(HBM,) * 6,
        scratch_shapes=buffers(arrays)
        + buffers(outs)
        + [pltpu.VMEM((count, count), F32)] * 2
        + [pltpu.SemaphoreType.DMA((9,)), pltpu.SemaphoreType.DMA((6,))],
        compiler_params=SHARED,
        name="loss_back",
        cost_estimate=COST,
    )(lengths, place, *arrays)


def run_norm(arrays):
    rows, width = arrays[2].shape
    outs = (
        (shaped((rows, width), F32),) * 2
        + (shaped((rows, width), BF16),) * 2
        + (shaped((8, width), F32),)
    )
    return pl.pallas_call(
        norm_back,
        out_shape=outs,
        in_specs=[HBM] * 12,
        out_specs=(HBM,) * 5,
        scratch_shapes=buffers(arrays)
        + buffers(outs)
        + [pltpu.SemaphoreType.DMA((12,)), pltpu.SemaphoreType.DMA((5,))],
        compiler_params=SMALL,
        name="norm_back",
        cost_estimate=COST,
    )(*arrays)


def run_join(place, pieces, copies_of_each):
    lead = (4,) if copies_of_each == 1 else (copies_of_each, 4)
    return pl.pallas_call(
        functools.partial(join, copies_of_each),
        out_shape=shaped(lead + pieces[0].shape, BF16),
        in_specs=[SMEM] + [HBM] * 4,
        out_specs=HBM,
        scratch_shapes=[pltpu.SemaphoreType.DMA((4 * copies_of_each,))],
        compiler_params=pltpu.CompilerParams(vmem_limit_bytes=1 << 20),
        name="join",
        cost_estimate=COST,
    )(place, *pieces)


def settle(core_ref, *refs):
    sources, output, semaphores = refs[:4], refs[4], refs[5]
    copies = []
    for k in range(4):
        first = (k // 2 + core_ref[0]) % 2 * (2 * QB) + k % 2 * QB
        spot = pl.ds(pl.multiple_of(first, QB), QB)
        copies.append(pltpu.make_async_copy(sources[k], output.at[spot, :], semaphores.at[k]))
        copies[-1].start()
    for copy in copies:
        copy.wait()


def run_settle(core, parts):
    rows, width = parts[0].shape
    return pl.pallas_call(
        settle,
        out_shape=shaped((4 * rows, width), BF16),
        in_specs=[SMEM] + [HBM] * 4,
        out_specs=HBM,
        scratch_shapes=[pltpu.SemaphoreType.DMA((4,))],
        compiler_params=pltpu.CompilerParams(vmem_limit_bytes=1 << 20),
        name="settle",
        cost_estimate=COST,
    )(core, *parts)


def spread_shapes(piece, width):
    shapes = [(4, 4, piece, width)] + [(4, piece, width)] * 4
    return shapes + [(width,)] * 7 + [(4 * piece,)] * 2


def run_spread_some(places, blocks, piece, part):
    width = blocks[0].shape[2]
    shapes = spread_shapes(piece, width)
    count = len(blocks)
    pair_of = [pltpu.VMEM((4, piece, width), F32), pltpu.VMEM((4, piece - part, width), F32)]
    return pl.pallas_call(
        functools.partial(spread_some, piece, part, count),
        out_shape=[shaped(shape, F32) for shape in shapes],
        in_specs=[SMEM] + [HBM] * count,
        out_specs=[HBM] * 14,
        scratch_shapes=buffers(blocks)
        + pair_of * count
        + [pltpu.VMEM(shape, F32) for shape in shapes[5:]]
        + [pltpu.SemaphoreType.DMA((count,)), pltpu.SemaphoreType.DMA((5 * count + 9,))],
        compiler_params=SHARED,
        name="spread_some",
        cost_estimate=COST,
    )(places, *blocks)


def run_spread_rest(places, blocks, gathered, so_far, piece, part):
    width = gathered.shape[3]
    shapes = spread_shapes(piece, width)
    outer = (4, 4, piece, width)
    pair_of = [pltpu.VMEM((4, piece, width), F32), pltpu.VMEM((4, piece - part, width), F32)]
    return pl.pallas_call(
        functools.partial(spread_rest, piece, part),
        out_shape=[shaped(shape, F32) for shape in shapes + [outer]],
        in_specs=[SMEM] + [HBM] * 17,
        out_specs=[HBM] * 15,
        input_output_aliases={4 + k: k for k in range(14)},
        scratch_shapes=buffers((*blocks, gathered))
        + pair_of * 2
        + [pltpu.VMEM(outer, F32), pltpu.VMEM((4, 4, part, width), F32)]
        + [pltpu.VMEM(shape, F32) for shape in shapes[5:]]
        + [pltpu.SemaphoreType.DMA((3,)), pltpu.SemaphoreType.DMA((24,))],
        compiler_params=SHARED,
        name="spread_rest",
        cost_estimate=COST,
    )(places, *blocks, gathered, *so_far)


def trade(values):
    return lax.all_to_all(
        values, "dp", split_axis=0, concat_axis=0, axis_index_groups=PLANES, tiled=True
    )


def share(values):
    spread_out = jnp.broadcast_to(values[None], (32,) + values.shape)
    return lax.all_to_all(spread_out, "dp", split_axis=0, concat_axis=0, tiled=True)


def trade_z(values):
    return lax.all_to_all(
        values, "dp", split_axis=0, concat_axis=0, axis_index_groups=Z_RINGS, tiled=True
    )


def ring_shift(axis, step):
    pairs = []
    for i in range(32):
        z, y, x = i // 8, (i // 2) % 4, i % 2
        z, y = ((z + step) % 4, y) if axis == "z" else (z, (y + step) % 4)
        pairs.append((i, (z * 4 + y) * 2 + x))
    return pairs


def ring_pieces(values, axis):
    return [lax.ppermute(values, "dp", ring_shift(axis, step)) for step in STEPS[1:]]


def tie(values, others):
    return lax.optimization_barrier((values, others))


class Marker:
    def __init__(self):
        self.state = jnp.zeros((8, 128), F32)

    def fence(self, ready, later):
        ready, state = tie(ready, self.state)
        later, self.state = tie(later, mark(state))
        return ready, later

    def moved(self, values, axis, pairs):
        values, state = tie(values, self.state)
        arrived, self.state = tie(lax.ppermute(values, axis, pairs), mark(state))
        return arrived

    def core_swap(self, values):
        return self.moved(values, "mp", CORE_SWAP)

    def near_swap(self, values):
        return self.moved(values, "dp", NEAR_SWAP)

    def both(self, own):
        return jnp.concatenate([own, self.core_swap(own)], axis=0)

    def near_sum(self, total):
        return (total.astype(F32) + self.near_swap(total).astype(F32)).astype(BF16)


def plane_sum(parts):
    return jnp.sum(parts.astype(F32), axis=0).astype(BF16)


def far_swap(values):
    return lax.ppermute(values, "mp", FAR_SWAP)


def norm_forward(values, gain_vec, shift_vec):
    average = jnp.mean(values, axis=-1, keepdims=True)
    centred = values - average
    rscale = lax.rsqrt(jnp.mean(centred * centred, axis=-1, keepdims=True) + EPS_NORM)
    normed = centred * rscale
    return (normed * gain_vec + shift_vec, normed, rscale[:, 0])


def gelu_and_slope(upper):
    below = 0.5 * (1.0 + lax.erf(upper * math.sqrt(0.5)))
    density = jnp.exp(-0.5 * upper * upper) * (1.0 / math.sqrt(2.0 * math.pi))
    return (upper * below).astype(BF16), (below + upper * density).astype(BF16)


def local(
    tokens,
    lengths,
    pair_index,
    query_proj,
    query_bias,
    key_proj,
    value_proj,
    value_bias,
    output_proj,
    output_bias,
    attn_gain,
    attn_shift,
    inner_proj,
    inner_bias,
    outer_proj,
    outer_bias,
    final_gain,
    final_shift,
):
    row_count, width = tokens.shape
    chunk = row_count // 2
    half = chunk // 2
    seq_count = lengths.shape[0]
    pair_count = seq_count // 2
    overall_pair_count = pair_index.shape[0]
    local_width = query_proj.shape[1]
    core = lax.axis_index("mp") % 2
    my_index = lax.axis_index("dp")
    marker = Marker()
    core_arg = jnp.reshape(core, (1,)).astype(jnp.int32)
    vectors = (output_bias, attn_gain, attn_shift, outer_bias, final_gain, final_shift)
    query_t, key_t, value_t = query_proj.T, key_proj.T, value_proj.T

    weights = (query_t, key_t, value_t, query_bias, value_bias, output_proj, *vectors)
    first = run_first(lengths, core_arg, tokens, weights, (0, 1))
    rows, query_b, key_b, value_b, key_tb, value_tb, mixed_a, lse_a = first[:8]
    attn_own_a, attn_other_a, members, vectors = first[8:]

    def own_and_other(values, weights):
        return nn(values[:half], weights), nn(values[half:], weights).astype(BF16)

    def pair(own, arrived):
        return (own + arrived.astype(F32)).astype(BF16)

    def first_norm(index, pair_here, far):
        attn_full = pair_here.astype(F32) + far.astype(F32) + output_bias
        own_tokens = rows[index * chunk : index * chunk + half].astype(F32)
        return norm_forward(own_tokens + attn_full, attn_gain_f, attn_shift_f)

    def feed_forward(own_hidden):
        whole = marker.both(own_hidden)
        act, slope = gelu_and_slope(nn(whole, inner_proj) + inner_bias.astype(F32))
        return whole, act, slope

    def last_norm(hidden, pair_here, far):
        ffn_full = pair_here.astype(F32) + far.astype(F32) + outer_bias
        return norm_forward(hidden + ffn_full, final_gain_f, final_shift_f)

    attn_pair_a = pair(attn_own_a, marker.core_swap(attn_other_a))
    attn_far_a = far_swap(attn_pair_a)
    output_bias, attn_gain_f, attn_shift_f = vectors[0], vectors[1], vectors[2]
    outer_bias, final_gain_f, final_shift_f = vectors[3], vectors[4], vectors[5]
    late_query, late_pair = tie(query_b, attn_pair_a)
    mixed_b, lse_b, attn_own_b, attn_other_b = run_more(
        lengths, core_arg, (late_query, key_b, value_tb, output_proj), (2, 3)
    )
    attn_pair_b = pair(attn_own_b, marker.core_swap(attn_other_b))
    attn_far_b = far_swap(attn_pair_b)
    attn_far_a, attn_pair_b = tie(attn_far_a, attn_pair_b)
    hidden_a, normed_one_a, rscale_one_a = first_norm(0, late_pair, attn_far_a)
    own_hidden_a = hidden_a.astype(BF16)
    hidden_ab, act_a, slope_a = feed_forward(own_hidden_a)
    ffn_own_a, ffn_other_a = own_and_other(act_a, outer_proj)
    ffn_pair_a = pair(ffn_own_a, marker.core_swap(ffn_other_a))
    attn_far_b, ffn_pair_late = tie(attn_far_b, ffn_pair_a)
    ffn_far_a = far_swap(ffn_pair_a)
    hidden_b, normed_one_b, rscale_one_b = first_norm(1, attn_pair_b, attn_far_b)
    own_hidden_b = hidden_b.astype(BF16)
    hidden_bb, act_b, slope_b = feed_forward(own_hidden_b)
    ffn_own_b, ffn_other_b = own_and_other(act_b, outer_proj)
    ffn_pair_b = pair(ffn_own_b, marker.core_swap(ffn_other_b))
    ffn_pair_b, ffn_far_a = marker.fence(ffn_pair_b, ffn_far_a)
    final_a, normed_two_a, rscale_two_a = last_norm(hidden_a, ffn_pair_late, ffn_far_a)
    pooled_a = jnp.dot(members[0], final_a, precision=HIGHEST)
    final_b, normed_two_b, rscale_two_b = last_norm(hidden_b, ffn_pair_b, far_swap(ffn_pair_b))
    pooled_part = pooled_a + jnp.dot(members[1], final_b, precision=HIGHEST)
    lse = (lse_a, lse_b)
    hidden_whole, act, slope = (hidden_ab, hidden_bb), (act_a, act_b), (slope_a, slope_b)
    normed_one, rscale_one = (normed_one_a, normed_one_b), (rscale_one_a, rscale_one_b)
    normed_two, rscale_two = (normed_two_a, normed_two_b), (rscale_two_a, rscale_two_b)
    pooled = pooled_part + marker.core_swap(pooled_part)
    pool_rscale = lax.rsqrt(jnp.sum(pooled * pooled, axis=-1, keepdims=True) + EPS_NORM)
    unit_b = (pooled * pool_rscale).astype(BF16)

    piece = lax.dynamic_slice_in_dim(unit_b, core * pair_count, pair_count, 0)
    piece = share(piece).reshape(overall_pair_count, width)
    place_arg = jnp.stack([core, my_index]).astype(jnp.int32)
    *grads, last_sums, loss = run_loss(
        lengths,
        place_arg,
        (
            piece,
            marker.core_swap(piece),
            pooled,
            pair_index,
            final_gain,
            normed_two[0],
            rscale_two[0],
            normed_two[1],
            rscale_two[1],
        ),
    )
    grad_second, own_grad = grads[:2], grads[2:]

    inner_sums, grad_ffn, grad_up, hidden_other, outer_sums = [], [], [], [], []
    for i in range(2):
        grad_ffn.append(marker.both(own_grad[i]))
        grad_up.append((nt(grad_ffn[i], outer_proj) * slope[i].astype(F32)).astype(BF16))
        inner_sums.append(jnp.sum(grad_up[i].astype(F32), axis=0))
        other = nt(grad_up[i][half:], inner_proj).astype(BF16)
        late_act, other = tie(act[i], other)
        outer_sums.append(tn(late_act, grad_ffn[i]))
        swap = marker.core_swap if i else lambda rows_here: lax.ppermute(rows_here, "mp", CORE_SWAP)
        arrived, outer_sums[i] = tie(swap(other), outer_sums[i])
        hidden_other.append(arrived)
    hidden_pair = [pair(nt(grad_up[i][:half], inner_proj), hidden_other[i]) for i in range(2)]
    hidden_far = [far_swap(hidden_pair[i]) for i in range(2)]
    late_hidden, hidden_pair = tie(hidden_whole, hidden_pair)
    outer_part = (outer_sums[0] + outer_sums[1]).astype(BF16).reshape(16, -1, width)
    inner_part = tn(late_hidden[0], grad_up[0]) + tn(late_hidden[1], grad_up[1])
    inner_part = inner_part.astype(BF16).reshape(16, -1, width)
    ffn_pack = room((16, width // 8, width))
    ffn_pack = lax.dynamic_update_slice(ffn_pack, outer_part, (0, 0, 0))
    ffn_pack = lax.dynamic_update_slice(ffn_pack, inner_part, (0, width // 16, 0))
    ffn_pack, hidden_far = marker.fence(ffn_pack, hidden_far)
    ffn_parts = trade(ffn_pack)

    *grads, sums = run_norm(
        (
            attn_gain,
            last_sums,
            grad_second[0],
            hidden_pair[0],
            hidden_far[0],
            normed_one[0],
            rscale_one[0],
            grad_second[1],
            hidden_pair[1],
            hidden_far[1],
            normed_one[1],
            rscale_one[1],
        )
    )
    grad_first, own_grad = grads[:2], grads[2:]
    (*own_grad, sums), state = tie((*own_grad, sums), marker.state)
    arrived = [lax.ppermute(values, "mp", CORE_SWAP) for values in (*own_grad, sums)]
    (*other_grad, other_sums), marker.state = tie(arrived, mark(state))
    grad_query, grad_key, grad_value, packed = run_back(
        lengths,
        core_arg,
        (
            own_grad[0],
            other_grad[0],
            own_grad[1],
            other_grad[1],
            mixed_a,
            mixed_b,
            *lse,
            output_proj,
            query_b,
            key_b,
            value_b,
            key_tb,
            sums,
            other_sums,
            *inner_sums,
            rows,
        ),
    )

    packed, (ffn_parts, grad_query) = marker.fence(packed, (ffn_parts, grad_query))
    packed_parts = trade(packed)

    def input_part(first):
        span = slice(first, first + half)
        return (
            nt(grad_query[span], query_proj)
            + nt(grad_key[span], key_proj)
            + nt(grad_value[span], value_proj)
        )

    token_pair = []
    for i in range(2):
        other = input_part(i * chunk + half).astype(BF16)
        token_pair.append(pair(input_part(i * chunk), marker.core_swap(other)))
    token_pair, packed_parts = marker.fence(token_pair, packed_parts)
    token_far = [far_swap(token_pair[i]) for i in range(2)]
    ffn_total = plane_sum(ffn_parts)
    ffn_near = lax.ppermute(ffn_total, "dp", NEAR_SWAP)
    ffn_reduced = (ffn_total.astype(F32) + ffn_near.astype(F32)).astype(BF16)
    ffn_reduced, packed_parts = tie(ffn_reduced, packed_parts)
    token_far[0], packed_parts = tie(token_far[0], packed_parts)
    packed_reduced = marker.near_sum(plane_sum(packed_parts))
    piece_rows = width // 16
    places = jnp.stack([my_index // 8, (my_index // 2) % 4]).astype(jnp.int32)
    halves = [
        jnp.concatenate([ffn_reduced[:piece_rows], packed_reduced[: piece_rows // 3]], axis=0),
        jnp.concatenate([ffn_reduced[piece_rows:], packed_reduced[piece_rows // 3 :]], axis=0),
    ]
    pieces = [ring_pieces(halves[1], "z"), ring_pieces(halves[0], "y")]
    halves, pieces = marker.fence(halves, pieces)
    other_ring = run_join(places[:1], (halves[1], *pieces[0]), 1)
    one_ring = run_join(places[1:], (halves[0], *pieces[1]), 4)
    pieces = ring_pieces(other_ring, "y")
    other_ring, one_ring = marker.fence(other_ring, one_ring)
    gathered = trade_z(one_ring)
    one_ring, token_far = marker.fence(one_ring, token_far)
    token_own = [
        (grad_first[i] + (token_pair[i].astype(F32) + token_far[i].astype(F32))).astype(BF16)
        for i in range(2)
    ]
    token_other = [lax.ppermute(rows_here, "mp", CORE_SWAP) for rows_here in token_own]
    token_grad = run_settle(core_arg, (*token_own, *token_other))
    closing = finish(marker.state)[0, 0]
    part = piece_rows // 3
    so_far = run_spread_some(places, (other_ring, pieces[0]), piece_rows, part)
    so_far, token_grad = tie(so_far, token_grad)
    *rest, outer_grad = run_spread_rest(
        places, pieces[1:], gathered, so_far, piece_rows, part
    )
    inner_grad, *rest = rest
    cuts = [values.reshape(local_width, width) for values in rest[:4]]
    vectors = rest[4:]
    return (
        loss[0, 0] + closing,
        token_grad,
        cuts[1].T,
        vectors[7],
        cuts[2].T,
        cuts[3].T,
        vectors[8],
        cuts[0],
        vectors[0],
        vectors[1],
        vectors[2],
        inner_grad.reshape(width, width),
        vectors[6],
        outer_grad.reshape(width, width),
        vectors[3],
        vectors[4],
        vectors[5],
    )


def solution(mesh):
    column, row, split = P(None, "mp"), P("mp", None), P("mp")
    placed = (
        (P("dp", None), P("dp"), P())
        + (column, split, column, column, split, row)
        + (P(), P(), P())
        + (column, split, row)
        + (P(), P(), P())
    )
    given = (
        (P(), P("dp", None))
        + (column, split, column, column, split, row)
        + (P(), P(), P())
        + (column, split, row)
        + (P(), P(), P())
    )
    return jax.shard_map(local, mesh=mesh, in_specs=placed, out_specs=given, check_vma=False)
```

```python
import functools
import math

import jax
import jax.numpy as jnp
from jax import lax
from jax.experimental import pallas as pl
from jax.experimental.pallas import tpu as pltpu
from jax.sharding import PartitionSpec as P

HD = 64
EPS_NORM = 1e-06
SOFTMAX_WARMTH = 0.01
NEG_FILL = -1e30
HIGHEST = lax.Precision.HIGHEST
F32 = jnp.float32
BF16 = jnp.bfloat16
QB = 256
KB = 256

CORE_SWAP = [(i, i ^ 1) for i in range(4)]
FAR_SWAP = [(i, i ^ 2) for i in range(4)]
NEAR_SWAP = [(i, i ^ 1) for i in range(32)]
PLANES = [[i * 2 + x for i in range(16)] for x in range(2)]
Z_RINGS = [[i + 8 * z for z in range(4)] for i in range(8)]

SMEM = pl.BlockSpec(memory_space=pltpu.SMEM)
VMEM = pl.BlockSpec(memory_space=pltpu.VMEM)
HBM = pl.BlockSpec(memory_space=pltpu.HBM)


def nn(left, right):
    return lax.dot_general(left, right, (((1,), (0,)), ((), ())), preferred_element_type=F32)


def nt(left, right):
    return lax.dot_general(left, right, (((1,), (1,)), ((), ())), preferred_element_type=F32)


def tn(left, right):
    return lax.dot_general(left, right, (((0,), (0,)), ((), ())), preferred_element_type=F32)


def place_of_block(block, core, rows):
    return ((block % 2) * 2 + block // 2) * QB + core * (rows // 2) & (rows - 1)


def spot_of_keys(j, core, rows):
    place = (j * KB + core * (rows // 2)) & (rows - 1)
    block = place // QB
    return pl.multiple_of(((block % 2) * 2 + block // 2) * QB + place % QB, KB)


def segment_bounds(lengths_ref):
    bounds, total = [], jnp.int32(0)
    for s in range(lengths_ref.shape[0]):
        start = total
        total = total + lengths_ref[s]
        bounds.append((start, total))
    return bounds


def block_span(bounds, first, rows):
    place = first + lax.broadcasted_iota(jnp.int32, (1, QB), 1)
    low, high = first, first + KB
    begin = jnp.full((1, QB), bounds[-1][1], jnp.int32)
    end = jnp.full((1, QB), rows, jnp.int32)
    for start, stop in bounds:
        inside = (place >= start) & (place < stop)
        begin = jnp.where(inside, start, begin)
        end = jnp.where(inside, stop, end)
        touches = (stop > first) & (start < first + QB) & (stop > start)
        low = jnp.where(touches, jnp.minimum(low, start), low)
        high = jnp.where(touches, jnp.maximum(high, stop), high)
    return low // KB, (high + KB - 1) // KB, begin, end


def head_copies(values, heads):
    lane = lax.broadcasted_iota(jnp.int32, values.shape, 1) // HD
    blank = jnp.zeros_like(values)
    return jnp.concatenate([jnp.where(lane == h, values, blank) for h in range(heads)], axis=0)


def span_mask(begin, end, block, heads):
    place = block * KB + lax.broadcasted_iota(jnp.int32, (KB, QB), 0)
    keep = (place >= begin) & (place < end)
    return jnp.concatenate([keep] * heads, axis=1)


def attend(heads, blocks, core, bounds, q_ref, k_ref, vt_ref, mixed_ref, lse_ref, acc_ref):
    rows = k_ref.shape[0]
    for i, block in enumerate(blocks):
        low, high, begin, end = block_span(bounds, place_of_block(block, core, rows), rows)
        stack = head_copies(q_ref[block * QB : (block + 1) * QB, :], heads)
        acc_ref[...] = jnp.zeros(acc_ref.shape, F32)

        def step(j, carry, stack=stack, begin=begin, end=end):
            top, total = carry
            spot = spot_of_keys(j, core, rows)
            scores = nt(k_ref[pl.ds(spot, KB), :], stack)
            scores = jnp.where(span_mask(begin, end, j, heads), scores, NEG_FILL)
            peak = jnp.maximum(top, jnp.max(scores, axis=0, keepdims=True))
            fade = jnp.exp(top - peak)
            probs = jnp.exp(scores - peak)
            total = total * fade + jnp.sum(probs, axis=0, keepdims=True)
            probs = probs.astype(BF16)
            for h in range(heads):
                part = slice(h * QB, (h + 1) * QB)
                span = slice(h * HD, (h + 1) * HD)
                acc_ref[span, :] = acc_ref[span, :] * fade[:, part] + nn(
                    vt_ref[span, pl.ds(spot, KB)], probs[:, part]
                )
            return peak, total

        top = jnp.full((1, heads * QB), NEG_FILL, F32)
        top, total = lax.fori_loop(
            low, high, step, (top, jnp.zeros((1, heads * QB), F32)), unroll=False
        )
        scale = 1.0 / total
        mixed = jnp.concatenate(
            [
                acc_ref[h * HD : (h + 1) * HD, :] * scale[:, h * QB : (h + 1) * QB]
                for h in range(heads)
            ],
            axis=0,
        )
        mixed_ref[i * QB : (i + 1) * QB, :] = mixed.T.astype(BF16)
        lse_ref[i, :, :] = jnp.broadcast_to(top + jnp.log(total), (8, heads * QB))


def fetch(sources, targets, semaphores, order=()):
    copies = [
        pltpu.make_async_copy(source, target, semaphores.at[i])
        for i, (source, target) in enumerate(zip(sources, targets))
    ]
    for i in [*order, *(i for i in range(len(copies)) if i not in order)]:
        copies[i].start()
    return copies


def project(mixed_ref, weights_ref, results, outputs, semaphores):
    results[1][...] = nn(mixed_ref[QB:, :], weights_ref[...]).astype(BF16)
    copies = send_out(results, outputs, semaphores, (1,))
    results[0][...] = nn(mixed_ref[:QB, :], weights_ref[...])
    return copies + send_out(results, outputs, semaphores, (0,))


def attend_first(heads, blocks, lengths_ref, core_ref, *refs):
    sources, outputs, refs = refs[:13], refs[13:25], refs[25:]
    results, targets, refs = refs[:12], refs[12:24], refs[24:]
    acc_ref, semaphores, out_semaphores = refs
    x_ref, q_ref, k_ref, v_ref, kt_ref, vt_ref, mixed_ref, lse_ref = results[:8]
    wqt_ref, wkt_ref, wvt_ref, bq_ref, bv_ref, wo_ref = targets[:6]
    rows = x_ref.shape[0]
    core = core_ref[0]
    copies = fetch(sources[1:], targets, semaphores)
    row_copies = []
    for block in range(rows // QB):
        first = pl.multiple_of(place_of_block(block, core, rows), QB)
        row_copies.append(
            pltpu.make_async_copy(
                sources[0].at[pl.ds(first, QB), :],
                x_ref.at[pl.ds(block * QB, QB), :],
                semaphores.at[12 + block],
            )
        )
        row_copies[-1].start()
    for copy in copies:
        copy.wait()
    query_bias, value_bias = row_of(bq_ref), row_of(bv_ref)
    for block in range(rows // QB):
        row_copies[block].wait()
        part = slice(block * QB, (block + 1) * QB)
        x = x_ref[part, :]
        q = (nt(x, wqt_ref[...]) + query_bias).astype(BF16)
        q_ref[part, :] = q * BF16(0.125)
        k_ref[part, :] = nt(x, wkt_ref[...]).astype(BF16)
        kt_ref[:, part] = nt(wkt_ref[...], x).astype(BF16)
        v = nt(x, wvt_ref[...]) + value_bias
        v_ref[part, :] = v.astype(BF16)
        vt_ref[:, part] = v.T.astype(BF16)
    outgoing = send_out(results, outputs, out_semaphores, range(6))
    bounds = segment_bounds(lengths_ref)
    place = core * (2 * QB) + lax.broadcasted_iota(jnp.int32, (1, QB), 1)
    for i in range(2):
        member = [
            jnp.where((place + i * QB >= start) & (place + i * QB < stop), 1.0, 0.0)
            for start, stop in bounds
        ]
        results[10][i] = jnp.concatenate(member, axis=0)
    lines = [row_of(ref) for ref in targets[6:]]
    results[11][...] = jnp.concatenate(lines + [jnp.zeros((2, lines[0].shape[1]), F32)], axis=0)
    outgoing += send_out(results, outputs, out_semaphores, (10, 11))
    attend(heads, blocks, core, bounds, q_ref, k_ref, vt_ref, mixed_ref, lse_ref, acc_ref)
    outgoing += project(mixed_ref, wo_ref, results[8:], outputs[8:], out_semaphores.at[8:10])
    outgoing += send_out(results, outputs, out_semaphores, (6, 7))
    for copy in outgoing:
        copy.wait()


def attend_more(heads, blocks, lengths_ref, core_ref, *refs):
    sources, outputs, refs = refs[:4], refs[4:8], refs[8:]
    targets, results, refs = refs[:4], refs[4:8], refs[8:]
    acc_ref, semaphores, out_semaphores = refs
    q_ref, k_ref, vt_ref, wo_ref = targets
    mixed_ref, lse_ref = results[:2]
    for copy in fetch(sources, targets, semaphores):
        copy.wait()
    bounds = segment_bounds(lengths_ref)
    attend(heads, blocks, core_ref[0], bounds, q_ref, k_ref, vt_ref, mixed_ref, lse_ref, acc_ref)
    outgoing = project(mixed_ref, wo_ref, results[2:], outputs[2:], out_semaphores.at[2:])
    outgoing += send_out(results, outputs, out_semaphores, (0, 1))
    for copy in outgoing:
        copy.wait()


def attend_back(heads, inputs, lengths_ref, core_ref, *refs):
    sources, refs = refs[:inputs], refs[inputs:]
    outputs, refs = refs[:2], refs[2:]
    joint_ref, pack_ref = refs[:2]
    dk_ref, dv_ref, dqt_ref, wo_acc_ref, semaphores, out_semaphores = refs[2:8]
    targets = refs[8:]
    copies = fetch(sources, targets, semaphores, (10, 9, 11, 12, 0, 4, 8, 6, 1, 2, 3, 5, 7))
    grads = targets[0:4]
    mixed = targets[4:6]
    lses = targets[6:8]
    wo_ref, q_ref, k_ref, v_ref, kt_ref = targets[8:13]
    own_sums, other_sums, inner_a, inner_b, x_ref = targets[13:]
    rows, width = q_ref.shape
    core = core_ref[0]
    bounds = segment_bounds(lengths_ref)
    dk_ref[...] = jnp.zeros(dk_ref.shape, F32)
    dv_ref[...] = jnp.zeros(dv_ref.shape, F32)
    joint_ref[...] = jnp.zeros(joint_ref.shape, BF16)
    lane = lax.broadcasted_iota(jnp.int32, (8, width), 1) // HD
    which = (lane == lax.broadcasted_iota(jnp.int32, (8, width), 0)).astype(F32).astype(BF16)
    for i in (0, 4, 6, 8, 9, 10, 11, 12):
        copies[i].wait()
    for block in range(rows // QB):
        if block > 0:
            copies[block].wait()
        if block == 2:
            copies[5].wait()
            copies[7].wait()
        low, high, begin, end = block_span(bounds, place_of_block(block, core, rows), rows)
        part = slice(block * QB, (block + 1) * QB)
        own = slice(block % 2 * QB, block % 2 * QB + QB)
        grad_attn = grads[block][...]
        mixed_here = mixed[block // 2][own, :]
        outer = tn(mixed_here, grad_attn)
        wo_acc_ref[...] = outer if block == 0 else wo_acc_ref[...] + outer
        grad_mixed = nt(grad_attn, wo_ref[...]).astype(BF16)
        product = grad_mixed.astype(F32) * mixed_here.astype(F32)
        sums = sum(nt(which, part) for part in in_three(product)[:2])
        delta = jnp.concatenate([sums[h : h + 1, :] for h in range(heads)], axis=1)
        lse = lses[block // 2][block % 2, 0:1, :]
        q_stack = head_copies(q_ref[part, :], heads)
        g_stack = head_copies(grad_mixed, heads)
        dqt_ref[...] = jnp.zeros(dqt_ref.shape, F32)

        def step(
            j, carry, delta=delta, lse=lse, q_stack=q_stack, g_stack=g_stack, begin=begin, end=end
        ):
            here = pl.ds(spot_of_keys(j, core, rows), KB)
            scores = nt(k_ref[here, :], q_stack)
            scores = jnp.where(span_mask(begin, end, j, heads), scores, NEG_FILL)
            probs = jnp.exp(scores - lse)
            grad = (probs * (nt(v_ref[here, :], g_stack) - delta)).astype(BF16)
            dv_ref[here, :] += nn(probs.astype(BF16), g_stack)
            dk_ref[here, :] += nn(grad, q_stack)
            for h in range(heads):
                span = slice(h * HD, (h + 1) * HD)
                dqt_ref[span, :] += nn(kt_ref[span, here], grad[:, h * QB : (h + 1) * QB])
            return carry

        lax.fori_loop(low, high, step, 0, unroll=False)
        joint_ref[part, :width] = (dqt_ref[...].T * 0.125).astype(BF16)
    spans = [slice(256 * k, 256 * k + width) for k in range(3)]
    joint_ref[:, spans[1]] = dk_ref[...].astype(BF16)
    joint_ref[:, spans[2]] = dv_ref[...].astype(BF16)
    for copy in copies[13:]:
        copy.wait()
    outgoing = send_out(refs, outputs, out_semaphores, (0,))
    sums = [column_sum(joint_ref[:, spans[k]].astype(F32)) for k in (0, 2)]
    blank = jnp.zeros((1, 256 - width), F32)
    tail = jnp.concatenate([sums[0], blank, sums[1], blank, jnp.zeros((1, 256), F32)], axis=1)
    inner = row_of(inner_a) + row_of(inner_b)
    paired = own_sums[0:6, :] + other_sums[0:6, :]
    small = [paired, inner, tail, jnp.zeros((8, tail.shape[1]), F32)]
    small = jnp.concatenate(small, axis=0).astype(BF16)
    piece = pack_ref.shape[1] - 16
    per = width // piece
    for m in range(4):
        total = wo_acc_ref[...] if m == 0 else tn(joint_ref[:, spans[m - 1]], x_ref[...])
        for t in range(per):
            cut = total[t * piece : (t + 1) * piece, :].astype(BF16)
            pack_ref[m * per + t, 0:piece, :] = cut
            pack_ref[m * per + t, piece:, :] = small if m + t == 0 else jnp.zeros_like(small)
        here = pl.ds(m * per, per)
        copy = pltpu.make_async_copy(
            pack_ref.at[here], outputs[1].at[here], out_semaphores.at[1 + m]
        )
        copy.start()
        outgoing.append(copy)
    for copy in outgoing:
        copy.wait()


def shaped(shape, dtype):
    return jax.ShapeDtypeStruct(shape, dtype)


PARAMS = pltpu.CompilerParams(vmem_limit_bytes=60 << 20)
SMALL = pltpu.CompilerParams(vmem_limit_bytes=60 << 20)
SHARED = pltpu.CompilerParams(vmem_limit_bytes=24 << 20)
COST = pl.CostEstimate(flops=1024, bytes_accessed=1024, transcendentals=0)


def buffers(arrays):
    return [pltpu.VMEM(array.shape, array.dtype) for array in arrays]


def attend_shapes(count, heads, width):
    rows = count * QB
    return (
        shaped((rows, heads * HD), BF16),
        shaped((count, 8, heads * QB), F32),
        shaped((rows // 2, width), F32),
        shaped((rows // 2, width), BF16),
    )


def run_first(lengths, core, tokens, weights, blocks):
    rows, width = tokens.shape
    local_width = weights[0].shape[0]
    heads = local_width // HD
    outs = (
        (shaped(tokens.shape, BF16),)
        + (shaped((rows, local_width), BF16),) * 3
        + (shaped((local_width, rows), BF16),) * 2
        + attend_shapes(len(blocks), heads, width)
        + (shaped((2, lengths.shape[0], QB), F32), shaped((8, width), F32))
    )
    return pl.pallas_call(
        functools.partial(attend_first, heads, blocks),
        out_shape=outs,
        in_specs=[SMEM] * 2 + [HBM] * 13,
        out_specs=(HBM,) * 12,
        scratch_shapes=buffers(outs)
        + buffers(weights)
        + [pltpu.VMEM((local_width, QB), F32)]
        + [pltpu.SemaphoreType.DMA((12 + rows // QB,)), pltpu.SemaphoreType.DMA((12,))],
        compiler_params=PARAMS,
        name="attend_first",
        cost_estimate=COST,
    )(lengths, core, tokens, *weights)


def run_more(lengths, core, arrays, blocks):
    rows, local_width = arrays[0].shape
    heads = local_width // HD
    outs = attend_shapes(len(blocks), heads, arrays[3].shape[1])
    return pl.pallas_call(
        functools.partial(attend_more, heads, blocks),
        out_shape=outs,
        in_specs=[SMEM] * 2 + [HBM] * 4,
        out_specs=(HBM,) * 4,
        scratch_shapes=buffers(arrays)
        + buffers(outs)
        + [pltpu.VMEM((local_width, QB), F32)]
        + [pltpu.SemaphoreType.DMA((4,)), pltpu.SemaphoreType.DMA((4,))],
        compiler_params=PARAMS,
        name="attend_more",
        cost_estimate=COST,
    )(lengths, core, *arrays)


def run_back(lengths, core, arrays):
    wo, q, x = arrays[8], arrays[9], arrays[-1]
    rows, width = q.shape
    heads = width // HD
    piece = 4 * width // 16
    outs = (shaped((rows, 3 * 256), BF16), shaped((16, piece + 16, x.shape[1]), BF16))
    return pl.pallas_call(
        functools.partial(attend_back, heads, len(arrays)),
        out_shape=outs,
        in_specs=[SMEM] * 2 + [HBM] * len(arrays),
        out_specs=(HBM,) * 2,
        scratch_shapes=buffers(outs)
        + [pltpu.VMEM((rows, width), F32)] * 2
        + [pltpu.VMEM((width, QB), F32), pltpu.VMEM(wo.shape, F32)]
        + [pltpu.SemaphoreType.DMA((len(arrays),)), pltpu.SemaphoreType.DMA((5,))]
        + buffers(arrays),
        compiler_params=PARAMS,
        name="attend_back",
        cost_estimate=COST,
    )(lengths, core, *arrays)


def mark_kernel(source_ref, target_ref):
    del source_ref, target_ref


def mark(values):
    return pl.pallas_call(
        mark_kernel,
        out_shape=shaped(values.shape, values.dtype),
        in_specs=[HBM],
        out_specs=HBM,
        compiler_params=pltpu.CompilerParams(vmem_limit_bytes=1 << 20),
        name="mark",
        cost_estimate=pl.CostEstimate(flops=1 << 36, bytes_accessed=1 << 10, transcendentals=0),
    )(values)


def finish_kernel(source_ref, target_ref):
    del source_ref
    target_ref[...] = jnp.zeros(target_ref.shape, F32)


def finish(values):
    return pl.pallas_call(
        finish_kernel,
        out_shape=shaped(values.shape, values.dtype),
        in_specs=[HBM],
        out_specs=VMEM,
        compiler_params=pltpu.CompilerParams(vmem_limit_bytes=1 << 20),
        name="finish",
        cost_estimate=COST,
    )(values)


def row_of(ref):
    return ref[...].astype(F32).reshape(1, -1)


def in_three(values):
    high = values.astype(BF16)
    rest = values - high.astype(F32)
    middle = rest.astype(BF16)
    return high, middle, (rest - middle.astype(F32)).astype(BF16)


def norm_step(grad, normed, rscale, gain):
    scaled = grad * gain
    first_mean = jnp.mean(scaled, axis=1, keepdims=True)
    cross_mean = jnp.mean(scaled * normed, axis=1, keepdims=True)
    return rscale * (scaled - first_mean - normed * cross_mean)


def column_of(ref):
    row = ref[...].reshape(1, -1)
    return jnp.broadcast_to(row, (128, row.shape[1])).T[:, 0:1]


def column_sum(values):
    return jnp.sum(values, axis=0, keepdims=True)


def send_out(results, outputs, semaphores, which):
    copies = [
        pltpu.make_async_copy(results[k], outputs[k], semaphores.at[k]) for k in which
    ]
    for copy in copies:
        copy.start()
    return copies


def loss_back(lengths_ref, place_ref, *refs):
    sources, outputs, refs = refs[:9], refs[9:15], refs[15:]
    targets, results = refs[:9], refs[9:15]
    coef_ref, turned_ref, semaphores, out_semaphores = refs[15:]
    copies = fetch(sources, targets, semaphores)
    piece_ref, swapped_ref, pooled_ref, match_ref, gain_ref = targets[:5]
    core, index = place_ref[0], place_ref[1]
    bounds = segment_bounds(lengths_ref)
    for copy in copies[:5]:
        copy.wait()
    first = core == 0
    queries = jnp.where(first, piece_ref[...], swapped_ref[...])
    passages = jnp.where(first, swapped_ref[...], piece_ref[...])
    count = queries.shape[0]
    own = pooled_ref.shape[0] // 2
    similarity = nt(queries, passages) / SOFTMAX_WARMTH
    match = match_ref[...].reshape(1, -1)
    match = match == lax.broadcasted_iota(jnp.int32, (count, count), 0)
    top = jnp.max(similarity, axis=1, keepdims=True)
    lse = top + jnp.log(jnp.sum(jnp.exp(similarity - top), axis=1, keepdims=True))
    positive = jnp.sum(jnp.where(match, similarity, 0.0), axis=1, keepdims=True)
    loss = jnp.sum(lse - positive, axis=0, keepdims=True) / count
    results[5][...] = jnp.broadcast_to(loss, results[5].shape)
    coef = (jnp.exp(similarity - lse) - match.astype(F32)) * (1.0 / (count * SOFTMAX_WARMTH))
    coef_ref[...] = coef
    turned_ref[...] = coef.T
    here = pl.ds(pl.multiple_of(index * own, own), own)
    grad_query = sum(nn(part, passages) for part in in_three(coef_ref[here, :]))
    grad_passage = sum(nn(part, queries) for part in in_three(turned_ref[here, :]))
    grad_unit = jnp.concatenate([grad_query, grad_passage], axis=0)
    pooled = pooled_ref[...]
    rscale = lax.rsqrt(jnp.sum(pooled * pooled, axis=1, keepdims=True) + EPS_NORM)
    inner = jnp.sum(pooled * grad_unit, axis=1, keepdims=True)
    grad_pooled = rscale * grad_unit - rscale * rscale * rscale * inner * pooled
    seqs = 2 * own
    grad_pooled = jnp.concatenate(
        [grad_pooled, jnp.zeros((128 - seqs, grad_pooled.shape[1]), F32)], axis=0
    )
    parts = in_three(grad_pooled)
    lane = lax.broadcasted_iota(jnp.int32, (1, 128), 1)
    begin = end = jnp.zeros((1, 128), jnp.int32)
    for seq, (start, stop) in enumerate(bounds):
        begin = jnp.where(lane == seq, start, begin)
        end = jnp.where(lane == seq, stop, end)
    gain = row_of(gain_ref)
    sums = [0.0, 0.0, 0.0]
    outgoing = []
    for i in range(2):
        copies[5 + 2 * i].wait()
        copies[6 + 2 * i].wait()
        normed = targets[5 + 2 * i][...]
        place = core * (2 * QB) + i * QB + lax.broadcasted_iota(jnp.int32, (QB, 128), 0)
        member = jnp.where((place >= begin) & (place < end), 1.0, 0.0).astype(BF16)
        grad = sum(nn(member, part) for part in parts)
        second = norm_step(grad, normed, column_of(targets[6 + 2 * i]), gain)
        rounded = second.astype(BF16)
        results[i][...] = second
        results[2 + i][...] = rounded
        for k, values in enumerate((rounded.astype(F32), grad * normed, grad)):
            sums[k] = sums[k] + column_sum(values)
        outgoing += send_out(results, outputs, out_semaphores, (2 + i, i))
    results[4][...] = jnp.concatenate(sums + [jnp.zeros((5, sums[0].shape[1]), F32)], axis=0)
    outgoing += send_out(results, outputs, out_semaphores, (4, 5))
    for copy in outgoing:
        copy.wait()


def norm_back(*refs):
    sources, outputs, refs = refs[:12], refs[12:17], refs[17:]
    targets, results = refs[:12], refs[12:17]
    semaphores, out_semaphores = refs[17:]
    copies = fetch(sources, targets, semaphores)
    copies[0].wait()
    copies[1].wait()
    gain = row_of(targets[0])
    sums = [0.0, 0.0, 0.0]
    outgoing = []
    for i in range(2):
        for copy in copies[2 + 5 * i : 7 + 5 * i]:
            copy.wait()
        second, pair_here, far, normed, rscale = targets[2 + 5 * i : 7 + 5 * i]
        grad = second[...] + (pair_here[...].astype(F32) + far[...].astype(F32))
        normed = normed[...]
        first = norm_step(grad, normed, column_of(rscale), gain)
        rounded = first.astype(BF16)
        results[i][...] = first
        results[2 + i][...] = rounded
        for k, values in enumerate((rounded.astype(F32), grad * normed, grad)):
            sums[k] = sums[k] + column_sum(values)
        outgoing += send_out(results, outputs, out_semaphores, (2 + i, i))
    blank = jnp.zeros((2, sums[0].shape[1]), F32)
    results[4][...] = jnp.concatenate(sums + [targets[1][0:3, :], blank], axis=0)
    outgoing += send_out(results, outputs, out_semaphores, (4,))
    for copy in outgoing:
        copy.wait()


STEPS = (0, 2, 1, 3)


def join(copies_of_each, place_ref, *refs):
    sources, output, semaphores = refs[:4], refs[4], refs[5]
    copies = []
    for k in range(4):
        spot = (place_ref[0] + 4 - STEPS[k]) % 4
        for r in range(copies_of_each):
            goal = output.at[spot] if copies_of_each == 1 else output.at[r, spot]
            semaphore = semaphores.at[k * copies_of_each + r]
            copies.append(pltpu.make_async_copy(sources[k], goal, semaphore))
            copies[-1].start()
    for copy in copies:
        copy.wait()


def place_block(piece, part, block_ref, spot, outputs, buffers_, semaphores, first):
    inner, cuts = buffers_
    inner[...] = block_ref[:, :piece, :].astype(F32)
    cuts[...] = block_ref[:, piece : 2 * piece - part, :].astype(F32)
    copies = [pltpu.make_async_copy(inner, outputs[0].at[:, spot], semaphores.at[first])]
    for m in range(4):
        goal = outputs[1 + m].at[spot, pl.ds(part, piece - part), :]
        copies.append(pltpu.make_async_copy(cuts.at[m], goal, semaphores.at[first + 1 + m]))
    for copy in copies:
        copy.start()
    return copies


def place_vectors(piece, part, block_ref, spot, outputs, vectors, semaphores, first):
    @pl.when(spot == 0)
    def _():
        small = block_ref[0, 2 * piece - part :, :].astype(F32)
        for k in range(7):
            vectors[k][...] = small[k : k + 1, :].reshape(-1)
        count = vectors[7].shape[0]
        for k in range(2):
            vectors[7 + k][...] = small[7:8, 256 * k : 256 * k + count].reshape(-1)
        copies = [
            pltpu.make_async_copy(vectors[k], outputs[5 + k], semaphores.at[first + k])
            for k in range(9)
        ]
        for copy in copies:
            copy.start()
        for copy in copies:
            copy.wait()


def spread_some(piece, part, count, place_ref, *refs):
    sources, outputs, refs = refs[:count], refs[count : count + 14], refs[count + 14 :]
    blocks, refs = refs[:count], refs[count:]
    buffers_, vectors, refs = refs[: 2 * count], refs[2 * count : 2 * count + 9], refs[-2:]
    arrivals = fetch(sources, blocks, refs[0])
    outgoing, spots = [], []
    for k in range(count):
        arrivals[k].wait()
        spots.append((place_ref[1] + 4 - STEPS[k]) % 4)
        outgoing += place_block(
            piece, part, blocks[k], spots[k], outputs, buffers_[2 * k : 2 * k + 2], refs[1], 5 * k
        )
    for k in range(count):
        place_vectors(piece, part, blocks[k], spots[k], outputs, vectors, refs[1], 5 * count)
    for copy in outgoing:
        copy.wait()


def spread_rest(piece, part, place_ref, *refs):
    sources, outputs, refs = refs[:3], refs[17:32], refs[32:]
    blocks, by_z, refs = refs[:2], refs[2], refs[3:]
    buffers_, outer, heads, vectors, refs = refs[:4], refs[4], refs[5], refs[6:15], refs[15:]
    semaphores, out_semaphores = refs
    arrivals = fetch(sources, (*blocks, by_z), semaphores)
    outgoing, spots = [], []
    for k in range(2):
        spots.append((place_ref[1] + 4 - STEPS[2 + k]) % 4)
        arrivals[k].wait()
        outgoing += place_block(
            piece,
            part,
            blocks[k],
            spots[k],
            outputs,
            buffers_[2 * k : 2 * k + 2],
            out_semaphores,
            5 * k,
        )
    arrivals[2].wait()
    outer[...] = by_z[:, :, :piece, :].astype(F32)
    copies = [pltpu.make_async_copy(outer, outputs[14], out_semaphores.at[10])]
    copies[0].start()
    heads[...] = by_z[:, :, piece:, :].astype(F32)
    for m in range(4):
        goal = outputs[1 + m].at[:, pl.ds(0, part), :]
        copies.append(pltpu.make_async_copy(heads.at[m], goal, out_semaphores.at[11 + m]))
        copies[-1].start()
    for k in range(2):
        place_vectors(piece, part, blocks[k], spots[k], outputs, vectors, out_semaphores, 15)
    for copy in outgoing + copies:
        copy.wait()


def run_loss(lengths, place, arrays):
    rows, width = arrays[5].shape
    count = arrays[0].shape[0]
    outs = (
        (shaped((rows, width), F32),) * 2
        + (shaped((rows, width), BF16),) * 2
        + (shaped((8, width), F32), shaped((8, 128), F32))
    )
    return pl.pallas_call(
        loss_back,
        out_shape=outs,
        in_specs=[SMEM] * 2 + [HBM] * 9,
        out_specs=(HBM,) * 6,
        scratch_shapes=buffers(arrays)
        + buffers(outs)
        + [pltpu.VMEM((count, count), F32)] * 2
        + [pltpu.SemaphoreType.DMA((9,)), pltpu.SemaphoreType.DMA((6,))],
        compiler_params=SHARED,
        name="loss_back",
        cost_estimate=COST,
    )(lengths, place, *arrays)


def run_norm(arrays):
    rows, width = arrays[2].shape
    outs = (
        (shaped((rows, width), F32),) * 2
        + (shaped((rows, width), BF16),) * 2
        + (shaped((8, width), F32),)
    )
    return pl.pallas_call(
        norm_back,
        out_shape=outs,
        in_specs=[HBM] * 12,
        out_specs=(HBM,) * 5,
        scratch_shapes=buffers(arrays)
        + buffers(outs)
        + [pltpu.SemaphoreType.DMA((12,)), pltpu.SemaphoreType.DMA((5,))],
        compiler_params=SMALL,
        name="norm_back",
        cost_estimate=COST,
    )(*arrays)


def run_join(place, pieces, copies_of_each):
    lead = (4,) if copies_of_each == 1 else (copies_of_each, 4)
    return pl.pallas_call(
        functools.partial(join, copies_of_each),
        out_shape=shaped(lead + pieces[0].shape, BF16),
        in_specs=[SMEM] + [HBM] * 4,
        out_specs=HBM,
        scratch_shapes=[pltpu.SemaphoreType.DMA((4 * copies_of_each,))],
        compiler_params=pltpu.CompilerParams(vmem_limit_bytes=1 << 20),
        name="join",
        cost_estimate=COST,
    )(place, *pieces)


def settle(core_ref, *refs):
    sources, output, semaphores = refs[:4], refs[4], refs[5]
    copies = []
    for k in range(4):
        first = (k // 2 + core_ref[0]) % 2 * (2 * QB) + k % 2 * QB
        spot = pl.ds(pl.multiple_of(first, QB), QB)
        copies.append(pltpu.make_async_copy(sources[k], output.at[spot, :], semaphores.at[k]))
        copies[-1].start()
    for copy in copies:
        copy.wait()


def run_settle(core, parts):
    rows, width = parts[0].shape
    return pl.pallas_call(
        settle,
        out_shape=shaped((4 * rows, width), BF16),
        in_specs=[SMEM] + [HBM] * 4,
        out_specs=HBM,
        scratch_shapes=[pltpu.SemaphoreType.DMA((4,))],
        compiler_params=pltpu.CompilerParams(vmem_limit_bytes=1 << 20),
        name="settle",
        cost_estimate=COST,
    )(core, *parts)


def spread_shapes(piece, width):
    shapes = [(4, 4, piece, width)] + [(4, piece, width)] * 4
    return shapes + [(width,)] * 7 + [(4 * piece,)] * 2


def run_spread_some(places, blocks, piece, part):
    width = blocks[0].shape[2]
    shapes = spread_shapes(piece, width)
    count = len(blocks)
    pair_of = [pltpu.VMEM((4, piece, width), F32), pltpu.VMEM((4, piece - part, width), F32)]
    return pl.pallas_call(
        functools.partial(spread_some, piece, part, count),
        out_shape=[shaped(shape, F32) for shape in shapes],
        in_specs=[SMEM] + [HBM] * count,
        out_specs=[HBM] * 14,
        scratch_shapes=buffers(blocks)
        + pair_of * count
        + [pltpu.VMEM(shape, F32) for shape in shapes[5:]]
        + [pltpu.SemaphoreType.DMA((count,)), pltpu.SemaphoreType.DMA((5 * count + 9,))],
        compiler_params=SHARED,
        name="spread_some",
        cost_estimate=COST,
    )(places, *blocks)


def run_spread_rest(places, blocks, gathered, so_far, piece, part):
    width = gathered.shape[3]
    shapes = spread_shapes(piece, width)
    outer = (4, 4, piece, width)
    pair_of = [pltpu.VMEM((4, piece, width), F32), pltpu.VMEM((4, piece - part, width), F32)]
    return pl.pallas_call(
        functools.partial(spread_rest, piece, part),
        out_shape=[shaped(shape, F32) for shape in shapes + [outer]],
        in_specs=[SMEM] + [HBM] * 17,
        out_specs=[HBM] * 15,
        input_output_aliases={4 + k: k for k in range(14)},
        scratch_shapes=buffers((*blocks, gathered))
        + pair_of * 2
        + [pltpu.VMEM(outer, F32), pltpu.VMEM((4, 4, part, width), F32)]
        + [pltpu.VMEM(shape, F32) for shape in shapes[5:]]
        + [pltpu.SemaphoreType.DMA((3,)), pltpu.SemaphoreType.DMA((24,))],
        compiler_params=SHARED,
        name="spread_rest",
        cost_estimate=COST,
    )(places, *blocks, gathered, *so_far)


def trade(values):
    return lax.all_to_all(
        values, "dp", split_axis=0, concat_axis=0, axis_index_groups=PLANES, tiled=True
    )


def share(values):
    spread_out = jnp.broadcast_to(values[None], (32,) + values.shape)
    return lax.all_to_all(spread_out, "dp", split_axis=0, concat_axis=0, tiled=True)


def trade_z(values):
    return lax.all_to_all(
        values, "dp", split_axis=0, concat_axis=0, axis_index_groups=Z_RINGS, tiled=True
    )


def ring_shift(axis, step):
    pairs = []
    for i in range(32):
        z, y, x = i // 8, (i // 2) % 4, i % 2
        z, y = ((z + step) % 4, y) if axis == "z" else (z, (y + step) % 4)
        pairs.append((i, (z * 4 + y) * 2 + x))
    return pairs


def ring_pieces(values, axis):
    return [lax.ppermute(values, "dp", ring_shift(axis, step)) for step in STEPS[1:]]


def tie(values, others):
    return lax.optimization_barrier((values, others))


class Marker:
    def __init__(self):
        self.state = jnp.zeros((8, 128), F32)

    def fence(self, ready, later):
        ready, state = tie(ready, self.state)
        later, self.state = tie(later, mark(state))
        return ready, later

    def moved(self, values, axis, pairs):
        values, state = tie(values, self.state)
        arrived, self.state = tie(lax.ppermute(values, axis, pairs), mark(state))
        return arrived

    def core_swap(self, values):
        return self.moved(values, "mp", CORE_SWAP)

    def near_swap(self, values):
        return self.moved(values, "dp", NEAR_SWAP)

    def both(self, own):
        return jnp.concatenate([own, self.core_swap(own)], axis=0)

    def near_sum(self, total):
        return (total.astype(F32) + self.near_swap(total).astype(F32)).astype(BF16)


def plane_sum(parts):
    return jnp.sum(parts.astype(F32), axis=0).astype(BF16)


def far_swap(values):
    return lax.ppermute(values, "mp", FAR_SWAP)


def norm_forward(values, gain_vec, shift_vec):
    average = jnp.mean(values, axis=-1, keepdims=True)
    centred = values - average
    rscale = lax.rsqrt(jnp.mean(centred * centred, axis=-1, keepdims=True) + EPS_NORM)
    normed = centred * rscale
    return (normed * gain_vec + shift_vec, normed, rscale[:, 0])


def gelu_and_slope(upper):
    below = 0.5 * (1.0 + lax.erf(upper * math.sqrt(0.5)))
    density = jnp.exp(-0.5 * upper * upper) * (1.0 / math.sqrt(2.0 * math.pi))
    return (upper * below).astype(BF16), (below + upper * density).astype(BF16)


def local(
    tokens,
    lengths,
    pair_index,
    query_proj,
    query_bias,
    key_proj,
    value_proj,
    value_bias,
    output_proj,
    output_bias,
    attn_gain,
    attn_shift,
    inner_proj,
    inner_bias,
    outer_proj,
    outer_bias,
    final_gain,
    final_shift,
):
    row_count, width = tokens.shape
    chunk = row_count // 2
    half = chunk // 2
    seq_count = lengths.shape[0]
    pair_count = seq_count // 2
    overall_pair_count = pair_index.shape[0]
    local_width = query_proj.shape[1]
    core = lax.axis_index("mp") % 2
    my_index = lax.axis_index("dp")
    marker = Marker()
    core_arg = jnp.reshape(core, (1,)).astype(jnp.int32)
    vectors = (output_bias, attn_gain, attn_shift, outer_bias, final_gain, final_shift)
    query_t, key_t, value_t = query_proj.T, key_proj.T, value_proj.T
    blank = jnp.zeros((256 - local_width, width), BF16)
    joint_proj = jnp.concatenate([query_t, blank, key_t, blank, value_t, blank], axis=0)

    weights = (query_t, key_t, value_t, query_bias, value_bias, output_proj, *vectors)
    first = run_first(lengths, core_arg, tokens, weights, (0, 1))
    rows, query_b, key_b, value_b, key_tb, value_tb, mixed_a, lse_a = first[:8]
    attn_own_a, attn_other_a, members, vectors = first[8:]

    def own_and_other(values, weights):
        return nn(values[:half], weights), nn(values[half:], weights).astype(BF16)

    def pair(own, arrived):
        return (own + arrived.astype(F32)).astype(BF16)

    def first_norm(index, pair_here, far):
        attn_full = pair_here.astype(F32) + far.astype(F32) + output_bias
        own_tokens = rows[index * chunk : index * chunk + half].astype(F32)
        return norm_forward(own_tokens + attn_full, attn_gain_f, attn_shift_f)

    def feed_forward(own_hidden):
        whole = marker.both(own_hidden)
        act, slope = gelu_and_slope(nn(whole, inner_proj) + inner_bias.astype(F32))
        act, slope = tie(act, slope)
        return whole, act, slope

    def last_norm(hidden, pair_here, far):
        ffn_full = pair_here.astype(F32) + far.astype(F32) + outer_bias
        return norm_forward(hidden + ffn_full, final_gain_f, final_shift_f)

    attn_pair_a = pair(attn_own_a, marker.core_swap(attn_other_a))
    attn_far_a = far_swap(attn_pair_a)
    output_bias, attn_gain_f, attn_shift_f = vectors[0], vectors[1], vectors[2]
    outer_bias, final_gain_f, final_shift_f = vectors[3], vectors[4], vectors[5]
    late_query, late_pair = tie(query_b, attn_pair_a)
    mixed_b, lse_b, attn_own_b, attn_other_b = run_more(
        lengths, core_arg, (late_query, key_b, value_tb, output_proj), (2, 3)
    )
    attn_pair_b = pair(attn_own_b, marker.core_swap(attn_other_b))
    attn_far_b = far_swap(attn_pair_b)
    attn_far_a, attn_pair_b = tie(attn_far_a, attn_pair_b)
    hidden_a, normed_one_a, rscale_one_a = first_norm(0, late_pair, attn_far_a)
    own_hidden_a = hidden_a.astype(BF16)
    hidden_ab, act_a, slope_a = feed_forward(own_hidden_a)
    ffn_own_a, ffn_other_a = own_and_other(act_a, outer_proj)
    ffn_pair_a = pair(ffn_own_a, marker.core_swap(ffn_other_a))
    attn_far_b, ffn_pair_late = tie(attn_far_b, ffn_pair_a)
    ffn_far_a = far_swap(ffn_pair_a)
    hidden_b, normed_one_b, rscale_one_b = first_norm(1, attn_pair_b, attn_far_b)
    own_hidden_b = hidden_b.astype(BF16)
    hidden_bb, act_b, slope_b = feed_forward(own_hidden_b)
    ffn_own_b, ffn_other_b = own_and_other(act_b, outer_proj)
    ffn_pair_b = pair(ffn_own_b, marker.core_swap(ffn_other_b))
    ffn_pair_b, ffn_far_a = marker.fence(ffn_pair_b, ffn_far_a)
    final_a, normed_two_a, rscale_two_a = last_norm(hidden_a, ffn_pair_late, ffn_far_a)
    pooled_a = jnp.dot(members[0], final_a, precision=HIGHEST)
    final_b, normed_two_b, rscale_two_b = last_norm(hidden_b, ffn_pair_b, far_swap(ffn_pair_b))
    pooled_part = pooled_a + jnp.dot(members[1], final_b, precision=HIGHEST)
    lse = (lse_a, lse_b)
    hidden_whole, act, slope = (hidden_ab, hidden_bb), (act_a, act_b), (slope_a, slope_b)
    normed_one, rscale_one = (normed_one_a, normed_one_b), (rscale_one_a, rscale_one_b)
    normed_two, rscale_two = (normed_two_a, normed_two_b), (rscale_two_a, rscale_two_b)
    pooled = pooled_part + marker.core_swap(pooled_part)
    pool_rscale = lax.rsqrt(jnp.sum(pooled * pooled, axis=-1, keepdims=True) + EPS_NORM)
    unit_b = (pooled * pool_rscale).astype(BF16)

    piece = lax.dynamic_slice_in_dim(unit_b, core * pair_count, pair_count, 0)
    piece = share(piece).reshape(overall_pair_count, width)
    place_arg = jnp.stack([core, my_index]).astype(jnp.int32)
    *grads, last_sums, loss = run_loss(
        lengths,
        place_arg,
        (
            piece,
            marker.core_swap(piece),
            pooled,
            pair_index,
            final_gain,
            normed_two[0],
            rscale_two[0],
            normed_two[1],
            rscale_two[1],
        ),
    )
    grad_second, own_grad = grads[:2], grads[2:]

    inner_sums, grad_ffn, grad_up, hidden_other, outer_sums = [], [], [], [], []
    for i in range(2):
        grad_ffn.append(marker.both(own_grad[i]))
        grad_up.append((nt(grad_ffn[i], outer_proj) * slope[i].astype(F32)).astype(BF16))
        inner_sums.append(jnp.sum(grad_up[i].astype(F32), axis=0))
        other = nt(grad_up[i][half:], inner_proj).astype(BF16)
        late_act, other = tie(act[i], other)
        outer_sums.append(tn(late_act, grad_ffn[i]))
        swap = marker.core_swap if i else lambda rows_here: lax.ppermute(rows_here, "mp", CORE_SWAP)
        arrived, outer_sums[i] = tie(swap(other), outer_sums[i])
        hidden_other.append(arrived)
    hidden_pair = [pair(nt(grad_up[i][:half], inner_proj), hidden_other[i]) for i in range(2)]
    hidden_far = [far_swap(hidden_pair[i]) for i in range(2)]
    late_hidden, hidden_pair = tie(hidden_whole, hidden_pair)
    ffn_pack = jnp.concatenate(
        [
            (outer_sums[0] + outer_sums[1])
            .astype(BF16)
            .reshape(16, -1, width),
            (tn(late_hidden[0], grad_up[0]) + tn(late_hidden[1], grad_up[1]))
            .astype(BF16)
            .reshape(16, -1, width),
        ],
        axis=1,
    )
    ffn_pack, hidden_far = marker.fence(ffn_pack, hidden_far)
    ffn_parts = trade(ffn_pack)

    *grads, sums = run_norm(
        (
            attn_gain,
            last_sums,
            grad_second[0],
            hidden_pair[0],
            hidden_far[0],
            normed_one[0],
            rscale_one[0],
            grad_second[1],
            hidden_pair[1],
            hidden_far[1],
            normed_one[1],
            rscale_one[1],
        )
    )
    grad_first, own_grad = grads[:2], grads[2:]
    (*own_grad, sums), state = tie((*own_grad, sums), marker.state)
    arrived = [lax.ppermute(values, "mp", CORE_SWAP) for values in (*own_grad, sums)]
    (*other_grad, other_sums), marker.state = tie(arrived, mark(state))
    grad_rows, packed = run_back(
        lengths,
        core_arg,
        (
            own_grad[0],
            other_grad[0],
            own_grad[1],
            other_grad[1],
            mixed_a,
            mixed_b,
            *lse,
            output_proj,
            query_b,
            key_b,
            value_b,
            key_tb,
            sums,
            other_sums,
            *inner_sums,
            rows,
        ),
    )

    def input_part(first):
        span = slice(first, first + half)
        return nn(grad_rows[span], joint_proj)

    token_pair = []
    for i in range(2):
        other = input_part(i * chunk + half).astype(BF16)
        token_pair.append(pair(input_part(i * chunk), marker.core_swap(other)))
    token_pair, (packed, ffn_parts) = marker.fence(token_pair, (packed, ffn_parts))
    (packed, token_pair), ffn_parts = marker.fence((packed, token_pair), ffn_parts)
    packed_parts = trade(packed)
    token_far = [far_swap(token_pair[i]) for i in range(2)]
    ffn_total = plane_sum(ffn_parts)
    ffn_near = lax.ppermute(ffn_total, "dp", NEAR_SWAP)
    ffn_reduced = (ffn_total.astype(F32) + ffn_near.astype(F32)).astype(BF16)
    ffn_reduced, packed_parts = tie(ffn_reduced, packed_parts)
    packed_reduced = marker.near_sum(plane_sum(packed_parts))
    token_far, packed_reduced = tie(token_far, packed_reduced)
    piece_rows = width // 16
    places = jnp.stack([my_index // 8, (my_index // 2) % 4]).astype(jnp.int32)
    halves = [
        jnp.concatenate([ffn_reduced[:piece_rows], packed_reduced[: piece_rows // 3]], axis=0),
        jnp.concatenate([ffn_reduced[piece_rows:], packed_reduced[piece_rows // 3 :]], axis=0),
    ]
    pieces = [ring_pieces(halves[1], "z"), ring_pieces(halves[0], "y")]
    halves, pieces = marker.fence(halves, pieces)
    other_ring = run_join(places[:1], (halves[1], *pieces[0]), 1)
    one_ring = run_join(places[1:], (halves[0], *pieces[1]), 4)
    pieces = ring_pieces(other_ring, "y")
    other_ring, one_ring = marker.fence(other_ring, one_ring)
    gathered = trade_z(one_ring)
    one_ring, token_far = marker.fence(one_ring, token_far)
    token_own = [
        (grad_first[i] + (token_pair[i].astype(F32) + token_far[i].astype(F32))).astype(BF16)
        for i in range(2)
    ]
    token_other = [lax.ppermute(rows_here, "mp", CORE_SWAP) for rows_here in token_own]
    token_grad = run_settle(core_arg, (*token_own, *token_other))
    closing = finish(marker.state)[0, 0]
    part = piece_rows // 3
    so_far = run_spread_some(places, (other_ring, pieces[0]), piece_rows, part)
    so_far, token_grad = tie(so_far, token_grad)
    *rest, outer_grad = run_spread_rest(
        places, pieces[1:], gathered, so_far, piece_rows, part
    )
    inner_grad, *rest = rest
    cuts = [values.reshape(local_width, width) for values in rest[:4]]
    vectors = rest[4:]
    return (
        loss[0, 0] + closing,
        token_grad,
        cuts[1].T,
        vectors[7],
        cuts[2].T,
        cuts[3].T,
        vectors[8],
        cuts[0],
        vectors[0],
        vectors[1],
        vectors[2],
        inner_grad.reshape(width, width),
        vectors[6],
        outer_grad.reshape(width, width),
        vectors[3],
        vectors[4],
        vectors[5],
    )


def solution(mesh):
    column, row, split = P(None, "mp"), P("mp", None), P("mp")
    placed = (
        (P("dp", None), P("dp"), P())
        + (column, split, column, column, split, row)
        + (P(), P(), P())
        + (column, split, row)
        + (P(), P(), P())
    )
    given = (
        (P(), P("dp", None))
        + (column, split, column, column, split, row)
        + (P(), P(), P())
        + (column, split, row)
        + (P(), P(), P())
    )
    return jax.shard_map(local, mesh=mesh, in_specs=placed, out_specs=given, check_vma=False)
```

```python
import functools
import math

import jax
import jax.numpy as jnp
from jax import lax
from jax.experimental import pallas as pl
from jax.experimental.pallas import tpu as pltpu
from jax.sharding import PartitionSpec as P

HD = 64
EPS_NORM = 1e-06
SOFTMAX_WARMTH = 0.01
NEG_FILL = -1e30
HIGHEST = lax.Precision.HIGHEST
F32 = jnp.float32
BF16 = jnp.bfloat16
QB = 256
KB = 256

CORE_SWAP = [(i, i ^ 1) for i in range(4)]
FAR_SWAP = [(i, i ^ 2) for i in range(4)]
NEAR_SWAP = [(i, i ^ 1) for i in range(32)]
PLANES = [[i * 2 + x for i in range(16)] for x in range(2)]
Z_RINGS = [[i + 8 * z for z in range(4)] for i in range(8)]

SMEM = pl.BlockSpec(memory_space=pltpu.SMEM)
VMEM = pl.BlockSpec(memory_space=pltpu.VMEM)
HBM = pl.BlockSpec(memory_space=pltpu.HBM)


def nn(left, right):
    return lax.dot_general(left, right, (((1,), (0,)), ((), ())), preferred_element_type=F32)


def nt(left, right):
    return lax.dot_general(left, right, (((1,), (1,)), ((), ())), preferred_element_type=F32)


def tn(left, right):
    return lax.dot_general(left, right, (((0,), (0,)), ((), ())), preferred_element_type=F32)


def place_of_block(block, core, rows):
    return ((block % 2) * 2 + block // 2) * QB + core * (rows // 2) & (rows - 1)


def spot_of_keys(j, core, rows):
    place = (j * KB + core * (rows // 2)) & (rows - 1)
    block = place // QB
    return pl.multiple_of(((block % 2) * 2 + block // 2) * QB + place % QB, KB)


def segment_bounds(lengths_ref):
    bounds, total = [], jnp.int32(0)
    for s in range(lengths_ref.shape[0]):
        start = total
        total = total + lengths_ref[s]
        bounds.append((start, total))
    return bounds


def block_span(bounds, first, rows):
    place = first + lax.broadcasted_iota(jnp.int32, (1, QB), 1)
    low, high = first, first + KB
    begin = jnp.full((1, QB), bounds[-1][1], jnp.int32)
    end = jnp.full((1, QB), rows, jnp.int32)
    for start, stop in bounds:
        inside = (place >= start) & (place < stop)
        begin = jnp.where(inside, start, begin)
        end = jnp.where(inside, stop, end)
        touches = (stop > first) & (start < first + QB) & (stop > start)
        low = jnp.where(touches, jnp.minimum(low, start), low)
        high = jnp.where(touches, jnp.maximum(high, stop), high)
    return low // KB, (high + KB - 1) // KB, begin, end


def head_copies(values, heads):
    lane = lax.broadcasted_iota(jnp.int32, values.shape, 1) // HD
    blank = jnp.zeros_like(values)
    return jnp.concatenate([jnp.where(lane == h, values, blank) for h in range(heads)], axis=0)


def span_mask(begin, end, block, heads):
    place = block * KB + lax.broadcasted_iota(jnp.int32, (KB, QB), 0)
    keep = (place >= begin) & (place < end)
    return jnp.concatenate([keep] * heads, axis=1)


def attend(heads, blocks, core, bounds, q_ref, k_ref, vt_ref, mixed_ref, lse_ref, acc_ref):
    rows = k_ref.shape[0]
    for i, block in enumerate(blocks):
        low, high, begin, end = block_span(bounds, place_of_block(block, core, rows), rows)
        stack = head_copies(q_ref[block * QB : (block + 1) * QB, :], heads)
        acc_ref[...] = jnp.zeros(acc_ref.shape, F32)

        def step(j, carry, stack=stack, begin=begin, end=end):
            top, total = carry
            spot = spot_of_keys(j, core, rows)
            scores = nt(k_ref[pl.ds(spot, KB), :], stack)
            scores = jnp.where(span_mask(begin, end, j, heads), scores, NEG_FILL)
            peak = jnp.maximum(top, jnp.max(scores, axis=0, keepdims=True))
            fade = jnp.exp(top - peak)
            probs = jnp.exp(scores - peak)
            total = total * fade + jnp.sum(probs, axis=0, keepdims=True)
            probs = probs.astype(BF16)
            for h in range(heads):
                part = slice(h * QB, (h + 1) * QB)
                span = slice(h * HD, (h + 1) * HD)
                acc_ref[span, :] = acc_ref[span, :] * fade[:, part] + nn(
                    vt_ref[span, pl.ds(spot, KB)], probs[:, part]
                )
            return peak, total

        top = jnp.full((1, heads * QB), NEG_FILL, F32)
        top, total = lax.fori_loop(
            low, high, step, (top, jnp.zeros((1, heads * QB), F32)), unroll=False
        )
        scale = 1.0 / total
        mixed = jnp.concatenate(
            [
                acc_ref[h * HD : (h + 1) * HD, :] * scale[:, h * QB : (h + 1) * QB]
                for h in range(heads)
            ],
            axis=0,
        )
        mixed_ref[i * QB : (i + 1) * QB, :] = mixed.T.astype(BF16)
        lse_ref[i, :, :] = jnp.broadcast_to(top + jnp.log(total), (8, heads * QB))


def fetch(sources, targets, semaphores, order=()):
    copies = [
        pltpu.make_async_copy(source, target, semaphores.at[i])
        for i, (source, target) in enumerate(zip(sources, targets))
    ]
    for i in [*order, *(i for i in range(len(copies)) if i not in order)]:
        copies[i].start()
    return copies


def project(mixed_ref, weights_ref, results, outputs, semaphores):
    results[1][...] = nn(mixed_ref[QB:, :], weights_ref[...]).astype(BF16)
    copies = send_out(results, outputs, semaphores, (1,))
    results[0][...] = nn(mixed_ref[:QB, :], weights_ref[...])
    return copies + send_out(results, outputs, semaphores, (0,))


def attend_first(heads, blocks, lengths_ref, core_ref, *refs):
    sources, outputs, refs = refs[:13], refs[13:25], refs[25:]
    results, targets, refs = refs[:12], refs[12:24], refs[24:]
    acc_ref, semaphores, out_semaphores = refs
    x_ref, q_ref, k_ref, v_ref, kt_ref, vt_ref, mixed_ref, lse_ref = results[:8]
    wqt_ref, wkt_ref, wvt_ref, bq_ref, bv_ref, wo_ref = targets[:6]
    rows = x_ref.shape[0]
    core = core_ref[0]
    copies = fetch(sources[1:], targets, semaphores)
    row_copies = []
    for block in range(rows // QB):
        first = pl.multiple_of(place_of_block(block, core, rows), QB)
        row_copies.append(
            pltpu.make_async_copy(
                sources[0].at[pl.ds(first, QB), :],
                x_ref.at[pl.ds(block * QB, QB), :],
                semaphores.at[12 + block],
            )
        )
        row_copies[-1].start()
    for copy in copies:
        copy.wait()
    query_bias, value_bias = row_of(bq_ref), row_of(bv_ref)
    for block in range(rows // QB):
        row_copies[block].wait()
        part = slice(block * QB, (block + 1) * QB)
        x = x_ref[part, :]
        q = (nt(x, wqt_ref[...]) + query_bias).astype(BF16)
        q_ref[part, :] = q * BF16(0.125)
        k_ref[part, :] = nt(x, wkt_ref[...]).astype(BF16)
        kt_ref[:, part] = nt(wkt_ref[...], x).astype(BF16)
        v = nt(x, wvt_ref[...]) + value_bias
        v_ref[part, :] = v.astype(BF16)
        vt_ref[:, part] = v.T.astype(BF16)
    outgoing = send_out(results, outputs, out_semaphores, range(6))
    bounds = segment_bounds(lengths_ref)
    place = core * (2 * QB) + lax.broadcasted_iota(jnp.int32, (1, QB), 1)
    for i in range(2):
        member = [
            jnp.where((place + i * QB >= start) & (place + i * QB < stop), 1.0, 0.0)
            for start, stop in bounds
        ]
        results[10][i] = jnp.concatenate(member, axis=0)
    lines = [row_of(ref) for ref in targets[6:]]
    results[11][...] = jnp.concatenate(lines + [jnp.zeros((2, lines[0].shape[1]), F32)], axis=0)
    outgoing += send_out(results, outputs, out_semaphores, (10, 11))
    attend(heads, blocks, core, bounds, q_ref, k_ref, vt_ref, mixed_ref, lse_ref, acc_ref)
    outgoing += project(mixed_ref, wo_ref, results[8:], outputs[8:], out_semaphores.at[8:10])
    outgoing += send_out(results, outputs, out_semaphores, (6, 7))
    for copy in outgoing:
        copy.wait()


def attend_more(heads, blocks, lengths_ref, core_ref, *refs):
    sources, outputs, refs = refs[:4], refs[4:8], refs[8:]
    targets, results, refs = refs[:4], refs[4:8], refs[8:]
    acc_ref, semaphores, out_semaphores = refs
    q_ref, k_ref, vt_ref, wo_ref = targets
    mixed_ref, lse_ref = results[:2]
    for copy in fetch(sources, targets, semaphores):
        copy.wait()
    bounds = segment_bounds(lengths_ref)
    attend(heads, blocks, core_ref[0], bounds, q_ref, k_ref, vt_ref, mixed_ref, lse_ref, acc_ref)
    outgoing = project(mixed_ref, wo_ref, results[2:], outputs[2:], out_semaphores.at[2:])
    outgoing += send_out(results, outputs, out_semaphores, (0, 1))
    for copy in outgoing:
        copy.wait()


def attend_back(heads, inputs, lengths_ref, core_ref, *refs):
    sources, refs = refs[:inputs], refs[inputs:]
    outputs, refs = refs[:2], refs[2:]
    joint_ref, pack_ref = refs[:2]
    dk_ref, dv_ref, dqt_ref, wo_acc_ref, semaphores, out_semaphores = refs[2:8]
    targets = refs[8:]
    copies = fetch(sources, targets, semaphores, (8, 7, 9, 10, 0, 2, 6, 4, 1, 3, 5))
    grads = targets[0:2]
    mixed = targets[2:4]
    lses = targets[4:6]
    wo_ref, q_ref, k_ref, v_ref, kt_ref = targets[6:11]
    own_sums, other_sums, inner_ref, x_ref = targets[11:]
    rows, width = q_ref.shape
    core = core_ref[0]
    bounds = segment_bounds(lengths_ref)
    dk_ref[...] = jnp.zeros(dk_ref.shape, F32)
    dv_ref[...] = jnp.zeros(dv_ref.shape, F32)
    joint_ref[...] = jnp.zeros(joint_ref.shape, BF16)
    lane = lax.broadcasted_iota(jnp.int32, (8, width), 1) // HD
    which = (lane == lax.broadcasted_iota(jnp.int32, (8, width), 0)).astype(F32).astype(BF16)
    for i in (0, 2, 4, 6, 7, 8, 9, 10):
        copies[i].wait()
    for block in range(rows // QB):
        if block == 1:
            copies[1].wait()
        if block == 2:
            copies[3].wait()
            copies[5].wait()
        low, high, begin, end = block_span(bounds, place_of_block(block, core, rows), rows)
        part = slice(block * QB, (block + 1) * QB)
        own = slice(block % 2 * QB, block % 2 * QB + QB)
        grad_attn = grads[block % 2][block // 2 * QB : block // 2 * QB + QB, :]
        mixed_here = mixed[block // 2][own, :]
        outer = tn(mixed_here, grad_attn)
        wo_acc_ref[...] = outer if block == 0 else wo_acc_ref[...] + outer
        grad_mixed = nt(grad_attn, wo_ref[...]).astype(BF16)
        product = grad_mixed.astype(F32) * mixed_here.astype(F32)
        sums = sum(nt(which, part) for part in in_three(product)[:2])
        delta = jnp.concatenate([sums[h : h + 1, :] for h in range(heads)], axis=1)
        lse = lses[block // 2][block % 2, 0:1, :]
        q_stack = head_copies(q_ref[part, :], heads)
        g_stack = head_copies(grad_mixed, heads)
        dqt_ref[...] = jnp.zeros(dqt_ref.shape, F32)

        def step(
            j, carry, delta=delta, lse=lse, q_stack=q_stack, g_stack=g_stack, begin=begin, end=end
        ):
            here = pl.ds(spot_of_keys(j, core, rows), KB)
            scores = nt(k_ref[here, :], q_stack)
            scores = jnp.where(span_mask(begin, end, j, heads), scores, NEG_FILL)
            probs = jnp.exp(scores - lse)
            grad = (probs * (nt(v_ref[here, :], g_stack) - delta)).astype(BF16)
            dv_ref[here, :] += nn(probs.astype(BF16), g_stack)
            dk_ref[here, :] += nn(grad, q_stack)
            for h in range(heads):
                span = slice(h * HD, (h + 1) * HD)
                dqt_ref[span, :] += nn(kt_ref[span, here], grad[:, h * QB : (h + 1) * QB])
            return carry

        lax.fori_loop(low, high, step, 0, unroll=False)
        joint_ref[part, :width] = (dqt_ref[...].T * 0.125).astype(BF16)
    spans = [slice(256 * k, 256 * k + width) for k in range(3)]
    joint_ref[:, spans[1]] = dk_ref[...].astype(BF16)
    joint_ref[:, spans[2]] = dv_ref[...].astype(BF16)
    for copy in copies[11:]:
        copy.wait()
    outgoing = send_out(refs, outputs, out_semaphores, (0,))
    sums = [column_sum(joint_ref[:, spans[k]].astype(F32)) for k in (0, 2)]
    blank = jnp.zeros((1, 256 - width), F32)
    tail = jnp.concatenate([sums[0], blank, sums[1], blank, jnp.zeros((1, 256), F32)], axis=1)
    inner = row_of(inner_ref)
    paired = own_sums[0:6, :] + other_sums[0:6, :]
    small = [paired, inner, tail, jnp.zeros((8, tail.shape[1]), F32)]
    small = jnp.concatenate(small, axis=0).astype(BF16)
    piece = pack_ref.shape[1] - 16
    per = width // piece
    for m in range(4):
        total = wo_acc_ref[...] if m == 0 else tn(joint_ref[:, spans[m - 1]], x_ref[...])
        for t in range(per):
            cut = total[t * piece : (t + 1) * piece, :].astype(BF16)
            pack_ref[m * per + t, 0:piece, :] = cut
            pack_ref[m * per + t, piece:, :] = small if m + t == 0 else jnp.zeros_like(small)
        here = pl.ds(m * per, per)
        copy = pltpu.make_async_copy(
            pack_ref.at[here], outputs[1].at[here], out_semaphores.at[1 + m]
        )
        copy.start()
        outgoing.append(copy)
    for copy in outgoing:
        copy.wait()


def shaped(shape, dtype):
    return jax.ShapeDtypeStruct(shape, dtype)


PARAMS = pltpu.CompilerParams(vmem_limit_bytes=60 << 20)
SMALL = pltpu.CompilerParams(vmem_limit_bytes=60 << 20)
SHARED = pltpu.CompilerParams(vmem_limit_bytes=24 << 20)
COST = pl.CostEstimate(flops=1024, bytes_accessed=1024, transcendentals=0)


def buffers(arrays):
    return [pltpu.VMEM(array.shape, array.dtype) for array in arrays]


def attend_shapes(count, heads, width):
    rows = count * QB
    return (
        shaped((rows, heads * HD), BF16),
        shaped((count, 8, heads * QB), F32),
        shaped((rows // 2, width), F32),
        shaped((rows // 2, width), BF16),
    )


def run_first(lengths, core, tokens, weights, blocks):
    rows, width = tokens.shape
    local_width = weights[0].shape[0]
    heads = local_width // HD
    outs = (
        (shaped(tokens.shape, BF16),)
        + (shaped((rows, local_width), BF16),) * 3
        + (shaped((local_width, rows), BF16),) * 2
        + attend_shapes(len(blocks), heads, width)
        + (shaped((2, lengths.shape[0], QB), F32), shaped((8, width), F32))
    )
    return pl.pallas_call(
        functools.partial(attend_first, heads, blocks),
        out_shape=outs,
        in_specs=[SMEM] * 2 + [HBM] * 13,
        out_specs=(HBM,) * 12,
        scratch_shapes=buffers(outs)
        + buffers(weights)
        + [pltpu.VMEM((local_width, QB), F32)]
        + [pltpu.SemaphoreType.DMA((12 + rows // QB,)), pltpu.SemaphoreType.DMA((12,))],
        compiler_params=PARAMS,
        name="attend_first",
        cost_estimate=COST,
    )(lengths, core, tokens, *weights)


def run_more(lengths, core, arrays, blocks):
    rows, local_width = arrays[0].shape
    heads = local_width // HD
    outs = attend_shapes(len(blocks), heads, arrays[3].shape[1])
    return pl.pallas_call(
        functools.partial(attend_more, heads, blocks),
        out_shape=outs,
        in_specs=[SMEM] * 2 + [HBM] * 4,
        out_specs=(HBM,) * 4,
        scratch_shapes=buffers(arrays)
        + buffers(outs)
        + [pltpu.VMEM((local_width, QB), F32)]
        + [pltpu.SemaphoreType.DMA((4,)), pltpu.SemaphoreType.DMA((4,))],
        compiler_params=PARAMS,
        name="attend_more",
        cost_estimate=COST,
    )(lengths, core, *arrays)


def run_back(lengths, core, arrays):
    wo, q, x = arrays[6], arrays[7], arrays[-1]
    rows, width = q.shape
    heads = width // HD
    piece = 4 * width // 16
    outs = (shaped((rows, 3 * 256), BF16), shaped((16, piece + 16, x.shape[1]), BF16))
    return pl.pallas_call(
        functools.partial(attend_back, heads, len(arrays)),
        out_shape=outs,
        in_specs=[SMEM] * 2 + [HBM] * len(arrays),
        out_specs=(HBM,) * 2,
        scratch_shapes=buffers(outs)
        + [pltpu.VMEM((rows, width), F32)] * 2
        + [pltpu.VMEM((width, QB), F32), pltpu.VMEM(wo.shape, F32)]
        + [pltpu.SemaphoreType.DMA((len(arrays),)), pltpu.SemaphoreType.DMA((5,))]
        + buffers(arrays),
        compiler_params=PARAMS,
        name="attend_back",
        cost_estimate=COST,
    )(lengths, core, *arrays)


def mark_kernel(source_ref, target_ref):
    del source_ref, target_ref


def mark(values):
    return pl.pallas_call(
        mark_kernel,
        out_shape=shaped(values.shape, values.dtype),
        in_specs=[HBM],
        out_specs=HBM,
        compiler_params=pltpu.CompilerParams(vmem_limit_bytes=1 << 20),
        name="mark",
        cost_estimate=pl.CostEstimate(flops=1 << 36, bytes_accessed=1 << 10, transcendentals=0),
    )(values)


def finish_kernel(source_ref, target_ref):
    del source_ref
    target_ref[...] = jnp.zeros(target_ref.shape, F32)


def finish(values):
    return pl.pallas_call(
        finish_kernel,
        out_shape=shaped(values.shape, values.dtype),
        in_specs=[HBM],
        out_specs=VMEM,
        compiler_params=pltpu.CompilerParams(vmem_limit_bytes=1 << 20),
        name="finish",
        cost_estimate=COST,
    )(values)


def row_of(ref):
    return ref[...].astype(F32).reshape(1, -1)


def in_three(values):
    high = values.astype(BF16)
    rest = values - high.astype(F32)
    middle = rest.astype(BF16)
    return high, middle, (rest - middle.astype(F32)).astype(BF16)


def norm_step(grad, normed, rscale, gain):
    scaled = grad * gain
    first_mean = jnp.mean(scaled, axis=1, keepdims=True)
    cross_mean = jnp.mean(scaled * normed, axis=1, keepdims=True)
    return rscale * (scaled - first_mean - normed * cross_mean)


def column_of(ref):
    row = ref[...].reshape(1, -1)
    return jnp.broadcast_to(row, (128, row.shape[1])).T[:, 0:1]


def column_sum(values):
    return jnp.sum(values, axis=0, keepdims=True)


def send_out(results, outputs, semaphores, which):
    copies = [
        pltpu.make_async_copy(results[k], outputs[k], semaphores.at[k]) for k in which
    ]
    for copy in copies:
        copy.start()
    return copies


def send_rows(results, outputs, semaphores, i):
    here = pl.ds(i * QB, QB)
    copies = [
        pltpu.make_async_copy(
            results[k].at[here, :], outputs[k].at[here, :], semaphores.at[4 + 2 * i + k]
        )
        for k in (1, 0)
    ]
    for copy in copies:
        copy.start()
    return copies


def loss_back(lengths_ref, place_ref, *refs):
    sources, outputs, refs = refs[:9], refs[9:13], refs[13:]
    targets, results = refs[:9], refs[9:13]
    coef_ref, turned_ref, semaphores, out_semaphores = refs[13:]
    copies = fetch(sources, targets, semaphores)
    piece_ref, swapped_ref, pooled_ref, match_ref, gain_ref = targets[:5]
    core, index = place_ref[0], place_ref[1]
    bounds = segment_bounds(lengths_ref)
    for copy in copies[:5]:
        copy.wait()
    first = core == 0
    queries = jnp.where(first, piece_ref[...], swapped_ref[...])
    passages = jnp.where(first, swapped_ref[...], piece_ref[...])
    count = queries.shape[0]
    own = pooled_ref.shape[0] // 2
    similarity = nt(queries, passages) / SOFTMAX_WARMTH
    match = match_ref[...].reshape(1, -1)
    match = match == lax.broadcasted_iota(jnp.int32, (count, count), 0)
    top = jnp.max(similarity, axis=1, keepdims=True)
    lse = top + jnp.log(jnp.sum(jnp.exp(similarity - top), axis=1, keepdims=True))
    positive = jnp.sum(jnp.where(match, similarity, 0.0), axis=1, keepdims=True)
    loss = jnp.sum(lse - positive, axis=0, keepdims=True) / count
    results[3][...] = jnp.broadcast_to(loss, results[3].shape)
    coef = (jnp.exp(similarity - lse) - match.astype(F32)) * (1.0 / (count * SOFTMAX_WARMTH))
    coef_ref[...] = coef
    turned_ref[...] = coef.T
    here = pl.ds(pl.multiple_of(index * own, own), own)
    grad_query = sum(nn(part, passages) for part in in_three(coef_ref[here, :])[:2])
    grad_passage = sum(nn(part, queries) for part in in_three(turned_ref[here, :])[:2])
    grad_unit = jnp.concatenate([grad_query, grad_passage], axis=0)
    pooled = pooled_ref[...]
    rscale = lax.rsqrt(jnp.sum(pooled * pooled, axis=1, keepdims=True) + EPS_NORM)
    inner = jnp.sum(pooled * grad_unit, axis=1, keepdims=True)
    grad_pooled = rscale * grad_unit - rscale * rscale * rscale * inner * pooled
    seqs = 2 * own
    grad_pooled = jnp.concatenate(
        [grad_pooled, jnp.zeros((128 - seqs, grad_pooled.shape[1]), F32)], axis=0
    )
    parts = in_three(grad_pooled)[:2]
    lane = lax.broadcasted_iota(jnp.int32, (1, 128), 1)
    begin = end = jnp.zeros((1, 128), jnp.int32)
    for seq, (start, stop) in enumerate(bounds):
        begin = jnp.where(lane == seq, start, begin)
        end = jnp.where(lane == seq, stop, end)
    gain = row_of(gain_ref)
    sums = [0.0, 0.0, 0.0]
    outgoing = []
    for i in range(2):
        copies[5 + 2 * i].wait()
        copies[6 + 2 * i].wait()
        normed = targets[5 + 2 * i][...]
        place = core * (2 * QB) + i * QB + lax.broadcasted_iota(jnp.int32, (QB, 128), 0)
        member = jnp.where((place >= begin) & (place < end), 1.0, 0.0).astype(BF16)
        grad = sum(nn(member, part) for part in parts)
        second = norm_step(grad, normed, column_of(targets[6 + 2 * i]), gain)
        rounded = second.astype(BF16)
        here = pl.ds(i * QB, QB)
        results[0][here, :] = second
        results[1][here, :] = rounded
        outgoing += send_rows(results, outputs, out_semaphores, i)
        for k, values in enumerate((rounded.astype(F32), grad * normed, grad)):
            sums[k] = sums[k] + column_sum(values)
    results[2][...] = jnp.concatenate(sums + [jnp.zeros((5, sums[0].shape[1]), F32)], axis=0)
    outgoing += send_out(results, outputs, out_semaphores, (2, 3))
    for copy in outgoing:
        copy.wait()


def norm_back(*refs):
    sources, outputs, refs = refs[:9], refs[9:12], refs[12:]
    targets, results = refs[:9], refs[9:12]
    semaphores, out_semaphores = refs[12:]
    copies = fetch(sources, targets, semaphores)
    for copy in copies[:5]:
        copy.wait()
    gain = row_of(targets[0])
    second, pair_here, far = targets[2:5]
    sums = [0.0, 0.0, 0.0]
    outgoing = []
    for i in range(2):
        copies[5 + 2 * i].wait()
        copies[6 + 2 * i].wait()
        here = pl.ds(i * QB, QB)
        exchanged = pair_here[here, :].astype(F32) + far[here, :].astype(F32)
        grad = second[here, :] + exchanged
        normed = targets[5 + 2 * i][...]
        first = norm_step(grad, normed, column_of(targets[6 + 2 * i]), gain)
        rounded = first.astype(BF16)
        results[0][here, :] = first
        results[1][here, :] = rounded
        outgoing += send_rows(results, outputs, out_semaphores, i)
        for k, values in enumerate((rounded.astype(F32), grad * normed, grad)):
            sums[k] = sums[k] + column_sum(values)
    blank = jnp.zeros((2, sums[0].shape[1]), F32)
    results[2][...] = jnp.concatenate(sums + [targets[1][0:3, :], blank], axis=0)
    outgoing += send_out(results, outputs, out_semaphores, (2,))
    for copy in outgoing:
        copy.wait()


STEPS = (0, 2, 1, 3)


def join(copies_of_each, place_ref, *refs):
    sources, output, semaphores = refs[:4], refs[4], refs[5]
    copies = []
    for k in range(4):
        spot = (place_ref[0] + 4 - STEPS[k]) % 4
        for r in range(copies_of_each):
            goal = output.at[spot] if copies_of_each == 1 else output.at[r, spot]
            semaphore = semaphores.at[k * copies_of_each + r]
            copies.append(pltpu.make_async_copy(sources[k], goal, semaphore))
            copies[-1].start()
    for copy in copies:
        copy.wait()


def place_block(piece, part, block_ref, spot, outputs, buffers_, semaphores, first):
    inner, cuts = buffers_
    inner[...] = block_ref[:, :piece, :].astype(F32)
    cuts[...] = block_ref[:, piece : 2 * piece - part, :].astype(F32)
    copies = [pltpu.make_async_copy(inner, outputs[0].at[:, spot], semaphores.at[first])]
    for m in range(4):
        goal = outputs[1 + m].at[spot, pl.ds(part, piece - part), :]
        copies.append(pltpu.make_async_copy(cuts.at[m], goal, semaphores.at[first + 1 + m]))
    for copy in copies:
        copy.start()
    return copies


def place_vectors(piece, part, block_ref, spot, outputs, vectors, semaphores, first):
    @pl.when(spot == 0)
    def _():
        small = block_ref[0, 2 * piece - part :, :].astype(F32)
        for k in range(7):
            vectors[k][...] = small[k : k + 1, :].reshape(-1)
        count = vectors[7].shape[0]
        for k in range(2):
            vectors[7 + k][...] = small[7:8, 256 * k : 256 * k + count].reshape(-1)
        copies = [
            pltpu.make_async_copy(vectors[k], outputs[5 + k], semaphores.at[first + k])
            for k in range(9)
        ]
        for copy in copies:
            copy.start()
        for copy in copies:
            copy.wait()


def spread_some(piece, part, count, place_ref, *refs):
    sources, outputs, refs = refs[:count], refs[count : count + 14], refs[count + 14 :]
    blocks, refs = refs[:count], refs[count:]
    buffers_, vectors, refs = refs[: 2 * count], refs[2 * count : 2 * count + 9], refs[-2:]
    arrivals = fetch(sources, blocks, refs[0])
    outgoing, spots = [], []
    for k in range(count):
        arrivals[k].wait()
        spots.append((place_ref[1] + 4 - STEPS[k]) % 4)
        outgoing += place_block(
            piece, part, blocks[k], spots[k], outputs, buffers_[2 * k : 2 * k + 2], refs[1], 5 * k
        )
    for k in range(count):
        place_vectors(piece, part, blocks[k], spots[k], outputs, vectors, refs[1], 5 * count)
    for copy in outgoing:
        copy.wait()


def spread_rest(piece, part, place_ref, *refs):
    sources, outputs, refs = refs[:3], refs[17:32], refs[32:]
    blocks, by_z, refs = refs[:2], refs[2], refs[3:]
    buffers_, outer, heads, vectors, refs = refs[:4], refs[4], refs[5], refs[6:15], refs[15:]
    semaphores, out_semaphores = refs
    arrivals = fetch(sources, (*blocks, by_z), semaphores)
    outgoing, spots = [], []
    for k in range(2):
        spots.append((place_ref[1] + 4 - STEPS[2 + k]) % 4)
        arrivals[k].wait()
        outgoing += place_block(
            piece,
            part,
            blocks[k],
            spots[k],
            outputs,
            buffers_[2 * k : 2 * k + 2],
            out_semaphores,
            5 * k,
        )
    arrivals[2].wait()
    outer[...] = by_z[:, :, :piece, :].astype(F32)
    copies = [pltpu.make_async_copy(outer, outputs[14], out_semaphores.at[10])]
    copies[0].start()
    heads[...] = by_z[:, :, piece:, :].astype(F32)
    for m in range(4):
        goal = outputs[1 + m].at[:, pl.ds(0, part), :]
        copies.append(pltpu.make_async_copy(heads.at[m], goal, out_semaphores.at[11 + m]))
        copies[-1].start()
    for k in range(2):
        place_vectors(piece, part, blocks[k], spots[k], outputs, vectors, out_semaphores, 15)
    for copy in outgoing + copies:
        copy.wait()


def run_loss(lengths, place, arrays):
    rows, width = arrays[5].shape
    count = arrays[0].shape[0]
    outs = (
        shaped((2 * rows, width), F32),
        shaped((2 * rows, width), BF16),
        shaped((8, width), F32),
        shaped((8, 128), F32),
    )
    return pl.pallas_call(
        loss_back,
        out_shape=outs,
        in_specs=[SMEM] * 2 + [HBM] * 9,
        out_specs=(HBM,) * 4,
        scratch_shapes=buffers(arrays)
        + buffers(outs)
        + [pltpu.VMEM((count, count), F32)] * 2
        + [pltpu.SemaphoreType.DMA((9,)), pltpu.SemaphoreType.DMA((8,))],
        compiler_params=SHARED,
        name="loss_back",
        cost_estimate=COST,
    )(lengths, place, *arrays)


def run_norm(arrays):
    rows, width = arrays[2].shape
    outs = (shaped((rows, width), F32), shaped((rows, width), BF16), shaped((8, width), F32))
    return pl.pallas_call(
        norm_back,
        out_shape=outs,
        in_specs=[HBM] * 9,
        out_specs=(HBM,) * 3,
        scratch_shapes=buffers(arrays)
        + buffers(outs)
        + [pltpu.SemaphoreType.DMA((9,)), pltpu.SemaphoreType.DMA((8,))],
        compiler_params=SMALL,
        name="norm_back",
        cost_estimate=COST,
    )(*arrays)


def run_join(place, pieces, copies_of_each):
    lead = (4,) if copies_of_each == 1 else (copies_of_each, 4)
    return pl.pallas_call(
        functools.partial(join, copies_of_each),
        out_shape=shaped(lead + pieces[0].shape, BF16),
        in_specs=[SMEM] + [HBM] * 4,
        out_specs=HBM,
        scratch_shapes=[pltpu.SemaphoreType.DMA((4 * copies_of_each,))],
        compiler_params=pltpu.CompilerParams(vmem_limit_bytes=1 << 20),
        name="join",
        cost_estimate=COST,
    )(place, *pieces)


def settle(core_ref, *refs):
    sources, output, semaphores = refs[:4], refs[4], refs[5]
    copies = []
    for k in range(4):
        first = (k // 2 + core_ref[0]) % 2 * (2 * QB) + k % 2 * QB
        spot = pl.ds(pl.multiple_of(first, QB), QB)
        copies.append(pltpu.make_async_copy(sources[k], output.at[spot, :], semaphores.at[k]))
        copies[-1].start()
    for copy in copies:
        copy.wait()


def run_settle(core, parts):
    rows, width = parts[0].shape
    return pl.pallas_call(
        settle,
        out_shape=shaped((4 * rows, width), BF16),
        in_specs=[SMEM] + [HBM] * 4,
        out_specs=HBM,
        scratch_shapes=[pltpu.SemaphoreType.DMA((4,))],
        compiler_params=pltpu.CompilerParams(vmem_limit_bytes=1 << 20),
        name="settle",
        cost_estimate=COST,
    )(core, *parts)


def spread_shapes(piece, width):
    shapes = [(4, 4, piece, width)] + [(4, piece, width)] * 4
    return shapes + [(width,)] * 7 + [(4 * piece,)] * 2


def run_spread_some(places, blocks, piece, part):
    width = blocks[0].shape[2]
    shapes = spread_shapes(piece, width)
    count = len(blocks)
    pair_of = [pltpu.VMEM((4, piece, width), F32), pltpu.VMEM((4, piece - part, width), F32)]
    return pl.pallas_call(
        functools.partial(spread_some, piece, part, count),
        out_shape=[shaped(shape, F32) for shape in shapes],
        in_specs=[SMEM] + [HBM] * count,
        out_specs=[HBM] * 14,
        scratch_shapes=buffers(blocks)
        + pair_of * count
        + [pltpu.VMEM(shape, F32) for shape in shapes[5:]]
        + [pltpu.SemaphoreType.DMA((count,)), pltpu.SemaphoreType.DMA((5 * count + 9,))],
        compiler_params=SHARED,
        name="spread_some",
        cost_estimate=COST,
    )(places, *blocks)


def run_spread_rest(places, blocks, gathered, so_far, piece, part):
    width = gathered.shape[3]
    shapes = spread_shapes(piece, width)
    outer = (4, 4, piece, width)
    pair_of = [pltpu.VMEM((4, piece, width), F32), pltpu.VMEM((4, piece - part, width), F32)]
    return pl.pallas_call(
        functools.partial(spread_rest, piece, part),
        out_shape=[shaped(shape, F32) for shape in shapes + [outer]],
        in_specs=[SMEM] + [HBM] * 17,
        out_specs=[HBM] * 15,
        input_output_aliases={4 + k: k for k in range(14)},
        scratch_shapes=buffers((*blocks, gathered))
        + pair_of * 2
        + [pltpu.VMEM(outer, F32), pltpu.VMEM((4, 4, part, width), F32)]
        + [pltpu.VMEM(shape, F32) for shape in shapes[5:]]
        + [pltpu.SemaphoreType.DMA((3,)), pltpu.SemaphoreType.DMA((24,))],
        compiler_params=SHARED,
        name="spread_rest",
        cost_estimate=COST,
    )(places, *blocks, gathered, *so_far)


def trade(values):
    return lax.all_to_all(
        values, "dp", split_axis=0, concat_axis=0, axis_index_groups=PLANES, tiled=True
    )


def share(values):
    spread_out = jnp.broadcast_to(values[None], (32,) + values.shape)
    return lax.all_to_all(spread_out, "dp", split_axis=0, concat_axis=0, tiled=True)


def trade_z(values):
    return lax.all_to_all(
        values, "dp", split_axis=0, concat_axis=0, axis_index_groups=Z_RINGS, tiled=True
    )


def ring_shift(axis, step):
    pairs = []
    for i in range(32):
        z, y, x = i // 8, (i // 2) % 4, i % 2
        z, y = ((z + step) % 4, y) if axis == "z" else (z, (y + step) % 4)
        pairs.append((i, (z * 4 + y) * 2 + x))
    return pairs


def ring_pieces(values, axis):
    return [lax.ppermute(values, "dp", ring_shift(axis, step)) for step in STEPS[1:]]


def tie(values, others):
    return lax.optimization_barrier((values, others))


class Marker:
    def __init__(self):
        self.state = jnp.zeros((8, 128), F32)

    def fence(self, ready, later):
        ready, state = tie(ready, self.state)
        later, self.state = tie(later, mark(state))
        return ready, later

    def moved(self, values, axis, pairs):
        values, state = tie(values, self.state)
        arrived, self.state = tie(lax.ppermute(values, axis, pairs), mark(state))
        return arrived

    def core_swap(self, values):
        return self.moved(values, "mp", CORE_SWAP)

    def near_swap(self, values):
        return self.moved(values, "dp", NEAR_SWAP)

    def both(self, own):
        return jnp.concatenate([own, self.core_swap(own)], axis=0)

    def near_sum(self, total):
        return (total.astype(F32) + self.near_swap(total).astype(F32)).astype(BF16)


def plane_sum(parts):
    return jnp.sum(parts.astype(F32), axis=0).astype(BF16)


def far_swap(values):
    return lax.ppermute(values, "mp", FAR_SWAP)


def norm_forward(values, gain_vec, shift_vec):
    average = jnp.mean(values, axis=-1, keepdims=True)
    centred = values - average
    rscale = lax.rsqrt(jnp.mean(centred * centred, axis=-1, keepdims=True) + EPS_NORM)
    normed = centred * rscale
    return (normed * gain_vec + shift_vec, normed, rscale[:, 0])


def gelu_and_slope(upper):
    below = 0.5 * (1.0 + lax.erf(upper * math.sqrt(0.5)))
    density = jnp.exp(-0.5 * upper * upper) * (1.0 / math.sqrt(2.0 * math.pi))
    return (upper * below).astype(BF16), (below + upper * density).astype(BF16)


def local(
    tokens,
    lengths,
    pair_index,
    query_proj,
    query_bias,
    key_proj,
    value_proj,
    value_bias,
    output_proj,
    output_bias,
    attn_gain,
    attn_shift,
    inner_proj,
    inner_bias,
    outer_proj,
    outer_bias,
    final_gain,
    final_shift,
):
    row_count, width = tokens.shape
    chunk = row_count // 2
    half = chunk // 2
    seq_count = lengths.shape[0]
    pair_count = seq_count // 2
    overall_pair_count = pair_index.shape[0]
    local_width = query_proj.shape[1]
    core = lax.axis_index("mp") % 2
    my_index = lax.axis_index("dp")
    marker = Marker()
    core_arg = jnp.reshape(core, (1,)).astype(jnp.int32)
    vectors = (output_bias, attn_gain, attn_shift, outer_bias, final_gain, final_shift)
    query_t, key_t, value_t = query_proj.T, key_proj.T, value_proj.T
    blank = jnp.zeros((256 - local_width, width), BF16)
    joint_proj = jnp.concatenate([query_t, blank, key_t, blank, value_t, blank], axis=0)

    weights = (query_t, key_t, value_t, query_bias, value_bias, output_proj, *vectors)
    first = run_first(lengths, core_arg, tokens, weights, (0, 1))
    rows, query_b, key_b, value_b, key_tb, value_tb, mixed_a, lse_a = first[:8]
    attn_own_a, attn_other_a, members, vectors = first[8:]

    def own_and_other(values, weights):
        return nn(values[:half], weights), nn(values[half:], weights).astype(BF16)

    def pair(own, arrived):
        return (own + arrived.astype(F32)).astype(BF16)

    def first_norm(index, pair_here, far):
        attn_full = pair_here.astype(F32) + far.astype(F32) + output_bias
        own_tokens = rows[index * chunk : index * chunk + half].astype(F32)
        return norm_forward(own_tokens + attn_full, attn_gain_f, attn_shift_f)

    def feed_forward(own_hidden):
        whole = marker.both(own_hidden)
        act, slope = gelu_and_slope(nn(whole, inner_proj) + inner_bias.astype(F32))
        act, slope = tie(act, slope)
        return whole, act, slope

    def last_norm(hidden, pair_here, far):
        ffn_full = pair_here.astype(F32) + far.astype(F32) + outer_bias
        return norm_forward(hidden + ffn_full, final_gain_f, final_shift_f)

    attn_pair_a = pair(attn_own_a, marker.core_swap(attn_other_a))
    attn_far_a = far_swap(attn_pair_a)
    output_bias, attn_gain_f, attn_shift_f = vectors[0], vectors[1], vectors[2]
    outer_bias, final_gain_f, final_shift_f = vectors[3], vectors[4], vectors[5]
    late_query, late_pair = tie(query_b, attn_pair_a)
    mixed_b, lse_b, attn_own_b, attn_other_b = run_more(
        lengths, core_arg, (late_query, key_b, value_tb, output_proj), (2, 3)
    )
    attn_pair_b = pair(attn_own_b, marker.core_swap(attn_other_b))
    attn_far_b = far_swap(attn_pair_b)
    attn_far_a, attn_pair_b = tie(attn_far_a, attn_pair_b)
    hidden_a, normed_one_a, rscale_one_a = first_norm(0, late_pair, attn_far_a)
    own_hidden_a = hidden_a.astype(BF16)
    hidden_ab, act_a, slope_a = feed_forward(own_hidden_a)
    ffn_own_a, ffn_other_a = own_and_other(act_a, outer_proj)
    ffn_pair_a = pair(ffn_own_a, marker.core_swap(ffn_other_a))
    attn_far_b, ffn_pair_late = tie(attn_far_b, ffn_pair_a)
    ffn_far_a = far_swap(ffn_pair_a)
    hidden_b, normed_one_b, rscale_one_b = first_norm(1, attn_pair_b, attn_far_b)
    own_hidden_b = hidden_b.astype(BF16)
    hidden_bb, act_b, slope_b = feed_forward(own_hidden_b)
    ffn_own_b, ffn_other_b = own_and_other(act_b, outer_proj)
    ffn_pair_b = pair(ffn_own_b, marker.core_swap(ffn_other_b))
    ffn_pair_b, ffn_far_a = marker.fence(ffn_pair_b, ffn_far_a)
    final_a, normed_two_a, rscale_two_a = last_norm(hidden_a, ffn_pair_late, ffn_far_a)
    pooled_a = jnp.dot(members[0], final_a, precision=HIGHEST)
    final_b, normed_two_b, rscale_two_b = last_norm(hidden_b, ffn_pair_b, far_swap(ffn_pair_b))
    pooled_part = pooled_a + jnp.dot(members[1], final_b, precision=HIGHEST)
    lse = (lse_a, lse_b)
    hidden_whole, act, slope = (hidden_ab, hidden_bb), (act_a, act_b), (slope_a, slope_b)
    normed_one, rscale_one = (normed_one_a, normed_one_b), (rscale_one_a, rscale_one_b)
    normed_two, rscale_two = (normed_two_a, normed_two_b), (rscale_two_a, rscale_two_b)
    pooled = pooled_part + marker.core_swap(pooled_part)
    pool_rscale = lax.rsqrt(jnp.sum(pooled * pooled, axis=-1, keepdims=True) + EPS_NORM)
    unit_b = (pooled * pool_rscale).astype(BF16)

    piece = lax.dynamic_slice_in_dim(unit_b, core * pair_count, pair_count, 0)
    piece = share(piece).reshape(overall_pair_count, width)
    place_arg = jnp.stack([core, my_index]).astype(jnp.int32)
    whole = [
        jnp.concatenate([a[:half], b[:half], a[half:], b[half:]], axis=0)
        for a, b in (act, slope, hidden_whole)
    ]
    piece, (whole_act, whole_slope, whole_hidden) = tie(piece, whole)
    grad_second, own_grad, last_sums, loss = run_loss(
        lengths,
        place_arg,
        (
            piece,
            marker.core_swap(piece),
            pooled,
            pair_index,
            final_gain,
            normed_two[0],
            rscale_two[0],
            normed_two[1],
            rscale_two[1],
        ),
    )

    grad_ffn = marker.both(own_grad)
    grad_up = (nt(grad_ffn, outer_proj) * whole_slope.astype(F32)).astype(BF16)
    inner_sum = jnp.sum(grad_up.astype(F32), axis=0)
    other = nt(grad_up[chunk:], inner_proj).astype(BF16)
    whole_act, other = tie(whole_act, other)
    outer_part = tn(whole_act, grad_ffn).astype(BF16)
    arrived, outer_part = tie(lax.ppermute(other, "mp", CORE_SWAP), outer_part)
    hidden_pair = pair(nt(grad_up[:chunk], inner_proj), arrived)
    hidden_far = far_swap(hidden_pair)
    whole_hidden, hidden_pair = tie(whole_hidden, hidden_pair)
    inner_part = tn(whole_hidden, grad_up).astype(BF16)
    ffn_pack = jnp.concatenate(
        [outer_part.reshape(16, -1, width), inner_part.reshape(16, -1, width)], axis=1
    )
    ffn_pack, hidden_far = marker.fence(ffn_pack, hidden_far)
    ffn_parts = trade(ffn_pack)

    grad_first, own_grad, sums = run_norm(
        (
            attn_gain,
            last_sums,
            grad_second,
            hidden_pair,
            hidden_far,
            normed_one[0],
            rscale_one[0],
            normed_one[1],
            rscale_one[1],
        )
    )
    (own_grad, sums), state = tie((own_grad, sums), marker.state)
    arrived = [lax.ppermute(values, "mp", CORE_SWAP) for values in (own_grad, sums)]
    (other_grad, other_sums), marker.state = tie(arrived, mark(state))
    grad_rows, packed = run_back(
        lengths,
        core_arg,
        (
            own_grad,
            other_grad,
            mixed_a,
            mixed_b,
            *lse,
            output_proj,
            query_b,
            key_b,
            value_b,
            key_tb,
            sums,
            other_sums,
            inner_sum,
            rows,
        ),
    )

    def input_part(first):
        span = slice(first, first + half)
        return nn(grad_rows[span], joint_proj)

    token_pair = []
    for i in range(2):
        other = input_part(i * chunk + half).astype(BF16)
        token_pair.append(pair(input_part(i * chunk), marker.core_swap(other)))
    token_pair, (packed, ffn_parts) = marker.fence(token_pair, (packed, ffn_parts))
    (packed, token_pair), ffn_parts = marker.fence((packed, token_pair), ffn_parts)
    packed_parts = trade(packed)
    token_far = [far_swap(token_pair[i]) for i in range(2)]
    ffn_total = plane_sum(ffn_parts)
    ffn_near = lax.ppermute(ffn_total, "dp", NEAR_SWAP)
    ffn_reduced = (ffn_total.astype(F32) + ffn_near.astype(F32)).astype(BF16)
    ffn_reduced, packed_parts = tie(ffn_reduced, packed_parts)
    packed_reduced = marker.near_sum(plane_sum(packed_parts))
    token_far, packed_reduced = tie(token_far, packed_reduced)
    piece_rows = width // 16
    places = jnp.stack([my_index // 8, (my_index // 2) % 4]).astype(jnp.int32)
    halves = [
        jnp.concatenate([ffn_reduced[:piece_rows], packed_reduced[: piece_rows // 3]], axis=0),
        jnp.concatenate([ffn_reduced[piece_rows:], packed_reduced[piece_rows // 3 :]], axis=0),
    ]
    pieces = [ring_pieces(halves[1], "z"), ring_pieces(halves[0], "y")]
    halves, pieces = marker.fence(halves, pieces)
    other_ring = run_join(places[:1], (halves[1], *pieces[0]), 1)
    one_ring = run_join(places[1:], (halves[0], *pieces[1]), 4)
    pieces = ring_pieces(other_ring, "y")
    other_ring, one_ring = marker.fence(other_ring, one_ring)
    gathered = trade_z(one_ring)
    one_ring, token_far = marker.fence(one_ring, token_far)
    token_own = [
        (grad_first[i * half : (i + 1) * half] + (token_pair[i].astype(F32) + token_far[i].astype(F32))).astype(BF16)
        for i in range(2)
    ]
    token_other = [lax.ppermute(rows_here, "mp", CORE_SWAP) for rows_here in token_own]
    token_grad = run_settle(core_arg, (*token_own, *token_other))
    closing = finish(marker.state)[0, 0]
    part = piece_rows // 3
    so_far = run_spread_some(places, (other_ring, pieces[0]), piece_rows, part)
    so_far, token_grad = tie(so_far, token_grad)
    *rest, outer_grad = run_spread_rest(
        places, pieces[1:], gathered, so_far, piece_rows, part
    )
    inner_grad, *rest = rest
    cuts = [values.reshape(local_width, width) for values in rest[:4]]
    vectors = rest[4:]
    return (
        loss[0, 0] + closing,
        token_grad,
        cuts[1].T,
        vectors[7],
        cuts[2].T,
        cuts[3].T,
        vectors[8],
        cuts[0],
        vectors[0],
        vectors[1],
        vectors[2],
        inner_grad.reshape(width, width),
        vectors[6],
        outer_grad.reshape(width, width),
        vectors[3],
        vectors[4],
        vectors[5],
    )


def solution(mesh):
    column, row, split = P(None, "mp"), P("mp", None), P("mp")
    placed = (
        (P("dp", None), P("dp"), P())
        + (column, split, column, column, split, row)
        + (P(), P(), P())
        + (column, split, row)
        + (P(), P(), P())
    )
    given = (
        (P(), P("dp", None))
        + (column, split, column, column, split, row)
        + (P(), P(), P())
        + (column, split, row)
        + (P(), P(), P())
    )
    return jax.shard_map(local, mesh=mesh, in_specs=placed, out_specs=given, check_vma=False)
```

```python
import functools
import math

import jax
import jax.numpy as jnp
from jax import lax
from jax.experimental import pallas as pl
from jax.experimental.pallas import tpu as pltpu
from jax.sharding import PartitionSpec as P

HD = 64
EPS_NORM = 1e-06
SOFTMAX_WARMTH = 0.01
NEG_FILL = -1e30
HIGHEST = lax.Precision.HIGHEST
F32 = jnp.float32
BF16 = jnp.bfloat16
QB = 256
KB = 256

CORE_SWAP = [(i, i ^ 1) for i in range(4)]
FAR_SWAP = [(i, i ^ 2) for i in range(4)]
NEAR_SWAP = [(i, i ^ 1) for i in range(32)]
PLANES = [[i * 2 + x for i in range(16)] for x in range(2)]
Z_RINGS = [[i + 8 * z for z in range(4)] for i in range(8)]

SMEM = pl.BlockSpec(memory_space=pltpu.SMEM)
VMEM = pl.BlockSpec(memory_space=pltpu.VMEM)
HBM = pl.BlockSpec(memory_space=pltpu.HBM)


def nn(left, right):
    return lax.dot_general(left, right, (((1,), (0,)), ((), ())), preferred_element_type=F32)


def nt(left, right):
    return lax.dot_general(left, right, (((1,), (1,)), ((), ())), preferred_element_type=F32)


def tn(left, right):
    return lax.dot_general(left, right, (((0,), (0,)), ((), ())), preferred_element_type=F32)


def place_of_block(block, core, rows):
    return ((block % 2) * 2 + block // 2) * QB + core * (rows // 2) & (rows - 1)


def spot_of_keys(j, core, rows):
    place = (j * KB + core * (rows // 2)) & (rows - 1)
    block = place // QB
    return pl.multiple_of(((block % 2) * 2 + block // 2) * QB + place % QB, KB)


def segment_bounds(lengths_ref):
    bounds, total = [], jnp.int32(0)
    for s in range(lengths_ref.shape[0]):
        start = total
        total = total + lengths_ref[s]
        bounds.append((start, total))
    return bounds


def block_span(bounds, first, rows):
    place = first + lax.broadcasted_iota(jnp.int32, (1, QB), 1)
    low, high = first, first + KB
    begin = jnp.full((1, QB), bounds[-1][1], jnp.int32)
    end = jnp.full((1, QB), rows, jnp.int32)
    for start, stop in bounds:
        inside = (place >= start) & (place < stop)
        begin = jnp.where(inside, start, begin)
        end = jnp.where(inside, stop, end)
        touches = (stop > first) & (start < first + QB) & (stop > start)
        low = jnp.where(touches, jnp.minimum(low, start), low)
        high = jnp.where(touches, jnp.maximum(high, stop), high)
    return low // KB, (high + KB - 1) // KB, begin, end


def head_copies(values, heads):
    lane = lax.broadcasted_iota(jnp.int32, values.shape, 1) // HD
    blank = jnp.zeros_like(values)
    return jnp.concatenate([jnp.where(lane == h, values, blank) for h in range(heads)], axis=0)


def span_mask(begin, end, block, heads):
    place = block * KB + lax.broadcasted_iota(jnp.int32, (KB, QB), 0)
    keep = (place >= begin) & (place < end)
    return jnp.concatenate([keep] * heads, axis=1)


def attend(heads, blocks, core, bounds, q_ref, k_ref, vt_ref, mixed_ref, lse_ref, acc_ref):
    rows = k_ref.shape[0]
    for i, block in enumerate(blocks):
        low, high, begin, end = block_span(bounds, place_of_block(block, core, rows), rows)
        stack = head_copies(q_ref[block * QB : (block + 1) * QB, :], heads)
        acc_ref[...] = jnp.zeros(acc_ref.shape, F32)

        def step(j, carry, stack=stack, begin=begin, end=end):
            top, total = carry
            spot = spot_of_keys(j, core, rows)
            scores = nt(k_ref[pl.ds(spot, KB), :], stack)
            scores = jnp.where(span_mask(begin, end, j, heads), scores, NEG_FILL)
            peak = jnp.maximum(top, jnp.max(scores, axis=0, keepdims=True))
            fade = jnp.exp(top - peak)
            probs = jnp.exp(scores - peak)
            total = total * fade + jnp.sum(probs, axis=0, keepdims=True)
            probs = probs.astype(BF16)
            for h in range(heads):
                part = slice(h * QB, (h + 1) * QB)
                span = slice(h * HD, (h + 1) * HD)
                acc_ref[span, :] = acc_ref[span, :] * fade[:, part] + nn(
                    vt_ref[span, pl.ds(spot, KB)], probs[:, part]
                )
            return peak, total

        top = jnp.full((1, heads * QB), NEG_FILL, F32)
        top, total = lax.fori_loop(
            low, high, step, (top, jnp.zeros((1, heads * QB), F32)), unroll=False
        )
        scale = 1.0 / total
        mixed = jnp.concatenate(
            [
                acc_ref[h * HD : (h + 1) * HD, :] * scale[:, h * QB : (h + 1) * QB]
                for h in range(heads)
            ],
            axis=0,
        )
        mixed_ref[i * QB : (i + 1) * QB, :] = mixed.T.astype(BF16)
        lse_ref[i, :, :] = jnp.broadcast_to(top + jnp.log(total), (8, heads * QB))


def fetch(sources, targets, semaphores, order=()):
    copies = [
        pltpu.make_async_copy(source, target, semaphores.at[i])
        for i, (source, target) in enumerate(zip(sources, targets))
    ]
    for i in [*order, *(i for i in range(len(copies)) if i not in order)]:
        copies[i].start()
    return copies


def project(mixed_ref, weights_ref, results, outputs, semaphores):
    results[1][...] = nn(mixed_ref[QB:, :], weights_ref[...]).astype(BF16)
    copies = send_out(results, outputs, semaphores, (1,))
    results[0][...] = nn(mixed_ref[:QB, :], weights_ref[...])
    return copies + send_out(results, outputs, semaphores, (0,))


def attend_first(heads, blocks, lengths_ref, core_ref, *refs):
    sources, outputs, refs = refs[:13], refs[13:25], refs[25:]
    results, targets, refs = refs[:12], refs[12:24], refs[24:]
    acc_ref, semaphores, out_semaphores = refs
    x_ref, q_ref, k_ref, v_ref, kt_ref, vt_ref, mixed_ref, lse_ref = results[:8]
    wqt_ref, wkt_ref, wvt_ref, bq_ref, bv_ref, wo_ref = targets[:6]
    rows = x_ref.shape[0]
    core = core_ref[0]
    copies = fetch(sources[1:], targets, semaphores)
    row_copies = []
    for block in range(rows // QB):
        first = pl.multiple_of(place_of_block(block, core, rows), QB)
        row_copies.append(
            pltpu.make_async_copy(
                sources[0].at[pl.ds(first, QB), :],
                x_ref.at[pl.ds(block * QB, QB), :],
                semaphores.at[12 + block],
            )
        )
        row_copies[-1].start()
    for copy in copies:
        copy.wait()
    query_bias, value_bias = row_of(bq_ref), row_of(bv_ref)
    for block in range(rows // QB):
        row_copies[block].wait()
        part = slice(block * QB, (block + 1) * QB)
        x = x_ref[part, :]
        q = (nt(x, wqt_ref[...]) + query_bias).astype(BF16)
        q_ref[part, :] = q * BF16(0.125)
        k_ref[part, :] = nt(x, wkt_ref[...]).astype(BF16)
        kt_ref[:, part] = nt(wkt_ref[...], x).astype(BF16)
        v = nt(x, wvt_ref[...]) + value_bias
        v_ref[part, :] = v.astype(BF16)
        vt_ref[:, part] = v.T.astype(BF16)
    outgoing = send_out(results, outputs, out_semaphores, range(6))
    bounds = segment_bounds(lengths_ref)
    place = core * (2 * QB) + lax.broadcasted_iota(jnp.int32, (1, QB), 1)
    for i in range(2):
        member = [
            jnp.where((place + i * QB >= start) & (place + i * QB < stop), 1.0, 0.0)
            for start, stop in bounds
        ]
        results[10][i] = jnp.concatenate(member, axis=0)
    lines = [row_of(ref) for ref in targets[6:]]
    results[11][...] = jnp.concatenate(lines + [jnp.zeros((2, lines[0].shape[1]), F32)], axis=0)
    outgoing += send_out(results, outputs, out_semaphores, (10, 11))
    attend(heads, blocks, core, bounds, q_ref, k_ref, vt_ref, mixed_ref, lse_ref, acc_ref)
    outgoing += project(mixed_ref, wo_ref, results[8:], outputs[8:], out_semaphores.at[8:10])
    outgoing += send_out(results, outputs, out_semaphores, (6, 7))
    for copy in outgoing:
        copy.wait()


def attend_more(heads, blocks, lengths_ref, core_ref, *refs):
    sources, outputs, refs = refs[:4], refs[4:8], refs[8:]
    targets, results, refs = refs[:4], refs[4:8], refs[8:]
    acc_ref, semaphores, out_semaphores = refs
    q_ref, k_ref, vt_ref, wo_ref = targets
    mixed_ref, lse_ref = results[:2]
    for copy in fetch(sources, targets, semaphores):
        copy.wait()
    bounds = segment_bounds(lengths_ref)
    attend(heads, blocks, core_ref[0], bounds, q_ref, k_ref, vt_ref, mixed_ref, lse_ref, acc_ref)
    outgoing = project(mixed_ref, wo_ref, results[2:], outputs[2:], out_semaphores.at[2:])
    outgoing += send_out(results, outputs, out_semaphores, (0, 1))
    for copy in outgoing:
        copy.wait()


def attend_back(heads, inputs, lengths_ref, core_ref, *refs):
    sources, refs = refs[:inputs], refs[inputs:]
    outputs, refs = refs[:2], refs[2:]
    joint_ref, pack_ref = refs[:2]
    dk_ref, dv_ref, dqt_ref, wo_acc_ref, semaphores, out_semaphores = refs[2:8]
    targets = refs[8:]
    copies = fetch(sources, targets, semaphores, (8, 7, 9, 10, 0, 2, 6, 4, 1, 3, 5))
    grads = targets[0:2]
    mixed = targets[2:4]
    lses = targets[4:6]
    wo_ref, q_ref, k_ref, v_ref, kt_ref = targets[6:11]
    own_sums, other_sums, inner_ref, x_ref = targets[11:]
    rows, width = q_ref.shape
    core = core_ref[0]
    bounds = segment_bounds(lengths_ref)
    dk_ref[...] = jnp.zeros(dk_ref.shape, F32)
    dv_ref[...] = jnp.zeros(dv_ref.shape, F32)
    joint_ref[...] = jnp.zeros(joint_ref.shape, BF16)
    lane = lax.broadcasted_iota(jnp.int32, (8, width), 1) // HD
    which = (lane == lax.broadcasted_iota(jnp.int32, (8, width), 0)).astype(F32).astype(BF16)
    for i in (0, 2, 4, 6, 7, 8, 9, 10):
        copies[i].wait()
    for block in range(rows // QB):
        if block == 1:
            copies[1].wait()
        if block == 2:
            copies[3].wait()
            copies[5].wait()
        low, high, begin, end = block_span(bounds, place_of_block(block, core, rows), rows)
        part = slice(block * QB, (block + 1) * QB)
        own = slice(block % 2 * QB, block % 2 * QB + QB)
        grad_attn = grads[block % 2][block // 2 * QB : block // 2 * QB + QB, :]
        mixed_here = mixed[block // 2][own, :]
        outer = tn(mixed_here, grad_attn)
        wo_acc_ref[...] = outer if block == 0 else wo_acc_ref[...] + outer
        grad_mixed = nt(grad_attn, wo_ref[...]).astype(BF16)
        product = grad_mixed.astype(F32) * mixed_here.astype(F32)
        sums = sum(nt(which, part) for part in in_three(product)[:2])
        delta = jnp.concatenate([sums[h : h + 1, :] for h in range(heads)], axis=1)
        lse = lses[block // 2][block % 2, 0:1, :]
        q_stack = head_copies(q_ref[part, :], heads)
        g_stack = head_copies(grad_mixed, heads)
        dqt_ref[...] = jnp.zeros(dqt_ref.shape, F32)

        def step(
            j, carry, delta=delta, lse=lse, q_stack=q_stack, g_stack=g_stack, begin=begin, end=end
        ):
            here = pl.ds(spot_of_keys(j, core, rows), KB)
            scores = nt(k_ref[here, :], q_stack)
            scores = jnp.where(span_mask(begin, end, j, heads), scores, NEG_FILL)
            probs = jnp.exp(scores - lse)
            grad = (probs * (nt(v_ref[here, :], g_stack) - delta)).astype(BF16)
            dv_ref[here, :] += nn(probs.astype(BF16), g_stack)
            dk_ref[here, :] += nn(grad, q_stack)
            for h in range(heads):
                span = slice(h * HD, (h + 1) * HD)
                dqt_ref[span, :] += nn(kt_ref[span, here], grad[:, h * QB : (h + 1) * QB])
            return carry

        lax.fori_loop(low, high, step, 0, unroll=False)
        joint_ref[part, :width] = (dqt_ref[...].T * 0.125).astype(BF16)
    spans = [slice(256 * k, 256 * k + width) for k in range(3)]
    joint_ref[:, spans[1]] = dk_ref[...].astype(BF16)
    joint_ref[:, spans[2]] = dv_ref[...].astype(BF16)
    for copy in copies[11:]:
        copy.wait()
    outgoing = send_out(refs, outputs, out_semaphores, (0,))
    sums = [column_sum(joint_ref[:, spans[k]].astype(F32)) for k in (0, 2)]
    blank = jnp.zeros((1, 256 - width), F32)
    tail = jnp.concatenate([sums[0], blank, sums[1], blank, jnp.zeros((1, 256), F32)], axis=1)
    inner = row_of(inner_ref)
    paired = own_sums[0:6, :] + other_sums[0:6, :]
    small = [paired, inner, tail, jnp.zeros((8, tail.shape[1]), F32)]
    small = jnp.concatenate(small, axis=0).astype(BF16)
    piece = pack_ref.shape[1] - 16
    per = width // piece
    for m in range(4):
        total = wo_acc_ref[...] if m == 0 else tn(joint_ref[:, spans[m - 1]], x_ref[...])
        for t in range(per):
            cut = total[t * piece : (t + 1) * piece, :].astype(BF16)
            pack_ref[m * per + t, 0:piece, :] = cut
            pack_ref[m * per + t, piece:, :] = small if m + t == 0 else jnp.zeros_like(small)
        here = pl.ds(m * per, per)
        copy = pltpu.make_async_copy(
            pack_ref.at[here], outputs[1].at[here], out_semaphores.at[1 + m]
        )
        copy.start()
        outgoing.append(copy)
    for copy in outgoing:
        copy.wait()


def shaped(shape, dtype):
    return jax.ShapeDtypeStruct(shape, dtype)


PARAMS = pltpu.CompilerParams(vmem_limit_bytes=60 << 20)
SMALL = pltpu.CompilerParams(vmem_limit_bytes=60 << 20)
SHARED = pltpu.CompilerParams(vmem_limit_bytes=24 << 20)
COST = pl.CostEstimate(flops=1024, bytes_accessed=1024, transcendentals=0)


def buffers(arrays):
    return [pltpu.VMEM(array.shape, array.dtype) for array in arrays]


def attend_shapes(count, heads, width):
    rows = count * QB
    return (
        shaped((rows, heads * HD), BF16),
        shaped((count, 8, heads * QB), F32),
        shaped((rows // 2, width), F32),
        shaped((rows // 2, width), BF16),
    )


def run_first(lengths, core, tokens, weights, blocks):
    rows, width = tokens.shape
    local_width = weights[0].shape[0]
    heads = local_width // HD
    outs = (
        (shaped(tokens.shape, BF16),)
        + (shaped((rows, local_width), BF16),) * 3
        + (shaped((local_width, rows), BF16),) * 2
        + attend_shapes(len(blocks), heads, width)
        + (shaped((2, lengths.shape[0], QB), F32), shaped((8, width), F32))
    )
    return pl.pallas_call(
        functools.partial(attend_first, heads, blocks),
        out_shape=outs,
        in_specs=[SMEM] * 2 + [HBM] * 13,
        out_specs=(HBM,) * 12,
        scratch_shapes=buffers(outs)
        + buffers(weights)
        + [pltpu.VMEM((local_width, QB), F32)]
        + [pltpu.SemaphoreType.DMA((12 + rows // QB,)), pltpu.SemaphoreType.DMA((12,))],
        compiler_params=PARAMS,
        name="attend_first",
        cost_estimate=COST,
    )(lengths, core, tokens, *weights)


def run_more(lengths, core, arrays, blocks):
    rows, local_width = arrays[0].shape
    heads = local_width // HD
    outs = attend_shapes(len(blocks), heads, arrays[3].shape[1])
    return pl.pallas_call(
        functools.partial(attend_more, heads, blocks),
        out_shape=outs,
        in_specs=[SMEM] * 2 + [HBM] * 4,
        out_specs=(HBM,) * 4,
        scratch_shapes=buffers(arrays)
        + buffers(outs)
        + [pltpu.VMEM((local_width, QB), F32)]
        + [pltpu.SemaphoreType.DMA((4,)), pltpu.SemaphoreType.DMA((4,))],
        compiler_params=PARAMS,
        name="attend_more",
        cost_estimate=COST,
    )(lengths, core, *arrays)


def run_back(lengths, core, arrays):
    wo, q, x = arrays[6], arrays[7], arrays[-1]
    rows, width = q.shape
    heads = width // HD
    piece = 4 * width // 16
    outs = (shaped((rows, 3 * 256), BF16), shaped((16, piece + 16, x.shape[1]), BF16))
    return pl.pallas_call(
        functools.partial(attend_back, heads, len(arrays)),
        out_shape=outs,
        in_specs=[SMEM] * 2 + [HBM] * len(arrays),
        out_specs=(HBM,) * 2,
        scratch_shapes=buffers(outs)
        + [pltpu.VMEM((rows, width), F32)] * 2
        + [pltpu.VMEM((width, QB), F32), pltpu.VMEM(wo.shape, F32)]
        + [pltpu.SemaphoreType.DMA((len(arrays),)), pltpu.SemaphoreType.DMA((5,))]
        + buffers(arrays),
        compiler_params=PARAMS,
        name="attend_back",
        cost_estimate=COST,
    )(lengths, core, *arrays)


def mark_kernel(source_ref, target_ref):
    del source_ref, target_ref


def mark(values):
    return pl.pallas_call(
        mark_kernel,
        out_shape=shaped(values.shape, values.dtype),
        in_specs=[HBM],
        out_specs=HBM,
        compiler_params=pltpu.CompilerParams(vmem_limit_bytes=1 << 20),
        name="mark",
        cost_estimate=pl.CostEstimate(flops=1 << 36, bytes_accessed=1 << 10, transcendentals=0),
    )(values)


def finish_kernel(source_ref, target_ref):
    del source_ref
    target_ref[...] = jnp.zeros(target_ref.shape, F32)


def finish(values):
    return pl.pallas_call(
        finish_kernel,
        out_shape=shaped(values.shape, values.dtype),
        in_specs=[HBM],
        out_specs=VMEM,
        compiler_params=pltpu.CompilerParams(vmem_limit_bytes=1 << 20),
        name="finish",
        cost_estimate=COST,
    )(values)


def row_of(ref):
    return ref[...].astype(F32).reshape(1, -1)


def in_three(values):
    high = values.astype(BF16)
    rest = values - high.astype(F32)
    middle = rest.astype(BF16)
    return high, middle, (rest - middle.astype(F32)).astype(BF16)


def norm_step(grad, normed, rscale, gain):
    scaled = grad * gain
    first_mean = jnp.mean(scaled, axis=1, keepdims=True)
    cross_mean = jnp.mean(scaled * normed, axis=1, keepdims=True)
    return rscale * (scaled - first_mean - normed * cross_mean)


def column_of(ref):
    row = ref[...].reshape(1, -1)
    return jnp.broadcast_to(row, (128, row.shape[1])).T[:, 0:1]


def column_sum(values):
    return jnp.sum(values, axis=0, keepdims=True)


def send_out(results, outputs, semaphores, which):
    copies = [
        pltpu.make_async_copy(results[k], outputs[k], semaphores.at[k]) for k in which
    ]
    for copy in copies:
        copy.start()
    return copies


def send_rows(results, outputs, semaphores, i):
    here = pl.ds(i * QB, QB)
    copies = [
        pltpu.make_async_copy(
            results[k].at[here, :], outputs[k].at[here, :], semaphores.at[4 + 2 * i + k]
        )
        for k in (1, 0)
    ]
    for copy in copies:
        copy.start()
    return copies


def loss_back(lengths_ref, place_ref, *refs):
    sources, outputs, refs = refs[:9], refs[9:13], refs[13:]
    targets, results = refs[:9], refs[9:13]
    coef_ref, turned_ref, semaphores, out_semaphores = refs[13:]
    copies = fetch(sources, targets, semaphores)
    piece_ref, swapped_ref, pooled_ref, match_ref, gain_ref = targets[:5]
    core, index = place_ref[0], place_ref[1]
    bounds = segment_bounds(lengths_ref)
    for copy in copies[:5]:
        copy.wait()
    first = core == 0
    queries = jnp.where(first, piece_ref[...], swapped_ref[...])
    passages = jnp.where(first, swapped_ref[...], piece_ref[...])
    count = queries.shape[0]
    own = pooled_ref.shape[0] // 2
    similarity = nt(queries, passages) / SOFTMAX_WARMTH
    match = match_ref[...].reshape(1, -1)
    match = match == lax.broadcasted_iota(jnp.int32, (count, count), 0)
    top = jnp.max(similarity, axis=1, keepdims=True)
    lse = top + jnp.log(jnp.sum(jnp.exp(similarity - top), axis=1, keepdims=True))
    positive = jnp.sum(jnp.where(match, similarity, 0.0), axis=1, keepdims=True)
    loss = jnp.sum(lse - positive, axis=0, keepdims=True) / count
    results[3][...] = jnp.broadcast_to(loss, results[3].shape)
    coef = (jnp.exp(similarity - lse) - match.astype(F32)) * (1.0 / (count * SOFTMAX_WARMTH))
    coef_ref[...] = coef
    turned_ref[...] = coef.T
    here = pl.ds(pl.multiple_of(index * own, own), own)
    grad_query = sum(nn(part, passages) for part in in_three(coef_ref[here, :])[:2])
    grad_passage = sum(nn(part, queries) for part in in_three(turned_ref[here, :])[:2])
    grad_unit = jnp.concatenate([grad_query, grad_passage], axis=0)
    pooled = pooled_ref[...]
    rscale = lax.rsqrt(jnp.sum(pooled * pooled, axis=1, keepdims=True) + EPS_NORM)
    inner = jnp.sum(pooled * grad_unit, axis=1, keepdims=True)
    grad_pooled = rscale * grad_unit - rscale * rscale * rscale * inner * pooled
    seqs = 2 * own
    grad_pooled = jnp.concatenate(
        [grad_pooled, jnp.zeros((128 - seqs, grad_pooled.shape[1]), F32)], axis=0
    )
    parts = in_three(grad_pooled)[:2]
    lane = lax.broadcasted_iota(jnp.int32, (1, 128), 1)
    begin = end = jnp.zeros((1, 128), jnp.int32)
    for seq, (start, stop) in enumerate(bounds):
        begin = jnp.where(lane == seq, start, begin)
        end = jnp.where(lane == seq, stop, end)
    gain = row_of(gain_ref)
    sums = [0.0, 0.0, 0.0]
    outgoing = []
    for i in range(2):
        copies[5 + 2 * i].wait()
        copies[6 + 2 * i].wait()
        normed = targets[5 + 2 * i][...]
        place = core * (2 * QB) + i * QB + lax.broadcasted_iota(jnp.int32, (QB, 128), 0)
        member = jnp.where((place >= begin) & (place < end), 1.0, 0.0).astype(BF16)
        grad = sum(nn(member, part) for part in parts)
        second = norm_step(grad, normed, column_of(targets[6 + 2 * i]), gain)
        rounded = second.astype(BF16)
        here = pl.ds(i * QB, QB)
        results[0][here, :] = second
        results[1][here, :] = rounded
        outgoing += send_rows(results, outputs, out_semaphores, i)
        for k, values in enumerate((rounded.astype(F32), grad * normed, grad)):
            sums[k] = sums[k] + column_sum(values)
    results[2][...] = jnp.concatenate(sums + [jnp.zeros((5, sums[0].shape[1]), F32)], axis=0)
    outgoing += send_out(results, outputs, out_semaphores, (2, 3))
    for copy in outgoing:
        copy.wait()


def norm_back(*refs):
    sources, outputs, refs = refs[:9], refs[9:12], refs[12:]
    targets, results = refs[:9], refs[9:12]
    semaphores, out_semaphores = refs[12:]
    copies = fetch(sources, targets, semaphores)
    for copy in copies[:5]:
        copy.wait()
    gain = row_of(targets[0])
    second, pair_here, far = targets[2:5]
    sums = [0.0, 0.0, 0.0]
    outgoing = []
    for i in range(2):
        copies[5 + 2 * i].wait()
        copies[6 + 2 * i].wait()
        here = pl.ds(i * QB, QB)
        exchanged = pair_here[here, :].astype(F32) + far[here, :].astype(F32)
        grad = second[here, :] + exchanged
        normed = targets[5 + 2 * i][...]
        first = norm_step(grad, normed, column_of(targets[6 + 2 * i]), gain)
        rounded = first.astype(BF16)
        results[0][here, :] = first
        results[1][here, :] = rounded
        outgoing += send_rows(results, outputs, out_semaphores, i)
        for k, values in enumerate((rounded.astype(F32), grad * normed, grad)):
            sums[k] = sums[k] + column_sum(values)
    blank = jnp.zeros((2, sums[0].shape[1]), F32)
    results[2][...] = jnp.concatenate(sums + [targets[1][0:3, :], blank], axis=0)
    outgoing += send_out(results, outputs, out_semaphores, (2,))
    for copy in outgoing:
        copy.wait()


STEPS = (0, 2, 1, 3)


def join(copies_of_each, place_ref, *refs):
    sources, output, semaphores = refs[:4], refs[4], refs[5]
    copies = []
    for k in range(4):
        spot = (place_ref[0] + 4 - STEPS[k]) % 4
        for r in range(copies_of_each):
            goal = output.at[spot] if copies_of_each == 1 else output.at[r, spot]
            semaphore = semaphores.at[k * copies_of_each + r]
            copies.append(pltpu.make_async_copy(sources[k], goal, semaphore))
            copies[-1].start()
    for copy in copies:
        copy.wait()


def place_block(piece, part, block_ref, spot, outputs, buffers_, semaphores, first):
    inner, cuts = buffers_
    inner[...] = block_ref[:, :piece, :].astype(F32)
    cuts[...] = block_ref[:, piece : 2 * piece - part, :].astype(F32)
    copies = [pltpu.make_async_copy(inner, outputs[0].at[:, spot], semaphores.at[first])]
    for m in range(4):
        goal = outputs[1 + m].at[spot, pl.ds(part, piece - part), :]
        copies.append(pltpu.make_async_copy(cuts.at[m], goal, semaphores.at[first + 1 + m]))
    for copy in copies:
        copy.start()
    return copies


def place_vectors(piece, part, block_ref, spot, outputs, vectors, semaphores, first):
    @pl.when(spot == 0)
    def _():
        small = block_ref[0, 2 * piece - part :, :].astype(F32)
        for k in range(7):
            vectors[k][...] = small[k : k + 1, :].reshape(-1)
        count = vectors[7].shape[0]
        for k in range(2):
            vectors[7 + k][...] = small[7:8, 256 * k : 256 * k + count].reshape(-1)
        copies = [
            pltpu.make_async_copy(vectors[k], outputs[5 + k], semaphores.at[first + k])
            for k in range(9)
        ]
        for copy in copies:
            copy.start()
        for copy in copies:
            copy.wait()


def spread_some(piece, part, count, place_ref, *refs):
    sources, outputs, refs = refs[:count], refs[count : count + 14], refs[count + 14 :]
    blocks, refs = refs[:count], refs[count:]
    buffers_, vectors, refs = refs[: 2 * count], refs[2 * count : 2 * count + 9], refs[-2:]
    arrivals = fetch(sources, blocks, refs[0])
    outgoing, spots = [], []
    for k in range(count):
        arrivals[k].wait()
        spots.append((place_ref[1] + 4 - STEPS[k]) % 4)
        outgoing += place_block(
            piece, part, blocks[k], spots[k], outputs, buffers_[2 * k : 2 * k + 2], refs[1], 5 * k
        )
    for k in range(count):
        place_vectors(piece, part, blocks[k], spots[k], outputs, vectors, refs[1], 5 * count)
    for copy in outgoing:
        copy.wait()


def spread_rest(piece, part, place_ref, *refs):
    sources, outputs, refs = refs[:3], refs[17:32], refs[32:]
    blocks, by_z, refs = refs[:2], refs[2], refs[3:]
    buffers_, outer, heads, vectors, refs = refs[:4], refs[4], refs[5], refs[6:15], refs[15:]
    semaphores, out_semaphores = refs
    arrivals = fetch(sources, (*blocks, by_z), semaphores)
    outgoing, spots = [], []
    for k in range(2):
        spots.append((place_ref[1] + 4 - STEPS[2 + k]) % 4)
        arrivals[k].wait()
        outgoing += place_block(
            piece,
            part,
            blocks[k],
            spots[k],
            outputs,
            buffers_[2 * k : 2 * k + 2],
            out_semaphores,
            5 * k,
        )
    arrivals[2].wait()
    outer[...] = by_z[:, :, :piece, :].astype(F32)
    copies = [pltpu.make_async_copy(outer, outputs[14], out_semaphores.at[10])]
    copies[0].start()
    heads[...] = by_z[:, :, piece:, :].astype(F32)
    for m in range(4):
        goal = outputs[1 + m].at[:, pl.ds(0, part), :]
        copies.append(pltpu.make_async_copy(heads.at[m], goal, out_semaphores.at[11 + m]))
        copies[-1].start()
    for k in range(2):
        place_vectors(piece, part, blocks[k], spots[k], outputs, vectors, out_semaphores, 15)
    for copy in outgoing + copies:
        copy.wait()


def run_loss(lengths, place, arrays):
    rows, width = arrays[5].shape
    count = arrays[0].shape[0]
    outs = (
        shaped((2 * rows, width), F32),
        shaped((2 * rows, width), BF16),
        shaped((8, width), F32),
        shaped((8, 128), F32),
    )
    return pl.pallas_call(
        loss_back,
        out_shape=outs,
        in_specs=[SMEM] * 2 + [HBM] * 9,
        out_specs=(HBM,) * 4,
        scratch_shapes=buffers(arrays)
        + buffers(outs)
        + [pltpu.VMEM((count, count), F32)] * 2
        + [pltpu.SemaphoreType.DMA((9,)), pltpu.SemaphoreType.DMA((8,))],
        compiler_params=SHARED,
        name="loss_back",
        cost_estimate=COST,
    )(lengths, place, *arrays)


def run_norm(arrays):
    rows, width = arrays[2].shape
    outs = (shaped((rows, width), F32), shaped((rows, width), BF16), shaped((8, width), F32))
    return pl.pallas_call(
        norm_back,
        out_shape=outs,
        in_specs=[HBM] * 9,
        out_specs=(HBM,) * 3,
        scratch_shapes=buffers(arrays)
        + buffers(outs)
        + [pltpu.SemaphoreType.DMA((9,)), pltpu.SemaphoreType.DMA((8,))],
        compiler_params=SMALL,
        name="norm_back",
        cost_estimate=COST,
    )(*arrays)


def run_join(place, pieces, copies_of_each):
    lead = (4,) if copies_of_each == 1 else (copies_of_each, 4)
    return pl.pallas_call(
        functools.partial(join, copies_of_each),
        out_shape=shaped(lead + pieces[0].shape, BF16),
        in_specs=[SMEM] + [HBM] * 4,
        out_specs=HBM,
        scratch_shapes=[pltpu.SemaphoreType.DMA((4 * copies_of_each,))],
        compiler_params=pltpu.CompilerParams(vmem_limit_bytes=1 << 20),
        name="join",
        cost_estimate=COST,
    )(place, *pieces)


def settle(core_ref, *refs):
    sources, output, semaphores = refs[:4], refs[4], refs[5]
    copies = []
    for k in range(4):
        first = (k // 2 + core_ref[0]) % 2 * (2 * QB) + k % 2 * QB
        spot = pl.ds(pl.multiple_of(first, QB), QB)
        copies.append(pltpu.make_async_copy(sources[k], output.at[spot, :], semaphores.at[k]))
        copies[-1].start()
    for copy in copies:
        copy.wait()


def weave(*refs):
    sources, outputs, semaphores = refs[:6], refs[6:9], refs[9]
    copies = []
    for k in range(3):
        for block in range(4):
            copies.append(
                pltpu.make_async_copy(
                    sources[2 * k + block % 2].at[pl.ds(block // 2 * QB, QB), :],
                    outputs[k].at[pl.ds(block * QB, QB), :],
                    semaphores.at[4 * k + block],
                )
            )
            copies[-1].start()
    for copy in copies:
        copy.wait()


def run_weave(arrays):
    rows, width = arrays[0].shape
    return pl.pallas_call(
        weave,
        out_shape=[shaped((2 * rows, width), BF16)] * 3,
        in_specs=[HBM] * 6,
        out_specs=[HBM] * 3,
        scratch_shapes=[pltpu.SemaphoreType.DMA((12,))],
        compiler_params=pltpu.CompilerParams(vmem_limit_bytes=1 << 20),
        name="weave",
        cost_estimate=COST,
    )(*arrays)


def run_settle(core, parts):
    rows, width = parts[0].shape
    return pl.pallas_call(
        settle,
        out_shape=shaped((4 * rows, width), BF16),
        in_specs=[SMEM] + [HBM] * 4,
        out_specs=HBM,
        scratch_shapes=[pltpu.SemaphoreType.DMA((4,))],
        compiler_params=pltpu.CompilerParams(vmem_limit_bytes=1 << 20),
        name="settle",
        cost_estimate=COST,
    )(core, *parts)


def spread_shapes(piece, width):
    shapes = [(4, 4, piece, width)] + [(4, piece, width)] * 4
    return shapes + [(width,)] * 7 + [(4 * piece,)] * 2


def run_spread_some(places, blocks, piece, part):
    width = blocks[0].shape[2]
    shapes = spread_shapes(piece, width)
    count = len(blocks)
    pair_of = [pltpu.VMEM((4, piece, width), F32), pltpu.VMEM((4, piece - part, width), F32)]
    return pl.pallas_call(
        functools.partial(spread_some, piece, part, count),
        out_shape=[shaped(shape, F32) for shape in shapes],
        in_specs=[SMEM] + [HBM] * count,
        out_specs=[HBM] * 14,
        scratch_shapes=buffers(blocks)
        + pair_of * count
        + [pltpu.VMEM(shape, F32) for shape in shapes[5:]]
        + [pltpu.SemaphoreType.DMA((count,)), pltpu.SemaphoreType.DMA((5 * count + 9,))],
        compiler_params=SHARED,
        name="spread_some",
        cost_estimate=COST,
    )(places, *blocks)


def run_spread_rest(places, blocks, gathered, so_far, piece, part):
    width = gathered.shape[3]
    shapes = spread_shapes(piece, width)
    outer = (4, 4, piece, width)
    pair_of = [pltpu.VMEM((4, piece, width), F32), pltpu.VMEM((4, piece - part, width), F32)]
    return pl.pallas_call(
        functools.partial(spread_rest, piece, part),
        out_shape=[shaped(shape, F32) for shape in shapes + [outer]],
        in_specs=[SMEM] + [HBM] * 17,
        out_specs=[HBM] * 15,
        input_output_aliases={4 + k: k for k in range(14)},
        scratch_shapes=buffers((*blocks, gathered))
        + pair_of * 2
        + [pltpu.VMEM(outer, F32), pltpu.VMEM((4, 4, part, width), F32)]
        + [pltpu.VMEM(shape, F32) for shape in shapes[5:]]
        + [pltpu.SemaphoreType.DMA((3,)), pltpu.SemaphoreType.DMA((24,))],
        compiler_params=SHARED,
        name="spread_rest",
        cost_estimate=COST,
    )(places, *blocks, gathered, *so_far)


def trade(values):
    return lax.all_to_all(
        values, "dp", split_axis=0, concat_axis=0, axis_index_groups=PLANES, tiled=True
    )


def share(values):
    spread_out = jnp.broadcast_to(values[None], (32,) + values.shape)
    return lax.all_to_all(spread_out, "dp", split_axis=0, concat_axis=0, tiled=True)


def trade_z(values):
    return lax.all_to_all(
        values, "dp", split_axis=0, concat_axis=0, axis_index_groups=Z_RINGS, tiled=True
    )


def ring_shift(axis, step):
    pairs = []
    for i in range(32):
        z, y, x = i // 8, (i // 2) % 4, i % 2
        z, y = ((z + step) % 4, y) if axis == "z" else (z, (y + step) % 4)
        pairs.append((i, (z * 4 + y) * 2 + x))
    return pairs


def ring_pieces(values, axis):
    return [lax.ppermute(values, "dp", ring_shift(axis, step)) for step in STEPS[1:]]


def tie(values, others):
    return lax.optimization_barrier((values, others))


class Marker:
    def __init__(self):
        self.state = jnp.zeros((8, 128), F32)

    def fence(self, ready, later):
        ready, state = tie(ready, self.state)
        later, self.state = tie(later, mark(state))
        return ready, later

    def moved(self, values, axis, pairs):
        values, state = tie(values, self.state)
        arrived, self.state = tie(lax.ppermute(values, axis, pairs), mark(state))
        return arrived

    def core_swap(self, values):
        return self.moved(values, "mp", CORE_SWAP)

    def near_swap(self, values):
        return self.moved(values, "dp", NEAR_SWAP)

    def both(self, own):
        return jnp.concatenate([own, self.core_swap(own)], axis=0)

    def near_sum(self, total):
        return (total.astype(F32) + self.near_swap(total).astype(F32)).astype(BF16)


def plane_sum(parts):
    return jnp.sum(parts.astype(F32), axis=0).astype(BF16)


def far_swap(values):
    return lax.ppermute(values, "mp", FAR_SWAP)


def norm_forward(values, gain_vec, shift_vec):
    average = jnp.mean(values, axis=-1, keepdims=True)
    centred = values - average
    rscale = lax.rsqrt(jnp.mean(centred * centred, axis=-1, keepdims=True) + EPS_NORM)
    normed = centred * rscale
    return (normed * gain_vec + shift_vec, normed, rscale[:, 0])


def gelu_and_slope(upper):
    below = 0.5 * (1.0 + lax.erf(upper * math.sqrt(0.5)))
    density = jnp.exp(-0.5 * upper * upper) * (1.0 / math.sqrt(2.0 * math.pi))
    return (upper * below).astype(BF16), (below + upper * density).astype(BF16)


def local(
    tokens,
    lengths,
    pair_index,
    query_proj,
    query_bias,
    key_proj,
    value_proj,
    value_bias,
    output_proj,
    output_bias,
    attn_gain,
    attn_shift,
    inner_proj,
    inner_bias,
    outer_proj,
    outer_bias,
    final_gain,
    final_shift,
):
    row_count, width = tokens.shape
    chunk = row_count // 2
    half = chunk // 2
    seq_count = lengths.shape[0]
    pair_count = seq_count // 2
    overall_pair_count = pair_index.shape[0]
    local_width = query_proj.shape[1]
    core = lax.axis_index("mp") % 2
    my_index = lax.axis_index("dp")
    marker = Marker()
    core_arg = jnp.reshape(core, (1,)).astype(jnp.int32)
    vectors = (output_bias, attn_gain, attn_shift, outer_bias, final_gain, final_shift)
    query_t, key_t, value_t = query_proj.T, key_proj.T, value_proj.T
    blank = jnp.zeros((256 - local_width, width), BF16)
    joint_proj = jnp.concatenate([query_t, blank, key_t, blank, value_t, blank], axis=0)

    weights = (query_t, key_t, value_t, query_bias, value_bias, output_proj, *vectors)
    first = run_first(lengths, core_arg, tokens, weights, (0, 1))
    rows, query_b, key_b, value_b, key_tb, value_tb, mixed_a, lse_a = first[:8]
    attn_own_a, attn_other_a, members, vectors = first[8:]

    def own_and_other(values, weights):
        return nn(values[:half], weights), nn(values[half:], weights).astype(BF16)

    def pair(own, arrived):
        return (own + arrived.astype(F32)).astype(BF16)

    def first_norm(index, pair_here, far):
        attn_full = pair_here.astype(F32) + far.astype(F32) + output_bias
        own_tokens = rows[index * chunk : index * chunk + half].astype(F32)
        return norm_forward(own_tokens + attn_full, attn_gain_f, attn_shift_f)

    def feed_forward(own_hidden):
        whole = marker.both(own_hidden)
        act, slope = gelu_and_slope(nn(whole, inner_proj) + inner_bias.astype(F32))
        act, slope = tie(act, slope)
        return whole, act, slope

    def last_norm(hidden, pair_here, far):
        ffn_full = pair_here.astype(F32) + far.astype(F32) + outer_bias
        return norm_forward(hidden + ffn_full, final_gain_f, final_shift_f)

    attn_pair_a = pair(attn_own_a, marker.core_swap(attn_other_a))
    attn_far_a = far_swap(attn_pair_a)
    output_bias, attn_gain_f, attn_shift_f = vectors[0], vectors[1], vectors[2]
    outer_bias, final_gain_f, final_shift_f = vectors[3], vectors[4], vectors[5]
    late_query, late_pair = tie(query_b, attn_pair_a)
    mixed_b, lse_b, attn_own_b, attn_other_b = run_more(
        lengths, core_arg, (late_query, key_b, value_tb, output_proj), (2, 3)
    )
    attn_pair_b = pair(attn_own_b, marker.core_swap(attn_other_b))
    attn_far_b = far_swap(attn_pair_b)
    attn_far_a, attn_pair_b = tie(attn_far_a, attn_pair_b)
    hidden_a, normed_one_a, rscale_one_a = first_norm(0, late_pair, attn_far_a)
    own_hidden_a = hidden_a.astype(BF16)
    hidden_ab, act_a, slope_a = feed_forward(own_hidden_a)
    ffn_own_a, ffn_other_a = own_and_other(act_a, outer_proj)
    ffn_pair_a = pair(ffn_own_a, marker.core_swap(ffn_other_a))
    attn_far_b, ffn_pair_late = tie(attn_far_b, ffn_pair_a)
    ffn_far_a = far_swap(ffn_pair_a)
    hidden_b, normed_one_b, rscale_one_b = first_norm(1, attn_pair_b, attn_far_b)
    own_hidden_b = hidden_b.astype(BF16)
    hidden_bb, act_b, slope_b = feed_forward(own_hidden_b)
    ffn_own_b, ffn_other_b = own_and_other(act_b, outer_proj)
    ffn_pair_b = pair(ffn_own_b, marker.core_swap(ffn_other_b))
    ffn_pair_b, ffn_far_a = marker.fence(ffn_pair_b, ffn_far_a)
    final_a, normed_two_a, rscale_two_a = last_norm(hidden_a, ffn_pair_late, ffn_far_a)
    pooled_a = jnp.dot(members[0], final_a, precision=HIGHEST)
    final_b, normed_two_b, rscale_two_b = last_norm(hidden_b, ffn_pair_b, far_swap(ffn_pair_b))
    pooled_part = pooled_a + jnp.dot(members[1], final_b, precision=HIGHEST)
    lse = (lse_a, lse_b)
    hidden_whole, act, slope = (hidden_ab, hidden_bb), (act_a, act_b), (slope_a, slope_b)
    normed_one, rscale_one = (normed_one_a, normed_one_b), (rscale_one_a, rscale_one_b)
    normed_two, rscale_two = (normed_two_a, normed_two_b), (rscale_two_a, rscale_two_b)
    pooled = pooled_part + marker.core_swap(pooled_part)
    pool_rscale = lax.rsqrt(jnp.sum(pooled * pooled, axis=-1, keepdims=True) + EPS_NORM)
    unit_b = (pooled * pool_rscale).astype(BF16)

    piece = lax.dynamic_slice_in_dim(unit_b, core * pair_count, pair_count, 0)
    piece = share(piece).reshape(overall_pair_count, width)
    place_arg = jnp.stack([core, my_index]).astype(jnp.int32)
    whole = run_weave((*act, *slope, *hidden_whole))
    piece, (whole_act, whole_slope, whole_hidden) = tie(piece, whole)
    grad_second, own_grad, last_sums, loss = run_loss(
        lengths,
        place_arg,
        (
            piece,
            marker.core_swap(piece),
            pooled,
            pair_index,
            final_gain,
            normed_two[0],
            rscale_two[0],
            normed_two[1],
            rscale_two[1],
        ),
    )

    grad_ffn = marker.both(own_grad)
    grad_up = (nt(grad_ffn, outer_proj) * whole_slope.astype(F32)).astype(BF16)
    inner_sum = jnp.sum(grad_up.astype(F32), axis=0)
    other = nt(grad_up[chunk:], inner_proj).astype(BF16)
    whole_act, other = tie(whole_act, other)
    outer_part = tn(whole_act, grad_ffn).astype(BF16)
    arrived, outer_part = tie(lax.ppermute(other, "mp", CORE_SWAP), outer_part)
    hidden_pair = pair(nt(grad_up[:chunk], inner_proj), arrived)
    hidden_far = far_swap(hidden_pair)
    whole_hidden, hidden_pair = tie(whole_hidden, hidden_pair)
    inner_part = tn(whole_hidden, grad_up).astype(BF16)
    ffn_pack = jnp.concatenate(
        [outer_part.reshape(16, -1, width), inner_part.reshape(16, -1, width)], axis=1
    )
    ffn_pack, hidden_far = marker.fence(ffn_pack, hidden_far)
    ffn_parts = trade(ffn_pack)

    grad_first, own_grad, sums = run_norm(
        (
            attn_gain,
            last_sums,
            grad_second,
            hidden_pair,
            hidden_far,
            normed_one[0],
            rscale_one[0],
            normed_one[1],
            rscale_one[1],
        )
    )
    (own_grad, sums), state = tie((own_grad, sums), marker.state)
    arrived = [lax.ppermute(values, "mp", CORE_SWAP) for values in (own_grad, sums)]
    (other_grad, other_sums), marker.state = tie(arrived, mark(state))
    grad_rows, packed = run_back(
        lengths,
        core_arg,
        (
            own_grad,
            other_grad,
            mixed_a,
            mixed_b,
            *lse,
            output_proj,
            query_b,
            key_b,
            value_b,
            key_tb,
            sums,
            other_sums,
            inner_sum,
            rows,
        ),
    )

    packed, (ffn_parts, grad_rows) = marker.fence(packed, (ffn_parts, grad_rows))
    packed_parts = trade(packed)

    def input_part(first):
        span = slice(first, first + half)
        return nn(grad_rows[span], joint_proj)

    token_pair = []
    for i in range(2):
        other = input_part(i * chunk + half).astype(BF16)
        token_pair.append(pair(input_part(i * chunk), marker.core_swap(other)))
    token_pair, ffn_parts = marker.fence(token_pair, ffn_parts)
    token_far = [far_swap(token_pair[i]) for i in range(2)]
    ffn_total = plane_sum(ffn_parts)
    ffn_near = lax.ppermute(ffn_total, "dp", NEAR_SWAP)
    ffn_reduced = (ffn_total.astype(F32) + ffn_near.astype(F32)).astype(BF16)
    ffn_reduced, packed_parts = tie(ffn_reduced, packed_parts)
    packed_reduced = marker.near_sum(plane_sum(packed_parts))
    token_far, packed_reduced = tie(token_far, packed_reduced)
    piece_rows = width // 16
    places = jnp.stack([my_index // 8, (my_index // 2) % 4]).astype(jnp.int32)
    halves = [
        jnp.concatenate([ffn_reduced[:piece_rows], packed_reduced[: piece_rows // 3]], axis=0),
        jnp.concatenate([ffn_reduced[piece_rows:], packed_reduced[piece_rows // 3 :]], axis=0),
    ]
    pieces = [ring_pieces(halves[1], "z"), ring_pieces(halves[0], "y")]
    halves, pieces = marker.fence(halves, pieces)
    other_ring = run_join(places[:1], (halves[1], *pieces[0]), 1)
    one_ring = run_join(places[1:], (halves[0], *pieces[1]), 4)
    pieces = ring_pieces(other_ring, "y")
    other_ring, one_ring = marker.fence(other_ring, one_ring)
    gathered = trade_z(one_ring)
    one_ring, token_far = marker.fence(one_ring, token_far)
    token_own = [
        (grad_first[i * half : (i + 1) * half] + (token_pair[i].astype(F32) + token_far[i].astype(F32))).astype(BF16)
        for i in range(2)
    ]
    token_other = [lax.ppermute(rows_here, "mp", CORE_SWAP) for rows_here in token_own]
    token_grad = run_settle(core_arg, (*token_own, *token_other))
    closing = finish(marker.state)[0, 0]
    part = piece_rows // 3
    so_far = run_spread_some(places, (other_ring, pieces[0]), piece_rows, part)
    so_far, token_grad = tie(so_far, token_grad)
    *rest, outer_grad = run_spread_rest(
        places, pieces[1:], gathered, so_far, piece_rows, part
    )
    inner_grad, *rest = rest
    cuts = [values.reshape(local_width, width) for values in rest[:4]]
    vectors = rest[4:]
    return (
        loss[0, 0] + closing,
        token_grad,
        cuts[1].T,
        vectors[7],
        cuts[2].T,
        cuts[3].T,
        vectors[8],
        cuts[0],
        vectors[0],
        vectors[1],
        vectors[2],
        inner_grad.reshape(width, width),
        vectors[6],
        outer_grad.reshape(width, width),
        vectors[3],
        vectors[4],
        vectors[5],
    )


def solution(mesh):
    column, row, split = P(None, "mp"), P("mp", None), P("mp")
    placed = (
        (P("dp", None), P("dp"), P())
        + (column, split, column, column, split, row)
        + (P(), P(), P())
        + (column, split, row)
        + (P(), P(), P())
    )
    given = (
        (P(), P("dp", None))
        + (column, split, column, column, split, row)
        + (P(), P(), P())
        + (column, split, row)
        + (P(), P(), P())
    )
    return jax.shard_map(local, mesh=mesh, in_specs=placed, out_specs=given, check_vma=False)
```

```python
import functools
import math

import jax
import jax.numpy as jnp
from jax import lax
from jax.experimental import pallas as pl
from jax.experimental.pallas import tpu as pltpu
from jax.sharding import PartitionSpec as P

HD = 64
EPS_NORM = 1e-06
SOFTMAX_WARMTH = 0.01
NEG_FILL = -1e30
HIGHEST = lax.Precision.HIGHEST
F32 = jnp.float32
BF16 = jnp.bfloat16
QB = 256
KB = 256

CORE_SWAP = [(i, i ^ 1) for i in range(4)]
FAR_SWAP = [(i, i ^ 2) for i in range(4)]
NEAR_SWAP = [(i, i ^ 1) for i in range(32)]
PLANES = [[i * 2 + x for i in range(16)] for x in range(2)]
Z_RINGS = [[i + 8 * z for z in range(4)] for i in range(8)]

SMEM = pl.BlockSpec(memory_space=pltpu.SMEM)
VMEM = pl.BlockSpec(memory_space=pltpu.VMEM)
HBM = pl.BlockSpec(memory_space=pltpu.HBM)


def nn(left, right):
    return lax.dot_general(left, right, (((1,), (0,)), ((), ())), preferred_element_type=F32)


def nt(left, right):
    return lax.dot_general(left, right, (((1,), (1,)), ((), ())), preferred_element_type=F32)


def tn(left, right):
    return lax.dot_general(left, right, (((0,), (0,)), ((), ())), preferred_element_type=F32)


def place_of_block(block, core, rows):
    return ((block % 2) * 2 + block // 2) * QB + core * (rows // 2) & (rows - 1)


def spot_of_keys(j, core, rows):
    place = (j * KB + core * (rows // 2)) & (rows - 1)
    block = place // QB
    return pl.multiple_of(((block % 2) * 2 + block // 2) * QB + place % QB, KB)


def segment_bounds(lengths_ref):
    bounds, total = [], jnp.int32(0)
    for s in range(lengths_ref.shape[0]):
        start = total
        total = total + lengths_ref[s]
        bounds.append((start, total))
    return bounds


def block_span(bounds, first, rows):
    place = first + lax.broadcasted_iota(jnp.int32, (1, QB), 1)
    low, high = first, first + KB
    begin = jnp.full((1, QB), bounds[-1][1], jnp.int32)
    end = jnp.full((1, QB), rows, jnp.int32)
    for start, stop in bounds:
        inside = (place >= start) & (place < stop)
        begin = jnp.where(inside, start, begin)
        end = jnp.where(inside, stop, end)
        touches = (stop > first) & (start < first + QB) & (stop > start)
        low = jnp.where(touches, jnp.minimum(low, start), low)
        high = jnp.where(touches, jnp.maximum(high, stop), high)
    return low // KB, (high + KB - 1) // KB, begin, end


def head_copies(values, heads):
    lane = lax.broadcasted_iota(jnp.int32, values.shape, 1) // HD
    blank = jnp.zeros_like(values)
    return jnp.concatenate([jnp.where(lane == h, values, blank) for h in range(heads)], axis=0)


def span_mask(begin, end, block, heads):
    place = block * KB + lax.broadcasted_iota(jnp.int32, (KB, QB), 0)
    keep = (place >= begin) & (place < end)
    return jnp.concatenate([keep] * heads, axis=1)


def attend(heads, blocks, core, bounds, q_ref, k_ref, vt_ref, mixed_ref, lse_ref, acc_ref):
    rows = k_ref.shape[0]
    for i, block in enumerate(blocks):
        low, high, begin, end = block_span(bounds, place_of_block(block, core, rows), rows)
        stack = head_copies(q_ref[block * QB : (block + 1) * QB, :], heads)
        acc_ref[...] = jnp.zeros(acc_ref.shape, F32)

        def step(j, carry, stack=stack, begin=begin, end=end):
            top, total = carry
            spot = spot_of_keys(j, core, rows)
            scores = nt(k_ref[pl.ds(spot, KB), :], stack)
            scores = jnp.where(span_mask(begin, end, j, heads), scores, NEG_FILL)
            peak = jnp.maximum(top, jnp.max(scores, axis=0, keepdims=True))
            fade = jnp.exp(top - peak)
            probs = jnp.exp(scores - peak)
            total = total * fade + jnp.sum(probs, axis=0, keepdims=True)
            probs = probs.astype(BF16)
            for h in range(heads):
                part = slice(h * QB, (h + 1) * QB)
                span = slice(h * HD, (h + 1) * HD)
                acc_ref[span, :] = acc_ref[span, :] * fade[:, part] + nn(
                    vt_ref[span, pl.ds(spot, KB)], probs[:, part]
                )
            return peak, total

        top = jnp.full((1, heads * QB), NEG_FILL, F32)
        top, total = lax.fori_loop(
            low, high, step, (top, jnp.zeros((1, heads * QB), F32)), unroll=False
        )
        scale = 1.0 / total
        mixed = jnp.concatenate(
            [
                acc_ref[h * HD : (h + 1) * HD, :] * scale[:, h * QB : (h + 1) * QB]
                for h in range(heads)
            ],
            axis=0,
        )
        mixed_ref[i * QB : (i + 1) * QB, :] = mixed.T.astype(BF16)
        lse_ref[i, :, :] = jnp.broadcast_to(top + jnp.log(total), (8, heads * QB))


def fetch(sources, targets, semaphores, order=()):
    copies = [
        pltpu.make_async_copy(source, target, semaphores.at[i])
        for i, (source, target) in enumerate(zip(sources, targets))
    ]
    for i in [*order, *(i for i in range(len(copies)) if i not in order)]:
        copies[i].start()
    return copies


def project(mixed_ref, weights_ref, results, outputs, semaphores):
    results[1][...] = nn(mixed_ref[QB:, :], weights_ref[...]).astype(BF16)
    copies = send_out(results, outputs, semaphores, (1,))
    results[0][...] = nn(mixed_ref[:QB, :], weights_ref[...])
    return copies + send_out(results, outputs, semaphores, (0,))


def attend_first(heads, blocks, lengths_ref, core_ref, *refs):
    sources, outputs, refs = refs[:13], refs[13:24], refs[24:]
    results, targets, refs = refs[:11], refs[11:23], refs[23:]
    acc_ref, semaphores, out_semaphores = refs
    x_ref, q_ref, k_ref, v_ref, vt_ref, mixed_ref, lse_ref = results[:7]
    wqt_ref, wkt_ref, wvt_ref, bq_ref, bv_ref, wo_ref = targets[:6]
    rows = x_ref.shape[0]
    core = core_ref[0]
    copies = fetch(sources[1:], targets, semaphores)
    row_copies = []
    for block in range(rows // QB):
        first = pl.multiple_of(place_of_block(block, core, rows), QB)
        row_copies.append(
            pltpu.make_async_copy(
                sources[0].at[pl.ds(first, QB), :],
                x_ref.at[pl.ds(block * QB, QB), :],
                semaphores.at[12 + block],
            )
        )
        row_copies[-1].start()
    for copy in copies:
        copy.wait()
    query_bias, value_bias = row_of(bq_ref), row_of(bv_ref)
    for block in range(rows // QB):
        row_copies[block].wait()
        part = slice(block * QB, (block + 1) * QB)
        x = x_ref[part, :]
        q = (nt(x, wqt_ref[...]) + query_bias).astype(BF16)
        q_ref[part, :] = q * BF16(0.125)
        k_ref[part, :] = nt(x, wkt_ref[...]).astype(BF16)
        v = nt(x, wvt_ref[...]) + value_bias
        v_ref[part, :] = v.astype(BF16)
        vt_ref[:, part] = v.T.astype(BF16)
    outgoing = send_out(results, outputs, out_semaphores, range(5))
    bounds = segment_bounds(lengths_ref)
    place = core * (2 * QB) + lax.broadcasted_iota(jnp.int32, (1, QB), 1)
    for i in range(2):
        member = [
            jnp.where((place + i * QB >= start) & (place + i * QB < stop), 1.0, 0.0)
            for start, stop in bounds
        ]
        results[9][i] = jnp.concatenate(member, axis=0)
    lines = [row_of(ref) for ref in targets[6:]]
    results[10][...] = jnp.concatenate(lines + [jnp.zeros((2, lines[0].shape[1]), F32)], axis=0)
    outgoing += send_out(results, outputs, out_semaphores, (9, 10))
    attend(heads, blocks, core, bounds, q_ref, k_ref, vt_ref, mixed_ref, lse_ref, acc_ref)
    outgoing += project(mixed_ref, wo_ref, results[7:], outputs[7:], out_semaphores.at[7:9])
    outgoing += send_out(results, outputs, out_semaphores, (5, 6))
    for copy in outgoing:
        copy.wait()


def attend_more(heads, blocks, lengths_ref, core_ref, *refs):
    sources, outputs, refs = refs[:4], refs[4:8], refs[8:]
    targets, results, refs = refs[:4], refs[4:8], refs[8:]
    acc_ref, semaphores, out_semaphores = refs
    q_ref, k_ref, vt_ref, wo_ref = targets
    mixed_ref, lse_ref = results[:2]
    for copy in fetch(sources, targets, semaphores):
        copy.wait()
    bounds = segment_bounds(lengths_ref)
    attend(heads, blocks, core_ref[0], bounds, q_ref, k_ref, vt_ref, mixed_ref, lse_ref, acc_ref)
    outgoing = project(mixed_ref, wo_ref, results[2:], outputs[2:], out_semaphores.at[2:])
    outgoing += send_out(results, outputs, out_semaphores, (0, 1))
    for copy in outgoing:
        copy.wait()


def attend_back(heads, inputs, lengths_ref, core_ref, *refs):
    sources, refs = refs[:inputs], refs[inputs:]
    outputs, refs = refs[:2], refs[2:]
    joint_ref, pack_ref = refs[:2]
    dk_ref, dv_ref, dqt_ref, wo_acc_ref, kt_ref, semaphores, out_semaphores = refs[2:9]
    targets = refs[9:]
    copies = fetch(sources, targets, semaphores, (10, 9, 11, 0, 4, 8, 6, 1, 2, 3, 5, 7))
    grads = targets[0:4]
    mixed = targets[4:6]
    lses = targets[6:8]
    wo_ref, q_ref, k_ref, v_ref = targets[8:12]
    own_sums, other_sums, inner_a, inner_b, x_ref = targets[12:]
    rows, width = q_ref.shape
    core = core_ref[0]
    bounds = segment_bounds(lengths_ref)
    dk_ref[...] = jnp.zeros(dk_ref.shape, F32)
    dv_ref[...] = jnp.zeros(dv_ref.shape, F32)
    joint_ref[...] = jnp.zeros(joint_ref.shape, BF16)
    lane = lax.broadcasted_iota(jnp.int32, (8, width), 1) // HD
    which = (lane == lax.broadcasted_iota(jnp.int32, (8, width), 0)).astype(F32).astype(BF16)
    copies[10].wait()
    for block in range(rows // QB):
        part = slice(block * QB, (block + 1) * QB)
        kt_ref[:, part] = k_ref[part, :].astype(F32).T.astype(BF16)
    for i in (0, 4, 6, 8, 9, 11):
        copies[i].wait()
    for block in range(rows // QB):
        if block > 0:
            copies[block].wait()
        if block == 2:
            copies[5].wait()
            copies[7].wait()
        low, high, begin, end = block_span(bounds, place_of_block(block, core, rows), rows)
        part = slice(block * QB, (block + 1) * QB)
        own = slice(block % 2 * QB, block % 2 * QB + QB)
        grad_attn = grads[block][...]
        mixed_here = mixed[block // 2][own, :]
        outer = tn(mixed_here, grad_attn)
        wo_acc_ref[...] = outer if block == 0 else wo_acc_ref[...] + outer
        grad_mixed = nt(grad_attn, wo_ref[...]).astype(BF16)
        product = grad_mixed.astype(F32) * mixed_here.astype(F32)
        sums = sum(nt(which, part) for part in in_three(product)[:2])
        delta = jnp.concatenate([sums[h : h + 1, :] for h in range(heads)], axis=1)
        lse = lses[block // 2][block % 2, 0:1, :]
        q_stack = head_copies(q_ref[part, :], heads)
        g_stack = head_copies(grad_mixed, heads)
        dqt_ref[...] = jnp.zeros(dqt_ref.shape, F32)

        def step(
            j, carry, delta=delta, lse=lse, q_stack=q_stack, g_stack=g_stack, begin=begin, end=end
        ):
            here = pl.ds(spot_of_keys(j, core, rows), KB)
            scores = nt(k_ref[here, :], q_stack)
            scores = jnp.where(span_mask(begin, end, j, heads), scores, NEG_FILL)
            probs = jnp.exp(scores - lse)
            grad = (probs * (nt(v_ref[here, :], g_stack) - delta)).astype(BF16)
            dv_ref[here, :] += nn(probs.astype(BF16), g_stack)
            dk_ref[here, :] += nn(grad, q_stack)
            for h in range(heads):
                span = slice(h * HD, (h + 1) * HD)
                dqt_ref[span, :] += nn(kt_ref[span, here], grad[:, h * QB : (h + 1) * QB])
            return carry

        lax.fori_loop(low, high, step, 0, unroll=False)
        joint_ref[part, :width] = (dqt_ref[...].T * 0.125).astype(BF16)
    spans = [slice(256 * k, 256 * k + width) for k in range(3)]
    joint_ref[:, spans[1]] = dk_ref[...].astype(BF16)
    joint_ref[:, spans[2]] = dv_ref[...].astype(BF16)
    for copy in copies[12:]:
        copy.wait()
    outgoing = send_out(refs, outputs, out_semaphores, (0,))
    sums = [column_sum(joint_ref[:, spans[k]].astype(F32)) for k in (0, 2)]
    blank = jnp.zeros((1, 256 - width), F32)
    tail = jnp.concatenate([sums[0], blank, sums[1], blank, jnp.zeros((1, 256), F32)], axis=1)
    inner = row_of(inner_a) + row_of(inner_b)
    paired = own_sums[0:6, :] + other_sums[0:6, :]
    small = [paired, inner, tail, jnp.zeros((8, tail.shape[1]), F32)]
    small = jnp.concatenate(small, axis=0).astype(BF16)
    piece = pack_ref.shape[1] - 16
    per = width // piece
    for m in range(4):
        total = wo_acc_ref[...] if m == 0 else tn(joint_ref[:, spans[m - 1]], x_ref[...])
        for t in range(per):
            cut = total[t * piece : (t + 1) * piece, :].astype(BF16)
            pack_ref[m * per + t, 0:piece, :] = cut
            pack_ref[m * per + t, piece:, :] = small if m + t == 0 else jnp.zeros_like(small)
        here = pl.ds(m * per, per)
        copy = pltpu.make_async_copy(
            pack_ref.at[here], outputs[1].at[here], out_semaphores.at[1 + m]
        )
        copy.start()
        outgoing.append(copy)
    for copy in outgoing:
        copy.wait()


def shaped(shape, dtype):
    return jax.ShapeDtypeStruct(shape, dtype)


PARAMS = pltpu.CompilerParams(vmem_limit_bytes=60 << 20)
SMALL = pltpu.CompilerParams(vmem_limit_bytes=60 << 20)
SHARED = pltpu.CompilerParams(vmem_limit_bytes=24 << 20)
COST = pl.CostEstimate(flops=1024, bytes_accessed=1024, transcendentals=0)


def buffers(arrays):
    return [pltpu.VMEM(array.shape, array.dtype) for array in arrays]


def attend_shapes(count, heads, width):
    rows = count * QB
    return (
        shaped((rows, heads * HD), BF16),
        shaped((count, 8, heads * QB), F32),
        shaped((rows // 2, width), F32),
        shaped((rows // 2, width), BF16),
    )


def run_first(lengths, core, tokens, weights, blocks):
    rows, width = tokens.shape
    local_width = weights[0].shape[0]
    heads = local_width // HD
    outs = (
        (shaped(tokens.shape, BF16),)
        + (shaped((rows, local_width), BF16),) * 3
        + (shaped((local_width, rows), BF16),)
        + attend_shapes(len(blocks), heads, width)
        + (shaped((2, lengths.shape[0], QB), F32), shaped((8, width), F32))
    )
    return pl.pallas_call(
        functools.partial(attend_first, heads, blocks),
        out_shape=outs,
        in_specs=[SMEM] * 2 + [HBM] * 13,
        out_specs=(HBM,) * 11,
        scratch_shapes=buffers(outs)
        + buffers(weights)
        + [pltpu.VMEM((local_width, QB), F32)]
        + [pltpu.SemaphoreType.DMA((12 + rows // QB,)), pltpu.SemaphoreType.DMA((11,))],
        compiler_params=PARAMS,
        name="attend_first",
        cost_estimate=COST,
    )(lengths, core, tokens, *weights)


def run_more(lengths, core, arrays, blocks):
    rows, local_width = arrays[0].shape
    heads = local_width // HD
    outs = attend_shapes(len(blocks), heads, arrays[3].shape[1])
    return pl.pallas_call(
        functools.partial(attend_more, heads, blocks),
        out_shape=outs,
        in_specs=[SMEM] * 2 + [HBM] * 4,
        out_specs=(HBM,) * 4,
        scratch_shapes=buffers(arrays)
        + buffers(outs)
        + [pltpu.VMEM((local_width, QB), F32)]
        + [pltpu.SemaphoreType.DMA((4,)), pltpu.SemaphoreType.DMA((4,))],
        compiler_params=PARAMS,
        name="attend_more",
        cost_estimate=COST,
    )(lengths, core, *arrays)


def run_back(lengths, core, arrays):
    wo, q, x = arrays[8], arrays[9], arrays[-1]
    rows, width = q.shape
    heads = width // HD
    piece = 4 * width // 16
    outs = (shaped((rows, 3 * 256), BF16), shaped((16, piece + 16, x.shape[1]), BF16))
    return pl.pallas_call(
        functools.partial(attend_back, heads, len(arrays)),
        out_shape=outs,
        in_specs=[SMEM] * 2 + [HBM] * len(arrays),
        out_specs=(HBM,) * 2,
        scratch_shapes=buffers(outs)
        + [pltpu.VMEM((rows, width), F32)] * 2
        + [pltpu.VMEM((width, QB), F32), pltpu.VMEM(wo.shape, F32), pltpu.VMEM((width, rows), BF16)]
        + [pltpu.SemaphoreType.DMA((len(arrays),)), pltpu.SemaphoreType.DMA((5,))]
        + buffers(arrays),
        compiler_params=PARAMS,
        name="attend_back",
        cost_estimate=COST,
    )(lengths, core, *arrays)


def mark_kernel(source_ref, target_ref):
    del source_ref, target_ref


def mark(values):
    return pl.pallas_call(
        mark_kernel,
        out_shape=shaped(values.shape, values.dtype),
        in_specs=[HBM],
        out_specs=HBM,
        compiler_params=pltpu.CompilerParams(vmem_limit_bytes=1 << 20),
        name="mark",
        cost_estimate=pl.CostEstimate(flops=1 << 36, bytes_accessed=1 << 10, transcendentals=0),
    )(values)


def finish_kernel(source_ref, target_ref):
    del source_ref
    target_ref[...] = jnp.zeros(target_ref.shape, F32)


def finish(values):
    return pl.pallas_call(
        finish_kernel,
        out_shape=shaped(values.shape, values.dtype),
        in_specs=[HBM],
        out_specs=VMEM,
        compiler_params=pltpu.CompilerParams(vmem_limit_bytes=1 << 20),
        name="finish",
        cost_estimate=COST,
    )(values)


def row_of(ref):
    return ref[...].astype(F32).reshape(1, -1)


def in_three(values):
    high = values.astype(BF16)
    rest = values - high.astype(F32)
    middle = rest.astype(BF16)
    return high, middle, (rest - middle.astype(F32)).astype(BF16)


def norm_step(grad, normed, rscale, gain):
    scaled = grad * gain
    first_mean = jnp.mean(scaled, axis=1, keepdims=True)
    cross_mean = jnp.mean(scaled * normed, axis=1, keepdims=True)
    return rscale * (scaled - first_mean - normed * cross_mean)


def column_of(ref):
    row = ref[...].reshape(1, -1)
    return jnp.broadcast_to(row, (128, row.shape[1])).T[:, 0:1]


def column_sum(values):
    return jnp.sum(values, axis=0, keepdims=True)


def send_out(results, outputs, semaphores, which):
    copies = [
        pltpu.make_async_copy(results[k], outputs[k], semaphores.at[k]) for k in which
    ]
    for copy in copies:
        copy.start()
    return copies


def loss_back(lengths_ref, place_ref, *refs):
    sources, outputs, refs = refs[:9], refs[9:15], refs[15:]
    targets, results = refs[:9], refs[9:15]
    coef_ref, turned_ref, semaphores, out_semaphores = refs[15:]
    copies = fetch(sources, targets, semaphores)
    piece_ref, swapped_ref, pooled_ref, match_ref, gain_ref = targets[:5]
    core, index = place_ref[0], place_ref[1]
    bounds = segment_bounds(lengths_ref)
    for copy in copies[:5]:
        copy.wait()
    first = core == 0
    queries = jnp.where(first, piece_ref[...], swapped_ref[...])
    passages = jnp.where(first, swapped_ref[...], piece_ref[...])
    count = queries.shape[0]
    own = pooled_ref.shape[0] // 2
    similarity = nt(queries, passages) / SOFTMAX_WARMTH
    match = match_ref[...].reshape(1, -1)
    match = match == lax.broadcasted_iota(jnp.int32, (count, count), 0)
    top = jnp.max(similarity, axis=1, keepdims=True)
    lse = top + jnp.log(jnp.sum(jnp.exp(similarity - top), axis=1, keepdims=True))
    positive = jnp.sum(jnp.where(match, similarity, 0.0), axis=1, keepdims=True)
    loss = jnp.sum(lse - positive, axis=0, keepdims=True) / count
    results[5][...] = jnp.broadcast_to(loss, results[5].shape)
    coef = (jnp.exp(similarity - lse) - match.astype(F32)) * (1.0 / (count * SOFTMAX_WARMTH))
    coef_ref[...] = coef
    turned_ref[...] = coef.T
    here = pl.ds(pl.multiple_of(index * own, own), own)
    grad_query = sum(nn(part, passages) for part in in_three(coef_ref[here, :])[:2])
    grad_passage = sum(nn(part, queries) for part in in_three(turned_ref[here, :])[:2])
    grad_unit = jnp.concatenate([grad_query, grad_passage], axis=0)
    pooled = pooled_ref[...]
    rscale = lax.rsqrt(jnp.sum(pooled * pooled, axis=1, keepdims=True) + EPS_NORM)
    inner = jnp.sum(pooled * grad_unit, axis=1, keepdims=True)
    grad_pooled = rscale * grad_unit - rscale * rscale * rscale * inner * pooled
    seqs = 2 * own
    grad_pooled = jnp.concatenate(
        [grad_pooled, jnp.zeros((128 - seqs, grad_pooled.shape[1]), F32)], axis=0
    )
    parts = in_three(grad_pooled)[:2]
    lane = lax.broadcasted_iota(jnp.int32, (1, 128), 1)
    begin = end = jnp.zeros((1, 128), jnp.int32)
    for seq, (start, stop) in enumerate(bounds):
        begin = jnp.where(lane == seq, start, begin)
        end = jnp.where(lane == seq, stop, end)
    gain = row_of(gain_ref)
    sums = [0.0, 0.0, 0.0]
    outgoing = []
    for i in range(2):
        copies[5 + 2 * i].wait()
        copies[6 + 2 * i].wait()
        normed = targets[5 + 2 * i][...]
        place = core * (2 * QB) + i * QB + lax.broadcasted_iota(jnp.int32, (QB, 128), 0)
        member = jnp.where((place >= begin) & (place < end), 1.0, 0.0).astype(BF16)
        grad = sum(nn(member, part) for part in parts)
        second = norm_step(grad, normed, column_of(targets[6 + 2 * i]), gain)
        rounded = second.astype(BF16)
        results[i][...] = second
        results[2 + i][...] = rounded
        for k, values in enumerate((rounded.astype(F32), grad * normed, grad)):
            sums[k] = sums[k] + column_sum(values)
        outgoing += send_out(results, outputs, out_semaphores, (2 + i, i))
    results[4][...] = jnp.concatenate(sums + [jnp.zeros((5, sums[0].shape[1]), F32)], axis=0)
    outgoing += send_out(results, outputs, out_semaphores, (4, 5))
    for copy in outgoing:
        copy.wait()


def norm_back(*refs):
    sources, outputs, refs = refs[:12], refs[12:17], refs[17:]
    targets, results = refs[:12], refs[12:17]
    semaphores, out_semaphores = refs[17:]
    copies = fetch(sources, targets, semaphores)
    copies[0].wait()
    copies[1].wait()
    gain = row_of(targets[0])
    sums = [0.0, 0.0, 0.0]
    outgoing = []
    for i in range(2):
        for copy in copies[2 + 5 * i : 7 + 5 * i]:
            copy.wait()
        second, pair_here, far, normed, rscale = targets[2 + 5 * i : 7 + 5 * i]
        grad = second[...] + (pair_here[...].astype(F32) + far[...].astype(F32))
        normed = normed[...]
        first = norm_step(grad, normed, column_of(rscale), gain)
        rounded = first.astype(BF16)
        results[i][...] = first
        results[2 + i][...] = rounded
        for k, values in enumerate((rounded.astype(F32), grad * normed, grad)):
            sums[k] = sums[k] + column_sum(values)
        outgoing += send_out(results, outputs, out_semaphores, (2 + i, i))
    blank = jnp.zeros((2, sums[0].shape[1]), F32)
    results[4][...] = jnp.concatenate(sums + [targets[1][0:3, :], blank], axis=0)
    outgoing += send_out(results, outputs, out_semaphores, (4,))
    for copy in outgoing:
        copy.wait()


STEPS = (0, 2, 1, 3)


def join(copies_of_each, place_ref, *refs):
    sources, output, semaphores = refs[:4], refs[4], refs[5]
    copies = []
    for k in range(4):
        spot = (place_ref[0] + 4 - STEPS[k]) % 4
        for r in range(copies_of_each):
            goal = output.at[spot] if copies_of_each == 1 else output.at[r, spot]
            semaphore = semaphores.at[k * copies_of_each + r]
            copies.append(pltpu.make_async_copy(sources[k], goal, semaphore))
            copies[-1].start()
    for copy in copies:
        copy.wait()


def place_block(piece, part, block_ref, spot, outputs, buffers_, semaphores, first):
    inner, cuts = buffers_
    inner[...] = block_ref[:, :piece, :].astype(F32)
    cuts[...] = block_ref[:, piece : 2 * piece - part, :].astype(F32)
    copies = [pltpu.make_async_copy(inner, outputs[0].at[:, spot], semaphores.at[first])]
    for m in range(4):
        goal = outputs[1 + m].at[spot, pl.ds(part, piece - part), :]
        copies.append(pltpu.make_async_copy(cuts.at[m], goal, semaphores.at[first + 1 + m]))
    for copy in copies:
        copy.start()
    return copies


def place_vectors(piece, part, block_ref, spot, outputs, vectors, semaphores, first):
    @pl.when(spot == 0)
    def _():
        small = block_ref[0, 2 * piece - part :, :].astype(F32)
        for k in range(7):
            vectors[k][...] = small[k : k + 1, :].reshape(-1)
        count = vectors[7].shape[0]
        for k in range(2):
            vectors[7 + k][...] = small[7:8, 256 * k : 256 * k + count].reshape(-1)
        copies = [
            pltpu.make_async_copy(vectors[k], outputs[5 + k], semaphores.at[first + k])
            for k in range(9)
        ]
        for copy in copies:
            copy.start()
        for copy in copies:
            copy.wait()


def spread_some(piece, part, count, place_ref, *refs):
    sources, outputs, refs = refs[:count], refs[count : count + 14], refs[count + 14 :]
    blocks, refs = refs[:count], refs[count:]
    buffers_, vectors, refs = refs[: 2 * count], refs[2 * count : 2 * count + 9], refs[-2:]
    arrivals = fetch(sources, blocks, refs[0])
    outgoing, spots = [], []
    for k in range(count):
        arrivals[k].wait()
        spots.append((place_ref[1] + 4 - STEPS[k]) % 4)
        outgoing += place_block(
            piece, part, blocks[k], spots[k], outputs, buffers_[2 * k : 2 * k + 2], refs[1], 5 * k
        )
    for k in range(count):
        place_vectors(piece, part, blocks[k], spots[k], outputs, vectors, refs[1], 5 * count)
    for copy in outgoing:
        copy.wait()


def spread_rest(piece, part, place_ref, *refs):
    sources, outputs, refs = refs[:3], refs[17:32], refs[32:]
    blocks, by_z, refs = refs[:2], refs[2], refs[3:]
    buffers_, outer, heads, vectors, refs = refs[:4], refs[4], refs[5], refs[6:15], refs[15:]
    semaphores, out_semaphores = refs
    arrivals = fetch(sources, (*blocks, by_z), semaphores)
    outgoing, spots = [], []
    for k in range(2):
        spots.append((place_ref[1] + 4 - STEPS[2 + k]) % 4)
        arrivals[k].wait()
        outgoing += place_block(
            piece,
            part,
            blocks[k],
            spots[k],
            outputs,
            buffers_[2 * k : 2 * k + 2],
            out_semaphores,
            5 * k,
        )
    arrivals[2].wait()
    outer[...] = by_z[:, :, :piece, :].astype(F32)
    copies = [pltpu.make_async_copy(outer, outputs[14], out_semaphores.at[10])]
    copies[0].start()
    heads[...] = by_z[:, :, piece:, :].astype(F32)
    for m in range(4):
        goal = outputs[1 + m].at[:, pl.ds(0, part), :]
        copies.append(pltpu.make_async_copy(heads.at[m], goal, out_semaphores.at[11 + m]))
        copies[-1].start()
    for k in range(2):
        place_vectors(piece, part, blocks[k], spots[k], outputs, vectors, out_semaphores, 15)
    for copy in outgoing + copies:
        copy.wait()


def run_loss(lengths, place, arrays):
    rows, width = arrays[5].shape
    count = arrays[0].shape[0]
    outs = (
        (shaped((rows, width), F32),) * 2
        + (shaped((rows, width), BF16),) * 2
        + (shaped((8, width), F32), shaped((8, 128), F32))
    )
    return pl.pallas_call(
        loss_back,
        out_shape=outs,
        in_specs=[SMEM] * 2 + [HBM] * 9,
        out_specs=(HBM,) * 6,
        scratch_shapes=buffers(arrays)
        + buffers(outs)
        + [pltpu.VMEM((count, count), F32)] * 2
        + [pltpu.SemaphoreType.DMA((9,)), pltpu.SemaphoreType.DMA((6,))],
        compiler_params=SHARED,
        name="loss_back",
        cost_estimate=COST,
    )(lengths, place, *arrays)


def run_norm(arrays):
    rows, width = arrays[2].shape
    outs = (
        (shaped((rows, width), F32),) * 2
        + (shaped((rows, width), BF16),) * 2
        + (shaped((8, width), F32),)
    )
    return pl.pallas_call(
        norm_back,
        out_shape=outs,
        in_specs=[HBM] * 12,
        out_specs=(HBM,) * 5,
        scratch_shapes=buffers(arrays)
        + buffers(outs)
        + [pltpu.SemaphoreType.DMA((12,)), pltpu.SemaphoreType.DMA((5,))],
        compiler_params=SMALL,
        name="norm_back",
        cost_estimate=COST,
    )(*arrays)


def run_join(place, pieces, copies_of_each):
    lead = (4,) if copies_of_each == 1 else (copies_of_each, 4)
    return pl.pallas_call(
        functools.partial(join, copies_of_each),
        out_shape=shaped(lead + pieces[0].shape, BF16),
        in_specs=[SMEM] + [HBM] * 4,
        out_specs=HBM,
        scratch_shapes=[pltpu.SemaphoreType.DMA((4 * copies_of_each,))],
        compiler_params=pltpu.CompilerParams(vmem_limit_bytes=1 << 20),
        name="join",
        cost_estimate=COST,
    )(place, *pieces)


def settle(core_ref, *refs):
    sources, output, semaphores = refs[:4], refs[4], refs[5]
    copies = []
    for k in range(4):
        first = (k // 2 + core_ref[0]) % 2 * (2 * QB) + k % 2 * QB
        spot = pl.ds(pl.multiple_of(first, QB), QB)
        copies.append(pltpu.make_async_copy(sources[k], output.at[spot, :], semaphores.at[k]))
        copies[-1].start()
    for copy in copies:
        copy.wait()


def run_settle(core, parts):
    rows, width = parts[0].shape
    return pl.pallas_call(
        settle,
        out_shape=shaped((4 * rows, width), BF16),
        in_specs=[SMEM] + [HBM] * 4,
        out_specs=HBM,
        scratch_shapes=[pltpu.SemaphoreType.DMA((4,))],
        compiler_params=pltpu.CompilerParams(vmem_limit_bytes=1 << 20),
        name="settle",
        cost_estimate=COST,
    )(core, *parts)


def spread_shapes(piece, width):
    shapes = [(4, 4, piece, width)] + [(4, piece, width)] * 4
    return shapes + [(width,)] * 7 + [(4 * piece,)] * 2


def run_spread_some(places, blocks, piece, part):
    width = blocks[0].shape[2]
    shapes = spread_shapes(piece, width)
    count = len(blocks)
    pair_of = [pltpu.VMEM((4, piece, width), F32), pltpu.VMEM((4, piece - part, width), F32)]
    return pl.pallas_call(
        functools.partial(spread_some, piece, part, count),
        out_shape=[shaped(shape, F32) for shape in shapes],
        in_specs=[SMEM] + [HBM] * count,
        out_specs=[HBM] * 14,
        scratch_shapes=buffers(blocks)
        + pair_of * count
        + [pltpu.VMEM(shape, F32) for shape in shapes[5:]]
        + [pltpu.SemaphoreType.DMA((count,)), pltpu.SemaphoreType.DMA((5 * count + 9,))],
        compiler_params=SHARED,
        name="spread_some",
        cost_estimate=COST,
    )(places, *blocks)


def run_spread_rest(places, blocks, gathered, so_far, piece, part):
    width = gathered.shape[3]
    shapes = spread_shapes(piece, width)
    outer = (4, 4, piece, width)
    pair_of = [pltpu.VMEM((4, piece, width), F32), pltpu.VMEM((4, piece - part, width), F32)]
    return pl.pallas_call(
        functools.partial(spread_rest, piece, part),
        out_shape=[shaped(shape, F32) for shape in shapes + [outer]],
        in_specs=[SMEM] + [HBM] * 17,
        out_specs=[HBM] * 15,
        input_output_aliases={4 + k: k for k in range(14)},
        scratch_shapes=buffers((*blocks, gathered))
        + pair_of * 2
        + [pltpu.VMEM(outer, F32), pltpu.VMEM((4, 4, part, width), F32)]
        + [pltpu.VMEM(shape, F32) for shape in shapes[5:]]
        + [pltpu.SemaphoreType.DMA((3,)), pltpu.SemaphoreType.DMA((24,))],
        compiler_params=SHARED,
        name="spread_rest",
        cost_estimate=COST,
    )(places, *blocks, gathered, *so_far)


def trade(values):
    return lax.all_to_all(
        values, "dp", split_axis=0, concat_axis=0, axis_index_groups=PLANES, tiled=True
    )


def share(values):
    spread_out = jnp.broadcast_to(values[None], (32,) + values.shape)
    return lax.all_to_all(spread_out, "dp", split_axis=0, concat_axis=0, tiled=True)


def trade_z(values):
    return lax.all_to_all(
        values, "dp", split_axis=0, concat_axis=0, axis_index_groups=Z_RINGS, tiled=True
    )


def ring_shift(axis, step):
    pairs = []
    for i in range(32):
        z, y, x = i // 8, (i // 2) % 4, i % 2
        z, y = ((z + step) % 4, y) if axis == "z" else (z, (y + step) % 4)
        pairs.append((i, (z * 4 + y) * 2 + x))
    return pairs


def ring_pieces(values, axis):
    return [lax.ppermute(values, "dp", ring_shift(axis, step)) for step in STEPS[1:]]


def tie(values, others):
    return lax.optimization_barrier((values, others))


class Marker:
    def __init__(self):
        self.state = jnp.zeros((8, 128), F32)

    def fence(self, ready, later):
        ready, state = tie(ready, self.state)
        later, self.state = tie(later, mark(state))
        return ready, later

    def moved(self, values, axis, pairs):
        values, state = tie(values, self.state)
        arrived, self.state = tie(lax.ppermute(values, axis, pairs), mark(state))
        return arrived

    def core_swap(self, values):
        return self.moved(values, "mp", CORE_SWAP)

    def near_swap(self, values):
        return self.moved(values, "dp", NEAR_SWAP)

    def both(self, own):
        return jnp.concatenate([own, self.core_swap(own)], axis=0)

    def near_sum(self, total):
        return (total.astype(F32) + self.near_swap(total).astype(F32)).astype(BF16)


def plane_sum(parts):
    return jnp.sum(parts.astype(F32), axis=0).astype(BF16)


def far_swap(values):
    return lax.ppermute(values, "mp", FAR_SWAP)


def norm_forward(values, gain_vec, shift_vec):
    average = jnp.mean(values, axis=-1, keepdims=True)
    centred = values - average
    rscale = lax.rsqrt(jnp.mean(centred * centred, axis=-1, keepdims=True) + EPS_NORM)
    normed = centred * rscale
    return (normed * gain_vec + shift_vec, normed, rscale[:, 0])


def gelu_and_slope(upper):
    below = 0.5 * (1.0 + lax.erf(upper * math.sqrt(0.5)))
    density = jnp.exp(-0.5 * upper * upper) * (1.0 / math.sqrt(2.0 * math.pi))
    return (upper * below).astype(BF16), (below + upper * density).astype(BF16)


def local(
    tokens,
    lengths,
    pair_index,
    query_proj,
    query_bias,
    key_proj,
    value_proj,
    value_bias,
    output_proj,
    output_bias,
    attn_gain,
    attn_shift,
    inner_proj,
    inner_bias,
    outer_proj,
    outer_bias,
    final_gain,
    final_shift,
):
    row_count, width = tokens.shape
    chunk = row_count // 2
    half = chunk // 2
    seq_count = lengths.shape[0]
    pair_count = seq_count // 2
    overall_pair_count = pair_index.shape[0]
    local_width = query_proj.shape[1]
    core = lax.axis_index("mp") % 2
    my_index = lax.axis_index("dp")
    marker = Marker()
    core_arg = jnp.reshape(core, (1,)).astype(jnp.int32)
    vectors = (output_bias, attn_gain, attn_shift, outer_bias, final_gain, final_shift)
    query_t, key_t, value_t = query_proj.T, key_proj.T, value_proj.T
    blank = jnp.zeros((256 - local_width, width), BF16)
    joint_proj = jnp.concatenate([query_t, blank, key_t, blank, value_t, blank], axis=0)

    weights = (query_t, key_t, value_t, query_bias, value_bias, output_proj, *vectors)
    first = run_first(lengths, core_arg, tokens, weights, (0, 1))
    rows, query_b, key_b, value_b, value_tb, mixed_a, lse_a = first[:7]
    attn_own_a, attn_other_a, members, vectors = first[7:]

    def own_and_other(values, weights):
        return nn(values[:half], weights), nn(values[half:], weights).astype(BF16)

    def pair(own, arrived):
        return (own + arrived.astype(F32)).astype(BF16)

    def first_norm(index, pair_here, far):
        attn_full = pair_here.astype(F32) + far.astype(F32) + output_bias
        own_tokens = rows[index * chunk : index * chunk + half].astype(F32)
        return norm_forward(own_tokens + attn_full, attn_gain_f, attn_shift_f)

    def feed_forward(own_hidden):
        whole = marker.both(own_hidden)
        act, slope = gelu_and_slope(nn(whole, inner_proj) + inner_bias.astype(F32))
        return whole, act, slope

    def last_norm(hidden, pair_here, far):
        ffn_full = pair_here.astype(F32) + far.astype(F32) + outer_bias
        return norm_forward(hidden + ffn_full, final_gain_f, final_shift_f)

    attn_pair_a = pair(attn_own_a, marker.core_swap(attn_other_a))
    attn_far_a = far_swap(attn_pair_a)
    output_bias, attn_gain_f, attn_shift_f = vectors[0], vectors[1], vectors[2]
    outer_bias, final_gain_f, final_shift_f = vectors[3], vectors[4], vectors[5]
    late_query, late_pair = tie(query_b, attn_pair_a)
    mixed_b, lse_b, attn_own_b, attn_other_b = run_more(
        lengths, core_arg, (late_query, key_b, value_tb, output_proj), (2, 3)
    )
    attn_pair_b = pair(attn_own_b, marker.core_swap(attn_other_b))
    attn_far_b = far_swap(attn_pair_b)
    attn_far_a, attn_pair_b = tie(attn_far_a, attn_pair_b)
    hidden_a, normed_one_a, rscale_one_a = first_norm(0, late_pair, attn_far_a)
    own_hidden_a = hidden_a.astype(BF16)
    hidden_ab, act_a, slope_a = feed_forward(own_hidden_a)
    ffn_own_a, ffn_other_a = own_and_other(act_a, outer_proj)
    ffn_pair_a = pair(ffn_own_a, marker.core_swap(ffn_other_a))
    attn_far_b, ffn_pair_late = tie(attn_far_b, ffn_pair_a)
    ffn_far_a = far_swap(ffn_pair_a)
    hidden_b, normed_one_b, rscale_one_b = first_norm(1, attn_pair_b, attn_far_b)
    own_hidden_b = hidden_b.astype(BF16)
    hidden_bb, act_b, slope_b = feed_forward(own_hidden_b)
    ffn_own_b, ffn_other_b = own_and_other(act_b, outer_proj)
    ffn_pair_b = pair(ffn_own_b, marker.core_swap(ffn_other_b))
    ffn_pair_b, ffn_far_a = marker.fence(ffn_pair_b, ffn_far_a)
    final_a, normed_two_a, rscale_two_a = last_norm(hidden_a, ffn_pair_late, ffn_far_a)
    pooled_a = jnp.dot(members[0], final_a, precision=HIGHEST)
    final_b, normed_two_b, rscale_two_b = last_norm(hidden_b, ffn_pair_b, far_swap(ffn_pair_b))
    pooled_part = pooled_a + jnp.dot(members[1], final_b, precision=HIGHEST)
    lse = (lse_a, lse_b)
    hidden_whole, act, slope = (hidden_ab, hidden_bb), (act_a, act_b), (slope_a, slope_b)
    normed_one, rscale_one = (normed_one_a, normed_one_b), (rscale_one_a, rscale_one_b)
    normed_two, rscale_two = (normed_two_a, normed_two_b), (rscale_two_a, rscale_two_b)
    pooled = pooled_part + marker.core_swap(pooled_part)
    pool_rscale = lax.rsqrt(jnp.sum(pooled * pooled, axis=-1, keepdims=True) + EPS_NORM)
    unit_b = (pooled * pool_rscale).astype(BF16)

    piece = lax.dynamic_slice_in_dim(unit_b, core * pair_count, pair_count, 0)
    piece = share(piece).reshape(overall_pair_count, width)
    place_arg = jnp.stack([core, my_index]).astype(jnp.int32)
    *grads, last_sums, loss = run_loss(
        lengths,
        place_arg,
        (
            piece,
            marker.core_swap(piece),
            pooled,
            pair_index,
            final_gain,
            normed_two[0],
            rscale_two[0],
            normed_two[1],
            rscale_two[1],
        ),
    )
    grad_second, own_grad = grads[:2], grads[2:]

    inner_sums, grad_ffn, grad_up, hidden_other, outer_sums = [], [], [], [], []
    for i in range(2):
        grad_ffn.append(marker.both(own_grad[i]))
        grad_up.append((nt(grad_ffn[i], outer_proj) * slope[i].astype(F32)).astype(BF16))
        inner_sums.append(jnp.sum(grad_up[i].astype(F32), axis=0))
        other = nt(grad_up[i][half:], inner_proj).astype(BF16)
        late_act, other = tie(act[i], other)
        outer_sums.append(tn(late_act, grad_ffn[i]))
        swap = marker.core_swap if i else lambda rows_here: lax.ppermute(rows_here, "mp", CORE_SWAP)
        arrived, outer_sums[i] = tie(swap(other), outer_sums[i])
        hidden_other.append(arrived)
    hidden_pair = [pair(nt(grad_up[i][:half], inner_proj), hidden_other[i]) for i in range(2)]
    hidden_far = [far_swap(hidden_pair[i]) for i in range(2)]
    late_hidden, hidden_pair = tie(hidden_whole, hidden_pair)
    ffn_pack = jnp.concatenate(
        [
            (outer_sums[0] + outer_sums[1])
            .astype(BF16)
            .reshape(16, -1, width),
            (tn(late_hidden[0], grad_up[0]) + tn(late_hidden[1], grad_up[1]))
            .astype(BF16)
            .reshape(16, -1, width),
        ],
        axis=1,
    )
    ffn_pack, hidden_far = marker.fence(ffn_pack, hidden_far)
    ffn_parts = trade(ffn_pack)

    *grads, sums = run_norm(
        (
            attn_gain,
            last_sums,
            grad_second[0],
            hidden_pair[0],
            hidden_far[0],
            normed_one[0],
            rscale_one[0],
            grad_second[1],
            hidden_pair[1],
            hidden_far[1],
            normed_one[1],
            rscale_one[1],
        )
    )
    grad_first, own_grad = grads[:2], grads[2:]
    (*own_grad, sums), state = tie((*own_grad, sums), marker.state)
    arrived = [lax.ppermute(values, "mp", CORE_SWAP) for values in (*own_grad, sums)]
    (*other_grad, other_sums), marker.state = tie(arrived, mark(state))
    grad_rows, packed = run_back(
        lengths,
        core_arg,
        (
            own_grad[0],
            other_grad[0],
            own_grad[1],
            other_grad[1],
            mixed_a,
            mixed_b,
            *lse,
            output_proj,
            query_b,
            key_b,
            value_b,
            sums,
            other_sums,
            *inner_sums,
            rows,
        ),
    )

    def input_part(first):
        span = slice(first, first + half)
        return nn(grad_rows[span], joint_proj)

    token_pair = []
    for i in range(2):
        other = input_part(i * chunk + half).astype(BF16)
        token_pair.append(pair(input_part(i * chunk), marker.core_swap(other)))
    token_pair, (packed, ffn_parts) = marker.fence(token_pair, (packed, ffn_parts))
    (packed, token_pair), ffn_parts = marker.fence((packed, token_pair), ffn_parts)
    packed_parts = trade(packed)
    token_far = [far_swap(token_pair[i]) for i in range(2)]
    ffn_total = plane_sum(ffn_parts)
    ffn_near = lax.ppermute(ffn_total, "dp", NEAR_SWAP)
    ffn_reduced = (ffn_total.astype(F32) + ffn_near.astype(F32)).astype(BF16)
    ffn_reduced, packed_parts = tie(ffn_reduced, packed_parts)
    packed_reduced = marker.near_sum(plane_sum(packed_parts))
    token_far, packed_reduced = tie(token_far, packed_reduced)
    piece_rows = width // 16
    places = jnp.stack([my_index // 8, (my_index // 2) % 4]).astype(jnp.int32)
    halves = [
        jnp.concatenate([ffn_reduced[:piece_rows], packed_reduced[: piece_rows // 3]], axis=0),
        jnp.concatenate([ffn_reduced[piece_rows:], packed_reduced[piece_rows // 3 :]], axis=0),
    ]
    pieces = [ring_pieces(halves[1], "z"), ring_pieces(halves[0], "y")]
    halves, pieces = marker.fence(halves, pieces)
    other_ring = run_join(places[:1], (halves[1], *pieces[0]), 1)
    one_ring = run_join(places[1:], (halves[0], *pieces[1]), 4)
    pieces = ring_pieces(other_ring, "y")
    other_ring, one_ring = marker.fence(other_ring, one_ring)
    gathered = trade_z(one_ring)
    one_ring, token_far = marker.fence(one_ring, token_far)
    token_own = [
        (grad_first[i] + (token_pair[i].astype(F32) + token_far[i].astype(F32))).astype(BF16)
        for i in range(2)
    ]
    token_other = [lax.ppermute(rows_here, "mp", CORE_SWAP) for rows_here in token_own]
    token_grad = run_settle(core_arg, (*token_own, *token_other))
    closing = finish(marker.state)[0, 0]
    part = piece_rows // 3
    so_far = run_spread_some(places, (other_ring, pieces[0]), piece_rows, part)
    so_far, token_grad = tie(so_far, token_grad)
    *rest, outer_grad = run_spread_rest(
        places, pieces[1:], gathered, so_far, piece_rows, part
    )
    inner_grad, *rest = rest
    cuts = [values.reshape(local_width, width) for values in rest[:4]]
    vectors = rest[4:]
    return (
        loss[0, 0] + closing,
        token_grad,
        cuts[1].T,
        vectors[7],
        cuts[2].T,
        cuts[3].T,
        vectors[8],
        cuts[0],
        vectors[0],
        vectors[1],
        vectors[2],
        inner_grad.reshape(width, width),
        vectors[6],
        outer_grad.reshape(width, width),
        vectors[3],
        vectors[4],
        vectors[5],
    )


def solution(mesh):
    column, row, split = P(None, "mp"), P("mp", None), P("mp")
    placed = (
        (P("dp", None), P("dp"), P())
        + (column, split, column, column, split, row)
        + (P(), P(), P())
        + (column, split, row)
        + (P(), P(), P())
    )
    given = (
        (P(), P("dp", None))
        + (column, split, column, column, split, row)
        + (P(), P(), P())
        + (column, split, row)
        + (P(), P(), P())
    )
    return jax.shard_map(local, mesh=mesh, in_specs=placed, out_specs=given, check_vma=False)
```

```python
import functools
import math

import jax
import jax.numpy as jnp
from jax import lax
from jax.experimental import pallas as pl
from jax.experimental.pallas import tpu as pltpu
from jax.sharding import PartitionSpec as P

HD = 64
EPS_NORM = 1e-06
SOFTMAX_WARMTH = 0.01
NEG_FILL = -1e30
HIGHEST = lax.Precision.HIGHEST
F32 = jnp.float32
BF16 = jnp.bfloat16
QB = 256
KB = 256

CORE_SWAP = [(i, i ^ 1) for i in range(4)]
FAR_SWAP = [(i, i ^ 2) for i in range(4)]
NEAR_SWAP = [(i, i ^ 1) for i in range(32)]
PLANES = [[i * 2 + x for i in range(16)] for x in range(2)]
Z_RINGS = [[i + 8 * z for z in range(4)] for i in range(8)]

SMEM = pl.BlockSpec(memory_space=pltpu.SMEM)
VMEM = pl.BlockSpec(memory_space=pltpu.VMEM)
HBM = pl.BlockSpec(memory_space=pltpu.HBM)


def nn(left, right):
    return lax.dot_general(left, right, (((1,), (0,)), ((), ())), preferred_element_type=F32)


def nt(left, right):
    return lax.dot_general(left, right, (((1,), (1,)), ((), ())), preferred_element_type=F32)


def tn(left, right):
    return lax.dot_general(left, right, (((0,), (0,)), ((), ())), preferred_element_type=F32)


def place_of_block(block, core, rows):
    return ((block % 2) * 2 + block // 2) * QB + core * (rows // 2) & (rows - 1)


def spot_of_keys(j, core, rows):
    place = (j * KB + core * (rows // 2)) & (rows - 1)
    block = place // QB
    return pl.multiple_of(((block % 2) * 2 + block // 2) * QB + place % QB, KB)


def segment_bounds(lengths_ref):
    bounds, total = [], jnp.int32(0)
    for s in range(lengths_ref.shape[0]):
        start = total
        total = total + lengths_ref[s]
        bounds.append((start, total))
    return bounds


def block_span(bounds, first, rows):
    place = first + lax.broadcasted_iota(jnp.int32, (1, QB), 1)
    low, high = first, first + KB
    begin = jnp.full((1, QB), bounds[-1][1], jnp.int32)
    end = jnp.full((1, QB), rows, jnp.int32)
    for start, stop in bounds:
        inside = (place >= start) & (place < stop)
        begin = jnp.where(inside, start, begin)
        end = jnp.where(inside, stop, end)
        touches = (stop > first) & (start < first + QB) & (stop > start)
        low = jnp.where(touches, jnp.minimum(low, start), low)
        high = jnp.where(touches, jnp.maximum(high, stop), high)
    return low // KB, (high + KB - 1) // KB, begin, end


def head_copies(values, heads):
    lane = lax.broadcasted_iota(jnp.int32, values.shape, 1) // HD
    blank = jnp.zeros_like(values)
    return jnp.concatenate([jnp.where(lane == h, values, blank) for h in range(heads)], axis=0)


def span_mask(begin, end, block, heads):
    place = block * KB + lax.broadcasted_iota(jnp.int32, (KB, QB), 0)
    keep = (place >= begin) & (place < end)
    return jnp.concatenate([keep] * heads, axis=1)


def attend(heads, blocks, core, bounds, q_ref, k_ref, vt_ref, mixed_ref, lse_ref, acc_ref):
    rows = k_ref.shape[0]
    for i, block in enumerate(blocks):
        low, high, begin, end = block_span(bounds, place_of_block(block, core, rows), rows)
        stack = head_copies(q_ref[block * QB : (block + 1) * QB, :], heads)
        acc_ref[...] = jnp.zeros(acc_ref.shape, F32)

        def step(j, carry, stack=stack, begin=begin, end=end):
            top, total = carry
            spot = spot_of_keys(j, core, rows)
            scores = nt(k_ref[pl.ds(spot, KB), :], stack)
            scores = jnp.where(span_mask(begin, end, j, heads), scores, NEG_FILL)
            peak = jnp.maximum(top, jnp.max(scores, axis=0, keepdims=True))
            fade = jnp.exp(top - peak)
            probs = jnp.exp(scores - peak)
            total = total * fade + jnp.sum(probs, axis=0, keepdims=True)
            probs = probs.astype(BF16)
            for h in range(heads):
                part = slice(h * QB, (h + 1) * QB)
                span = slice(h * HD, (h + 1) * HD)
                acc_ref[span, :] = acc_ref[span, :] * fade[:, part] + nn(
                    vt_ref[span, pl.ds(spot, KB)], probs[:, part]
                )
            return peak, total

        top = jnp.full((1, heads * QB), NEG_FILL, F32)
        top, total = lax.fori_loop(
            low, high, step, (top, jnp.zeros((1, heads * QB), F32)), unroll=False
        )
        scale = 1.0 / total
        mixed = jnp.concatenate(
            [
                acc_ref[h * HD : (h + 1) * HD, :] * scale[:, h * QB : (h + 1) * QB]
                for h in range(heads)
            ],
            axis=0,
        )
        mixed_ref[i * QB : (i + 1) * QB, :] = mixed.T.astype(BF16)
        lse_ref[i, :, :] = jnp.broadcast_to(top + jnp.log(total), (8, heads * QB))


def fetch(sources, targets, semaphores, order=()):
    copies = [
        pltpu.make_async_copy(source, target, semaphores.at[i])
        for i, (source, target) in enumerate(zip(sources, targets))
    ]
    for i in [*order, *(i for i in range(len(copies)) if i not in order)]:
        copies[i].start()
    return copies


def project(mixed_ref, weights_ref, results, outputs, semaphores):
    results[1][...] = nn(mixed_ref[QB:, :], weights_ref[...]).astype(BF16)
    copies = send_out(results, outputs, semaphores, (1,))
    results[0][...] = nn(mixed_ref[:QB, :], weights_ref[...])
    return copies + send_out(results, outputs, semaphores, (0,))


def attend_first(heads, blocks, lengths_ref, core_ref, *refs):
    sources, outputs, refs = refs[:13], refs[13:24], refs[24:]
    results, targets, refs = refs[:11], refs[11:23], refs[23:]
    acc_ref, semaphores, out_semaphores = refs
    x_ref, q_ref, k_ref, v_ref, vt_ref, mixed_ref, lse_ref = results[:7]
    wqt_ref, wkt_ref, wvt_ref, bq_ref, bv_ref, wo_ref = targets[:6]
    rows = x_ref.shape[0]
    core = core_ref[0]
    copies = fetch(sources[1:], targets, semaphores)
    row_copies = []
    for block in range(rows // QB):
        first = pl.multiple_of(place_of_block(block, core, rows), QB)
        row_copies.append(
            pltpu.make_async_copy(
                sources[0].at[pl.ds(first, QB), :],
                x_ref.at[pl.ds(block * QB, QB), :],
                semaphores.at[12 + block],
            )
        )
        row_copies[-1].start()
    for copy in copies:
        copy.wait()
    query_bias, value_bias = row_of(bq_ref), row_of(bv_ref)
    for block in range(rows // QB):
        row_copies[block].wait()
        part = slice(block * QB, (block + 1) * QB)
        x = x_ref[part, :]
        q = (nt(x, wqt_ref[...]) + query_bias).astype(BF16)
        q_ref[part, :] = q * BF16(0.125)
        k_ref[part, :] = nt(x, wkt_ref[...]).astype(BF16)
        v = nt(x, wvt_ref[...]) + value_bias
        v_ref[part, :] = v.astype(BF16)
        vt_ref[:, part] = v.T.astype(BF16)
    outgoing = send_out(results, outputs, out_semaphores, range(5))
    bounds = segment_bounds(lengths_ref)
    place = core * (2 * QB) + lax.broadcasted_iota(jnp.int32, (1, QB), 1)
    for i in range(2):
        member = [
            jnp.where((place + i * QB >= start) & (place + i * QB < stop), 1.0, 0.0)
            for start, stop in bounds
        ]
        results[9][i] = jnp.concatenate(member, axis=0)
    lines = [row_of(ref) for ref in targets[6:]]
    results[10][...] = jnp.concatenate(lines + [jnp.zeros((2, lines[0].shape[1]), F32)], axis=0)
    outgoing += send_out(results, outputs, out_semaphores, (9, 10))
    attend(heads, blocks, core, bounds, q_ref, k_ref, vt_ref, mixed_ref, lse_ref, acc_ref)
    outgoing += project(mixed_ref, wo_ref, results[7:], outputs[7:], out_semaphores.at[7:9])
    outgoing += send_out(results, outputs, out_semaphores, (5, 6))
    for copy in outgoing:
        copy.wait()


def attend_more(heads, blocks, lengths_ref, core_ref, *refs):
    sources, outputs, refs = refs[:4], refs[4:8], refs[8:]
    targets, results, refs = refs[:4], refs[4:8], refs[8:]
    acc_ref, semaphores, out_semaphores = refs
    q_ref, k_ref, vt_ref, wo_ref = targets
    mixed_ref, lse_ref = results[:2]
    for copy in fetch(sources, targets, semaphores):
        copy.wait()
    bounds = segment_bounds(lengths_ref)
    attend(heads, blocks, core_ref[0], bounds, q_ref, k_ref, vt_ref, mixed_ref, lse_ref, acc_ref)
    outgoing = project(mixed_ref, wo_ref, results[2:], outputs[2:], out_semaphores.at[2:])
    outgoing += send_out(results, outputs, out_semaphores, (0, 1))
    for copy in outgoing:
        copy.wait()


def attend_back(heads, inputs, lengths_ref, core_ref, *refs):
    sources, refs = refs[:inputs], refs[inputs:]
    outputs, refs = refs[:2], refs[2:]
    joint_ref, pack_ref = refs[:2]
    dk_ref, dv_ref, dqt_ref, wo_acc_ref, kt_ref, semaphores, out_semaphores = refs[2:9]
    targets = refs[9:]
    copies = fetch(sources, targets, semaphores, (10, 9, 11, 0, 4, 8, 6, 1, 2, 3, 5, 7))
    grads = targets[0:4]
    mixed = targets[4:6]
    lses = targets[6:8]
    wo_ref, q_ref, k_ref, v_ref = targets[8:12]
    own_sums, other_sums, inner_a, inner_b, x_ref = targets[12:]
    rows, width = q_ref.shape
    core = core_ref[0]
    bounds = segment_bounds(lengths_ref)
    dk_ref[...] = jnp.zeros(dk_ref.shape, F32)
    dv_ref[...] = jnp.zeros(dv_ref.shape, F32)
    joint_ref[...] = jnp.zeros(joint_ref.shape, BF16)
    lane = lax.broadcasted_iota(jnp.int32, (8, width), 1) // HD
    which = (lane == lax.broadcasted_iota(jnp.int32, (8, width), 0)).astype(F32).astype(BF16)
    copies[10].wait()
    for block in range(rows // QB):
        part = slice(block * QB, (block + 1) * QB)
        kt_ref[:, part] = k_ref[part, :].astype(F32).T.astype(BF16)
    for i in (0, 4, 6, 8, 9, 11):
        copies[i].wait()
    for block in range(rows // QB):
        if block > 0:
            copies[block].wait()
        if block == 2:
            copies[5].wait()
            copies[7].wait()
        low, high, begin, end = block_span(bounds, place_of_block(block, core, rows), rows)
        part = slice(block * QB, (block + 1) * QB)
        own = slice(block % 2 * QB, block % 2 * QB + QB)
        grad_attn = grads[block][...]
        mixed_here = mixed[block // 2][own, :]
        outer = tn(mixed_here, grad_attn)
        wo_acc_ref[...] = outer if block == 0 else wo_acc_ref[...] + outer
        grad_mixed = nt(grad_attn, wo_ref[...]).astype(BF16)
        product = grad_mixed.astype(F32) * mixed_here.astype(F32)
        sums = sum(nt(which, part) for part in in_three(product)[:2])
        delta = jnp.concatenate([sums[h : h + 1, :] for h in range(heads)], axis=1)
        lse = lses[block // 2][block % 2, 0:1, :]
        q_stack = head_copies(q_ref[part, :], heads)
        g_stack = head_copies(grad_mixed, heads)
        dqt_ref[...] = jnp.zeros(dqt_ref.shape, F32)

        def step(
            j, carry, delta=delta, lse=lse, q_stack=q_stack, g_stack=g_stack, begin=begin, end=end
        ):
            here = pl.ds(spot_of_keys(j, core, rows), KB)
            scores = nt(k_ref[here, :], q_stack)
            scores = jnp.where(span_mask(begin, end, j, heads), scores, NEG_FILL)
            probs = jnp.exp(scores - lse)
            grad = (probs * (nt(v_ref[here, :], g_stack) - delta)).astype(BF16)
            dv_ref[here, :] += nn(probs.astype(BF16), g_stack)
            dk_ref[here, :] += nn(grad, q_stack)
            for h in range(heads):
                span = slice(h * HD, (h + 1) * HD)
                dqt_ref[span, :] += nn(kt_ref[span, here], grad[:, h * QB : (h + 1) * QB])
            return carry

        lax.fori_loop(low, high, step, 0, unroll=False)
        joint_ref[part, :width] = (dqt_ref[...].T * 0.125).astype(BF16)
    spans = [slice(256 * k, 256 * k + width) for k in range(3)]
    joint_ref[:, spans[1]] = dk_ref[...].astype(BF16)
    joint_ref[:, spans[2]] = dv_ref[...].astype(BF16)
    for copy in copies[12:]:
        copy.wait()
    outgoing = send_out(refs, outputs, out_semaphores, (0,))
    sums = [column_sum(joint_ref[:, spans[k]].astype(F32)) for k in (0, 2)]
    blank = jnp.zeros((1, 256 - width), F32)
    tail = jnp.concatenate([sums[0], blank, sums[1], blank, jnp.zeros((1, 256), F32)], axis=1)
    inner = row_of(inner_a) + row_of(inner_b)
    paired = own_sums[0:6, :] + other_sums[0:6, :]
    small = [paired, inner, tail, jnp.zeros((8, tail.shape[1]), F32)]
    small = jnp.concatenate(small, axis=0).astype(BF16)
    piece = pack_ref.shape[1] - 16
    per = width // piece
    for m in range(4):
        total = wo_acc_ref[...] if m == 0 else tn(joint_ref[:, spans[m - 1]], x_ref[...])
        for t in range(per):
            cut = total[t * piece : (t + 1) * piece, :].astype(BF16)
            pack_ref[m * per + t, 0:piece, :] = cut
            pack_ref[m * per + t, piece:, :] = small if m + t == 0 else jnp.zeros_like(small)
        here = pl.ds(m * per, per)
        copy = pltpu.make_async_copy(
            pack_ref.at[here], outputs[1].at[here], out_semaphores.at[1 + m]
        )
        copy.start()
        outgoing.append(copy)
    for copy in outgoing:
        copy.wait()


def shaped(shape, dtype):
    return jax.ShapeDtypeStruct(shape, dtype)


PARAMS = pltpu.CompilerParams(vmem_limit_bytes=60 << 20)
SMALL = pltpu.CompilerParams(vmem_limit_bytes=60 << 20)
SHARED = pltpu.CompilerParams(vmem_limit_bytes=24 << 20)
COST = pl.CostEstimate(flops=1024, bytes_accessed=1024, transcendentals=0)


def buffers(arrays):
    return [pltpu.VMEM(array.shape, array.dtype) for array in arrays]


def attend_shapes(count, heads, width):
    rows = count * QB
    return (
        shaped((rows, heads * HD), BF16),
        shaped((count, 8, heads * QB), F32),
        shaped((rows // 2, width), F32),
        shaped((rows // 2, width), BF16),
    )


def run_first(lengths, core, tokens, weights, blocks):
    rows, width = tokens.shape
    local_width = weights[0].shape[0]
    heads = local_width // HD
    outs = (
        (shaped(tokens.shape, BF16),)
        + (shaped((rows, local_width), BF16),) * 3
        + (shaped((local_width, rows), BF16),)
        + attend_shapes(len(blocks), heads, width)
        + (shaped((2, lengths.shape[0], QB), F32), shaped((8, width), F32))
    )
    return pl.pallas_call(
        functools.partial(attend_first, heads, blocks),
        out_shape=outs,
        in_specs=[SMEM] * 2 + [HBM] * 13,
        out_specs=(HBM,) * 11,
        scratch_shapes=buffers(outs)
        + buffers(weights)
        + [pltpu.VMEM((local_width, QB), F32)]
        + [pltpu.SemaphoreType.DMA((12 + rows // QB,)), pltpu.SemaphoreType.DMA((11,))],
        compiler_params=PARAMS,
        name="attend_first",
        cost_estimate=COST,
    )(lengths, core, tokens, *weights)


def run_more(lengths, core, arrays, blocks):
    rows, local_width = arrays[0].shape
    heads = local_width // HD
    outs = attend_shapes(len(blocks), heads, arrays[3].shape[1])
    return pl.pallas_call(
        functools.partial(attend_more, heads, blocks),
        out_shape=outs,
        in_specs=[SMEM] * 2 + [HBM] * 4,
        out_specs=(HBM,) * 4,
        scratch_shapes=buffers(arrays)
        + buffers(outs)
        + [pltpu.VMEM((local_width, QB), F32)]
        + [pltpu.SemaphoreType.DMA((4,)), pltpu.SemaphoreType.DMA((4,))],
        compiler_params=PARAMS,
        name="attend_more",
        cost_estimate=COST,
    )(lengths, core, *arrays)


def run_back(lengths, core, arrays):
    wo, q, x = arrays[8], arrays[9], arrays[-1]
    rows, width = q.shape
    heads = width // HD
    piece = 4 * width // 16
    outs = (shaped((rows, 3 * 256), BF16), shaped((16, piece + 16, x.shape[1]), BF16))
    return pl.pallas_call(
        functools.partial(attend_back, heads, len(arrays)),
        out_shape=outs,
        in_specs=[SMEM] * 2 + [HBM] * len(arrays),
        out_specs=(HBM,) * 2,
        scratch_shapes=buffers(outs)
        + [pltpu.VMEM((rows, width), F32)] * 2
        + [pltpu.VMEM((width, QB), F32), pltpu.VMEM(wo.shape, F32), pltpu.VMEM((width, rows), BF16)]
        + [pltpu.SemaphoreType.DMA((len(arrays),)), pltpu.SemaphoreType.DMA((5,))]
        + buffers(arrays),
        compiler_params=PARAMS,
        name="attend_back",
        cost_estimate=COST,
    )(lengths, core, *arrays)


def mark_kernel(source_ref, target_ref):
    del source_ref, target_ref


def mark(values):
    return pl.pallas_call(
        mark_kernel,
        out_shape=shaped(values.shape, values.dtype),
        in_specs=[HBM],
        out_specs=HBM,
        compiler_params=pltpu.CompilerParams(vmem_limit_bytes=1 << 20),
        name="mark",
        cost_estimate=pl.CostEstimate(flops=1 << 36, bytes_accessed=1 << 10, transcendentals=0),
    )(values)


def finish_kernel(source_ref, target_ref):
    del source_ref
    target_ref[...] = jnp.zeros(target_ref.shape, F32)


def finish(values):
    return pl.pallas_call(
        finish_kernel,
        out_shape=shaped(values.shape, values.dtype),
        in_specs=[HBM],
        out_specs=VMEM,
        compiler_params=pltpu.CompilerParams(vmem_limit_bytes=1 << 20),
        name="finish",
        cost_estimate=COST,
    )(values)


def row_of(ref):
    return ref[...].astype(F32).reshape(1, -1)


def in_three(values):
    high = values.astype(BF16)
    rest = values - high.astype(F32)
    middle = rest.astype(BF16)
    return high, middle, (rest - middle.astype(F32)).astype(BF16)


def norm_step(grad, normed, rscale, gain):
    scaled = grad * gain
    first_mean = jnp.mean(scaled, axis=1, keepdims=True)
    cross_mean = jnp.mean(scaled * normed, axis=1, keepdims=True)
    return rscale * (scaled - first_mean - normed * cross_mean)


def column_of(ref):
    row = ref[...].reshape(1, -1)
    return jnp.broadcast_to(row, (128, row.shape[1])).T[:, 0:1]


def column_sum(values):
    return jnp.sum(values, axis=0, keepdims=True)


def send_out(results, outputs, semaphores, which):
    copies = [
        pltpu.make_async_copy(results[k], outputs[k], semaphores.at[k]) for k in which
    ]
    for copy in copies:
        copy.start()
    return copies


def loss_back(lengths_ref, place_ref, *refs):
    sources, outputs, refs = refs[:9], refs[9:15], refs[15:]
    targets, results = refs[:9], refs[9:15]
    coef_ref, turned_ref, semaphores, out_semaphores = refs[15:]
    copies = fetch(sources, targets, semaphores)
    piece_ref, swapped_ref, pooled_ref, match_ref, gain_ref = targets[:5]
    core, index = place_ref[0], place_ref[1]
    bounds = segment_bounds(lengths_ref)
    for copy in copies[:5]:
        copy.wait()
    first = core == 0
    queries = jnp.where(first, piece_ref[...], swapped_ref[...])
    passages = jnp.where(first, swapped_ref[...], piece_ref[...])
    count = queries.shape[0]
    own = pooled_ref.shape[0] // 2
    similarity = nt(queries, passages) / SOFTMAX_WARMTH
    match = match_ref[...].reshape(1, -1)
    match = match == lax.broadcasted_iota(jnp.int32, (count, count), 0)
    top = jnp.max(similarity, axis=1, keepdims=True)
    lse = top + jnp.log(jnp.sum(jnp.exp(similarity - top), axis=1, keepdims=True))
    positive = jnp.sum(jnp.where(match, similarity, 0.0), axis=1, keepdims=True)
    loss = jnp.sum(lse - positive, axis=0, keepdims=True) / count
    results[5][...] = jnp.broadcast_to(loss, results[5].shape)
    coef = (jnp.exp(similarity - lse) - match.astype(F32)) * (1.0 / (count * SOFTMAX_WARMTH))
    coef_ref[...] = coef
    turned_ref[...] = coef.T
    here = pl.ds(pl.multiple_of(index * own, own), own)
    grad_query = sum(nn(part, passages) for part in in_three(coef_ref[here, :])[:2])
    grad_passage = sum(nn(part, queries) for part in in_three(turned_ref[here, :])[:2])
    grad_unit = jnp.concatenate([grad_query, grad_passage], axis=0)
    pooled = pooled_ref[...]
    rscale = lax.rsqrt(jnp.sum(pooled * pooled, axis=1, keepdims=True) + EPS_NORM)
    inner = jnp.sum(pooled * grad_unit, axis=1, keepdims=True)
    grad_pooled = rscale * grad_unit - rscale * rscale * rscale * inner * pooled
    seqs = 2 * own
    grad_pooled = jnp.concatenate(
        [grad_pooled, jnp.zeros((128 - seqs, grad_pooled.shape[1]), F32)], axis=0
    )
    parts = in_three(grad_pooled)[:2]
    lane = lax.broadcasted_iota(jnp.int32, (1, 128), 1)
    begin = end = jnp.zeros((1, 128), jnp.int32)
    for seq, (start, stop) in enumerate(bounds):
        begin = jnp.where(lane == seq, start, begin)
        end = jnp.where(lane == seq, stop, end)
    gain = row_of(gain_ref)
    sums = [0.0, 0.0, 0.0]
    outgoing = []
    for i in range(2):
        copies[5 + 2 * i].wait()
        copies[6 + 2 * i].wait()
        normed = targets[5 + 2 * i][...]
        place = core * (2 * QB) + i * QB + lax.broadcasted_iota(jnp.int32, (QB, 128), 0)
        member = jnp.where((place >= begin) & (place < end), 1.0, 0.0).astype(BF16)
        grad = sum(nn(member, part) for part in parts)
        second = norm_step(grad, normed, column_of(targets[6 + 2 * i]), gain)
        rounded = second.astype(BF16)
        results[i][...] = second
        results[2 + i][...] = rounded
        for k, values in enumerate((rounded.astype(F32), grad * normed, grad)):
            sums[k] = sums[k] + column_sum(values)
        outgoing += send_out(results, outputs, out_semaphores, (2 + i, i))
    results[4][...] = jnp.concatenate(sums + [jnp.zeros((5, sums[0].shape[1]), F32)], axis=0)
    outgoing += send_out(results, outputs, out_semaphores, (4, 5))
    for copy in outgoing:
        copy.wait()


def norm_back(*refs):
    sources, outputs, refs = refs[:12], refs[12:17], refs[17:]
    targets, results = refs[:12], refs[12:17]
    semaphores, out_semaphores = refs[17:]
    copies = fetch(sources, targets, semaphores)
    copies[0].wait()
    copies[1].wait()
    gain = row_of(targets[0])
    sums = [0.0, 0.0, 0.0]
    outgoing = []
    for i in range(2):
        for copy in copies[2 + 5 * i : 7 + 5 * i]:
            copy.wait()
        second, pair_here, far, normed, rscale = targets[2 + 5 * i : 7 + 5 * i]
        grad = second[...] + (pair_here[...].astype(F32) + far[...].astype(F32))
        normed = normed[...]
        first = norm_step(grad, normed, column_of(rscale), gain)
        rounded = first.astype(BF16)
        results[i][...] = first
        results[2 + i][...] = rounded
        for k, values in enumerate((rounded.astype(F32), grad * normed, grad)):
            sums[k] = sums[k] + column_sum(values)
        outgoing += send_out(results, outputs, out_semaphores, (2 + i, i))
    blank = jnp.zeros((2, sums[0].shape[1]), F32)
    results[4][...] = jnp.concatenate(sums + [targets[1][0:3, :], blank], axis=0)
    outgoing += send_out(results, outputs, out_semaphores, (4,))
    for copy in outgoing:
        copy.wait()


STEPS = (0, 2, 1, 3)


def join(copies_of_each, place_ref, *refs):
    sources, output, semaphores = refs[:4], refs[4], refs[5]
    copies = []
    for k in range(4):
        spot = (place_ref[0] + 4 - STEPS[k]) % 4
        for r in range(copies_of_each):
            goal = output.at[spot] if copies_of_each == 1 else output.at[r, spot]
            semaphore = semaphores.at[k * copies_of_each + r]
            copies.append(pltpu.make_async_copy(sources[k], goal, semaphore))
            copies[-1].start()
    for copy in copies:
        copy.wait()


def place_block(piece, part, block_ref, spot, outputs, buffers_, semaphores, first):
    inner, cuts = buffers_
    inner[...] = block_ref[:, :piece, :].astype(F32)
    cuts[...] = block_ref[:, piece : 2 * piece - part, :].astype(F32)
    copies = [pltpu.make_async_copy(inner, outputs[0].at[:, spot], semaphores.at[first])]
    for m in range(4):
        goal = outputs[1 + m].at[spot, pl.ds(part, piece - part), :]
        copies.append(pltpu.make_async_copy(cuts.at[m], goal, semaphores.at[first + 1 + m]))
    for copy in copies:
        copy.start()
    return copies


def place_vectors(piece, part, block_ref, spot, outputs, vectors, semaphores, first):
    @pl.when(spot == 0)
    def _():
        small = block_ref[0, 2 * piece - part :, :].astype(F32)
        for k in range(7):
            vectors[k][...] = small[k : k + 1, :].reshape(-1)
        count = vectors[7].shape[0]
        for k in range(2):
            vectors[7 + k][...] = small[7:8, 256 * k : 256 * k + count].reshape(-1)
        copies = [
            pltpu.make_async_copy(vectors[k], outputs[5 + k], semaphores.at[first + k])
            for k in range(9)
        ]
        for copy in copies:
            copy.start()
        for copy in copies:
            copy.wait()


def spread_some(piece, part, count, place_ref, *refs):
    sources, outputs, refs = refs[:count], refs[count : count + 14], refs[count + 14 :]
    blocks, refs = refs[:count], refs[count:]
    buffers_, vectors, refs = refs[: 2 * count], refs[2 * count : 2 * count + 9], refs[-2:]
    arrivals = fetch(sources, blocks, refs[0])
    outgoing, spots = [], []
    for k in range(count):
        arrivals[k].wait()
        spots.append((place_ref[1] + 4 - STEPS[k]) % 4)
        outgoing += place_block(
            piece, part, blocks[k], spots[k], outputs, buffers_[2 * k : 2 * k + 2], refs[1], 5 * k
        )
    for k in range(count):
        place_vectors(piece, part, blocks[k], spots[k], outputs, vectors, refs[1], 5 * count)
    for copy in outgoing:
        copy.wait()


def spread_rest(piece, part, place_ref, *refs):
    sources, outputs, refs = refs[:3], refs[17:32], refs[32:]
    blocks, by_z, refs = refs[:2], refs[2], refs[3:]
    buffers_, outer, heads, vectors, refs = refs[:4], refs[4], refs[5], refs[6:15], refs[15:]
    semaphores, out_semaphores = refs
    arrivals = fetch(sources, (*blocks, by_z), semaphores)
    outgoing, spots = [], []
    for k in range(2):
        spots.append((place_ref[1] + 4 - STEPS[2 + k]) % 4)
        arrivals[k].wait()
        outgoing += place_block(
            piece,
            part,
            blocks[k],
            spots[k],
            outputs,
            buffers_[2 * k : 2 * k + 2],
            out_semaphores,
            5 * k,
        )
    arrivals[2].wait()
    outer[...] = by_z[:, :, :piece, :].astype(F32)
    copies = [pltpu.make_async_copy(outer, outputs[14], out_semaphores.at[10])]
    copies[0].start()
    heads[...] = by_z[:, :, piece:, :].astype(F32)
    for m in range(4):
        goal = outputs[1 + m].at[:, pl.ds(0, part), :]
        copies.append(pltpu.make_async_copy(heads.at[m], goal, out_semaphores.at[11 + m]))
        copies[-1].start()
    for k in range(2):
        place_vectors(piece, part, blocks[k], spots[k], outputs, vectors, out_semaphores, 15)
    for copy in outgoing + copies:
        copy.wait()


def run_loss(lengths, place, arrays):
    rows, width = arrays[5].shape
    count = arrays[0].shape[0]
    outs = (
        (shaped((rows, width), F32),) * 2
        + (shaped((rows, width), BF16),) * 2
        + (shaped((8, width), F32), shaped((8, 128), F32))
    )
    return pl.pallas_call(
        loss_back,
        out_shape=outs,
        in_specs=[SMEM] * 2 + [HBM] * 9,
        out_specs=(HBM,) * 6,
        scratch_shapes=buffers(arrays)
        + buffers(outs)
        + [pltpu.VMEM((count, count), F32)] * 2
        + [pltpu.SemaphoreType.DMA((9,)), pltpu.SemaphoreType.DMA((6,))],
        compiler_params=SHARED,
        name="loss_back",
        cost_estimate=COST,
    )(lengths, place, *arrays)


def run_norm(arrays):
    rows, width = arrays[2].shape
    outs = (
        (shaped((rows, width), F32),) * 2
        + (shaped((rows, width), BF16),) * 2
        + (shaped((8, width), F32),)
    )
    return pl.pallas_call(
        norm_back,
        out_shape=outs,
        in_specs=[HBM] * 12,
        out_specs=(HBM,) * 5,
        scratch_shapes=buffers(arrays)
        + buffers(outs)
        + [pltpu.SemaphoreType.DMA((12,)), pltpu.SemaphoreType.DMA((5,))],
        compiler_params=SMALL,
        name="norm_back",
        cost_estimate=COST,
    )(*arrays)


def run_join(place, pieces, copies_of_each):
    lead = (4,) if copies_of_each == 1 else (copies_of_each, 4)
    return pl.pallas_call(
        functools.partial(join, copies_of_each),
        out_shape=shaped(lead + pieces[0].shape, BF16),
        in_specs=[SMEM] + [HBM] * 4,
        out_specs=HBM,
        scratch_shapes=[pltpu.SemaphoreType.DMA((4 * copies_of_each,))],
        compiler_params=pltpu.CompilerParams(vmem_limit_bytes=1 << 20),
        name="join",
        cost_estimate=COST,
    )(place, *pieces)


def settle(core_ref, *refs):
    sources, output, semaphores = refs[:4], refs[4], refs[5]
    copies = []
    for k in range(4):
        first = (k // 2 + core_ref[0]) % 2 * (2 * QB) + k % 2 * QB
        spot = pl.ds(pl.multiple_of(first, QB), QB)
        copies.append(pltpu.make_async_copy(sources[k], output.at[spot, :], semaphores.at[k]))
        copies[-1].start()
    for copy in copies:
        copy.wait()


def run_settle(core, parts):
    rows, width = parts[0].shape
    return pl.pallas_call(
        settle,
        out_shape=shaped((4 * rows, width), BF16),
        in_specs=[SMEM] + [HBM] * 4,
        out_specs=HBM,
        scratch_shapes=[pltpu.SemaphoreType.DMA((4,))],
        compiler_params=pltpu.CompilerParams(vmem_limit_bytes=1 << 20),
        name="settle",
        cost_estimate=COST,
    )(core, *parts)


def spread_shapes(piece, width):
    shapes = [(4, 4, piece, width)] + [(4, piece, width)] * 4
    return shapes + [(width,)] * 7 + [(4 * piece,)] * 2


def run_spread_some(places, blocks, piece, part):
    width = blocks[0].shape[2]
    shapes = spread_shapes(piece, width)
    count = len(blocks)
    pair_of = [pltpu.VMEM((4, piece, width), F32), pltpu.VMEM((4, piece - part, width), F32)]
    return pl.pallas_call(
        functools.partial(spread_some, piece, part, count),
        out_shape=[shaped(shape, F32) for shape in shapes],
        in_specs=[SMEM] + [HBM] * count,
        out_specs=[HBM] * 14,
        scratch_shapes=buffers(blocks)
        + pair_of * count
        + [pltpu.VMEM(shape, F32) for shape in shapes[5:]]
        + [pltpu.SemaphoreType.DMA((count,)), pltpu.SemaphoreType.DMA((5 * count + 9,))],
        compiler_params=SHARED,
        name="spread_some",
        cost_estimate=COST,
    )(places, *blocks)


def run_spread_rest(places, blocks, gathered, so_far, piece, part):
    width = gathered.shape[3]
    shapes = spread_shapes(piece, width)
    outer = (4, 4, piece, width)
    pair_of = [pltpu.VMEM((4, piece, width), F32), pltpu.VMEM((4, piece - part, width), F32)]
    return pl.pallas_call(
        functools.partial(spread_rest, piece, part),
        out_shape=[shaped(shape, F32) for shape in shapes + [outer]],
        in_specs=[SMEM] + [HBM] * 17,
        out_specs=[HBM] * 15,
        input_output_aliases={4 + k: k for k in range(14)},
        scratch_shapes=buffers((*blocks, gathered))
        + pair_of * 2
        + [pltpu.VMEM(outer, F32), pltpu.VMEM((4, 4, part, width), F32)]
        + [pltpu.VMEM(shape, F32) for shape in shapes[5:]]
        + [pltpu.SemaphoreType.DMA((3,)), pltpu.SemaphoreType.DMA((24,))],
        compiler_params=SHARED,
        name="spread_rest",
        cost_estimate=COST,
    )(places, *blocks, gathered, *so_far)


def trade(values):
    return lax.all_to_all(
        values, "dp", split_axis=0, concat_axis=0, axis_index_groups=PLANES, tiled=True
    )


def share(values):
    spread_out = jnp.broadcast_to(values[None], (32,) + values.shape)
    return lax.all_to_all(spread_out, "dp", split_axis=0, concat_axis=0, tiled=True)


def trade_z(values):
    return lax.all_to_all(
        values, "dp", split_axis=0, concat_axis=0, axis_index_groups=Z_RINGS, tiled=True
    )


def ring_shift(axis, step):
    pairs = []
    for i in range(32):
        z, y, x = i // 8, (i // 2) % 4, i % 2
        z, y = ((z + step) % 4, y) if axis == "z" else (z, (y + step) % 4)
        pairs.append((i, (z * 4 + y) * 2 + x))
    return pairs


def ring_pieces(values, axis):
    return [lax.ppermute(values, "dp", ring_shift(axis, step)) for step in STEPS[1:]]


def tie(values, others):
    return lax.optimization_barrier((values, others))


class Marker:
    def __init__(self):
        self.state = jnp.zeros((8, 128), F32)

    def fence(self, ready, later):
        ready, state = tie(ready, self.state)
        later, self.state = tie(later, mark(state))
        return ready, later

    def moved(self, values, axis, pairs):
        values, state = tie(values, self.state)
        arrived, self.state = tie(lax.ppermute(values, axis, pairs), mark(state))
        return arrived

    def core_swap(self, values):
        return self.moved(values, "mp", CORE_SWAP)

    def near_swap(self, values):
        return self.moved(values, "dp", NEAR_SWAP)

    def both(self, own):
        return jnp.concatenate([own, self.core_swap(own)], axis=0)

    def near_sum(self, total):
        return (total.astype(F32) + self.near_swap(total).astype(F32)).astype(BF16)


def plane_sum(parts):
    return jnp.sum(parts.astype(F32), axis=0).astype(BF16)


def far_swap(values):
    return lax.ppermute(values, "mp", FAR_SWAP)


def norm_forward(values, gain_vec, shift_vec):
    average = jnp.mean(values, axis=-1, keepdims=True)
    centred = values - average
    rscale = lax.rsqrt(jnp.mean(centred * centred, axis=-1, keepdims=True) + EPS_NORM)
    normed = centred * rscale
    return (normed * gain_vec + shift_vec, normed, rscale[:, 0])


def gelu_and_slope(upper):
    below = 0.5 * (1.0 + lax.erf(upper * math.sqrt(0.5)))
    density = jnp.exp(-0.5 * upper * upper) * (1.0 / math.sqrt(2.0 * math.pi))
    return (upper * below).astype(BF16), (below + upper * density).astype(BF16)


def local(
    tokens,
    lengths,
    pair_index,
    query_proj,
    query_bias,
    key_proj,
    value_proj,
    value_bias,
    output_proj,
    output_bias,
    attn_gain,
    attn_shift,
    inner_proj,
    inner_bias,
    outer_proj,
    outer_bias,
    final_gain,
    final_shift,
):
    row_count, width = tokens.shape
    chunk = row_count // 2
    half = chunk // 2
    seq_count = lengths.shape[0]
    pair_count = seq_count // 2
    overall_pair_count = pair_index.shape[0]
    local_width = query_proj.shape[1]
    core = lax.axis_index("mp") % 2
    my_index = lax.axis_index("dp")
    marker = Marker()
    core_arg = jnp.reshape(core, (1,)).astype(jnp.int32)
    vectors = (output_bias, attn_gain, attn_shift, outer_bias, final_gain, final_shift)
    query_t, key_t, value_t = query_proj.T, key_proj.T, value_proj.T
    blank = jnp.zeros((256 - local_width, width), BF16)
    joint_proj = jnp.concatenate([query_t, blank, key_t, blank, value_t, blank], axis=0)

    weights = (query_t, key_t, value_t, query_bias, value_bias, output_proj, *vectors)
    first = run_first(lengths, core_arg, tokens, weights, (0, 1))
    rows, query_b, key_b, value_b, value_tb, mixed_a, lse_a = first[:7]
    attn_own_a, attn_other_a, members, vectors = first[7:]

    def own_and_other(values, weights):
        return nn(values[:half], weights), nn(values[half:], weights).astype(BF16)

    def pair(own, arrived):
        return (own + arrived.astype(F32)).astype(BF16)

    def first_norm(index, pair_here, far):
        attn_full = pair_here.astype(F32) + far.astype(F32) + output_bias
        own_tokens = rows[index * chunk : index * chunk + half].astype(F32)
        return norm_forward(own_tokens + attn_full, attn_gain_f, attn_shift_f)

    def feed_forward(own_hidden):
        whole = marker.both(own_hidden)
        act, slope = gelu_and_slope(nn(whole, inner_proj) + inner_bias.astype(F32))
        act, slope = tie(act, slope)
        return whole, act, slope

    def last_norm(hidden, pair_here, far):
        ffn_full = pair_here.astype(F32) + far.astype(F32) + outer_bias
        return norm_forward(hidden + ffn_full, final_gain_f, final_shift_f)

    attn_pair_a = pair(attn_own_a, marker.core_swap(attn_other_a))
    attn_far_a = far_swap(attn_pair_a)
    output_bias, attn_gain_f, attn_shift_f = vectors[0], vectors[1], vectors[2]
    outer_bias, final_gain_f, final_shift_f = vectors[3], vectors[4], vectors[5]
    late_query, late_pair = tie(query_b, attn_pair_a)
    mixed_b, lse_b, attn_own_b, attn_other_b = run_more(
        lengths, core_arg, (late_query, key_b, value_tb, output_proj), (2, 3)
    )
    attn_pair_b = pair(attn_own_b, marker.core_swap(attn_other_b))
    attn_far_b = far_swap(attn_pair_b)
    attn_far_a, attn_pair_b = tie(attn_far_a, attn_pair_b)
    hidden_a, normed_one_a, rscale_one_a = first_norm(0, late_pair, attn_far_a)
    own_hidden_a = hidden_a.astype(BF16)
    hidden_ab, act_a, slope_a = feed_forward(own_hidden_a)
    ffn_own_a, ffn_other_a = own_and_other(act_a, outer_proj)
    ffn_pair_a = pair(ffn_own_a, marker.core_swap(ffn_other_a))
    attn_far_b, ffn_pair_late = tie(attn_far_b, ffn_pair_a)
    ffn_far_a = far_swap(ffn_pair_a)
    hidden_b, normed_one_b, rscale_one_b = first_norm(1, attn_pair_b, attn_far_b)
    own_hidden_b = hidden_b.astype(BF16)
    hidden_bb, act_b, slope_b = feed_forward(own_hidden_b)
    ffn_own_b, ffn_other_b = own_and_other(act_b, outer_proj)
    ffn_pair_b = pair(ffn_own_b, marker.core_swap(ffn_other_b))
    ffn_pair_b, ffn_far_a = marker.fence(ffn_pair_b, ffn_far_a)
    final_a, normed_two_a, rscale_two_a = last_norm(hidden_a, ffn_pair_late, ffn_far_a)
    pooled_a = jnp.dot(members[0], final_a, precision=HIGHEST)
    final_b, normed_two_b, rscale_two_b = last_norm(hidden_b, ffn_pair_b, far_swap(ffn_pair_b))
    pooled_part = pooled_a + jnp.dot(members[1], final_b, precision=HIGHEST)
    lse = (lse_a, lse_b)
    hidden_whole, act, slope = (hidden_ab, hidden_bb), (act_a, act_b), (slope_a, slope_b)
    normed_one, rscale_one = (normed_one_a, normed_one_b), (rscale_one_a, rscale_one_b)
    normed_two, rscale_two = (normed_two_a, normed_two_b), (rscale_two_a, rscale_two_b)
    pooled = pooled_part + marker.core_swap(pooled_part)
    pool_rscale = lax.rsqrt(jnp.sum(pooled * pooled, axis=-1, keepdims=True) + EPS_NORM)
    unit_b = (pooled * pool_rscale).astype(BF16)

    piece = lax.dynamic_slice_in_dim(unit_b, core * pair_count, pair_count, 0)
    piece = share(piece).reshape(overall_pair_count, width)
    place_arg = jnp.stack([core, my_index]).astype(jnp.int32)
    *grads, last_sums, loss = run_loss(
        lengths,
        place_arg,
        (
            piece,
            marker.core_swap(piece),
            pooled,
            pair_index,
            final_gain,
            normed_two[0],
            rscale_two[0],
            normed_two[1],
            rscale_two[1],
        ),
    )
    grad_second, own_grad = grads[:2], grads[2:]

    inner_sums, grad_ffn, grad_up, hidden_other, outer_sums = [], [], [], [], []
    for i in range(2):
        grad_ffn.append(marker.both(own_grad[i]))
        grad_up.append((nt(grad_ffn[i], outer_proj) * slope[i].astype(F32)).astype(BF16))
        inner_sums.append(jnp.sum(grad_up[i].astype(F32), axis=0))
        other = nt(grad_up[i][half:], inner_proj).astype(BF16)
        late_act, other = tie(act[i], other)
        outer_sums.append(tn(late_act, grad_ffn[i]))
        swap = marker.core_swap if i else lambda rows_here: lax.ppermute(rows_here, "mp", CORE_SWAP)
        arrived, outer_sums[i] = tie(swap(other), outer_sums[i])
        hidden_other.append(arrived)
    hidden_pair = [pair(nt(grad_up[i][:half], inner_proj), hidden_other[i]) for i in range(2)]
    hidden_far = [far_swap(hidden_pair[i]) for i in range(2)]
    late_hidden, hidden_pair = tie(hidden_whole, hidden_pair)
    ffn_pack = jnp.concatenate(
        [
            (outer_sums[0] + outer_sums[1])
            .astype(BF16)
            .reshape(16, -1, width),
            (tn(late_hidden[0], grad_up[0]) + tn(late_hidden[1], grad_up[1]))
            .astype(BF16)
            .reshape(16, -1, width),
        ],
        axis=1,
    )
    ffn_pack, hidden_far = marker.fence(ffn_pack, hidden_far)
    ffn_parts = trade(ffn_pack)

    *grads, sums = run_norm(
        (
            attn_gain,
            last_sums,
            grad_second[0],
            hidden_pair[0],
            hidden_far[0],
            normed_one[0],
            rscale_one[0],
            grad_second[1],
            hidden_pair[1],
            hidden_far[1],
            normed_one[1],
            rscale_one[1],
        )
    )
    grad_first, own_grad = grads[:2], grads[2:]
    (*own_grad, sums), state = tie((*own_grad, sums), marker.state)
    arrived = [lax.ppermute(values, "mp", CORE_SWAP) for values in (*own_grad, sums)]
    (*other_grad, other_sums), marker.state = tie(arrived, mark(state))
    grad_rows, packed = run_back(
        lengths,
        core_arg,
        (
            own_grad[0],
            other_grad[0],
            own_grad[1],
            other_grad[1],
            mixed_a,
            mixed_b,
            *lse,
            output_proj,
            query_b,
            key_b,
            value_b,
            sums,
            other_sums,
            *inner_sums,
            rows,
        ),
    )

    def input_part(first):
        span = slice(first, first + half)
        return nn(grad_rows[span], joint_proj)

    token_pair = []
    for i in range(2):
        other = input_part(i * chunk + half).astype(BF16)
        token_pair.append(pair(input_part(i * chunk), marker.core_swap(other)))
    token_pair, (packed, ffn_parts) = marker.fence(token_pair, (packed, ffn_parts))
    (packed, token_pair), ffn_parts = marker.fence((packed, token_pair), ffn_parts)
    packed_parts = trade(packed)
    token_far = [far_swap(token_pair[i]) for i in range(2)]
    ffn_total = plane_sum(ffn_parts)
    ffn_near = lax.ppermute(ffn_total, "dp", NEAR_SWAP)
    ffn_reduced = (ffn_total.astype(F32) + ffn_near.astype(F32)).astype(BF16)
    ffn_reduced, packed_parts = tie(ffn_reduced, packed_parts)
    packed_reduced = marker.near_sum(plane_sum(packed_parts))
    token_far, packed_reduced = tie(token_far, packed_reduced)
    piece_rows = width // 16
    places = jnp.stack([my_index // 8, (my_index // 2) % 4]).astype(jnp.int32)
    halves = [
        jnp.concatenate([ffn_reduced[:piece_rows], packed_reduced[: piece_rows // 3]], axis=0),
        jnp.concatenate([ffn_reduced[piece_rows:], packed_reduced[piece_rows // 3 :]], axis=0),
    ]
    pieces = [ring_pieces(halves[1], "z"), ring_pieces(halves[0], "y")]
    halves, pieces = marker.fence(halves, pieces)
    other_ring = run_join(places[:1], (halves[1], *pieces[0]), 1)
    one_ring = run_join(places[1:], (halves[0], *pieces[1]), 4)
    pieces = ring_pieces(other_ring, "y")
    other_ring, one_ring = marker.fence(other_ring, one_ring)
    gathered = trade_z(one_ring)
    one_ring, token_far = marker.fence(one_ring, token_far)
    token_own = [
        (grad_first[i] + (token_pair[i].astype(F32) + token_far[i].astype(F32))).astype(BF16)
        for i in range(2)
    ]
    token_other = [lax.ppermute(rows_here, "mp", CORE_SWAP) for rows_here in token_own]
    token_grad = run_settle(core_arg, (*token_own, *token_other))
    closing = finish(marker.state)[0, 0]
    part = piece_rows // 3
    so_far = run_spread_some(places, (other_ring, pieces[0]), piece_rows, part)
    so_far, token_grad = tie(so_far, token_grad)
    *rest, outer_grad = run_spread_rest(
        places, pieces[1:], gathered, so_far, piece_rows, part
    )
    inner_grad, *rest = rest
    cuts = [values.reshape(local_width, width) for values in rest[:4]]
    vectors = rest[4:]
    return (
        loss[0, 0] + closing,
        token_grad,
        cuts[1].T,
        vectors[7],
        cuts[2].T,
        cuts[3].T,
        vectors[8],
        cuts[0],
        vectors[0],
        vectors[1],
        vectors[2],
        inner_grad.reshape(width, width),
        vectors[6],
        outer_grad.reshape(width, width),
        vectors[3],
        vectors[4],
        vectors[5],
    )


def solution(mesh):
    column, row, split = P(None, "mp"), P("mp", None), P("mp")
    placed = (
        (P("dp", None), P("dp"), P())
        + (column, split, column, column, split, row)
        + (P(), P(), P())
        + (column, split, row)
        + (P(), P(), P())
    )
    given = (
        (P(), P("dp", None))
        + (column, split, column, column, split, row)
        + (P(), P(), P())
        + (column, split, row)
        + (P(), P(), P())
    )
    return jax.shard_map(local, mesh=mesh, in_specs=placed, out_specs=given, check_vma=False)
```
